32 devices in a mesh: wide: 8 (over y, x, core), narrow: 4 (over z).
Axes of the slice: x: 2, y: 2, z: 4, core: 2. Of those that a mesh axis runs over, the one named last changes fastest.
Arguments:
- layer_input: bfloat16 [8192, 2048], P(('wide', 'narrow')), may hold values from -6 to 6
- heads_weight: bfloat16 [2048, 6144], P(('wide', 'narrow')), may hold values from -0.125 to 0.125
- heads_bias: bfloat16 [6144], P(('wide', 'narrow')), may hold values from -3 to 3
- merge_weight: bfloat16 [2048, 2048], P(('wide', 'narrow')), may hold values from -2 to 2
- merge_bias: bfloat16 [2048], P(('wide', 'narrow')), may hold values from -5 to 5
- norm_gains: bfloat16 [2, 2048], P(None, ('wide', 'narrow')), may hold values from 0.25 to 1.75
- norm_shifts: bfloat16 [2, 2048], P(None, ('wide', 'narrow')), may hold values from -3 to 3
- expand_weight: bfloat16 [2048, 2, 5504], P('narrow', None, 'wide'), may hold values from -0.125 to 0.125
- expand_bias: bfloat16 [2, 5504], P(None, ('wide', 'narrow')), may hold values from -3 to 3
- reduce_weight: bfloat16 [5504, 2048], P('wide', 'narrow'), may hold values from -0.625 to 0.625
- reduce_bias: bfloat16 [2048], P('narrow'), may hold values from -5 to 5
- joined: int32 [8], P('wide'), may hold values from 0 to 1, as said below
- prefix: int32 [8, 2], P('wide'), may hold values from 1 to 512
- cotangent: bfloat16 [8192, 2048], P(('wide', 'narrow')), may hold values from -6 to 6
Outputs:
- layer_output: bfloat16 [8192, 2048], P(('wide', 'narrow'))
- input_gradient: float32 [8192, 2048], P(('wide', 'narrow'))
- heads_weight_gradient: float32 [2048, 6144], P(('wide', 'narrow'))
- heads_bias_gradient: float32 [6144], P(('wide', 'narrow'))
- merge_weight_gradient: float32 [2048, 2048], P(('wide', 'narrow'))
- merge_bias_gradient: float32 [2048], P(('wide', 'narrow'))
- gains_gradient: float32 [2, 2048], P(None, ('wide', 'narrow'))
- shifts_gradient: float32 [2, 2048], P(None, ('wide', 'narrow'))
- expand_weight_gradient: float32 [2048, 2, 5504], P('narrow', None, 'wide')
- expand_bias_gradient: float32 [2, 5504], P(None, ('wide', 'narrow'))
- reduce_weight_gradient: float32 [5504, 2048], P('wide', 'narrow')
- reduce_bias_gradient: float32 [2048], P('narrow')
The draws below stay inside these ranges and needn't reach their ends.
Inputs may be any that keep to these rules, and one draw needn't show every extreme that they name: `joined`: exactly half of the 8 buckets, rounded up, hold one sequence (1); the others hold two sequences of half a bucket each (0).
All inputs are finite; a program needn't handle non-finite values.
Results may differ from the reference program's by a relative error of at most 0.015.
Values may be sent and summed in bfloat16 or wider, within the bound.
A program may use at most 256 MiB of HBM per device.

```python
import jax
import jax.numpy as jnp
from jax import lax

D = 2048
HEADS = 16
HDIM = 128
FF = 5504
BUCKET = 1024
BUCKETS = 8
TOKENS = 8192


def draw_joined(key, part):
    key = jax.random.fold_in(key, 17)
    order = jax.random.permutation(key, BUCKETS)
    return (order < (BUCKETS + 1) // 2).astype(jnp.int32)


def plant(result, own_key, smallest, high):
    shape = result.shape
    index_at = [jax.random.randint(jax.random.fold_in(own_key, axis), (), 0, shape[axis]) for axis in range(len(shape))]
    result = result.at[tuple(index_at)].set(smallest)
    longest = shape.index(max(shape))
    index_at[longest] = (index_at[longest] + 1) % shape[longest]
    return result.at[tuple(index_at)].set(high)


def strengthened(entries, own_key, source, target, parts, factor):
    owner, partner = [(jnp.arange(entries.shape[position]) // (entries.shape[position] // parts)).reshape([-1 if axis == position else 1 for axis in range(entries.ndim)]) for position in (source, target)]
    chosen = jax.random.permutation(own_key, parts)[partner]
    strong = (owner == chosen) | (owner == (partner + parts // 2) % parts)
    return jnp.where(strong, factor * entries, entries)


def block_scale(key, dims, split, smallest, largest):
    def one(position, blocks):
        draws = jax.random.uniform(jax.random.fold_in(jax.random.fold_in(key, 6), position), (blocks,), jnp.float32, smallest / len(split), largest / len(split))
        return jnp.repeat(jnp.exp(draws), dims[position] // blocks).reshape((-1,) + (1,) * (len(dims) - position - 1))

    loudness = one(*split[0])
    for cut in split[1:]:
        loudness = loudness * one(*cut)
    return loudness


def noise(key, extent, scale, bound, cuts=(), kind=jnp.bfloat16):
    entries = scale * jax.random.normal(key, extent, jnp.float32)
    if cuts:
        entries = entries * block_scale(key, extent, cuts, -0.22, 0.18)
    return jnp.clip(entries, -bound, bound).astype(kind)


def heavy_noise(own_key, shape, width, limit, split, heavy, held_as=jnp.bfloat16):
    array = width * jax.random.normal(own_key, shape, jnp.float32)
    if split:
        array = array * block_scale(own_key, shape, split, -0.22, 0.18)
    return jnp.clip(strengthened(array, jax.random.fold_in(own_key, 3), *heavy), -limit, limit).astype(held_as)


def setup_inputs(seed: int = 0) -> dict:
    arg_keys = jax.random.split(jax.random.key(seed), 15)
    layer_input = heavy_noise(arg_keys[0], (TOKENS, D), 1.0, 6.0, ((0, 32),), (0, 1, 32, 2.75))
    heads_weight = noise(arg_keys[1], (D, 3 * D), D ** -0.5, 0.125, ((0, 32),))
    heads_bias = noise(arg_keys[2], (3 * D,), 0.5, 3.0, ((0, 32),))
    merge_weight = noise(arg_keys[3], (D, D), 8 ** -0.5, 2.0, ((0, 32),))
    merge_bias = noise(arg_keys[4], (D,), 1.0, 5.0, ((0, 32),))
    norm_gains = jnp.clip(1.0 + 0.15 * jax.random.normal(arg_keys[5], (2, D), jnp.float32), 0.25, 1.75).astype(jnp.bfloat16)
    norm_shifts = noise(arg_keys[6], (2, D), 0.5, 3.0, ((1, 32),))
    expand_weight = noise(arg_keys[7], (D, 2, FF), D ** -0.5, 0.125, ((0, 4), (2, 8)))
    expand_bias = noise(arg_keys[8], (2, FF), 0.5, 3.0, ((1, 32),))
    reduce_weight = noise(arg_keys[9], (FF, D), (FF // 64) ** -0.5, 0.625, ((0, 8), (1, 4)))
    reduce_bias = noise(arg_keys[10], (D,), 1.0, 5.0, ((0, 4),))
    joined = draw_joined(jax.random.fold_in(arg_keys[14], 71), 0)
    prefix = plant(jax.random.randint(arg_keys[12], (BUCKETS, 2), 1, BUCKET // 2 + 1), jax.random.fold_in(arg_keys[12], 1), 1, (BUCKET // 2 + 1) - 1).astype(jnp.int32)
    cotangent = heavy_noise(arg_keys[13], (TOKENS, D), 1.0, 6.0, ((0, 32),), (0, 1, 32, 2.75))
    return dict(layer_input=layer_input, heads_weight=heads_weight, heads_bias=heads_bias, merge_weight=merge_weight, merge_bias=merge_bias, norm_gains=norm_gains, norm_shifts=norm_shifts, expand_weight=expand_weight, expand_bias=expand_bias, reduce_weight=reduce_weight, reduce_bias=reduce_bias, joined=joined, prefix=prefix, cotangent=cotangent)


residual_scale = 48.0 ** 0.5
norm_eps = 1e-05
masked_value = -1e+30

@jax.custom_vjp
def low(v):
    return lax.optimization_barrier(v.astype(jnp.bfloat16)).astype(jnp.float32)

@jax.custom_vjp
def low_back(v):
    return v

def low_keep(v):
    return (low(v), None)

def low_pass(kept, grad):
    return (grad,)

def back_keep(v):
    return (v, None)

def back_low(kept, grad):
    return (low(grad),)
low.defvjp(low_keep, low_pass)
low_back.defvjp(back_keep, back_low)

def matmul(left, right):
    return jnp.dot(left, right, precision=lax.Precision.HIGHEST, preferred_element_type=jnp.float32)

def layout(positions, joined_flag, prefix_pair, bucket_len):
    halfway = bucket_len // 2
    second_seq = (positions >= halfway).astype(jnp.int32) * (1 - joined_flag)
    local_pos = positions - second_seq * halfway
    prefix_len = jnp.where(joined_flag == 1, prefix_pair[0] + prefix_pair[1], jnp.where(second_seq == 1, prefix_pair[1], prefix_pair[0]))
    return (second_seq, local_pos, prefix_len)

def visible(query_pos, key_pos, joined_flag, prefix_pair, bucket_len):
    query_seq, query_local, query_prefix = layout(query_pos, joined_flag, prefix_pair, bucket_len)
    key_seq, key_local, key_prefix = layout(key_pos, joined_flag, prefix_pair, bucket_len)
    same_seq = query_seq[:, None] == key_seq[None, :]
    return same_seq & ((key_local[None, :] < key_prefix[None, :]) | (key_local[None, :] <= query_local[:, None]))

def rotary_tables(local_pos, head_size):
    halfway = head_size // 2
    inverse = 10000.0 ** (-(2.0 * jnp.arange(halfway).astype(jnp.float32)) / head_size)
    angles = local_pos.astype(jnp.float32)[:, None] * inverse[None, :]
    return (jnp.cos(angles)[:, None, :], jnp.sin(angles)[:, None, :])

def rotate(vectors, cosine, sine_table):
    halfway = vectors.shape[-1] // 2
    first_part, second_part = (vectors[..., :halfway], vectors[..., halfway:])
    return jnp.concatenate([first_part * cosine - second_part * sine_table, second_part * cosine + first_part * sine_table], axis=-1)

def normalize(values, gain, shift):
    centre = lax.optimization_barrier(jnp.mean(values, axis=-1, keepdims=True))
    centred = values - centre
    variance = lax.optimization_barrier(jnp.mean(centred * centred, axis=-1, keepdims=True))
    return centred * lax.rsqrt(variance + norm_eps) * gain + shift

def bucket_forward(params, bucket_rows, joined_flag, prefix_pair):
    heads_weight, heads_bias, merge_weight, merge_bias, norm_gains, norm_shifts, expand_weight, expand_bias, reduce_weight, reduce_bias = params
    bucket_len = bucket_rows.shape[0]
    positions = jnp.arange(bucket_len, dtype=jnp.int32)
    second_seq, local_pos, prefix_len = layout(positions, joined_flag, prefix_pair, bucket_len)
    cosine, sine_table = rotary_tables(local_pos, HDIM)
    key_mask = visible(positions, positions, joined_flag, prefix_pair, bucket_len)
    triple = low_back(matmul(bucket_rows, heads_weight) + heads_bias).reshape(bucket_len, 3, HEADS, HDIM)
    queries = low(rotate(triple[:, 0], cosine, sine_table))
    keys = low(rotate(triple[:, 1], cosine, sine_table))
    values = low(triple[:, 2])
    scores = low_back(jnp.einsum('qhd,khd->hqk', queries, keys, precision=lax.Precision.HIGHEST) * HDIM ** (-0.5))
    probs = low(jax.nn.softmax(jnp.where(key_mask[None], scores, masked_value), axis=-1))
    mixed = jnp.einsum('hqk,khd->qhd', probs, values, precision=lax.Precision.HIGHEST).reshape(bucket_len, D)
    mixed = low(low_back(mixed))
    attended = low_back(matmul(mixed, merge_weight) + merge_bias)
    hidden = normalize(residual_scale * bucket_rows + attended, norm_gains[0], norm_shifts[0])
    gate_up = low_back(matmul(low(hidden), expand_weight.reshape(D, 2 * FF)) + expand_bias.reshape(2 * FF))
    active = low(jax.nn.gelu(gate_up[:, :FF]) * gate_up[:, FF:])
    feed = low_back(matmul(active, reduce_weight) + reduce_bias)
    return normalize(residual_scale * hidden + feed, norm_gains[1], norm_shifts[1])

def layer_forward(params, layer_rows, joined, prefix):
    buckets = layer_rows.reshape(BUCKETS, BUCKET, D)

    def one_bucket(item):
        return bucket_forward(params, item[0], item[1], item[2])
    results = lax.map(jax.checkpoint(one_bucket), (buckets, joined, prefix))
    return results.reshape(TOKENS, D)

def reference(layer_input, heads_weight, heads_bias, merge_weight, merge_bias, norm_gains, norm_shifts, expand_weight, expand_bias, reduce_weight, reduce_bias, joined, prefix, cotangent):
    params = (heads_weight.astype(jnp.float32), heads_bias.astype(jnp.float32), merge_weight.astype(jnp.float32), merge_bias.astype(jnp.float32), norm_gains.astype(jnp.float32), norm_shifts.astype(jnp.float32), expand_weight.astype(jnp.float32), expand_bias.astype(jnp.float32), reduce_weight.astype(jnp.float32), reduce_bias.astype(jnp.float32))
    outputs, pullback = jax.vjp(lambda weights, inputs: layer_forward(weights, inputs, joined, prefix), params, layer_input.astype(jnp.float32))
    weight_grads, input_gradient = pullback(cotangent.astype(jnp.float32))
    return (outputs.astype(jnp.bfloat16), input_gradient, weight_grads[0], weight_grads[1], weight_grads[2], weight_grads[3], weight_grads[4], weight_grads[5], weight_grads[6], weight_grads[7], weight_grads[8], weight_grads[9])
```

```python
import jax
import jax.numpy as jnp
from jax import lax
from jax.sharding import PartitionSpec as P

HEADS = 16
HDIM = 128


residual_scale = 48.0**0.5
norm_eps = 1e-05
masked_value = -1e30
both_axes = ("wide", "narrow")


def layout(positions, joined_flag, prefix_pair, bucket_len):
    halfway = bucket_len // 2
    second_seq = (positions >= halfway).astype(jnp.int32) * (1 - joined_flag)
    local_pos = positions - second_seq * halfway
    prefix_len = jnp.where(
        joined_flag == 1,
        prefix_pair[0] + prefix_pair[1],
        jnp.where(second_seq == 1, prefix_pair[1], prefix_pair[0]),
    )
    return (second_seq, local_pos, prefix_len)


def visible(query_pos, key_pos, joined_flag, prefix_pair, bucket_len):
    query_seq, query_local, query_prefix = layout(query_pos, joined_flag, prefix_pair, bucket_len)
    key_seq, key_local, key_prefix = layout(key_pos, joined_flag, prefix_pair, bucket_len)
    same_seq = query_seq[:, None] == key_seq[None, :]
    return same_seq & (
        (key_local[None, :] < key_prefix[None, :]) | (key_local[None, :] <= query_local[:, None])
    )


def rotary_tables(local_pos, head_size):
    halfway = head_size // 2
    inverse = 10000.0 ** (-(2.0 * jnp.arange(halfway).astype(jnp.float32)) / head_size)
    angles = local_pos.astype(jnp.float32)[:, None] * inverse[None, :]
    return (jnp.cos(angles)[:, None, :], jnp.sin(angles)[:, None, :])


def rotate(vectors, cosine, sine_table):
    halfway = vectors.shape[-1] // 2
    first_part, second_part = (vectors[..., :halfway], vectors[..., halfway:])
    return jnp.concatenate(
        [
            first_part * cosine - second_part * sine_table,
            second_part * cosine + first_part * sine_table,
        ],
        axis=-1,
    )


def normalize(values, gain, shift):
    centre = jnp.mean(values, axis=-1, keepdims=True)
    centred = values - centre
    variance = jnp.mean(centred * centred, axis=-1, keepdims=True)
    inv_std = lax.rsqrt(variance + norm_eps)
    normed = centred * inv_std
    return (normed * gain + shift, normed, inv_std)


def normalize_back(upstream, normed, inv_std, gain):
    scaled = upstream * gain
    return inv_std * (
        scaled
        - jnp.mean(scaled, axis=-1, keepdims=True)
        - normed * jnp.mean(scaled * normed, axis=-1, keepdims=True)
    )


def dot(left, right, dims):
    return lax.dot_general(left, right, (dims, ((), ())), preferred_element_type=jnp.float32)


def low(values):
    return values.astype(jnp.bfloat16)


def gather_small(heads_bias, merge_bias, norm_gains, norm_shifts, expand_bias, reduce_bias):
    parts = (heads_bias, merge_bias, norm_gains, norm_shifts, expand_bias, reduce_bias)
    packed = jnp.concatenate([part.reshape(1, -1) for part in parts], axis=1)
    wide_count = lax.axis_size("wide")
    narrow_count = lax.axis_size("narrow")
    count = wide_count * narrow_count
    everyone = lax.all_gather(packed, both_axes, axis=0, tiled=True).astype(jnp.float32)
    pieces = []
    start = 0
    for part in parts:
        pieces.append(everyone[:, start : start + part.size])
        start += part.size

    def pairs(piece):
        return piece.reshape(piece.shape[0], 2, -1).transpose(1, 0, 2).reshape(2, -1)

    own_expand = lax.dynamic_index_in_dim(
        pieces[4].reshape(wide_count, narrow_count, -1), lax.axis_index("wide"), 0, keepdims=False
    )
    reduce_shift = pieces[5].reshape(wide_count, narrow_count, -1)[0].reshape(-1)
    return (
        pieces[0].reshape(-1),
        pieces[1].reshape(-1),
        pairs(pieces[2]),
        pairs(pieces[3]),
        pairs(own_expand),
        reduce_shift,
    )


def shards(
    layer_input,
    heads_weight,
    heads_bias,
    merge_weight,
    merge_bias,
    norm_gains,
    norm_shifts,
    expand_weight,
    expand_bias,
    reduce_weight,
    reduce_bias,
    joined,
    prefix,
    cotangent,
):
    tok_rows, model_width = layer_input.shape
    wide_count = lax.axis_size("wide")
    narrow_count = lax.axis_size("narrow")
    count = wide_count * narrow_count
    bucket_len = tok_rows * narrow_count
    own_heads = HEADS // narrow_count
    own_cols = own_heads * HDIM
    share = expand_weight.shape[2]
    score_scale = HDIM ** (-0.5)
    joined_flag = joined[0]
    prefix_pair = prefix[0]
    narrow_index = lax.axis_index("narrow")
    positions = jnp.arange(bucket_len, dtype=jnp.int32)
    second_seq, local_pos, prefix_len = layout(positions, joined_flag, prefix_pair, bucket_len)
    cosine, sine_table = rotary_tables(local_pos, HDIM)
    key_mask = visible(positions, positions, joined_flag, prefix_pair, bucket_len)

    rows_input = lax.all_gather(layer_input, "narrow", axis=0, tiled=True)
    swapped = lax.all_to_all(
        heads_weight.reshape(-1, 3, narrow_count, own_cols).transpose(2, 0, 1, 3),
        "narrow",
        split_axis=0,
        concat_axis=0,
        tiled=True,
    ).reshape(-1, 3 * own_cols)
    heads_mat = lax.all_gather(swapped, "wide", axis=0, tiled=True)
    heads_shift, merge_shift, gains, shifts, expand_shift, reduce_shift = gather_small(
        heads_bias, merge_bias, norm_gains, norm_shifts, expand_bias, reduce_bias
    )
    merge_full = lax.all_gather(merge_weight, both_axes, axis=0, tiled=True)
    own_shift = lax.dynamic_index_in_dim(
        heads_shift.reshape(3, narrow_count, own_cols), narrow_index, 1, keepdims=False
    ).reshape(-1)
    triple = dot(rows_input, heads_mat, ((1,), (0,))) + own_shift
    triple = triple.reshape(bucket_len, 3, own_heads, HDIM)
    queries = low(rotate(triple[:, 0], cosine, sine_table))
    keys = low(rotate(triple[:, 1], cosine, sine_table))
    values = low(triple[:, 2])
    scores = (
        jnp.einsum("qgd,kgd->gqk", queries, keys, preferred_element_type=jnp.float32) * score_scale
    )
    scores = jnp.where(key_mask[None], scores, masked_value)
    expo = jnp.exp(scores - jnp.max(scores, axis=-1, keepdims=True))
    probs_low = low(expo / jnp.sum(expo, axis=-1, keepdims=True))
    mixed_own = low(
        jnp.einsum("gqk,kgd->qgd", probs_low, values, preferred_element_type=jnp.float32)
    ).reshape(bucket_len, own_cols)
    mixed = lax.all_to_all(mixed_own, "narrow", split_axis=0, concat_axis=1, tiled=True)
    attended = dot(mixed, merge_full, ((1,), (0,))) + merge_shift
    hidden, normed_one, inv_one = normalize(
        residual_scale * layer_input.astype(jnp.float32) + attended, gains[0], shifts[0]
    )
    hidden_low = low(hidden)

    expand_full = lax.all_gather(
        expand_weight.transpose(1, 2, 0), "narrow", axis=2, tiled=True
    ).reshape(2 * share, model_width)
    reduce_full = lax.all_gather(reduce_weight, "narrow", axis=1, tiled=True)
    rows_all = lax.all_gather(hidden_low, "wide", axis=0, tiled=True)
    both = dot(rows_all, expand_full, ((1,), (1,))) + expand_shift.reshape(-1)
    gate, upper = both[:, :share], both[:, share:]
    gelu_value, gelu_pull = jax.vjp(jax.nn.gelu, gate)
    active = low(gelu_value * upper)
    gate_slope = low(gelu_pull(upper)[0])
    gelu_low = low(gelu_value)
    feed = (
        lax.psum_scatter(
            low(dot(active, reduce_full, ((1,), (0,)))), "wide", scatter_dimension=0, tiled=True
        ).astype(jnp.float32)
        + reduce_shift
    )
    output_float, normed_two, inv_two = normalize(
        residual_scale * hidden + feed, gains[1], shifts[1]
    )
    layer_output = low(output_float)

    grad_out = cotangent.astype(jnp.float32)
    gain_two_grad = jnp.sum(grad_out * normed_two, axis=0)
    shift_two_grad = jnp.sum(grad_out, axis=0)
    sum_two_grad = normalize_back(grad_out, normed_two, inv_two, gains[1])
    feed_grad = low(sum_two_grad)
    feed_grads_all = lax.all_gather(feed_grad, "wide", axis=0, tiled=True)
    active_grad = dot(feed_grads_all, reduce_full, ((1,), (1,)))
    gate_up_grad = low(
        jnp.concatenate([active_grad * gate_slope, active_grad * gelu_low], axis=1)
    )
    hidden_part = lax.psum_scatter(
        low(dot(gate_up_grad, expand_full, ((1,), (0,)))),
        "wide",
        scatter_dimension=0,
        tiled=True,
    )
    reduce_part = low(dot(active, feed_grads_all, ((0,), (0,))))
    expand_part = low(dot(gate_up_grad, rows_all, ((0,), (0,)))).reshape(2, share, model_width)
    reduce_weight_gradient = lax.psum_scatter(
        reduce_part, "narrow", scatter_dimension=1, tiled=True
    ).astype(jnp.float32)
    expand_weight_gradient = (
        lax.psum_scatter(expand_part, "narrow", scatter_dimension=2, tiled=True)
        .astype(jnp.float32)
        .transpose(2, 0, 1)
    )
    hidden_grad = residual_scale * sum_two_grad + hidden_part.astype(jnp.float32)
    gain_one_grad = jnp.sum(hidden_grad * normed_one, axis=0)
    shift_one_grad = jnp.sum(hidden_grad, axis=0)
    sum_one_grad = normalize_back(hidden_grad, normed_one, inv_one, gains[0])
    attended_grad = low(sum_one_grad)
    mixed_grad = low(dot(attended_grad, merge_full, ((1,), (1,))))
    upstream = lax.all_to_all(
        mixed_grad, "narrow", split_axis=1, concat_axis=0, tiled=True
    ).reshape(bucket_len, own_heads, HDIM)
    merge_part = low(dot(mixed, attended_grad, ((0,), (0,))))
    merge_weight_gradient = lax.psum_scatter(
        merge_part, both_axes, scatter_dimension=0, tiled=True
    ).astype(jnp.float32)
    probs_grad = jnp.einsum("qgd,kgd->gqk", upstream, values, preferred_element_type=jnp.float32)
    probs = probs_low.astype(jnp.float32)
    scores_grad = low(probs * (probs_grad - jnp.sum(probs * probs_grad, axis=-1, keepdims=True)))
    query_grads = (
        jnp.einsum("gqk,kgd->qgd", scores_grad, keys, preferred_element_type=jnp.float32)
        * score_scale
    )
    key_grads = (
        jnp.einsum("gqk,qgd->kgd", scores_grad, queries, preferred_element_type=jnp.float32)
        * score_scale
    )
    value_grads = jnp.einsum("gqk,qgd->kgd", probs_low, upstream, preferred_element_type=jnp.float32)
    triple_grad = low(
        jnp.stack(
            [
                rotate(query_grads, cosine, -sine_table),
                rotate(key_grads, cosine, -sine_table),
                value_grads,
            ],
            axis=1,
        )
    ).reshape(bucket_len, 3 * own_cols)
    input_part = lax.psum_scatter(
        low(dot(triple_grad, heads_mat, ((1,), (1,)))), "narrow", scatter_dimension=0, tiled=True
    )
    input_gradient = residual_scale * sum_one_grad + input_part.astype(jnp.float32)
    heads_part = lax.psum_scatter(
        low(dot(rows_input, triple_grad, ((0,), (0,)))), "wide", scatter_dimension=0, tiled=True
    )
    heads_weight_gradient = (
        lax.all_to_all(
            heads_part.reshape(narrow_count, -1, 3 * own_cols),
            "narrow",
            split_axis=0,
            concat_axis=0,
            tiled=True,
        )
        .reshape(narrow_count, -1, 3, own_cols)
        .transpose(1, 2, 0, 3)
        .reshape(heads_weight.shape)
        .astype(jnp.float32)
    )

    mine_narrow = (jnp.arange(narrow_count) == narrow_index).astype(jnp.float32)
    mine_wide = (jnp.arange(wide_count) == lax.axis_index("wide")).astype(jnp.float32)
    heads_sums = jnp.sum(triple_grad, axis=0, dtype=jnp.float32).reshape(3, 1, own_cols)
    heads_sums = (heads_sums * mine_narrow[None, :, None]).reshape(count, -1)
    merge_sums = jnp.sum(attended_grad, axis=0, dtype=jnp.float32).reshape(count, -1)
    norm_sums = (
        jnp.stack([gain_one_grad, gain_two_grad, shift_one_grad, shift_two_grad])
        .reshape(4, count, -1)
        .transpose(1, 0, 2)
        .reshape(count, -1)
    )
    expand_sums = jnp.sum(gate_up_grad, axis=0, dtype=jnp.float32)
    expand_sums = (
        expand_sums.reshape(2, narrow_count, -1).transpose(1, 0, 2).reshape(1, narrow_count, -1)
        * mine_wide[:, None, None]
    ).reshape(count, -1)
    reduce_sums = jnp.sum(feed_grad, axis=0, dtype=jnp.float32).reshape(1, narrow_count, -1)
    reduce_sums = jnp.broadcast_to(
        reduce_sums, (wide_count, narrow_count, reduce_sums.shape[2])
    ).reshape(count, -1)
    pieces = (heads_sums, merge_sums, norm_sums, expand_sums, reduce_sums)
    summed = lax.psum_scatter(
        jnp.concatenate(pieces, axis=1), both_axes, scatter_dimension=0, tiled=True
    )[0]
    ends = []
    start = 0
    for piece in pieces:
        ends.append(summed[start : start + piece.shape[1]])
        start += piece.shape[1]
    norm_ends = ends[2].reshape(4, -1)
    return (
        layer_output,
        input_gradient,
        heads_weight_gradient,
        ends[0],
        merge_weight_gradient,
        ends[1],
        norm_ends[:2],
        norm_ends[2:],
        expand_weight_gradient,
        ends[3].reshape(2, -1),
        reduce_weight_gradient,
        ends[4],
    )


def solution(mesh):
    return jax.shard_map(
        shards,
        mesh=mesh,
        in_specs=(
            P(("wide", "narrow"), None),
            P(("wide", "narrow"), None),
            P(("wide", "narrow")),
            P(("wide", "narrow"), None),
            P(("wide", "narrow")),
            P(None, ("wide", "narrow")),
            P(None, ("wide", "narrow")),
            P("narrow", None, "wide"),
            P(None, ("wide", "narrow")),
            P("wide", "narrow"),
            P("narrow"),
            P("wide"),
            P("wide", None),
            P(("wide", "narrow"), None),
        ),
        out_specs=(
            P(("wide", "narrow"), None),
            P(("wide", "narrow"), None),
            P(("wide", "narrow"), None),
            P(("wide", "narrow")),
            P(("wide", "narrow"), None),
            P(("wide", "narrow")),
            P(None, ("wide", "narrow")),
            P(None, ("wide", "narrow")),
            P("narrow", None, "wide"),
            P(None, ("wide", "narrow")),
            P("wide", "narrow"),
            P("narrow"),
        ),
        check_vma=False,
    )
```

```python
import functools
import math

import jax
import jax.numpy as jnp
from jax import lax
from jax.experimental import pallas as pl
from jax.experimental.pallas import tpu as pltpu
from jax.sharding import PartitionSpec as P

HEADS = 16
HDIM = 128


residual_scale = 48.0**0.5
norm_eps = 1e-05
masked_value = -1e30
both_axes = ("wide", "narrow")
kernel_memory = 60 * 2**20


def layout(positions, joined_flag, prefix_pair, bucket_len):
    halfway = bucket_len // 2
    second_seq = (positions >= halfway).astype(jnp.int32) * (1 - joined_flag)
    local_pos = positions - second_seq * halfway
    prefix_len = jnp.where(
        joined_flag == 1,
        prefix_pair[0] + prefix_pair[1],
        jnp.where(second_seq == 1, prefix_pair[1], prefix_pair[0]),
    )
    return (second_seq, local_pos, prefix_len)


def visible(query_pos, key_pos, joined_flag, prefix_pair, bucket_len):
    query_seq, query_local, query_prefix = layout(query_pos, joined_flag, prefix_pair, bucket_len)
    key_seq, key_local, key_prefix = layout(key_pos, joined_flag, prefix_pair, bucket_len)
    same_seq = query_seq[:, None] == key_seq[None, :]
    return same_seq & (
        (key_local[None, :] < key_prefix[None, :]) | (key_local[None, :] <= query_local[:, None])
    )


def rotary_tables(local_pos, head_size):
    halfway = head_size // 2
    inverse = 10000.0 ** (-(2.0 * jnp.arange(halfway).astype(jnp.float32)) / head_size)
    angles = local_pos.astype(jnp.float32)[:, None] * inverse[None, :]
    return (jnp.cos(angles)[:, None, :], jnp.sin(angles)[:, None, :])


def rotate(vectors, cosine, sine_table):
    halfway = vectors.shape[-1] // 2
    first_part, second_part = (vectors[..., :halfway], vectors[..., halfway:])
    return jnp.concatenate(
        [
            first_part * cosine - second_part * sine_table,
            second_part * cosine + first_part * sine_table,
        ],
        axis=-1,
    )


def normalize(values, gain, shift):
    centre = jnp.mean(values, axis=-1, keepdims=True)
    centred = values - centre
    variance = jnp.mean(centred * centred, axis=-1, keepdims=True)
    inv_std = lax.rsqrt(variance + norm_eps)
    normed = centred * inv_std
    return (normed * gain + shift, normed, inv_std)


def normalize_back(upstream, normed, inv_std, gain):
    scaled = upstream * gain
    return inv_std * (
        scaled
        - jnp.mean(scaled, axis=-1, keepdims=True)
        - normed * jnp.mean(scaled * normed, axis=-1, keepdims=True)
    )


def dot(left, right, dims):
    return lax.dot_general(left, right, (dims, ((), ())), preferred_element_type=jnp.float32)


def low(values):
    return values.astype(jnp.bfloat16)


def gather_small(heads_bias, merge_bias, norm_gains, norm_shifts, expand_bias, reduce_bias):
    parts = (heads_bias, merge_bias, norm_gains, norm_shifts, expand_bias, reduce_bias)
    packed = jnp.concatenate([part.reshape(1, -1) for part in parts], axis=1)
    wide_count = lax.axis_size("wide")
    narrow_count = lax.axis_size("narrow")
    count = wide_count * narrow_count
    everyone = lax.all_gather(packed, both_axes, axis=0, tiled=True).astype(jnp.float32)
    pieces = []
    start = 0
    for part in parts:
        pieces.append(everyone[:, start : start + part.size])
        start += part.size

    def pairs(piece):
        return piece.reshape(piece.shape[0], 2, -1).transpose(1, 0, 2).reshape(2, -1)

    own_expand = lax.dynamic_index_in_dim(
        pieces[4].reshape(wide_count, narrow_count, -1), lax.axis_index("wide"), 0, keepdims=False
    )
    reduce_shift = pieces[5].reshape(wide_count, narrow_count, -1)[0].reshape(-1)
    return (
        pieces[0].reshape(-1),
        pieces[1].reshape(-1),
        pairs(pieces[2]),
        pairs(pieces[3]),
        pairs(own_expand),
        reduce_shift,
    )


def ring_place(wide_count):
    ring = wide_count // 2
    mine = lax.axis_index("wide")
    chip = mine // 2
    core = mine % 2
    position = 2 * (chip // 2) + (chip % 2 + chip // 2) % 2
    return ring, position, core


def chip_at(position, ring):
    position = (position + 2 * ring) % ring
    return 2 * (position // 2) + (position + position // 2) % 2


class PlaneExchange:
    def __init__(self, wide_count, own, blocks, parts, from_mate, outgoing, incoming, sems):
        self.ring, self.position, self.core = ring_place(wide_count)
        self.own, self.blocks, self.parts = own, blocks, parts
        self.from_mate, self.outgoing, self.incoming = from_mate, outgoing, incoming
        (
            self.gather_send,
            self.gather_recv,
            self.mate_send,
            self.mate_recv,
            self.sum_send,
            self.sum_recv,
            self.own_sem,
        ) = sems
        self.half = blocks.shape[1] // 2
        self.far = self.ring // 2
        self.started = []

    def device(self, offset, mate=False):
        core = 1 - self.core if mate else self.core
        return {"wide": 2 * chip_at(self.position + offset, self.ring) + core}

    def slot(self, offset, mate=False):
        core = 1 - self.core if mate else self.core
        return 2 * chip_at(self.position + offset, self.ring) + core

    def rows(self, part):
        return pl.ds(part * self.half, self.half)

    def greet(self):
        barrier = pltpu.get_barrier_semaphore()
        for where in (self.device(-1), self.device(1), self.device(0, True)):
            pl.semaphore_signal(
                barrier, inc=1, device_id=where, device_id_type=pl.DeviceIdType.MESH
            )
        pl.semaphore_wait(barrier, 3)

    def start(self, source, target, send_sem, recv_sem, where):
        copy = pltpu.make_async_remote_copy(
            src_ref=source,
            dst_ref=target,
            send_sem=send_sem,
            recv_sem=recv_sem,
            device_id=where,
            device_id_type=pl.DeviceIdType.MESH,
        )
        copy.start()
        self.started.append(copy)

    def pass_on(self, lane, slot, part, where, source=None):
        target = self.blocks.at[slot, self.rows(part)]
        self.start(
            target if source is None else source,
            target,
            self.gather_send.at[lane, slot, part],
            self.gather_recv.at[slot, part],
            where,
        )

    def arrived(self, slot, part):
        target = self.blocks.at[slot, self.rows(part)]
        pltpu.make_async_remote_copy(
            src_ref=target,
            dst_ref=target,
            send_sem=self.gather_send.at[0, slot, part],
            recv_sem=self.gather_recv.at[slot, part],
            device_id=self.device(1),
            device_id_type=pl.DeviceIdType.MESH,
        ).wait_recv()

    def send_own(self):
        slot = self.slot(0)
        keep = pltpu.make_async_copy(self.own, self.blocks.at[slot], self.own_sem)
        keep.start()
        first, second = self.own.at[self.rows(0)], self.own.at[self.rows(1)]
        self.pass_on(0, slot, 0, self.device(1), first)
        self.pass_on(1, slot, 1, self.device(-1), second)
        self.pass_on(2, slot, 0, self.device(0, True), first)
        self.pass_on(2, slot, 1, self.device(0, True), second)
        self.pass_on(0, slot, 1, self.device(1), second)
        self.pass_on(1, slot, 0, self.device(-1), first)
        return keep

    def receive(self, distance):
        mate = self.device(0, True)
        left, right = self.slot(-distance), self.slot(distance)
        if distance == self.far:
            for part in range(2):
                self.arrived(left, part)
                self.pass_on(2, left, part, mate)
            return
        further = distance < self.far - 1
        self.arrived(left, 0)
        self.pass_on(0, left, 0, self.device(1))
        self.pass_on(2, left, 0, mate)
        self.arrived(right, 1)
        self.pass_on(1, right, 1, self.device(-1))
        self.pass_on(2, right, 1, mate)
        self.arrived(left, 1)
        if further:
            self.pass_on(0, left, 1, self.device(1))
        self.pass_on(2, left, 1, mate)
        self.arrived(right, 0)
        if further:
            self.pass_on(1, right, 0, self.device(-1))
        self.pass_on(2, right, 0, mate)

    def receive_mate(self, offset):
        for part in range(2):
            self.arrived(self.slot(offset, True), part)

    def share(self, offset):
        chip = chip_at(self.position + offset, self.ring)
        self.start(
            self.parts.at[self.slot(offset, True)],
            self.from_mate.at[chip],
            self.mate_send.at[chip],
            self.mate_recv.at[chip],
            self.device(0, True),
        )

    def shared(self, offset):
        chip = chip_at(self.position + offset, self.ring)
        pltpu.make_async_remote_copy(
            src_ref=self.parts.at[self.slot(offset)],
            dst_ref=self.from_mate.at[chip],
            send_sem=self.mate_send.at[chip],
            recv_sem=self.mate_recv.at[chip],
            device_id=self.device(0, True),
            device_id_type=pl.DeviceIdType.MESH,
        ).wait_recv()

    def chip_sum(self, offset, rows):
        chip = chip_at(self.position + offset, self.ring)
        return self.parts[self.slot(offset), rows].astype(jnp.float32) + self.from_mate[
            chip, rows
        ].astype(jnp.float32)

    def send_sum(self, way, distance, part):
        offset = distance if way == 0 else -distance
        begins = self.far if part == way else self.far - 1
        target = self.outgoing.at[way, distance - 1, part]
        if distance < begins:
            self.sum_arrived(way, distance, part)

        def chunk(i, carry):
            here = pl.ds(pl.multiple_of(i * 16, 16), 16)
            there = pl.ds(pl.multiple_of(part * self.half + i * 16, 16), 16)
            total = self.chip_sum(offset, there)
            if distance < begins:
                total += self.incoming[way, distance, part, here].astype(jnp.float32)
            target[here] = total.astype(jnp.bfloat16)
            return carry

        lax.fori_loop(0, self.half // 16, chunk, 0)
        self.start(
            target,
            self.incoming.at[way, distance - 1, part],
            self.sum_send.at[way, distance - 1, part],
            self.sum_recv.at[way, distance - 1, part],
            self.device(1 if way == 0 else -1),
        )

    def sum_arrived(self, way, distance, part):
        target = self.incoming.at[way, distance, part]
        pltpu.make_async_remote_copy(
            src_ref=target,
            dst_ref=target,
            send_sem=self.sum_send.at[way, distance, part],
            recv_sem=self.sum_recv.at[way, distance, part],
            device_id=self.device(1),
            device_id_type=pl.DeviceIdType.MESH,
        ).wait_recv()

    def run(self, compute):
        keep = self.send_own()
        keep.wait()
        self.receive_mate(0)
        compute(chip_at(self.position, self.ring))
        self.share(0)
        for distance in range(1, self.far):
            self.receive(distance)
            for offset in (-distance, distance):
                self.receive_mate(offset)
                compute(chip_at(self.position + offset, self.ring))
                self.share(offset)
            if distance == self.far - 1:
                self.shared(distance)
                self.send_sum(0, distance, 1)
                self.shared(-distance)
                self.send_sum(1, distance, 0)
        self.receive(self.far)
        self.receive_mate(self.far)
        compute(chip_at(self.position + self.far, self.ring))
        self.share(self.far)
        self.shared(self.far)
        self.send_sum(0, self.far, 0)
        self.send_sum(1, self.far, 1)
        for distance in range(self.far - 1, 0, -1):
            if distance < self.far - 1:
                self.shared(distance)
                self.shared(-distance)
            self.send_sum(0, distance, 0)
            self.send_sum(1, distance, 1)
            if distance < self.far - 1:
                self.send_sum(0, distance, 1)
                self.send_sum(1, distance, 0)

    def finish(self, result):
        self.shared(0)
        for part in range(2):
            for way in range(2):
                self.sum_arrived(way, 0, part)

            def chunk(i, carry):
                here = pl.ds(pl.multiple_of(i * 16, 16), 16)
                there = pl.ds(pl.multiple_of(part * self.half + i * 16, 16), 16)
                total = self.chip_sum(0, there)
                for way in range(2):
                    total += self.incoming[way, 0, part, here].astype(jnp.float32)
                result[there] = total
                return carry

            lax.fori_loop(0, self.half // 16, chunk, 0)
        for copy in self.started:
            copy.wait_send()


def exchange_scratch(wide_count, rows, width):
    ring = wide_count // 2
    far = ring // 2
    half = rows // 2
    dma = pltpu.SemaphoreType.DMA
    return [
        pltpu.VMEM((wide_count, rows, width), jnp.bfloat16),
        pltpu.VMEM((wide_count, rows, width), jnp.bfloat16),
        pltpu.VMEM((ring, rows, width), jnp.bfloat16),
        pltpu.VMEM((2, far, 2, half, width), jnp.bfloat16),
        pltpu.VMEM((2, far, 2, half, width), jnp.bfloat16),
        dma((3, wide_count, 2)),
        dma((wide_count, 2)),
        dma((ring,)),
        dma((ring,)),
        dma((2, far, 2)),
        dma((2, far, 2)),
        dma(()),
    ]


def load_padded(source, target, sem):
    filled = source.shape[0]
    copy = pltpu.make_async_copy(source, target.at[pl.ds(0, filled)], sem)
    copy.start()
    if filled < target.shape[0]:
        target[pl.ds(filled, target.shape[0] - filled)] = jnp.zeros(
            (target.shape[0] - filled, target.shape[1]), target.dtype
        )
    return copy


def pair_rows(ref, chip):
    block = ref[pl.ds(2 * chip, 2)]
    return block.reshape(2 * block.shape[1], block.shape[2])


def set_pair(ref, chip, cols, value):
    rows = ref.shape[1]
    ref[2 * chip, :, cols] = value[:rows].astype(ref.dtype)
    ref[2 * chip + 1, :, cols] = value[rows:].astype(ref.dtype)


def tiles(count, tile, body):
    def step(i, carry):
        body(pl.ds(pl.multiple_of(i * tile, tile), tile))
        return carry

    lax.fori_loop(0, count // tile, step, 0)


def geglu_forward_kernel(
    wide_count,
    own,
    expand,
    reduce,
    shift,
    rows_all,
    active_out,
    slope_out,
    gelu_out,
    feed,
    blocks,
    parts,
    from_mate,
    outgoing,
    incoming,
    gather_send,
    gather_recv,
    mate_send,
    mate_recv,
    sum_send,
    sum_recv,
    own_sem,
    expand_mat,
    reduce_mat,
    active,
    slope,
    gelu,
    load_sems,
    keep_sems,
):
    sems = (gather_send, gather_recv, mate_send, mate_recv, sum_send, sum_recv, own_sem)
    plane = PlaneExchange(wide_count, own, blocks, parts, from_mate, outgoing, incoming, sems)
    loads = [
        load_padded(expand.at[0], expand_mat.at[0], load_sems.at[0]),
        load_padded(expand.at[1], expand_mat.at[1], load_sems.at[1]),
        load_padded(reduce, reduce_mat, load_sems.at[2]),
    ]
    plane.greet()
    kept = []
    waiting = list(loads)

    def compute(chip):
        while waiting:
            waiting.pop().wait()

        def units(cols):
            rows = pair_rows(blocks, chip)
            gate = dot(rows, expand_mat[0, cols], ((1,), (1,))) + shift[0:1, cols]
            upper = dot(rows, expand_mat[1, cols], ((1,), (1,))) + shift[1:2, cols]
            factor = math.sqrt(2 / math.pi)
            square = gate * gate
            bend = jnp.tanh(factor * gate * (1 + 0.044715 * square))
            value = 0.5 * gate * (1 + bend)
            pull = 0.5 * (1 + bend) + 0.5 * gate * (1 - bend * bend) * factor * (
                1 + 3 * 0.044715 * square
            )
            set_pair(active, chip, cols, value * upper)
            set_pair(slope, chip, cols, pull * upper)
            set_pair(gelu, chip, cols, value)

        tiles(active.shape[2], 256, units)

        def outputs(cols):
            set_pair(
                parts, chip, cols, dot(pair_rows(active, chip), reduce_mat[:, cols], ((1,), (0,)))
            )

        tiles(parts.shape[2], 256, outputs)
        pair = pl.ds(2 * chip, 2)
        for index, (source, target) in enumerate(
            ((active, active_out), (slope, slope_out), (gelu, gelu_out), (blocks, rows_all))
        ):
            copy = pltpu.make_async_copy(
                source.at[pair], target.at[pair], keep_sems.at[chip, index]
            )
            copy.start()
            kept.append(copy)

    plane.run(compute)
    plane.finish(feed)
    for copy in kept:
        copy.wait()


def geglu_forward(wide_count, hidden_low, expand_full, reduce_full, shift):
    rows, width = hidden_low.shape
    padded = shift.shape[1]
    anywhere = pl.BlockSpec(memory_space=pl.ANY)
    vmem = pl.BlockSpec(memory_space=pltpu.VMEM)
    kept = jax.ShapeDtypeStruct((wide_count, rows, padded), jnp.bfloat16)
    scratch = exchange_scratch(wide_count, rows, width) + [
        pltpu.VMEM((2, padded, width), jnp.bfloat16),
        pltpu.VMEM((padded, width), jnp.bfloat16),
        pltpu.VMEM((wide_count, rows, padded), jnp.bfloat16),
        pltpu.VMEM((wide_count, rows, padded), jnp.bfloat16),
        pltpu.VMEM((wide_count, rows, padded), jnp.bfloat16),
        pltpu.SemaphoreType.DMA((3,)),
        pltpu.SemaphoreType.DMA((wide_count // 2, 4)),
    ]
    return pl.pallas_call(
        functools.partial(geglu_forward_kernel, wide_count),
        out_shape=(
            jax.ShapeDtypeStruct((wide_count, rows, width), jnp.bfloat16),
            kept,
            kept,
            kept,
            jax.ShapeDtypeStruct((rows, width), jnp.float32),
        ),
        in_specs=[anywhere, anywhere, anywhere, vmem],
        out_specs=(anywhere, anywhere, anywhere, anywhere, vmem),
        scratch_shapes=scratch,
        compiler_params=pltpu.CompilerParams(
            collective_id=1, has_side_effects=True, vmem_limit_bytes=kernel_memory
        ),
        cost_estimate=pl.CostEstimate(
            flops=6 * wide_count * rows * padded * width, bytes_accessed=200 * 2**20, transcendentals=0
        ),
        name="geglu_forward",
    )(hidden_low, expand_full, reduce_full, shift)


def geglu_backward_kernel(
    wide_count,
    own,
    expand,
    reduce,
    slope_in,
    gelu_in,
    rows_all,
    unit_grads,
    hidden_grad,
    blocks,
    parts,
    from_mate,
    outgoing,
    incoming,
    gather_send,
    gather_recv,
    mate_send,
    mate_recv,
    sum_send,
    sum_recv,
    own_sem,
    expand_mat,
    reduce_mat,
    slope,
    gelu,
    load_sems,
    keep_sems,
):
    sems = (gather_send, gather_recv, mate_send, mate_recv, sum_send, sum_recv, own_sem)
    plane = PlaneExchange(wide_count, own, blocks, parts, from_mate, outgoing, incoming, sems)
    loads = [
        load_padded(expand.at[0], expand_mat.at[0], load_sems.at[0]),
        load_padded(expand.at[1], expand_mat.at[1], load_sems.at[1]),
        load_padded(reduce, reduce_mat, load_sems.at[2]),
        pltpu.make_async_copy(slope_in, slope, load_sems.at[3]),
        pltpu.make_async_copy(gelu_in, gelu, load_sems.at[4]),
    ]
    for copy in loads[3:]:
        copy.start()
    plane.greet()
    kept = []
    waiting = list(loads)

    def compute(chip):
        while waiting:
            waiting.pop().wait()

        def units(cols):
            pulled = dot(pair_rows(blocks, chip), reduce_mat[cols], ((1,), (1,)))
            pair = pl.ds(2 * chip, 2)
            shape = pulled.shape
            gate_grad = pulled * slope[pair, :, cols].reshape(shape).astype(jnp.float32)
            upper_grad = pulled * gelu[pair, :, cols].reshape(shape).astype(jnp.float32)
            set_pair(slope, chip, cols, gate_grad)
            set_pair(gelu, chip, cols, upper_grad)

        tiles(slope.shape[2], 256, units)

        def outputs(cols):
            set_pair(
                parts,
                chip,
                cols,
                dot(pair_rows(slope, chip), expand_mat[0, :, cols], ((1,), (0,)))
                + dot(pair_rows(gelu, chip), expand_mat[1, :, cols], ((1,), (0,))),
            )

        tiles(parts.shape[2], 256, outputs)
        pair = pl.ds(2 * chip, 2)
        for index, (source, target) in enumerate(
            ((slope, unit_grads.at[0]), (gelu, unit_grads.at[1]), (blocks, rows_all))
        ):
            copy = pltpu.make_async_copy(
                source.at[pair], target.at[pair], keep_sems.at[chip, index]
            )
            copy.start()
            kept.append(copy)

    plane.run(compute)
    plane.finish(hidden_grad)
    for copy in kept:
        copy.wait()


def geglu_backward(wide_count, feed_grad, expand_full, reduce_full, slope, gelu):
    rows, width = feed_grad.shape
    padded = slope.shape[2]
    anywhere = pl.BlockSpec(memory_space=pl.ANY)
    vmem = pl.BlockSpec(memory_space=pltpu.VMEM)
    scratch = exchange_scratch(wide_count, rows, width) + [
        pltpu.VMEM((2, padded, width), jnp.bfloat16),
        pltpu.VMEM((padded, width), jnp.bfloat16),
        pltpu.VMEM((wide_count, rows, padded), jnp.bfloat16),
        pltpu.VMEM((wide_count, rows, padded), jnp.bfloat16),
        pltpu.SemaphoreType.DMA((5,)),
        pltpu.SemaphoreType.DMA((wide_count // 2, 3)),
    ]
    return pl.pallas_call(
        functools.partial(geglu_backward_kernel, wide_count),
        out_shape=(
            jax.ShapeDtypeStruct((wide_count, rows, width), jnp.bfloat16),
            jax.ShapeDtypeStruct((2, wide_count, rows, padded), jnp.bfloat16),
            jax.ShapeDtypeStruct((rows, width), jnp.float32),
        ),
        in_specs=[anywhere] * 5,
        out_specs=(anywhere, anywhere, vmem),
        scratch_shapes=scratch,
        compiler_params=pltpu.CompilerParams(
            collective_id=2, has_side_effects=True, vmem_limit_bytes=kernel_memory
        ),
        cost_estimate=pl.CostEstimate(
            flops=6 * wide_count * rows * padded * width, bytes_accessed=200 * 2**20, transcendentals=0
        ),
        name="geglu_backward",
    )(feed_grad, expand_full, reduce_full, slope, gelu)


def shards(
    layer_input,
    heads_weight,
    heads_bias,
    merge_weight,
    merge_bias,
    norm_gains,
    norm_shifts,
    expand_weight,
    expand_bias,
    reduce_weight,
    reduce_bias,
    joined,
    prefix,
    cotangent,
):
    tok_rows, model_width = layer_input.shape
    wide_count = lax.axis_size("wide")
    narrow_count = lax.axis_size("narrow")
    count = wide_count * narrow_count
    bucket_len = tok_rows * narrow_count
    own_heads = HEADS // narrow_count
    own_cols = own_heads * HDIM
    share = expand_weight.shape[2]
    score_scale = HDIM ** (-0.5)
    joined_flag = joined[0]
    prefix_pair = prefix[0]
    narrow_index = lax.axis_index("narrow")
    positions = jnp.arange(bucket_len, dtype=jnp.int32)
    second_seq, local_pos, prefix_len = layout(positions, joined_flag, prefix_pair, bucket_len)
    cosine, sine_table = rotary_tables(local_pos, HDIM)
    key_mask = visible(positions, positions, joined_flag, prefix_pair, bucket_len)

    rows_input = lax.all_gather(layer_input, "narrow", axis=0, tiled=True)
    swapped = lax.all_to_all(
        heads_weight.reshape(-1, 3, narrow_count, own_cols).transpose(2, 0, 1, 3),
        "narrow",
        split_axis=0,
        concat_axis=0,
        tiled=True,
    ).reshape(-1, 3 * own_cols)
    heads_mat = lax.all_gather(swapped, "wide", axis=0, tiled=True)
    heads_shift, merge_shift, gains, shifts, expand_shift, reduce_shift = gather_small(
        heads_bias, merge_bias, norm_gains, norm_shifts, expand_bias, reduce_bias
    )
    merge_full = lax.all_gather(merge_weight, both_axes, axis=0, tiled=True)
    own_shift = lax.dynamic_index_in_dim(
        heads_shift.reshape(3, narrow_count, own_cols), narrow_index, 1, keepdims=False
    ).reshape(-1)
    triple = dot(rows_input, heads_mat, ((1,), (0,))) + own_shift
    triple = triple.reshape(bucket_len, 3, own_heads, HDIM)
    queries = low(rotate(triple[:, 0], cosine, sine_table))
    keys = low(rotate(triple[:, 1], cosine, sine_table))
    values = low(triple[:, 2])
    scores = (
        jnp.einsum("qgd,kgd->gqk", queries, keys, preferred_element_type=jnp.float32) * score_scale
    )
    scores = jnp.where(key_mask[None], scores, masked_value)
    expo = jnp.exp(scores - jnp.max(scores, axis=-1, keepdims=True))
    probs_low = low(expo / jnp.sum(expo, axis=-1, keepdims=True))
    mixed_own = low(
        jnp.einsum("gqk,kgd->qgd", probs_low, values, preferred_element_type=jnp.float32)
    ).reshape(bucket_len, own_cols)
    mixed = lax.all_to_all(mixed_own, "narrow", split_axis=0, concat_axis=1, tiled=True)
    attended = dot(mixed, merge_full, ((1,), (0,))) + merge_shift
    hidden, normed_one, inv_one = normalize(
        residual_scale * layer_input.astype(jnp.float32) + attended, gains[0], shifts[0]
    )
    hidden_low = low(hidden)

    tile_rows = -share % 16
    padded = -(-share // 256) * 256
    expand_full = lax.all_gather(
        jnp.pad(expand_weight.transpose(1, 2, 0), ((0, 0), (0, tile_rows), (0, 0))),
        "narrow",
        axis=2,
        tiled=True,
    )
    reduce_full = lax.all_gather(
        jnp.pad(reduce_weight, ((0, tile_rows), (0, 0))), "narrow", axis=1, tiled=True
    )
    rows_all, active, slope, gelu, feed_sum = geglu_forward(
        wide_count,
        hidden_low,
        expand_full,
        reduce_full,
        jnp.pad(expand_shift, ((0, 0), (0, padded - share))),
    )
    feed = feed_sum + reduce_shift
    output_float, normed_two, inv_two = normalize(
        residual_scale * hidden + feed, gains[1], shifts[1]
    )
    layer_output = low(output_float)

    grad_out = cotangent.astype(jnp.float32)
    gain_two_grad = jnp.sum(grad_out * normed_two, axis=0)
    shift_two_grad = jnp.sum(grad_out, axis=0)
    sum_two_grad = normalize_back(grad_out, normed_two, inv_two, gains[1])
    feed_grad = low(sum_two_grad)
    feed_grads_all, unit_grads, hidden_part = geglu_backward(
        wide_count, feed_grad, expand_full, reduce_full, slope, gelu
    )
    tokens_all = wide_count * tok_rows
    rows_all = rows_all.reshape(tokens_all, model_width)
    feed_grads_all = feed_grads_all.reshape(tokens_all, model_width)
    unit_grads = unit_grads.reshape(2, tokens_all, padded)
    reduce_part = low(dot(active.reshape(tokens_all, padded), feed_grads_all, ((0,), (0,))))[:share]
    expand_part = low(dot(unit_grads, rows_all, ((1,), (0,))))[:, :share]
    reduce_weight_gradient = lax.psum_scatter(
        reduce_part, "narrow", scatter_dimension=1, tiled=True
    ).astype(jnp.float32)
    expand_weight_gradient = (
        lax.psum_scatter(expand_part, "narrow", scatter_dimension=2, tiled=True)
        .astype(jnp.float32)
        .transpose(2, 0, 1)
    )
    hidden_grad = residual_scale * sum_two_grad + hidden_part
    gain_one_grad = jnp.sum(hidden_grad * normed_one, axis=0)
    shift_one_grad = jnp.sum(hidden_grad, axis=0)
    sum_one_grad = normalize_back(hidden_grad, normed_one, inv_one, gains[0])
    attended_grad = low(sum_one_grad)
    mixed_grad = low(dot(attended_grad, merge_full, ((1,), (1,))))
    upstream = lax.all_to_all(
        mixed_grad, "narrow", split_axis=1, concat_axis=0, tiled=True
    ).reshape(bucket_len, own_heads, HDIM)
    merge_part = low(dot(mixed, attended_grad, ((0,), (0,))))
    merge_weight_gradient = lax.psum_scatter(
        merge_part, both_axes, scatter_dimension=0, tiled=True
    ).astype(jnp.float32)
    probs_grad = jnp.einsum("qgd,kgd->gqk", upstream, values, preferred_element_type=jnp.float32)
    probs = probs_low.astype(jnp.float32)
    scores_grad = low(probs * (probs_grad - jnp.sum(probs * probs_grad, axis=-1, keepdims=True)))
    query_grads = (
        jnp.einsum("gqk,kgd->qgd", scores_grad, keys, preferred_element_type=jnp.float32)
        * score_scale
    )
    key_grads = (
        jnp.einsum("gqk,qgd->kgd", scores_grad, queries, preferred_element_type=jnp.float32)
        * score_scale
    )
    value_grads = jnp.einsum("gqk,qgd->kgd", probs_low, upstream, preferred_element_type=jnp.float32)
    triple_grad = low(
        jnp.stack(
            [
                rotate(query_grads, cosine, -sine_table),
                rotate(key_grads, cosine, -sine_table),
                value_grads,
            ],
            axis=1,
        )
    ).reshape(bucket_len, 3 * own_cols)
    input_part = lax.psum_scatter(
        low(dot(triple_grad, heads_mat, ((1,), (1,)))), "narrow", scatter_dimension=0, tiled=True
    )
    input_gradient = residual_scale * sum_one_grad + input_part.astype(jnp.float32)
    heads_part = lax.psum_scatter(
        low(dot(rows_input, triple_grad, ((0,), (0,)))), "wide", scatter_dimension=0, tiled=True
    )
    heads_weight_gradient = (
        lax.all_to_all(
            heads_part.reshape(narrow_count, -1, 3 * own_cols),
            "narrow",
            split_axis=0,
            concat_axis=0,
            tiled=True,
        )
        .reshape(narrow_count, -1, 3, own_cols)
        .transpose(1, 2, 0, 3)
        .reshape(heads_weight.shape)
        .astype(jnp.float32)
    )

    mine_narrow = (jnp.arange(narrow_count) == narrow_index).astype(jnp.float32)
    mine_wide = (jnp.arange(wide_count) == lax.axis_index("wide")).astype(jnp.float32)
    heads_sums = jnp.sum(triple_grad, axis=0, dtype=jnp.float32).reshape(3, 1, own_cols)
    heads_sums = (heads_sums * mine_narrow[None, :, None]).reshape(count, -1)
    merge_sums = jnp.sum(attended_grad, axis=0, dtype=jnp.float32).reshape(count, -1)
    norm_sums = (
        jnp.stack([gain_one_grad, gain_two_grad, shift_one_grad, shift_two_grad])
        .reshape(4, count, -1)
        .transpose(1, 0, 2)
        .reshape(count, -1)
    )
    expand_sums = jnp.sum(unit_grads, axis=1, dtype=jnp.float32)[:, :share]
    expand_sums = (
        expand_sums.reshape(2, narrow_count, -1).transpose(1, 0, 2).reshape(1, narrow_count, -1)
        * mine_wide[:, None, None]
    ).reshape(count, -1)
    reduce_sums = jnp.sum(feed_grad, axis=0, dtype=jnp.float32).reshape(1, narrow_count, -1)
    reduce_sums = jnp.broadcast_to(
        reduce_sums, (wide_count, narrow_count, reduce_sums.shape[2])
    ).reshape(count, -1)
    pieces = (heads_sums, merge_sums, norm_sums, expand_sums, reduce_sums)
    summed = lax.psum_scatter(
        jnp.concatenate(pieces, axis=1), both_axes, scatter_dimension=0, tiled=True
    )[0]
    ends = []
    start = 0
    for piece in pieces:
        ends.append(summed[start : start + piece.shape[1]])
        start += piece.shape[1]
    norm_ends = ends[2].reshape(4, -1)
    return (
        layer_output,
        input_gradient,
        heads_weight_gradient,
        ends[0],
        merge_weight_gradient,
        ends[1],
        norm_ends[:2],
        norm_ends[2:],
        expand_weight_gradient,
        ends[3].reshape(2, -1),
        reduce_weight_gradient,
        ends[4],
    )


def solution(mesh):
    return jax.shard_map(
        shards,
        mesh=mesh,
        in_specs=(
            P(("wide", "narrow"), None),
            P(("wide", "narrow"), None),
            P(("wide", "narrow")),
            P(("wide", "narrow"), None),
            P(("wide", "narrow")),
            P(None, ("wide", "narrow")),
            P(None, ("wide", "narrow")),
            P("narrow", None, "wide"),
            P(None, ("wide", "narrow")),
            P("wide", "narrow"),
            P("narrow"),
            P("wide"),
            P("wide", None),
            P(("wide", "narrow"), None),
        ),
        out_specs=(
            P(("wide", "narrow"), None),
            P(("wide", "narrow"), None),
            P(("wide", "narrow"), None),
            P(("wide", "narrow")),
            P(("wide", "narrow"), None),
            P(("wide", "narrow")),
            P(None, ("wide", "narrow")),
            P(None, ("wide", "narrow")),
            P("narrow", None, "wide"),
            P(None, ("wide", "narrow")),
            P("wide", "narrow"),
            P("narrow"),
        ),
        check_vma=False,
    )
```

```python
import functools
import math

import jax
import jax.numpy as jnp
from jax import lax
from jax.experimental import pallas as pl
from jax.experimental.pallas import tpu as pltpu
from jax.sharding import PartitionSpec as P

HEADS = 16
HDIM = 128


residual_scale = 48.0**0.5
norm_eps = 1e-05
masked_value = -1e30
both_axes = ("wide", "narrow")
kernel_memory = 60 * 2**20


def layout(positions, joined_flag, prefix_pair, bucket_len):
    halfway = bucket_len // 2
    second_seq = (positions >= halfway).astype(jnp.int32) * (1 - joined_flag)
    local_pos = positions - second_seq * halfway
    prefix_len = jnp.where(
        joined_flag == 1,
        prefix_pair[0] + prefix_pair[1],
        jnp.where(second_seq == 1, prefix_pair[1], prefix_pair[0]),
    )
    return (second_seq, local_pos, prefix_len)


def visible(query_pos, key_pos, joined_flag, prefix_pair, bucket_len):
    query_seq, query_local, query_prefix = layout(query_pos, joined_flag, prefix_pair, bucket_len)
    key_seq, key_local, key_prefix = layout(key_pos, joined_flag, prefix_pair, bucket_len)
    same_seq = query_seq[:, None] == key_seq[None, :]
    return same_seq & (
        (key_local[None, :] < key_prefix[None, :]) | (key_local[None, :] <= query_local[:, None])
    )


def rotary_tables(local_pos, head_size):
    halfway = head_size // 2
    inverse = 10000.0 ** (-(2.0 * jnp.arange(halfway).astype(jnp.float32)) / head_size)
    angles = local_pos.astype(jnp.float32)[:, None] * inverse[None, :]
    return (jnp.cos(angles)[:, None, :], jnp.sin(angles)[:, None, :])


def rotate(vectors, cosine, sine_table):
    halfway = vectors.shape[-1] // 2
    first_part, second_part = (vectors[..., :halfway], vectors[..., halfway:])
    return jnp.concatenate(
        [
            first_part * cosine - second_part * sine_table,
            second_part * cosine + first_part * sine_table,
        ],
        axis=-1,
    )


def normalize(values, gain, shift):
    centre = jnp.mean(values, axis=-1, keepdims=True)
    centred = values - centre
    variance = jnp.mean(centred * centred, axis=-1, keepdims=True)
    inv_std = lax.rsqrt(variance + norm_eps)
    normed = centred * inv_std
    return (normed * gain + shift, normed, inv_std)


def normalize_back(upstream, normed, inv_std, gain):
    scaled = upstream * gain
    return inv_std * (
        scaled
        - jnp.mean(scaled, axis=-1, keepdims=True)
        - normed * jnp.mean(scaled * normed, axis=-1, keepdims=True)
    )


def dot(left, right, dims):
    return lax.dot_general(left, right, (dims, ((), ())), preferred_element_type=jnp.float32)


def low(values):
    return values.astype(jnp.bfloat16)


def gather_small(heads_bias, merge_bias, norm_gains, norm_shifts, expand_bias, reduce_bias):
    parts = (heads_bias, merge_bias, norm_gains, norm_shifts, expand_bias, reduce_bias)
    packed = jnp.concatenate([part.reshape(1, -1) for part in parts], axis=1)
    wide_count = lax.axis_size("wide")
    narrow_count = lax.axis_size("narrow")
    count = wide_count * narrow_count
    everyone = lax.all_gather(packed, both_axes, axis=0, tiled=True).astype(jnp.float32)
    pieces = []
    start = 0
    for part in parts:
        pieces.append(everyone[:, start : start + part.size])
        start += part.size

    def pairs(piece):
        return piece.reshape(piece.shape[0], 2, -1).transpose(1, 0, 2).reshape(2, -1)

    own_expand = lax.dynamic_index_in_dim(
        pieces[4].reshape(wide_count, narrow_count, -1), lax.axis_index("wide"), 0, keepdims=False
    )
    reduce_shift = pieces[5].reshape(wide_count, narrow_count, -1)[0].reshape(-1)
    return (
        pieces[0].reshape(-1),
        pieces[1].reshape(-1),
        pairs(pieces[2]),
        pairs(pieces[3]),
        pairs(own_expand),
        reduce_shift,
    )


def ring_place(wide_count):
    ring = wide_count // 2
    mine = lax.axis_index("wide")
    chip = mine // 2
    core = mine % 2
    position = 2 * (chip // 2) + (chip % 2 + chip // 2) % 2
    return ring, position, core


def chip_at(position, ring):
    position = (position + 2 * ring) % ring
    return 2 * (position // 2) + (position + position // 2) % 2


class PlaneExchange:
    def __init__(self, wide_count, own, blocks, parts, from_mate, incoming, sems):
        self.ring, self.position, self.core = ring_place(wide_count)
        self.own, self.blocks, self.parts = own, blocks, parts
        self.from_mate, self.incoming = from_mate, incoming
        (
            self.gather_send,
            self.gather_recv,
            self.mate_send,
            self.mate_recv,
            self.sum_send,
            self.sum_recv,
            self.own_sem,
        ) = sems
        self.half = parts.shape[1] // 2
        self.far = self.ring // 2
        self.started = []

    def device(self, offset, mate=False):
        core = 1 - self.core if mate else self.core
        return {"wide": 2 * chip_at(self.position + offset, self.ring) + core}

    def slot(self, offset, mate=False):
        core = 1 - self.core if mate else self.core
        return 2 * chip_at(self.position + offset, self.ring) + core

    def rows(self, part):
        return pl.ds(part * self.half, self.half)

    def greet(self):
        barrier = pltpu.get_barrier_semaphore()
        for where in (self.device(-1), self.device(1), self.device(0, True)):
            pl.semaphore_signal(
                barrier, inc=1, device_id=where, device_id_type=pl.DeviceIdType.MESH
            )
        pl.semaphore_wait(barrier, 3)

    def start(self, source, target, send_sem, recv_sem, where):
        copy = pltpu.make_async_remote_copy(
            src_ref=source,
            dst_ref=target,
            send_sem=send_sem,
            recv_sem=recv_sem,
            device_id=where,
            device_id_type=pl.DeviceIdType.MESH,
        )
        copy.start()
        self.started.append(copy)

    def pass_on(self, lane, slot, part, where, source=None):
        target = self.blocks.at[slot, self.rows(part)]
        self.start(
            target if source is None else source,
            target,
            self.gather_send.at[lane, slot, part],
            self.gather_recv.at[slot, part],
            where,
        )

    def arrived(self, slot, part):
        target = self.blocks.at[slot, self.rows(part)]
        pltpu.make_async_remote_copy(
            src_ref=target,
            dst_ref=target,
            send_sem=self.gather_send.at[0, slot, part],
            recv_sem=self.gather_recv.at[slot, part],
            device_id=self.device(1),
            device_id_type=pl.DeviceIdType.MESH,
        ).wait_recv()

    def send_own(self):
        slot = self.slot(0)
        keep = pltpu.make_async_copy(self.own, self.blocks.at[slot], self.own_sem)
        keep.start()
        first, second = self.own.at[self.rows(0)], self.own.at[self.rows(1)]
        self.pass_on(0, slot, 0, self.device(1), first)
        self.pass_on(1, slot, 1, self.device(-1), second)
        self.pass_on(2, slot, 0, self.device(0, True), first)
        self.pass_on(2, slot, 1, self.device(0, True), second)
        self.pass_on(0, slot, 1, self.device(1), second)
        self.pass_on(1, slot, 0, self.device(-1), first)
        return keep

    def receive(self, distance):
        mate = self.device(0, True)
        left, right = self.slot(-distance), self.slot(distance)
        if distance == self.far:
            for part in range(2):
                self.arrived(left, part)
                self.pass_on(2, left, part, mate)
            return
        further = distance < self.far - 1
        self.arrived(left, 0)
        self.pass_on(0, left, 0, self.device(1))
        self.pass_on(2, left, 0, mate)
        self.arrived(right, 1)
        self.pass_on(1, right, 1, self.device(-1))
        self.pass_on(2, right, 1, mate)
        self.arrived(left, 1)
        if further:
            self.pass_on(0, left, 1, self.device(1))
        self.pass_on(2, left, 1, mate)
        self.arrived(right, 0)
        if further:
            self.pass_on(1, right, 0, self.device(-1))
        self.pass_on(2, right, 0, mate)

    def receive_mate(self, offset):
        for part in range(2):
            self.arrived(self.slot(offset, True), part)

    def share(self, offset):
        chip = chip_at(self.position + offset, self.ring)
        self.start(
            self.parts.at[self.slot(offset, True)],
            self.from_mate.at[chip],
            self.mate_send.at[chip],
            self.mate_recv.at[chip],
            self.device(0, True),
        )

    def shared(self, offset):
        chip = chip_at(self.position + offset, self.ring)
        pltpu.make_async_remote_copy(
            src_ref=self.parts.at[self.slot(offset)],
            dst_ref=self.from_mate.at[chip],
            send_sem=self.mate_send.at[chip],
            recv_sem=self.mate_recv.at[chip],
            device_id=self.device(0, True),
            device_id_type=pl.DeviceIdType.MESH,
        ).wait_recv()

    def chip_sum(self, offset, rows):
        chip = chip_at(self.position + offset, self.ring)
        return self.parts[self.slot(offset), rows].astype(jnp.float32) + self.from_mate[
            chip, rows
        ].astype(jnp.float32)

    def send_sum(self, way, distance, part):
        offset = distance if way == 0 else -distance
        begins = self.far if part == way else self.far - 1
        slot = self.slot(offset)
        if distance < begins:
            self.sum_arrived(way, distance, part)

        def chunk(i, carry):
            here = pl.ds(pl.multiple_of(i * 16, 16), 16)
            there = pl.ds(pl.multiple_of(part * self.half + i * 16, 16), 16)
            total = self.chip_sum(offset, there)
            if distance < begins:
                total += self.incoming[way, distance, part, here].astype(jnp.float32)
            self.parts[slot, there] = total.astype(jnp.bfloat16)
            return carry

        lax.fori_loop(0, self.half // 16, chunk, 0)
        self.start(
            self.parts.at[slot, self.rows(part)],
            self.incoming.at[way, distance - 1, part],
            self.sum_send.at[way, distance - 1, part],
            self.sum_recv.at[way, distance - 1, part],
            self.device(1 if way == 0 else -1),
        )

    def sum_arrived(self, way, distance, part):
        target = self.incoming.at[way, distance, part]
        pltpu.make_async_remote_copy(
            src_ref=target,
            dst_ref=target,
            send_sem=self.sum_send.at[way, distance, part],
            recv_sem=self.sum_recv.at[way, distance, part],
            device_id=self.device(1),
            device_id_type=pl.DeviceIdType.MESH,
        ).wait_recv()

    def run(self, compute):
        keep = self.send_own()
        keep.wait()
        self.receive_mate(0)
        compute(chip_at(self.position, self.ring))
        self.share(0)
        for distance in range(1, self.far):
            self.receive(distance)
            for offset in (-distance, distance):
                self.receive_mate(offset)
                compute(chip_at(self.position + offset, self.ring))
                self.share(offset)
            if distance == self.far - 1:
                self.first_sums()
        self.receive(self.far)
        self.receive_mate(self.far)
        compute(chip_at(self.position + self.far, self.ring))
        self.share(self.far)
        self.far_sums()
        self.last_sums()

    def first_sums(self):
        distance = self.far - 1
        self.shared(distance)
        self.send_sum(0, distance, 1)
        self.shared(-distance)
        self.send_sum(1, distance, 0)

    def far_sums(self):
        self.shared(self.far)
        self.send_sum(0, self.far, 0)
        self.send_sum(1, self.far, 1)

    def last_sums(self):
        for distance in range(self.far - 1, 0, -1):
            if distance < self.far - 1:
                self.shared(distance)
                self.shared(-distance)
            self.send_sum(0, distance, 0)
            self.send_sum(1, distance, 1)
            if distance < self.far - 1:
                self.send_sum(0, distance, 1)
                self.send_sum(1, distance, 0)

    def finish(self, result):
        self.shared(0)
        for part in range(2):
            for way in range(2):
                self.sum_arrived(way, 0, part)

            def chunk(i, carry):
                here = pl.ds(pl.multiple_of(i * 16, 16), 16)
                there = pl.ds(pl.multiple_of(part * self.half + i * 16, 16), 16)
                total = self.chip_sum(0, there)
                for way in range(2):
                    total += self.incoming[way, 0, part, here].astype(jnp.float32)
                result[there] = total.astype(result.dtype)
                return carry

            lax.fori_loop(0, self.half // 16, chunk, 0)

    def drain(self):
        for copy in self.started:
            copy.wait_send()


def sum_scratch(wide_count, rows, width):
    ring = wide_count // 2
    far = ring // 2
    dma = pltpu.SemaphoreType.DMA
    return [
        pltpu.VMEM((wide_count, rows, width), jnp.bfloat16),
        pltpu.VMEM((ring, rows, width), jnp.bfloat16),
        pltpu.VMEM((2, far, 2, rows // 2, width), jnp.bfloat16),
        dma((ring,)),
        dma((ring,)),
        dma((2, far, 2)),
        dma((2, far, 2)),
    ]


def exchange_scratch(wide_count, rows, width):
    dma = pltpu.SemaphoreType.DMA
    return [
        pltpu.VMEM((wide_count, rows, width), jnp.bfloat16),
        dma((3, wide_count, 2)),
        dma((wide_count, 2)),
        dma(()),
    ] + sum_scratch(wide_count, rows, width)


def load_padded(source, target, sem):
    filled = source.shape[0]
    copy = pltpu.make_async_copy(source, target.at[pl.ds(0, filled)], sem)
    copy.start()
    if filled < target.shape[0]:
        target[pl.ds(filled, target.shape[0] - filled)] = jnp.zeros(
            (target.shape[0] - filled, target.shape[1]), target.dtype
        )
    return copy


def pair_rows(ref, chip):
    block = ref[pl.ds(2 * chip, 2)]
    return block.reshape(2 * block.shape[1], block.shape[2])


def set_pair(ref, chip, cols, value):
    rows = ref.shape[1]
    ref[2 * chip, :, cols] = value[:rows].astype(ref.dtype)
    ref[2 * chip + 1, :, cols] = value[rows:].astype(ref.dtype)


def tiles(count, tile, body):
    def step(i, carry):
        body(pl.ds(pl.multiple_of(i * tile, tile), tile))
        return carry

    lax.fori_loop(0, count // tile, step, 0)


def geglu_forward_kernel(
    wide_count,
    own,
    expand,
    reduce,
    shift,
    rows_all,
    active_out,
    slope_out,
    gelu_out,
    feed,
    blocks,
    gather_send,
    gather_recv,
    own_sem,
    parts,
    from_mate,
    incoming,
    mate_send,
    mate_recv,
    sum_send,
    sum_recv,
    expand_mat,
    reduce_mat,
    active,
    slope,
    gelu,
    load_sems,
    keep_sems,
):
    sems = (gather_send, gather_recv, mate_send, mate_recv, sum_send, sum_recv, own_sem)
    plane = PlaneExchange(wide_count, own, blocks, parts, from_mate, incoming, sems)
    loads = [
        load_padded(expand.at[0], expand_mat.at[0], load_sems.at[0]),
        load_padded(expand.at[1], expand_mat.at[1], load_sems.at[1]),
        load_padded(reduce, reduce_mat, load_sems.at[2]),
    ]
    plane.greet()
    kept = []
    waiting = list(loads)

    def compute(chip):
        while waiting:
            waiting.pop().wait()

        def units(cols):
            rows = pair_rows(blocks, chip)
            gate = dot(rows, expand_mat[0, cols], ((1,), (1,))) + shift[0:1, cols]
            upper = dot(rows, expand_mat[1, cols], ((1,), (1,))) + shift[1:2, cols]
            factor = math.sqrt(2 / math.pi)
            square = gate * gate
            bend = jnp.tanh(factor * gate * (1 + 0.044715 * square))
            value = 0.5 * gate * (1 + bend)
            pull = 0.5 * (1 + bend) + 0.5 * gate * (1 - bend * bend) * factor * (
                1 + 3 * 0.044715 * square
            )
            set_pair(active, chip, cols, value * upper)
            set_pair(slope, chip, cols, pull * upper)
            set_pair(gelu, chip, cols, value)

        tiles(active.shape[2], 256, units)

        def outputs(cols):
            set_pair(
                parts, chip, cols, dot(pair_rows(active, chip), reduce_mat[:, cols], ((1,), (0,)))
            )

        tiles(parts.shape[2], 256, outputs)
        pair = pl.ds(2 * chip, 2)
        for index, (source, target) in enumerate(
            ((active, active_out), (slope, slope_out), (gelu, gelu_out), (blocks, rows_all))
        ):
            copy = pltpu.make_async_copy(
                source.at[pair], target.at[pair], keep_sems.at[chip, index]
            )
            copy.start()
            kept.append(copy)

    plane.run(compute)
    plane.finish(feed)
    plane.drain()
    for copy in kept:
        copy.wait()


def geglu_forward(wide_count, hidden_low, expand_full, reduce_full, shift):
    rows, width = hidden_low.shape
    padded = shift.shape[1]
    anywhere = pl.BlockSpec(memory_space=pl.ANY)
    vmem = pl.BlockSpec(memory_space=pltpu.VMEM)
    kept = jax.ShapeDtypeStruct((wide_count, rows, padded), jnp.bfloat16)
    scratch = exchange_scratch(wide_count, rows, width) + [
        pltpu.VMEM((2, padded, width), jnp.bfloat16),
        pltpu.VMEM((padded, width), jnp.bfloat16),
        pltpu.VMEM((wide_count, rows, padded), jnp.bfloat16),
        pltpu.VMEM((wide_count, rows, padded), jnp.bfloat16),
        pltpu.VMEM((wide_count, rows, padded), jnp.bfloat16),
        pltpu.SemaphoreType.DMA((3,)),
        pltpu.SemaphoreType.DMA((wide_count // 2, 4)),
    ]
    return pl.pallas_call(
        functools.partial(geglu_forward_kernel, wide_count),
        out_shape=(
            jax.ShapeDtypeStruct((wide_count, rows, width), jnp.bfloat16),
            kept,
            kept,
            kept,
            jax.ShapeDtypeStruct((rows, width), jnp.float32),
        ),
        in_specs=[anywhere, anywhere, anywhere, vmem],
        out_specs=(anywhere, anywhere, anywhere, anywhere, vmem),
        scratch_shapes=scratch,
        compiler_params=pltpu.CompilerParams(
            collective_id=1, has_side_effects=True, vmem_limit_bytes=kernel_memory
        ),
        cost_estimate=pl.CostEstimate(
            flops=6 * wide_count * rows * padded * width, bytes_accessed=200 * 2**20, transcendentals=0
        ),
        name="geglu_forward",
    )(hidden_low, expand_full, reduce_full, shift)


def geglu_backward_kernel(
    wide_count,
    own,
    expand,
    reduce,
    slope_in,
    gelu_in,
    rows_all,
    unit_grads,
    hidden_grad,
    unit_sums,
    blocks,
    gather_send,
    gather_recv,
    own_sem,
    parts,
    from_mate,
    incoming,
    mate_send,
    mate_recv,
    sum_send,
    sum_recv,
    expand_mat,
    reduce_mat,
    slope,
    gelu,
    load_sems,
    keep_sems,
):
    sems = (gather_send, gather_recv, mate_send, mate_recv, sum_send, sum_recv, own_sem)
    plane = PlaneExchange(wide_count, own, blocks, parts, from_mate, incoming, sems)
    loads = [
        load_padded(expand.at[0], expand_mat.at[0], load_sems.at[0]),
        load_padded(expand.at[1], expand_mat.at[1], load_sems.at[1]),
        load_padded(reduce, reduce_mat, load_sems.at[2]),
        pltpu.make_async_copy(slope_in, slope, load_sems.at[3]),
        pltpu.make_async_copy(gelu_in, gelu, load_sems.at[4]),
    ]
    for copy in loads[3:]:
        copy.start()
    unit_sums[...] = jnp.zeros_like(unit_sums)
    plane.greet()
    kept = []
    waiting = list(loads)

    def compute(chip):
        while waiting:
            waiting.pop().wait()

        def units(cols):
            pulled = dot(pair_rows(blocks, chip), reduce_mat[cols], ((1,), (1,)))
            pair = pl.ds(2 * chip, 2)
            shape = pulled.shape
            gate_grad = pulled * slope[pair, :, cols].reshape(shape).astype(jnp.float32)
            upper_grad = pulled * gelu[pair, :, cols].reshape(shape).astype(jnp.float32)
            set_pair(slope, chip, cols, gate_grad)
            set_pair(gelu, chip, cols, upper_grad)
            unit_sums[0:1, cols] += jnp.sum(gate_grad, axis=0, keepdims=True)
            unit_sums[1:2, cols] += jnp.sum(upper_grad, axis=0, keepdims=True)

        tiles(slope.shape[2], 256, units)

        def outputs(cols):
            set_pair(
                parts,
                chip,
                cols,
                dot(pair_rows(slope, chip), expand_mat[0, :, cols], ((1,), (0,)))
                + dot(pair_rows(gelu, chip), expand_mat[1, :, cols], ((1,), (0,))),
            )

        tiles(parts.shape[2], 256, outputs)
        pair = pl.ds(2 * chip, 2)
        for index, (source, target) in enumerate(
            ((slope, unit_grads.at[0]), (gelu, unit_grads.at[1]), (blocks, rows_all))
        ):
            copy = pltpu.make_async_copy(
                source.at[pair], target.at[pair], keep_sems.at[chip, index]
            )
            copy.start()
            kept.append(copy)

    plane.run(compute)
    plane.finish(hidden_grad)
    plane.drain()
    for copy in kept:
        copy.wait()


def geglu_backward(wide_count, feed_grad, expand_full, reduce_full, slope, gelu):
    rows, width = feed_grad.shape
    padded = slope.shape[2]
    anywhere = pl.BlockSpec(memory_space=pl.ANY)
    vmem = pl.BlockSpec(memory_space=pltpu.VMEM)
    scratch = exchange_scratch(wide_count, rows, width) + [
        pltpu.VMEM((2, padded, width), jnp.bfloat16),
        pltpu.VMEM((padded, width), jnp.bfloat16),
        pltpu.VMEM((wide_count, rows, padded), jnp.bfloat16),
        pltpu.VMEM((wide_count, rows, padded), jnp.bfloat16),
        pltpu.SemaphoreType.DMA((5,)),
        pltpu.SemaphoreType.DMA((wide_count // 2, 3)),
    ]
    return pl.pallas_call(
        functools.partial(geglu_backward_kernel, wide_count),
        out_shape=(
            jax.ShapeDtypeStruct((wide_count, rows, width), jnp.bfloat16),
            jax.ShapeDtypeStruct((2, wide_count, rows, padded), jnp.bfloat16),
            jax.ShapeDtypeStruct((rows, width), jnp.float32),
            jax.ShapeDtypeStruct((2, padded), jnp.float32),
        ),
        in_specs=[anywhere] * 5,
        out_specs=(anywhere, anywhere, vmem, vmem),
        scratch_shapes=scratch,
        compiler_params=pltpu.CompilerParams(
            collective_id=2, has_side_effects=True, vmem_limit_bytes=kernel_memory
        ),
        cost_estimate=pl.CostEstimate(
            flops=6 * wide_count * rows * padded * width, bytes_accessed=200 * 2**20, transcendentals=0
        ),
        name="geglu_backward",
    )(feed_grad, expand_full, reduce_full, slope, gelu)


class LineExchange:
    def __init__(self, narrow_count):
        self.count = narrow_count
        self.mine = lax.axis_index("narrow")
        self.started = []

    def peer(self, offset):
        return (self.mine + offset) % self.count

    def greet(self, extra=0):
        barrier = pltpu.get_barrier_semaphore()
        for offset in range(1, self.count):
            pl.semaphore_signal(
                barrier,
                inc=1,
                device_id={"narrow": self.peer(offset)},
                device_id_type=pl.DeviceIdType.MESH,
            )
        pl.semaphore_wait(barrier, self.count - 1 + extra)

    def copy(self, source, target, send_sem, recv_sem, where):
        return pltpu.make_async_remote_copy(
            src_ref=source,
            dst_ref=target,
            send_sem=send_sem,
            recv_sem=recv_sem,
            device_id={"narrow": where},
            device_id_type=pl.DeviceIdType.MESH,
        )

    def send(self, offset, source, landing, send_sems, recv_sems):
        peer = self.peer(offset)
        copy = self.copy(
            source, landing.at[self.mine], send_sems.at[offset - 1], recv_sems.at[self.mine], peer
        )
        copy.start()
        self.started.append(copy)

    def arrived(self, offset, landing, send_sems, recv_sems):
        peer = self.peer(offset)
        self.copy(
            landing.at[peer], landing.at[peer], send_sems.at[offset - 1], recv_sems.at[peer], peer
        ).wait_recv()

    def drain(self):
        for copy in self.started:
            copy.wait_send()


def greet_plane(plane):
    barrier = pltpu.get_barrier_semaphore()
    for where in (plane.device(-1), plane.device(1), plane.device(0, True)):
        pl.semaphore_signal(barrier, inc=1, device_id=where, device_id_type=pl.DeviceIdType.MESH)


def rotate_lanes(vectors, cosine, signed_sine):
    return vectors * cosine + pltpu.roll(vectors, vectors.shape[1] // 2, 1) * signed_sine


def attention_backward_kernel(
    wide_count,
    narrow_count,
    attended,
    merge,
    mixed,
    queries,
    keys,
    values,
    probs,
    cosine,
    signed_sine,
    triple,
    merge_grad,
    heads_sums,
    merge_sums,
    upstream,
    outbound,
    probs_held,
    keys_turned,
    key_total,
    value_total,
    merge_out,
    merge_in,
    mixed_send,
    mixed_recv,
    merge_send,
    merge_recv,
    load_sems,
    parts,
    from_mate,
    incoming,
    mate_send,
    mate_recv,
    sum_send,
    sum_recv,
):
    sems = (None, None, mate_send, mate_recv, sum_send, sum_recv, None)
    plane = PlaneExchange(wide_count, None, None, parts, from_mate, incoming, sems)
    line = LineExchange(narrow_count)
    rows, width = attended.shape
    own_cols = queries.shape[1]
    heads = own_cols // HDIM
    scale = HDIM ** (-0.5)

    def load(head):
        return pltpu.make_async_copy(
            probs.at[head], probs_held.at[head % 2], load_sems.at[head % 2]
        )

    load(0).start()
    greet_plane(plane)
    line.greet(3)

    def mixed_part(target, where):
        part = dot(
            attended[...],
            merge[pl.ds(pl.multiple_of(where * own_cols, own_cols), own_cols)],
            ((1,), (1,)),
        )
        target[...] = part.astype(jnp.bfloat16)

    for offset in range(1, narrow_count):
        place = line.peer(offset)
        mixed_part(outbound.at[offset - 1], place)
        line.send(offset, outbound.at[offset - 1], upstream, mixed_send, mixed_recv)
    mixed_part(upstream.at[line.mine], line.mine)

    block = parts.shape[1]

    def merge_rows(i, carry):
        cols = pl.ds(pl.multiple_of(i * block, block), block)
        parts[i] = dot(mixed[:, cols], attended[...], ((0,), (0,))).astype(jnp.bfloat16)
        return carry

    lax.fori_loop(0, wide_count, merge_rows, 0)
    for offset in range(plane.ring):
        plane.share(offset)
    merge_sums[...] = jnp.sum(attended[...].astype(jnp.float32), axis=0, keepdims=True)
    plane.first_sums()
    plane.far_sums()
    for offset in range(1, narrow_count):
        line.arrived(offset, upstream, mixed_send, mixed_recv)

    def one_head(head):
        cols = pl.ds(head * HDIM, HDIM)
        load(head).wait()
        if head + 1 < heads:
            load(head + 1).start()
        held = probs_held.at[head % 2]
        keys_turned[...] = keys[:, cols].astype(jnp.float32).T.astype(jnp.bfloat16)
        key_total[...] = jnp.zeros_like(key_total)
        value_total[...] = jnp.zeros_like(value_total)

        def chunk(i, carry):
            here = pl.ds(pl.multiple_of(i * rows, rows), rows)
            weights_low = held[:, here]
            up = upstream[i, :, cols]
            pulled = dot(values[:, cols], up, ((1,), (1,)))
            weights = weights_low.astype(jnp.float32)
            scaled = weights * pulled
            change = (scaled - weights * jnp.sum(scaled, axis=0, keepdims=True)).astype(
                jnp.bfloat16
            )
            key_total[...] += dot(change, queries[here, cols], ((1,), (0,)))
            value_total[...] += dot(weights_low, up, ((1,), (0,)))
            query_grad = dot(keys_turned[...], change, ((1,), (0,))).T * scale
            triple[here, cols] = rotate_lanes(
                query_grad, cosine[here], signed_sine[here]
            ).astype(jnp.bfloat16)
            return carry

        lax.fori_loop(0, narrow_count, chunk, 0)

        def ending(i, carry):
            here = pl.ds(pl.multiple_of(i * rows, rows), rows)
            triple[here, pl.ds(own_cols + head * HDIM, HDIM)] = rotate_lanes(
                key_total[here] * scale, cosine[here], signed_sine[here]
            ).astype(jnp.bfloat16)
            triple[here, pl.ds(2 * own_cols + head * HDIM, HDIM)] = value_total[here].astype(
                jnp.bfloat16
            )
            return carry

        lax.fori_loop(0, narrow_count, ending, 0)

    for head in range(heads):
        one_head(head)
        if head == heads // 2 - 1:
            plane.last_sums()
    total = merge_out.at[...]
    plane.finish(merge_out)
    count = merge_grad.shape[0]

    def z_rows(where):
        return pl.ds(pl.multiple_of(where * count, count), count)

    for offset in range(1, narrow_count):
        line.send(
            offset, total.at[z_rows(line.peer(offset))], merge_in, merge_send, merge_recv
        )

    def column_sums(cols):
        heads_sums[:, cols] = jnp.sum(
            triple[:, cols].astype(jnp.float32), axis=0, keepdims=True
        )

    tiles(3 * own_cols, 256, column_sums)
    summed = merge_out[z_rows(line.mine)].astype(jnp.float32)
    for offset in range(1, narrow_count):
        line.arrived(offset, merge_in, merge_send, merge_recv)
        summed += merge_in[line.peer(offset)].astype(jnp.float32)
    merge_grad[...] = summed
    line.drain()
    plane.drain()


def attention_backward(
    wide_count,
    narrow_count,
    attended_grad,
    merge_full,
    mixed,
    queries,
    keys,
    values,
    probs,
    cosine,
    signed_sine,
):
    rows, width = attended_grad.shape
    bucket, own_cols = queries.shape
    block = width // wide_count
    count = block // narrow_count
    anywhere = pl.BlockSpec(memory_space=pl.ANY)
    vmem = pl.BlockSpec(memory_space=pltpu.VMEM)
    dma = pltpu.SemaphoreType.DMA
    return pl.pallas_call(
        functools.partial(attention_backward_kernel, wide_count, narrow_count),
        out_shape=(
            jax.ShapeDtypeStruct((bucket, 3 * own_cols), jnp.bfloat16),
            jax.ShapeDtypeStruct((count, width), jnp.float32),
            jax.ShapeDtypeStruct((1, 3 * own_cols), jnp.float32),
            jax.ShapeDtypeStruct((1, width), jnp.float32),
        ),
        in_specs=[vmem] * 6 + [anywhere] + [vmem] * 2,
        out_specs=(vmem, vmem, vmem, vmem),
        scratch_shapes=[
            pltpu.VMEM((narrow_count, rows, own_cols), jnp.bfloat16),
            pltpu.VMEM((narrow_count - 1, rows, own_cols), jnp.bfloat16),
            pltpu.VMEM((2, bucket, bucket), jnp.bfloat16),
            pltpu.VMEM((HDIM, bucket), jnp.bfloat16),
            pltpu.VMEM((bucket, HDIM), jnp.float32),
            pltpu.VMEM((bucket, HDIM), jnp.float32),
            pltpu.VMEM((block, width), jnp.bfloat16),
            pltpu.VMEM((narrow_count, count, width), jnp.bfloat16),
            dma((narrow_count - 1,)),
            dma((narrow_count,)),
            dma((narrow_count - 1,)),
            dma((narrow_count,)),
            dma((2,)),
        ]
        + sum_scratch(wide_count, block, width),
        compiler_params=pltpu.CompilerParams(
            collective_id=3, has_side_effects=True, vmem_limit_bytes=kernel_memory
        ),
        cost_estimate=pl.CostEstimate(
            flops=60 * 10**9, bytes_accessed=200 * 2**20, transcendentals=0
        ),
        name="attention_backward",
    )(
        attended_grad, merge_full, mixed, queries, keys, values, probs, cosine, signed_sine
    )


def input_backward_kernel(
    wide_count,
    narrow_count,
    inputs,
    triple,
    heads_mat,
    small,
    input_part,
    heads_grad,
    small_out,
    line_parts,
    line_in,
    heads_out,
    heads_in,
    small_wide,
    small_sum,
    small_line,
    line_send,
    line_recv,
    heads_send,
    heads_recv,
    wide_send,
    wide_recv,
    small_send,
    small_recv,
    parts,
    from_mate,
    incoming,
    mate_send,
    mate_recv,
    sum_send,
    sum_recv,
):
    sems = (None, None, mate_send, mate_recv, sum_send, sum_recv, None)
    plane = PlaneExchange(wide_count, None, None, parts, from_mate, incoming, sems)
    line = LineExchange(narrow_count)
    rows, width = input_part.shape
    here = line.mine
    last = narrow_count - 1
    place = lax.axis_index("wide")

    def wide_peer(offset):
        return (place + offset) % wide_count

    barrier = pltpu.get_barrier_semaphore()
    for offset in range(1, wide_count):
        pl.semaphore_signal(
            barrier,
            inc=1,
            device_id={"wide": wide_peer(offset)},
            device_id_type=pl.DeviceIdType.MESH,
        )
    line.greet(wide_count - 1)

    def small_copy(offset, source, slot):
        return pltpu.make_async_remote_copy(
            src_ref=source,
            dst_ref=small_wide.at[slot],
            send_sem=wide_send.at[offset - 1],
            recv_sem=wide_recv.at[slot],
            device_id={"wide": wide_peer(offset)},
            device_id_type=pl.DeviceIdType.MESH,
        )

    small_copies = [
        small_copy(offset, small.at[wide_peer(offset)], place) for offset in range(1, wide_count)
    ]
    for copy in small_copies:
        copy.start()

    def input_cols(cols):
        part = dot(triple[...], heads_mat[cols], ((1,), (1,)))
        for index in range(narrow_count):
            line_parts[index, :, cols] = part[index * rows : (index + 1) * rows].astype(
                jnp.bfloat16
            )

    tiles(width, 256, input_cols)

    def line_copy(way, offset):
        target = here + offset if way == 0 else here - offset
        return line.copy(
            line_parts.at[target],
            line_in.at[way, offset - 1],
            line_send.at[way, offset - 1],
            line_recv.at[way, offset - 1],
            here + 1 if way == 0 else here - 1,
        )

    def line_arrived(way, offset):
        landing = line_in.at[way, offset]
        line.copy(
            landing, landing, line_send.at[way, offset], line_recv.at[way, offset], here
        ).wait_recv()

    def add_line(way, offset, slot):
        def chunk(i, carry):
            some = pl.ds(pl.multiple_of(i * 16, 16), 16)
            line_parts[slot, some] = (
                line_parts[slot, some].astype(jnp.float32)
                + line_in[way, offset, some].astype(jnp.float32)
            ).astype(jnp.bfloat16)
            return carry

        lax.fori_loop(0, rows // 16, chunk, 0)

    def line_step(offset):
        for way in range(2):
            reaches = here + offset <= last if way == 0 else here - offset >= 0
            follows = here > 0 if way == 0 else here < last

            @pl.when(reaches)
            def _():
                if offset < last:

                    @pl.when(follows)
                    def _():
                        line_arrived(way, offset)
                        add_line(way, offset, here + offset if way == 0 else here - offset)

                line_copy(way, offset).start()

    line_step(last)

    block = parts.shape[1]

    def heads_rows(i, carry):
        cols = pl.ds(pl.multiple_of(i * block, block), block)
        parts[i] = dot(inputs[:, cols], triple[...], ((0,), (0,))).astype(jnp.bfloat16)
        return carry

    lax.fori_loop(0, wide_count, heads_rows, 0)
    for offset in range(plane.ring):
        plane.share(offset)
    for offset in range(last - 1, last // 2, -1):
        line_step(offset)
    plane.first_sums()
    plane.far_sums()

    for offset in range(1, wide_count):
        peer = wide_peer(offset)
        small_copy(offset, small_wide.at[peer], peer).wait_recv()
    small_wide[place] = small[place]
    total = small_wide[0]
    for index in range(1, wide_count):
        total += small_wide[index]
    small_sum[...] = total
    for offset in range(1, narrow_count):
        line.send(offset, small_sum.at[line.peer(offset)], small_line, small_send, small_recv)

    plane.last_sums()
    for offset in range(last // 2, 0, -1):
        line_step(offset)
    plane.finish(heads_out)
    count = heads_grad.shape[0]

    def z_rows(where):
        return pl.ds(pl.multiple_of(where * count, count), count)

    for offset in range(1, narrow_count):
        line.send(
            offset, heads_out.at[z_rows(line.peer(offset))], heads_in, heads_send, heads_recv
        )
    heads_in[line.mine] = heads_out[z_rows(line.mine)]
    small_line[line.mine] = small_sum[line.mine]
    for offset in range(1, narrow_count):
        line.arrived(offset, small_line, small_send, small_recv)
    result = small_line[0]
    for index in range(1, narrow_count):
        result += small_line[index]
    small_out[...] = result

    def own_rows(i, carry):
        some = pl.ds(pl.multiple_of(i * 16, 16), 16)
        input_part[some] = line_parts[here, some].astype(jnp.float32)
        return carry

    lax.fori_loop(0, rows // 16, own_rows, 0)
    for way in range(2):
        follows = here > 0 if way == 0 else here < last

        @pl.when(follows)
        def _():
            line_arrived(way, 0)

            def chunk(i, carry):
                some = pl.ds(pl.multiple_of(i * 16, 16), 16)
                input_part[some] += line_in[way, 0, some].astype(jnp.float32)
                return carry

            lax.fori_loop(0, rows // 16, chunk, 0)

    for offset in range(1, narrow_count):
        line.arrived(offset, heads_in, heads_send, heads_recv)
    own_cols = triple.shape[1] // 3
    for index in range(narrow_count):
        for which in range(3):
            start = (which * narrow_count + index) * own_cols
            heads_grad[:, start : start + own_cols] = heads_in[
                index, :, which * own_cols : (which + 1) * own_cols
            ].astype(jnp.float32)
    for offset in range(1, narrow_count):
        for way in range(2):
            reaches = here + offset <= last if way == 0 else here - offset >= 0

            @pl.when(reaches)
            def _():
                line_copy(way, offset).wait_send()

    for copy in small_copies:
        copy.wait_send()
    line.drain()
    plane.drain()


def input_backward(wide_count, narrow_count, inputs, triple_grad, heads_mat, small):
    bucket, width = inputs.shape
    rows = bucket // narrow_count
    columns = triple_grad.shape[1]
    block = width // wide_count
    count = block // narrow_count
    vmem = pl.BlockSpec(memory_space=pltpu.VMEM)
    dma = pltpu.SemaphoreType.DMA
    lines = small.shape[2]
    return pl.pallas_call(
        functools.partial(input_backward_kernel, wide_count, narrow_count),
        out_shape=(
            jax.ShapeDtypeStruct((rows, width), jnp.float32),
            jax.ShapeDtypeStruct((count, narrow_count * columns), jnp.float32),
            jax.ShapeDtypeStruct((lines, 128), jnp.float32),
        ),
        in_specs=[vmem] * 4,
        out_specs=(vmem, vmem, vmem),
        scratch_shapes=[
            pltpu.VMEM((narrow_count, rows, width), jnp.bfloat16),
            pltpu.VMEM((2, narrow_count - 1, rows, width), jnp.bfloat16),
            pltpu.VMEM((block, columns), jnp.bfloat16),
            pltpu.VMEM((narrow_count, count, columns), jnp.bfloat16),
            pltpu.VMEM((wide_count, narrow_count, lines, 128), jnp.float32),
            pltpu.VMEM((narrow_count, lines, 128), jnp.float32),
            pltpu.VMEM((narrow_count, lines, 128), jnp.float32),
            dma((2, narrow_count - 1)),
            dma((2, narrow_count - 1)),
            dma((narrow_count - 1,)),
            dma((narrow_count,)),
            dma((wide_count - 1,)),
            dma((wide_count,)),
            dma((narrow_count - 1,)),
            dma((narrow_count,)),
        ]
        + sum_scratch(wide_count, block, columns),
        compiler_params=pltpu.CompilerParams(
            collective_id=4, has_side_effects=True, vmem_limit_bytes=kernel_memory
        ),
        cost_estimate=pl.CostEstimate(
            flops=80 * 10**9, bytes_accessed=200 * 2**20, transcendentals=0
        ),
        name="input_backward",
    )(inputs, triple_grad, heads_mat, small)


def shards(
    layer_input,
    heads_weight,
    heads_bias,
    merge_weight,
    merge_bias,
    norm_gains,
    norm_shifts,
    expand_weight,
    expand_bias,
    reduce_weight,
    reduce_bias,
    joined,
    prefix,
    cotangent,
):
    tok_rows, model_width = layer_input.shape
    wide_count = lax.axis_size("wide")
    narrow_count = lax.axis_size("narrow")
    count = wide_count * narrow_count
    bucket_len = tok_rows * narrow_count
    own_heads = HEADS // narrow_count
    own_cols = own_heads * HDIM
    share = expand_weight.shape[2]
    score_scale = HDIM ** (-0.5)
    joined_flag = joined[0]
    prefix_pair = prefix[0]
    narrow_index = lax.axis_index("narrow")
    positions = jnp.arange(bucket_len, dtype=jnp.int32)
    second_seq, local_pos, prefix_len = layout(positions, joined_flag, prefix_pair, bucket_len)
    cosine, sine_table = rotary_tables(local_pos, HDIM)
    key_mask = visible(positions, positions, joined_flag, prefix_pair, bucket_len)

    rows_input = lax.all_gather(layer_input, "narrow", axis=0, tiled=True)
    swapped = lax.all_to_all(
        heads_weight.reshape(-1, 3, narrow_count, own_cols).transpose(2, 0, 1, 3),
        "narrow",
        split_axis=0,
        concat_axis=0,
        tiled=True,
    ).reshape(-1, 3 * own_cols)
    heads_mat = lax.all_gather(swapped, "wide", axis=0, tiled=True)
    heads_shift, merge_shift, gains, shifts, expand_shift, reduce_shift = gather_small(
        heads_bias, merge_bias, norm_gains, norm_shifts, expand_bias, reduce_bias
    )
    merge_full = lax.all_gather(merge_weight, both_axes, axis=0, tiled=True)
    own_shift = lax.dynamic_index_in_dim(
        heads_shift.reshape(3, narrow_count, own_cols), narrow_index, 1, keepdims=False
    ).reshape(-1)
    triple = dot(rows_input, heads_mat, ((1,), (0,))) + own_shift
    triple = triple.reshape(bucket_len, 3, own_heads, HDIM)
    queries = low(rotate(triple[:, 0], cosine, sine_table))
    keys = low(rotate(triple[:, 1], cosine, sine_table))
    values = low(triple[:, 2])
    scores = (
        jnp.einsum("kgd,qgd->gkq", keys, queries, preferred_element_type=jnp.float32) * score_scale
    )
    scores = jnp.where(key_mask.T[None], scores, masked_value)
    expo = jnp.exp(scores - jnp.max(scores, axis=1, keepdims=True))
    probs_low = low(expo / jnp.sum(expo, axis=1, keepdims=True))
    mixed_own = low(
        jnp.einsum("gkq,kgd->qgd", probs_low, values, preferred_element_type=jnp.float32)
    ).reshape(bucket_len, own_cols)
    mixed = lax.all_to_all(mixed_own, "narrow", split_axis=0, concat_axis=1, tiled=True)
    attended = dot(mixed, merge_full, ((1,), (0,))) + merge_shift
    hidden, normed_one, inv_one = normalize(
        residual_scale * layer_input.astype(jnp.float32) + attended, gains[0], shifts[0]
    )
    hidden_low = low(hidden)

    tile_rows = -share % 16
    padded = -(-share // 256) * 256
    expand_full = lax.all_gather(
        jnp.pad(expand_weight.transpose(1, 2, 0), ((0, 0), (0, tile_rows), (0, 0))),
        "narrow",
        axis=2,
        tiled=True,
    )
    reduce_full = lax.all_gather(
        jnp.pad(reduce_weight, ((0, tile_rows), (0, 0))), "narrow", axis=1, tiled=True
    )
    rows_all, active, slope, gelu, feed_sum = geglu_forward(
        wide_count,
        hidden_low,
        expand_full,
        reduce_full,
        jnp.pad(expand_shift, ((0, 0), (0, padded - share))),
    )
    feed = feed_sum + reduce_shift
    output_float, normed_two, inv_two = normalize(
        residual_scale * hidden + feed, gains[1], shifts[1]
    )
    layer_output = low(output_float)

    grad_out = cotangent.astype(jnp.float32)
    gain_two_grad = jnp.sum(grad_out * normed_two, axis=0)
    shift_two_grad = jnp.sum(grad_out, axis=0)
    sum_two_grad = normalize_back(grad_out, normed_two, inv_two, gains[1])
    feed_grad = low(sum_two_grad)
    feed_grads_all, unit_grads, hidden_part, unit_sums = geglu_backward(
        wide_count, feed_grad, expand_full, reduce_full, slope, gelu
    )
    tokens_all = wide_count * tok_rows
    rows_all = rows_all.reshape(tokens_all, model_width)
    feed_grads_all = feed_grads_all.reshape(tokens_all, model_width)
    unit_grads = unit_grads.reshape(2, tokens_all, padded)
    reduce_part = low(dot(active.reshape(tokens_all, padded), feed_grads_all, ((0,), (0,))))[:share]
    expand_part = low(dot(unit_grads, rows_all, ((1,), (0,))))[:, :share]
    reduce_part, expand_part, hidden_part = lax.optimization_barrier(
        (reduce_part, expand_part, hidden_part)
    )
    reduce_weight_gradient = lax.psum_scatter(
        reduce_part, "narrow", scatter_dimension=1, tiled=True
    ).astype(jnp.float32)
    expand_weight_gradient = (
        lax.psum_scatter(expand_part, "narrow", scatter_dimension=2, tiled=True)
        .astype(jnp.float32)
        .transpose(2, 0, 1)
    )
    hidden_grad = residual_scale * sum_two_grad + hidden_part
    gain_one_grad = jnp.sum(hidden_grad * normed_one, axis=0)
    shift_one_grad = jnp.sum(hidden_grad, axis=0)
    sum_one_grad = normalize_back(hidden_grad, normed_one, inv_one, gains[0])
    attended_grad = low(sum_one_grad)
    triple_grad, merge_weight_gradient, heads_sums, merge_sums = attention_backward(
        wide_count,
        narrow_count,
        attended_grad,
        merge_full,
        mixed,
        queries.reshape(bucket_len, own_cols),
        keys.reshape(bucket_len, own_cols),
        values.reshape(bucket_len, own_cols),
        probs_low,
        jnp.concatenate([cosine[:, 0], cosine[:, 0]], axis=1),
        jnp.concatenate([sine_table[:, 0], -sine_table[:, 0]], axis=1),
    )

    mine_narrow = (jnp.arange(narrow_count) == narrow_index).astype(jnp.float32)
    mine_wide = (jnp.arange(wide_count) == lax.axis_index("wide")).astype(jnp.float32)
    heads_sums = heads_sums.reshape(3, 1, own_cols)
    heads_sums = (heads_sums * mine_narrow[None, :, None]).reshape(count, -1)
    merge_sums = merge_sums.reshape(count, -1)
    norm_sums = (
        jnp.stack([gain_one_grad, gain_two_grad, shift_one_grad, shift_two_grad])
        .reshape(4, count, -1)
        .transpose(1, 0, 2)
        .reshape(count, -1)
    )
    expand_sums = unit_sums[:, :share]
    expand_sums = (
        expand_sums.reshape(2, narrow_count, -1).transpose(1, 0, 2).reshape(1, narrow_count, -1)
        * mine_wide[:, None, None]
    ).reshape(count, -1)
    reduce_sums = jnp.sum(feed_grad, axis=0, dtype=jnp.float32).reshape(1, narrow_count, -1)
    reduce_sums = jnp.broadcast_to(
        reduce_sums, (wide_count, narrow_count, reduce_sums.shape[2])
    ).reshape(count, -1)
    pieces = (heads_sums, merge_sums, norm_sums, expand_sums, reduce_sums)
    packed = jnp.concatenate(pieces, axis=1)
    packed = jnp.pad(packed, ((0, 0), (0, -packed.shape[1] % 1024)))
    input_part, heads_weight_gradient, summed = input_backward(
        wide_count,
        narrow_count,
        rows_input,
        triple_grad,
        heads_mat,
        packed.reshape(wide_count, narrow_count, -1, 128),
    )
    input_gradient = residual_scale * sum_one_grad + input_part
    summed = summed.reshape(-1)
    ends = []
    start = 0
    for piece in pieces:
        ends.append(summed[start : start + piece.shape[1]])
        start += piece.shape[1]
    norm_ends = ends[2].reshape(4, -1)
    return (
        layer_output,
        input_gradient,
        heads_weight_gradient,
        ends[0],
        merge_weight_gradient,
        ends[1],
        norm_ends[:2],
        norm_ends[2:],
        expand_weight_gradient,
        ends[3].reshape(2, -1),
        reduce_weight_gradient,
        ends[4],
    )


def solution(mesh):
    return jax.shard_map(
        shards,
        mesh=mesh,
        in_specs=(
            P(("wide", "narrow"), None),
            P(("wide", "narrow"), None),
            P(("wide", "narrow")),
            P(("wide", "narrow"), None),
            P(("wide", "narrow")),
            P(None, ("wide", "narrow")),
            P(None, ("wide", "narrow")),
            P("narrow", None, "wide"),
            P(None, ("wide", "narrow")),
            P("wide", "narrow"),
            P("narrow"),
            P("wide"),
            P("wide", None),
            P(("wide", "narrow"), None),
        ),
        out_specs=(
            P(("wide", "narrow"), None),
            P(("wide", "narrow"), None),
            P(("wide", "narrow"), None),
            P(("wide", "narrow")),
            P(("wide", "narrow"), None),
            P(("wide", "narrow")),
            P(None, ("wide", "narrow")),
            P(None, ("wide", "narrow")),
            P("narrow", None, "wide"),
            P(None, ("wide", "narrow")),
            P("wide", "narrow"),
            P("narrow"),
        ),
        check_vma=False,
    )
```

```python
import functools
import math

import jax
import jax.numpy as jnp
from jax import lax
from jax.experimental import pallas as pl
from jax.experimental.pallas import tpu as pltpu
from jax.sharding import PartitionSpec as P

HEADS = 16
HDIM = 128


residual_scale = 48.0**0.5
norm_eps = 1e-05
masked_value = -1e30
kernel_memory = 60 * 2**20


def layout(positions, joined_flag, prefix_pair, bucket_len):
    halfway = bucket_len // 2
    second_seq = (positions >= halfway).astype(jnp.int32) * (1 - joined_flag)
    local_pos = positions - second_seq * halfway
    prefix_len = jnp.where(
        joined_flag == 1,
        prefix_pair[0] + prefix_pair[1],
        jnp.where(second_seq == 1, prefix_pair[1], prefix_pair[0]),
    )
    return (second_seq, local_pos, prefix_len)


def rotary_tables(local_pos, head_size):
    halfway = head_size // 2
    inverse = 10000.0 ** (-(2.0 * jnp.arange(halfway).astype(jnp.float32)) / head_size)
    angles = local_pos.astype(jnp.float32)[:, None] * inverse[None, :]
    return (jnp.cos(angles), jnp.sin(angles))


def normalize(values, gain, shift):
    centre = jnp.mean(values, axis=-1, keepdims=True)
    centred = values - centre
    variance = jnp.mean(centred * centred, axis=-1, keepdims=True)
    inv_std = lax.rsqrt(variance + norm_eps)
    normed = centred * inv_std
    return (normed * gain + shift, normed, inv_std)


def normalize_back(upstream, normed, inv_std, gain):
    scaled = upstream * gain
    return inv_std * (
        scaled
        - jnp.mean(scaled, axis=-1, keepdims=True)
        - normed * jnp.mean(scaled * normed, axis=-1, keepdims=True)
    )


def dot(left, right, dims):
    return lax.dot_general(left, right, (dims, ((), ())), preferred_element_type=jnp.float32)


def low(values):
    return values.astype(jnp.bfloat16)


def pack_small(parts):
    packed = jnp.concatenate([part.reshape(-1) for part in parts])
    return jnp.pad(packed, (0, -packed.size % 2048)).reshape(-1, 128)


def unpack_small(everyone, parts):
    wide_count, narrow_count = everyone.shape[:2]
    everyone = everyone.reshape(wide_count, narrow_count, -1).astype(jnp.float32)
    pieces = []
    start = 0
    for part in parts:
        pieces.append(everyone[:, :, start : start + part.size])
        start += part.size

    def pairs(piece):
        piece = piece.reshape(-1, 2, piece.shape[-1] // 2)
        return piece.transpose(1, 0, 2).reshape(2, -1)

    own_expand = lax.dynamic_index_in_dim(
        pieces[4], lax.axis_index("wide"), 0, keepdims=False
    )
    return (
        pieces[0].reshape(-1),
        pieces[1].reshape(-1),
        pairs(pieces[2]),
        pairs(pieces[3]),
        pairs(own_expand),
        pieces[5][0].reshape(-1),
    )


def ring_place(wide_count):
    ring = wide_count // 2
    mine = lax.axis_index("wide")
    chip = mine // 2
    core = mine % 2
    position = 2 * (chip // 2) + (chip % 2 + chip // 2) % 2
    return ring, position, core


def chip_at(position, ring):
    position = (position + 2 * ring) % ring
    return 2 * (position // 2) + (position + position // 2) % 2


class PlaneExchange:
    def __init__(self, wide_count, own, blocks, parts, from_mate, incoming, sems):
        self.ring, self.position, self.core = ring_place(wide_count)
        self.own, self.blocks, self.parts = own, blocks, parts
        self.from_mate, self.incoming = from_mate, incoming
        (
            self.gather_send,
            self.gather_recv,
            self.mate_send,
            self.mate_recv,
            self.sum_send,
            self.sum_recv,
            self.own_sem,
        ) = sems
        self.half = parts.shape[1] // 2
        self.far = self.ring // 2
        self.started = []

    def device(self, offset, mate=False):
        core = 1 - self.core if mate else self.core
        return {"wide": 2 * chip_at(self.position + offset, self.ring) + core}

    def slot(self, offset, mate=False):
        core = 1 - self.core if mate else self.core
        return 2 * chip_at(self.position + offset, self.ring) + core

    def rows(self, part):
        return pl.ds(part * self.half, self.half)

    def greet(self):
        barrier = pltpu.get_barrier_semaphore()
        for where in (self.device(-1), self.device(1), self.device(0, True)):
            pl.semaphore_signal(
                barrier, inc=1, device_id=where, device_id_type=pl.DeviceIdType.MESH
            )
        pl.semaphore_wait(barrier, 3)

    def start(self, source, target, send_sem, recv_sem, where):
        copy = pltpu.make_async_remote_copy(
            src_ref=source,
            dst_ref=target,
            send_sem=send_sem,
            recv_sem=recv_sem,
            device_id=where,
            device_id_type=pl.DeviceIdType.MESH,
        )
        copy.start()
        self.started.append(copy)

    def pass_on(self, lane, slot, part, where, source=None):
        target = self.blocks.at[slot, self.rows(part)]
        self.start(
            target if source is None else source,
            target,
            self.gather_send.at[lane, slot, part],
            self.gather_recv.at[slot, part],
            where,
        )

    def arrived(self, slot, part):
        target = self.blocks.at[slot, self.rows(part)]
        pltpu.make_async_remote_copy(
            src_ref=target,
            dst_ref=target,
            send_sem=self.gather_send.at[0, slot, part],
            recv_sem=self.gather_recv.at[slot, part],
            device_id=self.device(1),
            device_id_type=pl.DeviceIdType.MESH,
        ).wait_recv()

    def send_own(self):
        slot = self.slot(0)
        keep = None
        own = self.blocks.at[slot]
        if self.own is not None:
            own = self.own
            keep = pltpu.make_async_copy(own, self.blocks.at[slot], self.own_sem)
            keep.start()
        first, second = own.at[self.rows(0)], own.at[self.rows(1)]
        self.pass_on(0, slot, 0, self.device(1), first)
        self.pass_on(1, slot, 1, self.device(-1), second)
        self.pass_on(2, slot, 0, self.device(0, True), first)
        self.pass_on(2, slot, 1, self.device(0, True), second)
        self.pass_on(0, slot, 1, self.device(1), second)
        self.pass_on(1, slot, 0, self.device(-1), first)
        return keep

    def receive(self, distance):
        mate = self.device(0, True)
        left, right = self.slot(-distance), self.slot(distance)
        if distance == self.far:
            for part in range(2):
                self.arrived(left, part)
                self.pass_on(2, left, part, mate)
            return
        further = distance < self.far - 1
        self.arrived(left, 0)
        self.pass_on(0, left, 0, self.device(1))
        self.pass_on(2, left, 0, mate)
        self.arrived(right, 1)
        self.pass_on(1, right, 1, self.device(-1))
        self.pass_on(2, right, 1, mate)
        self.arrived(left, 1)
        if further:
            self.pass_on(0, left, 1, self.device(1))
        self.pass_on(2, left, 1, mate)
        self.arrived(right, 0)
        if further:
            self.pass_on(1, right, 0, self.device(-1))
        self.pass_on(2, right, 0, mate)

    def receive_mate(self, offset):
        for part in range(2):
            self.arrived(self.slot(offset, True), part)

    def share(self, offset):
        chip = chip_at(self.position + offset, self.ring)
        self.start(
            self.parts.at[self.slot(offset, True)],
            self.from_mate.at[chip],
            self.mate_send.at[chip],
            self.mate_recv.at[chip],
            self.device(0, True),
        )

    def shared(self, offset):
        chip = chip_at(self.position + offset, self.ring)
        pltpu.make_async_remote_copy(
            src_ref=self.parts.at[self.slot(offset)],
            dst_ref=self.from_mate.at[chip],
            send_sem=self.mate_send.at[chip],
            recv_sem=self.mate_recv.at[chip],
            device_id=self.device(0, True),
            device_id_type=pl.DeviceIdType.MESH,
        ).wait_recv()

    def chip_sum(self, offset, rows):
        chip = chip_at(self.position + offset, self.ring)
        return self.parts[self.slot(offset), rows].astype(jnp.float32) + self.from_mate[
            chip, rows
        ].astype(jnp.float32)

    def send_sum(self, way, distance, part):
        offset = distance if way == 0 else -distance
        begins = self.far if part == way else self.far - 1
        slot = self.slot(offset)
        if distance < begins:
            self.sum_arrived(way, distance, part)

        def chunk(i, carry):
            here = pl.ds(pl.multiple_of(i * 16, 16), 16)
            there = pl.ds(pl.multiple_of(part * self.half + i * 16, 16), 16)
            total = self.chip_sum(offset, there)
            if distance < begins:
                total += self.incoming[way, distance, part, here].astype(jnp.float32)
            self.parts[slot, there] = total.astype(jnp.bfloat16)
            return carry

        lax.fori_loop(0, self.half // 16, chunk, 0)
        self.start(
            self.parts.at[slot, self.rows(part)],
            self.incoming.at[way, distance - 1, part],
            self.sum_send.at[way, distance - 1, part],
            self.sum_recv.at[way, distance - 1, part],
            self.device(1 if way == 0 else -1),
        )

    def sum_arrived(self, way, distance, part):
        target = self.incoming.at[way, distance, part]
        pltpu.make_async_remote_copy(
            src_ref=target,
            dst_ref=target,
            send_sem=self.sum_send.at[way, distance, part],
            recv_sem=self.sum_recv.at[way, distance, part],
            device_id=self.device(1),
            device_id_type=pl.DeviceIdType.MESH,
        ).wait_recv()

    def run(self, compute):
        keep = self.send_own()
        keep.wait()
        self.receive_mate(0)
        compute(chip_at(self.position, self.ring))
        self.share(0)
        for distance in range(1, self.far):
            self.receive(distance)
            for offset in (-distance, distance):
                self.receive_mate(offset)
                compute(chip_at(self.position + offset, self.ring))
                self.share(offset)
            if distance == self.far - 1:
                self.first_sums()
        self.receive(self.far)
        self.receive_mate(self.far)
        compute(chip_at(self.position + self.far, self.ring))
        self.share(self.far)
        self.far_sums()
        self.last_sums()

    def first_sums(self):
        distance = self.far - 1
        self.shared(distance)
        self.send_sum(0, distance, 1)
        self.shared(-distance)
        self.send_sum(1, distance, 0)

    def far_sums(self):
        self.shared(self.far)
        self.send_sum(0, self.far, 0)
        self.send_sum(1, self.far, 1)

    def last_sums(self):
        for distance in range(self.far - 1, 0, -1):
            if distance < self.far - 1:
                self.shared(distance)
                self.shared(-distance)
            self.send_sum(0, distance, 0)
            self.send_sum(1, distance, 1)
            if distance < self.far - 1:
                self.send_sum(0, distance, 1)
                self.send_sum(1, distance, 0)

    def finish(self, result):
        self.shared(0)
        for part in range(2):
            for way in range(2):
                self.sum_arrived(way, 0, part)

            def chunk(i, carry):
                here = pl.ds(pl.multiple_of(i * 16, 16), 16)
                there = pl.ds(pl.multiple_of(part * self.half + i * 16, 16), 16)
                total = self.chip_sum(0, there)
                for way in range(2):
                    total += self.incoming[way, 0, part, here].astype(jnp.float32)
                result[there] = total.astype(result.dtype)
                return carry

            lax.fori_loop(0, self.half // 16, chunk, 0)

    def drain(self):
        for copy in self.started:
            copy.wait_send()


def sum_scratch(wide_count, rows, width):
    ring = wide_count // 2
    far = ring // 2
    dma = pltpu.SemaphoreType.DMA
    return [
        pltpu.VMEM((wide_count, rows, width), jnp.bfloat16),
        pltpu.VMEM((ring, rows, width), jnp.bfloat16),
        pltpu.VMEM((2, far, 2, rows // 2, width), jnp.bfloat16),
        dma((ring,)),
        dma((ring,)),
        dma((2, far, 2)),
        dma((2, far, 2)),
    ]


def exchange_scratch(wide_count, rows, width):
    dma = pltpu.SemaphoreType.DMA
    return [
        pltpu.VMEM((wide_count, rows, width), jnp.bfloat16),
        dma((3, wide_count, 2)),
        dma((wide_count, 2)),
        dma(()),
    ] + sum_scratch(wide_count, rows, width)


def load_padded(source, target, sem):
    filled = source.shape[0]
    copy = pltpu.make_async_copy(source, target.at[pl.ds(0, filled)], sem)
    copy.start()
    if filled < target.shape[0]:
        target[pl.ds(filled, target.shape[0] - filled)] = jnp.zeros(
            (target.shape[0] - filled, target.shape[1]), target.dtype
        )
    return copy


def pair_rows(ref, chip):
    block = ref[pl.ds(2 * chip, 2)]
    return block.reshape(2 * block.shape[1], block.shape[2])


def set_pair(ref, chip, cols, value):
    rows = ref.shape[1]
    ref[2 * chip, :, cols] = value[:rows].astype(ref.dtype)
    ref[2 * chip + 1, :, cols] = value[rows:].astype(ref.dtype)


def tiles(count, tile, body):
    def step(i, carry):
        body(pl.ds(pl.multiple_of(i * tile, tile), tile))
        return carry

    lax.fori_loop(0, count // tile, step, 0)


def geglu_forward_kernel(
    wide_count,
    own,
    expand,
    reduce,
    shift,
    rows_all,
    active_out,
    slope_out,
    gelu_out,
    feed,
    blocks,
    gather_send,
    gather_recv,
    own_sem,
    parts,
    from_mate,
    incoming,
    mate_send,
    mate_recv,
    sum_send,
    sum_recv,
    expand_mat,
    reduce_mat,
    active,
    slope,
    gelu,
    load_sems,
    keep_sems,
):
    sems = (gather_send, gather_recv, mate_send, mate_recv, sum_send, sum_recv, own_sem)
    plane = PlaneExchange(wide_count, own, blocks, parts, from_mate, incoming, sems)
    loads = [
        load_padded(expand.at[0], expand_mat.at[0], load_sems.at[0]),
        load_padded(expand.at[1], expand_mat.at[1], load_sems.at[1]),
        load_padded(reduce, reduce_mat, load_sems.at[2]),
    ]
    plane.greet()
    kept = []
    waiting = list(loads)

    def compute(chip):
        while waiting:
            waiting.pop().wait()

        def units(cols):
            rows = pair_rows(blocks, chip)
            gate = dot(rows, expand_mat[0, cols], ((1,), (1,))) + shift[0:1, cols]
            upper = dot(rows, expand_mat[1, cols], ((1,), (1,))) + shift[1:2, cols]
            factor = math.sqrt(2 / math.pi)
            square = gate * gate
            bend = jnp.tanh(factor * gate * (1 + 0.044715 * square))
            value = 0.5 * gate * (1 + bend)
            pull = 0.5 * (1 + bend) + 0.5 * gate * (1 - bend * bend) * factor * (
                1 + 3 * 0.044715 * square
            )
            set_pair(active, chip, cols, value * upper)
            set_pair(slope, chip, cols, pull * upper)
            set_pair(gelu, chip, cols, value)

        tiles(active.shape[2], 256, units)

        def outputs(cols):
            set_pair(
                parts, chip, cols, dot(pair_rows(active, chip), reduce_mat[:, cols], ((1,), (0,)))
            )

        tiles(parts.shape[2], 256, outputs)
        pair = pl.ds(2 * chip, 2)
        for index, (source, target) in enumerate(
            ((active, active_out), (slope, slope_out), (gelu, gelu_out), (blocks, rows_all))
        ):
            copy = pltpu.make_async_copy(
                source.at[pair], target.at[pair], keep_sems.at[chip, index]
            )
            copy.start()
            kept.append(copy)

    plane.run(compute)
    plane.finish(feed)
    plane.drain()
    for copy in kept:
        copy.wait()


def geglu_forward(wide_count, hidden_low, expand_full, reduce_full, shift):
    rows, width = hidden_low.shape
    padded = shift.shape[1]
    anywhere = pl.BlockSpec(memory_space=pl.ANY)
    vmem = pl.BlockSpec(memory_space=pltpu.VMEM)
    kept = jax.ShapeDtypeStruct((wide_count, rows, padded), jnp.bfloat16)
    scratch = exchange_scratch(wide_count, rows, width) + [
        pltpu.VMEM((2, padded, width), jnp.bfloat16),
        pltpu.VMEM((padded, width), jnp.bfloat16),
        pltpu.VMEM((wide_count, rows, padded), jnp.bfloat16),
        pltpu.VMEM((wide_count, rows, padded), jnp.bfloat16),
        pltpu.VMEM((wide_count, rows, padded), jnp.bfloat16),
        pltpu.SemaphoreType.DMA((3,)),
        pltpu.SemaphoreType.DMA((wide_count // 2, 4)),
    ]
    return pl.pallas_call(
        functools.partial(geglu_forward_kernel, wide_count),
        out_shape=(
            jax.ShapeDtypeStruct((wide_count, rows, width), jnp.bfloat16),
            kept,
            kept,
            kept,
            jax.ShapeDtypeStruct((rows, width), jnp.float32),
        ),
        in_specs=[anywhere, anywhere, anywhere, vmem],
        out_specs=(anywhere, anywhere, anywhere, anywhere, vmem),
        scratch_shapes=scratch,
        compiler_params=pltpu.CompilerParams(
            collective_id=1, has_side_effects=True, vmem_limit_bytes=kernel_memory
        ),
        cost_estimate=pl.CostEstimate(
            flops=6 * wide_count * rows * padded * width, bytes_accessed=200 * 2**20, transcendentals=0
        ),
        name="geglu_forward",
    )(hidden_low, expand_full, reduce_full, shift)


def geglu_backward_kernel(
    wide_count,
    own,
    expand,
    reduce,
    slope_in,
    gelu_in,
    rows_all,
    unit_grads,
    hidden_grad,
    unit_sums,
    blocks,
    gather_send,
    gather_recv,
    own_sem,
    parts,
    from_mate,
    incoming,
    mate_send,
    mate_recv,
    sum_send,
    sum_recv,
    expand_mat,
    reduce_mat,
    slope,
    gelu,
    load_sems,
    keep_sems,
):
    sems = (gather_send, gather_recv, mate_send, mate_recv, sum_send, sum_recv, own_sem)
    plane = PlaneExchange(wide_count, own, blocks, parts, from_mate, incoming, sems)
    loads = [
        load_padded(expand.at[0], expand_mat.at[0], load_sems.at[0]),
        load_padded(expand.at[1], expand_mat.at[1], load_sems.at[1]),
        load_padded(reduce, reduce_mat, load_sems.at[2]),
        pltpu.make_async_copy(slope_in, slope, load_sems.at[3]),
        pltpu.make_async_copy(gelu_in, gelu, load_sems.at[4]),
    ]
    for copy in loads[3:]:
        copy.start()
    unit_sums[...] = jnp.zeros_like(unit_sums)
    plane.greet()
    kept = []
    waiting = list(loads)

    def compute(chip):
        while waiting:
            waiting.pop().wait()

        def units(cols):
            pulled = dot(pair_rows(blocks, chip), reduce_mat[cols], ((1,), (1,)))
            pair = pl.ds(2 * chip, 2)
            shape = pulled.shape
            gate_grad = pulled * slope[pair, :, cols].reshape(shape).astype(jnp.float32)
            upper_grad = pulled * gelu[pair, :, cols].reshape(shape).astype(jnp.float32)
            set_pair(slope, chip, cols, gate_grad)
            set_pair(gelu, chip, cols, upper_grad)
            unit_sums[0:1, cols] += jnp.sum(gate_grad, axis=0, keepdims=True)
            unit_sums[1:2, cols] += jnp.sum(upper_grad, axis=0, keepdims=True)

        tiles(slope.shape[2], 256, units)

        def outputs(cols):
            set_pair(
                parts,
                chip,
                cols,
                dot(pair_rows(slope, chip), expand_mat[0, :, cols], ((1,), (0,)))
                + dot(pair_rows(gelu, chip), expand_mat[1, :, cols], ((1,), (0,))),
            )

        tiles(parts.shape[2], 256, outputs)
        pair = pl.ds(2 * chip, 2)
        for index, (source, target) in enumerate(
            ((slope, unit_grads.at[0]), (gelu, unit_grads.at[1]), (blocks, rows_all))
        ):
            copy = pltpu.make_async_copy(
                source.at[pair], target.at[pair], keep_sems.at[chip, index]
            )
            copy.start()
            kept.append(copy)

    plane.run(compute)
    plane.finish(hidden_grad)
    plane.drain()
    for copy in kept:
        copy.wait()


def geglu_backward(wide_count, feed_grad, expand_full, reduce_full, slope, gelu):
    rows, width = feed_grad.shape
    padded = slope.shape[2]
    anywhere = pl.BlockSpec(memory_space=pl.ANY)
    vmem = pl.BlockSpec(memory_space=pltpu.VMEM)
    scratch = exchange_scratch(wide_count, rows, width) + [
        pltpu.VMEM((2, padded, width), jnp.bfloat16),
        pltpu.VMEM((padded, width), jnp.bfloat16),
        pltpu.VMEM((wide_count, rows, padded), jnp.bfloat16),
        pltpu.VMEM((wide_count, rows, padded), jnp.bfloat16),
        pltpu.SemaphoreType.DMA((5,)),
        pltpu.SemaphoreType.DMA((wide_count // 2, 3)),
    ]
    return pl.pallas_call(
        functools.partial(geglu_backward_kernel, wide_count),
        out_shape=(
            jax.ShapeDtypeStruct((wide_count, rows, width), jnp.bfloat16),
            jax.ShapeDtypeStruct((2, wide_count, rows, padded), jnp.bfloat16),
            jax.ShapeDtypeStruct((rows, width), jnp.float32),
            jax.ShapeDtypeStruct((2, padded), jnp.float32),
        ),
        in_specs=[anywhere] * 5,
        out_specs=(anywhere, anywhere, vmem, vmem),
        scratch_shapes=scratch,
        compiler_params=pltpu.CompilerParams(
            collective_id=2, has_side_effects=True, vmem_limit_bytes=kernel_memory
        ),
        cost_estimate=pl.CostEstimate(
            flops=6 * wide_count * rows * padded * width, bytes_accessed=200 * 2**20, transcendentals=0
        ),
        name="geglu_backward",
    )(feed_grad, expand_full, reduce_full, slope, gelu)


class LineExchange:
    def __init__(self, narrow_count):
        self.count = narrow_count
        self.mine = lax.axis_index("narrow")
        self.started = []

    def peer(self, offset):
        return (self.mine + offset) % self.count

    def greet(self, extra=0):
        barrier = pltpu.get_barrier_semaphore()
        for offset in range(1, self.count):
            pl.semaphore_signal(
                barrier,
                inc=1,
                device_id={"narrow": self.peer(offset)},
                device_id_type=pl.DeviceIdType.MESH,
            )
        pl.semaphore_wait(barrier, self.count - 1 + extra)

    def copy(self, source, target, send_sem, recv_sem, where):
        return pltpu.make_async_remote_copy(
            src_ref=source,
            dst_ref=target,
            send_sem=send_sem,
            recv_sem=recv_sem,
            device_id={"narrow": where},
            device_id_type=pl.DeviceIdType.MESH,
        )

    def send(self, offset, source, landing, send_sems, recv_sems):
        peer = self.peer(offset)
        copy = self.copy(
            source, landing.at[self.mine], send_sems.at[offset - 1], recv_sems.at[self.mine], peer
        )
        copy.start()
        self.started.append(copy)

    def arrived(self, offset, landing, send_sems, recv_sems):
        peer = self.peer(offset)
        self.copy(
            landing.at[peer], landing.at[peer], send_sems.at[offset - 1], recv_sems.at[peer], peer
        ).wait_recv()

    def drain(self):
        for copy in self.started:
            copy.wait_send()


def greet_plane(plane):
    barrier = pltpu.get_barrier_semaphore()
    for where in (plane.device(-1), plane.device(1), plane.device(0, True)):
        pl.semaphore_signal(barrier, inc=1, device_id=where, device_id_type=pl.DeviceIdType.MESH)


def rotate_lanes(vectors, cosine, signed_sine):
    return vectors * cosine + pltpu.roll(vectors, vectors.shape[1] // 2, 1) * signed_sine


def attention_backward_kernel(
    wide_count,
    narrow_count,
    attended,
    merge,
    mixed,
    queries,
    keys,
    values,
    probs,
    cosine,
    signed_sine,
    triple,
    merge_grad,
    heads_sums,
    merge_sums,
    upstream,
    outbound,
    probs_held,
    keys_turned,
    key_total,
    value_total,
    merge_out,
    merge_in,
    mixed_send,
    mixed_recv,
    merge_send,
    merge_recv,
    load_sems,
    parts,
    from_mate,
    incoming,
    mate_send,
    mate_recv,
    sum_send,
    sum_recv,
):
    sems = (None, None, mate_send, mate_recv, sum_send, sum_recv, None)
    plane = PlaneExchange(wide_count, None, None, parts, from_mate, incoming, sems)
    line = LineExchange(narrow_count)
    rows, width = attended.shape
    own_cols = queries.shape[1]
    heads = own_cols // HDIM
    scale = HDIM ** (-0.5)

    def load(head):
        return pltpu.make_async_copy(
            probs.at[head], probs_held.at[head % 2], load_sems.at[head % 2]
        )

    load(0).start()
    greet_plane(plane)
    line.greet(3)

    def mixed_part(target, where):
        part = dot(
            attended[...],
            merge[pl.ds(pl.multiple_of(where * own_cols, own_cols), own_cols)],
            ((1,), (1,)),
        )
        target[...] = part.astype(jnp.bfloat16)

    for offset in range(1, narrow_count):
        place = line.peer(offset)
        mixed_part(outbound.at[offset - 1], place)
        line.send(offset, outbound.at[offset - 1], upstream, mixed_send, mixed_recv)
    mixed_part(upstream.at[line.mine], line.mine)

    block = parts.shape[1]

    def merge_rows(i, carry):
        cols = pl.ds(pl.multiple_of(i * block, block), block)
        parts[i] = dot(mixed[:, cols], attended[...], ((0,), (0,))).astype(jnp.bfloat16)
        return carry

    lax.fori_loop(0, wide_count, merge_rows, 0)
    for offset in range(plane.ring):
        plane.share(offset)
    merge_sums[...] = jnp.sum(attended[...].astype(jnp.float32), axis=0, keepdims=True)
    plane.first_sums()
    plane.far_sums()
    for offset in range(1, narrow_count):
        line.arrived(offset, upstream, mixed_send, mixed_recv)

    def one_head(head):
        cols = pl.ds(head * HDIM, HDIM)
        load(head).wait()
        if head + 1 < heads:
            load(head + 1).start()
        held = probs_held.at[head % 2]
        keys_turned[...] = keys[:, cols].astype(jnp.float32).T.astype(jnp.bfloat16)
        key_total[...] = jnp.zeros_like(key_total)
        value_total[...] = jnp.zeros_like(value_total)

        def chunk(i, carry):
            here = pl.ds(pl.multiple_of(i * rows, rows), rows)
            weights_low = held[:, here]
            up = upstream[i, :, cols]
            pulled = dot(values[:, cols], up, ((1,), (1,)))
            weights = weights_low.astype(jnp.float32)
            scaled = weights * pulled
            change = (scaled - weights * jnp.sum(scaled, axis=0, keepdims=True)).astype(
                jnp.bfloat16
            )
            key_total[...] += dot(change, queries[here, cols], ((1,), (0,)))
            value_total[...] += dot(weights_low, up, ((1,), (0,)))
            query_grad = dot(keys_turned[...], change, ((1,), (0,))).T * scale
            triple[here, cols] = rotate_lanes(
                query_grad, cosine[here], signed_sine[here]
            ).astype(jnp.bfloat16)
            return carry

        lax.fori_loop(0, narrow_count, chunk, 0)

        def ending(i, carry):
            here = pl.ds(pl.multiple_of(i * rows, rows), rows)
            triple[here, pl.ds(own_cols + head * HDIM, HDIM)] = rotate_lanes(
                key_total[here] * scale, cosine[here], signed_sine[here]
            ).astype(jnp.bfloat16)
            triple[here, pl.ds(2 * own_cols + head * HDIM, HDIM)] = value_total[here].astype(
                jnp.bfloat16
            )
            return carry

        lax.fori_loop(0, narrow_count, ending, 0)

    for head in range(heads):
        one_head(head)
        if head == heads // 2 - 1:
            plane.last_sums()
    total = merge_out.at[...]
    plane.finish(merge_out)
    count = merge_grad.shape[0]

    def z_rows(where):
        return pl.ds(pl.multiple_of(where * count, count), count)

    for offset in range(1, narrow_count):
        line.send(
            offset, total.at[z_rows(line.peer(offset))], merge_in, merge_send, merge_recv
        )

    def column_sums(cols):
        heads_sums[:, cols] = jnp.sum(
            triple[:, cols].astype(jnp.float32), axis=0, keepdims=True
        )

    tiles(3 * own_cols, 256, column_sums)
    summed = merge_out[z_rows(line.mine)].astype(jnp.float32)
    for offset in range(1, narrow_count):
        line.arrived(offset, merge_in, merge_send, merge_recv)
        summed += merge_in[line.peer(offset)].astype(jnp.float32)
    merge_grad[...] = summed
    line.drain()
    plane.drain()


def attention_backward(
    wide_count,
    narrow_count,
    attended_grad,
    merge_full,
    mixed,
    queries,
    keys,
    values,
    probs,
    cosine,
    signed_sine,
):
    rows, width = attended_grad.shape
    bucket, own_cols = queries.shape
    block = width // wide_count
    count = block // narrow_count
    anywhere = pl.BlockSpec(memory_space=pl.ANY)
    vmem = pl.BlockSpec(memory_space=pltpu.VMEM)
    dma = pltpu.SemaphoreType.DMA
    return pl.pallas_call(
        functools.partial(attention_backward_kernel, wide_count, narrow_count),
        out_shape=(
            jax.ShapeDtypeStruct((bucket, 3 * own_cols), jnp.bfloat16),
            jax.ShapeDtypeStruct((count, width), jnp.float32),
            jax.ShapeDtypeStruct((1, 3 * own_cols), jnp.float32),
            jax.ShapeDtypeStruct((1, width), jnp.float32),
        ),
        in_specs=[vmem] * 6 + [anywhere] + [vmem] * 2,
        out_specs=(vmem, vmem, vmem, vmem),
        scratch_shapes=[
            pltpu.VMEM((narrow_count, rows, own_cols), jnp.bfloat16),
            pltpu.VMEM((narrow_count - 1, rows, own_cols), jnp.bfloat16),
            pltpu.VMEM((2, bucket, bucket), jnp.bfloat16),
            pltpu.VMEM((HDIM, bucket), jnp.bfloat16),
            pltpu.VMEM((bucket, HDIM), jnp.float32),
            pltpu.VMEM((bucket, HDIM), jnp.float32),
            pltpu.VMEM((block, width), jnp.bfloat16),
            pltpu.VMEM((narrow_count, count, width), jnp.bfloat16),
            dma((narrow_count - 1,)),
            dma((narrow_count,)),
            dma((narrow_count - 1,)),
            dma((narrow_count,)),
            dma((2,)),
        ]
        + sum_scratch(wide_count, block, width),
        compiler_params=pltpu.CompilerParams(
            collective_id=3, has_side_effects=True, vmem_limit_bytes=kernel_memory
        ),
        cost_estimate=pl.CostEstimate(
            flops=60 * 10**9, bytes_accessed=200 * 2**20, transcendentals=0
        ),
        name="attention_backward",
    )(
        attended_grad, merge_full, mixed, queries, keys, values, probs, cosine, signed_sine
    )


def input_backward_kernel(
    wide_count,
    narrow_count,
    inputs,
    triple,
    heads_mat,
    small,
    input_part,
    heads_grad,
    small_out,
    line_parts,
    line_in,
    heads_out,
    heads_in,
    small_wide,
    small_sum,
    small_line,
    line_send,
    line_recv,
    heads_send,
    heads_recv,
    wide_send,
    wide_recv,
    small_send,
    small_recv,
    parts,
    from_mate,
    incoming,
    mate_send,
    mate_recv,
    sum_send,
    sum_recv,
):
    sems = (None, None, mate_send, mate_recv, sum_send, sum_recv, None)
    plane = PlaneExchange(wide_count, None, None, parts, from_mate, incoming, sems)
    line = LineExchange(narrow_count)
    rows, width = input_part.shape
    here = line.mine
    last = narrow_count - 1
    place = lax.axis_index("wide")

    def wide_peer(offset):
        return (place + offset) % wide_count

    barrier = pltpu.get_barrier_semaphore()
    for offset in range(1, wide_count):
        pl.semaphore_signal(
            barrier,
            inc=1,
            device_id={"wide": wide_peer(offset)},
            device_id_type=pl.DeviceIdType.MESH,
        )
    line.greet(wide_count - 1)

    def small_copy(offset, source, slot):
        return pltpu.make_async_remote_copy(
            src_ref=source,
            dst_ref=small_wide.at[slot],
            send_sem=wide_send.at[offset - 1],
            recv_sem=wide_recv.at[slot],
            device_id={"wide": wide_peer(offset)},
            device_id_type=pl.DeviceIdType.MESH,
        )

    small_copies = [
        small_copy(offset, small.at[wide_peer(offset)], place) for offset in range(1, wide_count)
    ]
    for copy in small_copies:
        copy.start()

    def input_cols(cols):
        part = dot(triple[...], heads_mat[cols], ((1,), (1,)))
        for index in range(narrow_count):
            line_parts[index, :, cols] = part[index * rows : (index + 1) * rows].astype(
                jnp.bfloat16
            )

    tiles(width, 256, input_cols)

    def line_copy(way, offset):
        target = here + offset if way == 0 else here - offset
        return line.copy(
            line_parts.at[target],
            line_in.at[way, offset - 1],
            line_send.at[way, offset - 1],
            line_recv.at[way, offset - 1],
            here + 1 if way == 0 else here - 1,
        )

    def line_arrived(way, offset):
        landing = line_in.at[way, offset]
        line.copy(
            landing, landing, line_send.at[way, offset], line_recv.at[way, offset], here
        ).wait_recv()

    def add_line(way, offset, slot):
        def chunk(i, carry):
            some = pl.ds(pl.multiple_of(i * 16, 16), 16)
            line_parts[slot, some] = (
                line_parts[slot, some].astype(jnp.float32)
                + line_in[way, offset, some].astype(jnp.float32)
            ).astype(jnp.bfloat16)
            return carry

        lax.fori_loop(0, rows // 16, chunk, 0)

    def line_step(offset):
        for way in range(2):
            reaches = here + offset <= last if way == 0 else here - offset >= 0
            follows = here > 0 if way == 0 else here < last

            @pl.when(reaches)
            def _():
                if offset < last:

                    @pl.when(follows)
                    def _():
                        line_arrived(way, offset)
                        add_line(way, offset, here + offset if way == 0 else here - offset)

                line_copy(way, offset).start()

    line_step(last)

    block = parts.shape[1]

    def heads_rows(i, carry):
        cols = pl.ds(pl.multiple_of(i * block, block), block)
        parts[i] = dot(inputs[:, cols], triple[...], ((0,), (0,))).astype(jnp.bfloat16)
        return carry

    lax.fori_loop(0, wide_count, heads_rows, 0)
    for offset in range(plane.ring):
        plane.share(offset)
    for offset in range(last - 1, last // 2, -1):
        line_step(offset)
    plane.first_sums()
    plane.far_sums()

    for offset in range(1, wide_count):
        peer = wide_peer(offset)
        small_copy(offset, small_wide.at[peer], peer).wait_recv()
    small_wide[place] = small[place]
    total = small_wide[0]
    for index in range(1, wide_count):
        total += small_wide[index]
    small_sum[...] = total
    for offset in range(1, narrow_count):
        line.send(offset, small_sum.at[line.peer(offset)], small_line, small_send, small_recv)

    plane.last_sums()
    for offset in range(last // 2, 0, -1):
        line_step(offset)
    plane.finish(heads_out)
    count = heads_grad.shape[0]

    def z_rows(where):
        return pl.ds(pl.multiple_of(where * count, count), count)

    for offset in range(1, narrow_count):
        line.send(
            offset, heads_out.at[z_rows(line.peer(offset))], heads_in, heads_send, heads_recv
        )
    heads_in[line.mine] = heads_out[z_rows(line.mine)]
    small_line[line.mine] = small_sum[line.mine]
    for offset in range(1, narrow_count):
        line.arrived(offset, small_line, small_send, small_recv)
    result = small_line[0]
    for index in range(1, narrow_count):
        result += small_line[index]
    small_out[...] = result

    def own_rows(i, carry):
        some = pl.ds(pl.multiple_of(i * 16, 16), 16)
        input_part[some] = line_parts[here, some].astype(jnp.float32)
        return carry

    lax.fori_loop(0, rows // 16, own_rows, 0)
    for way in range(2):
        follows = here > 0 if way == 0 else here < last

        @pl.when(follows)
        def _():
            line_arrived(way, 0)

            def chunk(i, carry):
                some = pl.ds(pl.multiple_of(i * 16, 16), 16)
                input_part[some] += line_in[way, 0, some].astype(jnp.float32)
                return carry

            lax.fori_loop(0, rows // 16, chunk, 0)

    for offset in range(1, narrow_count):
        line.arrived(offset, heads_in, heads_send, heads_recv)
    own_cols = triple.shape[1] // 3
    for index in range(narrow_count):
        for which in range(3):
            start = (which * narrow_count + index) * own_cols
            heads_grad[:, start : start + own_cols] = heads_in[
                index, :, which * own_cols : (which + 1) * own_cols
            ].astype(jnp.float32)
    for offset in range(1, narrow_count):
        for way in range(2):
            reaches = here + offset <= last if way == 0 else here - offset >= 0

            @pl.when(reaches)
            def _():
                line_copy(way, offset).wait_send()

    for copy in small_copies:
        copy.wait_send()
    line.drain()
    plane.drain()


def input_backward(wide_count, narrow_count, inputs, triple_grad, heads_mat, small):
    bucket, width = inputs.shape
    rows = bucket // narrow_count
    columns = triple_grad.shape[1]
    block = width // wide_count
    count = block // narrow_count
    vmem = pl.BlockSpec(memory_space=pltpu.VMEM)
    dma = pltpu.SemaphoreType.DMA
    lines = small.shape[2]
    return pl.pallas_call(
        functools.partial(input_backward_kernel, wide_count, narrow_count),
        out_shape=(
            jax.ShapeDtypeStruct((rows, width), jnp.float32),
            jax.ShapeDtypeStruct((count, narrow_count * columns), jnp.float32),
            jax.ShapeDtypeStruct((lines, 128), jnp.float32),
        ),
        in_specs=[vmem] * 4,
        out_specs=(vmem, vmem, vmem),
        scratch_shapes=[
            pltpu.VMEM((narrow_count, rows, width), jnp.bfloat16),
            pltpu.VMEM((2, narrow_count - 1, rows, width), jnp.bfloat16),
            pltpu.VMEM((block, columns), jnp.bfloat16),
            pltpu.VMEM((narrow_count, count, columns), jnp.bfloat16),
            pltpu.VMEM((wide_count, narrow_count, lines, 128), jnp.float32),
            pltpu.VMEM((narrow_count, lines, 128), jnp.float32),
            pltpu.VMEM((narrow_count, lines, 128), jnp.float32),
            dma((2, narrow_count - 1)),
            dma((2, narrow_count - 1)),
            dma((narrow_count - 1,)),
            dma((narrow_count,)),
            dma((wide_count - 1,)),
            dma((wide_count,)),
            dma((narrow_count - 1,)),
            dma((narrow_count,)),
        ]
        + sum_scratch(wide_count, block, columns),
        compiler_params=pltpu.CompilerParams(
            collective_id=4, has_side_effects=True, vmem_limit_bytes=kernel_memory
        ),
        cost_estimate=pl.CostEstimate(
            flops=80 * 10**9, bytes_accessed=200 * 2**20, transcendentals=0
        ),
        name="input_backward",
    )(inputs, triple_grad, heads_mat, small)


def greet_all(wide_count, narrow_count):
    barrier = pltpu.get_barrier_semaphore()
    for axis, count in (("wide", wide_count), ("narrow", narrow_count)):
        place = lax.axis_index(axis)
        for offset in range(1, count):
            pl.semaphore_signal(
                barrier,
                inc=1,
                device_id={axis: (place + offset) % count},
                device_id_type=pl.DeviceIdType.MESH,
            )
    pl.semaphore_wait(barrier, wide_count + narrow_count - 2)


def gather_kernel(
    wide_count,
    narrow_count,
    own,
    heads_weight,
    merge_weight,
    small,
    rows_out,
    heads_out,
    merge_out,
    small_out,
    triple,
    rows_all,
    heads_all,
    merge_all,
    small_all,
    rows_send,
    rows_recv,
    heads_send,
    heads_recv,
    merge_send,
    merge_recv,
    small_send,
    small_recv,
    wide_send,
    wide_recv,
    local_sems,
    out_sems,
    heads_ring_send,
    heads_ring_recv,
    merge_ring_send,
    merge_ring_recv,
):
    def ring_of(blocks, send, recv):
        sems = (send, recv, None, None, None, None, None)
        return PlaneExchange(wide_count, None, blocks, blocks, None, None, sems)

    heads_ring = ring_of(heads_all, heads_ring_send, heads_ring_recv)
    merge_ring = ring_of(merge_all, merge_ring_send, merge_ring_recv)
    line = LineExchange(narrow_count)
    here = line.mine
    last = narrow_count - 1
    place = lax.axis_index("wide")
    slot = heads_ring.slot(0)
    rows, width = own.shape
    count = heads_weight.shape[0]
    columns = heads_all.shape[2]
    own_cols = columns // 3

    def z_rows(where):
        return pl.ds(pl.multiple_of(where * count, count), count)

    def head_cols(which, where):
        start = which * narrow_count * own_cols + where * own_cols
        return pl.ds(pl.multiple_of(start, own_cols), own_cols)

    def line_rows(way, block):
        source = rows_all.at[block]
        return line.copy(
            source,
            source,
            rows_send.at[way, block],
            rows_recv.at[block],
            here + 1 if way == 0 else here - 1,
        )

    def goes(way):
        return here < last if way == 0 else here > 0

    def has(way, step):
        return here - step >= 0 if way == 0 else here + step <= last

    def block_of(way, step):
        return here - step if way == 0 else here + step

    keep_rows = pltpu.make_async_copy(own, rows_all.at[here], local_sems.at[0])
    keep_rows.start()
    keeps = [
        pltpu.make_async_copy(
            heads_weight.at[:, head_cols(which, here)],
            heads_all.at[slot, z_rows(here), pl.ds(which * own_cols, own_cols)],
            local_sems.at[2 + which],
        )
        for which in range(3)
    ]
    keep_merge = pltpu.make_async_copy(
        merge_weight, merge_all.at[slot, z_rows(here)], local_sems.at[1]
    )
    for copy in keeps + [keep_merge]:
        copy.start()
    small_all[place, here] = small[...]
    greet_all(wide_count, narrow_count)

    def heads_copy(offset, which, where, sender):
        return line.copy(
            heads_weight.at[:, head_cols(which, where)],
            heads_all.at[slot, z_rows(sender), pl.ds(which * own_cols, own_cols)],
            heads_send.at[offset - 1, which],
            heads_recv.at[sender, which],
            where,
        )

    def merge_copy(offset, where, sender):
        return line.copy(
            merge_weight,
            merge_all.at[slot, z_rows(sender)],
            merge_send.at[offset - 1],
            merge_recv.at[sender],
            where,
        )

    def small_copy(offset, where, sender):
        return line.copy(
            small,
            small_all.at[place, sender],
            small_send.at[offset - 1],
            small_recv.at[sender],
            where,
        )

    started = []

    def start(copy):
        copy.start()
        started.append(copy)

    for offset in range(1, narrow_count):
        for which in range(3):
            start(heads_copy(offset, which, line.peer(offset), here))
    for offset in range(1, narrow_count):
        start(small_copy(offset, line.peer(offset), here))
    keep_rows.wait()
    for way in range(2):

        @pl.when(goes(way))
        def _():
            line_rows(way, here).start()

    for offset in range(1, narrow_count):
        start(merge_copy(offset, line.peer(offset), here))

    for copy in keeps:
        copy.wait()
    for offset in range(1, narrow_count):
        for which in range(3):
            heads_copy(offset, which, line.peer(offset), line.peer(offset)).wait_recv()
    heads_ring.send_own()
    for offset in range(1, narrow_count):
        small_copy(offset, line.peer(offset), line.peer(offset)).wait_recv()

    def wide_copy(offset, sender):
        return pltpu.make_async_remote_copy(
            src_ref=small_all.at[sender],
            dst_ref=small_all.at[sender],
            send_sem=wide_send.at[offset - 1],
            recv_sem=wide_recv.at[sender],
            device_id={"wide": (place + offset) % wide_count},
            device_id_type=pl.DeviceIdType.MESH,
        )

    for offset in range(1, wide_count):
        start(wide_copy(offset, place))

    def rows_step(step):
        for way in range(2):

            @pl.when(has(way, step))
            def _():
                line_rows(way, block_of(way, step)).wait_recv()

                @pl.when(goes(way))
                def _():
                    line_rows(way, block_of(way, step)).start()

    def project(block):
        def cols_step(cols):
            weight = heads_all[:, :, cols].reshape(width, cols.size)
            triple[pl.ds(pl.multiple_of(block * rows, rows), rows), cols] = dot(
                rows_all[block], weight, ((1,), (0,))
            )

        tiles(columns, 256, cols_step)

    def project_step(step):
        for way in range(2):

            @pl.when(has(way, step))
            def _():
                project(block_of(way, step))

    keep_merge.wait()
    for offset in range(1, narrow_count):
        merge_copy(offset, line.peer(offset), line.peer(offset)).wait_recv()
    rows_step(1)
    merge_ring.send_own()

    def gather(ring, distance):
        ring.receive(distance)
        ring.receive_mate(-distance)
        if distance < ring.far:
            ring.receive_mate(distance)

    heads_ring.receive_mate(0)
    for distance in range(1, heads_ring.far + 1):
        gather(heads_ring, distance)
    outs = []

    def keep_out(source, target):
        copy = pltpu.make_async_copy(source, target, out_sems.at[len(outs)])
        copy.start()
        outs.append(copy)

    keep_out(heads_all, heads_out)
    project(here)
    merge_ring.receive_mate(0)
    for distance in range(1, merge_ring.far):
        gather(merge_ring, distance)
    project_step(1)
    rows_step(2)
    gather(merge_ring, merge_ring.far)
    keep_out(merge_all, merge_out)
    project_step(2)
    for step in range(3, narrow_count):
        rows_step(step)
        project_step(step)
    keep_out(rows_all, rows_out)
    for offset in range(1, wide_count):
        wide_copy(offset, (place + offset) % wide_count).wait_recv()
    keep_out(small_all, small_out)
    for way in range(2):
        for step in range(narrow_count):

            @pl.when(has(way, step) & goes(way))
            def _():
                line_rows(way, block_of(way, step)).wait_send()

    for copy in started:
        copy.wait_send()
    heads_ring.drain()
    merge_ring.drain()
    for copy in outs:
        copy.wait()


def gather_front(wide_count, narrow_count, layer_input, heads_weight, merge_weight, small):
    rows, width = layer_input.shape
    count, all_columns = heads_weight.shape
    columns = all_columns // narrow_count
    block = count * narrow_count
    anywhere = pl.BlockSpec(memory_space=pl.ANY)
    vmem = pl.BlockSpec(memory_space=pltpu.VMEM)
    dma = pltpu.SemaphoreType.DMA
    lines = small.shape[0]
    shapes = (
        (narrow_count, rows, width),
        (wide_count, block, columns),
        (wide_count, block, width),
        (wide_count, narrow_count, lines, 128),
    )
    far = narrow_count - 1
    return pl.pallas_call(
        functools.partial(gather_kernel, wide_count, narrow_count),
        out_shape=tuple(jax.ShapeDtypeStruct(shape, jnp.bfloat16) for shape in shapes)
        + (jax.ShapeDtypeStruct((narrow_count * rows, columns), jnp.float32),),
        in_specs=[anywhere, anywhere, anywhere, vmem],
        out_specs=(anywhere, anywhere, anywhere, anywhere, vmem),
        scratch_shapes=[pltpu.VMEM(shape, jnp.bfloat16) for shape in shapes]
        + [
            dma((2, narrow_count)),
            dma((narrow_count,)),
            dma((far, 3)),
            dma((narrow_count, 3)),
            dma((far,)),
            dma((narrow_count,)),
            dma((far,)),
            dma((narrow_count,)),
            dma((wide_count - 1,)),
            dma((wide_count,)),
            dma((5,)),
            dma((4,)),
            dma((3, wide_count, 2)),
            dma((wide_count, 2)),
            dma((3, wide_count, 2)),
            dma((wide_count, 2)),
        ],
        compiler_params=pltpu.CompilerParams(
            collective_id=5, has_side_effects=True, vmem_limit_bytes=kernel_memory
        ),
        cost_estimate=pl.CostEstimate(
            flops=80 * 10**9, bytes_accessed=200 * 2**20, transcendentals=0
        ),
        name="gather_front",
    )(layer_input, heads_weight, merge_weight, small)


def attention_forward_kernel(
    narrow_count,
    triple,
    heads_shift,
    cosine,
    signed_sine,
    first_query,
    last_query,
    own,
    merge,
    merge_shift,
    gain,
    shift,
    queries,
    keys,
    values,
    probs,
    mixed_out,
    hidden,
    hidden_low,
    normed,
    inv_std,
    merge_mat,
    probs_held,
    values_turned,
    outbound,
    mixed,
    mixed_send,
    mixed_recv,
    local_sems,
):
    line = LineExchange(narrow_count)
    bucket, own_cols = queries.shape
    rows, width = own.shape
    heads = own_cols // HDIM
    scale = HDIM ** (-0.5)
    load_merge = pltpu.make_async_copy(merge, merge_mat, local_sems.at[2])
    load_merge.start()
    line.greet()

    def keep(head):
        return pltpu.make_async_copy(
            probs_held.at[head % 2], probs.at[head], local_sems.at[head % 2]
        )

    def mixed_copy(head, offset, where, sender):
        cols = pl.ds(pl.multiple_of(sender * own_cols + head * HDIM, HDIM), HDIM)
        return line.copy(
            outbound.at[where, :, pl.ds(head * HDIM, HDIM)],
            mixed.at[:, cols],
            mixed_send.at[offset - 1, head],
            mixed_recv.at[sender, head],
            where,
        )

    started = []
    for head in range(heads):
        cols = pl.ds(head * HDIM, HDIM)

        def turn(i, carry):
            here = pl.ds(pl.multiple_of(i * rows, rows), rows)
            for which, target in enumerate((queries, keys, values)):
                wanted = pl.ds(which * own_cols + head * HDIM, HDIM)
                part = triple[here, wanted] + heads_shift[:, wanted]
                if which < 2:
                    part = rotate_lanes(part, cosine[here], -signed_sine[here])
                else:
                    values_turned[:, here] = part.T.astype(jnp.bfloat16)
                target[here, cols] = part.astype(jnp.bfloat16)
            return carry

        lax.fori_loop(0, narrow_count, turn, 0)
        if head >= 2:
            keep(head - 2).wait()
        held = probs_held.at[head % 2]

        def chunk(i, carry):
            here = pl.ds(pl.multiple_of(i * rows, rows), rows)
            scores = dot(keys[:, cols], queries[here, cols], ((1,), (1,))) * scale
            token = i * rows + lax.broadcasted_iota(jnp.int32, (bucket, rows), 1)
            seen = (token >= first_query[...]) & (token <= last_query[...])
            scores = jnp.where(seen, scores, masked_value)
            expo = jnp.exp(scores - jnp.max(scores, axis=0, keepdims=True))
            weights = (expo * (1 / jnp.sum(expo, axis=0, keepdims=True))).astype(jnp.bfloat16)
            held[:, here] = weights
            mixed_part = dot(values_turned[...], weights, ((1,), (0,)))
            outbound[i, :, cols] = mixed_part.T.astype(jnp.bfloat16)
            return carry

        lax.fori_loop(0, narrow_count, chunk, 0)
        keep(head).start()
        for offset in range(1, narrow_count):
            copy = mixed_copy(head, offset, line.peer(offset), line.mine)
            copy.start()
            started.append(copy)
    own_mixed = pltpu.make_async_copy(
        outbound.at[line.mine],
        mixed.at[:, pl.ds(pl.multiple_of(line.mine * own_cols, own_cols), own_cols)],
        local_sems.at[3],
    )
    own_mixed.start()
    own_mixed.wait()
    load_merge.wait()
    for offset in range(1, narrow_count):
        for head in range(heads):
            mixed_copy(head, offset, line.peer(offset), line.peer(offset)).wait_recv()
    mixed_out[...] = mixed[...]

    def merge_cols(cols):
        hidden[:, cols] = (
            residual_scale * own[:, cols].astype(jnp.float32)
            + dot(mixed[...], merge_mat[:, cols], ((1,), (0,)))
            + merge_shift[:, cols]
        )

    tiles(width, 256, merge_cols)

    def norm_rows(i, carry):
        some = pl.ds(pl.multiple_of(i * 16, 16), 16)
        result, centred, inverse = normalize(hidden[some], gain[...], shift[...])
        hidden[some] = result
        hidden_low[some] = result.astype(jnp.bfloat16)
        normed[some] = centred
        inv_std[some] = inverse
        return carry

    lax.fori_loop(0, rows // 16, norm_rows, 0)
    for head in range(max(heads - 2, 0), heads):
        keep(head).wait()
    for copy in started:
        copy.wait_send()


def attention_forward(
    narrow_count,
    triple,
    heads_shift,
    cosine,
    signed_sine,
    first_query,
    last_query,
    layer_input,
    merge_full,
    merge_shift,
    gain,
    shift,
):
    bucket, columns = triple.shape
    rows, width = layer_input.shape
    own_cols = columns // 3
    heads = own_cols // HDIM
    anywhere = pl.BlockSpec(memory_space=pl.ANY)
    vmem = pl.BlockSpec(memory_space=pltpu.VMEM)
    dma = pltpu.SemaphoreType.DMA

    def low_shape(*shape):
        return jax.ShapeDtypeStruct(shape, jnp.bfloat16)

    def wide_shape(*shape):
        return jax.ShapeDtypeStruct(shape, jnp.float32)

    return pl.pallas_call(
        functools.partial(attention_forward_kernel, narrow_count),
        out_shape=(
            low_shape(bucket, own_cols),
            low_shape(bucket, own_cols),
            low_shape(bucket, own_cols),
            low_shape(heads, bucket, bucket),
            low_shape(rows, width),
            wide_shape(rows, width),
            low_shape(rows, width),
            wide_shape(rows, width),
            wide_shape(rows, 1),
        ),
        in_specs=[vmem] * 7 + [anywhere] + [vmem] * 3,
        out_specs=(vmem, vmem, vmem, anywhere) + (vmem,) * 5,
        scratch_shapes=[
            pltpu.VMEM((width, width), jnp.bfloat16),
            pltpu.VMEM((2, bucket, bucket), jnp.bfloat16),
            pltpu.VMEM((HDIM, bucket), jnp.bfloat16),
            pltpu.VMEM((narrow_count, rows, own_cols), jnp.bfloat16),
            pltpu.VMEM((rows, width), jnp.bfloat16),
            dma((narrow_count - 1, heads)),
            dma((narrow_count, heads)),
            dma((4,)),
        ],
        compiler_params=pltpu.CompilerParams(
            collective_id=6, has_side_effects=True, vmem_limit_bytes=kernel_memory
        ),
        cost_estimate=pl.CostEstimate(
            flops=60 * 10**9, bytes_accessed=200 * 2**20, transcendentals=0
        ),
        name="attention_forward",
    )(
        triple,
        heads_shift,
        cosine,
        signed_sine,
        first_query,
        last_query,
        layer_input,
        merge_full,
        merge_shift,
        gain,
        shift,
    )


def shards(
    layer_input,
    heads_weight,
    heads_bias,
    merge_weight,
    merge_bias,
    norm_gains,
    norm_shifts,
    expand_weight,
    expand_bias,
    reduce_weight,
    reduce_bias,
    joined,
    prefix,
    cotangent,
):
    tok_rows, model_width = layer_input.shape
    wide_count = lax.axis_size("wide")
    narrow_count = lax.axis_size("narrow")
    count = wide_count * narrow_count
    bucket_len = tok_rows * narrow_count
    own_heads = HEADS // narrow_count
    own_cols = own_heads * HDIM
    share = expand_weight.shape[2]
    joined_flag = joined[0]
    prefix_pair = prefix[0]
    narrow_index = lax.axis_index("narrow")
    positions = jnp.arange(bucket_len, dtype=jnp.int32)
    second_seq, local_pos, prefix_len = layout(positions, joined_flag, prefix_pair, bucket_len)
    cosine, sine_table = rotary_tables(local_pos, HDIM)
    first_query = jnp.where(local_pos < prefix_len, positions - local_pos, positions)
    last_query = jnp.where(
        (joined_flag == 1) | (second_seq == 1), bucket_len - 1, bucket_len // 2 - 1
    )

    smalls = (heads_bias, merge_bias, norm_gains, norm_shifts, expand_bias, reduce_bias)
    rows_input, heads_mat, merge_full, small_all, triple = gather_front(
        wide_count, narrow_count, layer_input, heads_weight, merge_weight, pack_small(smalls)
    )
    rows_input = rows_input.reshape(bucket_len, model_width)
    heads_mat = heads_mat.reshape(model_width, 3 * own_cols)
    merge_full = merge_full.reshape(model_width, model_width)
    heads_shift, merge_shift, gains, shifts, expand_shift, reduce_shift = unpack_small(
        small_all, smalls
    )
    own_shift = lax.dynamic_index_in_dim(
        heads_shift.reshape(3, narrow_count, own_cols), narrow_index, 1, keepdims=False
    ).reshape(1, -1)
    cosine_wide = jnp.concatenate([cosine, cosine], axis=1)
    signed_sine = jnp.concatenate([sine_table, -sine_table], axis=1)
    (
        queries,
        keys,
        values,
        probs_low,
        mixed,
        hidden,
        hidden_low,
        normed_one,
        inv_one,
    ) = attention_forward(
        narrow_count,
        triple,
        own_shift,
        cosine_wide,
        signed_sine,
        first_query.reshape(-1, 1),
        last_query.reshape(-1, 1),
        layer_input,
        merge_full,
        merge_shift.reshape(1, -1),
        gains[0].reshape(1, -1),
        shifts[0].reshape(1, -1),
    )

    tile_rows = -share % 16
    padded = -(-share // 256) * 256
    expand_full = lax.all_gather(
        jnp.pad(expand_weight.transpose(1, 2, 0), ((0, 0), (0, tile_rows), (0, 0))),
        "narrow",
        axis=2,
        tiled=True,
    )
    reduce_full = lax.all_gather(
        jnp.pad(reduce_weight, ((0, tile_rows), (0, 0))), "narrow", axis=1, tiled=True
    )
    rows_all, active, slope, gelu, feed_sum = geglu_forward(
        wide_count,
        hidden_low,
        expand_full,
        reduce_full,
        jnp.pad(expand_shift, ((0, 0), (0, padded - share))),
    )
    feed = feed_sum + reduce_shift
    output_float, normed_two, inv_two = normalize(
        residual_scale * hidden + feed, gains[1], shifts[1]
    )
    layer_output = low(output_float)

    grad_out = cotangent.astype(jnp.float32)
    gain_two_grad = jnp.sum(grad_out * normed_two, axis=0)
    shift_two_grad = jnp.sum(grad_out, axis=0)
    sum_two_grad = normalize_back(grad_out, normed_two, inv_two, gains[1])
    feed_grad = low(sum_two_grad)
    feed_grads_all, unit_grads, hidden_part, unit_sums = geglu_backward(
        wide_count, feed_grad, expand_full, reduce_full, slope, gelu
    )
    tokens_all = wide_count * tok_rows
    rows_all = rows_all.reshape(tokens_all, model_width)
    feed_grads_all = feed_grads_all.reshape(tokens_all, model_width)
    unit_grads = unit_grads.reshape(2, tokens_all, padded)
    reduce_part = low(dot(active.reshape(tokens_all, padded), feed_grads_all, ((0,), (0,))))[:share]
    expand_part = low(dot(unit_grads, rows_all, ((1,), (0,))))[:, :share]
    reduce_part, expand_part, hidden_part = lax.optimization_barrier(
        (reduce_part, expand_part, hidden_part)
    )
    reduce_weight_gradient = lax.psum_scatter(
        reduce_part, "narrow", scatter_dimension=1, tiled=True
    ).astype(jnp.float32)
    expand_weight_gradient = (
        lax.psum_scatter(expand_part, "narrow", scatter_dimension=2, tiled=True)
        .astype(jnp.float32)
        .transpose(2, 0, 1)
    )
    hidden_grad = residual_scale * sum_two_grad + hidden_part
    gain_one_grad = jnp.sum(hidden_grad * normed_one, axis=0)
    shift_one_grad = jnp.sum(hidden_grad, axis=0)
    sum_one_grad = normalize_back(hidden_grad, normed_one, inv_one, gains[0])
    attended_grad = low(sum_one_grad)
    triple_grad, merge_weight_gradient, heads_sums, merge_sums = attention_backward(
        wide_count,
        narrow_count,
        attended_grad,
        merge_full,
        mixed,
        queries,
        keys,
        values,
        probs_low,
        cosine_wide,
        signed_sine,
    )

    mine_narrow = (jnp.arange(narrow_count) == narrow_index).astype(jnp.float32)
    mine_wide = (jnp.arange(wide_count) == lax.axis_index("wide")).astype(jnp.float32)
    heads_sums = heads_sums.reshape(3, 1, own_cols)
    heads_sums = (heads_sums * mine_narrow[None, :, None]).reshape(count, -1)
    merge_sums = merge_sums.reshape(count, -1)
    norm_sums = (
        jnp.stack([gain_one_grad, gain_two_grad, shift_one_grad, shift_two_grad])
        .reshape(4, count, -1)
        .transpose(1, 0, 2)
        .reshape(count, -1)
    )
    expand_sums = unit_sums[:, :share]
    expand_sums = (
        expand_sums.reshape(2, narrow_count, -1).transpose(1, 0, 2).reshape(1, narrow_count, -1)
        * mine_wide[:, None, None]
    ).reshape(count, -1)
    reduce_sums = jnp.sum(feed_grad, axis=0, dtype=jnp.float32).reshape(1, narrow_count, -1)
    reduce_sums = jnp.broadcast_to(
        reduce_sums, (wide_count, narrow_count, reduce_sums.shape[2])
    ).reshape(count, -1)
    pieces = (heads_sums, merge_sums, norm_sums, expand_sums, reduce_sums)
    packed = jnp.concatenate(pieces, axis=1)
    packed = jnp.pad(packed, ((0, 0), (0, -packed.shape[1] % 1024)))
    input_part, heads_weight_gradient, summed = input_backward(
        wide_count,
        narrow_count,
        rows_input,
        triple_grad,
        heads_mat,
        packed.reshape(wide_count, narrow_count, -1, 128),
    )
    input_gradient = residual_scale * sum_one_grad + input_part
    summed = summed.reshape(-1)
    ends = []
    start = 0
    for piece in pieces:
        ends.append(summed[start : start + piece.shape[1]])
        start += piece.shape[1]
    norm_ends = ends[2].reshape(4, -1)
    return (
        layer_output,
        input_gradient,
        heads_weight_gradient,
        ends[0],
        merge_weight_gradient,
        ends[1],
        norm_ends[:2],
        norm_ends[2:],
        expand_weight_gradient,
        ends[3].reshape(2, -1),
        reduce_weight_gradient,
        ends[4],
    )


def solution(mesh):
    return jax.shard_map(
        shards,
        mesh=mesh,
        in_specs=(
            P(("wide", "narrow"), None),
            P(("wide", "narrow"), None),
            P(("wide", "narrow")),
            P(("wide", "narrow"), None),
            P(("wide", "narrow")),
            P(None, ("wide", "narrow")),
            P(None, ("wide", "narrow")),
            P("narrow", None, "wide"),
            P(None, ("wide", "narrow")),
            P("wide", "narrow"),
            P("narrow"),
            P("wide"),
            P("wide", None),
            P(("wide", "narrow"), None),
        ),
        out_specs=(
            P(("wide", "narrow"), None),
            P(("wide", "narrow"), None),
            P(("wide", "narrow"), None),
            P(("wide", "narrow")),
            P(("wide", "narrow"), None),
            P(("wide", "narrow")),
            P(None, ("wide", "narrow")),
            P(None, ("wide", "narrow")),
            P("narrow", None, "wide"),
            P(None, ("wide", "narrow")),
            P("wide", "narrow"),
            P("narrow"),
        ),
        check_vma=False,
    )
```

```python
import functools
import math

import jax
import jax.numpy as jnp
from jax import lax
from jax.experimental import pallas as pl
from jax.experimental.pallas import tpu as pltpu
from jax.sharding import PartitionSpec as P

HEADS = 16
HDIM = 128


residual_scale = 48.0**0.5
norm_eps = 1e-05
masked_value = -1e30
kernel_memory = 60 * 2**20


def layout(positions, joined_flag, prefix_pair, bucket_len):
    halfway = bucket_len // 2
    second_seq = (positions >= halfway).astype(jnp.int32) * (1 - joined_flag)
    local_pos = positions - second_seq * halfway
    prefix_len = jnp.where(
        joined_flag == 1,
        prefix_pair[0] + prefix_pair[1],
        jnp.where(second_seq == 1, prefix_pair[1], prefix_pair[0]),
    )
    return (second_seq, local_pos, prefix_len)


def rotary_tables(local_pos, head_size):
    halfway = head_size // 2
    inverse = 10000.0 ** (-(2.0 * jnp.arange(halfway).astype(jnp.float32)) / head_size)
    angles = local_pos.astype(jnp.float32)[:, None] * inverse[None, :]
    return (jnp.cos(angles), jnp.sin(angles))


def normalize(values, gain, shift):
    centre = jnp.mean(values, axis=-1, keepdims=True)
    centred = values - centre
    variance = jnp.mean(centred * centred, axis=-1, keepdims=True)
    inv_std = lax.rsqrt(variance + norm_eps)
    normed = centred * inv_std
    return (normed * gain + shift, normed, inv_std)


def normalize_back(upstream, normed, inv_std, gain):
    scaled = upstream * gain
    return inv_std * (
        scaled
        - jnp.mean(scaled, axis=-1, keepdims=True)
        - normed * jnp.mean(scaled * normed, axis=-1, keepdims=True)
    )


def dot(left, right, dims):
    return lax.dot_general(left, right, (dims, ((), ())), preferred_element_type=jnp.float32)


def low(values):
    return values.astype(jnp.bfloat16)


def pack_small(parts):
    packed = jnp.concatenate([part.reshape(-1) for part in parts])
    return jnp.pad(packed, (0, -packed.size % 2048)).reshape(-1, 128)


def unpack_small(everyone, parts):
    wide_count, narrow_count = everyone.shape[:2]
    everyone = everyone.reshape(wide_count, narrow_count, -1).astype(jnp.float32)
    pieces = []
    start = 0
    for part in parts:
        pieces.append(everyone[:, :, start : start + part.size])
        start += part.size

    def pairs(piece):
        piece = piece.reshape(-1, 2, piece.shape[-1] // 2)
        return piece.transpose(1, 0, 2).reshape(2, -1)

    own_expand = lax.dynamic_index_in_dim(
        pieces[4], lax.axis_index("wide"), 0, keepdims=False
    )
    return (
        pieces[0].reshape(-1),
        pieces[1].reshape(-1),
        pairs(pieces[2]),
        pairs(pieces[3]),
        pairs(own_expand),
        pieces[5][0].reshape(-1),
    )


def ring_place(wide_count):
    ring = wide_count // 2
    mine = lax.axis_index("wide")
    chip = mine // 2
    core = mine % 2
    position = 2 * (chip // 2) + (chip % 2 + chip // 2) % 2
    return ring, position, core


def chip_at(position, ring):
    position = (position + 2 * ring) % ring
    return 2 * (position // 2) + (position + position // 2) % 2


class PlaneExchange:
    def __init__(self, wide_count, own, blocks, parts, from_mate, incoming, sems):
        self.ring, self.position, self.core = ring_place(wide_count)
        self.own, self.blocks, self.parts = own, blocks, parts
        self.from_mate, self.incoming = from_mate, incoming
        (
            self.gather_send,
            self.gather_recv,
            self.mate_send,
            self.mate_recv,
            self.sum_send,
            self.sum_recv,
            self.own_sem,
        ) = sems
        self.half = parts.shape[1] // 2
        self.far = self.ring // 2
        self.started = []

    def device(self, offset, mate=False):
        core = 1 - self.core if mate else self.core
        return {"wide": 2 * chip_at(self.position + offset, self.ring) + core}

    def slot(self, offset, mate=False):
        core = 1 - self.core if mate else self.core
        return 2 * chip_at(self.position + offset, self.ring) + core

    def rows(self, part):
        return pl.ds(part * self.half, self.half)

    def greet(self):
        barrier = pltpu.get_barrier_semaphore()
        for where in (self.device(-1), self.device(1), self.device(0, True)):
            pl.semaphore_signal(
                barrier, inc=1, device_id=where, device_id_type=pl.DeviceIdType.MESH
            )
        pl.semaphore_wait(barrier, 3)

    def start(self, source, target, send_sem, recv_sem, where):
        copy = pltpu.make_async_remote_copy(
            src_ref=source,
            dst_ref=target,
            send_sem=send_sem,
            recv_sem=recv_sem,
            device_id=where,
            device_id_type=pl.DeviceIdType.MESH,
        )
        copy.start()
        self.started.append(copy)

    def pass_on(self, lane, slot, part, where, source=None):
        target = self.blocks.at[slot, self.rows(part)]
        self.start(
            target if source is None else source,
            target,
            self.gather_send.at[lane, slot, part],
            self.gather_recv.at[slot, part],
            where,
        )

    def arrived(self, slot, part):
        target = self.blocks.at[slot, self.rows(part)]
        pltpu.make_async_remote_copy(
            src_ref=target,
            dst_ref=target,
            send_sem=self.gather_send.at[0, slot, part],
            recv_sem=self.gather_recv.at[slot, part],
            device_id=self.device(1),
            device_id_type=pl.DeviceIdType.MESH,
        ).wait_recv()

    def send_own(self):
        slot = self.slot(0)
        keep = None
        own = self.blocks.at[slot]
        if self.own is not None:
            own = self.own
            keep = pltpu.make_async_copy(own, self.blocks.at[slot], self.own_sem)
            keep.start()
        first, second = own.at[self.rows(0)], own.at[self.rows(1)]
        self.pass_on(0, slot, 0, self.device(1), first)
        self.pass_on(1, slot, 1, self.device(-1), second)
        self.pass_on(2, slot, 0, self.device(0, True), first)
        self.pass_on(2, slot, 1, self.device(0, True), second)
        self.pass_on(0, slot, 1, self.device(1), second)
        self.pass_on(1, slot, 0, self.device(-1), first)
        return keep

    def receive(self, distance):
        mate = self.device(0, True)
        left, right = self.slot(-distance), self.slot(distance)
        if distance == self.far:
            for part in range(2):
                self.arrived(left, part)
                self.pass_on(2, left, part, mate)
            return
        further = distance < self.far - 1
        self.arrived(left, 0)
        self.pass_on(0, left, 0, self.device(1))
        self.pass_on(2, left, 0, mate)
        self.arrived(right, 1)
        self.pass_on(1, right, 1, self.device(-1))
        self.pass_on(2, right, 1, mate)
        self.arrived(left, 1)
        if further:
            self.pass_on(0, left, 1, self.device(1))
        self.pass_on(2, left, 1, mate)
        self.arrived(right, 0)
        if further:
            self.pass_on(1, right, 0, self.device(-1))
        self.pass_on(2, right, 0, mate)

    def receive_mate(self, offset):
        for part in range(2):
            self.arrived(self.slot(offset, True), part)

    def share(self, offset):
        chip = chip_at(self.position + offset, self.ring)
        self.start(
            self.parts.at[self.slot(offset, True)],
            self.from_mate.at[chip],
            self.mate_send.at[chip],
            self.mate_recv.at[chip],
            self.device(0, True),
        )

    def shared(self, offset):
        chip = chip_at(self.position + offset, self.ring)
        pltpu.make_async_remote_copy(
            src_ref=self.parts.at[self.slot(offset)],
            dst_ref=self.from_mate.at[chip],
            send_sem=self.mate_send.at[chip],
            recv_sem=self.mate_recv.at[chip],
            device_id=self.device(0, True),
            device_id_type=pl.DeviceIdType.MESH,
        ).wait_recv()

    def chip_sum(self, offset, rows):
        chip = chip_at(self.position + offset, self.ring)
        return self.parts[self.slot(offset), rows].astype(jnp.float32) + self.from_mate[
            chip, rows
        ].astype(jnp.float32)

    def send_sum(self, way, distance, part):
        offset = distance if way == 0 else -distance
        begins = self.far if part == way else self.far - 1
        slot = self.slot(offset)
        if distance < begins:
            self.sum_arrived(way, distance, part)

        def chunk(i, carry):
            here = pl.ds(pl.multiple_of(i * 16, 16), 16)
            there = pl.ds(pl.multiple_of(part * self.half + i * 16, 16), 16)
            total = self.chip_sum(offset, there)
            if distance < begins:
                total += self.incoming[way, distance, part, here].astype(jnp.float32)
            self.parts[slot, there] = total.astype(jnp.bfloat16)
            return carry

        lax.fori_loop(0, self.half // 16, chunk, 0)
        self.start(
            self.parts.at[slot, self.rows(part)],
            self.incoming.at[way, distance - 1, part],
            self.sum_send.at[way, distance - 1, part],
            self.sum_recv.at[way, distance - 1, part],
            self.device(1 if way == 0 else -1),
        )

    def sum_arrived(self, way, distance, part):
        target = self.incoming.at[way, distance, part]
        pltpu.make_async_remote_copy(
            src_ref=target,
            dst_ref=target,
            send_sem=self.sum_send.at[way, distance, part],
            recv_sem=self.sum_recv.at[way, distance, part],
            device_id=self.device(1),
            device_id_type=pl.DeviceIdType.MESH,
        ).wait_recv()

    def run(self, compute, beside=()):
        beside = list(beside)
        keep = self.send_own()
        keep.wait()
        self.receive_mate(0)
        compute(chip_at(self.position, self.ring))
        self.share(0)
        for distance in range(1, self.far):
            self.receive(distance)
            for offset in (-distance, distance):
                self.receive_mate(offset)
                compute(chip_at(self.position + offset, self.ring))
                self.share(offset)
            if distance == self.far - 1:
                self.first_sums()
        self.receive(self.far)
        self.receive_mate(self.far)
        compute(chip_at(self.position + self.far, self.ring))
        self.share(self.far)
        for work in beside[: len(beside) // 4]:
            work()
        self.far_sums()
        for work in beside[len(beside) // 4 : (5 * len(beside)) // 8]:
            work()
        self.last_sums()
        for work in beside[(5 * len(beside)) // 8 :]:
            work()

    def first_sums(self):
        distance = self.far - 1
        self.shared(distance)
        self.send_sum(0, distance, 1)
        self.shared(-distance)
        self.send_sum(1, distance, 0)

    def far_sums(self):
        self.shared(self.far)
        self.send_sum(0, self.far, 0)
        self.send_sum(1, self.far, 1)

    def last_sums(self):
        for distance in range(self.far - 1, 0, -1):
            if distance < self.far - 1:
                self.shared(distance)
                self.shared(-distance)
            self.send_sum(0, distance, 0)
            self.send_sum(1, distance, 1)
            if distance < self.far - 1:
                self.send_sum(0, distance, 1)
                self.send_sum(1, distance, 0)

    def finish(self, result):
        self.shared(0)
        for part in range(2):
            for way in range(2):
                self.sum_arrived(way, 0, part)

            def chunk(i, carry):
                here = pl.ds(pl.multiple_of(i * 16, 16), 16)
                there = pl.ds(pl.multiple_of(part * self.half + i * 16, 16), 16)
                total = self.chip_sum(0, there)
                for way in range(2):
                    total += self.incoming[way, 0, part, here].astype(jnp.float32)
                result[there] = total.astype(result.dtype)
                return carry

            lax.fori_loop(0, self.half // 16, chunk, 0)

    def drain(self):
        for copy in self.started:
            copy.wait_send()


def sum_scratch(wide_count, rows, width):
    ring = wide_count // 2
    far = ring // 2
    dma = pltpu.SemaphoreType.DMA
    return [
        pltpu.VMEM((wide_count, rows, width), jnp.bfloat16),
        pltpu.VMEM((ring, rows, width), jnp.bfloat16),
        pltpu.VMEM((2, far, 2, rows // 2, width), jnp.bfloat16),
        dma((ring,)),
        dma((ring,)),
        dma((2, far, 2)),
        dma((2, far, 2)),
    ]


def exchange_scratch(wide_count, rows, width):
    dma = pltpu.SemaphoreType.DMA
    return [
        pltpu.VMEM((wide_count, rows, width), jnp.bfloat16),
        dma((3, wide_count, 2)),
        dma((wide_count, 2)),
        dma(()),
    ] + sum_scratch(wide_count, rows, width)


def load_padded(source, target, sem):
    filled = source.shape[0]
    copy = pltpu.make_async_copy(source, target.at[pl.ds(0, filled)], sem)
    copy.start()
    if filled < target.shape[0]:
        target[pl.ds(filled, target.shape[0] - filled)] = jnp.zeros(
            (target.shape[0] - filled, target.shape[1]), target.dtype
        )
    return copy


def pair_rows(ref, chip):
    block = ref[pl.ds(2 * chip, 2)]
    return block.reshape(2 * block.shape[1], block.shape[2])


def set_pair(ref, chip, cols, value):
    rows = ref.shape[1]
    ref[2 * chip, :, cols] = value[:rows].astype(ref.dtype)
    ref[2 * chip + 1, :, cols] = value[rows:].astype(ref.dtype)


def tiles(count, tile, body):
    def step(i, carry):
        body(pl.ds(pl.multiple_of(i * tile, tile), tile))
        return carry

    lax.fori_loop(0, count // tile, step, 0)


def geglu_forward_kernel(
    wide_count,
    own,
    expand,
    reduce,
    shift,
    rows_all,
    active_out,
    slope_out,
    gelu_out,
    feed,
    blocks,
    gather_send,
    gather_recv,
    own_sem,
    parts,
    from_mate,
    incoming,
    mate_send,
    mate_recv,
    sum_send,
    sum_recv,
    expand_mat,
    reduce_mat,
    active,
    slope,
    gelu,
    load_sems,
    keep_sems,
):
    sems = (gather_send, gather_recv, mate_send, mate_recv, sum_send, sum_recv, own_sem)
    plane = PlaneExchange(wide_count, own, blocks, parts, from_mate, incoming, sems)
    loads = [
        load_padded(expand.at[0], expand_mat.at[0], load_sems.at[0]),
        load_padded(expand.at[1], expand_mat.at[1], load_sems.at[1]),
        load_padded(reduce, reduce_mat, load_sems.at[2]),
    ]
    plane.greet()
    kept = []
    waiting = list(loads)

    def compute(chip):
        while waiting:
            waiting.pop().wait()

        def units(cols):
            rows = pair_rows(blocks, chip)
            gate = dot(rows, expand_mat[0, cols], ((1,), (1,))) + shift[0:1, cols]
            upper = dot(rows, expand_mat[1, cols], ((1,), (1,))) + shift[1:2, cols]
            factor = math.sqrt(2 / math.pi)
            square = gate * gate
            bend = jnp.tanh(factor * gate * (1 + 0.044715 * square))
            value = 0.5 * gate * (1 + bend)
            pull = 0.5 * (1 + bend) + 0.5 * gate * (1 - bend * bend) * factor * (
                1 + 3 * 0.044715 * square
            )
            set_pair(active, chip, cols, value * upper)
            set_pair(slope, chip, cols, pull * upper)
            set_pair(gelu, chip, cols, value)

        tiles(active.shape[2], 256, units)

        def outputs(cols):
            set_pair(
                parts, chip, cols, dot(pair_rows(active, chip), reduce_mat[:, cols], ((1,), (0,)))
            )

        tiles(parts.shape[2], 256, outputs)
        pair = pl.ds(2 * chip, 2)
        for index, (source, target) in enumerate(
            ((active, active_out), (slope, slope_out), (gelu, gelu_out), (blocks, rows_all))
        ):
            copy = pltpu.make_async_copy(
                source.at[pair], target.at[pair], keep_sems.at[chip, index]
            )
            copy.start()
            kept.append(copy)

    plane.run(compute)
    plane.finish(feed)
    plane.drain()
    for copy in kept:
        copy.wait()


def geglu_forward(wide_count, hidden_low, expand_full, reduce_full, shift):
    rows, width = hidden_low.shape
    padded = shift.shape[1]
    anywhere = pl.BlockSpec(memory_space=pl.ANY)
    vmem = pl.BlockSpec(memory_space=pltpu.VMEM)
    kept = jax.ShapeDtypeStruct((wide_count, rows, padded), jnp.bfloat16)
    scratch = exchange_scratch(wide_count, rows, width) + [
        pltpu.VMEM((2, padded, width), jnp.bfloat16),
        pltpu.VMEM((padded, width), jnp.bfloat16),
        pltpu.VMEM((wide_count, rows, padded), jnp.bfloat16),
        pltpu.VMEM((wide_count, rows, padded), jnp.bfloat16),
        pltpu.VMEM((wide_count, rows, padded), jnp.bfloat16),
        pltpu.SemaphoreType.DMA((3,)),
        pltpu.SemaphoreType.DMA((wide_count // 2, 4)),
    ]
    return pl.pallas_call(
        functools.partial(geglu_forward_kernel, wide_count),
        out_shape=(
            jax.ShapeDtypeStruct((wide_count, rows, width), jnp.bfloat16),
            kept,
            kept,
            kept,
            jax.ShapeDtypeStruct((rows, width), jnp.float32),
        ),
        in_specs=[anywhere, anywhere, anywhere, vmem],
        out_specs=(anywhere, anywhere, anywhere, anywhere, vmem),
        scratch_shapes=scratch,
        compiler_params=pltpu.CompilerParams(
            collective_id=1, has_side_effects=True, vmem_limit_bytes=kernel_memory
        ),
        cost_estimate=pl.CostEstimate(
            flops=6 * wide_count * rows * padded * width, bytes_accessed=200 * 2**20, transcendentals=0
        ),
        name="geglu_forward",
    )(hidden_low, expand_full, reduce_full, shift)


def geglu_backward_kernel(
    wide_count,
    own,
    expand,
    reduce,
    slope_in,
    gelu_in,
    active_in,
    rows_in,
    reduce_part,
    expand_part,
    hidden_grad,
    unit_sums,
    blocks,
    gather_send,
    gather_recv,
    own_sem,
    parts,
    from_mate,
    incoming,
    mate_send,
    mate_recv,
    sum_send,
    sum_recv,
    expand_mat,
    reduce_mat,
    slope,
    gelu,
    active,
    rows_all,
    staged,
    load_sems,
    keep_sems,
):
    sems = (gather_send, gather_recv, mate_send, mate_recv, sum_send, sum_recv, own_sem)
    plane = PlaneExchange(wide_count, own, blocks, parts, from_mate, incoming, sems)
    loads = [
        load_padded(expand.at[0], expand_mat.at[0], load_sems.at[0]),
        load_padded(expand.at[1], expand_mat.at[1], load_sems.at[1]),
        load_padded(reduce, reduce_mat, load_sems.at[2]),
        pltpu.make_async_copy(slope_in, slope, load_sems.at[3]),
        pltpu.make_async_copy(gelu_in, gelu, load_sems.at[4]),
    ]
    late_loads = [
        pltpu.make_async_copy(active_in, active, load_sems.at[5]),
        pltpu.make_async_copy(rows_in, rows_all, load_sems.at[6]),
    ]
    for copy in loads[3:]:
        copy.start()
    unit_sums[...] = jnp.zeros_like(unit_sums)
    plane.greet()
    for copy in late_loads:
        copy.start()
    kept = []
    waiting = list(loads)

    def compute(chip):
        while waiting:
            waiting.pop().wait()

        def units(cols):
            pulled = dot(pair_rows(blocks, chip), reduce_mat[cols], ((1,), (1,)))
            pair = pl.ds(2 * chip, 2)
            shape = pulled.shape
            gate_grad = pulled * slope[pair, :, cols].reshape(shape).astype(jnp.float32)
            upper_grad = pulled * gelu[pair, :, cols].reshape(shape).astype(jnp.float32)
            set_pair(slope, chip, cols, gate_grad)
            set_pair(gelu, chip, cols, upper_grad)
            unit_sums[0:1, cols] += jnp.sum(gate_grad, axis=0, keepdims=True)
            unit_sums[1:2, cols] += jnp.sum(upper_grad, axis=0, keepdims=True)

        tiles(slope.shape[2], 256, units)

        def outputs(cols):
            set_pair(
                parts,
                chip,
                cols,
                dot(pair_rows(slope, chip), expand_mat[0, :, cols], ((1,), (0,)))
                + dot(pair_rows(gelu, chip), expand_mat[1, :, cols], ((1,), (0,))),
            )

        tiles(parts.shape[2], 256, outputs)

    def weight_part(left, right, start, target):
        def work():
            index = len(kept)
            if index >= 2:
                kept[index - 2].wait()
            tokens = left.shape[0] * left.shape[1]
            part = dot(
                left[:, :, start : start + 256].reshape(tokens, 256),
                right[...].reshape(tokens, right.shape[2]),
                ((0,), (0,)),
            )
            staged[index % 2] = part.astype(jnp.bfloat16)
            filled = min(256, target.shape[0] - start)
            copy = pltpu.make_async_copy(
                staged.at[index % 2, pl.ds(0, filled)],
                target.at[pl.ds(start, filled)],
                keep_sems.at[index % 2],
            )
            copy.start()
            kept.append(copy)

        return work

    works = []
    for left, right, target in (
        (active, blocks, reduce_part),
        (slope, rows_all, expand_part.at[0]),
        (gelu, rows_all, expand_part.at[1]),
    ):
        for start in range(0, target.shape[0], 256):
            works.append(weight_part(left, right, start, target))

    def load_late():
        for copy in late_loads:
            copy.wait()

    works[0] = functools.partial(lambda first: (load_late(), first()), works[0])
    plane.run(compute, works)
    plane.finish(hidden_grad)
    plane.drain()
    for copy in kept[-2:]:
        copy.wait()


def geglu_backward(
    wide_count, feed_grad, expand_full, reduce_full, slope, gelu, active, rows_all
):
    rows, width = feed_grad.shape
    padded = slope.shape[2]
    anywhere = pl.BlockSpec(memory_space=pl.ANY)
    vmem = pl.BlockSpec(memory_space=pltpu.VMEM)
    scratch = exchange_scratch(wide_count, rows, width) + [
        pltpu.VMEM((2, padded, width), jnp.bfloat16),
        pltpu.VMEM((padded, width), jnp.bfloat16),
        pltpu.VMEM((wide_count, rows, padded), jnp.bfloat16),
        pltpu.VMEM((wide_count, rows, padded), jnp.bfloat16),
        pltpu.VMEM((wide_count, rows, padded), jnp.bfloat16),
        pltpu.VMEM((wide_count, rows, width), jnp.bfloat16),
        pltpu.VMEM((2, 256, width), jnp.bfloat16),
        pltpu.SemaphoreType.DMA((7,)),
        pltpu.SemaphoreType.DMA((2,)),
    ]
    return pl.pallas_call(
        functools.partial(geglu_backward_kernel, wide_count),
        out_shape=(
            jax.ShapeDtypeStruct(reduce_full.shape, jnp.bfloat16),
            jax.ShapeDtypeStruct(expand_full.shape, jnp.bfloat16),
            jax.ShapeDtypeStruct((rows, width), jnp.float32),
            jax.ShapeDtypeStruct((2, padded), jnp.float32),
        ),
        in_specs=[anywhere] * 7,
        out_specs=(anywhere, anywhere, vmem, vmem),
        scratch_shapes=scratch,
        compiler_params=pltpu.CompilerParams(
            collective_id=2, has_side_effects=True, vmem_limit_bytes=kernel_memory
        ),
        cost_estimate=pl.CostEstimate(
            flops=12 * wide_count * rows * padded * width, bytes_accessed=200 * 2**20, transcendentals=0
        ),
        name="geglu_backward",
    )(feed_grad, expand_full, reduce_full, slope, gelu, active, rows_all)


class LineExchange:
    def __init__(self, narrow_count):
        self.count = narrow_count
        self.mine = lax.axis_index("narrow")
        self.started = []

    def peer(self, offset):
        return (self.mine + offset) % self.count

    def greet(self, extra=0):
        barrier = pltpu.get_barrier_semaphore()
        for offset in range(1, self.count):
            pl.semaphore_signal(
                barrier,
                inc=1,
                device_id={"narrow": self.peer(offset)},
                device_id_type=pl.DeviceIdType.MESH,
            )
        pl.semaphore_wait(barrier, self.count - 1 + extra)

    def copy(self, source, target, send_sem, recv_sem, where):
        return pltpu.make_async_remote_copy(
            src_ref=source,
            dst_ref=target,
            send_sem=send_sem,
            recv_sem=recv_sem,
            device_id={"narrow": where},
            device_id_type=pl.DeviceIdType.MESH,
        )

    def send(self, offset, source, landing, send_sems, recv_sems):
        peer = self.peer(offset)
        copy = self.copy(
            source, landing.at[self.mine], send_sems.at[offset - 1], recv_sems.at[self.mine], peer
        )
        copy.start()
        self.started.append(copy)

    def arrived(self, offset, landing, send_sems, recv_sems):
        peer = self.peer(offset)
        self.copy(
            landing.at[peer], landing.at[peer], send_sems.at[offset - 1], recv_sems.at[peer], peer
        ).wait_recv()

    def drain(self):
        for copy in self.started:
            copy.wait_send()


def greet_plane(plane):
    barrier = pltpu.get_barrier_semaphore()
    for where in (plane.device(-1), plane.device(1), plane.device(0, True)):
        pl.semaphore_signal(barrier, inc=1, device_id=where, device_id_type=pl.DeviceIdType.MESH)


def rotate_lanes(vectors, cosine, signed_sine):
    return vectors * cosine + pltpu.roll(vectors, vectors.shape[1] // 2, 1) * signed_sine


def attention_backward_kernel(
    wide_count,
    narrow_count,
    attended,
    merge,
    mixed,
    queries,
    keys,
    values,
    probs,
    cosine,
    signed_sine,
    triple,
    merge_grad,
    heads_sums,
    merge_sums,
    upstream,
    outbound,
    probs_held,
    keys_turned,
    key_total,
    value_total,
    merge_out,
    merge_in,
    mixed_send,
    mixed_recv,
    merge_send,
    merge_recv,
    load_sems,
    parts,
    from_mate,
    incoming,
    mate_send,
    mate_recv,
    sum_send,
    sum_recv,
):
    sems = (None, None, mate_send, mate_recv, sum_send, sum_recv, None)
    plane = PlaneExchange(wide_count, None, None, parts, from_mate, incoming, sems)
    line = LineExchange(narrow_count)
    rows, width = attended.shape
    own_cols = queries.shape[1]
    heads = own_cols // HDIM
    scale = HDIM ** (-0.5)

    def load(head):
        return pltpu.make_async_copy(
            probs.at[head], probs_held.at[head % 2], load_sems.at[head % 2]
        )

    load(0).start()
    greet_plane(plane)
    line.greet(3)

    def mixed_part(target, where):
        part = dot(
            attended[...],
            merge[pl.ds(pl.multiple_of(where * own_cols, own_cols), own_cols)],
            ((1,), (1,)),
        )
        target[...] = part.astype(jnp.bfloat16)

    for offset in range(1, narrow_count):
        place = line.peer(offset)
        mixed_part(outbound.at[offset - 1], place)
        line.send(offset, outbound.at[offset - 1], upstream, mixed_send, mixed_recv)
    mixed_part(upstream.at[line.mine], line.mine)

    block = parts.shape[1]

    def merge_rows(i, carry):
        cols = pl.ds(pl.multiple_of(i * block, block), block)
        parts[i] = dot(mixed[:, cols], attended[...], ((0,), (0,))).astype(jnp.bfloat16)
        return carry

    lax.fori_loop(0, wide_count, merge_rows, 0)
    for offset in range(plane.ring):
        plane.share(offset)
    merge_sums[...] = jnp.sum(attended[...].astype(jnp.float32), axis=0, keepdims=True)
    plane.first_sums()
    plane.far_sums()
    for offset in range(1, narrow_count):
        line.arrived(offset, upstream, mixed_send, mixed_recv)

    def one_head(head):
        cols = pl.ds(head * HDIM, HDIM)
        load(head).wait()
        if head + 1 < heads:
            load(head + 1).start()
        held = probs_held.at[head % 2]
        keys_turned[...] = keys[:, cols].astype(jnp.float32).T.astype(jnp.bfloat16)
        key_total[...] = jnp.zeros_like(key_total)
        value_total[...] = jnp.zeros_like(value_total)

        def chunk(i, carry):
            here = pl.ds(pl.multiple_of(i * rows, rows), rows)
            weights_low = held[:, here]
            up = upstream[i, :, cols]
            pulled = dot(values[:, cols], up, ((1,), (1,)))
            weights = weights_low.astype(jnp.float32)
            scaled = weights * pulled
            change = (scaled - weights * jnp.sum(scaled, axis=0, keepdims=True)).astype(
                jnp.bfloat16
            )
            key_total[...] += dot(change, queries[here, cols], ((1,), (0,)))
            value_total[...] += dot(weights_low, up, ((1,), (0,)))
            query_grad = dot(keys_turned[...], change, ((1,), (0,))).T * scale
            triple[here, cols] = rotate_lanes(
                query_grad, cosine[here], signed_sine[here]
            ).astype(jnp.bfloat16)
            return carry

        lax.fori_loop(0, narrow_count, chunk, 0)

        def ending(i, carry):
            here = pl.ds(pl.multiple_of(i * rows, rows), rows)
            triple[here, pl.ds(own_cols + head * HDIM, HDIM)] = rotate_lanes(
                key_total[here] * scale, cosine[here], signed_sine[here]
            ).astype(jnp.bfloat16)
            triple[here, pl.ds(2 * own_cols + head * HDIM, HDIM)] = value_total[here].astype(
                jnp.bfloat16
            )
            return carry

        lax.fori_loop(0, narrow_count, ending, 0)

    for head in range(heads):
        one_head(head)
        if head == heads // 2 - 1:
            plane.last_sums()
    total = merge_out.at[...]
    plane.finish(merge_out)
    count = merge_grad.shape[0]

    def z_rows(where):
        return pl.ds(pl.multiple_of(where * count, count), count)

    for offset in range(1, narrow_count):
        line.send(
            offset, total.at[z_rows(line.peer(offset))], merge_in, merge_send, merge_recv
        )

    def column_sums(cols):
        heads_sums[:, cols] = jnp.sum(
            triple[:, cols].astype(jnp.float32), axis=0, keepdims=True
        )

    tiles(3 * own_cols, 256, column_sums)
    summed = merge_out[z_rows(line.mine)].astype(jnp.float32)
    for offset in range(1, narrow_count):
        line.arrived(offset, merge_in, merge_send, merge_recv)
        summed += merge_in[line.peer(offset)].astype(jnp.float32)
    merge_grad[...] = summed
    line.drain()
    plane.drain()


def attention_backward(
    wide_count,
    narrow_count,
    attended_grad,
    merge_full,
    mixed,
    queries,
    keys,
    values,
    probs,
    cosine,
    signed_sine,
):
    rows, width = attended_grad.shape
    bucket, own_cols = queries.shape
    block = width // wide_count
    count = block // narrow_count
    anywhere = pl.BlockSpec(memory_space=pl.ANY)
    vmem = pl.BlockSpec(memory_space=pltpu.VMEM)
    dma = pltpu.SemaphoreType.DMA
    return pl.pallas_call(
        functools.partial(attention_backward_kernel, wide_count, narrow_count),
        out_shape=(
            jax.ShapeDtypeStruct((bucket, 3 * own_cols), jnp.bfloat16),
            jax.ShapeDtypeStruct((count, width), jnp.float32),
            jax.ShapeDtypeStruct((1, 3 * own_cols), jnp.float32),
            jax.ShapeDtypeStruct((1, width), jnp.float32),
        ),
        in_specs=[vmem] * 6 + [anywhere] + [vmem] * 2,
        out_specs=(vmem, vmem, vmem, vmem),
        scratch_shapes=[
            pltpu.VMEM((narrow_count, rows, own_cols), jnp.bfloat16),
            pltpu.VMEM((narrow_count - 1, rows, own_cols), jnp.bfloat16),
            pltpu.VMEM((2, bucket, bucket), jnp.bfloat16),
            pltpu.VMEM((HDIM, bucket), jnp.bfloat16),
            pltpu.VMEM((bucket, HDIM), jnp.float32),
            pltpu.VMEM((bucket, HDIM), jnp.float32),
            pltpu.VMEM((block, width), jnp.bfloat16),
            pltpu.VMEM((narrow_count, count, width), jnp.bfloat16),
            dma((narrow_count - 1,)),
            dma((narrow_count,)),
            dma((narrow_count - 1,)),
            dma((narrow_count,)),
            dma((2,)),
        ]
        + sum_scratch(wide_count, block, width),
        compiler_params=pltpu.CompilerParams(
            collective_id=3, has_side_effects=True, vmem_limit_bytes=kernel_memory
        ),
        cost_estimate=pl.CostEstimate(
            flops=60 * 10**9, bytes_accessed=200 * 2**20, transcendentals=0
        ),
        name="attention_backward",
    )(
        attended_grad, merge_full, mixed, queries, keys, values, probs, cosine, signed_sine
    )


def input_backward_kernel(
    wide_count,
    narrow_count,
    inputs,
    triple,
    heads_mat,
    small,
    input_part,
    heads_grad,
    small_out,
    line_parts,
    line_in,
    heads_out,
    heads_in,
    small_wide,
    small_sum,
    small_line,
    line_send,
    line_recv,
    heads_send,
    heads_recv,
    wide_send,
    wide_recv,
    small_send,
    small_recv,
    parts,
    from_mate,
    incoming,
    mate_send,
    mate_recv,
    sum_send,
    sum_recv,
):
    sems = (None, None, mate_send, mate_recv, sum_send, sum_recv, None)
    plane = PlaneExchange(wide_count, None, None, parts, from_mate, incoming, sems)
    line = LineExchange(narrow_count)
    rows, width = input_part.shape
    here = line.mine
    last = narrow_count - 1
    place = lax.axis_index("wide")

    def wide_peer(offset):
        return (place + offset) % wide_count

    barrier = pltpu.get_barrier_semaphore()
    for offset in range(1, wide_count):
        pl.semaphore_signal(
            barrier,
            inc=1,
            device_id={"wide": wide_peer(offset)},
            device_id_type=pl.DeviceIdType.MESH,
        )
    line.greet(wide_count - 1)

    def small_copy(offset, source, slot):
        return pltpu.make_async_remote_copy(
            src_ref=source,
            dst_ref=small_wide.at[slot],
            send_sem=wide_send.at[offset - 1],
            recv_sem=wide_recv.at[slot],
            device_id={"wide": wide_peer(offset)},
            device_id_type=pl.DeviceIdType.MESH,
        )

    small_copies = [
        small_copy(offset, small.at[wide_peer(offset)], place) for offset in range(1, wide_count)
    ]
    for copy in small_copies:
        copy.start()

    def input_cols(cols):
        part = dot(triple[...], heads_mat[cols], ((1,), (1,)))
        for index in range(narrow_count):
            line_parts[index, :, cols] = part[index * rows : (index + 1) * rows].astype(
                jnp.bfloat16
            )

    tiles(width, 256, input_cols)

    def line_copy(way, offset):
        target = here + offset if way == 0 else here - offset
        return line.copy(
            line_parts.at[target],
            line_in.at[way, offset - 1],
            line_send.at[way, offset - 1],
            line_recv.at[way, offset - 1],
            here + 1 if way == 0 else here - 1,
        )

    def line_arrived(way, offset):
        landing = line_in.at[way, offset]
        line.copy(
            landing, landing, line_send.at[way, offset], line_recv.at[way, offset], here
        ).wait_recv()

    def add_line(way, offset, slot):
        def chunk(i, carry):
            some = pl.ds(pl.multiple_of(i * 16, 16), 16)
            line_parts[slot, some] = (
                line_parts[slot, some].astype(jnp.float32)
                + line_in[way, offset, some].astype(jnp.float32)
            ).astype(jnp.bfloat16)
            return carry

        lax.fori_loop(0, rows // 16, chunk, 0)

    def line_step(offset):
        for way in range(2):
            reaches = here + offset <= last if way == 0 else here - offset >= 0
            follows = here > 0 if way == 0 else here < last

            @pl.when(reaches)
            def _():
                if offset < last:

                    @pl.when(follows)
                    def _():
                        line_arrived(way, offset)
                        add_line(way, offset, here + offset if way == 0 else here - offset)

                line_copy(way, offset).start()

    line_step(last)

    block = parts.shape[1]

    def heads_rows(i, carry):
        cols = pl.ds(pl.multiple_of(i * block, block), block)
        parts[i] = dot(inputs[:, cols], triple[...], ((0,), (0,))).astype(jnp.bfloat16)
        return carry

    lax.fori_loop(0, wide_count, heads_rows, 0)
    for offset in range(plane.ring):
        plane.share(offset)
    for offset in range(last - 1, last // 2, -1):
        line_step(offset)
    plane.first_sums()
    plane.far_sums()

    for offset in range(1, wide_count):
        peer = wide_peer(offset)
        small_copy(offset, small_wide.at[peer], peer).wait_recv()
    small_wide[place] = small[place]
    total = small_wide[0]
    for index in range(1, wide_count):
        total += small_wide[index]
    small_sum[...] = total
    for offset in range(1, narrow_count):
        line.send(offset, small_sum.at[line.peer(offset)], small_line, small_send, small_recv)

    plane.last_sums()
    for offset in range(last // 2, 0, -1):
        line_step(offset)
    plane.finish(heads_out)
    count = heads_grad.shape[0]

    def z_rows(where):
        return pl.ds(pl.multiple_of(where * count, count), count)

    for offset in range(1, narrow_count):
        line.send(
            offset, heads_out.at[z_rows(line.peer(offset))], heads_in, heads_send, heads_recv
        )
    heads_in[line.mine] = heads_out[z_rows(line.mine)]
    small_line[line.mine] = small_sum[line.mine]
    for offset in range(1, narrow_count):
        line.arrived(offset, small_line, small_send, small_recv)
    result = small_line[0]
    for index in range(1, narrow_count):
        result += small_line[index]
    small_out[...] = result

    def own_rows(i, carry):
        some = pl.ds(pl.multiple_of(i * 16, 16), 16)
        input_part[some] = line_parts[here, some].astype(jnp.float32)
        return carry

    lax.fori_loop(0, rows // 16, own_rows, 0)
    for way in range(2):
        follows = here > 0 if way == 0 else here < last

        @pl.when(follows)
        def _():
            line_arrived(way, 0)

            def chunk(i, carry):
                some = pl.ds(pl.multiple_of(i * 16, 16), 16)
                input_part[some] += line_in[way, 0, some].astype(jnp.float32)
                return carry

            lax.fori_loop(0, rows // 16, chunk, 0)

    for offset in range(1, narrow_count):
        line.arrived(offset, heads_in, heads_send, heads_recv)
    own_cols = triple.shape[1] // 3
    for index in range(narrow_count):
        for which in range(3):
            start = (which * narrow_count + index) * own_cols
            heads_grad[:, start : start + own_cols] = heads_in[
                index, :, which * own_cols : (which + 1) * own_cols
            ].astype(jnp.float32)
    for offset in range(1, narrow_count):
        for way in range(2):
            reaches = here + offset <= last if way == 0 else here - offset >= 0

            @pl.when(reaches)
            def _():
                line_copy(way, offset).wait_send()

    for copy in small_copies:
        copy.wait_send()
    line.drain()
    plane.drain()


def input_backward(wide_count, narrow_count, inputs, triple_grad, heads_mat, small):
    bucket, width = inputs.shape
    rows = bucket // narrow_count
    columns = triple_grad.shape[1]
    block = width // wide_count
    count = block // narrow_count
    vmem = pl.BlockSpec(memory_space=pltpu.VMEM)
    dma = pltpu.SemaphoreType.DMA
    lines = small.shape[2]
    return pl.pallas_call(
        functools.partial(input_backward_kernel, wide_count, narrow_count),
        out_shape=(
            jax.ShapeDtypeStruct((rows, width), jnp.float32),
            jax.ShapeDtypeStruct((count, narrow_count * columns), jnp.float32),
            jax.ShapeDtypeStruct((lines, 128), jnp.float32),
        ),
        in_specs=[vmem] * 4,
        out_specs=(vmem, vmem, vmem),
        scratch_shapes=[
            pltpu.VMEM((narrow_count, rows, width), jnp.bfloat16),
            pltpu.VMEM((2, narrow_count - 1, rows, width), jnp.bfloat16),
            pltpu.VMEM((block, columns), jnp.bfloat16),
            pltpu.VMEM((narrow_count, count, columns), jnp.bfloat16),
            pltpu.VMEM((wide_count, narrow_count, lines, 128), jnp.float32),
            pltpu.VMEM((narrow_count, lines, 128), jnp.float32),
            pltpu.VMEM((narrow_count, lines, 128), jnp.float32),
            dma((2, narrow_count - 1)),
            dma((2, narrow_count - 1)),
            dma((narrow_count - 1,)),
            dma((narrow_count,)),
            dma((wide_count - 1,)),
            dma((wide_count,)),
            dma((narrow_count - 1,)),
            dma((narrow_count,)),
        ]
        + sum_scratch(wide_count, block, columns),
        compiler_params=pltpu.CompilerParams(
            collective_id=4, has_side_effects=True, vmem_limit_bytes=kernel_memory
        ),
        cost_estimate=pl.CostEstimate(
            flops=80 * 10**9, bytes_accessed=200 * 2**20, transcendentals=0
        ),
        name="input_backward",
    )(inputs, triple_grad, heads_mat, small)


def greet_all(wide_count, narrow_count):
    barrier = pltpu.get_barrier_semaphore()
    for axis, count in (("wide", wide_count), ("narrow", narrow_count)):
        place = lax.axis_index(axis)
        for offset in range(1, count):
            pl.semaphore_signal(
                barrier,
                inc=1,
                device_id={axis: (place + offset) % count},
                device_id_type=pl.DeviceIdType.MESH,
            )
    pl.semaphore_wait(barrier, wide_count + narrow_count - 2)


def gather_kernel(
    wide_count,
    narrow_count,
    own,
    heads_weight,
    merge_weight,
    small,
    rows_out,
    heads_out,
    merge_out,
    small_out,
    triple,
    rows_all,
    heads_all,
    merge_all,
    small_all,
    rows_send,
    rows_recv,
    heads_send,
    heads_recv,
    merge_send,
    merge_recv,
    small_send,
    small_recv,
    wide_send,
    wide_recv,
    local_sems,
    out_sems,
    heads_ring_send,
    heads_ring_recv,
    merge_ring_send,
    merge_ring_recv,
):
    def ring_of(blocks, send, recv):
        sems = (send, recv, None, None, None, None, None)
        return PlaneExchange(wide_count, None, blocks, blocks, None, None, sems)

    heads_ring = ring_of(heads_all, heads_ring_send, heads_ring_recv)
    merge_ring = ring_of(merge_all, merge_ring_send, merge_ring_recv)
    line = LineExchange(narrow_count)
    here = line.mine
    last = narrow_count - 1
    place = lax.axis_index("wide")
    slot = heads_ring.slot(0)
    rows, width = own.shape
    count = heads_weight.shape[0]
    columns = heads_all.shape[2]
    own_cols = columns // 3

    def z_rows(where):
        return pl.ds(pl.multiple_of(where * count, count), count)

    def head_cols(which, where):
        start = which * narrow_count * own_cols + where * own_cols
        return pl.ds(pl.multiple_of(start, own_cols), own_cols)

    def line_rows(way, block):
        source = rows_all.at[block]
        return line.copy(
            source,
            source,
            rows_send.at[way, block],
            rows_recv.at[block],
            here + 1 if way == 0 else here - 1,
        )

    def goes(way):
        return here < last if way == 0 else here > 0

    def has(way, step):
        return here - step >= 0 if way == 0 else here + step <= last

    def block_of(way, step):
        return here - step if way == 0 else here + step

    keep_rows = pltpu.make_async_copy(own, rows_all.at[here], local_sems.at[0])
    keep_rows.start()
    keeps = [
        pltpu.make_async_copy(
            heads_weight.at[:, head_cols(which, here)],
            heads_all.at[slot, z_rows(here), pl.ds(which * own_cols, own_cols)],
            local_sems.at[2 + which],
        )
        for which in range(3)
    ]
    keep_merge = pltpu.make_async_copy(
        merge_weight, merge_all.at[slot, z_rows(here)], local_sems.at[1]
    )
    for copy in keeps + [keep_merge]:
        copy.start()
    small_all[place, here] = small[...]
    greet_all(wide_count, narrow_count)

    def heads_copy(offset, which, where, sender):
        return line.copy(
            heads_weight.at[:, head_cols(which, where)],
            heads_all.at[slot, z_rows(sender), pl.ds(which * own_cols, own_cols)],
            heads_send.at[offset - 1, which],
            heads_recv.at[sender, which],
            where,
        )

    def merge_copy(offset, where, sender):
        return line.copy(
            merge_weight,
            merge_all.at[slot, z_rows(sender)],
            merge_send.at[offset - 1],
            merge_recv.at[sender],
            where,
        )

    def small_copy(offset, where, sender):
        return line.copy(
            small,
            small_all.at[place, sender],
            small_send.at[offset - 1],
            small_recv.at[sender],
            where,
        )

    started = []

    def start(copy):
        copy.start()
        started.append(copy)

    for offset in range(1, narrow_count):
        for which in range(3):
            start(heads_copy(offset, which, line.peer(offset), here))
    for offset in range(1, narrow_count):
        start(small_copy(offset, line.peer(offset), here))
    keep_rows.wait()
    for way in range(2):

        @pl.when(goes(way))
        def _():
            line_rows(way, here).start()

    for offset in range(1, narrow_count):
        start(merge_copy(offset, line.peer(offset), here))

    for copy in keeps:
        copy.wait()
    for offset in range(1, narrow_count):
        for which in range(3):
            heads_copy(offset, which, line.peer(offset), line.peer(offset)).wait_recv()
    heads_ring.send_own()
    for offset in range(1, narrow_count):
        small_copy(offset, line.peer(offset), line.peer(offset)).wait_recv()

    def wide_copy(offset, sender):
        return pltpu.make_async_remote_copy(
            src_ref=small_all.at[sender],
            dst_ref=small_all.at[sender],
            send_sem=wide_send.at[offset - 1],
            recv_sem=wide_recv.at[sender],
            device_id={"wide": (place + offset) % wide_count},
            device_id_type=pl.DeviceIdType.MESH,
        )

    for offset in range(1, wide_count):
        start(wide_copy(offset, place))

    def rows_step(step):
        for way in range(2):

            @pl.when(has(way, step))
            def _():
                line_rows(way, block_of(way, step)).wait_recv()

                @pl.when(goes(way))
                def _():
                    line_rows(way, block_of(way, step)).start()

    def project(block):
        def cols_step(cols):
            weight = heads_all[:, :, cols].reshape(width, cols.size)
            triple[pl.ds(pl.multiple_of(block * rows, rows), rows), cols] = dot(
                rows_all[block], weight, ((1,), (0,))
            )

        tiles(columns, 256, cols_step)

    def project_step(step):
        for way in range(2):

            @pl.when(has(way, step))
            def _():
                project(block_of(way, step))

    def gather(ring, distance):
        ring.receive(distance)
        ring.receive_mate(-distance)
        if distance < ring.far:
            ring.receive_mate(distance)

    outs = []

    def keep_out(source, target):
        copy = pltpu.make_async_copy(source, target, out_sems.at[len(outs)])
        copy.start()
        outs.append(copy)

    rows_step(1)
    heads_ring.receive_mate(0)
    for distance in range(1, heads_ring.far):
        gather(heads_ring, distance)
    keep_merge.wait()
    for offset in range(1, narrow_count):
        merge_copy(offset, line.peer(offset), line.peer(offset)).wait_recv()
    merge_ring.send_own()
    gather(heads_ring, heads_ring.far)
    keep_out(heads_all, heads_out)
    project(here)
    for step in range(2, narrow_count):
        rows_step(step)
        project_step(step - 1)
        if step == 2:
            merge_ring.receive_mate(0)
            for distance in range(1, merge_ring.far):
                gather(merge_ring, distance)
    gather(merge_ring, merge_ring.far)
    keep_out(merge_all, merge_out)
    project_step(last)
    keep_out(rows_all, rows_out)
    for offset in range(1, wide_count):
        wide_copy(offset, (place + offset) % wide_count).wait_recv()
    keep_out(small_all, small_out)
    for way in range(2):
        for step in range(narrow_count):

            @pl.when(has(way, step) & goes(way))
            def _():
                line_rows(way, block_of(way, step)).wait_send()

    for copy in started:
        copy.wait_send()
    heads_ring.drain()
    merge_ring.drain()
    for copy in outs:
        copy.wait()


def gather_front(wide_count, narrow_count, layer_input, heads_weight, merge_weight, small):
    rows, width = layer_input.shape
    count, all_columns = heads_weight.shape
    columns = all_columns // narrow_count
    block = count * narrow_count
    anywhere = pl.BlockSpec(memory_space=pl.ANY)
    vmem = pl.BlockSpec(memory_space=pltpu.VMEM)
    dma = pltpu.SemaphoreType.DMA
    lines = small.shape[0]
    shapes = (
        (narrow_count, rows, width),
        (wide_count, block, columns),
        (wide_count, block, width),
        (wide_count, narrow_count, lines, 128),
    )
    far = narrow_count - 1
    return pl.pallas_call(
        functools.partial(gather_kernel, wide_count, narrow_count),
        out_shape=tuple(jax.ShapeDtypeStruct(shape, jnp.bfloat16) for shape in shapes)
        + (jax.ShapeDtypeStruct((narrow_count * rows, columns), jnp.float32),),
        in_specs=[anywhere, anywhere, anywhere, vmem],
        out_specs=(anywhere, anywhere, anywhere, anywhere, vmem),
        scratch_shapes=[pltpu.VMEM(shape, jnp.bfloat16) for shape in shapes]
        + [
            dma((2, narrow_count)),
            dma((narrow_count,)),
            dma((far, 3)),
            dma((narrow_count, 3)),
            dma((far,)),
            dma((narrow_count,)),
            dma((far,)),
            dma((narrow_count,)),
            dma((wide_count - 1,)),
            dma((wide_count,)),
            dma((5,)),
            dma((4,)),
            dma((3, wide_count, 2)),
            dma((wide_count, 2)),
            dma((3, wide_count, 2)),
            dma((wide_count, 2)),
        ],
        compiler_params=pltpu.CompilerParams(
            collective_id=5, has_side_effects=True, vmem_limit_bytes=kernel_memory
        ),
        cost_estimate=pl.CostEstimate(
            flops=80 * 10**9, bytes_accessed=200 * 2**20, transcendentals=0
        ),
        name="gather_front",
    )(layer_input, heads_weight, merge_weight, small)


def attention_forward_kernel(
    narrow_count,
    triple,
    heads_shift,
    cosine,
    signed_sine,
    first_query,
    last_query,
    own,
    merge,
    merge_shift,
    gain,
    shift,
    queries,
    keys,
    values,
    probs,
    mixed_out,
    hidden,
    hidden_low,
    normed,
    inv_std,
    merge_mat,
    probs_held,
    values_turned,
    outbound,
    mixed,
    mixed_send,
    mixed_recv,
    local_sems,
):
    line = LineExchange(narrow_count)
    bucket, own_cols = queries.shape
    rows, width = own.shape
    heads = own_cols // HDIM
    scale = HDIM ** (-0.5)
    load_merge = pltpu.make_async_copy(merge, merge_mat, local_sems.at[2])
    load_merge.start()
    line.greet()

    def keep(head):
        return pltpu.make_async_copy(
            probs_held.at[head % 2], probs.at[head], local_sems.at[head % 2]
        )

    def mixed_copy(head, offset, where, sender):
        cols = pl.ds(pl.multiple_of(sender * own_cols + head * HDIM, HDIM), HDIM)
        return line.copy(
            outbound.at[where, :, pl.ds(head * HDIM, HDIM)],
            mixed.at[:, cols],
            mixed_send.at[offset - 1, head],
            mixed_recv.at[sender, head],
            where,
        )

    started = []
    for head in range(heads):
        cols = pl.ds(head * HDIM, HDIM)

        def turn(i, carry):
            here = pl.ds(pl.multiple_of(i * rows, rows), rows)
            for which, target in enumerate((queries, keys, values)):
                wanted = pl.ds(which * own_cols + head * HDIM, HDIM)
                part = triple[here, wanted] + heads_shift[:, wanted]
                if which < 2:
                    part = rotate_lanes(part, cosine[here], -signed_sine[here])
                else:
                    values_turned[:, here] = part.T.astype(jnp.bfloat16)
                target[here, cols] = part.astype(jnp.bfloat16)
            return carry

        lax.fori_loop(0, narrow_count, turn, 0)
        if head >= 2:
            keep(head - 2).wait()
        held = probs_held.at[head % 2]

        def chunk(i, carry):
            here = pl.ds(pl.multiple_of(i * rows, rows), rows)
            scores = dot(keys[:, cols], queries[here, cols], ((1,), (1,))) * scale
            token = i * rows + lax.broadcasted_iota(jnp.int32, (bucket, rows), 1)
            seen = (token >= first_query[...]) & (token <= last_query[...])
            scores = jnp.where(seen, scores, masked_value)
            expo = jnp.exp(scores - jnp.max(scores, axis=0, keepdims=True))
            weights = (expo * (1 / jnp.sum(expo, axis=0, keepdims=True))).astype(jnp.bfloat16)
            held[:, here] = weights
            mixed_part = dot(values_turned[...], weights, ((1,), (0,)))
            outbound[i, :, cols] = mixed_part.T.astype(jnp.bfloat16)
            return carry

        lax.fori_loop(0, narrow_count, chunk, 0)
        keep(head).start()
        for offset in range(1, narrow_count):
            copy = mixed_copy(head, offset, line.peer(offset), line.mine)
            copy.start()
            started.append(copy)
    own_mixed = pltpu.make_async_copy(
        outbound.at[line.mine],
        mixed.at[:, pl.ds(pl.multiple_of(line.mine * own_cols, own_cols), own_cols)],
        local_sems.at[3],
    )
    own_mixed.start()
    own_mixed.wait()
    load_merge.wait()
    for offset in range(1, narrow_count):
        for head in range(heads):
            mixed_copy(head, offset, line.peer(offset), line.peer(offset)).wait_recv()
    mixed_out[...] = mixed[...]

    def merge_cols(cols):
        hidden[:, cols] = (
            residual_scale * own[:, cols].astype(jnp.float32)
            + dot(mixed[...], merge_mat[:, cols], ((1,), (0,)))
            + merge_shift[:, cols]
        )

    tiles(width, 256, merge_cols)

    def norm_rows(i, carry):
        some = pl.ds(pl.multiple_of(i * 16, 16), 16)
        result, centred, inverse = normalize(hidden[some], gain[...], shift[...])
        hidden[some] = result
        hidden_low[some] = result.astype(jnp.bfloat16)
        normed[some] = centred
        inv_std[some] = inverse
        return carry

    lax.fori_loop(0, rows // 16, norm_rows, 0)
    for head in range(max(heads - 2, 0), heads):
        keep(head).wait()
    for copy in started:
        copy.wait_send()


def attention_forward(
    narrow_count,
    triple,
    heads_shift,
    cosine,
    signed_sine,
    first_query,
    last_query,
    layer_input,
    merge_full,
    merge_shift,
    gain,
    shift,
):
    bucket, columns = triple.shape
    rows, width = layer_input.shape
    own_cols = columns // 3
    heads = own_cols // HDIM
    anywhere = pl.BlockSpec(memory_space=pl.ANY)
    vmem = pl.BlockSpec(memory_space=pltpu.VMEM)
    dma = pltpu.SemaphoreType.DMA

    def low_shape(*shape):
        return jax.ShapeDtypeStruct(shape, jnp.bfloat16)

    def wide_shape(*shape):
        return jax.ShapeDtypeStruct(shape, jnp.float32)

    return pl.pallas_call(
        functools.partial(attention_forward_kernel, narrow_count),
        out_shape=(
            low_shape(bucket, own_cols),
            low_shape(bucket, own_cols),
            low_shape(bucket, own_cols),
            low_shape(heads, bucket, bucket),
            low_shape(rows, width),
            wide_shape(rows, width),
            low_shape(rows, width),
            wide_shape(rows, width),
            wide_shape(rows, 1),
        ),
        in_specs=[vmem] * 7 + [anywhere] + [vmem] * 3,
        out_specs=(vmem, vmem, vmem, anywhere) + (vmem,) * 5,
        scratch_shapes=[
            pltpu.VMEM((width, width), jnp.bfloat16),
            pltpu.VMEM((2, bucket, bucket), jnp.bfloat16),
            pltpu.VMEM((HDIM, bucket), jnp.bfloat16),
            pltpu.VMEM((narrow_count, rows, own_cols), jnp.bfloat16),
            pltpu.VMEM((rows, width), jnp.bfloat16),
            dma((narrow_count - 1, heads)),
            dma((narrow_count, heads)),
            dma((4,)),
        ],
        compiler_params=pltpu.CompilerParams(
            collective_id=6, has_side_effects=True, vmem_limit_bytes=kernel_memory
        ),
        cost_estimate=pl.CostEstimate(
            flops=60 * 10**9, bytes_accessed=200 * 2**20, transcendentals=0
        ),
        name="attention_forward",
    )(
        triple,
        heads_shift,
        cosine,
        signed_sine,
        first_query,
        last_query,
        layer_input,
        merge_full,
        merge_shift,
        gain,
        shift,
    )


def shards(
    layer_input,
    heads_weight,
    heads_bias,
    merge_weight,
    merge_bias,
    norm_gains,
    norm_shifts,
    expand_weight,
    expand_bias,
    reduce_weight,
    reduce_bias,
    joined,
    prefix,
    cotangent,
):
    tok_rows, model_width = layer_input.shape
    wide_count = lax.axis_size("wide")
    narrow_count = lax.axis_size("narrow")
    count = wide_count * narrow_count
    bucket_len = tok_rows * narrow_count
    own_heads = HEADS // narrow_count
    own_cols = own_heads * HDIM
    share = expand_weight.shape[2]
    joined_flag = joined[0]
    prefix_pair = prefix[0]
    narrow_index = lax.axis_index("narrow")
    positions = jnp.arange(bucket_len, dtype=jnp.int32)
    second_seq, local_pos, prefix_len = layout(positions, joined_flag, prefix_pair, bucket_len)
    cosine, sine_table = rotary_tables(local_pos, HDIM)
    first_query = jnp.where(local_pos < prefix_len, positions - local_pos, positions)
    last_query = jnp.where(
        (joined_flag == 1) | (second_seq == 1), bucket_len - 1, bucket_len // 2 - 1
    )

    smalls = (heads_bias, merge_bias, norm_gains, norm_shifts, expand_bias, reduce_bias)
    rows_input, heads_mat, merge_full, small_all, triple = gather_front(
        wide_count, narrow_count, layer_input, heads_weight, merge_weight, pack_small(smalls)
    )
    rows_input = rows_input.reshape(bucket_len, model_width)
    heads_mat = heads_mat.reshape(model_width, 3 * own_cols)
    merge_full = merge_full.reshape(model_width, model_width)
    heads_shift, merge_shift, gains, shifts, expand_shift, reduce_shift = unpack_small(
        small_all, smalls
    )
    own_shift = lax.dynamic_index_in_dim(
        heads_shift.reshape(3, narrow_count, own_cols), narrow_index, 1, keepdims=False
    ).reshape(1, -1)
    cosine_wide = jnp.concatenate([cosine, cosine], axis=1)
    signed_sine = jnp.concatenate([sine_table, -sine_table], axis=1)
    (
        queries,
        keys,
        values,
        probs_low,
        mixed,
        hidden,
        hidden_low,
        normed_one,
        inv_one,
    ) = attention_forward(
        narrow_count,
        triple,
        own_shift,
        cosine_wide,
        signed_sine,
        first_query.reshape(-1, 1),
        last_query.reshape(-1, 1),
        layer_input,
        merge_full,
        merge_shift.reshape(1, -1),
        gains[0].reshape(1, -1),
        shifts[0].reshape(1, -1),
    )

    tile_rows = -share % 16
    padded = -(-share // 256) * 256
    expand_full = lax.all_gather(
        jnp.pad(expand_weight.transpose(1, 2, 0), ((0, 0), (0, tile_rows), (0, 0))),
        "narrow",
        axis=2,
        tiled=True,
    )
    reduce_weight, _ = lax.optimization_barrier((reduce_weight, small_all))
    reduce_full = lax.all_gather(
        jnp.pad(reduce_weight, ((0, tile_rows), (0, 0))), "narrow", axis=1, tiled=True
    )
    rows_all, active, slope, gelu, feed_sum = geglu_forward(
        wide_count,
        hidden_low,
        expand_full,
        reduce_full,
        jnp.pad(expand_shift, ((0, 0), (0, padded - share))),
    )
    feed = feed_sum + reduce_shift
    output_float, normed_two, inv_two = normalize(
        residual_scale * hidden + feed, gains[1], shifts[1]
    )
    layer_output = low(output_float)

    grad_out = cotangent.astype(jnp.float32)
    gain_two_grad = jnp.sum(grad_out * normed_two, axis=0)
    shift_two_grad = jnp.sum(grad_out, axis=0)
    sum_two_grad = normalize_back(grad_out, normed_two, inv_two, gains[1])
    feed_grad = low(sum_two_grad)
    reduce_part, expand_part, hidden_part, unit_sums = geglu_backward(
        wide_count, feed_grad, expand_full, reduce_full, slope, gelu, active, rows_all
    )
    reduce_weight_gradient = lax.psum_scatter(
        reduce_part, "narrow", scatter_dimension=1, tiled=True
    )[:share].astype(jnp.float32)
    expand_weight_gradient = (
        lax.psum_scatter(expand_part, "narrow", scatter_dimension=2, tiled=True)[:, :share]
        .astype(jnp.float32)
        .transpose(2, 0, 1)
    )
    hidden_grad = residual_scale * sum_two_grad + hidden_part
    gain_one_grad = jnp.sum(hidden_grad * normed_one, axis=0)
    shift_one_grad = jnp.sum(hidden_grad, axis=0)
    sum_one_grad = normalize_back(hidden_grad, normed_one, inv_one, gains[0])
    attended_grad = low(sum_one_grad)
    triple_grad, merge_weight_gradient, heads_sums, merge_sums = attention_backward(
        wide_count,
        narrow_count,
        attended_grad,
        merge_full,
        mixed,
        queries,
        keys,
        values,
        probs_low,
        cosine_wide,
        signed_sine,
    )

    mine_narrow = (jnp.arange(narrow_count) == narrow_index).astype(jnp.float32)
    mine_wide = (jnp.arange(wide_count) == lax.axis_index("wide")).astype(jnp.float32)
    heads_sums = heads_sums.reshape(3, 1, own_cols)
    heads_sums = (heads_sums * mine_narrow[None, :, None]).reshape(count, -1)
    merge_sums = merge_sums.reshape(count, -1)
    norm_sums = (
        jnp.stack([gain_one_grad, gain_two_grad, shift_one_grad, shift_two_grad])
        .reshape(4, count, -1)
        .transpose(1, 0, 2)
        .reshape(count, -1)
    )
    expand_sums = unit_sums[:, :share]
    expand_sums = (
        expand_sums.reshape(2, narrow_count, -1).transpose(1, 0, 2).reshape(1, narrow_count, -1)
        * mine_wide[:, None, None]
    ).reshape(count, -1)
    reduce_sums = jnp.sum(feed_grad, axis=0, dtype=jnp.float32).reshape(1, narrow_count, -1)
    reduce_sums = jnp.broadcast_to(
        reduce_sums, (wide_count, narrow_count, reduce_sums.shape[2])
    ).reshape(count, -1)
    pieces = (heads_sums, merge_sums, norm_sums, expand_sums, reduce_sums)
    packed = jnp.concatenate(pieces, axis=1)
    packed = jnp.pad(packed, ((0, 0), (0, -packed.shape[1] % 1024)))
    input_part, heads_weight_gradient, summed = input_backward(
        wide_count,
        narrow_count,
        rows_input,
        triple_grad,
        heads_mat,
        packed.reshape(wide_count, narrow_count, -1, 128),
    )
    input_gradient = residual_scale * sum_one_grad + input_part
    summed = summed.reshape(-1)
    ends = []
    start = 0
    for piece in pieces:
        ends.append(summed[start : start + piece.shape[1]])
        start += piece.shape[1]
    norm_ends = ends[2].reshape(4, -1)
    return (
        layer_output,
        input_gradient,
        heads_weight_gradient,
        ends[0],
        merge_weight_gradient,
        ends[1],
        norm_ends[:2],
        norm_ends[2:],
        expand_weight_gradient,
        ends[3].reshape(2, -1),
        reduce_weight_gradient,
        ends[4],
    )


def solution(mesh):
    return jax.shard_map(
        shards,
        mesh=mesh,
        in_specs=(
            P(("wide", "narrow"), None),
            P(("wide", "narrow"), None),
            P(("wide", "narrow")),
            P(("wide", "narrow"), None),
            P(("wide", "narrow")),
            P(None, ("wide", "narrow")),
            P(None, ("wide", "narrow")),
            P("narrow", None, "wide"),
            P(None, ("wide", "narrow")),
            P("wide", "narrow"),
            P("narrow"),
            P("wide"),
            P("wide", None),
            P(("wide", "narrow"), None),
        ),
        out_specs=(
            P(("wide", "narrow"), None),
            P(("wide", "narrow"), None),
            P(("wide", "narrow"), None),
            P(("wide", "narrow")),
            P(("wide", "narrow"), None),
            P(("wide", "narrow")),
            P(None, ("wide", "narrow")),
            P(None, ("wide", "narrow")),
            P("narrow", None, "wide"),
            P(None, ("wide", "narrow")),
            P("wide", "narrow"),
            P("narrow"),
        ),
        check_vma=False,
    )
```

```python
import functools
import math

import jax
import jax.numpy as jnp
from jax import lax
from jax.experimental import pallas as pl
from jax.experimental.pallas import tpu as pltpu
from jax.sharding import PartitionSpec as P

HEADS = 16
HDIM = 128


residual_scale = 48.0**0.5
norm_eps = 1e-05
masked_value = -1e30
kernel_memory = 60 * 2**20


def layout(positions, joined_flag, prefix_pair, bucket_len):
    halfway = bucket_len // 2
    second_seq = (positions >= halfway).astype(jnp.int32) * (1 - joined_flag)
    local_pos = positions - second_seq * halfway
    prefix_len = jnp.where(
        joined_flag == 1,
        prefix_pair[0] + prefix_pair[1],
        jnp.where(second_seq == 1, prefix_pair[1], prefix_pair[0]),
    )
    return (second_seq, local_pos, prefix_len)


def rotary_tables(local_pos, head_size):
    halfway = head_size // 2
    inverse = 10000.0 ** (-(2.0 * jnp.arange(halfway).astype(jnp.float32)) / head_size)
    angles = local_pos.astype(jnp.float32)[:, None] * inverse[None, :]
    return (jnp.cos(angles), jnp.sin(angles))


def normalize(values, gain, shift):
    centre = jnp.mean(values, axis=-1, keepdims=True)
    centred = values - centre
    variance = jnp.mean(centred * centred, axis=-1, keepdims=True)
    inv_std = lax.rsqrt(variance + norm_eps)
    normed = centred * inv_std
    return (normed * gain + shift, normed, inv_std)


def normalize_back(upstream, normed, inv_std, gain):
    scaled = upstream * gain
    return inv_std * (
        scaled
        - jnp.mean(scaled, axis=-1, keepdims=True)
        - normed * jnp.mean(scaled * normed, axis=-1, keepdims=True)
    )


def dot(left, right, dims):
    return lax.dot_general(left, right, (dims, ((), ())), preferred_element_type=jnp.float32)


def low(values):
    return values.astype(jnp.bfloat16)


def pack_small(parts):
    packed = jnp.concatenate([part.reshape(-1) for part in parts])
    return jnp.pad(packed, (0, -packed.size % 2048)).reshape(-1, 128)


def unpack_small(everyone, parts):
    wide_count, narrow_count = everyone.shape[:2]
    everyone = everyone.reshape(wide_count, narrow_count, -1).astype(jnp.float32)
    pieces = []
    start = 0
    for part in parts:
        pieces.append(everyone[:, :, start : start + part.size])
        start += part.size

    def pairs(piece):
        piece = piece.reshape(-1, 2, piece.shape[-1] // 2)
        return piece.transpose(1, 0, 2).reshape(2, -1)

    own_expand = lax.dynamic_index_in_dim(
        pieces[4], lax.axis_index("wide"), 0, keepdims=False
    )
    return (
        pieces[0].reshape(-1),
        pieces[1].reshape(-1),
        pairs(pieces[2]),
        pairs(pieces[3]),
        pairs(own_expand),
        pieces[5][0].reshape(-1),
    )


def ring_place(wide_count):
    ring = wide_count // 2
    mine = lax.axis_index("wide")
    chip = mine // 2
    core = mine % 2
    position = 2 * (chip // 2) + (chip % 2 + chip // 2) % 2
    return ring, position, core


def chip_at(position, ring):
    position = (position + 2 * ring) % ring
    return 2 * (position // 2) + (position + position // 2) % 2


class PlaneExchange:
    def __init__(self, wide_count, own, blocks, parts, from_mate, incoming, sems, cols=None):
        self.ring, self.position, self.core = ring_place(wide_count)
        self.own, self.blocks, self.parts = own, blocks, parts
        self.from_mate, self.incoming = from_mate, incoming
        (
            self.gather_send,
            self.gather_recv,
            self.mate_send,
            self.mate_recv,
            self.sum_send,
            self.sum_recv,
            self.own_sem,
        ) = sems
        self.half = parts.shape[1] // 2
        self.cols = slice(None) if cols is None else cols
        self.far = self.ring // 2
        self.started = []

    def device(self, offset, mate=False):
        core = 1 - self.core if mate else self.core
        return {"wide": 2 * chip_at(self.position + offset, self.ring) + core}

    def slot(self, offset, mate=False):
        core = 1 - self.core if mate else self.core
        return 2 * chip_at(self.position + offset, self.ring) + core

    def rows(self, part):
        return pl.ds(part * self.half, self.half)

    def greet(self):
        barrier = pltpu.get_barrier_semaphore()
        for where in (self.device(-1), self.device(1), self.device(0, True)):
            pl.semaphore_signal(
                barrier, inc=1, device_id=where, device_id_type=pl.DeviceIdType.MESH
            )
        pl.semaphore_wait(barrier, 3)

    def start(self, source, target, send_sem, recv_sem, where):
        copy = pltpu.make_async_remote_copy(
            src_ref=source,
            dst_ref=target,
            send_sem=send_sem,
            recv_sem=recv_sem,
            device_id=where,
            device_id_type=pl.DeviceIdType.MESH,
        )
        copy.start()
        self.started.append(copy)

    def pass_on(self, lane, slot, part, where, source=None):
        target = self.blocks.at[slot, self.rows(part)]
        self.start(
            target if source is None else source,
            target,
            self.gather_send.at[lane, slot, part],
            self.gather_recv.at[slot, part],
            where,
        )

    def arrived(self, slot, part):
        target = self.blocks.at[slot, self.rows(part)]
        pltpu.make_async_remote_copy(
            src_ref=target,
            dst_ref=target,
            send_sem=self.gather_send.at[0, slot, part],
            recv_sem=self.gather_recv.at[slot, part],
            device_id=self.device(1),
            device_id_type=pl.DeviceIdType.MESH,
        ).wait_recv()

    def send_own(self):
        slot = self.slot(0)
        keep = None
        own = self.blocks.at[slot]
        if self.own is not None:
            own = self.own
            keep = pltpu.make_async_copy(own, self.blocks.at[slot], self.own_sem)
            keep.start()
        first, second = own.at[self.rows(0)], own.at[self.rows(1)]
        self.pass_on(0, slot, 0, self.device(1), first)
        self.pass_on(1, slot, 1, self.device(-1), second)
        self.pass_on(2, slot, 0, self.device(0, True), first)
        self.pass_on(2, slot, 1, self.device(0, True), second)
        self.pass_on(0, slot, 1, self.device(1), second)
        self.pass_on(1, slot, 0, self.device(-1), first)
        return keep

    def receive(self, distance):
        mate = self.device(0, True)
        left, right = self.slot(-distance), self.slot(distance)
        if distance == self.far:
            for part in range(2):
                self.arrived(left, part)
                self.pass_on(2, left, part, mate)
            return
        further = distance < self.far - 1
        self.arrived(left, 0)
        self.pass_on(0, left, 0, self.device(1))
        self.pass_on(2, left, 0, mate)
        self.arrived(right, 1)
        self.pass_on(1, right, 1, self.device(-1))
        self.pass_on(2, right, 1, mate)
        self.arrived(left, 1)
        if further:
            self.pass_on(0, left, 1, self.device(1))
        self.pass_on(2, left, 1, mate)
        self.arrived(right, 0)
        if further:
            self.pass_on(1, right, 0, self.device(-1))
        self.pass_on(2, right, 0, mate)

    def receive_mate(self, offset):
        for part in range(2):
            self.arrived(self.slot(offset, True), part)

    def share(self, offset):
        chip = chip_at(self.position + offset, self.ring)
        self.start(
            self.parts.at[self.slot(offset, True), :, self.cols],
            self.from_mate.at[chip, :, self.cols],
            self.mate_send.at[chip],
            self.mate_recv.at[chip],
            self.device(0, True),
        )

    def shared(self, offset):
        chip = chip_at(self.position + offset, self.ring)
        pltpu.make_async_remote_copy(
            src_ref=self.parts.at[self.slot(offset), :, self.cols],
            dst_ref=self.from_mate.at[chip, :, self.cols],
            send_sem=self.mate_send.at[chip],
            recv_sem=self.mate_recv.at[chip],
            device_id=self.device(0, True),
            device_id_type=pl.DeviceIdType.MESH,
        ).wait_recv()

    def chip_sum(self, offset, rows):
        chip = chip_at(self.position + offset, self.ring)
        return self.parts[self.slot(offset), rows, self.cols].astype(
            jnp.float32
        ) + self.from_mate[chip, rows, self.cols].astype(jnp.float32)

    def send_sum(self, way, distance, part):
        offset = distance if way == 0 else -distance
        begins = self.far if part == way else self.far - 1
        slot = self.slot(offset)
        if distance < begins:
            self.sum_arrived(way, distance, part)

        def chunk(i, carry):
            here = pl.ds(pl.multiple_of(i * 16, 16), 16)
            there = pl.ds(pl.multiple_of(part * self.half + i * 16, 16), 16)
            total = self.chip_sum(offset, there)
            if distance < begins:
                total += self.incoming[way, distance, part, here, self.cols].astype(jnp.float32)
            self.parts[slot, there, self.cols] = total.astype(jnp.bfloat16)
            return carry

        lax.fori_loop(0, self.half // 16, chunk, 0)
        self.start(
            self.parts.at[slot, self.rows(part), self.cols],
            self.incoming.at[way, distance - 1, part, :, self.cols],
            self.sum_send.at[way, distance - 1, part],
            self.sum_recv.at[way, distance - 1, part],
            self.device(1 if way == 0 else -1),
        )

    def sum_arrived(self, way, distance, part):
        target = self.incoming.at[way, distance, part, :, self.cols]
        pltpu.make_async_remote_copy(
            src_ref=target,
            dst_ref=target,
            send_sem=self.sum_send.at[way, distance, part],
            recv_sem=self.sum_recv.at[way, distance, part],
            device_id=self.device(1),
            device_id_type=pl.DeviceIdType.MESH,
        ).wait_recv()

    def run(self, compute, before, between):
        keep = self.send_own()
        keep.wait()
        self.receive_mate(0)
        compute(chip_at(self.position, self.ring))
        self.share(0)
        for distance in range(1, self.far):
            self.receive(distance)
            for offset in (-distance, distance):
                self.receive_mate(offset)
                compute(chip_at(self.position + offset, self.ring))
                self.share(offset)
            if distance == self.far - 1:
                self.first_sums()
        self.receive(self.far)
        self.receive_mate(self.far)
        compute(chip_at(self.position + self.far, self.ring))
        self.share(self.far)
        before()
        self.far_sums()
        between()
        self.last_sums()

    def run_gather(self, compute, between):
        keep = self.send_own()
        keep.wait()
        self.receive_mate(0)
        compute(chip_at(self.position, self.ring))
        done = 1
        for distance in range(1, self.far):
            self.receive(distance)
            between(done)
            done += 1
            for offset in (-distance, distance):
                self.receive_mate(offset)
                compute(chip_at(self.position + offset, self.ring))
        self.receive(self.far)
        between(done)
        done += 1
        self.receive_mate(self.far)
        compute(chip_at(self.position + self.far, self.ring))
        return done

    def run_sums(self, compute):
        compute(chip_at(self.position + self.far, self.ring))
        self.share(self.far)
        for distance in range(self.far - 1, 0, -1):
            for offset in (-distance, distance):
                compute(chip_at(self.position + offset, self.ring))
                self.share(offset)
            if distance == self.far - 1:
                self.far_sums()
                self.first_sums()
        compute(chip_at(self.position, self.ring))
        self.share(0)
        self.last_sums()

    def first_sums(self):
        distance = self.far - 1
        self.shared(distance)
        self.send_sum(0, distance, 1)
        self.shared(-distance)
        self.send_sum(1, distance, 0)

    def far_sums(self):
        self.shared(self.far)
        self.send_sum(0, self.far, 0)
        self.send_sum(1, self.far, 1)

    def last_sums(self):
        for distance in range(self.far - 1, 0, -1):
            if distance < self.far - 1:
                self.shared(distance)
                self.shared(-distance)
            self.send_sum(0, distance, 0)
            self.send_sum(1, distance, 1)
            if distance < self.far - 1:
                self.send_sum(0, distance, 1)
                self.send_sum(1, distance, 0)

    def finish(self, result):
        self.shared(0)
        for part in range(2):
            for way in range(2):
                self.sum_arrived(way, 0, part)

            def chunk(i, carry):
                here = pl.ds(pl.multiple_of(i * 16, 16), 16)
                there = pl.ds(pl.multiple_of(part * self.half + i * 16, 16), 16)
                total = self.chip_sum(0, there)
                for way in range(2):
                    total += self.incoming[way, 0, part, here, self.cols].astype(jnp.float32)
                result[there, self.cols] = total.astype(result.dtype)
                return carry

            lax.fori_loop(0, self.half // 16, chunk, 0)

    def drain(self):
        for copy in self.started:
            copy.wait_send()


def sum_scratch(wide_count, rows, width):
    ring = wide_count // 2
    far = ring // 2
    dma = pltpu.SemaphoreType.DMA
    return [
        pltpu.VMEM((wide_count, rows, width), jnp.bfloat16),
        pltpu.VMEM((ring, rows, width), jnp.bfloat16),
        pltpu.VMEM((2, far, 2, rows // 2, width), jnp.bfloat16),
        dma((ring,)),
        dma((ring,)),
        dma((2, far, 2)),
        dma((2, far, 2)),
    ]


def exchange_scratch(wide_count, rows, width):
    dma = pltpu.SemaphoreType.DMA
    return [
        pltpu.VMEM((wide_count, rows, width), jnp.bfloat16),
        dma((3, wide_count, 2)),
        dma((wide_count, 2)),
        dma(()),
    ] + sum_scratch(wide_count, rows, width)


def load_padded(source, target, sem):
    filled = source.shape[0]
    copy = pltpu.make_async_copy(source, target.at[pl.ds(0, filled)], sem)
    copy.start()
    if filled < target.shape[0]:
        target[pl.ds(filled, target.shape[0] - filled)] = jnp.zeros(
            (target.shape[0] - filled, target.shape[1]), target.dtype
        )
    return copy


def pair_rows(ref, chip):
    block = ref[pl.ds(2 * chip, 2)]
    return block.reshape(2 * block.shape[1], block.shape[2])


def set_pair(ref, chip, cols, value):
    rows = ref.shape[1]
    ref[2 * chip, :, cols] = value[:rows].astype(ref.dtype)
    ref[2 * chip + 1, :, cols] = value[rows:].astype(ref.dtype)


def tiles(count, tile, body, start=0):
    def step(i, carry):
        body(pl.ds(pl.multiple_of(start + i * tile, tile), tile))
        return carry

    lax.fori_loop(0, count // tile, step, 0)


class LineExchange:
    def __init__(self, narrow_count):
        self.count = narrow_count
        self.mine = lax.axis_index("narrow")
        self.started = []

    def peer(self, offset):
        return (self.mine + offset) % self.count

    def greet(self, extra=0):
        barrier = pltpu.get_barrier_semaphore()
        for offset in range(1, self.count):
            pl.semaphore_signal(
                barrier,
                inc=1,
                device_id={"narrow": self.peer(offset)},
                device_id_type=pl.DeviceIdType.MESH,
            )
        pl.semaphore_wait(barrier, self.count - 1 + extra)

    def copy(self, source, target, send_sem, recv_sem, where):
        return pltpu.make_async_remote_copy(
            src_ref=source,
            dst_ref=target,
            send_sem=send_sem,
            recv_sem=recv_sem,
            device_id={"narrow": where},
            device_id_type=pl.DeviceIdType.MESH,
        )

    def send(self, offset, source, landing, send_sems, recv_sems):
        peer = self.peer(offset)
        copy = self.copy(
            source, landing.at[self.mine], send_sems.at[offset - 1], recv_sems.at[self.mine], peer
        )
        copy.start()
        self.started.append(copy)

    def arrived(self, offset, landing, send_sems, recv_sems):
        peer = self.peer(offset)
        self.copy(
            landing.at[peer], landing.at[peer], send_sems.at[offset - 1], recv_sems.at[peer], peer
        ).wait_recv()

    def drain(self):
        for copy in self.started:
            copy.wait_send()


class LineSum:
    def __init__(self, line, view, landing, send_sems, recv_sems):
        self.line, self.view, self.landing = line, view, landing
        self.send_sems, self.recv_sems = send_sems, recv_sems
        self.last = line.count - 1

    def reaches(self, way, offset):
        here = self.line.mine
        return here + offset <= self.last if way == 0 else here - offset >= 0

    def follows(self, way):
        here = self.line.mine
        return here > 0 if way == 0 else here < self.last

    def target(self, way, offset):
        return self.line.mine + offset if way == 0 else self.line.mine - offset

    def copy(self, way, offset):
        return self.line.copy(
            self.view(self.target(way, offset)),
            self.landing.at[way, offset - 1],
            self.send_sems.at[way, offset - 1],
            self.recv_sems.at[way, offset - 1],
            self.line.mine + 1 if way == 0 else self.line.mine - 1,
        )

    def arrived(self, way, offset):
        landing = self.landing.at[way, offset]
        self.line.copy(
            landing,
            landing,
            self.send_sems.at[way, offset],
            self.recv_sems.at[way, offset],
            self.line.mine,
        ).wait_recv()

    def add(self, way, offset):
        held = self.view(self.target(way, offset))

        def chunk(i, carry):
            some = pl.ds(pl.multiple_of(i * 16, 16), 16)
            held[some] = (
                held[some].astype(jnp.float32)
                + self.landing[way, offset, some].astype(jnp.float32)
            ).astype(jnp.bfloat16)
            return carry

        lax.fori_loop(0, self.landing.shape[2] // 16, chunk, 0)

    def begin(self):
        for offset in range(self.last, 0, -1):
            for way in range(2):

                @pl.when(self.reaches(way, offset) & jnp.logical_not(self.follows(way)))
                def _():
                    self.copy(way, offset).start()

    def step(self, offset):
        for way in range(2):

            @pl.when(self.reaches(way, offset) & self.follows(way))
            def _():
                self.arrived(way, offset)
                self.add(way, offset)
                self.copy(way, offset).start()

    def finish(self, result):
        held = self.view(self.line.mine)
        count = self.landing.shape[2] // 16

        def begin(i, carry):
            some = pl.ds(pl.multiple_of(i * 16, 16), 16)
            result[some] = held[some].astype(result.dtype)
            return carry

        lax.fori_loop(0, count, begin, 0)
        for way in range(2):

            @pl.when(self.follows(way))
            def _():
                self.arrived(way, 0)

                def chunk(i, carry):
                    some = pl.ds(pl.multiple_of(i * 16, 16), 16)
                    result[some] += self.landing[way, 0, some].astype(result.dtype)
                    return carry

                lax.fori_loop(0, count, chunk, 0)

    def drain(self):
        for offset in range(1, self.last + 1):
            for way in range(2):

                @pl.when(self.reaches(way, offset))
                def _():
                    self.copy(way, offset).wait_send()


class LineGather:
    def __init__(self, line, view, send_sems, recv_sems):
        self.line, self.view = line, view
        self.send_sems, self.recv_sems = send_sems, recv_sems
        self.last = line.count - 1

    def copy(self, way, block):
        target = self.view(block)
        here = self.line.mine
        return self.line.copy(
            target,
            target,
            self.send_sems.at[way, block],
            self.recv_sems.at[block],
            here + 1 if way == 0 else here - 1,
        )

    def goes(self, way):
        return self.line.mine < self.last if way == 0 else self.line.mine > 0

    def has(self, way, step):
        here = self.line.mine
        return here - step >= 0 if way == 0 else here + step <= self.last

    def block(self, way, step):
        return self.line.mine - step if way == 0 else self.line.mine + step

    def send_own(self):
        for way in range(2):

            @pl.when(self.goes(way))
            def _():
                self.copy(way, self.line.mine).start()

    def step(self, step):
        for way in range(2):

            @pl.when(self.has(way, step))
            def _():
                self.copy(way, self.block(way, step)).wait_recv()

                @pl.when(self.goes(way))
                def _():
                    self.copy(way, self.block(way, step)).start()

    def each(self, step, body):
        for way in range(2):

            @pl.when(self.has(way, step))
            def _():
                body(self.block(way, step))

    def drain(self):
        for way in range(2):
            for step in range(self.last + 1):

                @pl.when(self.has(way, step) & self.goes(way))
                def _():
                    self.copy(way, self.block(way, step)).wait_send()


def greet_plane(plane):
    barrier = pltpu.get_barrier_semaphore()
    for where in (plane.device(-1), plane.device(1), plane.device(0, True)):
        pl.semaphore_signal(barrier, inc=1, device_id=where, device_id_type=pl.DeviceIdType.MESH)


def geglu_forward_kernel(
    wide_count,
    narrow_count,
    own,
    gate_expand,
    upper_expand,
    reduce,
    shift,
    reduce_out,
    rows_all,
    active_out,
    slope_out,
    gelu_out,
    feed,
    blocks,
    gather_send,
    gather_recv,
    own_sem,
    parts,
    from_mate,
    incoming,
    mate_send,
    mate_recv,
    sum_send,
    sum_recv,
    expand_mat,
    reduce_mat,
    active,
    slope,
    gelu,
    load_sems,
    keep_sems,
    reduce_send,
    reduce_recv,
    late_mate_send,
    late_mate_recv,
    late_sum_send,
    late_sum_recv,
):
    sems = (gather_send, gather_recv, mate_send, mate_recv, sum_send, sum_recv, own_sem)
    late_sems = (None, None, late_mate_send, late_mate_recv, late_sum_send, late_sum_recv, None)
    line = LineExchange(narrow_count)
    filled, cols = reduce.shape
    width = own.shape[1]
    upper = (2 * line.mine) // narrow_count
    late = pl.multiple_of((1 - upper) * (width - cols), cols)
    early = pl.multiple_of(upper * cols, cols)
    plane = PlaneExchange(
        wide_count, own, blocks, parts, from_mate, incoming, sems, pl.ds(early, width - cols)
    )
    late_plane = PlaneExchange(
        wide_count, None, None, parts, from_mate, incoming, late_sems, pl.ds(late, cols)
    )
    loads = [
        load_padded(gate_expand, expand_mat.at[0], load_sems.at[0]),
        load_padded(upper_expand, expand_mat.at[1], load_sems.at[1]),
    ]

    def reduce_cols(block):
        return reduce_mat.at[
            pl.ds(0, filled), pl.ds(pl.multiple_of(block * cols, cols), cols)
        ]

    line_reduce = LineGather(line, reduce_cols, reduce_send, reduce_recv)
    own_reduce = pltpu.make_async_copy(reduce, reduce_cols(line.mine), load_sems.at[2])
    own_reduce.start()
    if filled < reduce_mat.shape[0]:
        reduce_mat[filled:] = jnp.zeros(
            (reduce_mat.shape[0] - filled, reduce_mat.shape[1]), reduce_mat.dtype
        )
    greet_plane(plane)
    line.greet(3)
    own_reduce.wait()
    line_reduce.send_own()
    kept = []
    waiting = list(loads)

    def compute(chip):
        while waiting:
            waiting.pop().wait()

        def units(cols):
            rows = pair_rows(blocks, chip)
            gate = dot(rows, expand_mat[0, cols], ((1,), (1,))) + shift[0:1, cols]
            upper = dot(rows, expand_mat[1, cols], ((1,), (1,))) + shift[1:2, cols]
            factor = math.sqrt(2 / math.pi)
            square = gate * gate
            bend = jnp.tanh(factor * gate * (1 + 0.044715 * square))
            value = 0.5 * gate * (1 + bend)
            pull = 0.5 * (1 + bend) + 0.5 * gate * (1 - bend * bend) * factor * (
                1 + 3 * 0.044715 * square
            )
            set_pair(active, chip, cols, value * upper)
            set_pair(slope, chip, cols, pull * upper)
            set_pair(gelu, chip, cols, value)

        tiles(active.shape[2], 256, units)

        pair = pl.ds(2 * chip, 2)
        for index, (source, target) in enumerate(
            ((active, active_out), (slope, slope_out), (gelu, gelu_out), (blocks, rows_all))
        ):
            copy = pltpu.make_async_copy(
                source.at[pair], target.at[pair], keep_sems.at[chip, index]
            )
            copy.start()
            kept.append(copy)

    def compute_sums(start, count):
        def compute(chip):
            def outputs(some):
                part = dot(pair_rows(active, chip), reduce_mat[:, some], ((1,), (0,)))
                set_pair(parts, chip, some, part)

            tiles(count, 256, outputs, start)

        return compute

    def between(index):
        if index < narrow_count:
            line_reduce.step(index)

    done = plane.run_gather(compute, between)
    for step in range(done, narrow_count - 1):
        line_reduce.step(step)
    plane.run_sums(compute_sums(early, width - cols))
    line_reduce.step(narrow_count - 1)
    keep_reduce = pltpu.make_async_copy(
        reduce_mat.at[pl.ds(0, filled)], reduce_out, load_sems.at[3]
    )
    keep_reduce.start()
    late_plane.run_sums(compute_sums(late, cols))
    plane.finish(feed)
    late_plane.finish(feed)
    plane.drain()
    late_plane.drain()
    keep_reduce.wait()
    line_reduce.drain()
    for copy in kept:
        copy.wait()


def geglu_forward(
    wide_count, narrow_count, hidden_low, gate_expand, upper_expand, reduce_weight, shift
):
    rows, width = hidden_low.shape
    padded = shift.shape[1]
    anywhere = pl.BlockSpec(memory_space=pl.ANY)
    vmem = pl.BlockSpec(memory_space=pltpu.VMEM)
    kept = jax.ShapeDtypeStruct((wide_count, rows, padded), jnp.bfloat16)
    scratch = exchange_scratch(wide_count, rows, width) + [
        pltpu.VMEM((2, padded, width), jnp.bfloat16),
        pltpu.VMEM((padded, width), jnp.bfloat16),
        pltpu.VMEM((wide_count, rows, padded), jnp.bfloat16),
        pltpu.VMEM((wide_count, rows, padded), jnp.bfloat16),
        pltpu.VMEM((wide_count, rows, padded), jnp.bfloat16),
        pltpu.SemaphoreType.DMA((4,)),
        pltpu.SemaphoreType.DMA((wide_count // 2, 4)),
        pltpu.SemaphoreType.DMA((2, narrow_count)),
        pltpu.SemaphoreType.DMA((narrow_count,)),
    ] + sum_scratch(wide_count, rows, width)[3:]
    return pl.pallas_call(
        functools.partial(geglu_forward_kernel, wide_count, narrow_count),
        out_shape=(
            jax.ShapeDtypeStruct((reduce_weight.shape[0], width), jnp.bfloat16),
            jax.ShapeDtypeStruct((wide_count, rows, width), jnp.bfloat16),
            kept,
            kept,
            kept,
            jax.ShapeDtypeStruct((rows, width), jnp.float32),
        ),
        in_specs=[anywhere, anywhere, anywhere, anywhere, vmem],
        out_specs=(anywhere, anywhere, anywhere, anywhere, anywhere, vmem),
        scratch_shapes=scratch,
        compiler_params=pltpu.CompilerParams(
            collective_id=1, has_side_effects=True, vmem_limit_bytes=kernel_memory
        ),
        cost_estimate=pl.CostEstimate(
            flops=6 * wide_count * rows * padded * width, bytes_accessed=200 * 2**20, transcendentals=0
        ),
        name="geglu_forward",
    )(hidden_low, gate_expand, upper_expand, reduce_weight, shift)


def geglu_backward_kernel(
    wide_count,
    narrow_count,
    own,
    gate_expand,
    upper_expand,
    reduce,
    slope_in,
    gelu_in,
    active_in,
    rows_in,
    reduce_grad,
    expand_part,
    hidden_grad,
    unit_sums,
    blocks,
    gather_send,
    gather_recv,
    own_sem,
    parts,
    from_mate,
    incoming,
    mate_send,
    mate_recv,
    sum_send,
    sum_recv,
    expand_mat,
    reduce_mat,
    slope,
    gelu,
    active,
    rows_all,
    staged,
    load_sems,
    keep_sems,
    line_in,
    line_send,
    line_recv,
):
    sems = (gather_send, gather_recv, mate_send, mate_recv, sum_send, sum_recv, own_sem)
    plane = PlaneExchange(wide_count, own, blocks, parts, from_mate, incoming, sems)
    loads = [
        load_padded(gate_expand, expand_mat.at[0], load_sems.at[0]),
        load_padded(upper_expand, expand_mat.at[1], load_sems.at[1]),
        load_padded(reduce, reduce_mat, load_sems.at[2]),
        pltpu.make_async_copy(slope_in, slope, load_sems.at[3]),
        pltpu.make_async_copy(gelu_in, gelu, load_sems.at[4]),
    ]
    late_loads = [
        pltpu.make_async_copy(active_in, active, load_sems.at[5]),
        pltpu.make_async_copy(rows_in, rows_all, load_sems.at[6]),
    ]
    for copy in loads[3:]:
        copy.start()
    unit_sums[...] = jnp.zeros_like(unit_sums)
    line = LineExchange(narrow_count)
    filled, line_cols = line_in.shape[2:]

    def line_part(block):
        return reduce_mat.at[
            pl.ds(0, filled), pl.ds(pl.multiple_of(block * line_cols, line_cols), line_cols)
        ]

    line_sum = LineSum(line, line_part, line_in, line_send, line_recv)
    greet_plane(plane)
    line.greet(3)
    for copy in late_loads:
        copy.start()
    kept = []
    waiting = list(loads)

    def compute(chip):
        while waiting:
            waiting.pop().wait()

        def units(cols):
            pulled = dot(pair_rows(blocks, chip), reduce_mat[cols], ((1,), (1,)))
            pair = pl.ds(2 * chip, 2)
            shape = pulled.shape
            gate_grad = pulled * slope[pair, :, cols].reshape(shape).astype(jnp.float32)
            upper_grad = pulled * gelu[pair, :, cols].reshape(shape).astype(jnp.float32)
            set_pair(slope, chip, cols, gate_grad)
            set_pair(gelu, chip, cols, upper_grad)
            unit_sums[0:1, cols] += jnp.sum(gate_grad, axis=0, keepdims=True)
            unit_sums[1:2, cols] += jnp.sum(upper_grad, axis=0, keepdims=True)

        tiles(slope.shape[2], 256, units)

        def outputs(cols):
            set_pair(
                parts,
                chip,
                cols,
                dot(pair_rows(slope, chip), expand_mat[0, :, cols], ((1,), (0,)))
                + dot(pair_rows(gelu, chip), expand_mat[1, :, cols], ((1,), (0,))),
            )

        tiles(parts.shape[2], 256, outputs)

    def product(left, right, start):
        tokens = left.shape[0] * left.shape[1]
        return dot(
            left[:, :, start : start + 256].reshape(tokens, 256),
            right[...].reshape(tokens, right.shape[2]),
            ((0,), (0,)),
        ).astype(jnp.bfloat16)

    def reduce_work():
        for copy in late_loads:
            copy.wait()
        for start in range(0, active.shape[2], 256):
            reduce_mat[start : start + 256] = product(active, blocks, start)
        line_sum.begin()

    def expand_work(left, start, target):
        def work():
            index = len(kept)
            if index >= 2:
                kept[index - 2].wait()
            staged[index % 2] = product(left, rows_all, start)
            stop = min(256, target.shape[0] - start)
            copy = pltpu.make_async_copy(
                staged.at[index % 2, pl.ds(0, stop)],
                target.at[pl.ds(start, stop)],
                keep_sems.at[index % 2],
            )
            copy.start()
            kept.append(copy)

        return work

    works = [
        expand_work(left, start, target)
        for left, target in ((slope, expand_part.at[0]), (gelu, expand_part.at[1]))
        for start in range(0, target.shape[0], 256)
    ]
    steps = [
        functools.partial(line_sum.step, offset) for offset in range(narrow_count - 2, 0, -1)
    ]
    middle = len(works) // 2
    works = [works[:middle], steps[: len(steps) // 2], works[middle:], steps[len(steps) // 2 :]]

    def many(calls):
        for call in calls:
            call()

    plane.run(compute, reduce_work, functools.partial(many, works[0] + works[1]))
    many(works[2])
    plane.finish(hidden_grad)
    many(works[3])
    line_sum.finish(reduce_grad)
    line_sum.drain()
    plane.drain()
    for copy in kept[-2:]:
        copy.wait()


def geglu_backward(
    wide_count,
    narrow_count,
    feed_grad,
    gate_expand,
    upper_expand,
    reduce_full,
    slope,
    gelu,
    active,
    rows_all,
):
    rows, width = feed_grad.shape
    padded = slope.shape[2]
    anywhere = pl.BlockSpec(memory_space=pl.ANY)
    vmem = pl.BlockSpec(memory_space=pltpu.VMEM)
    scratch = exchange_scratch(wide_count, rows, width) + [
        pltpu.VMEM((2, padded, width), jnp.bfloat16),
        pltpu.VMEM((padded, width), jnp.bfloat16),
        pltpu.VMEM((wide_count, rows, padded), jnp.bfloat16),
        pltpu.VMEM((wide_count, rows, padded), jnp.bfloat16),
        pltpu.VMEM((wide_count, rows, padded), jnp.bfloat16),
        pltpu.VMEM((wide_count, rows, width), jnp.bfloat16),
        pltpu.VMEM((2, 256, width), jnp.bfloat16),
        pltpu.SemaphoreType.DMA((7,)),
        pltpu.SemaphoreType.DMA((2,)),
        pltpu.VMEM(
            (2, narrow_count - 1, reduce_full.shape[0], width // narrow_count), jnp.bfloat16
        ),
        pltpu.SemaphoreType.DMA((2, narrow_count - 1)),
        pltpu.SemaphoreType.DMA((2, narrow_count - 1)),
    ]
    return pl.pallas_call(
        functools.partial(geglu_backward_kernel, wide_count, narrow_count),
        out_shape=(
            jax.ShapeDtypeStruct(
                (reduce_full.shape[0], width // narrow_count), jnp.float32
            ),
            jax.ShapeDtypeStruct((2, *gate_expand.shape), jnp.bfloat16),
            jax.ShapeDtypeStruct((rows, width), jnp.float32),
            jax.ShapeDtypeStruct((2, padded), jnp.float32),
        ),
        in_specs=[anywhere] * 8,
        out_specs=(vmem, anywhere, vmem, vmem),
        scratch_shapes=scratch,
        compiler_params=pltpu.CompilerParams(
            collective_id=2, has_side_effects=True, vmem_limit_bytes=63 * 2**20
        ),
        cost_estimate=pl.CostEstimate(
            flops=12 * wide_count * rows * padded * width, bytes_accessed=200 * 2**20, transcendentals=0
        ),
        name="geglu_backward",
    )(feed_grad, gate_expand, upper_expand, reduce_full, slope, gelu, active, rows_all)


def rotate_lanes(vectors, cosine, signed_sine):
    return vectors * cosine + pltpu.roll(vectors, vectors.shape[1] // 2, 1) * signed_sine


def attention_backward_kernel(
    wide_count,
    narrow_count,
    attended,
    merge,
    mixed,
    queries,
    keys,
    values,
    probs,
    cosine,
    signed_sine,
    triple,
    merge_grad,
    heads_sums,
    merge_sums,
    upstream,
    outbound,
    probs_held,
    keys_turned,
    key_total,
    value_total,
    merge_out,
    merge_in,
    mixed_send,
    mixed_recv,
    merge_send,
    merge_recv,
    load_sems,
    parts,
    from_mate,
    incoming,
    mate_send,
    mate_recv,
    sum_send,
    sum_recv,
):
    sems = (None, None, mate_send, mate_recv, sum_send, sum_recv, None)
    plane = PlaneExchange(wide_count, None, None, parts, from_mate, incoming, sems)
    line = LineExchange(narrow_count)
    rows, width = attended.shape
    own_cols = queries.shape[1]
    heads = own_cols // HDIM
    scale = HDIM ** (-0.5)

    def load(head):
        return pltpu.make_async_copy(
            probs.at[head], probs_held.at[head % 2], load_sems.at[head % 2]
        )

    load(0).start()
    greet_plane(plane)
    line.greet(3)

    def mixed_part(target, where):
        part = dot(
            attended[...],
            merge[pl.ds(pl.multiple_of(where * own_cols, own_cols), own_cols)],
            ((1,), (1,)),
        )
        target[...] = part.astype(jnp.bfloat16)

    for offset in range(1, narrow_count):
        place = line.peer(offset)
        mixed_part(outbound.at[offset - 1], place)
        line.send(offset, outbound.at[offset - 1], upstream, mixed_send, mixed_recv)
    mixed_part(upstream.at[line.mine], line.mine)

    block = parts.shape[1]

    def merge_rows(i, carry):
        cols = pl.ds(pl.multiple_of(i * block, block), block)
        parts[i] = dot(mixed[:, cols], attended[...], ((0,), (0,))).astype(jnp.bfloat16)
        return carry

    lax.fori_loop(0, wide_count, merge_rows, 0)
    for offset in range(plane.ring):
        plane.share(offset)
    merge_sums[...] = jnp.sum(attended[...].astype(jnp.float32), axis=0, keepdims=True)
    plane.first_sums()
    plane.far_sums()
    for offset in range(1, narrow_count):
        line.arrived(offset, upstream, mixed_send, mixed_recv)

    def one_head(head):
        cols = pl.ds(head * HDIM, HDIM)
        load(head).wait()
        if head + 1 < heads:
            load(head + 1).start()
        held = probs_held.at[head % 2]
        keys_turned[...] = keys[:, cols].astype(jnp.float32).T.astype(jnp.bfloat16)
        key_total[...] = jnp.zeros_like(key_total)
        value_total[...] = jnp.zeros_like(value_total)

        def chunk(i, carry):
            here = pl.ds(pl.multiple_of(i * rows, rows), rows)
            weights_low = held[:, here]
            up = upstream[i, :, cols]
            pulled = dot(values[:, cols], up, ((1,), (1,)))
            weights = weights_low.astype(jnp.float32)
            scaled = weights * pulled
            change = (scaled - weights * jnp.sum(scaled, axis=0, keepdims=True)).astype(
                jnp.bfloat16
            )
            key_total[...] += dot(change, queries[here, cols], ((1,), (0,)))
            value_total[...] += dot(weights_low, up, ((1,), (0,)))
            query_grad = dot(keys_turned[...], change, ((1,), (0,))).T * scale
            triple[here, cols] = rotate_lanes(
                query_grad, cosine[here], signed_sine[here]
            ).astype(jnp.bfloat16)
            return carry

        lax.fori_loop(0, narrow_count, chunk, 0)

        def ending(i, carry):
            here = pl.ds(pl.multiple_of(i * rows, rows), rows)
            triple[here, pl.ds(own_cols + head * HDIM, HDIM)] = rotate_lanes(
                key_total[here] * scale, cosine[here], signed_sine[here]
            ).astype(jnp.bfloat16)
            triple[here, pl.ds(2 * own_cols + head * HDIM, HDIM)] = value_total[here].astype(
                jnp.bfloat16
            )
            return carry

        lax.fori_loop(0, narrow_count, ending, 0)

    for head in range(heads):
        one_head(head)
        if head == heads // 2 - 1:
            plane.last_sums()
    total = merge_out.at[...]
    plane.finish(merge_out)
    count = merge_grad.shape[0]

    def z_rows(where):
        return pl.ds(pl.multiple_of(where * count, count), count)

    for offset in range(1, narrow_count):
        line.send(
            offset, total.at[z_rows(line.peer(offset))], merge_in, merge_send, merge_recv
        )

    def column_sums(cols):
        heads_sums[:, cols] = jnp.sum(
            triple[:, cols].astype(jnp.float32), axis=0, keepdims=True
        )

    tiles(3 * own_cols, 256, column_sums)
    summed = merge_out[z_rows(line.mine)].astype(jnp.float32)
    for offset in range(1, narrow_count):
        line.arrived(offset, merge_in, merge_send, merge_recv)
        summed += merge_in[line.peer(offset)].astype(jnp.float32)
    merge_grad[...] = summed
    line.drain()
    plane.drain()


def attention_backward(
    wide_count,
    narrow_count,
    attended_grad,
    merge_full,
    mixed,
    queries,
    keys,
    values,
    probs,
    cosine,
    signed_sine,
):
    rows, width = attended_grad.shape
    bucket, own_cols = queries.shape
    block = width // wide_count
    count = block // narrow_count
    anywhere = pl.BlockSpec(memory_space=pl.ANY)
    vmem = pl.BlockSpec(memory_space=pltpu.VMEM)
    dma = pltpu.SemaphoreType.DMA
    return pl.pallas_call(
        functools.partial(attention_backward_kernel, wide_count, narrow_count),
        out_shape=(
            jax.ShapeDtypeStruct((bucket, 3 * own_cols), jnp.bfloat16),
            jax.ShapeDtypeStruct((count, width), jnp.float32),
            jax.ShapeDtypeStruct((1, 3 * own_cols), jnp.float32),
            jax.ShapeDtypeStruct((1, width), jnp.float32),
        ),
        in_specs=[vmem] * 6 + [anywhere] + [vmem] * 2,
        out_specs=(vmem, vmem, vmem, vmem),
        scratch_shapes=[
            pltpu.VMEM((narrow_count, rows, own_cols), jnp.bfloat16),
            pltpu.VMEM((narrow_count - 1, rows, own_cols), jnp.bfloat16),
            pltpu.VMEM((2, bucket, bucket), jnp.bfloat16),
            pltpu.VMEM((HDIM, bucket), jnp.bfloat16),
            pltpu.VMEM((bucket, HDIM), jnp.float32),
            pltpu.VMEM((bucket, HDIM), jnp.float32),
            pltpu.VMEM((block, width), jnp.bfloat16),
            pltpu.VMEM((narrow_count, count, width), jnp.bfloat16),
            dma((narrow_count - 1,)),
            dma((narrow_count,)),
            dma((narrow_count - 1,)),
            dma((narrow_count,)),
            dma((2,)),
        ]
        + sum_scratch(wide_count, block, width),
        compiler_params=pltpu.CompilerParams(
            collective_id=3, has_side_effects=True, vmem_limit_bytes=kernel_memory
        ),
        cost_estimate=pl.CostEstimate(
            flops=60 * 10**9, bytes_accessed=200 * 2**20, transcendentals=0
        ),
        name="attention_backward",
    )(
        attended_grad, merge_full, mixed, queries, keys, values, probs, cosine, signed_sine
    )


def input_backward_kernel(
    wide_count,
    narrow_count,
    inputs,
    triple,
    heads_mat,
    small,
    input_part,
    heads_grad,
    small_out,
    line_parts,
    line_in,
    heads_out,
    heads_in,
    small_wide,
    small_sum,
    small_line,
    line_send,
    line_recv,
    heads_send,
    heads_recv,
    wide_send,
    wide_recv,
    small_send,
    small_recv,
    parts,
    from_mate,
    incoming,
    mate_send,
    mate_recv,
    sum_send,
    sum_recv,
):
    sems = (None, None, mate_send, mate_recv, sum_send, sum_recv, None)
    plane = PlaneExchange(wide_count, None, None, parts, from_mate, incoming, sems)
    line = LineExchange(narrow_count)
    rows, width = input_part.shape
    here = line.mine
    last = narrow_count - 1
    place = lax.axis_index("wide")

    def wide_peer(offset):
        return (place + offset) % wide_count

    barrier = pltpu.get_barrier_semaphore()
    for offset in range(1, wide_count):
        pl.semaphore_signal(
            barrier,
            inc=1,
            device_id={"wide": wide_peer(offset)},
            device_id_type=pl.DeviceIdType.MESH,
        )
    line.greet(wide_count - 1)

    def small_copy(offset, source, slot):
        return pltpu.make_async_remote_copy(
            src_ref=source,
            dst_ref=small_wide.at[slot],
            send_sem=wide_send.at[offset - 1],
            recv_sem=wide_recv.at[slot],
            device_id={"wide": wide_peer(offset)},
            device_id_type=pl.DeviceIdType.MESH,
        )

    small_copies = [
        small_copy(offset, small.at[wide_peer(offset)], place) for offset in range(1, wide_count)
    ]
    for copy in small_copies:
        copy.start()

    def input_cols(cols):
        part = dot(triple[...], heads_mat[cols], ((1,), (1,)))
        for index in range(narrow_count):
            line_parts[index, :, cols] = part[index * rows : (index + 1) * rows].astype(
                jnp.bfloat16
            )

    tiles(width, 256, input_cols)

    line_sum = LineSum(line, lambda target: line_parts.at[target], line_in, line_send, line_recv)
    line_sum.begin()

    block = parts.shape[1]

    def heads_rows(i, carry):
        cols = pl.ds(pl.multiple_of(i * block, block), block)
        parts[i] = dot(inputs[:, cols], triple[...], ((0,), (0,))).astype(jnp.bfloat16)
        return carry

    lax.fori_loop(0, wide_count, heads_rows, 0)
    for offset in range(plane.ring):
        plane.share(offset)
    for offset in range(last - 1, last // 2, -1):
        line_sum.step(offset)
    plane.first_sums()
    plane.far_sums()

    for offset in range(1, wide_count):
        peer = wide_peer(offset)
        small_copy(offset, small_wide.at[peer], peer).wait_recv()
    small_wide[place] = small[place]
    total = small_wide[0]
    for index in range(1, wide_count):
        total += small_wide[index]
    small_sum[...] = total
    for offset in range(1, narrow_count):
        line.send(offset, small_sum.at[line.peer(offset)], small_line, small_send, small_recv)

    plane.last_sums()
    for offset in range(last // 2, 0, -1):
        line_sum.step(offset)
    plane.finish(heads_out)
    count = heads_grad.shape[0]

    def z_rows(where):
        return pl.ds(pl.multiple_of(where * count, count), count)

    for offset in range(1, narrow_count):
        line.send(
            offset, heads_out.at[z_rows(line.peer(offset))], heads_in, heads_send, heads_recv
        )
    heads_in[line.mine] = heads_out[z_rows(line.mine)]
    small_line[line.mine] = small_sum[line.mine]
    for offset in range(1, narrow_count):
        line.arrived(offset, small_line, small_send, small_recv)
    result = small_line[0]
    for index in range(1, narrow_count):
        result += small_line[index]
    small_out[...] = result

    line_sum.finish(input_part)
    for offset in range(1, narrow_count):
        line.arrived(offset, heads_in, heads_send, heads_recv)
    own_cols = triple.shape[1] // 3
    for index in range(narrow_count):
        for which in range(3):
            start = (which * narrow_count + index) * own_cols
            heads_grad[:, start : start + own_cols] = heads_in[
                index, :, which * own_cols : (which + 1) * own_cols
            ].astype(jnp.float32)
    line_sum.drain()
    for copy in small_copies:
        copy.wait_send()
    line.drain()
    plane.drain()


def input_backward(wide_count, narrow_count, inputs, triple_grad, heads_mat, small):
    bucket, width = inputs.shape
    rows = bucket // narrow_count
    columns = triple_grad.shape[1]
    block = width // wide_count
    count = block // narrow_count
    vmem = pl.BlockSpec(memory_space=pltpu.VMEM)
    dma = pltpu.SemaphoreType.DMA
    lines = small.shape[2]
    return pl.pallas_call(
        functools.partial(input_backward_kernel, wide_count, narrow_count),
        out_shape=(
            jax.ShapeDtypeStruct((rows, width), jnp.float32),
            jax.ShapeDtypeStruct((count, narrow_count * columns), jnp.float32),
            jax.ShapeDtypeStruct((lines, 128), jnp.float32),
        ),
        in_specs=[vmem] * 4,
        out_specs=(vmem, vmem, vmem),
        scratch_shapes=[
            pltpu.VMEM((narrow_count, rows, width), jnp.bfloat16),
            pltpu.VMEM((2, narrow_count - 1, rows, width), jnp.bfloat16),
            pltpu.VMEM((block, columns), jnp.bfloat16),
            pltpu.VMEM((narrow_count, count, columns), jnp.bfloat16),
            pltpu.VMEM((wide_count, narrow_count, lines, 128), jnp.float32),
            pltpu.VMEM((narrow_count, lines, 128), jnp.float32),
            pltpu.VMEM((narrow_count, lines, 128), jnp.float32),
            dma((2, narrow_count - 1)),
            dma((2, narrow_count - 1)),
            dma((narrow_count - 1,)),
            dma((narrow_count,)),
            dma((wide_count - 1,)),
            dma((wide_count,)),
            dma((narrow_count - 1,)),
            dma((narrow_count,)),
        ]
        + sum_scratch(wide_count, block, columns),
        compiler_params=pltpu.CompilerParams(
            collective_id=4, has_side_effects=True, vmem_limit_bytes=kernel_memory
        ),
        cost_estimate=pl.CostEstimate(
            flops=80 * 10**9, bytes_accessed=200 * 2**20, transcendentals=0
        ),
        name="input_backward",
    )(inputs, triple_grad, heads_mat, small)


def greet_all(wide_count, narrow_count):
    barrier = pltpu.get_barrier_semaphore()
    for axis, count in (("wide", wide_count), ("narrow", narrow_count)):
        place = lax.axis_index(axis)
        for offset in range(1, count):
            pl.semaphore_signal(
                barrier,
                inc=1,
                device_id={axis: (place + offset) % count},
                device_id_type=pl.DeviceIdType.MESH,
            )
    pl.semaphore_wait(barrier, wide_count + narrow_count - 2)


def gather_kernel(
    wide_count,
    narrow_count,
    own,
    heads_weight,
    merge_weight,
    small,
    rows_out,
    heads_out,
    merge_out,
    small_out,
    triple,
    rows_all,
    heads_all,
    merge_all,
    small_all,
    rows_send,
    rows_recv,
    heads_send,
    heads_recv,
    merge_send,
    merge_recv,
    small_send,
    small_recv,
    wide_send,
    wide_recv,
    local_sems,
    out_sems,
    heads_ring_send,
    heads_ring_recv,
    merge_ring_send,
    merge_ring_recv,
):
    def ring_of(blocks, send, recv):
        sems = (send, recv, None, None, None, None, None)
        return PlaneExchange(wide_count, None, blocks, blocks, None, None, sems)

    heads_ring = ring_of(heads_all, heads_ring_send, heads_ring_recv)
    merge_ring = ring_of(merge_all, merge_ring_send, merge_ring_recv)
    line = LineExchange(narrow_count)
    here = line.mine
    last = narrow_count - 1
    place = lax.axis_index("wide")
    slot = heads_ring.slot(0)
    rows, width = own.shape
    count = heads_weight.shape[0]
    columns = heads_all.shape[2]
    own_cols = columns // 3

    def z_rows(where):
        return pl.ds(pl.multiple_of(where * count, count), count)

    def head_cols(which, where):
        start = which * narrow_count * own_cols + where * own_cols
        return pl.ds(pl.multiple_of(start, own_cols), own_cols)

    line_rows = LineGather(line, lambda block: rows_all.at[block], rows_send, rows_recv)

    keep_rows = pltpu.make_async_copy(own, rows_all.at[here], local_sems.at[0])
    keep_rows.start()
    keeps = [
        pltpu.make_async_copy(
            heads_weight.at[:, head_cols(which, here)],
            heads_all.at[slot, z_rows(here), pl.ds(which * own_cols, own_cols)],
            local_sems.at[2 + which],
        )
        for which in range(3)
    ]
    keep_merge = pltpu.make_async_copy(
        merge_weight, merge_all.at[slot, z_rows(here)], local_sems.at[1]
    )
    for copy in keeps + [keep_merge]:
        copy.start()
    small_all[place, here] = small[...]
    greet_all(wide_count, narrow_count)

    def heads_copy(offset, which, where, sender):
        return line.copy(
            heads_weight.at[:, head_cols(which, where)],
            heads_all.at[slot, z_rows(sender), pl.ds(which * own_cols, own_cols)],
            heads_send.at[offset - 1, which],
            heads_recv.at[sender, which],
            where,
        )

    def merge_copy(offset, where, sender):
        return line.copy(
            merge_weight,
            merge_all.at[slot, z_rows(sender)],
            merge_send.at[offset - 1],
            merge_recv.at[sender],
            where,
        )

    def small_copy(offset, where, sender):
        return line.copy(
            small,
            small_all.at[place, sender],
            small_send.at[offset - 1],
            small_recv.at[sender],
            where,
        )

    started = []

    def start(copy):
        copy.start()
        started.append(copy)

    for offset in range(1, narrow_count):
        for which in range(3):
            start(heads_copy(offset, which, line.peer(offset), here))
    for offset in range(1, narrow_count):
        start(small_copy(offset, line.peer(offset), here))
    keep_rows.wait()
    line_rows.send_own()

    for offset in range(1, narrow_count):
        start(merge_copy(offset, line.peer(offset), here))

    for copy in keeps:
        copy.wait()
    for offset in range(1, narrow_count):
        for which in range(3):
            heads_copy(offset, which, line.peer(offset), line.peer(offset)).wait_recv()
    heads_ring.send_own()
    for offset in range(1, narrow_count):
        small_copy(offset, line.peer(offset), line.peer(offset)).wait_recv()

    def wide_copy(offset, sender):
        return pltpu.make_async_remote_copy(
            src_ref=small_all.at[sender],
            dst_ref=small_all.at[sender],
            send_sem=wide_send.at[offset - 1],
            recv_sem=wide_recv.at[sender],
            device_id={"wide": (place + offset) % wide_count},
            device_id_type=pl.DeviceIdType.MESH,
        )

    for offset in range(1, wide_count):
        start(wide_copy(offset, place))

    def project(block):
        def cols_step(cols):
            weight = heads_all[:, :, cols].reshape(width, cols.size)
            triple[pl.ds(pl.multiple_of(block * rows, rows), rows), cols] = dot(
                rows_all[block], weight, ((1,), (0,))
            )

        tiles(columns, 256, cols_step)

    def project_step(step):
        line_rows.each(step, project)

    def gather(ring, distance):
        ring.receive(distance)
        ring.receive_mate(-distance)
        if distance < ring.far:
            ring.receive_mate(distance)

    outs = []

    def keep_out(source, target):
        copy = pltpu.make_async_copy(source, target, out_sems.at[len(outs)])
        copy.start()
        outs.append(copy)

    line_rows.step(1)
    heads_ring.receive_mate(0)
    for distance in range(1, heads_ring.far):
        gather(heads_ring, distance)
    keep_merge.wait()
    for offset in range(1, narrow_count):
        merge_copy(offset, line.peer(offset), line.peer(offset)).wait_recv()
    merge_ring.send_own()
    gather(heads_ring, heads_ring.far)
    keep_out(heads_all, heads_out)
    project(here)
    for step in range(2, narrow_count):
        line_rows.step(step)
        project_step(step - 1)
        if step == 2:
            merge_ring.receive_mate(0)
            for distance in range(1, merge_ring.far):
                gather(merge_ring, distance)
    gather(merge_ring, merge_ring.far)
    keep_out(merge_all, merge_out)
    project_step(last)
    keep_out(rows_all, rows_out)
    for offset in range(1, wide_count):
        wide_copy(offset, (place + offset) % wide_count).wait_recv()
    keep_out(small_all, small_out)
    line_rows.drain()
    for copy in started:
        copy.wait_send()
    heads_ring.drain()
    merge_ring.drain()
    for copy in outs:
        copy.wait()


def gather_front(wide_count, narrow_count, layer_input, heads_weight, merge_weight, small):
    rows, width = layer_input.shape
    count, all_columns = heads_weight.shape
    columns = all_columns // narrow_count
    block = count * narrow_count
    anywhere = pl.BlockSpec(memory_space=pl.ANY)
    vmem = pl.BlockSpec(memory_space=pltpu.VMEM)
    dma = pltpu.SemaphoreType.DMA
    lines = small.shape[0]
    shapes = (
        (narrow_count, rows, width),
        (wide_count, block, columns),
        (wide_count, block, width),
        (wide_count, narrow_count, lines, 128),
    )
    far = narrow_count - 1
    return pl.pallas_call(
        functools.partial(gather_kernel, wide_count, narrow_count),
        out_shape=tuple(jax.ShapeDtypeStruct(shape, jnp.bfloat16) for shape in shapes)
        + (jax.ShapeDtypeStruct((narrow_count * rows, columns), jnp.float32),),
        in_specs=[anywhere, anywhere, anywhere, vmem],
        out_specs=(anywhere, anywhere, anywhere, anywhere, vmem),
        scratch_shapes=[pltpu.VMEM(shape, jnp.bfloat16) for shape in shapes]
        + [
            dma((2, narrow_count)),
            dma((narrow_count,)),
            dma((far, 3)),
            dma((narrow_count, 3)),
            dma((far,)),
            dma((narrow_count,)),
            dma((far,)),
            dma((narrow_count,)),
            dma((wide_count - 1,)),
            dma((wide_count,)),
            dma((5,)),
            dma((4,)),
            dma((3, wide_count, 2)),
            dma((wide_count, 2)),
            dma((3, wide_count, 2)),
            dma((wide_count, 2)),
        ],
        compiler_params=pltpu.CompilerParams(
            collective_id=5, has_side_effects=True, vmem_limit_bytes=kernel_memory
        ),
        cost_estimate=pl.CostEstimate(
            flops=80 * 10**9, bytes_accessed=200 * 2**20, transcendentals=0
        ),
        name="gather_front",
    )(layer_input, heads_weight, merge_weight, small)


def attention_forward_kernel(
    narrow_count,
    triple,
    heads_shift,
    cosine,
    signed_sine,
    first_query,
    last_query,
    own,
    merge,
    merge_shift,
    gain,
    shift,
    queries,
    keys,
    values,
    probs,
    mixed_out,
    hidden,
    hidden_low,
    normed,
    inv_std,
    merge_mat,
    probs_held,
    values_turned,
    outbound,
    mixed,
    mixed_send,
    mixed_recv,
    local_sems,
):
    line = LineExchange(narrow_count)
    bucket, own_cols = queries.shape
    rows, width = own.shape
    heads = own_cols // HDIM
    scale = HDIM ** (-0.5)
    load_merge = pltpu.make_async_copy(merge, merge_mat, local_sems.at[2])
    load_merge.start()
    line.greet()

    def keep(head):
        return pltpu.make_async_copy(
            probs_held.at[head % 2], probs.at[head], local_sems.at[head % 2]
        )

    def mixed_copy(head, offset, where, sender):
        cols = pl.ds(pl.multiple_of(sender * own_cols + head * HDIM, HDIM), HDIM)
        return line.copy(
            outbound.at[where, :, pl.ds(head * HDIM, HDIM)],
            mixed.at[:, cols],
            mixed_send.at[offset - 1, head],
            mixed_recv.at[sender, head],
            where,
        )

    started = []
    for head in range(heads):
        cols = pl.ds(head * HDIM, HDIM)

        def turn(i, carry):
            here = pl.ds(pl.multiple_of(i * rows, rows), rows)
            for which, target in enumerate((queries, keys, values)):
                wanted = pl.ds(which * own_cols + head * HDIM, HDIM)
                part = triple[here, wanted] + heads_shift[:, wanted]
                if which < 2:
                    part = rotate_lanes(part, cosine[here], -signed_sine[here])
                else:
                    values_turned[:, here] = part.T.astype(jnp.bfloat16)
                target[here, cols] = part.astype(jnp.bfloat16)
            return carry

        lax.fori_loop(0, narrow_count, turn, 0)
        if head >= 2:
            keep(head - 2).wait()
        held = probs_held.at[head % 2]

        def chunk(i, carry):
            here = pl.ds(pl.multiple_of(i * rows, rows), rows)
            scores = dot(keys[:, cols], queries[here, cols], ((1,), (1,))) * scale
            token = i * rows + lax.broadcasted_iota(jnp.int32, (bucket, rows), 1)
            seen = (token >= first_query[...]) & (token <= last_query[...])
            scores = jnp.where(seen, scores, masked_value)
            expo = jnp.exp(scores - jnp.max(scores, axis=0, keepdims=True))
            weights = (expo * (1 / jnp.sum(expo, axis=0, keepdims=True))).astype(jnp.bfloat16)
            held[:, here] = weights
            mixed_part = dot(values_turned[...], weights, ((1,), (0,)))
            outbound[i, :, cols] = mixed_part.T.astype(jnp.bfloat16)
            return carry

        lax.fori_loop(0, narrow_count, chunk, 0)
        keep(head).start()
        for offset in range(1, narrow_count):
            copy = mixed_copy(head, offset, line.peer(offset), line.mine)
            copy.start()
            started.append(copy)
    own_mixed = pltpu.make_async_copy(
        outbound.at[line.mine],
        mixed.at[:, pl.ds(pl.multiple_of(line.mine * own_cols, own_cols), own_cols)],
        local_sems.at[3],
    )
    own_mixed.start()
    own_mixed.wait()
    load_merge.wait()
    for offset in range(1, narrow_count):
        for head in range(heads):
            mixed_copy(head, offset, line.peer(offset), line.peer(offset)).wait_recv()
    mixed_out[...] = mixed[...]

    def merge_cols(cols):
        hidden[:, cols] = (
            residual_scale * own[:, cols].astype(jnp.float32)
            + dot(mixed[...], merge_mat[:, cols], ((1,), (0,)))
            + merge_shift[:, cols]
        )

    tiles(width, 256, merge_cols)

    def norm_rows(i, carry):
        some = pl.ds(pl.multiple_of(i * 16, 16), 16)
        result, centred, inverse = normalize(hidden[some], gain[...], shift[...])
        hidden[some] = result
        hidden_low[some] = result.astype(jnp.bfloat16)
        normed[some] = centred
        inv_std[some] = inverse
        return carry

    lax.fori_loop(0, rows // 16, norm_rows, 0)
    for head in range(max(heads - 2, 0), heads):
        keep(head).wait()
    for copy in started:
        copy.wait_send()


def attention_forward(
    narrow_count,
    triple,
    heads_shift,
    cosine,
    signed_sine,
    first_query,
    last_query,
    layer_input,
    merge_full,
    merge_shift,
    gain,
    shift,
):
    bucket, columns = triple.shape
    rows, width = layer_input.shape
    own_cols = columns // 3
    heads = own_cols // HDIM
    anywhere = pl.BlockSpec(memory_space=pl.ANY)
    vmem = pl.BlockSpec(memory_space=pltpu.VMEM)
    dma = pltpu.SemaphoreType.DMA

    def low_shape(*shape):
        return jax.ShapeDtypeStruct(shape, jnp.bfloat16)

    def wide_shape(*shape):
        return jax.ShapeDtypeStruct(shape, jnp.float32)

    return pl.pallas_call(
        functools.partial(attention_forward_kernel, narrow_count),
        out_shape=(
            low_shape(bucket, own_cols),
            low_shape(bucket, own_cols),
            low_shape(bucket, own_cols),
            low_shape(heads, bucket, bucket),
            low_shape(rows, width),
            wide_shape(rows, width),
            low_shape(rows, width),
            wide_shape(rows, width),
            wide_shape(rows, 1),
        ),
        in_specs=[vmem] * 7 + [anywhere] + [vmem] * 3,
        out_specs=(vmem, vmem, vmem, anywhere) + (vmem,) * 5,
        scratch_shapes=[
            pltpu.VMEM((width, width), jnp.bfloat16),
            pltpu.VMEM((2, bucket, bucket), jnp.bfloat16),
            pltpu.VMEM((HDIM, bucket), jnp.bfloat16),
            pltpu.VMEM((narrow_count, rows, own_cols), jnp.bfloat16),
            pltpu.VMEM((rows, width), jnp.bfloat16),
            dma((narrow_count - 1, heads)),
            dma((narrow_count, heads)),
            dma((4,)),
        ],
        compiler_params=pltpu.CompilerParams(
            collective_id=6, has_side_effects=True, vmem_limit_bytes=kernel_memory
        ),
        cost_estimate=pl.CostEstimate(
            flops=60 * 10**9, bytes_accessed=200 * 2**20, transcendentals=0
        ),
        name="attention_forward",
    )(
        triple,
        heads_shift,
        cosine,
        signed_sine,
        first_query,
        last_query,
        layer_input,
        merge_full,
        merge_shift,
        gain,
        shift,
    )


def shards(
    layer_input,
    heads_weight,
    heads_bias,
    merge_weight,
    merge_bias,
    norm_gains,
    norm_shifts,
    expand_weight,
    expand_bias,
    reduce_weight,
    reduce_bias,
    joined,
    prefix,
    cotangent,
):
    tok_rows, model_width = layer_input.shape
    wide_count = lax.axis_size("wide")
    narrow_count = lax.axis_size("narrow")
    count = wide_count * narrow_count
    bucket_len = tok_rows * narrow_count
    own_heads = HEADS // narrow_count
    own_cols = own_heads * HDIM
    share = expand_weight.shape[2]
    joined_flag = joined[0]
    prefix_pair = prefix[0]
    narrow_index = lax.axis_index("narrow")
    positions = jnp.arange(bucket_len, dtype=jnp.int32)
    second_seq, local_pos, prefix_len = layout(positions, joined_flag, prefix_pair, bucket_len)
    cosine, sine_table = rotary_tables(local_pos, HDIM)
    first_query = jnp.where(local_pos < prefix_len, positions - local_pos, positions)
    last_query = jnp.where(
        (joined_flag == 1) | (second_seq == 1), bucket_len - 1, bucket_len // 2 - 1
    )

    smalls = (heads_bias, merge_bias, norm_gains, norm_shifts, expand_bias, reduce_bias)
    rows_input, heads_mat, merge_full, small_all, triple = gather_front(
        wide_count, narrow_count, layer_input, heads_weight, merge_weight, pack_small(smalls)
    )
    rows_input = rows_input.reshape(bucket_len, model_width)
    heads_mat = heads_mat.reshape(model_width, 3 * own_cols)
    merge_full = merge_full.reshape(model_width, model_width)
    heads_shift, merge_shift, gains, shifts, expand_shift, reduce_shift = unpack_small(
        small_all, smalls
    )
    own_shift = lax.dynamic_index_in_dim(
        heads_shift.reshape(3, narrow_count, own_cols), narrow_index, 1, keepdims=False
    ).reshape(1, -1)
    cosine_wide = jnp.concatenate([cosine, cosine], axis=1)
    signed_sine = jnp.concatenate([sine_table, -sine_table], axis=1)
    (
        queries,
        keys,
        values,
        probs_low,
        mixed,
        hidden,
        hidden_low,
        normed_one,
        inv_one,
    ) = attention_forward(
        narrow_count,
        triple,
        own_shift,
        cosine_wide,
        signed_sine,
        first_query.reshape(-1, 1),
        last_query.reshape(-1, 1),
        layer_input,
        merge_full,
        merge_shift.reshape(1, -1),
        gains[0].reshape(1, -1),
        shifts[0].reshape(1, -1),
    )

    tile_rows = -share % 16
    padded = -(-share // 256) * 256
    expand_low = jnp.pad(expand_weight.transpose(1, 2, 0), ((0, 0), (0, tile_rows), (0, 0)))
    gate_expand = lax.all_gather(expand_low[0], "narrow", axis=1, tiled=True)
    upper_low, _ = lax.optimization_barrier((expand_low[1], small_all))
    upper_expand = lax.all_gather(upper_low, "narrow", axis=1, tiled=True)
    reduce_low = jnp.pad(reduce_weight, ((0, tile_rows), (0, 0)))
    reduce_full, rows_all, active, slope, gelu, feed_sum = geglu_forward(
        wide_count,
        narrow_count,
        hidden_low,
        gate_expand,
        upper_expand,
        reduce_low,
        jnp.pad(expand_shift, ((0, 0), (0, padded - share))),
    )
    feed = feed_sum + reduce_shift
    output_float, normed_two, inv_two = normalize(
        residual_scale * hidden + feed, gains[1], shifts[1]
    )
    layer_output = low(output_float)

    grad_out = cotangent.astype(jnp.float32)
    gain_two_grad = jnp.sum(grad_out * normed_two, axis=0)
    shift_two_grad = jnp.sum(grad_out, axis=0)
    sum_two_grad = normalize_back(grad_out, normed_two, inv_two, gains[1])
    feed_grad = low(sum_two_grad)
    reduce_weight_gradient, expand_part, hidden_part, unit_sums = geglu_backward(
        wide_count,
        narrow_count,
        feed_grad,
        gate_expand,
        upper_expand,
        reduce_full,
        slope,
        gelu,
        active,
        rows_all,
    )
    expand_weight_gradient = (
        lax.psum_scatter(expand_part, "narrow", scatter_dimension=2, tiled=True)[:, :share]
        .astype(jnp.float32)
        .transpose(2, 0, 1)
    )
    hidden_grad = residual_scale * sum_two_grad + hidden_part
    gain_one_grad = jnp.sum(hidden_grad * normed_one, axis=0)
    shift_one_grad = jnp.sum(hidden_grad, axis=0)
    sum_one_grad = normalize_back(hidden_grad, normed_one, inv_one, gains[0])
    attended_grad = low(sum_one_grad)
    triple_grad, merge_weight_gradient, heads_sums, merge_sums = attention_backward(
        wide_count,
        narrow_count,
        attended_grad,
        merge_full,
        mixed,
        queries,
        keys,
        values,
        probs_low,
        cosine_wide,
        signed_sine,
    )

    mine_narrow = (jnp.arange(narrow_count) == narrow_index).astype(jnp.float32)
    mine_wide = (jnp.arange(wide_count) == lax.axis_index("wide")).astype(jnp.float32)
    heads_sums = heads_sums.reshape(3, 1, own_cols)
    heads_sums = (heads_sums * mine_narrow[None, :, None]).reshape(count, -1)
    merge_sums = merge_sums.reshape(count, -1)
    norm_sums = (
        jnp.stack([gain_one_grad, gain_two_grad, shift_one_grad, shift_two_grad])
        .reshape(4, count, -1)
        .transpose(1, 0, 2)
        .reshape(count, -1)
    )
    expand_sums = unit_sums[:, :share]
    expand_sums = (
        expand_sums.reshape(2, narrow_count, -1).transpose(1, 0, 2).reshape(1, narrow_count, -1)
        * mine_wide[:, None, None]
    ).reshape(count, -1)
    reduce_sums = jnp.sum(feed_grad, axis=0, dtype=jnp.float32).reshape(1, narrow_count, -1)
    reduce_sums = jnp.broadcast_to(
        reduce_sums, (wide_count, narrow_count, reduce_sums.shape[2])
    ).reshape(count, -1)
    pieces = (heads_sums, merge_sums, norm_sums, expand_sums, reduce_sums)
    packed = jnp.concatenate(pieces, axis=1)
    packed = jnp.pad(packed, ((0, 0), (0, -packed.shape[1] % 1024)))
    input_part, heads_weight_gradient, summed = input_backward(
        wide_count,
        narrow_count,
        rows_input,
        triple_grad,
        heads_mat,
        packed.reshape(wide_count, narrow_count, -1, 128),
    )
    input_gradient = residual_scale * sum_one_grad + input_part
    summed = summed.reshape(-1)
    ends = []
    start = 0
    for piece in pieces:
        ends.append(summed[start : start + piece.shape[1]])
        start += piece.shape[1]
    norm_ends = ends[2].reshape(4, -1)
    return (
        layer_output,
        input_gradient,
        heads_weight_gradient,
        ends[0],
        merge_weight_gradient,
        ends[1],
        norm_ends[:2],
        norm_ends[2:],
        expand_weight_gradient,
        ends[3].reshape(2, -1),
        reduce_weight_gradient[:share],
        ends[4],
    )


def solution(mesh):
    return jax.shard_map(
        shards,
        mesh=mesh,
        in_specs=(
            P(("wide", "narrow"), None),
            P(("wide", "narrow"), None),
            P(("wide", "narrow")),
            P(("wide", "narrow"), None),
            P(("wide", "narrow")),
            P(None, ("wide", "narrow")),
            P(None, ("wide", "narrow")),
            P("narrow", None, "wide"),
            P(None, ("wide", "narrow")),
            P("wide", "narrow"),
            P("narrow"),
            P("wide"),
            P("wide", None),
            P(("wide", "narrow"), None),
        ),
        out_specs=(
            P(("wide", "narrow"), None),
            P(("wide", "narrow"), None),
            P(("wide", "narrow"), None),
            P(("wide", "narrow")),
            P(("wide", "narrow"), None),
            P(("wide", "narrow")),
            P(None, ("wide", "narrow")),
            P(None, ("wide", "narrow")),
            P("narrow", None, "wide"),
            P(None, ("wide", "narrow")),
            P("wide", "narrow"),
            P("narrow"),
        ),
        check_vma=False,
    )
```

```python
import functools
import math

import jax
import jax.numpy as jnp
import numpy as np
from jax import lax
from jax.experimental import pallas as pl
from jax.experimental.pallas import tpu as pltpu
from jax.sharding import PartitionSpec as P

HEADS = 16
HDIM = 128


residual_scale = 48.0**0.5
norm_eps = 1e-05
masked_value = -1e30
kernel_memory = 60 * 2**20


def rotary_speeds(head_size):
    index = np.arange(head_size) % (head_size // 2)
    return (10000.0 ** (-2.0 * index / head_size)).astype(np.float32)[None]


def normalize(values, gain, shift):
    centre = jnp.mean(values, axis=-1, keepdims=True)
    centred = values - centre
    variance = jnp.mean(centred * centred, axis=-1, keepdims=True)
    inv_std = lax.rsqrt(variance + norm_eps)
    normed = centred * inv_std
    return (normed * gain + shift, normed, inv_std)


def normalize_back(upstream, normed, inv_std, gain):
    scaled = upstream * gain
    return inv_std * (
        scaled
        - jnp.mean(scaled, axis=-1, keepdims=True)
        - normed * jnp.mean(scaled * normed, axis=-1, keepdims=True)
    )


def dot(left, right, dims):
    return lax.dot_general(left, right, (dims, ((), ())), preferred_element_type=jnp.float32)


def low(values):
    return values.astype(jnp.bfloat16)


def pack_small(parts):
    packed = jnp.concatenate([part.reshape(-1) for part in parts])
    return jnp.pad(packed, (0, -packed.size % 2048)).reshape(-1, 128)


def unpack_small(everyone, parts):
    wide_count, narrow_count = everyone.shape[:2]
    everyone = everyone.reshape(wide_count, narrow_count, -1).astype(jnp.float32)
    pieces = []
    start = 0
    for part in parts:
        pieces.append(everyone[:, :, start : start + part.size])
        start += part.size

    def pairs(piece):
        piece = piece.reshape(-1, 2, piece.shape[-1] // 2)
        return piece.transpose(1, 0, 2).reshape(2, -1)

    own_expand = lax.dynamic_index_in_dim(
        pieces[4], lax.axis_index("wide"), 0, keepdims=False
    )
    return (
        pieces[0].reshape(-1),
        pieces[1].reshape(-1),
        pairs(pieces[2]),
        pairs(pieces[3]),
        pairs(own_expand),
        pieces[5][0].reshape(-1),
    )


def ring_place(wide_count):
    ring = wide_count // 2
    mine = lax.axis_index("wide")
    chip = mine // 2
    core = mine % 2
    position = 2 * (chip // 2) + (chip % 2 + chip // 2) % 2
    return ring, position, core


def chip_at(position, ring):
    position = (position + 2 * ring) % ring
    return 2 * (position // 2) + (position + position // 2) % 2


class PlaneExchange:
    def __init__(self, wide_count, own, blocks, parts, from_mate, incoming, sems, cols=None):
        self.ring, self.position, self.core = ring_place(wide_count)
        self.own, self.blocks, self.parts = own, blocks, parts
        self.from_mate, self.incoming = from_mate, incoming
        (
            self.gather_send,
            self.gather_recv,
            self.mate_send,
            self.mate_recv,
            self.sum_send,
            self.sum_recv,
            self.own_sem,
        ) = sems
        self.half = parts.shape[1] // 2
        self.cols = slice(None) if cols is None else cols
        self.far = self.ring // 2
        self.started = []

    def device(self, offset, mate=False):
        core = 1 - self.core if mate else self.core
        return {"wide": 2 * chip_at(self.position + offset, self.ring) + core}

    def slot(self, offset, mate=False):
        core = 1 - self.core if mate else self.core
        return 2 * chip_at(self.position + offset, self.ring) + core

    def rows(self, part):
        return pl.ds(part * self.half, self.half)

    def greet(self):
        barrier = pltpu.get_barrier_semaphore()
        for where in (self.device(-1), self.device(1), self.device(0, True)):
            pl.semaphore_signal(
                barrier, inc=1, device_id=where, device_id_type=pl.DeviceIdType.MESH
            )
        pl.semaphore_wait(barrier, 3)

    def start(self, source, target, send_sem, recv_sem, where):
        copy = pltpu.make_async_remote_copy(
            src_ref=source,
            dst_ref=target,
            send_sem=send_sem,
            recv_sem=recv_sem,
            device_id=where,
            device_id_type=pl.DeviceIdType.MESH,
        )
        copy.start()
        self.started.append(copy)

    def pass_on(self, lane, slot, part, where, source=None):
        target = self.blocks.at[slot, self.rows(part)]
        self.start(
            target if source is None else source,
            target,
            self.gather_send.at[lane, slot, part],
            self.gather_recv.at[slot, part],
            where,
        )

    def arrived(self, slot, part):
        target = self.blocks.at[slot, self.rows(part)]
        pltpu.make_async_remote_copy(
            src_ref=target,
            dst_ref=target,
            send_sem=self.gather_send.at[0, slot, part],
            recv_sem=self.gather_recv.at[slot, part],
            device_id=self.device(1),
            device_id_type=pl.DeviceIdType.MESH,
        ).wait_recv()

    def send_own(self):
        slot = self.slot(0)
        keep = None
        own = self.blocks.at[slot]
        if self.own is not None:
            own = self.own
            keep = pltpu.make_async_copy(own, self.blocks.at[slot], self.own_sem)
            keep.start()
        first, second = own.at[self.rows(0)], own.at[self.rows(1)]
        self.pass_on(0, slot, 0, self.device(1), first)
        self.pass_on(1, slot, 1, self.device(-1), second)
        self.pass_on(2, slot, 0, self.device(0, True), first)
        self.pass_on(2, slot, 1, self.device(0, True), second)
        self.pass_on(0, slot, 1, self.device(1), second)
        self.pass_on(1, slot, 0, self.device(-1), first)
        return keep

    def receive(self, distance):
        mate = self.device(0, True)
        left, right = self.slot(-distance), self.slot(distance)
        if distance == self.far:
            for part in range(2):
                self.arrived(left, part)
                self.pass_on(2, left, part, mate)
            return
        further = distance < self.far - 1
        self.arrived(left, 0)
        self.pass_on(0, left, 0, self.device(1))
        self.pass_on(2, left, 0, mate)
        self.arrived(right, 1)
        self.pass_on(1, right, 1, self.device(-1))
        self.pass_on(2, right, 1, mate)
        self.arrived(left, 1)
        if further:
            self.pass_on(0, left, 1, self.device(1))
        self.pass_on(2, left, 1, mate)
        self.arrived(right, 0)
        if further:
            self.pass_on(1, right, 0, self.device(-1))
        self.pass_on(2, right, 0, mate)

    def receive_mate(self, offset):
        for part in range(2):
            self.arrived(self.slot(offset, True), part)

    def share(self, offset):
        chip = chip_at(self.position + offset, self.ring)
        self.start(
            self.parts.at[self.slot(offset, True), :, self.cols],
            self.from_mate.at[chip, :, self.cols],
            self.mate_send.at[chip],
            self.mate_recv.at[chip],
            self.device(0, True),
        )

    def shared(self, offset):
        chip = chip_at(self.position + offset, self.ring)
        pltpu.make_async_remote_copy(
            src_ref=self.parts.at[self.slot(offset), :, self.cols],
            dst_ref=self.from_mate.at[chip, :, self.cols],
            send_sem=self.mate_send.at[chip],
            recv_sem=self.mate_recv.at[chip],
            device_id=self.device(0, True),
            device_id_type=pl.DeviceIdType.MESH,
        ).wait_recv()

    def chip_sum(self, offset, rows):
        chip = chip_at(self.position + offset, self.ring)
        return self.parts[self.slot(offset), rows, self.cols].astype(
            jnp.float32
        ) + self.from_mate[chip, rows, self.cols].astype(jnp.float32)

    def send_sum(self, way, distance, part):
        offset = distance if way == 0 else -distance
        begins = self.far if part == way else self.far - 1
        slot = self.slot(offset)
        if distance < begins:
            self.sum_arrived(way, distance, part)

        def chunk(i, carry):
            here = pl.ds(pl.multiple_of(i * 16, 16), 16)
            there = pl.ds(pl.multiple_of(part * self.half + i * 16, 16), 16)
            total = self.chip_sum(offset, there)
            if distance < begins:
                total += self.incoming[way, distance, part, here, self.cols].astype(jnp.float32)
            self.parts[slot, there, self.cols] = total.astype(jnp.bfloat16)
            return carry

        lax.fori_loop(0, self.half // 16, chunk, 0)
        self.start(
            self.parts.at[slot, self.rows(part), self.cols],
            self.incoming.at[way, distance - 1, part, :, self.cols],
            self.sum_send.at[way, distance - 1, part],
            self.sum_recv.at[way, distance - 1, part],
            self.device(1 if way == 0 else -1),
        )

    def sum_arrived(self, way, distance, part):
        target = self.incoming.at[way, distance, part, :, self.cols]
        pltpu.make_async_remote_copy(
            src_ref=target,
            dst_ref=target,
            send_sem=self.sum_send.at[way, distance, part],
            recv_sem=self.sum_recv.at[way, distance, part],
            device_id=self.device(1),
            device_id_type=pl.DeviceIdType.MESH,
        ).wait_recv()

    def run(self, compute, before, between):
        keep = self.send_own()
        keep.wait()
        self.receive_mate(0)
        compute(chip_at(self.position, self.ring))
        self.share(0)
        for distance in range(1, self.far):
            self.receive(distance)
            for offset in (-distance, distance):
                self.receive_mate(offset)
                compute(chip_at(self.position + offset, self.ring))
                self.share(offset)
            if distance == self.far - 1:
                self.first_sums()
        self.receive(self.far)
        self.receive_mate(self.far)
        compute(chip_at(self.position + self.far, self.ring))
        self.share(self.far)
        before()
        self.far_sums()
        between()
        self.last_sums()

    def run_gather(self, compute, between):
        keep = self.send_own()
        keep.wait()
        self.receive_mate(0)
        compute(chip_at(self.position, self.ring))
        done = 1
        for distance in range(1, self.far):
            self.receive(distance)
            between(done)
            done += 1
            for offset in (-distance, distance):
                self.receive_mate(offset)
                compute(chip_at(self.position + offset, self.ring))
        self.receive(self.far)
        between(done)
        done += 1
        self.receive_mate(self.far)
        compute(chip_at(self.position + self.far, self.ring))
        return done

    def run_sums(self, compute):
        compute(chip_at(self.position + self.far, self.ring))
        self.share(self.far)
        for distance in range(self.far - 1, 0, -1):
            for offset in (-distance, distance):
                compute(chip_at(self.position + offset, self.ring))
                self.share(offset)
            if distance == self.far - 1:
                self.far_sums()
                self.first_sums()
        compute(chip_at(self.position, self.ring))
        self.share(0)
        self.last_sums()

    def first_sums(self):
        distance = self.far - 1
        self.shared(distance)
        self.send_sum(0, distance, 1)
        self.shared(-distance)
        self.send_sum(1, distance, 0)

    def far_sums(self):
        self.shared(self.far)
        self.send_sum(0, self.far, 0)
        self.send_sum(1, self.far, 1)

    def last_sums(self):
        for distance in range(self.far - 1, 0, -1):
            if distance < self.far - 1:
                self.shared(distance)
                self.shared(-distance)
            self.send_sum(0, distance, 0)
            self.send_sum(1, distance, 1)
            if distance < self.far - 1:
                self.send_sum(0, distance, 1)
                self.send_sum(1, distance, 0)

    def finish(self, result):
        self.shared(0)
        for part in range(2):
            for way in range(2):
                self.sum_arrived(way, 0, part)

            def chunk(i, carry):
                here = pl.ds(pl.multiple_of(i * 16, 16), 16)
                there = pl.ds(pl.multiple_of(part * self.half + i * 16, 16), 16)
                total = self.chip_sum(0, there)
                for way in range(2):
                    total += self.incoming[way, 0, part, here, self.cols].astype(jnp.float32)
                result[there, self.cols] = total.astype(result.dtype)
                return carry

            lax.fori_loop(0, self.half // 16, chunk, 0)

    def drain(self):
        for copy in self.started:
            copy.wait_send()


def sum_scratch(wide_count, rows, width):
    ring = wide_count // 2
    far = ring // 2
    dma = pltpu.SemaphoreType.DMA
    return [
        pltpu.VMEM((wide_count, rows, width), jnp.bfloat16),
        pltpu.VMEM((ring, rows, width), jnp.bfloat16),
        pltpu.VMEM((2, far, 2, rows // 2, width), jnp.bfloat16),
        dma((ring,)),
        dma((ring,)),
        dma((2, far, 2)),
        dma((2, far, 2)),
    ]


def exchange_scratch(wide_count, rows, width):
    dma = pltpu.SemaphoreType.DMA
    return [
        pltpu.VMEM((wide_count, rows, width), jnp.bfloat16),
        dma((3, wide_count, 2)),
        dma((wide_count, 2)),
        dma(()),
    ] + sum_scratch(wide_count, rows, width)


def load_padded(source, target, sem):
    filled = source.shape[0]
    copy = pltpu.make_async_copy(source, target.at[pl.ds(0, filled)], sem)
    copy.start()
    if filled < target.shape[0]:
        target[pl.ds(filled, target.shape[0] - filled)] = jnp.zeros(
            (target.shape[0] - filled, target.shape[1]), target.dtype
        )
    return copy


def pair_rows(ref, chip):
    block = ref[pl.ds(2 * chip, 2)]
    return block.reshape(2 * block.shape[1], block.shape[2])


def set_pair(ref, chip, cols, value):
    rows = ref.shape[1]
    ref[2 * chip, :, cols] = value[:rows].astype(ref.dtype)
    ref[2 * chip + 1, :, cols] = value[rows:].astype(ref.dtype)


def tiles(count, tile, body, start=0):
    def step(i, carry):
        body(pl.ds(pl.multiple_of(start + i * tile, tile), tile))
        return carry

    lax.fori_loop(0, count // tile, step, 0)


class LineExchange:
    def __init__(self, narrow_count):
        self.count = narrow_count
        self.mine = lax.axis_index("narrow")
        self.started = []

    def peer(self, offset):
        return (self.mine + offset) % self.count

    def greet(self, extra=0):
        barrier = pltpu.get_barrier_semaphore()
        for offset in range(1, self.count):
            pl.semaphore_signal(
                barrier,
                inc=1,
                device_id={"narrow": self.peer(offset)},
                device_id_type=pl.DeviceIdType.MESH,
            )
        pl.semaphore_wait(barrier, self.count - 1 + extra)

    def copy(self, source, target, send_sem, recv_sem, where):
        return pltpu.make_async_remote_copy(
            src_ref=source,
            dst_ref=target,
            send_sem=send_sem,
            recv_sem=recv_sem,
            device_id={"narrow": where},
            device_id_type=pl.DeviceIdType.MESH,
        )

    def send(self, offset, source, landing, send_sems, recv_sems):
        peer = self.peer(offset)
        copy = self.copy(
            source, landing.at[self.mine], send_sems.at[offset - 1], recv_sems.at[self.mine], peer
        )
        copy.start()
        self.started.append(copy)

    def arrived(self, offset, landing, send_sems, recv_sems):
        peer = self.peer(offset)
        self.copy(
            landing.at[peer], landing.at[peer], send_sems.at[offset - 1], recv_sems.at[peer], peer
        ).wait_recv()

    def drain(self):
        for copy in self.started:
            copy.wait_send()


class LineSum:
    def __init__(self, line, view, landing, send_sems, recv_sems):
        self.line, self.view, self.landing = line, view, landing
        self.send_sems, self.recv_sems = send_sems, recv_sems
        self.last = line.count - 1

    def reaches(self, way, offset):
        here = self.line.mine
        return here + offset <= self.last if way == 0 else here - offset >= 0

    def follows(self, way):
        here = self.line.mine
        return here > 0 if way == 0 else here < self.last

    def target(self, way, offset):
        return self.line.mine + offset if way == 0 else self.line.mine - offset

    def copy(self, way, offset):
        return self.line.copy(
            self.view(self.target(way, offset)),
            self.landing.at[way, offset - 1],
            self.send_sems.at[way, offset - 1],
            self.recv_sems.at[way, offset - 1],
            self.line.mine + 1 if way == 0 else self.line.mine - 1,
        )

    def arrived(self, way, offset):
        landing = self.landing.at[way, offset]
        self.line.copy(
            landing,
            landing,
            self.send_sems.at[way, offset],
            self.recv_sems.at[way, offset],
            self.line.mine,
        ).wait_recv()

    def add(self, way, offset):
        held = self.view(self.target(way, offset))

        def chunk(i, carry):
            some = pl.ds(pl.multiple_of(i * 16, 16), 16)
            held[some] = (
                held[some].astype(jnp.float32)
                + self.landing[way, offset, some].astype(jnp.float32)
            ).astype(jnp.bfloat16)
            return carry

        lax.fori_loop(0, self.landing.shape[2] // 16, chunk, 0)

    def begin(self, offset):
        for way in range(2):

            @pl.when(self.reaches(way, offset) & jnp.logical_not(self.follows(way)))
            def _():
                self.copy(way, offset).start()

    def step(self, offset):
        for way in range(2):

            @pl.when(self.reaches(way, offset) & self.follows(way))
            def _():
                self.arrived(way, offset)
                self.add(way, offset)
                self.copy(way, offset).start()

    def finish(self, result):
        held = self.view(self.line.mine)
        count = self.landing.shape[2] // 16

        def begin(i, carry):
            some = pl.ds(pl.multiple_of(i * 16, 16), 16)
            result[some] = held[some].astype(result.dtype)
            return carry

        lax.fori_loop(0, count, begin, 0)
        for way in range(2):

            @pl.when(self.follows(way))
            def _():
                self.arrived(way, 0)

                def chunk(i, carry):
                    some = pl.ds(pl.multiple_of(i * 16, 16), 16)
                    result[some] += self.landing[way, 0, some].astype(result.dtype)
                    return carry

                lax.fori_loop(0, count, chunk, 0)

    def drain(self):
        for offset in range(1, self.last + 1):
            for way in range(2):

                @pl.when(self.reaches(way, offset))
                def _():
                    self.copy(way, offset).wait_send()


class LineGather:
    def __init__(self, line, view, send_sems, recv_sems):
        self.line, self.view = line, view
        self.send_sems, self.recv_sems = send_sems, recv_sems
        self.last = line.count - 1

    def copy(self, way, block):
        target = self.view(block)
        here = self.line.mine
        return self.line.copy(
            target,
            target,
            self.send_sems.at[way, block],
            self.recv_sems.at[block],
            here + 1 if way == 0 else here - 1,
        )

    def goes(self, way):
        return self.line.mine < self.last if way == 0 else self.line.mine > 0

    def has(self, way, step):
        here = self.line.mine
        return here - step >= 0 if way == 0 else here + step <= self.last

    def block(self, way, step):
        return self.line.mine - step if way == 0 else self.line.mine + step

    def send_own(self):
        for way in range(2):

            @pl.when(self.goes(way))
            def _():
                self.copy(way, self.line.mine).start()

    def step(self, step):
        for way in range(2):

            @pl.when(self.has(way, step))
            def _():
                self.copy(way, self.block(way, step)).wait_recv()

                @pl.when(self.goes(way))
                def _():
                    self.copy(way, self.block(way, step)).start()

    def each(self, step, body):
        for way in range(2):

            @pl.when(self.has(way, step))
            def _():
                body(self.block(way, step))

    def drain(self):
        for way in range(2):
            for step in range(self.last + 1):

                @pl.when(self.has(way, step) & self.goes(way))
                def _():
                    self.copy(way, self.block(way, step)).wait_send()


def greet_plane(plane):
    barrier = pltpu.get_barrier_semaphore()
    for where in (plane.device(-1), plane.device(1), plane.device(0, True)):
        pl.semaphore_signal(barrier, inc=1, device_id=where, device_id_type=pl.DeviceIdType.MESH)


def geglu_forward_kernel(
    wide_count,
    narrow_count,
    own,
    gate_expand,
    upper_expand,
    reduce,
    shift,
    hidden,
    cotangent,
    reduce_shift,
    gain,
    norm_shift,
    reduce_out,
    rows_all,
    active_out,
    slope_out,
    gelu_out,
    layer_output,
    sum_grad,
    feed_grad,
    row_sums,
    feed,
    blocks,
    gather_send,
    gather_recv,
    own_sem,
    parts,
    from_mate,
    incoming,
    mate_send,
    mate_recv,
    sum_send,
    sum_recv,
    expand_mat,
    reduce_mat,
    active,
    slope,
    gelu,
    load_sems,
    keep_sems,
    reduce_send,
    reduce_recv,
    late_mate_send,
    late_mate_recv,
    late_sum_send,
    late_sum_recv,
):
    sems = (gather_send, gather_recv, mate_send, mate_recv, sum_send, sum_recv, own_sem)
    late_sems = (None, None, late_mate_send, late_mate_recv, late_sum_send, late_sum_recv, None)
    line = LineExchange(narrow_count)
    filled, cols = reduce.shape
    width = own.shape[1]
    upper = (2 * line.mine) // narrow_count
    late = pl.multiple_of((1 - upper) * (width - cols), cols)
    early = pl.multiple_of(upper * cols, cols)
    plane = PlaneExchange(
        wide_count, own, blocks, parts, from_mate, incoming, sems, pl.ds(early, width - cols)
    )
    late_plane = PlaneExchange(
        wide_count, None, None, parts, from_mate, incoming, late_sems, pl.ds(late, cols)
    )
    loads = [
        load_padded(gate_expand, expand_mat.at[0], load_sems.at[0]),
        load_padded(upper_expand, expand_mat.at[1], load_sems.at[1]),
    ]

    def reduce_cols(block):
        return reduce_mat.at[
            pl.ds(0, filled), pl.ds(pl.multiple_of(block * cols, cols), cols)
        ]

    line_reduce = LineGather(line, reduce_cols, reduce_send, reduce_recv)
    own_reduce = pltpu.make_async_copy(reduce, reduce_cols(line.mine), load_sems.at[2])
    own_reduce.start()
    if filled < reduce_mat.shape[0]:
        reduce_mat[filled:] = jnp.zeros(
            (reduce_mat.shape[0] - filled, reduce_mat.shape[1]), reduce_mat.dtype
        )
    greet_plane(plane)
    line.greet(3)
    own_reduce.wait()
    line_reduce.send_own()
    kept = []
    waiting = list(loads)

    def compute(chip):
        while waiting:
            waiting.pop().wait()

        def units(cols):
            rows = pair_rows(blocks, chip)
            gate = dot(rows, expand_mat[0, cols], ((1,), (1,))) + shift[0:1, cols]
            upper = dot(rows, expand_mat[1, cols], ((1,), (1,))) + shift[1:2, cols]
            factor = math.sqrt(2 / math.pi)
            square = gate * gate
            bend = jnp.tanh(factor * gate * (1 + 0.044715 * square))
            value = 0.5 * gate * (1 + bend)
            pull = 0.5 * (1 + bend) + 0.5 * gate * (1 - bend * bend) * factor * (
                1 + 3 * 0.044715 * square
            )
            set_pair(active, chip, cols, value * upper)
            set_pair(slope, chip, cols, pull * upper)
            set_pair(gelu, chip, cols, value)

        tiles(active.shape[2], 256, units)

        pair = pl.ds(2 * chip, 2)
        for index, (source, target) in enumerate(
            ((active, active_out), (slope, slope_out), (gelu, gelu_out), (blocks, rows_all))
        ):
            copy = pltpu.make_async_copy(
                source.at[pair], target.at[pair], keep_sems.at[chip, index]
            )
            copy.start()
            kept.append(copy)

    def compute_sums(start, count):
        def compute(chip):
            def outputs(some):
                part = dot(pair_rows(active, chip), reduce_mat[:, some], ((1,), (0,)))
                set_pair(parts, chip, some, part)

            tiles(count, 256, outputs, start)

        return compute

    def between(index):
        if index < narrow_count:
            line_reduce.step(index)

    done = plane.run_gather(compute, between)
    for step in range(done, narrow_count - 1):
        line_reduce.step(step)
    plane.run_sums(compute_sums(early, width - cols))
    line_reduce.step(narrow_count - 1)
    keep_reduce = pltpu.make_async_copy(
        reduce_mat.at[pl.ds(0, filled)], reduce_out, load_sems.at[3]
    )
    keep_reduce.start()
    late_plane.run_sums(compute_sums(late, cols))
    plane.finish(feed)
    late_plane.finish(feed)

    row_sums[...] = jnp.zeros_like(row_sums)

    def norm_rows(i, carry):
        some = pl.ds(pl.multiple_of(i * 16, 16), 16)
        result, normed, inverse = normalize(
            residual_scale * hidden[some] + feed[some] + reduce_shift[...],
            gain[...],
            norm_shift[...],
        )
        layer_output[some] = result.astype(jnp.bfloat16)
        upstream = cotangent[some].astype(jnp.float32)
        total = normalize_back(upstream, normed, inverse, gain[...])
        sum_grad[some] = total
        feed_grad[some] = total.astype(jnp.bfloat16)
        row_sums[0:1] += jnp.sum(upstream * normed, axis=0, keepdims=True)
        row_sums[1:2] += jnp.sum(upstream, axis=0, keepdims=True)
        row_sums[2:3] += jnp.sum(total, axis=0, keepdims=True)
        return carry

    lax.fori_loop(0, own.shape[0] // 16, norm_rows, 0)
    plane.drain()
    late_plane.drain()
    keep_reduce.wait()
    line_reduce.drain()
    for copy in kept:
        copy.wait()


def geglu_forward(
    wide_count,
    narrow_count,
    hidden_low,
    gate_expand,
    upper_expand,
    reduce_weight,
    shift,
    hidden,
    cotangent,
    reduce_shift,
    gain,
    norm_shift,
):
    rows, width = hidden_low.shape
    padded = shift.shape[1]
    anywhere = pl.BlockSpec(memory_space=pl.ANY)
    vmem = pl.BlockSpec(memory_space=pltpu.VMEM)
    kept = jax.ShapeDtypeStruct((wide_count, rows, padded), jnp.bfloat16)
    scratch = [pltpu.VMEM((rows, width), jnp.float32)]
    scratch += exchange_scratch(wide_count, rows, width) + [
        pltpu.VMEM((2, padded, width), jnp.bfloat16),
        pltpu.VMEM((padded, width), jnp.bfloat16),
        pltpu.VMEM((wide_count, rows, padded), jnp.bfloat16),
        pltpu.VMEM((wide_count, rows, padded), jnp.bfloat16),
        pltpu.VMEM((wide_count, rows, padded), jnp.bfloat16),
        pltpu.SemaphoreType.DMA((4,)),
        pltpu.SemaphoreType.DMA((wide_count // 2, 4)),
        pltpu.SemaphoreType.DMA((2, narrow_count)),
        pltpu.SemaphoreType.DMA((narrow_count,)),
    ] + sum_scratch(wide_count, rows, width)[3:]
    return pl.pallas_call(
        functools.partial(geglu_forward_kernel, wide_count, narrow_count),
        out_shape=(
            jax.ShapeDtypeStruct((reduce_weight.shape[0], width), jnp.bfloat16),
            jax.ShapeDtypeStruct((wide_count, rows, width), jnp.bfloat16),
            kept,
            kept,
            kept,
            jax.ShapeDtypeStruct((rows, width), jnp.bfloat16),
            jax.ShapeDtypeStruct((rows, width), jnp.float32),
            jax.ShapeDtypeStruct((rows, width), jnp.bfloat16),
            jax.ShapeDtypeStruct((3, width), jnp.float32),
        ),
        in_specs=[anywhere] * 4 + [vmem] * 6,
        out_specs=(anywhere,) * 5 + (vmem,) * 4,
        scratch_shapes=scratch,
        compiler_params=pltpu.CompilerParams(
            collective_id=1, has_side_effects=True, vmem_limit_bytes=kernel_memory
        ),
        cost_estimate=pl.CostEstimate(
            flops=6 * wide_count * rows * padded * width, bytes_accessed=200 * 2**20, transcendentals=0
        ),
        name="geglu_forward",
    )(
        hidden_low,
        gate_expand,
        upper_expand,
        reduce_weight,
        shift,
        hidden,
        cotangent,
        reduce_shift,
        gain,
        norm_shift,
    )


def geglu_backward_kernel(
    wide_count,
    narrow_count,
    own,
    gate_expand,
    upper_expand,
    reduce,
    slope_in,
    gelu_in,
    active_in,
    rows_in,
    reduce_grad,
    expand_part,
    hidden_grad,
    unit_sums,
    blocks,
    gather_send,
    gather_recv,
    own_sem,
    parts,
    from_mate,
    incoming,
    mate_send,
    mate_recv,
    sum_send,
    sum_recv,
    expand_mat,
    reduce_mat,
    slope,
    gelu,
    active,
    rows_all,
    staged,
    load_sems,
    keep_sems,
    line_in,
    line_send,
    line_recv,
):
    sems = (gather_send, gather_recv, mate_send, mate_recv, sum_send, sum_recv, own_sem)
    plane = PlaneExchange(wide_count, own, blocks, parts, from_mate, incoming, sems)
    loads = [
        load_padded(gate_expand, expand_mat.at[0], load_sems.at[0]),
        load_padded(upper_expand, expand_mat.at[1], load_sems.at[1]),
        load_padded(reduce, reduce_mat, load_sems.at[2]),
        pltpu.make_async_copy(slope_in, slope, load_sems.at[3]),
        pltpu.make_async_copy(gelu_in, gelu, load_sems.at[4]),
    ]
    late_loads = [
        pltpu.make_async_copy(active_in, active, load_sems.at[5]),
        pltpu.make_async_copy(rows_in, rows_all, load_sems.at[6]),
    ]
    for copy in loads[3:]:
        copy.start()
    unit_sums[...] = jnp.zeros_like(unit_sums)
    line = LineExchange(narrow_count)
    filled, line_cols = line_in.shape[2:]

    def line_part(block):
        return reduce_mat.at[
            pl.ds(0, filled), pl.ds(pl.multiple_of(block * line_cols, line_cols), line_cols)
        ]

    line_sum = LineSum(line, line_part, line_in, line_send, line_recv)
    greet_plane(plane)
    line.greet(3)
    for copy in late_loads:
        copy.start()
    kept = []
    waiting = list(loads)

    def compute(chip):
        while waiting:
            waiting.pop().wait()

        def units(cols):
            pulled = dot(pair_rows(blocks, chip), reduce_mat[cols], ((1,), (1,)))
            pair = pl.ds(2 * chip, 2)
            shape = pulled.shape
            gate_grad = pulled * slope[pair, :, cols].reshape(shape).astype(jnp.float32)
            upper_grad = pulled * gelu[pair, :, cols].reshape(shape).astype(jnp.float32)
            set_pair(slope, chip, cols, gate_grad)
            set_pair(gelu, chip, cols, upper_grad)
            unit_sums[0:1, cols] += jnp.sum(gate_grad, axis=0, keepdims=True)
            unit_sums[1:2, cols] += jnp.sum(upper_grad, axis=0, keepdims=True)

        tiles(slope.shape[2], 256, units)

        def outputs(cols):
            set_pair(
                parts,
                chip,
                cols,
                dot(pair_rows(slope, chip), expand_mat[0, :, cols], ((1,), (0,)))
                + dot(pair_rows(gelu, chip), expand_mat[1, :, cols], ((1,), (0,))),
            )

        tiles(parts.shape[2], 256, outputs)

    def product(left, right, start):
        tokens = left.shape[0] * left.shape[1]
        return dot(
            left[:, :, start : start + 256].reshape(tokens, 256),
            right[...].reshape(tokens, right.shape[2]),
            ((0,), (0,)),
        ).astype(jnp.bfloat16)

    def reduce_work():
        for copy in late_loads:
            copy.wait()
        for start in range(0, active.shape[2], 256):
            reduce_mat[start : start + 256] = product(active, blocks, start)
        for offset in range(narrow_count - 1, 0, -1):
            line_sum.begin(offset)

    def expand_work(left, start, target):
        def work():
            index = len(kept)
            if index >= 2:
                kept[index - 2].wait()
            staged[index % 2] = product(left, rows_all, start)
            stop = min(256, target.shape[0] - start)
            copy = pltpu.make_async_copy(
                staged.at[index % 2, pl.ds(0, stop)],
                target.at[pl.ds(start, stop)],
                keep_sems.at[index % 2],
            )
            copy.start()
            kept.append(copy)

        return work

    works = [
        expand_work(left, start, target)
        for left, target in ((slope, expand_part.at[0]), (gelu, expand_part.at[1]))
        for start in range(0, target.shape[0], 256)
    ]
    steps = [
        functools.partial(line_sum.step, offset) for offset in range(narrow_count - 2, 0, -1)
    ]
    middle = len(works) // 2
    works = [works[:middle], steps[: len(steps) // 2], works[middle:], steps[len(steps) // 2 :]]

    def many(calls):
        for call in calls:
            call()

    plane.run(compute, reduce_work, functools.partial(many, works[0] + works[1]))
    many(works[2])
    plane.finish(hidden_grad)
    many(works[3])
    line_sum.finish(reduce_grad)
    line_sum.drain()
    plane.drain()
    for copy in kept[-2:]:
        copy.wait()


def geglu_backward(
    wide_count,
    narrow_count,
    feed_grad,
    gate_expand,
    upper_expand,
    reduce_full,
    slope,
    gelu,
    active,
    rows_all,
):
    rows, width = feed_grad.shape
    padded = slope.shape[2]
    anywhere = pl.BlockSpec(memory_space=pl.ANY)
    vmem = pl.BlockSpec(memory_space=pltpu.VMEM)
    scratch = exchange_scratch(wide_count, rows, width) + [
        pltpu.VMEM((2, padded, width), jnp.bfloat16),
        pltpu.VMEM((padded, width), jnp.bfloat16),
        pltpu.VMEM((wide_count, rows, padded), jnp.bfloat16),
        pltpu.VMEM((wide_count, rows, padded), jnp.bfloat16),
        pltpu.VMEM((wide_count, rows, padded), jnp.bfloat16),
        pltpu.VMEM((wide_count, rows, width), jnp.bfloat16),
        pltpu.VMEM((2, 256, width), jnp.bfloat16),
        pltpu.SemaphoreType.DMA((7,)),
        pltpu.SemaphoreType.DMA((2,)),
        pltpu.VMEM(
            (2, narrow_count - 1, reduce_full.shape[0], width // narrow_count), jnp.bfloat16
        ),
        pltpu.SemaphoreType.DMA((2, narrow_count - 1)),
        pltpu.SemaphoreType.DMA((2, narrow_count - 1)),
    ]
    return pl.pallas_call(
        functools.partial(geglu_backward_kernel, wide_count, narrow_count),
        out_shape=(
            jax.ShapeDtypeStruct(
                (reduce_full.shape[0], width // narrow_count), jnp.float32
            ),
            jax.ShapeDtypeStruct((2, *gate_expand.shape), jnp.bfloat16),
            jax.ShapeDtypeStruct((rows, width), jnp.float32),
            jax.ShapeDtypeStruct((2, padded), jnp.float32),
        ),
        in_specs=[anywhere] * 8,
        out_specs=(vmem, anywhere, vmem, vmem),
        scratch_shapes=scratch,
        compiler_params=pltpu.CompilerParams(
            collective_id=2, has_side_effects=True, vmem_limit_bytes=63 * 2**20
        ),
        cost_estimate=pl.CostEstimate(
            flops=12 * wide_count * rows * padded * width, bytes_accessed=200 * 2**20, transcendentals=0
        ),
        name="geglu_backward",
    )(feed_grad, gate_expand, upper_expand, reduce_full, slope, gelu, active, rows_all)


def rotate_lanes(vectors, cosine, signed_sine):
    return vectors * cosine + pltpu.roll(vectors, vectors.shape[1] // 2, 1) * signed_sine


def attention_backward_kernel(
    wide_count,
    narrow_count,
    upper_grad,
    hidden_part,
    normed,
    inv_std,
    gain,
    merge,
    mixed,
    queries,
    keys,
    values,
    probs,
    cosine,
    signed_sine,
    triple,
    merge_grad,
    heads_sums,
    merge_sums,
    sum_grad,
    norm_sums,
    attended,
    upstream,
    outbound,
    probs_held,
    keys_turned,
    key_total,
    value_total,
    merge_out,
    merge_in,
    mixed_send,
    mixed_recv,
    merge_send,
    merge_recv,
    load_sems,
    parts,
    from_mate,
    incoming,
    mate_send,
    mate_recv,
    sum_send,
    sum_recv,
):
    sems = (None, None, mate_send, mate_recv, sum_send, sum_recv, None)
    plane = PlaneExchange(wide_count, None, None, parts, from_mate, incoming, sems)
    line = LineExchange(narrow_count)
    rows, width = sum_grad.shape
    own_cols = queries.shape[1]
    heads = own_cols // HDIM
    scale = HDIM ** (-0.5)

    def load(head):
        return pltpu.make_async_copy(
            probs.at[head], probs_held.at[head % 2], load_sems.at[head % 2]
        )

    load(0).start()
    greet_plane(plane)

    norm_sums[...] = jnp.zeros_like(norm_sums)
    merge_sums[...] = jnp.zeros_like(merge_sums)

    def norm_rows(i, carry):
        some = pl.ds(pl.multiple_of(i * 16, 16), 16)
        hidden_grad = residual_scale * upper_grad[some] + hidden_part[some]
        norm_sums[0:1] += jnp.sum(hidden_grad * normed[some], axis=0, keepdims=True)
        norm_sums[1:2] += jnp.sum(hidden_grad, axis=0, keepdims=True)
        total = normalize_back(hidden_grad, normed[some], inv_std[some], gain[...])
        sum_grad[some] = total
        merge_sums[...] += jnp.sum(total, axis=0, keepdims=True)
        attended[some] = total.astype(jnp.bfloat16)
        return carry

    lax.fori_loop(0, rows // 16, norm_rows, 0)
    line.greet(3)

    def mixed_part(target, where):
        part = dot(
            attended[...],
            merge[pl.ds(pl.multiple_of(where * own_cols, own_cols), own_cols)],
            ((1,), (1,)),
        )
        target[...] = part.astype(jnp.bfloat16)

    for offset in range(1, narrow_count):
        place = line.peer(offset)
        mixed_part(outbound.at[offset - 1], place)
        line.send(offset, outbound.at[offset - 1], upstream, mixed_send, mixed_recv)
    mixed_part(upstream.at[line.mine], line.mine)

    block = parts.shape[1]

    def merge_rows(i, carry):
        cols = pl.ds(pl.multiple_of(i * block, block), block)
        parts[i] = dot(mixed[:, cols], attended[...], ((0,), (0,))).astype(jnp.bfloat16)
        return carry

    lax.fori_loop(0, wide_count, merge_rows, 0)
    for offset in range(plane.ring):
        plane.share(offset)
    plane.first_sums()
    plane.far_sums()
    plane.last_sums()
    plane.finish(merge_out)
    count = merge_grad.shape[0]

    def z_rows(where):
        return pl.ds(pl.multiple_of(where * count, count), count)

    for offset in range(1, narrow_count):
        line.send(
            offset, merge_out.at[z_rows(line.peer(offset))], merge_in, merge_send, merge_recv
        )
    for offset in range(1, narrow_count):
        line.arrived(offset, upstream, mixed_send, mixed_recv)

    def one_head(head):
        cols = pl.ds(head * HDIM, HDIM)
        load(head).wait()
        if head + 1 < heads:
            load(head + 1).start()
        held = probs_held.at[head % 2]
        keys_turned[...] = keys[:, cols].astype(jnp.float32).T.astype(jnp.bfloat16)
        key_total[...] = jnp.zeros_like(key_total)
        value_total[...] = jnp.zeros_like(value_total)

        def chunk(i, carry):
            here = pl.ds(pl.multiple_of(i * rows, rows), rows)
            weights_low = held[:, here]
            up = upstream[i, :, cols]
            pulled = dot(values[:, cols], up, ((1,), (1,)))
            weights = weights_low.astype(jnp.float32)
            scaled = weights * pulled
            change = (scaled - weights * jnp.sum(scaled, axis=0, keepdims=True)).astype(
                jnp.bfloat16
            )
            key_total[...] += dot(change, queries[here, cols], ((1,), (0,)))
            value_total[...] += dot(weights_low, up, ((1,), (0,)))
            query_grad = dot(keys_turned[...], change, ((1,), (0,))).T * scale
            triple[here, cols] = rotate_lanes(
                query_grad, cosine[here], signed_sine[here]
            ).astype(jnp.bfloat16)
            return carry

        lax.fori_loop(0, narrow_count, chunk, 0)

        def ending(i, carry):
            here = pl.ds(pl.multiple_of(i * rows, rows), rows)
            triple[here, pl.ds(own_cols + head * HDIM, HDIM)] = rotate_lanes(
                key_total[here] * scale, cosine[here], signed_sine[here]
            ).astype(jnp.bfloat16)
            triple[here, pl.ds(2 * own_cols + head * HDIM, HDIM)] = value_total[here].astype(
                jnp.bfloat16
            )
            return carry

        lax.fori_loop(0, narrow_count, ending, 0)

    for head in range(heads):
        one_head(head)

    def column_sums(cols):
        heads_sums[:, cols] = jnp.sum(
            triple[:, cols].astype(jnp.float32), axis=0, keepdims=True
        )

    tiles(3 * own_cols, 256, column_sums)
    summed = merge_out[z_rows(line.mine)].astype(jnp.float32)
    for offset in range(1, narrow_count):
        line.arrived(offset, merge_in, merge_send, merge_recv)
        summed += merge_in[line.peer(offset)].astype(jnp.float32)
    merge_grad[...] = summed
    line.drain()
    plane.drain()


def attention_backward(
    wide_count,
    narrow_count,
    upper_grad,
    hidden_part,
    normed,
    inv_std,
    gain,
    merge_full,
    mixed,
    queries,
    keys,
    values,
    probs,
    cosine,
    signed_sine,
):
    rows, width = normed.shape
    bucket, own_cols = queries.shape
    block = width // wide_count
    count = block // narrow_count
    anywhere = pl.BlockSpec(memory_space=pl.ANY)
    vmem = pl.BlockSpec(memory_space=pltpu.VMEM)
    dma = pltpu.SemaphoreType.DMA
    return pl.pallas_call(
        functools.partial(attention_backward_kernel, wide_count, narrow_count),
        out_shape=(
            jax.ShapeDtypeStruct((bucket, 3 * own_cols), jnp.bfloat16),
            jax.ShapeDtypeStruct((count, width), jnp.float32),
            jax.ShapeDtypeStruct((1, 3 * own_cols), jnp.float32),
            jax.ShapeDtypeStruct((1, width), jnp.float32),
            jax.ShapeDtypeStruct((rows, width), jnp.float32),
            jax.ShapeDtypeStruct((2, width), jnp.float32),
        ),
        in_specs=[vmem] * 10 + [anywhere] + [vmem] * 2,
        out_specs=(vmem,) * 6,
        scratch_shapes=[
            pltpu.VMEM((rows, width), jnp.bfloat16),
            pltpu.VMEM((narrow_count, rows, own_cols), jnp.bfloat16),
            pltpu.VMEM((narrow_count - 1, rows, own_cols), jnp.bfloat16),
            pltpu.VMEM((2, bucket, bucket), jnp.bfloat16),
            pltpu.VMEM((HDIM, bucket), jnp.bfloat16),
            pltpu.VMEM((bucket, HDIM), jnp.float32),
            pltpu.VMEM((bucket, HDIM), jnp.float32),
            pltpu.VMEM((block, width), jnp.bfloat16),
            pltpu.VMEM((narrow_count, count, width), jnp.bfloat16),
            dma((narrow_count - 1,)),
            dma((narrow_count,)),
            dma((narrow_count - 1,)),
            dma((narrow_count,)),
            dma((2,)),
        ]
        + sum_scratch(wide_count, block, width),
        compiler_params=pltpu.CompilerParams(
            collective_id=3, has_side_effects=True, vmem_limit_bytes=kernel_memory
        ),
        cost_estimate=pl.CostEstimate(
            flops=60 * 10**9, bytes_accessed=200 * 2**20, transcendentals=0
        ),
        name="attention_backward",
    )(
        upper_grad,
        hidden_part,
        normed,
        inv_std,
        gain,
        merge_full,
        mixed,
        queries,
        keys,
        values,
        probs,
        cosine,
        signed_sine,
    )


def input_backward_kernel(
    wide_count,
    narrow_count,
    inputs,
    triple,
    heads_mat,
    small,
    input_part,
    heads_grad,
    small_out,
    line_parts,
    line_in,
    heads_out,
    heads_in,
    small_wide,
    small_sum,
    small_line,
    line_send,
    line_recv,
    heads_send,
    heads_recv,
    wide_send,
    wide_recv,
    small_send,
    small_recv,
    parts,
    from_mate,
    incoming,
    mate_send,
    mate_recv,
    sum_send,
    sum_recv,
):
    sems = (None, None, mate_send, mate_recv, sum_send, sum_recv, None)
    plane = PlaneExchange(wide_count, None, None, parts, from_mate, incoming, sems)
    line = LineExchange(narrow_count)
    rows, width = input_part.shape
    here = line.mine
    last = narrow_count - 1
    place = lax.axis_index("wide")

    def wide_peer(offset):
        return (place + offset) % wide_count

    barrier = pltpu.get_barrier_semaphore()
    for offset in range(1, wide_count):
        pl.semaphore_signal(
            barrier,
            inc=1,
            device_id={"wide": wide_peer(offset)},
            device_id_type=pl.DeviceIdType.MESH,
        )
    line.greet(wide_count - 1)

    def small_copy(offset, source, slot):
        return pltpu.make_async_remote_copy(
            src_ref=source,
            dst_ref=small_wide.at[slot],
            send_sem=wide_send.at[offset - 1],
            recv_sem=wide_recv.at[slot],
            device_id={"wide": wide_peer(offset)},
            device_id_type=pl.DeviceIdType.MESH,
        )

    small_copies = [
        small_copy(offset, small.at[wide_peer(offset)], place) for offset in range(1, wide_count)
    ]
    for copy in small_copies:
        copy.start()

    line_sum = LineSum(line, lambda target: line_parts.at[target], line_in, line_send, line_recv)

    def input_rows(index):
        some = pl.ds(pl.multiple_of(index * rows, rows), rows)

        def input_cols(cols):
            part = dot(triple[some], heads_mat[cols], ((1,), (1,)))
            line_parts[index, :, cols] = part.astype(jnp.bfloat16)

        tiles(width, 256, input_cols)

    for offset in range(last, 0, -1):
        for way in range(2):

            @pl.when(line_sum.reaches(way, offset))
            def _():
                input_rows(line_sum.target(way, offset))

        line_sum.begin(offset)
    input_rows(here)

    block = parts.shape[1]

    def heads_rows(i, carry):
        cols = pl.ds(pl.multiple_of(i * block, block), block)
        parts[i] = dot(inputs[:, cols], triple[...], ((0,), (0,))).astype(jnp.bfloat16)
        return carry

    lax.fori_loop(0, wide_count, heads_rows, 0)
    for offset in range(plane.ring):
        plane.share(offset)
    for offset in range(last - 1, last // 2, -1):
        line_sum.step(offset)
    plane.first_sums()
    plane.far_sums()

    for offset in range(1, wide_count):
        peer = wide_peer(offset)
        small_copy(offset, small_wide.at[peer], peer).wait_recv()
    small_wide[place] = small[place]
    total = small_wide[0]
    for index in range(1, wide_count):
        total += small_wide[index]
    small_sum[...] = total
    for offset in range(1, narrow_count):
        line.send(offset, small_sum.at[line.peer(offset)], small_line, small_send, small_recv)

    plane.last_sums()
    for offset in range(last // 2, 0, -1):
        line_sum.step(offset)
    plane.finish(heads_out)
    count = heads_grad.shape[0]

    def z_rows(where):
        return pl.ds(pl.multiple_of(where * count, count), count)

    for offset in range(1, narrow_count):
        line.send(
            offset, heads_out.at[z_rows(line.peer(offset))], heads_in, heads_send, heads_recv
        )
    heads_in[line.mine] = heads_out[z_rows(line.mine)]
    small_line[line.mine] = small_sum[line.mine]
    for offset in range(1, narrow_count):
        line.arrived(offset, small_line, small_send, small_recv)
    result = small_line[0]
    for index in range(1, narrow_count):
        result += small_line[index]
    small_out[...] = result

    line_sum.finish(input_part)
    for offset in range(1, narrow_count):
        line.arrived(offset, heads_in, heads_send, heads_recv)
    own_cols = triple.shape[1] // 3
    for index in range(narrow_count):
        for which in range(3):
            start = (which * narrow_count + index) * own_cols
            heads_grad[:, start : start + own_cols] = heads_in[
                index, :, which * own_cols : (which + 1) * own_cols
            ].astype(jnp.float32)
    line_sum.drain()
    for copy in small_copies:
        copy.wait_send()
    line.drain()
    plane.drain()


def input_backward(wide_count, narrow_count, inputs, triple_grad, heads_mat, small):
    bucket, width = inputs.shape
    rows = bucket // narrow_count
    columns = triple_grad.shape[1]
    block = width // wide_count
    count = block // narrow_count
    vmem = pl.BlockSpec(memory_space=pltpu.VMEM)
    dma = pltpu.SemaphoreType.DMA
    lines = small.shape[2]
    return pl.pallas_call(
        functools.partial(input_backward_kernel, wide_count, narrow_count),
        out_shape=(
            jax.ShapeDtypeStruct((rows, width), jnp.float32),
            jax.ShapeDtypeStruct((count, narrow_count * columns), jnp.float32),
            jax.ShapeDtypeStruct((lines, 128), jnp.float32),
        ),
        in_specs=[vmem] * 4,
        out_specs=(vmem, vmem, vmem),
        scratch_shapes=[
            pltpu.VMEM((narrow_count, rows, width), jnp.bfloat16),
            pltpu.VMEM((2, narrow_count - 1, rows, width), jnp.bfloat16),
            pltpu.VMEM((block, columns), jnp.bfloat16),
            pltpu.VMEM((narrow_count, count, columns), jnp.bfloat16),
            pltpu.VMEM((wide_count, narrow_count, lines, 128), jnp.float32),
            pltpu.VMEM((narrow_count, lines, 128), jnp.float32),
            pltpu.VMEM((narrow_count, lines, 128), jnp.float32),
            dma((2, narrow_count - 1)),
            dma((2, narrow_count - 1)),
            dma((narrow_count - 1,)),
            dma((narrow_count,)),
            dma((wide_count - 1,)),
            dma((wide_count,)),
            dma((narrow_count - 1,)),
            dma((narrow_count,)),
        ]
        + sum_scratch(wide_count, block, columns),
        compiler_params=pltpu.CompilerParams(
            collective_id=4, has_side_effects=True, vmem_limit_bytes=kernel_memory
        ),
        cost_estimate=pl.CostEstimate(
            flops=80 * 10**9, bytes_accessed=200 * 2**20, transcendentals=0
        ),
        name="input_backward",
    )(inputs, triple_grad, heads_mat, small)


def greet_all(wide_count, narrow_count):
    barrier = pltpu.get_barrier_semaphore()
    for axis, count in (("wide", wide_count), ("narrow", narrow_count)):
        place = lax.axis_index(axis)
        for offset in range(1, count):
            pl.semaphore_signal(
                barrier,
                inc=1,
                device_id={axis: (place + offset) % count},
                device_id_type=pl.DeviceIdType.MESH,
            )
    pl.semaphore_wait(barrier, wide_count + narrow_count - 2)


def gather_kernel(
    wide_count,
    narrow_count,
    own,
    heads_weight,
    merge_weight,
    small,
    buckets,
    speeds,
    rows_out,
    heads_out,
    merge_out,
    small_out,
    triple,
    cosine,
    signed_sine,
    first_query,
    last_query,
    rows_all,
    heads_all,
    merge_own,
    small_all,
    rows_send,
    rows_recv,
    heads_send,
    heads_recv,
    merge_send,
    merge_recv,
    small_send,
    small_recv,
    wide_send,
    wide_recv,
    local_sems,
    out_sems,
    heads_ring_send,
    heads_ring_recv,
):
    ring_sems = (heads_ring_send, heads_ring_recv, None, None, None, None, None)
    heads_ring = PlaneExchange(wide_count, None, heads_all, heads_all, None, None, ring_sems)
    line = LineExchange(narrow_count)
    here = line.mine
    last = narrow_count - 1
    place = lax.axis_index("wide")
    slot = heads_ring.slot(0)
    rows, width = own.shape
    count = heads_weight.shape[0]
    columns = heads_all.shape[2]
    own_cols = columns // 3

    def z_rows(where):
        return pl.ds(pl.multiple_of(where * count, count), count)

    def head_cols(which, where):
        start = which * narrow_count * own_cols + where * own_cols
        return pl.ds(pl.multiple_of(start, own_cols), own_cols)

    line_rows = LineGather(line, lambda block: rows_all.at[block], rows_send, rows_recv)

    keep_rows = pltpu.make_async_copy(own, rows_all.at[here], local_sems.at[0])
    keep_rows.start()
    keeps = [
        pltpu.make_async_copy(
            heads_weight.at[:, head_cols(which, here)],
            heads_all.at[slot, z_rows(here), pl.ds(which * own_cols, own_cols)],
            local_sems.at[2 + which],
        )
        for which in range(3)
    ]
    keep_merge = pltpu.make_async_copy(
        merge_weight, merge_own.at[z_rows(here)], local_sems.at[1]
    )
    for copy in keeps + [keep_merge]:
        copy.start()
    small_all[place, here] = small[...]
    greet_all(wide_count, narrow_count)

    def heads_copy(offset, which, where, sender):
        return line.copy(
            heads_weight.at[:, head_cols(which, where)],
            heads_all.at[slot, z_rows(sender), pl.ds(which * own_cols, own_cols)],
            heads_send.at[offset - 1, which],
            heads_recv.at[sender, which],
            where,
        )

    def merge_copy(offset, where, sender):
        return line.copy(
            merge_weight,
            merge_own.at[z_rows(sender)],
            merge_send.at[offset - 1],
            merge_recv.at[sender],
            where,
        )

    def small_copy(offset, where, sender):
        return line.copy(
            small,
            small_all.at[place, sender],
            small_send.at[offset - 1],
            small_recv.at[sender],
            where,
        )

    started = []

    def start(copy):
        copy.start()
        started.append(copy)

    for offset in range(1, narrow_count):
        for which in range(3):
            start(heads_copy(offset, which, line.peer(offset), here))
    for offset in range(1, narrow_count):
        start(small_copy(offset, line.peer(offset), here))
    keep_rows.wait()
    line_rows.send_own()

    halfway = narrow_count * rows // 2
    joined = buckets[0]

    def tables(i, carry):
        some = pl.ds(pl.multiple_of(i * rows, rows), rows)
        place_in = i * rows + lax.broadcasted_iota(jnp.int32, (rows, 1), 0)
        second = jnp.where(place_in >= halfway, 1 - joined, 0)
        local = place_in - second * halfway
        reach = jnp.where(
            joined == 1,
            buckets[1] + buckets[2],
            jnp.where(second == 1, buckets[2], buckets[1]),
        )
        first_query[some] = jnp.where(local < reach, place_in - local, place_in)
        last_query[some] = jnp.where(
            (joined == 1) | (second == 1), 2 * halfway - 1, halfway - 1
        ) + jnp.zeros_like(place_in)
        angles = local.astype(jnp.float32) * speeds[...]
        lane = lax.broadcasted_iota(jnp.int32, (rows, HDIM), 1)
        cosine[some] = jnp.cos(angles)
        sine = jnp.sin(angles)
        signed_sine[some] = jnp.where(lane < HDIM // 2, sine, -sine)
        return carry

    lax.fori_loop(0, narrow_count, tables, 0)

    for copy in keeps:
        copy.wait()
    for offset in range(1, narrow_count):
        for which in range(3):
            heads_copy(offset, which, line.peer(offset), line.peer(offset)).wait_recv()
    heads_ring.send_own()
    for offset in range(1, narrow_count):
        small_copy(offset, line.peer(offset), line.peer(offset)).wait_recv()

    def wide_copy(offset, sender):
        return pltpu.make_async_remote_copy(
            src_ref=small_all.at[sender],
            dst_ref=small_all.at[sender],
            send_sem=wide_send.at[offset - 1],
            recv_sem=wide_recv.at[sender],
            device_id={"wide": (place + offset) % wide_count},
            device_id_type=pl.DeviceIdType.MESH,
        )

    for offset in range(1, wide_count):
        start(wide_copy(offset, place))

    def project(block):
        def cols_step(cols):
            weight = heads_all[:, :, cols].reshape(width, cols.size)
            triple[pl.ds(pl.multiple_of(block * rows, rows), rows), cols] = dot(
                rows_all[block], weight, ((1,), (0,))
            )

        tiles(columns, 256, cols_step)

    def project_step(step):
        line_rows.each(step, project)

    def gather(ring, distance):
        ring.receive(distance)
        ring.receive_mate(-distance)
        if distance < ring.far:
            ring.receive_mate(distance)

    outs = []

    def keep_out(source, target):
        copy = pltpu.make_async_copy(source, target, out_sems.at[len(outs)])
        copy.start()
        outs.append(copy)

    line_rows.step(1)
    for offset in range(1, narrow_count):
        start(merge_copy(offset, line.peer(offset), here))
    heads_ring.receive_mate(0)
    for distance in range(1, heads_ring.far + 1):
        gather(heads_ring, distance)
    keep_out(heads_all, heads_out)
    project(here)
    for step in range(2, narrow_count):
        line_rows.step(step)
        project_step(step - 1)
    project_step(last)
    keep_merge.wait()
    for offset in range(1, narrow_count):
        merge_copy(offset, line.peer(offset), line.peer(offset)).wait_recv()
    keep_out(merge_own, merge_out)
    keep_out(rows_all, rows_out)
    for offset in range(1, wide_count):
        wide_copy(offset, (place + offset) % wide_count).wait_recv()
    keep_out(small_all, small_out)
    line_rows.drain()
    for copy in started:
        copy.wait_send()
    heads_ring.drain()
    for copy in outs:
        copy.wait()


def gather_front(
    wide_count, narrow_count, layer_input, heads_weight, merge_weight, small, buckets, speeds
):
    rows, width = layer_input.shape
    count, all_columns = heads_weight.shape
    columns = all_columns // narrow_count
    block = count * narrow_count
    anywhere = pl.BlockSpec(memory_space=pl.ANY)
    vmem = pl.BlockSpec(memory_space=pltpu.VMEM)
    dma = pltpu.SemaphoreType.DMA
    lines = small.shape[0]
    shapes = (
        (narrow_count, rows, width),
        (wide_count, block, columns),
        (block, width),
        (wide_count, narrow_count, lines, 128),
    )
    far = narrow_count - 1
    bucket = narrow_count * rows
    table = jax.ShapeDtypeStruct((bucket, HDIM), jnp.float32)
    reach = jax.ShapeDtypeStruct((bucket, 1), jnp.int32)
    return pl.pallas_call(
        functools.partial(gather_kernel, wide_count, narrow_count),
        out_shape=tuple(jax.ShapeDtypeStruct(shape, jnp.bfloat16) for shape in shapes)
        + (jax.ShapeDtypeStruct((bucket, columns), jnp.float32), table, table, reach, reach),
        in_specs=[anywhere, anywhere, anywhere, vmem, pl.BlockSpec(memory_space=pltpu.SMEM), vmem],
        out_specs=(anywhere,) * 4 + (vmem,) * 5,
        scratch_shapes=[pltpu.VMEM(shape, jnp.bfloat16) for shape in shapes]
        + [
            dma((2, narrow_count)),
            dma((narrow_count,)),
            dma((far, 3)),
            dma((narrow_count, 3)),
            dma((far,)),
            dma((narrow_count,)),
            dma((far,)),
            dma((narrow_count,)),
            dma((wide_count - 1,)),
            dma((wide_count,)),
            dma((5,)),
            dma((4,)),
            dma((3, wide_count, 2)),
            dma((wide_count, 2)),
        ],
        compiler_params=pltpu.CompilerParams(
            collective_id=5, has_side_effects=True, vmem_limit_bytes=kernel_memory
        ),
        cost_estimate=pl.CostEstimate(
            flops=80 * 10**9, bytes_accessed=200 * 2**20, transcendentals=0
        ),
        name="gather_front",
    )(layer_input, heads_weight, merge_weight, small, buckets, speeds)


def attention_forward_kernel(
    wide_count,
    narrow_count,
    triple,
    heads_shift,
    cosine,
    signed_sine,
    first_query,
    last_query,
    own,
    merge,
    merge_shift,
    gain,
    shift,
    queries,
    keys,
    values,
    probs,
    mixed_out,
    hidden,
    hidden_low,
    normed,
    inv_std,
    merge_out,
    merge_mat,
    probs_held,
    values_turned,
    outbound,
    mixed,
    mixed_send,
    mixed_recv,
    local_sems,
    ring_send,
    ring_recv,
    own_sem,
):
    line = LineExchange(narrow_count)
    ring_sems = (ring_send, ring_recv, None, None, None, None, own_sem)
    ring = PlaneExchange(wide_count, merge, merge_mat, merge_mat, None, None, ring_sems)
    bucket, own_cols = queries.shape
    rows, width = own.shape
    heads = own_cols // HDIM
    scale = HDIM ** (-0.5)
    greet_plane(ring)
    line.greet(3)
    keep_own = ring.send_own()
    ring_steps = [functools.partial(ring.receive, step) for step in range(1, ring.far + 1)]

    def keep(head):
        return pltpu.make_async_copy(
            probs_held.at[head % 2], probs.at[head], local_sems.at[head % 2]
        )

    def mixed_copy(head, offset, where, sender):
        cols = pl.ds(pl.multiple_of(sender * own_cols + head * HDIM, HDIM), HDIM)
        return line.copy(
            outbound.at[where, :, pl.ds(head * HDIM, HDIM)],
            mixed.at[:, cols],
            mixed_send.at[offset - 1, head],
            mixed_recv.at[sender, head],
            where,
        )

    started = []
    for head in range(heads):
        cols = pl.ds(head * HDIM, HDIM)

        def turn(i, carry):
            here = pl.ds(pl.multiple_of(i * rows, rows), rows)
            for which, target in enumerate((queries, keys, values)):
                wanted = pl.ds(which * own_cols + head * HDIM, HDIM)
                part = triple[here, wanted] + heads_shift[:, wanted]
                if which < 2:
                    part = rotate_lanes(part, cosine[here], -signed_sine[here])
                else:
                    values_turned[:, here] = part.T.astype(jnp.bfloat16)
                target[here, cols] = part.astype(jnp.bfloat16)
            return carry

        lax.fori_loop(0, narrow_count, turn, 0)
        if head >= 2:
            keep(head - 2).wait()
        held = probs_held.at[head % 2]

        def chunk(i, carry):
            here = pl.ds(pl.multiple_of(i * rows, rows), rows)
            scores = dot(keys[:, cols], queries[here, cols], ((1,), (1,))) * scale
            token = i * rows + lax.broadcasted_iota(jnp.int32, (bucket, rows), 1)
            seen = (token >= first_query[...]) & (token <= last_query[...])
            scores = jnp.where(seen, scores, masked_value)
            expo = jnp.exp(scores - jnp.max(scores, axis=0, keepdims=True))
            weights = (expo * (1 / jnp.sum(expo, axis=0, keepdims=True))).astype(jnp.bfloat16)
            held[:, here] = weights
            mixed_part = dot(values_turned[...], weights, ((1,), (0,)))
            outbound[i, :, cols] = mixed_part.T.astype(jnp.bfloat16)
            return carry

        lax.fori_loop(0, narrow_count, chunk, 0)
        keep(head).start()
        for offset in range(1, narrow_count):
            copy = mixed_copy(head, offset, line.peer(offset), line.mine)
            copy.start()
            started.append(copy)
        if ring_steps:
            ring_steps.pop(0)()
    own_mixed = pltpu.make_async_copy(
        outbound.at[line.mine],
        mixed.at[:, pl.ds(pl.multiple_of(line.mine * own_cols, own_cols), own_cols)],
        local_sems.at[3],
    )
    own_mixed.start()
    own_mixed.wait()
    keep_own.wait()
    for step in ring_steps:
        step()
    for offset in range(ring.ring):
        ring.receive_mate(offset)
    keep_merge = pltpu.make_async_copy(merge_mat, merge_out, local_sems.at[2])
    keep_merge.start()
    for offset in range(1, narrow_count):
        for head in range(heads):
            mixed_copy(head, offset, line.peer(offset), line.peer(offset)).wait_recv()
    mixed_out[...] = mixed[...]

    def merge_cols(cols):
        hidden[:, cols] = (
            residual_scale * own[:, cols].astype(jnp.float32)
            + dot(mixed[...], merge_mat[:, :, cols].reshape(width, cols.size), ((1,), (0,)))
            + merge_shift[:, cols]
        )

    tiles(width, 256, merge_cols)

    def norm_rows(i, carry):
        some = pl.ds(pl.multiple_of(i * 16, 16), 16)
        result, centred, inverse = normalize(hidden[some], gain[...], shift[...])
        hidden[some] = result
        hidden_low[some] = result.astype(jnp.bfloat16)
        normed[some] = centred
        inv_std[some] = inverse
        return carry

    lax.fori_loop(0, rows // 16, norm_rows, 0)
    for head in range(max(heads - 2, 0), heads):
        keep(head).wait()
    for copy in started:
        copy.wait_send()
    ring.drain()
    keep_merge.wait()


def attention_forward(
    wide_count,
    narrow_count,
    triple,
    heads_shift,
    cosine,
    signed_sine,
    first_query,
    last_query,
    layer_input,
    merge_block,
    merge_shift,
    gain,
    shift,
):
    bucket, columns = triple.shape
    rows, width = layer_input.shape
    own_cols = columns // 3
    heads = own_cols // HDIM
    anywhere = pl.BlockSpec(memory_space=pl.ANY)
    vmem = pl.BlockSpec(memory_space=pltpu.VMEM)
    dma = pltpu.SemaphoreType.DMA

    def low_shape(*shape):
        return jax.ShapeDtypeStruct(shape, jnp.bfloat16)

    def wide_shape(*shape):
        return jax.ShapeDtypeStruct(shape, jnp.float32)

    return pl.pallas_call(
        functools.partial(attention_forward_kernel, wide_count, narrow_count),
        out_shape=(
            low_shape(bucket, own_cols),
            low_shape(bucket, own_cols),
            low_shape(bucket, own_cols),
            low_shape(heads, bucket, bucket),
            low_shape(rows, width),
            wide_shape(rows, width),
            low_shape(rows, width),
            wide_shape(rows, width),
            wide_shape(rows, 1),
            low_shape(wide_count, *merge_block.shape),
        ),
        in_specs=[vmem] * 7 + [anywhere] + [vmem] * 3,
        out_specs=(vmem, vmem, vmem, anywhere) + (vmem,) * 5 + (anywhere,),
        scratch_shapes=[
            pltpu.VMEM((wide_count, *merge_block.shape), jnp.bfloat16),
            pltpu.VMEM((2, bucket, bucket), jnp.bfloat16),
            pltpu.VMEM((HDIM, bucket), jnp.bfloat16),
            pltpu.VMEM((narrow_count, rows, own_cols), jnp.bfloat16),
            pltpu.VMEM((rows, width), jnp.bfloat16),
            dma((narrow_count - 1, heads)),
            dma((narrow_count, heads)),
            dma((4,)),
            dma((3, wide_count, 2)),
            dma((wide_count, 2)),
            dma(()),
        ],
        compiler_params=pltpu.CompilerParams(
            collective_id=6, has_side_effects=True, vmem_limit_bytes=kernel_memory
        ),
        cost_estimate=pl.CostEstimate(
            flops=60 * 10**9, bytes_accessed=200 * 2**20, transcendentals=0
        ),
        name="attention_forward",
    )(
        triple,
        heads_shift,
        cosine,
        signed_sine,
        first_query,
        last_query,
        layer_input,
        merge_block,
        merge_shift,
        gain,
        shift,
    )


def shards(
    layer_input,
    heads_weight,
    heads_bias,
    merge_weight,
    merge_bias,
    norm_gains,
    norm_shifts,
    expand_weight,
    expand_bias,
    reduce_weight,
    reduce_bias,
    joined,
    prefix,
    cotangent,
):
    tok_rows, model_width = layer_input.shape
    wide_count = lax.axis_size("wide")
    narrow_count = lax.axis_size("narrow")
    count = wide_count * narrow_count
    bucket_len = tok_rows * narrow_count
    own_heads = HEADS // narrow_count
    own_cols = own_heads * HDIM
    share = expand_weight.shape[2]
    narrow_index = lax.axis_index("narrow")
    smalls = (heads_bias, merge_bias, norm_gains, norm_shifts, expand_bias, reduce_bias)
    (
        rows_input,
        heads_mat,
        merge_block,
        small_all,
        triple,
        cosine,
        signed_sine,
        first_query,
        last_query,
    ) = gather_front(
        wide_count,
        narrow_count,
        layer_input,
        heads_weight,
        merge_weight,
        pack_small(smalls),
        jnp.concatenate([joined, prefix[0]]),
        jnp.asarray(rotary_speeds(HDIM)),
    )
    rows_input = rows_input.reshape(bucket_len, model_width)
    heads_mat = heads_mat.reshape(model_width, 3 * own_cols)
    heads_shift, merge_shift, gains, shifts, expand_shift, reduce_shift = unpack_small(
        small_all, smalls
    )
    own_shift = lax.dynamic_index_in_dim(
        heads_shift.reshape(3, narrow_count, own_cols), narrow_index, 1, keepdims=False
    ).reshape(1, -1)
    (
        queries,
        keys,
        values,
        probs_low,
        mixed,
        hidden,
        hidden_low,
        normed_one,
        inv_one,
        merge_full,
    ) = attention_forward(
        wide_count,
        narrow_count,
        triple,
        own_shift,
        cosine,
        signed_sine,
        first_query,
        last_query,
        layer_input,
        merge_block,
        merge_shift.reshape(1, -1),
        gains[0].reshape(1, -1),
        shifts[0].reshape(1, -1),
    )

    tile_rows = -share % 16
    padded = -(-share // 256) * 256
    expand_low = jnp.pad(expand_weight.transpose(1, 2, 0), ((0, 0), (0, tile_rows), (0, 0)))
    gate_expand = lax.all_gather(expand_low[0], "narrow", axis=1, tiled=True)
    upper_low, _ = lax.optimization_barrier((expand_low[1], small_all))
    upper_expand = lax.all_gather(upper_low, "narrow", axis=1, tiled=True)
    reduce_low = jnp.pad(reduce_weight, ((0, tile_rows), (0, 0)))
    (
        reduce_full,
        rows_all,
        active,
        slope,
        gelu,
        layer_output,
        sum_two_grad,
        feed_grad,
        row_sums,
    ) = geglu_forward(
        wide_count,
        narrow_count,
        hidden_low,
        gate_expand,
        upper_expand,
        reduce_low,
        jnp.pad(expand_shift, ((0, 0), (0, padded - share))),
        hidden,
        cotangent,
        reduce_shift.reshape(1, -1),
        gains[1].reshape(1, -1),
        shifts[1].reshape(1, -1),
    )
    reduce_weight_gradient, expand_part, hidden_part, unit_sums = geglu_backward(
        wide_count,
        narrow_count,
        feed_grad,
        gate_expand,
        upper_expand,
        reduce_full,
        slope,
        gelu,
        active,
        rows_all,
    )
    expand_weight_gradient = (
        lax.psum_scatter(expand_part, "narrow", scatter_dimension=2, tiled=True)[:, :share]
        .astype(jnp.float32)
        .transpose(2, 0, 1)
    )
    (
        triple_grad,
        merge_weight_gradient,
        heads_sums,
        merge_sums,
        sum_one_grad,
        norm_one_sums,
    ) = attention_backward(
        wide_count,
        narrow_count,
        sum_two_grad,
        hidden_part,
        normed_one,
        inv_one,
        gains[0].reshape(1, -1),
        merge_full.reshape(model_width, model_width),
        mixed,
        queries,
        keys,
        values,
        probs_low,
        cosine,
        signed_sine,
    )

    mine_narrow = (jnp.arange(narrow_count) == narrow_index).astype(jnp.float32)
    mine_wide = (jnp.arange(wide_count) == lax.axis_index("wide")).astype(jnp.float32)
    heads_sums = heads_sums.reshape(3, 1, own_cols)
    heads_sums = (heads_sums * mine_narrow[None, :, None]).reshape(count, -1)
    merge_sums = merge_sums.reshape(count, -1)
    norm_sums = (
        jnp.stack([norm_one_sums[0], row_sums[0], norm_one_sums[1], row_sums[1]])
        .reshape(4, count, -1)
        .transpose(1, 0, 2)
        .reshape(count, -1)
    )
    expand_sums = unit_sums[:, :share]
    expand_sums = (
        expand_sums.reshape(2, narrow_count, -1).transpose(1, 0, 2).reshape(1, narrow_count, -1)
        * mine_wide[:, None, None]
    ).reshape(count, -1)
    reduce_sums = row_sums[2].reshape(1, narrow_count, -1)
    reduce_sums = jnp.broadcast_to(
        reduce_sums, (wide_count, narrow_count, reduce_sums.shape[2])
    ).reshape(count, -1)
    pieces = (heads_sums, merge_sums, norm_sums, expand_sums, reduce_sums)
    packed = jnp.concatenate(pieces, axis=1)
    packed = jnp.pad(packed, ((0, 0), (0, -packed.shape[1] % 1024)))
    input_part, heads_weight_gradient, summed = input_backward(
        wide_count,
        narrow_count,
        rows_input,
        triple_grad,
        heads_mat,
        packed.reshape(wide_count, narrow_count, -1, 128),
    )
    input_gradient = residual_scale * sum_one_grad + input_part
    summed = summed.reshape(-1)
    ends = []
    start = 0
    for piece in pieces:
        ends.append(summed[start : start + piece.shape[1]])
        start += piece.shape[1]
    norm_ends = ends[2].reshape(4, -1)
    return (
        layer_output,
        input_gradient,
        heads_weight_gradient,
        ends[0],
        merge_weight_gradient,
        ends[1],
        norm_ends[:2],
        norm_ends[2:],
        expand_weight_gradient,
        ends[3].reshape(2, -1),
        reduce_weight_gradient[:share],
        ends[4],
    )


def solution(mesh):
    return jax.shard_map(
        shards,
        mesh=mesh,
        in_specs=(
            P(("wide", "narrow"), None),
            P(("wide", "narrow"), None),
            P(("wide", "narrow")),
            P(("wide", "narrow"), None),
            P(("wide", "narrow")),
            P(None, ("wide", "narrow")),
            P(None, ("wide", "narrow")),
            P("narrow", None, "wide"),
            P(None, ("wide", "narrow")),
            P("wide", "narrow"),
            P("narrow"),
            P("wide"),
            P("wide", None),
            P(("wide", "narrow"), None),
        ),
        out_specs=(
            P(("wide", "narrow"), None),
            P(("wide", "narrow"), None),
            P(("wide", "narrow"), None),
            P(("wide", "narrow")),
            P(("wide", "narrow"), None),
            P(("wide", "narrow")),
            P(None, ("wide", "narrow")),
            P(None, ("wide", "narrow")),
            P("narrow", None, "wide"),
            P(None, ("wide", "narrow")),
            P("wide", "narrow"),
            P("narrow"),
        ),
        check_vma=False,
    )
```

```python
import functools
import math

import jax
import jax.numpy as jnp
import numpy as np
from jax import lax
from jax.experimental import pallas as pl
from jax.experimental.pallas import tpu as pltpu
from jax.sharding import PartitionSpec as P

HEADS = 16
HDIM = 128


residual_scale = 48.0**0.5
norm_eps = 1e-05
masked_value = -1e30
key_tile = 128
kernel_memory = 60 * 2**20


def rotary_speeds(head_size):
    index = np.arange(head_size) % (head_size // 2)
    return (10000.0 ** (-2.0 * index / head_size)).astype(np.float32)[None]


def normalize(values, gain, shift):
    centre = jnp.mean(values, axis=-1, keepdims=True)
    centred = values - centre
    variance = jnp.mean(centred * centred, axis=-1, keepdims=True)
    inv_std = lax.rsqrt(variance + norm_eps)
    normed = centred * inv_std
    return (normed * gain + shift, normed, inv_std)


def normalize_back(upstream, normed, inv_std, gain):
    scaled = upstream * gain
    return inv_std * (
        scaled
        - jnp.mean(scaled, axis=-1, keepdims=True)
        - normed * jnp.mean(scaled * normed, axis=-1, keepdims=True)
    )


def dot(left, right, dims):
    return lax.dot_general(left, right, (dims, ((), ())), preferred_element_type=jnp.float32)


def low(values):
    return values.astype(jnp.bfloat16)


def pack_small(parts):
    packed = jnp.concatenate([part.reshape(-1) for part in parts])
    return jnp.pad(packed, (0, -packed.size % 2048)).reshape(-1, 128)


def unpack_small(everyone, parts):
    wide_count, narrow_count = everyone.shape[:2]
    everyone = everyone.reshape(wide_count, narrow_count, -1).astype(jnp.float32)
    pieces = []
    start = 0
    for part in parts:
        pieces.append(everyone[:, :, start : start + part.size])
        start += part.size

    def pairs(piece):
        piece = piece.reshape(-1, 2, piece.shape[-1] // 2)
        return piece.transpose(1, 0, 2).reshape(2, -1)

    own_expand = lax.dynamic_index_in_dim(
        pieces[4], lax.axis_index("wide"), 0, keepdims=False
    )
    return (
        pieces[0].reshape(-1),
        pieces[1].reshape(-1),
        pairs(pieces[2]),
        pairs(pieces[3]),
        pairs(own_expand),
        pieces[5][0].reshape(-1),
    )


def ring_place(wide_count):
    ring = wide_count // 2
    mine = lax.axis_index("wide")
    chip = mine // 2
    core = mine % 2
    position = 2 * (chip // 2) + (chip % 2 + chip // 2) % 2
    return ring, position, core


def chip_at(position, ring):
    position = (position + 2 * ring) % ring
    return 2 * (position // 2) + (position + position // 2) % 2


class PlaneExchange:
    def __init__(self, wide_count, own, blocks, parts, from_mate, incoming, sems, cols=None):
        self.ring, self.position, self.core = ring_place(wide_count)
        self.own, self.blocks, self.parts = own, blocks, parts
        self.from_mate, self.incoming = from_mate, incoming
        (
            self.gather_send,
            self.gather_recv,
            self.mate_send,
            self.mate_recv,
            self.sum_send,
            self.sum_recv,
            self.own_sem,
        ) = sems
        self.half = parts.shape[1] // 2
        self.cols = slice(None) if cols is None else cols
        self.far = self.ring // 2
        self.started = []

    def device(self, offset, mate=False):
        core = 1 - self.core if mate else self.core
        return {"wide": 2 * chip_at(self.position + offset, self.ring) + core}

    def slot(self, offset, mate=False):
        core = 1 - self.core if mate else self.core
        return 2 * chip_at(self.position + offset, self.ring) + core

    def rows(self, part):
        return pl.ds(part * self.half, self.half)

    def greet(self):
        barrier = pltpu.get_barrier_semaphore()
        for where in (self.device(-1), self.device(1), self.device(0, True)):
            pl.semaphore_signal(
                barrier, inc=1, device_id=where, device_id_type=pl.DeviceIdType.MESH
            )
        pl.semaphore_wait(barrier, 3)

    def start(self, source, target, send_sem, recv_sem, where):
        copy = pltpu.make_async_remote_copy(
            src_ref=source,
            dst_ref=target,
            send_sem=send_sem,
            recv_sem=recv_sem,
            device_id=where,
            device_id_type=pl.DeviceIdType.MESH,
        )
        copy.start()
        self.started.append(copy)

    def pass_on(self, lane, slot, part, where, source=None):
        target = self.blocks.at[slot, self.rows(part)]
        self.start(
            target if source is None else source,
            target,
            self.gather_send.at[lane, slot, part],
            self.gather_recv.at[slot, part],
            where,
        )

    def arrived(self, slot, part):
        target = self.blocks.at[slot, self.rows(part)]
        pltpu.make_async_remote_copy(
            src_ref=target,
            dst_ref=target,
            send_sem=self.gather_send.at[0, slot, part],
            recv_sem=self.gather_recv.at[slot, part],
            device_id=self.device(1),
            device_id_type=pl.DeviceIdType.MESH,
        ).wait_recv()

    def send_own(self):
        slot = self.slot(0)
        keep = None
        own = self.blocks.at[slot]
        if self.own is not None:
            own = self.own
            keep = pltpu.make_async_copy(own, self.blocks.at[slot], self.own_sem)
            keep.start()
        first, second = own.at[self.rows(0)], own.at[self.rows(1)]
        self.pass_on(0, slot, 0, self.device(1), first)
        self.pass_on(1, slot, 1, self.device(-1), second)
        self.pass_on(2, slot, 0, self.device(0, True), first)
        self.pass_on(2, slot, 1, self.device(0, True), second)
        self.pass_on(0, slot, 1, self.device(1), second)
        self.pass_on(1, slot, 0, self.device(-1), first)
        return keep

    def receive(self, distance):
        mate = self.device(0, True)
        left, right = self.slot(-distance), self.slot(distance)
        if distance == self.far:
            for part in range(2):
                self.arrived(left, part)
                self.pass_on(2, left, part, mate)
            return
        further = distance < self.far - 1
        self.arrived(left, 0)
        self.pass_on(0, left, 0, self.device(1))
        self.pass_on(2, left, 0, mate)
        self.arrived(right, 1)
        self.pass_on(1, right, 1, self.device(-1))
        self.pass_on(2, right, 1, mate)
        self.arrived(left, 1)
        if further:
            self.pass_on(0, left, 1, self.device(1))
        self.pass_on(2, left, 1, mate)
        self.arrived(right, 0)
        if further:
            self.pass_on(1, right, 0, self.device(-1))
        self.pass_on(2, right, 0, mate)

    def receive_mate(self, offset):
        for part in range(2):
            self.arrived(self.slot(offset, True), part)

    def share(self, offset):
        chip = chip_at(self.position + offset, self.ring)
        self.start(
            self.parts.at[self.slot(offset, True), :, self.cols],
            self.from_mate.at[chip, :, self.cols],
            self.mate_send.at[chip],
            self.mate_recv.at[chip],
            self.device(0, True),
        )

    def shared(self, offset):
        chip = chip_at(self.position + offset, self.ring)
        pltpu.make_async_remote_copy(
            src_ref=self.parts.at[self.slot(offset), :, self.cols],
            dst_ref=self.from_mate.at[chip, :, self.cols],
            send_sem=self.mate_send.at[chip],
            recv_sem=self.mate_recv.at[chip],
            device_id=self.device(0, True),
            device_id_type=pl.DeviceIdType.MESH,
        ).wait_recv()

    def chip_sum(self, offset, rows):
        chip = chip_at(self.position + offset, self.ring)
        return self.parts[self.slot(offset), rows, self.cols].astype(
            jnp.float32
        ) + self.from_mate[chip, rows, self.cols].astype(jnp.float32)

    def send_sum(self, way, distance, part):
        offset = distance if way == 0 else -distance
        begins = self.far if part == way else self.far - 1
        slot = self.slot(offset)
        if distance < begins:
            self.sum_arrived(way, distance, part)

        def chunk(i, carry):
            here = pl.ds(pl.multiple_of(i * 16, 16), 16)
            there = pl.ds(pl.multiple_of(part * self.half + i * 16, 16), 16)
            total = self.chip_sum(offset, there)
            if distance < begins:
                total += self.incoming[way, distance, part, here, self.cols].astype(jnp.float32)
            self.parts[slot, there, self.cols] = total.astype(jnp.bfloat16)
            return carry

        lax.fori_loop(0, self.half // 16, chunk, 0)
        self.start(
            self.parts.at[slot, self.rows(part), self.cols],
            self.incoming.at[way, distance - 1, part, :, self.cols],
            self.sum_send.at[way, distance - 1, part],
            self.sum_recv.at[way, distance - 1, part],
            self.device(1 if way == 0 else -1),
        )

    def sum_arrived(self, way, distance, part):
        target = self.incoming.at[way, distance, part, :, self.cols]
        pltpu.make_async_remote_copy(
            src_ref=target,
            dst_ref=target,
            send_sem=self.sum_send.at[way, distance, part],
            recv_sem=self.sum_recv.at[way, distance, part],
            device_id=self.device(1),
            device_id_type=pl.DeviceIdType.MESH,
        ).wait_recv()

    def run(self, first, second, before, after_far):
        def compute(chip):
            first(chip)
            second(chip)

        keep = self.send_own()
        keep.wait()
        self.receive_mate(0)
        compute(chip_at(self.position, self.ring))
        self.share(0)
        for distance in range(1, self.far):
            self.receive(distance)
            for offset in (-distance, distance):
                self.receive_mate(offset)
                compute(chip_at(self.position + offset, self.ring))
                self.share(offset)
            if distance == self.far - 1:
                self.first_sums()
        self.receive(self.far)
        self.receive_mate(self.far)
        farthest = chip_at(self.position + self.far, self.ring)
        first(farthest)
        before()
        second(farthest)
        self.share(self.far)
        self.far_sums()
        after_far()
        self.last_sums()

    def run_gather(self, compute, between):
        keep = self.send_own()
        keep.wait()
        self.receive_mate(0)
        compute(chip_at(self.position, self.ring))
        done = 1
        for distance in range(1, self.far):
            self.receive(distance)
            between(done)
            done += 1
            for offset in (-distance, distance):
                self.receive_mate(offset)
                compute(chip_at(self.position + offset, self.ring))
        self.receive(self.far)
        between(done)
        done += 1
        self.receive_mate(self.far)
        compute(chip_at(self.position + self.far, self.ring))
        return done

    def start_sums(self, compute):
        compute(chip_at(self.position + self.far, self.ring))
        self.share(self.far)
        for distance in range(self.far - 1, 0, -1):
            for offset in (-distance, distance):
                compute(chip_at(self.position + offset, self.ring))
                self.share(offset)
            if distance == self.far - 1:
                self.far_sums()
                self.first_sums()
        compute(chip_at(self.position, self.ring))
        self.share(0)

    def first_sums(self):
        distance = self.far - 1
        self.shared(distance)
        self.send_sum(0, distance, 1)
        self.shared(-distance)
        self.send_sum(1, distance, 0)

    def far_sums(self):
        self.shared(self.far)
        self.send_sum(0, self.far, 0)
        self.send_sum(1, self.far, 1)

    def last_sums(self):
        for distance in range(self.far - 1, 0, -1):
            if distance < self.far - 1:
                self.shared(distance)
                self.shared(-distance)
            self.send_sum(0, distance, 0)
            self.send_sum(1, distance, 1)
            if distance < self.far - 1:
                self.send_sum(0, distance, 1)
                self.send_sum(1, distance, 0)

    def finish(self, result):
        self.shared(0)
        for part in range(2):
            for way in range(2):
                self.sum_arrived(way, 0, part)

            def chunk(i, carry):
                here = pl.ds(pl.multiple_of(i * 16, 16), 16)
                there = pl.ds(pl.multiple_of(part * self.half + i * 16, 16), 16)
                total = self.chip_sum(0, there)
                for way in range(2):
                    total += self.incoming[way, 0, part, here, self.cols].astype(jnp.float32)
                result[there, self.cols] = total.astype(result.dtype)
                return carry

            lax.fori_loop(0, self.half // 16, chunk, 0)

    def drain(self):
        for copy in self.started:
            copy.wait_send()


def sum_scratch(wide_count, rows, width):
    ring = wide_count // 2
    far = ring // 2
    dma = pltpu.SemaphoreType.DMA
    return [
        pltpu.VMEM((wide_count, rows, width), jnp.bfloat16),
        pltpu.VMEM((ring, rows, width), jnp.bfloat16),
        pltpu.VMEM((2, far, 2, rows // 2, width), jnp.bfloat16),
        dma((ring,)),
        dma((ring,)),
        dma((2, far, 2)),
        dma((2, far, 2)),
    ]


def exchange_scratch(wide_count, rows, width):
    dma = pltpu.SemaphoreType.DMA
    return [
        pltpu.VMEM((wide_count, rows, width), jnp.bfloat16),
        dma((3, wide_count, 2)),
        dma((wide_count, 2)),
        dma(()),
    ] + sum_scratch(wide_count, rows, width)


def load_padded(source, target, sem):
    filled = source.shape[0]
    copy = pltpu.make_async_copy(source, target.at[pl.ds(0, filled)], sem)
    copy.start()
    if filled < target.shape[0]:
        target[pl.ds(filled, target.shape[0] - filled)] = jnp.zeros(
            (target.shape[0] - filled, target.shape[1]), target.dtype
        )
    return copy


def pair_rows(ref, chip):
    block = ref[pl.ds(2 * chip, 2)]
    return block.reshape(2 * block.shape[1], block.shape[2])


def set_pair(ref, chip, cols, value):
    rows = ref.shape[1]
    ref[2 * chip, :, cols] = value[:rows].astype(ref.dtype)
    ref[2 * chip + 1, :, cols] = value[rows:].astype(ref.dtype)


def tiles(count, tile, body, start=0):
    def step(i, carry):
        body(pl.ds(pl.multiple_of(start + i * tile, tile), tile))
        return carry

    lax.fori_loop(0, count // tile, step, 0)


class LineExchange:
    def __init__(self, narrow_count):
        self.count = narrow_count
        self.mine = lax.axis_index("narrow")
        self.started = []

    def peer(self, offset):
        return (self.mine + offset) % self.count

    def greet(self, extra=0):
        barrier = pltpu.get_barrier_semaphore()
        for offset in range(1, self.count):
            pl.semaphore_signal(
                barrier,
                inc=1,
                device_id={"narrow": self.peer(offset)},
                device_id_type=pl.DeviceIdType.MESH,
            )
        pl.semaphore_wait(barrier, self.count - 1 + extra)

    def copy(self, source, target, send_sem, recv_sem, where):
        return pltpu.make_async_remote_copy(
            src_ref=source,
            dst_ref=target,
            send_sem=send_sem,
            recv_sem=recv_sem,
            device_id={"narrow": where},
            device_id_type=pl.DeviceIdType.MESH,
        )

    def send(self, offset, source, landing, send_sems, recv_sems):
        peer = self.peer(offset)
        copy = self.copy(
            source, landing.at[self.mine], send_sems.at[offset - 1], recv_sems.at[self.mine], peer
        )
        copy.start()
        self.started.append(copy)

    def arrived(self, offset, landing, send_sems, recv_sems):
        peer = self.peer(offset)
        self.copy(
            landing.at[peer], landing.at[peer], send_sems.at[offset - 1], recv_sems.at[peer], peer
        ).wait_recv()

    def drain(self):
        for copy in self.started:
            copy.wait_send()


class LineSum:
    def __init__(self, line, view, landing, send_sems, recv_sems):
        self.line, self.view, self.landing = line, view, landing
        self.send_sems, self.recv_sems = send_sems, recv_sems
        self.last = line.count - 1

    def reaches(self, way, offset):
        here = self.line.mine
        return here + offset <= self.last if way == 0 else here - offset >= 0

    def follows(self, way):
        here = self.line.mine
        return here > 0 if way == 0 else here < self.last

    def target(self, way, offset):
        return self.line.mine + offset if way == 0 else self.line.mine - offset

    def copy(self, way, offset):
        return self.line.copy(
            self.view(self.target(way, offset)),
            self.landing.at[way, offset - 1],
            self.send_sems.at[way, offset - 1],
            self.recv_sems.at[way, offset - 1],
            self.line.mine + 1 if way == 0 else self.line.mine - 1,
        )

    def arrived(self, way, offset):
        landing = self.landing.at[way, offset]
        self.line.copy(
            landing,
            landing,
            self.send_sems.at[way, offset],
            self.recv_sems.at[way, offset],
            self.line.mine,
        ).wait_recv()

    def add(self, way, offset):
        held = self.view(self.target(way, offset))

        def chunk(i, carry):
            some = pl.ds(pl.multiple_of(i * 16, 16), 16)
            held[some] = (
                held[some].astype(jnp.float32)
                + self.landing[way, offset, some].astype(jnp.float32)
            ).astype(jnp.bfloat16)
            return carry

        lax.fori_loop(0, self.landing.shape[2] // 16, chunk, 0)

    def begin(self, offset):
        for way in range(2):

            @pl.when(self.reaches(way, offset) & jnp.logical_not(self.follows(way)))
            def _():
                self.copy(way, offset).start()

    def step(self, offset):
        for way in range(2):

            @pl.when(self.reaches(way, offset) & self.follows(way))
            def _():
                self.arrived(way, offset)
                self.add(way, offset)
                self.copy(way, offset).start()

    def finish(self, result):
        held = self.view(self.line.mine)
        count = self.landing.shape[2] // 16

        def begin(i, carry):
            some = pl.ds(pl.multiple_of(i * 16, 16), 16)
            result[some] = held[some].astype(result.dtype)
            return carry

        lax.fori_loop(0, count, begin, 0)
        for way in range(2):

            @pl.when(self.follows(way))
            def _():
                self.arrived(way, 0)

                def chunk(i, carry):
                    some = pl.ds(pl.multiple_of(i * 16, 16), 16)
                    result[some] += self.landing[way, 0, some].astype(result.dtype)
                    return carry

                lax.fori_loop(0, count, chunk, 0)

    def drain(self):
        for offset in range(1, self.last + 1):
            for way in range(2):

                @pl.when(self.reaches(way, offset))
                def _():
                    self.copy(way, offset).wait_send()


class LineGather:
    def __init__(self, line, view, send_sems, recv_sems):
        self.line, self.view = line, view
        self.send_sems, self.recv_sems = send_sems, recv_sems
        self.last = line.count - 1

    def copy(self, way, block):
        target = self.view(block)
        here = self.line.mine
        return self.line.copy(
            target,
            target,
            self.send_sems.at[way, block],
            self.recv_sems.at[block],
            here + 1 if way == 0 else here - 1,
        )

    def goes(self, way):
        return self.line.mine < self.last if way == 0 else self.line.mine > 0

    def has(self, way, step):
        here = self.line.mine
        return here - step >= 0 if way == 0 else here + step <= self.last

    def block(self, way, step):
        return self.line.mine - step if way == 0 else self.line.mine + step

    def send_own(self):
        for way in range(2):

            @pl.when(self.goes(way))
            def _():
                self.copy(way, self.line.mine).start()

    def step(self, step):
        for way in range(2):

            @pl.when(self.has(way, step))
            def _():
                self.copy(way, self.block(way, step)).wait_recv()

                @pl.when(self.goes(way))
                def _():
                    self.copy(way, self.block(way, step)).start()

    def each(self, step, body):
        for way in range(2):

            @pl.when(self.has(way, step))
            def _():
                body(self.block(way, step))

    def drain(self):
        for way in range(2):
            for step in range(self.last + 1):

                @pl.when(self.has(way, step) & self.goes(way))
                def _():
                    self.copy(way, self.block(way, step)).wait_send()


def greet_plane(plane):
    barrier = pltpu.get_barrier_semaphore()
    for where in (plane.device(-1), plane.device(1), plane.device(0, True)):
        pl.semaphore_signal(barrier, inc=1, device_id=where, device_id_type=pl.DeviceIdType.MESH)


def geglu_forward_kernel(
    wide_count,
    narrow_count,
    own,
    expand,
    reduce,
    shift,
    hidden,
    cotangent,
    reduce_shift,
    gain,
    norm_shift,
    reduce_out,
    rows_all,
    active_out,
    slope_out,
    gelu_out,
    layer_output,
    sum_grad,
    feed_grad,
    row_sums,
    feed,
    blocks,
    gather_send,
    gather_recv,
    own_sem,
    parts,
    from_mate,
    incoming,
    mate_send,
    mate_recv,
    sum_send,
    sum_recv,
    expand_mat,
    reduce_mat,
    active,
    slope,
    gelu,
    load_sems,
    keep_sems,
    reduce_send,
    reduce_recv,
    late_mate_send,
    late_mate_recv,
    late_sum_send,
    late_sum_recv,
):
    sems = (gather_send, gather_recv, mate_send, mate_recv, sum_send, sum_recv, own_sem)
    late_sems = (None, None, late_mate_send, late_mate_recv, late_sum_send, late_sum_recv, None)
    line = LineExchange(narrow_count)
    filled, cols = reduce.shape
    width = own.shape[1]
    upper = (2 * line.mine) // narrow_count
    late = pl.multiple_of((1 - upper) * (width - cols), cols)
    early = pl.multiple_of(upper * cols, cols)
    plane = PlaneExchange(
        wide_count, own, blocks, parts, from_mate, incoming, sems, pl.ds(early, width - cols)
    )
    late_plane = PlaneExchange(
        wide_count, None, None, parts, from_mate, incoming, late_sems, pl.ds(late, cols)
    )
    loads = [
        load_padded(expand.at[0], expand_mat.at[0], load_sems.at[0]),
        load_padded(expand.at[1], expand_mat.at[1], load_sems.at[1]),
    ]

    def reduce_cols(block):
        return reduce_mat.at[
            pl.ds(0, filled), pl.ds(pl.multiple_of(block * cols, cols), cols)
        ]

    line_reduce = LineGather(line, reduce_cols, reduce_send, reduce_recv)
    own_reduce = pltpu.make_async_copy(reduce, reduce_cols(line.mine), load_sems.at[2])
    own_reduce.start()
    if filled < reduce_mat.shape[0]:
        reduce_mat[filled:] = jnp.zeros(
            (reduce_mat.shape[0] - filled, reduce_mat.shape[1]), reduce_mat.dtype
        )
    greet_plane(plane)
    line.greet(3)
    own_reduce.wait()
    line_reduce.send_own()
    kept = []
    waiting = list(loads)

    def compute(chip):
        while waiting:
            waiting.pop().wait()

        def units(cols):
            rows = pair_rows(blocks, chip)
            gate = dot(rows, expand_mat[0, cols], ((1,), (1,))) + shift[0:1, cols]
            upper = dot(rows, expand_mat[1, cols], ((1,), (1,))) + shift[1:2, cols]
            factor = math.sqrt(2 / math.pi)
            square = gate * gate
            bend = jnp.tanh(factor * gate * (1 + 0.044715 * square))
            value = 0.5 * gate * (1 + bend)
            pull = 0.5 * (1 + bend) + 0.5 * gate * (1 - bend * bend) * factor * (
                1 + 3 * 0.044715 * square
            )
            set_pair(active, chip, cols, value * upper)
            set_pair(slope, chip, cols, pull * upper)
            set_pair(gelu, chip, cols, value)

        tiles(active.shape[2], 256, units)

        pair = pl.ds(2 * chip, 2)
        for index, (source, target) in enumerate(
            ((active, active_out), (slope, slope_out), (gelu, gelu_out), (blocks, rows_all))
        ):
            copy = pltpu.make_async_copy(
                source.at[pair], target.at[pair], keep_sems.at[chip, index]
            )
            copy.start()
            kept.append(copy)

    def compute_sums(start, count):
        def compute(chip):
            def outputs(some):
                part = dot(pair_rows(active, chip), reduce_mat[:, some], ((1,), (0,)))
                set_pair(parts, chip, some, part)

            tiles(count, 256, outputs, start)

        return compute

    def between(index):
        if index < narrow_count:
            line_reduce.step(index)

    done = plane.run_gather(compute, between)
    for step in range(done, narrow_count - 1):
        line_reduce.step(step)
    plane.start_sums(compute_sums(early, width - cols))
    line_reduce.step(narrow_count - 1)
    keep_reduce = pltpu.make_async_copy(
        reduce_mat.at[pl.ds(0, filled)], reduce_out, load_sems.at[3]
    )
    keep_reduce.start()
    late_plane.start_sums(compute_sums(late, cols))
    plane.last_sums()
    late_plane.last_sums()
    plane.finish(feed)
    late_plane.finish(feed)

    row_sums[...] = jnp.zeros_like(row_sums)

    def norm_rows(i, carry):
        some = pl.ds(pl.multiple_of(i * 16, 16), 16)
        result, normed, inverse = normalize(
            residual_scale * hidden[some] + feed[some] + reduce_shift[...],
            gain[...],
            norm_shift[...],
        )
        layer_output[some] = result.astype(jnp.bfloat16)
        upstream = cotangent[some].astype(jnp.float32)
        total = normalize_back(upstream, normed, inverse, gain[...])
        sum_grad[some] = total
        feed_grad[some] = total.astype(jnp.bfloat16)
        row_sums[0:1] += jnp.sum(upstream * normed, axis=0, keepdims=True)
        row_sums[1:2] += jnp.sum(upstream, axis=0, keepdims=True)
        row_sums[2:3] += jnp.sum(total, axis=0, keepdims=True)
        return carry

    lax.fori_loop(0, own.shape[0] // 16, norm_rows, 0)
    plane.drain()
    late_plane.drain()
    keep_reduce.wait()
    line_reduce.drain()
    for copy in kept:
        copy.wait()


def geglu_forward(
    wide_count,
    narrow_count,
    hidden_low,
    expand,
    reduce_weight,
    shift,
    hidden,
    cotangent,
    reduce_shift,
    gain,
    norm_shift,
):
    rows, width = hidden_low.shape
    padded = shift.shape[1]
    anywhere = pl.BlockSpec(memory_space=pl.ANY)
    vmem = pl.BlockSpec(memory_space=pltpu.VMEM)
    kept = jax.ShapeDtypeStruct((wide_count, rows, padded), jnp.bfloat16)
    scratch = [pltpu.VMEM((rows, width), jnp.float32)]
    scratch += exchange_scratch(wide_count, rows, width) + [
        pltpu.VMEM((2, padded, width), jnp.bfloat16),
        pltpu.VMEM((padded, width), jnp.bfloat16),
        pltpu.VMEM((wide_count, rows, padded), jnp.bfloat16),
        pltpu.VMEM((wide_count, rows, padded), jnp.bfloat16),
        pltpu.VMEM((wide_count, rows, padded), jnp.bfloat16),
        pltpu.SemaphoreType.DMA((4,)),
        pltpu.SemaphoreType.DMA((wide_count // 2, 4)),
        pltpu.SemaphoreType.DMA((2, narrow_count)),
        pltpu.SemaphoreType.DMA((narrow_count,)),
    ] + sum_scratch(wide_count, rows, width)[3:]
    return pl.pallas_call(
        functools.partial(geglu_forward_kernel, wide_count, narrow_count),
        out_shape=(
            jax.ShapeDtypeStruct((reduce_weight.shape[0], width), jnp.bfloat16),
            jax.ShapeDtypeStruct((wide_count, rows, width), jnp.bfloat16),
            kept,
            kept,
            kept,
            jax.ShapeDtypeStruct((rows, width), jnp.bfloat16),
            jax.ShapeDtypeStruct((rows, width), jnp.float32),
            jax.ShapeDtypeStruct((rows, width), jnp.bfloat16),
            jax.ShapeDtypeStruct((3, width), jnp.float32),
        ),
        in_specs=[anywhere] * 3 + [vmem] * 6,
        out_specs=(anywhere,) * 5 + (vmem,) * 4,
        scratch_shapes=scratch,
        compiler_params=pltpu.CompilerParams(
            collective_id=1, has_side_effects=True, vmem_limit_bytes=kernel_memory
        ),
        cost_estimate=pl.CostEstimate(
            flops=6 * wide_count * rows * padded * width, bytes_accessed=200 * 2**20, transcendentals=0
        ),
        name="geglu_forward",
    )(
        hidden_low,
        expand,
        reduce_weight,
        shift,
        hidden,
        cotangent,
        reduce_shift,
        gain,
        norm_shift,
    )


def geglu_backward_kernel(
    wide_count,
    narrow_count,
    own,
    expand,
    reduce,
    slope_in,
    gelu_in,
    active_in,
    rows_in,
    reduce_grad,
    expand_part,
    hidden_grad,
    unit_sums,
    blocks,
    gather_send,
    gather_recv,
    own_sem,
    parts,
    from_mate,
    incoming,
    mate_send,
    mate_recv,
    sum_send,
    sum_recv,
    expand_mat,
    reduce_mat,
    slope,
    gelu,
    active,
    rows_all,
    staged,
    load_sems,
    keep_sems,
    line_in,
    line_send,
    line_recv,
):
    sems = (gather_send, gather_recv, mate_send, mate_recv, sum_send, sum_recv, own_sem)
    plane = PlaneExchange(wide_count, own, blocks, parts, from_mate, incoming, sems)
    loads = [
        load_padded(expand.at[0], expand_mat.at[0], load_sems.at[0]),
        load_padded(expand.at[1], expand_mat.at[1], load_sems.at[1]),
        load_padded(reduce, reduce_mat, load_sems.at[2]),
        pltpu.make_async_copy(slope_in, slope, load_sems.at[3]),
        pltpu.make_async_copy(gelu_in, gelu, load_sems.at[4]),
    ]
    late_loads = [
        pltpu.make_async_copy(active_in, active, load_sems.at[5]),
        pltpu.make_async_copy(rows_in, rows_all, load_sems.at[6]),
    ]
    for copy in loads[3:]:
        copy.start()
    unit_sums[...] = jnp.zeros_like(unit_sums)
    line = LineExchange(narrow_count)
    filled, line_cols = line_in.shape[2:]

    def line_part(block):
        return reduce_mat.at[
            pl.ds(0, filled), pl.ds(pl.multiple_of(block * line_cols, line_cols), line_cols)
        ]

    line_sum = LineSum(line, line_part, line_in, line_send, line_recv)
    greet_plane(plane)
    line.greet(3)
    for copy in late_loads:
        copy.start()
    kept = []
    waiting = list(loads)

    def compute(chip):
        while waiting:
            waiting.pop().wait()

        def units(cols):
            pulled = dot(pair_rows(blocks, chip), reduce_mat[cols], ((1,), (1,)))
            pair = pl.ds(2 * chip, 2)
            shape = pulled.shape
            gate_grad = pulled * slope[pair, :, cols].reshape(shape).astype(jnp.float32)
            upper_grad = pulled * gelu[pair, :, cols].reshape(shape).astype(jnp.float32)
            set_pair(slope, chip, cols, gate_grad)
            set_pair(gelu, chip, cols, upper_grad)
            unit_sums[0:1, cols] += jnp.sum(gate_grad, axis=0, keepdims=True)
            unit_sums[1:2, cols] += jnp.sum(upper_grad, axis=0, keepdims=True)

        tiles(slope.shape[2], 256, units)

    def compute_sums(chip):
        def outputs(cols):
            set_pair(
                parts,
                chip,
                cols,
                dot(pair_rows(slope, chip), expand_mat[0, :, cols], ((1,), (0,)))
                + dot(pair_rows(gelu, chip), expand_mat[1, :, cols], ((1,), (0,))),
            )

        tiles(parts.shape[2], 256, outputs)

    def product(left, right, start):
        tokens = left.shape[0] * left.shape[1]
        return dot(
            left[:, :, start : start + 256].reshape(tokens, 256),
            right[...].reshape(tokens, right.shape[2]),
            ((0,), (0,)),
        ).astype(jnp.bfloat16)

    def reduce_work():
        for copy in late_loads:
            copy.wait()

        def reduce_cols(index):
            cols = pl.ds(pl.multiple_of(index * line_cols, line_cols), line_cols)

            def units(some):
                tokens = active.shape[0] * active.shape[1]
                part = dot(
                    active[:, :, some].reshape(tokens, some.size),
                    blocks[:, :, cols].reshape(tokens, line_cols),
                    ((0,), (0,)),
                )
                reduce_mat[some, cols] = part.astype(jnp.bfloat16)

            tiles(active.shape[2], 256, units)

        for offset in range(narrow_count - 1, 0, -1):
            for way in range(2):

                @pl.when(line_sum.reaches(way, offset))
                def _():
                    reduce_cols(line_sum.target(way, offset))

            line_sum.begin(offset)
        reduce_cols(line.mine)

    def expand_work(left, start, target):
        def work():
            index = len(kept)
            if index >= 2:
                kept[index - 2].wait()
            staged[index % 2] = product(left, rows_all, start)
            stop = min(256, target.shape[0] - start)
            copy = pltpu.make_async_copy(
                staged.at[index % 2, pl.ds(0, stop)],
                target.at[pl.ds(start, stop)],
                keep_sems.at[index % 2],
            )
            copy.start()
            kept.append(copy)

        return work

    works = [
        expand_work(left, start, target)
        for left, target in ((slope, expand_part.at[0]), (gelu, expand_part.at[1]))
        for start in range(0, target.shape[0], 256)
    ]
    steps = [
        functools.partial(line_sum.step, offset) for offset in range(narrow_count - 2, 0, -1)
    ]
    third = len(works) // 3
    middle = (len(steps) + 1) // 2

    def many(calls):
        for call in calls:
            call()

    beside = functools.partial(many, steps[:middle] + works[:third])
    plane.run(compute, compute_sums, reduce_work, beside)
    many(works[third : 2 * third] + steps[middle:] + works[2 * third :])
    plane.finish(hidden_grad)
    plane.drain()
    line_sum.finish(reduce_grad)
    line_sum.drain()
    for copy in kept[-2:]:
        copy.wait()


def geglu_backward(
    wide_count,
    narrow_count,
    feed_grad,
    expand,
    reduce_full,
    slope,
    gelu,
    active,
    rows_all,
):
    rows, width = feed_grad.shape
    padded = slope.shape[2]
    anywhere = pl.BlockSpec(memory_space=pl.ANY)
    vmem = pl.BlockSpec(memory_space=pltpu.VMEM)
    scratch = exchange_scratch(wide_count, rows, width) + [
        pltpu.VMEM((2, padded, width), jnp.bfloat16),
        pltpu.VMEM((padded, width), jnp.bfloat16),
        pltpu.VMEM((wide_count, rows, padded), jnp.bfloat16),
        pltpu.VMEM((wide_count, rows, padded), jnp.bfloat16),
        pltpu.VMEM((wide_count, rows, padded), jnp.bfloat16),
        pltpu.VMEM((wide_count, rows, width), jnp.bfloat16),
        pltpu.VMEM((2, 256, width), jnp.bfloat16),
        pltpu.SemaphoreType.DMA((7,)),
        pltpu.SemaphoreType.DMA((2,)),
        pltpu.VMEM(
            (2, narrow_count - 1, reduce_full.shape[0], width // narrow_count), jnp.bfloat16
        ),
        pltpu.SemaphoreType.DMA((2, narrow_count - 1)),
        pltpu.SemaphoreType.DMA((2, narrow_count - 1)),
    ]
    return pl.pallas_call(
        functools.partial(geglu_backward_kernel, wide_count, narrow_count),
        out_shape=(
            jax.ShapeDtypeStruct(
                (reduce_full.shape[0], width // narrow_count), jnp.float32
            ),
            jax.ShapeDtypeStruct(expand.shape, jnp.bfloat16),
            jax.ShapeDtypeStruct((rows, width), jnp.float32),
            jax.ShapeDtypeStruct((2, padded), jnp.float32),
        ),
        in_specs=[anywhere] * 7,
        out_specs=(vmem, anywhere, vmem, vmem),
        scratch_shapes=scratch,
        compiler_params=pltpu.CompilerParams(
            collective_id=2, has_side_effects=True, vmem_limit_bytes=63 * 2**20
        ),
        cost_estimate=pl.CostEstimate(
            flops=12 * wide_count * rows * padded * width, bytes_accessed=200 * 2**20, transcendentals=0
        ),
        name="geglu_backward",
    )(feed_grad, expand, reduce_full, slope, gelu, active, rows_all)


def key_slices(bucket):
    return [slice(start, start + key_tile) for start in range(0, bucket, key_tile)]


def rotate_lanes(vectors, cosine, signed_sine):
    return vectors * cosine + pltpu.roll(vectors, vectors.shape[1] // 2, 1) * signed_sine


def attention_backward_kernel(
    wide_count,
    narrow_count,
    upper_grad,
    hidden_part,
    normed,
    inv_std,
    gain,
    merge,
    mixed,
    queries,
    keys,
    values,
    probs,
    cosine,
    signed_sine,
    triple,
    merge_grad,
    heads_sums,
    merge_sums,
    sum_grad,
    norm_sums,
    attended,
    upstream,
    outbound,
    probs_held,
    keys_turned,
    key_total,
    value_total,
    merge_out,
    merge_in,
    mixed_send,
    mixed_recv,
    merge_send,
    merge_recv,
    load_sems,
    scaled_held,
    change_held,
    parts,
    from_mate,
    incoming,
    mate_send,
    mate_recv,
    sum_send,
    sum_recv,
):
    sems = (None, None, mate_send, mate_recv, sum_send, sum_recv, None)
    plane = PlaneExchange(wide_count, None, None, parts, from_mate, incoming, sems)
    line = LineExchange(narrow_count)
    rows, width = sum_grad.shape
    own_cols = queries.shape[1]
    heads = own_cols // HDIM
    bucket = queries.shape[0]
    scale = HDIM ** (-0.5)

    def load(head):
        return pltpu.make_async_copy(
            probs.at[head], probs_held.at[head % 2], load_sems.at[head % 2]
        )

    load(0).start()
    greet_plane(plane)

    norm_sums[...] = jnp.zeros_like(norm_sums)
    merge_sums[...] = jnp.zeros_like(merge_sums)

    def norm_rows(i, carry):
        some = pl.ds(pl.multiple_of(i * 16, 16), 16)
        hidden_grad = residual_scale * upper_grad[some] + hidden_part[some]
        norm_sums[0:1] += jnp.sum(hidden_grad * normed[some], axis=0, keepdims=True)
        norm_sums[1:2] += jnp.sum(hidden_grad, axis=0, keepdims=True)
        total = normalize_back(hidden_grad, normed[some], inv_std[some], gain[...])
        sum_grad[some] = total
        merge_sums[...] += jnp.sum(total, axis=0, keepdims=True)
        attended[some] = total.astype(jnp.bfloat16)
        return carry

    lax.fori_loop(0, rows // 16, norm_rows, 0)
    line.greet(3)

    def mixed_part(target, where):
        part = dot(
            attended[...],
            merge[pl.ds(pl.multiple_of(where * own_cols, own_cols), own_cols)],
            ((1,), (1,)),
        )
        target[...] = part.astype(jnp.bfloat16)

    for offset in range(1, narrow_count):
        place = line.peer(offset)
        mixed_part(outbound.at[offset - 1], place)
        line.send(offset, outbound.at[offset - 1], upstream, mixed_send, mixed_recv)
    mixed_part(upstream.at[line.mine], line.mine)

    block = parts.shape[1]

    def merge_rows(i, carry):
        cols = pl.ds(pl.multiple_of(i * block, block), block)
        parts[i] = dot(mixed[:, cols], attended[...], ((0,), (0,))).astype(jnp.bfloat16)
        return carry

    lax.fori_loop(0, wide_count, merge_rows, 0)
    for offset in range(plane.ring):
        plane.share(offset)
    plane.first_sums()
    plane.far_sums()
    plane.last_sums()
    plane.finish(merge_out)
    count = merge_grad.shape[0]

    def z_rows(where):
        return pl.ds(pl.multiple_of(where * count, count), count)

    for offset in range(1, narrow_count):
        line.send(
            offset, merge_out.at[z_rows(line.peer(offset))], merge_in, merge_send, merge_recv
        )
    for offset in range(1, narrow_count):
        line.arrived(offset, upstream, mixed_send, mixed_recv)

    def one_head(head):
        cols = pl.ds(head * HDIM, HDIM)
        load(head).wait()
        if head + 1 < heads:
            load(head + 1).start()
        held = probs_held.at[head % 2]
        keys_turned[...] = keys[:, cols].astype(jnp.float32).T.astype(jnp.bfloat16)
        key_total[...] = jnp.zeros_like(key_total)
        value_total[...] = jnp.zeros_like(value_total)

        def chunk(i, carry):
            here = pl.ds(pl.multiple_of(i * rows, rows), rows)
            up = upstream[i, :, cols]
            query = queries[here, cols]
            sums = None
            for some in key_slices(bucket):
                weights = held[some, here]
                scaled = weights.astype(jnp.float32) * dot(values[some, cols], up, ((1,), (1,)))
                scaled_held[some] = scaled
                part = jnp.sum(scaled.reshape(-1, 8, rows), axis=0)
                sums = part if sums is None else sums + part
                value_total[some] += dot(weights, up, ((1,), (0,)))
            total = jnp.sum(sums, axis=0, keepdims=True)
            for some in key_slices(bucket):
                change = scaled_held[some] - held[some, here].astype(jnp.float32) * total
                change = change.astype(jnp.bfloat16)
                change_held[some] = change
                key_total[some] += dot(change, query, ((1,), (0,)))
            query_grad = dot(keys_turned[...], change_held[...], ((1,), (0,))).T * scale
            triple[here, cols] = rotate_lanes(
                query_grad, cosine[here], signed_sine[here]
            ).astype(jnp.bfloat16)
            return carry

        lax.fori_loop(0, narrow_count, chunk, 0)

        def ending(i, carry):
            here = pl.ds(pl.multiple_of(i * rows, rows), rows)
            triple[here, pl.ds(own_cols + head * HDIM, HDIM)] = rotate_lanes(
                key_total[here] * scale, cosine[here], signed_sine[here]
            ).astype(jnp.bfloat16)
            triple[here, pl.ds(2 * own_cols + head * HDIM, HDIM)] = value_total[here].astype(
                jnp.bfloat16
            )
            return carry

        lax.fori_loop(0, narrow_count, ending, 0)

    for head in range(heads):
        one_head(head)

    def column_sums(cols):
        heads_sums[:, cols] = jnp.sum(
            triple[:, cols].astype(jnp.float32), axis=0, keepdims=True
        )

    tiles(3 * own_cols, 256, column_sums)
    summed = merge_out[z_rows(line.mine)].astype(jnp.float32)
    for offset in range(1, narrow_count):
        line.arrived(offset, merge_in, merge_send, merge_recv)
        summed += merge_in[line.peer(offset)].astype(jnp.float32)
    merge_grad[...] = summed
    line.drain()
    plane.drain()


def attention_backward(
    wide_count,
    narrow_count,
    upper_grad,
    hidden_part,
    normed,
    inv_std,
    gain,
    merge_full,
    mixed,
    queries,
    keys,
    values,
    probs,
    cosine,
    signed_sine,
):
    rows, width = normed.shape
    bucket, own_cols = queries.shape
    block = width // wide_count
    count = block // narrow_count
    anywhere = pl.BlockSpec(memory_space=pl.ANY)
    vmem = pl.BlockSpec(memory_space=pltpu.VMEM)
    dma = pltpu.SemaphoreType.DMA
    return pl.pallas_call(
        functools.partial(attention_backward_kernel, wide_count, narrow_count),
        out_shape=(
            jax.ShapeDtypeStruct((bucket, 3 * own_cols), jnp.bfloat16),
            jax.ShapeDtypeStruct((count, width), jnp.float32),
            jax.ShapeDtypeStruct((1, 3 * own_cols), jnp.float32),
            jax.ShapeDtypeStruct((1, width), jnp.float32),
            jax.ShapeDtypeStruct((rows, width), jnp.float32),
            jax.ShapeDtypeStruct((2, width), jnp.float32),
        ),
        in_specs=[vmem] * 10 + [anywhere] + [vmem] * 2,
        out_specs=(vmem,) * 6,
        scratch_shapes=[
            pltpu.VMEM((rows, width), jnp.bfloat16),
            pltpu.VMEM((narrow_count, rows, own_cols), jnp.bfloat16),
            pltpu.VMEM((narrow_count - 1, rows, own_cols), jnp.bfloat16),
            pltpu.VMEM((2, bucket, bucket), jnp.bfloat16),
            pltpu.VMEM((HDIM, bucket), jnp.bfloat16),
            pltpu.VMEM((bucket, HDIM), jnp.float32),
            pltpu.VMEM((bucket, HDIM), jnp.float32),
            pltpu.VMEM((block, width), jnp.bfloat16),
            pltpu.VMEM((narrow_count, count, width), jnp.bfloat16),
            dma((narrow_count - 1,)),
            dma((narrow_count,)),
            dma((narrow_count - 1,)),
            dma((narrow_count,)),
            dma((2,)),
            pltpu.VMEM((bucket, rows), jnp.float32),
            pltpu.VMEM((bucket, rows), jnp.bfloat16),
        ]
        + sum_scratch(wide_count, block, width),
        compiler_params=pltpu.CompilerParams(
            collective_id=3, has_side_effects=True, vmem_limit_bytes=kernel_memory
        ),
        cost_estimate=pl.CostEstimate(
            flops=60 * 10**9, bytes_accessed=200 * 2**20, transcendentals=0
        ),
        name="attention_backward",
    )(
        upper_grad,
        hidden_part,
        normed,
        inv_std,
        gain,
        merge_full,
        mixed,
        queries,
        keys,
        values,
        probs,
        cosine,
        signed_sine,
    )


def input_backward_kernel(
    wide_count,
    narrow_count,
    inputs,
    triple,
    heads_mat,
    small,
    input_part,
    heads_grad,
    small_out,
    line_parts,
    line_in,
    heads_out,
    heads_in,
    small_wide,
    small_sum,
    small_line,
    line_send,
    line_recv,
    heads_send,
    heads_recv,
    wide_send,
    wide_recv,
    small_send,
    small_recv,
    parts,
    from_mate,
    incoming,
    mate_send,
    mate_recv,
    sum_send,
    sum_recv,
):
    sems = (None, None, mate_send, mate_recv, sum_send, sum_recv, None)
    plane = PlaneExchange(wide_count, None, None, parts, from_mate, incoming, sems)
    line = LineExchange(narrow_count)
    rows, width = input_part.shape
    here = line.mine
    last = narrow_count - 1
    place = lax.axis_index("wide")

    def wide_peer(offset):
        return (place + offset) % wide_count

    barrier = pltpu.get_barrier_semaphore()
    for offset in range(1, wide_count):
        pl.semaphore_signal(
            barrier,
            inc=1,
            device_id={"wide": wide_peer(offset)},
            device_id_type=pl.DeviceIdType.MESH,
        )
    line.greet(wide_count - 1)

    def small_copy(offset, source, slot):
        return pltpu.make_async_remote_copy(
            src_ref=source,
            dst_ref=small_wide.at[slot],
            send_sem=wide_send.at[offset - 1],
            recv_sem=wide_recv.at[slot],
            device_id={"wide": wide_peer(offset)},
            device_id_type=pl.DeviceIdType.MESH,
        )

    small_copies = [
        small_copy(offset, small.at[wide_peer(offset)], place) for offset in range(1, wide_count)
    ]
    for copy in small_copies:
        copy.start()

    line_sum = LineSum(line, lambda target: line_parts.at[target], line_in, line_send, line_recv)

    def input_rows(index):
        some = pl.ds(pl.multiple_of(index * rows, rows), rows)

        def input_cols(cols):
            part = dot(triple[some], heads_mat[cols], ((1,), (1,)))
            line_parts[index, :, cols] = part.astype(jnp.bfloat16)

        tiles(width, 256, input_cols)

    for offset in range(last, 0, -1):
        for way in range(2):

            @pl.when(line_sum.reaches(way, offset))
            def _():
                input_rows(line_sum.target(way, offset))

        line_sum.begin(offset)
    input_rows(here)

    block = parts.shape[1]

    def heads_rows(i, carry):
        cols = pl.ds(pl.multiple_of(i * block, block), block)
        parts[i] = dot(inputs[:, cols], triple[...], ((0,), (0,))).astype(jnp.bfloat16)
        return carry

    lax.fori_loop(0, wide_count, heads_rows, 0)
    for offset in range(plane.ring):
        plane.share(offset)
    for offset in range(last - 1, last // 2, -1):
        line_sum.step(offset)
    plane.first_sums()
    plane.far_sums()

    for offset in range(1, wide_count):
        peer = wide_peer(offset)
        small_copy(offset, small_wide.at[peer], peer).wait_recv()
    small_wide[place] = small[place]
    total = small_wide[0]
    for index in range(1, wide_count):
        total += small_wide[index]
    small_sum[...] = total
    for offset in range(1, narrow_count):
        line.send(offset, small_sum.at[line.peer(offset)], small_line, small_send, small_recv)

    plane.last_sums()
    for offset in range(last // 2, 0, -1):
        line_sum.step(offset)
    plane.finish(heads_out)
    count = heads_grad.shape[0]

    def z_rows(where):
        return pl.ds(pl.multiple_of(where * count, count), count)

    for offset in range(1, narrow_count):
        line.send(
            offset, heads_out.at[z_rows(line.peer(offset))], heads_in, heads_send, heads_recv
        )
    heads_in[line.mine] = heads_out[z_rows(line.mine)]
    small_line[line.mine] = small_sum[line.mine]
    for offset in range(1, narrow_count):
        line.arrived(offset, small_line, small_send, small_recv)
    result = small_line[0]
    for index in range(1, narrow_count):
        result += small_line[index]
    small_out[...] = result

    line_sum.finish(input_part)
    for offset in range(1, narrow_count):
        line.arrived(offset, heads_in, heads_send, heads_recv)
    own_cols = triple.shape[1] // 3
    for index in range(narrow_count):
        for which in range(3):
            start = (which * narrow_count + index) * own_cols
            heads_grad[:, start : start + own_cols] = heads_in[
                index, :, which * own_cols : (which + 1) * own_cols
            ].astype(jnp.float32)
    line_sum.drain()
    for copy in small_copies:
        copy.wait_send()
    line.drain()
    plane.drain()


def input_backward(wide_count, narrow_count, inputs, triple_grad, heads_mat, small):
    bucket, width = inputs.shape
    rows = bucket // narrow_count
    columns = triple_grad.shape[1]
    block = width // wide_count
    count = block // narrow_count
    vmem = pl.BlockSpec(memory_space=pltpu.VMEM)
    dma = pltpu.SemaphoreType.DMA
    lines = small.shape[2]
    return pl.pallas_call(
        functools.partial(input_backward_kernel, wide_count, narrow_count),
        out_shape=(
            jax.ShapeDtypeStruct((rows, width), jnp.float32),
            jax.ShapeDtypeStruct((count, narrow_count * columns), jnp.float32),
            jax.ShapeDtypeStruct((lines, 128), jnp.float32),
        ),
        in_specs=[vmem] * 4,
        out_specs=(vmem, vmem, vmem),
        scratch_shapes=[
            pltpu.VMEM((narrow_count, rows, width), jnp.bfloat16),
            pltpu.VMEM((2, narrow_count - 1, rows, width), jnp.bfloat16),
            pltpu.VMEM((block, columns), jnp.bfloat16),
            pltpu.VMEM((narrow_count, count, columns), jnp.bfloat16),
            pltpu.VMEM((wide_count, narrow_count, lines, 128), jnp.float32),
            pltpu.VMEM((narrow_count, lines, 128), jnp.float32),
            pltpu.VMEM((narrow_count, lines, 128), jnp.float32),
            dma((2, narrow_count - 1)),
            dma((2, narrow_count - 1)),
            dma((narrow_count - 1,)),
            dma((narrow_count,)),
            dma((wide_count - 1,)),
            dma((wide_count,)),
            dma((narrow_count - 1,)),
            dma((narrow_count,)),
        ]
        + sum_scratch(wide_count, block, columns),
        compiler_params=pltpu.CompilerParams(
            collective_id=4, has_side_effects=True, vmem_limit_bytes=kernel_memory
        ),
        cost_estimate=pl.CostEstimate(
            flops=80 * 10**9, bytes_accessed=200 * 2**20, transcendentals=0
        ),
        name="input_backward",
    )(inputs, triple_grad, heads_mat, small)


def greet_all(wide_count, narrow_count):
    barrier = pltpu.get_barrier_semaphore()
    for axis, count in (("wide", wide_count), ("narrow", narrow_count)):
        place = lax.axis_index(axis)
        for offset in range(1, count):
            pl.semaphore_signal(
                barrier,
                inc=1,
                device_id={axis: (place + offset) % count},
                device_id_type=pl.DeviceIdType.MESH,
            )
    pl.semaphore_wait(barrier, wide_count + narrow_count - 2)


def gather_kernel(
    wide_count,
    narrow_count,
    own,
    heads_weight,
    merge_weight,
    small,
    buckets,
    speeds,
    rows_out,
    heads_out,
    merge_out,
    small_out,
    triple,
    cosine,
    signed_sine,
    first_query,
    last_query,
    rows_all,
    heads_all,
    merge_all,
    small_all,
    rows_send,
    rows_recv,
    heads_send,
    heads_recv,
    merge_send,
    merge_recv,
    small_send,
    small_recv,
    wide_send,
    wide_recv,
    local_sems,
    out_sems,
    heads_ring_send,
    heads_ring_recv,
    merge_ring_send,
    merge_ring_recv,
):
    def ring_of(blocks, send, recv):
        sems = (send, recv, None, None, None, None, None)
        return PlaneExchange(wide_count, None, blocks, blocks, None, None, sems)

    heads_ring = ring_of(heads_all, heads_ring_send, heads_ring_recv)
    merge_ring = ring_of(merge_all, merge_ring_send, merge_ring_recv)
    line = LineExchange(narrow_count)
    here = line.mine
    last = narrow_count - 1
    place = lax.axis_index("wide")
    slot = heads_ring.slot(0)
    rows, width = own.shape
    count = heads_weight.shape[0]
    columns = heads_all.shape[2]
    own_cols = columns // 3

    def z_rows(where):
        return pl.ds(pl.multiple_of(where * count, count), count)

    def head_cols(which, where):
        start = which * narrow_count * own_cols + where * own_cols
        return pl.ds(pl.multiple_of(start, own_cols), own_cols)

    line_rows = LineGather(line, lambda block: rows_all.at[block], rows_send, rows_recv)

    keep_rows = pltpu.make_async_copy(own, rows_all.at[here], local_sems.at[0])
    keep_rows.start()
    keeps = [
        pltpu.make_async_copy(
            heads_weight.at[:, head_cols(which, here)],
            heads_all.at[slot, z_rows(here), pl.ds(which * own_cols, own_cols)],
            local_sems.at[2 + which],
        )
        for which in range(3)
    ]
    keep_merge = pltpu.make_async_copy(
        merge_weight, merge_all.at[slot, z_rows(here)], local_sems.at[1]
    )
    for copy in keeps + [keep_merge]:
        copy.start()
    small_all[place, here] = small[...]
    greet_all(wide_count, narrow_count)

    def heads_copy(offset, which, where, sender):
        return line.copy(
            heads_weight.at[:, head_cols(which, where)],
            heads_all.at[slot, z_rows(sender), pl.ds(which * own_cols, own_cols)],
            heads_send.at[offset - 1, which],
            heads_recv.at[sender, which],
            where,
        )

    def merge_copy(offset, where, sender):
        return line.copy(
            merge_weight,
            merge_all.at[slot, z_rows(sender)],
            merge_send.at[offset - 1],
            merge_recv.at[sender],
            where,
        )

    def small_copy(offset, where, sender):
        return line.copy(
            small,
            small_all.at[place, sender],
            small_send.at[offset - 1],
            small_recv.at[sender],
            where,
        )

    started = []

    def start(copy):
        copy.start()
        started.append(copy)

    for offset in range(1, narrow_count):
        for which in range(3):
            start(heads_copy(offset, which, line.peer(offset), here))
    for offset in range(1, narrow_count):
        start(small_copy(offset, line.peer(offset), here))
    keep_rows.wait()
    line_rows.send_own()

    halfway = narrow_count * rows // 2
    joined = buckets[0]

    def tables(i, carry):
        some = pl.ds(pl.multiple_of(i * rows, rows), rows)
        place_in = i * rows + lax.broadcasted_iota(jnp.int32, (rows, 1), 0)
        second = jnp.where(place_in >= halfway, 1 - joined, 0)
        local = place_in - second * halfway
        reach = jnp.where(
            joined == 1,
            buckets[1] + buckets[2],
            jnp.where(second == 1, buckets[2], buckets[1]),
        )
        first_query[some] = jnp.where(local < reach, place_in - local, place_in)
        last_query[some] = jnp.where(
            (joined == 1) | (second == 1), 2 * halfway - 1, halfway - 1
        ) + jnp.zeros_like(place_in)
        angles = local.astype(jnp.float32) * speeds[...]
        lane = lax.broadcasted_iota(jnp.int32, (rows, HDIM), 1)
        cosine[some] = jnp.cos(angles)
        sine = jnp.sin(angles)
        signed_sine[some] = jnp.where(lane < HDIM // 2, sine, -sine)
        return carry

    lax.fori_loop(0, narrow_count, tables, 0)

    for copy in keeps:
        copy.wait()
    for offset in range(1, narrow_count):
        for which in range(3):
            heads_copy(offset, which, line.peer(offset), line.peer(offset)).wait_recv()
    heads_ring.send_own()
    for offset in range(1, narrow_count):
        small_copy(offset, line.peer(offset), line.peer(offset)).wait_recv()

    def wide_copy(offset, sender):
        return pltpu.make_async_remote_copy(
            src_ref=small_all.at[sender],
            dst_ref=small_all.at[sender],
            send_sem=wide_send.at[offset - 1],
            recv_sem=wide_recv.at[sender],
            device_id={"wide": (place + offset) % wide_count},
            device_id_type=pl.DeviceIdType.MESH,
        )

    for offset in range(1, wide_count):
        start(wide_copy(offset, place))

    def project(block):
        def cols_step(cols):
            weight = heads_all[:, :, cols].reshape(width, cols.size)
            triple[pl.ds(pl.multiple_of(block * rows, rows), rows), cols] = dot(
                rows_all[block], weight, ((1,), (0,))
            )

        tiles(columns, 256, cols_step)

    def project_step(step):
        line_rows.each(step, project)

    def gather(ring, distance):
        ring.receive(distance)
        ring.receive_mate(-distance)
        if distance < ring.far:
            ring.receive_mate(distance)

    outs = []

    def keep_out(source, target):
        copy = pltpu.make_async_copy(source, target, out_sems.at[len(outs)])
        copy.start()
        outs.append(copy)

    line_rows.step(1)
    for offset in range(1, narrow_count):
        start(merge_copy(offset, line.peer(offset), here))
    heads_ring.receive_mate(0)
    for distance in range(1, heads_ring.far + 1):
        gather(heads_ring, distance)
    keep_out(heads_all, heads_out)
    project(here)
    for step in range(2, narrow_count):
        line_rows.step(step)
        if step == 2:
            keep_merge.wait()
            for offset in range(1, narrow_count):
                merge_copy(offset, line.peer(offset), line.peer(offset)).wait_recv()
            merge_ring.send_own()
        project_step(step - 1)
        if step == 2:
            merge_ring.receive_mate(0)
            for distance in range(1, merge_ring.far + 1):
                gather(merge_ring, distance)
            keep_out(merge_all, merge_out)
    project_step(last)
    keep_out(rows_all, rows_out)
    for offset in range(1, wide_count):
        wide_copy(offset, (place + offset) % wide_count).wait_recv()
    keep_out(small_all, small_out)
    line_rows.drain()
    for copy in started:
        copy.wait_send()
    heads_ring.drain()
    merge_ring.drain()
    for copy in outs:
        copy.wait()


def gather_front(
    wide_count, narrow_count, layer_input, heads_weight, merge_weight, small, buckets, speeds
):
    rows, width = layer_input.shape
    count, all_columns = heads_weight.shape
    columns = all_columns // narrow_count
    block = count * narrow_count
    anywhere = pl.BlockSpec(memory_space=pl.ANY)
    vmem = pl.BlockSpec(memory_space=pltpu.VMEM)
    dma = pltpu.SemaphoreType.DMA
    lines = small.shape[0]
    shapes = (
        (narrow_count, rows, width),
        (wide_count, block, columns),
        (wide_count, block, width),
        (wide_count, narrow_count, lines, 128),
    )
    far = narrow_count - 1
    bucket = narrow_count * rows
    table = jax.ShapeDtypeStruct((bucket, HDIM), jnp.float32)
    reach = jax.ShapeDtypeStruct((bucket, 1), jnp.int32)
    return pl.pallas_call(
        functools.partial(gather_kernel, wide_count, narrow_count),
        out_shape=tuple(jax.ShapeDtypeStruct(shape, jnp.bfloat16) for shape in shapes)
        + (jax.ShapeDtypeStruct((bucket, columns), jnp.float32), table, table, reach, reach),
        in_specs=[anywhere, anywhere, anywhere, vmem, pl.BlockSpec(memory_space=pltpu.SMEM), vmem],
        out_specs=(anywhere,) * 4 + (vmem,) * 5,
        scratch_shapes=[pltpu.VMEM(shape, jnp.bfloat16) for shape in shapes]
        + [
            dma((2, narrow_count)),
            dma((narrow_count,)),
            dma((far, 3)),
            dma((narrow_count, 3)),
            dma((far,)),
            dma((narrow_count,)),
            dma((far,)),
            dma((narrow_count,)),
            dma((wide_count - 1,)),
            dma((wide_count,)),
            dma((5,)),
            dma((4,)),
            dma((3, wide_count, 2)),
            dma((wide_count, 2)),
            dma((3, wide_count, 2)),
            dma((wide_count, 2)),
        ],
        compiler_params=pltpu.CompilerParams(
            collective_id=5, has_side_effects=True, vmem_limit_bytes=kernel_memory
        ),
        cost_estimate=pl.CostEstimate(
            flops=80 * 10**9, bytes_accessed=200 * 2**20, transcendentals=0
        ),
        name="gather_front",
    )(layer_input, heads_weight, merge_weight, small, buckets, speeds)


def attention_forward_kernel(
    narrow_count,
    triple,
    heads_shift,
    cosine,
    signed_sine,
    first_query,
    last_query,
    own,
    merge,
    merge_shift,
    gain,
    shift,
    queries,
    keys,
    values,
    probs,
    mixed_out,
    hidden,
    hidden_low,
    normed,
    inv_std,
    merge_mat,
    probs_held,
    values_turned,
    outbound,
    mixed,
    mixed_send,
    mixed_recv,
    local_sems,
    scores_held,
):
    line = LineExchange(narrow_count)
    bucket, own_cols = queries.shape
    rows, width = own.shape
    heads = own_cols // HDIM
    scale = HDIM ** (-0.5)
    load_merge = pltpu.make_async_copy(merge, merge_mat, local_sems.at[2])
    load_merge.start()
    line.greet()

    def keep(head):
        return pltpu.make_async_copy(
            probs_held.at[head % 2], probs.at[head], local_sems.at[head % 2]
        )

    def mixed_copy(head, offset, where, sender):
        cols = pl.ds(pl.multiple_of(sender * own_cols + head * HDIM, HDIM), HDIM)
        return line.copy(
            outbound.at[where, :, pl.ds(head * HDIM, HDIM)],
            mixed.at[:, cols],
            mixed_send.at[offset - 1, head],
            mixed_recv.at[sender, head],
            where,
        )

    started = []
    for head in range(heads):
        cols = pl.ds(head * HDIM, HDIM)

        def turn(i, carry):
            here = pl.ds(pl.multiple_of(i * rows, rows), rows)
            for which, target in enumerate((queries, keys, values)):
                wanted = pl.ds(which * own_cols + head * HDIM, HDIM)
                part = triple[here, wanted] + heads_shift[:, wanted]
                if which < 2:
                    part = rotate_lanes(part, cosine[here], -signed_sine[here])
                else:
                    values_turned[:, here] = part.T.astype(jnp.bfloat16)
                target[here, cols] = part.astype(jnp.bfloat16)
            return carry

        lax.fori_loop(0, narrow_count, turn, 0)
        if head >= 2:
            keep(head - 2).wait()
        held = probs_held.at[head % 2]

        def chunk(i, carry):
            here = pl.ds(pl.multiple_of(i * rows, rows), rows)
            query = queries[here, cols]
            token = i * rows + lax.broadcasted_iota(jnp.int32, (key_tile, rows), 1)
            tops, sums = None, None
            for some in key_slices(bucket):
                scores = dot(keys[some, cols], query, ((1,), (1,))) * scale
                seen = (token >= first_query[some]) & (token <= last_query[some])
                scores = jnp.where(seen, scores, masked_value)
                scores_held[some] = scores
                top = jnp.max(scores.reshape(-1, 8, rows), axis=0)
                tops = top if tops is None else jnp.maximum(tops, top)
            top = jnp.max(tops, axis=0, keepdims=True)
            for some in key_slices(bucket):
                expo = jnp.exp(scores_held[some] - top)
                scores_held[some] = expo
                part = jnp.sum(expo.reshape(-1, 8, rows), axis=0)
                sums = part if sums is None else sums + part
            share = 1 / jnp.sum(sums, axis=0, keepdims=True)
            for some in key_slices(bucket):
                held[some, here] = (scores_held[some] * share).astype(jnp.bfloat16)
            mixed_part = dot(values_turned[...], held[:, here], ((1,), (0,)))
            outbound[i, :, cols] = mixed_part.T.astype(jnp.bfloat16)
            return carry

        lax.fori_loop(0, narrow_count, chunk, 0)
        keep(head).start()
        for offset in range(1, narrow_count):
            copy = mixed_copy(head, offset, line.peer(offset), line.mine)
            copy.start()
            started.append(copy)
    own_mixed = pltpu.make_async_copy(
        outbound.at[line.mine],
        mixed.at[:, pl.ds(pl.multiple_of(line.mine * own_cols, own_cols), own_cols)],
        local_sems.at[3],
    )
    own_mixed.start()
    own_mixed.wait()
    load_merge.wait()
    for offset in range(1, narrow_count):
        for head in range(heads):
            mixed_copy(head, offset, line.peer(offset), line.peer(offset)).wait_recv()
    mixed_out[...] = mixed[...]

    def merge_cols(cols):
        hidden[:, cols] = (
            residual_scale * own[:, cols].astype(jnp.float32)
            + dot(mixed[...], merge_mat[:, cols], ((1,), (0,)))
            + merge_shift[:, cols]
        )

    tiles(width, 256, merge_cols)

    def norm_rows(i, carry):
        some = pl.ds(pl.multiple_of(i * 16, 16), 16)
        result, centred, inverse = normalize(hidden[some], gain[...], shift[...])
        hidden[some] = result
        hidden_low[some] = result.astype(jnp.bfloat16)
        normed[some] = centred
        inv_std[some] = inverse
        return carry

    lax.fori_loop(0, rows // 16, norm_rows, 0)
    for head in range(max(heads - 2, 0), heads):
        keep(head).wait()
    for copy in started:
        copy.wait_send()


def attention_forward(
    narrow_count,
    triple,
    heads_shift,
    cosine,
    signed_sine,
    first_query,
    last_query,
    layer_input,
    merge_full,
    merge_shift,
    gain,
    shift,
):
    bucket, columns = triple.shape
    rows, width = layer_input.shape
    own_cols = columns // 3
    heads = own_cols // HDIM
    anywhere = pl.BlockSpec(memory_space=pl.ANY)
    vmem = pl.BlockSpec(memory_space=pltpu.VMEM)
    dma = pltpu.SemaphoreType.DMA

    def low_shape(*shape):
        return jax.ShapeDtypeStruct(shape, jnp.bfloat16)

    def wide_shape(*shape):
        return jax.ShapeDtypeStruct(shape, jnp.float32)

    return pl.pallas_call(
        functools.partial(attention_forward_kernel, narrow_count),
        out_shape=(
            low_shape(bucket, own_cols),
            low_shape(bucket, own_cols),
            low_shape(bucket, own_cols),
            low_shape(heads, bucket, bucket),
            low_shape(rows, width),
            wide_shape(rows, width),
            low_shape(rows, width),
            wide_shape(rows, width),
            wide_shape(rows, 1),
        ),
        in_specs=[vmem] * 7 + [anywhere] + [vmem] * 3,
        out_specs=(vmem, vmem, vmem, anywhere) + (vmem,) * 5,
        scratch_shapes=[
            pltpu.VMEM((width, width), jnp.bfloat16),
            pltpu.VMEM((2, bucket, bucket), jnp.bfloat16),
            pltpu.VMEM((HDIM, bucket), jnp.bfloat16),
            pltpu.VMEM((narrow_count, rows, own_cols), jnp.bfloat16),
            pltpu.VMEM((rows, width), jnp.bfloat16),
            dma((narrow_count - 1, heads)),
            dma((narrow_count, heads)),
            dma((4,)),
            pltpu.VMEM((bucket, rows), jnp.float32),
        ],
        compiler_params=pltpu.CompilerParams(
            collective_id=6, has_side_effects=True, vmem_limit_bytes=kernel_memory
        ),
        cost_estimate=pl.CostEstimate(
            flops=60 * 10**9, bytes_accessed=200 * 2**20, transcendentals=0
        ),
        name="attention_forward",
    )(
        triple,
        heads_shift,
        cosine,
        signed_sine,
        first_query,
        last_query,
        layer_input,
        merge_full,
        merge_shift,
        gain,
        shift,
    )


def shards(
    layer_input,
    heads_weight,
    heads_bias,
    merge_weight,
    merge_bias,
    norm_gains,
    norm_shifts,
    expand_weight,
    expand_bias,
    reduce_weight,
    reduce_bias,
    joined,
    prefix,
    cotangent,
):
    tok_rows, model_width = layer_input.shape
    wide_count = lax.axis_size("wide")
    narrow_count = lax.axis_size("narrow")
    count = wide_count * narrow_count
    bucket_len = tok_rows * narrow_count
    own_heads = HEADS // narrow_count
    own_cols = own_heads * HDIM
    share = expand_weight.shape[2]
    narrow_index = lax.axis_index("narrow")
    smalls = (heads_bias, merge_bias, norm_gains, norm_shifts, expand_bias, reduce_bias)
    (
        rows_input,
        heads_mat,
        merge_full,
        small_all,
        triple,
        cosine,
        signed_sine,
        first_query,
        last_query,
    ) = gather_front(
        wide_count,
        narrow_count,
        layer_input,
        heads_weight,
        merge_weight,
        pack_small(smalls),
        jnp.concatenate([joined, prefix[0]]),
        jnp.asarray(rotary_speeds(HDIM)),
    )
    rows_input = rows_input.reshape(bucket_len, model_width)
    merge_full = merge_full.reshape(model_width, model_width)
    heads_mat = heads_mat.reshape(model_width, 3 * own_cols)
    heads_shift, merge_shift, gains, shifts, expand_shift, reduce_shift = unpack_small(
        small_all, smalls
    )
    own_shift = lax.dynamic_index_in_dim(
        heads_shift.reshape(3, narrow_count, own_cols), narrow_index, 1, keepdims=False
    ).reshape(1, -1)
    (
        queries,
        keys,
        values,
        probs_low,
        mixed,
        hidden,
        hidden_low,
        normed_one,
        inv_one,
    ) = attention_forward(
        narrow_count,
        triple,
        own_shift,
        cosine,
        signed_sine,
        first_query,
        last_query,
        layer_input,
        merge_full,
        merge_shift.reshape(1, -1),
        gains[0].reshape(1, -1),
        shifts[0].reshape(1, -1),
    )

    tile_rows = -share % 16
    padded = -(-share // 256) * 256
    expand_low = jnp.pad(expand_weight.transpose(1, 2, 0), ((0, 0), (0, tile_rows), (0, 0)))
    expand_full = lax.all_gather(expand_low, "narrow", axis=2, tiled=True)
    reduce_low = jnp.pad(reduce_weight, ((0, tile_rows), (0, 0)))
    (
        reduce_full,
        rows_all,
        active,
        slope,
        gelu,
        layer_output,
        sum_two_grad,
        feed_grad,
        row_sums,
    ) = geglu_forward(
        wide_count,
        narrow_count,
        hidden_low,
        expand_full,
        reduce_low,
        jnp.pad(expand_shift, ((0, 0), (0, padded - share))),
        hidden,
        cotangent,
        reduce_shift.reshape(1, -1),
        gains[1].reshape(1, -1),
        shifts[1].reshape(1, -1),
    )
    reduce_weight_gradient, expand_part, hidden_part, unit_sums = geglu_backward(
        wide_count,
        narrow_count,
        feed_grad,
        expand_full,
        reduce_full,
        slope,
        gelu,
        active,
        rows_all,
    )
    expand_weight_gradient = (
        lax.psum_scatter(expand_part, "narrow", scatter_dimension=2, tiled=True)[:, :share]
        .astype(jnp.float32)
        .transpose(2, 0, 1)
    )
    (
        triple_grad,
        merge_weight_gradient,
        heads_sums,
        merge_sums,
        sum_one_grad,
        norm_one_sums,
    ) = attention_backward(
        wide_count,
        narrow_count,
        sum_two_grad,
        hidden_part,
        normed_one,
        inv_one,
        gains[0].reshape(1, -1),
        merge_full,
        mixed,
        queries,
        keys,
        values,
        probs_low,
        cosine,
        signed_sine,
    )

    mine_narrow = (jnp.arange(narrow_count) == narrow_index).astype(jnp.float32)
    mine_wide = (jnp.arange(wide_count) == lax.axis_index("wide")).astype(jnp.float32)
    heads_sums = heads_sums.reshape(3, 1, own_cols)
    heads_sums = (heads_sums * mine_narrow[None, :, None]).reshape(count, -1)
    merge_sums = merge_sums.reshape(count, -1)
    norm_sums = (
        jnp.stack([norm_one_sums[0], row_sums[0], norm_one_sums[1], row_sums[1]])
        .reshape(4, count, -1)
        .transpose(1, 0, 2)
        .reshape(count, -1)
    )
    expand_sums = unit_sums[:, :share]
    expand_sums = (
        expand_sums.reshape(2, narrow_count, -1).transpose(1, 0, 2).reshape(1, narrow_count, -1)
        * mine_wide[:, None, None]
    ).reshape(count, -1)
    reduce_sums = row_sums[2].reshape(1, narrow_count, -1)
    reduce_sums = jnp.broadcast_to(
        reduce_sums, (wide_count, narrow_count, reduce_sums.shape[2])
    ).reshape(count, -1)
    pieces = (heads_sums, merge_sums, norm_sums, expand_sums, reduce_sums)
    packed = jnp.concatenate(pieces, axis=1)
    packed = jnp.pad(packed, ((0, 0), (0, -packed.shape[1] % 1024)))
    input_part, heads_weight_gradient, summed = input_backward(
        wide_count,
        narrow_count,
        rows_input,
        triple_grad,
        heads_mat,
        packed.reshape(wide_count, narrow_count, -1, 128),
    )
    input_gradient = residual_scale * sum_one_grad + input_part
    summed = summed.reshape(-1)
    ends = []
    start = 0
    for piece in pieces:
        ends.append(summed[start : start + piece.shape[1]])
        start += piece.shape[1]
    norm_ends = ends[2].reshape(4, -1)
    return (
        layer_output,
        input_gradient,
        heads_weight_gradient,
        ends[0],
        merge_weight_gradient,
        ends[1],
        norm_ends[:2],
        norm_ends[2:],
        expand_weight_gradient,
        ends[3].reshape(2, -1),
        reduce_weight_gradient[:share],
        ends[4],
    )


def solution(mesh):
    return jax.shard_map(
        shards,
        mesh=mesh,
        in_specs=(
            P(("wide", "narrow"), None),
            P(("wide", "narrow"), None),
            P(("wide", "narrow")),
            P(("wide", "narrow"), None),
            P(("wide", "narrow")),
            P(None, ("wide", "narrow")),
            P(None, ("wide", "narrow")),
            P("narrow", None, "wide"),
            P(None, ("wide", "narrow")),
            P("wide", "narrow"),
            P("narrow"),
            P("wide"),
            P("wide", None),
            P(("wide", "narrow"), None),
        ),
        out_specs=(
            P(("wide", "narrow"), None),
            P(("wide", "narrow"), None),
            P(("wide", "narrow"), None),
            P(("wide", "narrow")),
            P(("wide", "narrow"), None),
            P(("wide", "narrow")),
            P(None, ("wide", "narrow")),
            P(None, ("wide", "narrow")),
            P("narrow", None, "wide"),
            P(None, ("wide", "narrow")),
            P("wide", "narrow"),
            P("narrow"),
        ),
        check_vma=False,
    )
```

```python
import functools
import math

import jax
import jax.numpy as jnp
import numpy as np
from jax import lax
from jax.experimental import pallas as pl
from jax.experimental.pallas import tpu as pltpu
from jax.sharding import PartitionSpec as P

HEADS = 16
HDIM = 128


residual_scale = 48.0**0.5
norm_eps = 1e-05
masked_value = -1e30
kernel_memory = 60 * 2**20


def rotary_speeds(head_size):
    index = np.arange(head_size) % (head_size // 2)
    return (10000.0 ** (-2.0 * index / head_size)).astype(np.float32)[None]


def normalize(values, gain, shift):
    centre = jnp.mean(values, axis=-1, keepdims=True)
    centred = values - centre
    variance = jnp.mean(centred * centred, axis=-1, keepdims=True)
    inv_std = lax.rsqrt(variance + norm_eps)
    normed = centred * inv_std
    return (normed * gain + shift, normed, inv_std)


def normalize_back(upstream, normed, inv_std, gain):
    scaled = upstream * gain
    return inv_std * (
        scaled
        - jnp.mean(scaled, axis=-1, keepdims=True)
        - normed * jnp.mean(scaled * normed, axis=-1, keepdims=True)
    )


def dot(left, right, dims):
    return lax.dot_general(left, right, (dims, ((), ())), preferred_element_type=jnp.float32)


def low(values):
    return values.astype(jnp.bfloat16)


def pack_small(parts):
    packed = jnp.concatenate([part.reshape(-1) for part in parts])
    return jnp.pad(packed, (0, -packed.size % 2048)).reshape(-1, 128)


def unpack_small(everyone, parts):
    wide_count, narrow_count = everyone.shape[:2]
    everyone = everyone.reshape(wide_count, narrow_count, -1).astype(jnp.float32)
    pieces = []
    start = 0
    for part in parts:
        pieces.append(everyone[:, :, start : start + part.size])
        start += part.size

    def pairs(piece):
        piece = piece.reshape(-1, 2, piece.shape[-1] // 2)
        return piece.transpose(1, 0, 2).reshape(2, -1)

    own_expand = lax.dynamic_index_in_dim(
        pieces[4], lax.axis_index("wide"), 0, keepdims=False
    )
    return (
        pieces[0].reshape(-1),
        pieces[1].reshape(-1),
        pairs(pieces[2]),
        pairs(pieces[3]),
        pairs(own_expand),
        pieces[5][0].reshape(-1),
    )


def ring_place(wide_count):
    ring = wide_count // 2
    mine = lax.axis_index("wide")
    chip = mine // 2
    core = mine % 2
    position = 2 * (chip // 2) + (chip % 2 + chip // 2) % 2
    return ring, position, core


def chip_at(position, ring):
    position = (position + 2 * ring) % ring
    return 2 * (position // 2) + (position + position // 2) % 2


class PlaneExchange:
    def __init__(self, wide_count, own, blocks, parts, from_mate, incoming, sems, cols=None):
        self.ring, self.position, self.core = ring_place(wide_count)
        self.own, self.blocks, self.parts = own, blocks, parts
        self.from_mate, self.incoming = from_mate, incoming
        (
            self.gather_send,
            self.gather_recv,
            self.mate_send,
            self.mate_recv,
            self.sum_send,
            self.sum_recv,
            self.own_sem,
        ) = sems
        self.half = parts.shape[1] // 2
        self.cols = slice(None) if cols is None else cols
        self.far = self.ring // 2
        self.started = []

    def device(self, offset, mate=False):
        core = 1 - self.core if mate else self.core
        return {"wide": 2 * chip_at(self.position + offset, self.ring) + core}

    def slot(self, offset, mate=False):
        core = 1 - self.core if mate else self.core
        return 2 * chip_at(self.position + offset, self.ring) + core

    def rows(self, part):
        return pl.ds(part * self.half, self.half)

    def greet(self):
        barrier = pltpu.get_barrier_semaphore()
        for where in (self.device(-1), self.device(1), self.device(0, True)):
            pl.semaphore_signal(
                barrier, inc=1, device_id=where, device_id_type=pl.DeviceIdType.MESH
            )
        pl.semaphore_wait(barrier, 3)

    def start(self, source, target, send_sem, recv_sem, where):
        copy = pltpu.make_async_remote_copy(
            src_ref=source,
            dst_ref=target,
            send_sem=send_sem,
            recv_sem=recv_sem,
            device_id=where,
            device_id_type=pl.DeviceIdType.MESH,
        )
        copy.start()
        self.started.append(copy)

    def pass_on(self, lane, slot, part, where, source=None):
        target = self.blocks.at[slot, self.rows(part)]
        self.start(
            target if source is None else source,
            target,
            self.gather_send.at[lane, slot, part],
            self.gather_recv.at[slot, part],
            where,
        )

    def arrived(self, slot, part):
        target = self.blocks.at[slot, self.rows(part)]
        pltpu.make_async_remote_copy(
            src_ref=target,
            dst_ref=target,
            send_sem=self.gather_send.at[0, slot, part],
            recv_sem=self.gather_recv.at[slot, part],
            device_id=self.device(1),
            device_id_type=pl.DeviceIdType.MESH,
        ).wait_recv()

    def send_own(self):
        slot = self.slot(0)
        keep = None
        own = self.blocks.at[slot]
        if self.own is not None:
            own = self.own
            keep = pltpu.make_async_copy(own, self.blocks.at[slot], self.own_sem)
            keep.start()
        first, second = own.at[self.rows(0)], own.at[self.rows(1)]
        self.pass_on(0, slot, 0, self.device(1), first)
        self.pass_on(1, slot, 1, self.device(-1), second)
        self.pass_on(2, slot, 0, self.device(0, True), first)
        self.pass_on(2, slot, 1, self.device(0, True), second)
        self.pass_on(0, slot, 1, self.device(1), second)
        self.pass_on(1, slot, 0, self.device(-1), first)
        return keep

    def receive(self, distance):
        mate = self.device(0, True)
        left, right = self.slot(-distance), self.slot(distance)
        if distance == self.far:
            for part in range(2):
                self.arrived(left, part)
                self.pass_on(2, left, part, mate)
            return
        further = distance < self.far - 1
        self.arrived(left, 0)
        self.pass_on(0, left, 0, self.device(1))
        self.pass_on(2, left, 0, mate)
        self.arrived(right, 1)
        self.pass_on(1, right, 1, self.device(-1))
        self.pass_on(2, right, 1, mate)
        self.arrived(left, 1)
        if further:
            self.pass_on(0, left, 1, self.device(1))
        self.pass_on(2, left, 1, mate)
        self.arrived(right, 0)
        if further:
            self.pass_on(1, right, 0, self.device(-1))
        self.pass_on(2, right, 0, mate)

    def receive_mate(self, offset):
        for part in range(2):
            self.arrived(self.slot(offset, True), part)

    def share(self, offset):
        chip = chip_at(self.position + offset, self.ring)
        self.start(
            self.parts.at[self.slot(offset, True), :, self.cols],
            self.from_mate.at[chip, :, self.cols],
            self.mate_send.at[chip],
            self.mate_recv.at[chip],
            self.device(0, True),
        )

    def shared(self, offset):
        chip = chip_at(self.position + offset, self.ring)
        pltpu.make_async_remote_copy(
            src_ref=self.parts.at[self.slot(offset), :, self.cols],
            dst_ref=self.from_mate.at[chip, :, self.cols],
            send_sem=self.mate_send.at[chip],
            recv_sem=self.mate_recv.at[chip],
            device_id=self.device(0, True),
            device_id_type=pl.DeviceIdType.MESH,
        ).wait_recv()

    def chip_sum(self, offset, rows):
        chip = chip_at(self.position + offset, self.ring)
        return self.parts[self.slot(offset), rows, self.cols].astype(
            jnp.float32
        ) + self.from_mate[chip, rows, self.cols].astype(jnp.float32)

    def send_sum(self, way, distance, part):
        offset = distance if way == 0 else -distance
        begins = self.far if part == way else self.far - 1
        slot = self.slot(offset)
        if distance < begins:
            self.sum_arrived(way, distance, part)

        def chunk(i, carry):
            here = pl.ds(pl.multiple_of(i * 16, 16), 16)
            there = pl.ds(pl.multiple_of(part * self.half + i * 16, 16), 16)
            total = self.chip_sum(offset, there)
            if distance < begins:
                total += self.incoming[way, distance, part, here, self.cols].astype(jnp.float32)
            self.parts[slot, there, self.cols] = total.astype(jnp.bfloat16)
            return carry

        lax.fori_loop(0, self.half // 16, chunk, 0)
        self.start(
            self.parts.at[slot, self.rows(part), self.cols],
            self.incoming.at[way, distance - 1, part, :, self.cols],
            self.sum_send.at[way, distance - 1, part],
            self.sum_recv.at[way, distance - 1, part],
            self.device(1 if way == 0 else -1),
        )

    def sum_arrived(self, way, distance, part):
        target = self.incoming.at[way, distance, part, :, self.cols]
        pltpu.make_async_remote_copy(
            src_ref=target,
            dst_ref=target,
            send_sem=self.sum_send.at[way, distance, part],
            recv_sem=self.sum_recv.at[way, distance, part],
            device_id=self.device(1),
            device_id_type=pl.DeviceIdType.MESH,
        ).wait_recv()

    def run(self, first, second, before, after_far):
        def compute(chip):
            first(chip)
            second(chip)

        keep = self.send_own()
        keep.wait()
        self.receive_mate(0)
        compute(chip_at(self.position, self.ring))
        self.share(0)
        for distance in range(1, self.far):
            self.receive(distance)
            for offset in (-distance, distance):
                self.receive_mate(offset)
                compute(chip_at(self.position + offset, self.ring))
                self.share(offset)
            if distance == self.far - 1:
                self.first_sums()
        self.receive(self.far)
        self.receive_mate(self.far)
        farthest = chip_at(self.position + self.far, self.ring)
        first(farthest)
        before()
        second(farthest)
        self.share(self.far)
        self.far_sums()
        after_far()
        self.last_sums()

    def run_gather(self, compute, between):
        keep = self.send_own()
        keep.wait()
        self.receive_mate(0)
        compute(chip_at(self.position, self.ring))
        done = 1
        for distance in range(1, self.far):
            self.receive(distance)
            between(done)
            done += 1
            for offset in (-distance, distance):
                self.receive_mate(offset)
                compute(chip_at(self.position + offset, self.ring))
        self.receive(self.far)
        between(done)
        done += 1
        self.receive_mate(self.far)
        compute(chip_at(self.position + self.far, self.ring))
        return done

    def start_sums(self, compute):
        compute(chip_at(self.position + self.far, self.ring))
        self.share(self.far)
        for distance in range(self.far - 1, 0, -1):
            for offset in (-distance, distance):
                compute(chip_at(self.position + offset, self.ring))
                self.share(offset)
            if distance == self.far - 1:
                self.far_sums()
                self.first_sums()
        compute(chip_at(self.position, self.ring))
        self.share(0)

    def first_sums(self):
        distance = self.far - 1
        self.shared(distance)
        self.send_sum(0, distance, 1)
        self.shared(-distance)
        self.send_sum(1, distance, 0)

    def far_sums(self):
        self.shared(self.far)
        self.send_sum(0, self.far, 0)
        self.send_sum(1, self.far, 1)

    def last_sums(self):
        for distance in range(self.far - 1, 0, -1):
            if distance < self.far - 1:
                self.shared(distance)
                self.shared(-distance)
            self.send_sum(0, distance, 0)
            self.send_sum(1, distance, 1)
            if distance < self.far - 1:
                self.send_sum(0, distance, 1)
                self.send_sum(1, distance, 0)

    def finish(self, result):
        self.shared(0)
        for part in range(2):
            for way in range(2):
                self.sum_arrived(way, 0, part)

            def chunk(i, carry):
                here = pl.ds(pl.multiple_of(i * 16, 16), 16)
                there = pl.ds(pl.multiple_of(part * self.half + i * 16, 16), 16)
                total = self.chip_sum(0, there)
                for way in range(2):
                    total += self.incoming[way, 0, part, here, self.cols].astype(jnp.float32)
                result[there, self.cols] = total.astype(result.dtype)
                return carry

            lax.fori_loop(0, self.half // 16, chunk, 0)

    def drain(self):
        for copy in self.started:
            copy.wait_send()


def sum_scratch(wide_count, rows, width):
    ring = wide_count // 2
    far = ring // 2
    dma = pltpu.SemaphoreType.DMA
    return [
        pltpu.VMEM((wide_count, rows, width), jnp.bfloat16),
        pltpu.VMEM((ring, rows, width), jnp.bfloat16),
        pltpu.VMEM((2, far, 2, rows // 2, width), jnp.bfloat16),
        dma((ring,)),
        dma((ring,)),
        dma((2, far, 2)),
        dma((2, far, 2)),
    ]


def exchange_scratch(wide_count, rows, width):
    dma = pltpu.SemaphoreType.DMA
    return [
        pltpu.VMEM((wide_count, rows, width), jnp.bfloat16),
        dma((3, wide_count, 2)),
        dma((wide_count, 2)),
        dma(()),
    ] + sum_scratch(wide_count, rows, width)


def load_padded(source, target, sem):
    filled = source.shape[0]
    copy = pltpu.make_async_copy(source, target.at[pl.ds(0, filled)], sem)
    copy.start()
    if filled < target.shape[0]:
        target[pl.ds(filled, target.shape[0] - filled)] = jnp.zeros(
            (target.shape[0] - filled, target.shape[1]), target.dtype
        )
    return copy


def pair_rows(ref, chip):
    block = ref[pl.ds(2 * chip, 2)]
    return block.reshape(2 * block.shape[1], block.shape[2])


def set_pair(ref, chip, cols, value):
    rows = ref.shape[1]
    ref[2 * chip, :, cols] = value[:rows].astype(ref.dtype)
    ref[2 * chip + 1, :, cols] = value[rows:].astype(ref.dtype)


def tiles(count, tile, body, start=0):
    def step(i, carry):
        body(pl.ds(pl.multiple_of(start + i * tile, tile), tile))
        return carry

    lax.fori_loop(0, count // tile, step, 0)


class LineExchange:
    def __init__(self, narrow_count):
        self.count = narrow_count
        self.mine = lax.axis_index("narrow")
        self.started = []

    def peer(self, offset):
        return (self.mine + offset) % self.count

    def greet(self, extra=0):
        barrier = pltpu.get_barrier_semaphore()
        for offset in range(1, self.count):
            pl.semaphore_signal(
                barrier,
                inc=1,
                device_id={"narrow": self.peer(offset)},
                device_id_type=pl.DeviceIdType.MESH,
            )
        pl.semaphore_wait(barrier, self.count - 1 + extra)

    def copy(self, source, target, send_sem, recv_sem, where):
        return pltpu.make_async_remote_copy(
            src_ref=source,
            dst_ref=target,
            send_sem=send_sem,
            recv_sem=recv_sem,
            device_id={"narrow": where},
            device_id_type=pl.DeviceIdType.MESH,
        )

    def send(self, offset, source, landing, send_sems, recv_sems):
        peer = self.peer(offset)
        copy = self.copy(
            source, landing.at[self.mine], send_sems.at[offset - 1], recv_sems.at[self.mine], peer
        )
        copy.start()
        self.started.append(copy)

    def arrived(self, offset, landing, send_sems, recv_sems):
        peer = self.peer(offset)
        self.copy(
            landing.at[peer], landing.at[peer], send_sems.at[offset - 1], recv_sems.at[peer], peer
        ).wait_recv()

    def drain(self):
        for copy in self.started:
            copy.wait_send()


class LineSum:
    def __init__(self, line, view, landing, send_sems, recv_sems):
        self.line, self.view, self.landing = line, view, landing
        self.send_sems, self.recv_sems = send_sems, recv_sems
        self.last = line.count - 1

    def reaches(self, way, offset):
        here = self.line.mine
        return here + offset <= self.last if way == 0 else here - offset >= 0

    def follows(self, way):
        here = self.line.mine
        return here > 0 if way == 0 else here < self.last

    def target(self, way, offset):
        return self.line.mine + offset if way == 0 else self.line.mine - offset

    def copy(self, way, offset):
        return self.line.copy(
            self.view(self.target(way, offset)),
            self.landing.at[way, offset - 1],
            self.send_sems.at[way, offset - 1],
            self.recv_sems.at[way, offset - 1],
            self.line.mine + 1 if way == 0 else self.line.mine - 1,
        )

    def arrived(self, way, offset):
        landing = self.landing.at[way, offset]
        self.line.copy(
            landing,
            landing,
            self.send_sems.at[way, offset],
            self.recv_sems.at[way, offset],
            self.line.mine,
        ).wait_recv()

    def add(self, way, offset):
        held = self.view(self.target(way, offset))

        def chunk(i, carry):
            some = pl.ds(pl.multiple_of(i * 16, 16), 16)
            held[some] = (
                held[some].astype(jnp.float32)
                + self.landing[way, offset, some].astype(jnp.float32)
            ).astype(jnp.bfloat16)
            return carry

        lax.fori_loop(0, self.landing.shape[2] // 16, chunk, 0)

    def begin(self, offset):
        for way in range(2):

            @pl.when(self.reaches(way, offset) & jnp.logical_not(self.follows(way)))
            def _():
                self.copy(way, offset).start()

    def step(self, offset):
        for way in range(2):

            @pl.when(self.reaches(way, offset) & self.follows(way))
            def _():
                self.arrived(way, offset)
                self.add(way, offset)
                self.copy(way, offset).start()

    def finish(self, result):
        held = self.view(self.line.mine)
        count = self.landing.shape[2] // 16

        def begin(i, carry):
            some = pl.ds(pl.multiple_of(i * 16, 16), 16)
            result[some] = held[some].astype(result.dtype)
            return carry

        lax.fori_loop(0, count, begin, 0)
        for way in range(2):

            @pl.when(self.follows(way))
            def _():
                self.arrived(way, 0)

                def chunk(i, carry):
                    some = pl.ds(pl.multiple_of(i * 16, 16), 16)
                    result[some] += self.landing[way, 0, some].astype(result.dtype)
                    return carry

                lax.fori_loop(0, count, chunk, 0)

    def drain(self):
        for offset in range(1, self.last + 1):
            for way in range(2):

                @pl.when(self.reaches(way, offset))
                def _():
                    self.copy(way, offset).wait_send()


class LineGather:
    def __init__(self, line, view, send_sems, recv_sems):
        self.line, self.view = line, view
        self.send_sems, self.recv_sems = send_sems, recv_sems
        self.last = line.count - 1

    def copy(self, way, block):
        target = self.view(block)
        here = self.line.mine
        return self.line.copy(
            target,
            target,
            self.send_sems.at[way, block],
            self.recv_sems.at[block],
            here + 1 if way == 0 else here - 1,
        )

    def goes(self, way):
        return self.line.mine < self.last if way == 0 else self.line.mine > 0

    def has(self, way, step):
        here = self.line.mine
        return here - step >= 0 if way == 0 else here + step <= self.last

    def block(self, way, step):
        return self.line.mine - step if way == 0 else self.line.mine + step

    def send_own(self):
        for way in range(2):

            @pl.when(self.goes(way))
            def _():
                self.copy(way, self.line.mine).start()

    def step(self, step):
        for way in range(2):

            @pl.when(self.has(way, step))
            def _():
                self.copy(way, self.block(way, step)).wait_recv()

                @pl.when(self.goes(way))
                def _():
                    self.copy(way, self.block(way, step)).start()

    def each(self, step, body):
        for way in range(2):

            @pl.when(self.has(way, step))
            def _():
                body(self.block(way, step))

    def drain(self):
        for way in range(2):
            for step in range(self.last + 1):

                @pl.when(self.has(way, step) & self.goes(way))
                def _():
                    self.copy(way, self.block(way, step)).wait_send()


def greet_plane(plane):
    barrier = pltpu.get_barrier_semaphore()
    for where in (plane.device(-1), plane.device(1), plane.device(0, True)):
        pl.semaphore_signal(barrier, inc=1, device_id=where, device_id_type=pl.DeviceIdType.MESH)


def geglu_forward_kernel(
    wide_count,
    narrow_count,
    own,
    expand,
    reduce,
    shift,
    hidden,
    cotangent,
    reduce_shift,
    gain,
    norm_shift,
    reduce_out,
    rows_all,
    active_out,
    slope_out,
    gelu_out,
    layer_output,
    sum_grad,
    feed_grad,
    row_sums,
    feed,
    blocks,
    gather_send,
    gather_recv,
    own_sem,
    parts,
    from_mate,
    incoming,
    mate_send,
    mate_recv,
    sum_send,
    sum_recv,
    expand_mat,
    reduce_mat,
    active,
    slope,
    gelu,
    load_sems,
    keep_sems,
    reduce_send,
    reduce_recv,
    late_mate_send,
    late_mate_recv,
    late_sum_send,
    late_sum_recv,
):
    sems = (gather_send, gather_recv, mate_send, mate_recv, sum_send, sum_recv, own_sem)
    late_sems = (None, None, late_mate_send, late_mate_recv, late_sum_send, late_sum_recv, None)
    line = LineExchange(narrow_count)
    filled, cols = reduce.shape
    width = own.shape[1]
    upper = (2 * line.mine) // narrow_count
    late = pl.multiple_of((1 - upper) * (width - cols), cols)
    early = pl.multiple_of(upper * cols, cols)
    plane = PlaneExchange(
        wide_count, own, blocks, parts, from_mate, incoming, sems, pl.ds(early, width - cols)
    )
    late_plane = PlaneExchange(
        wide_count, None, None, parts, from_mate, incoming, late_sems, pl.ds(late, cols)
    )
    loads = [
        load_padded(expand.at[0], expand_mat.at[0], load_sems.at[0]),
        load_padded(expand.at[1], expand_mat.at[1], load_sems.at[1]),
    ]

    def reduce_cols(block):
        return reduce_mat.at[
            pl.ds(0, filled), pl.ds(pl.multiple_of(block * cols, cols), cols)
        ]

    line_reduce = LineGather(line, reduce_cols, reduce_send, reduce_recv)
    own_reduce = pltpu.make_async_copy(reduce, reduce_cols(line.mine), load_sems.at[2])
    own_reduce.start()
    if filled < reduce_mat.shape[0]:
        reduce_mat[filled:] = jnp.zeros(
            (reduce_mat.shape[0] - filled, reduce_mat.shape[1]), reduce_mat.dtype
        )
    greet_plane(plane)
    line.greet(3)
    own_reduce.wait()
    line_reduce.send_own()
    kept = []
    waiting = list(loads)

    def compute(chip):
        while waiting:
            waiting.pop().wait()

        def units(cols):
            rows = pair_rows(blocks, chip)
            gate = dot(rows, expand_mat[0, cols], ((1,), (1,))) + shift[0:1, cols]
            upper = dot(rows, expand_mat[1, cols], ((1,), (1,))) + shift[1:2, cols]
            factor = math.sqrt(2 / math.pi)
            square = gate * gate
            bend = jnp.tanh(factor * gate * (1 + 0.044715 * square))
            value = 0.5 * gate * (1 + bend)
            pull = 0.5 * (1 + bend) + 0.5 * gate * (1 - bend * bend) * factor * (
                1 + 3 * 0.044715 * square
            )
            set_pair(active, chip, cols, value * upper)
            set_pair(slope, chip, cols, pull * upper)
            set_pair(gelu, chip, cols, value)

        tiles(active.shape[2], 256, units)

        pair = pl.ds(2 * chip, 2)
        for index, (source, target) in enumerate(
            ((active, active_out), (slope, slope_out), (gelu, gelu_out), (blocks, rows_all))
        ):
            copy = pltpu.make_async_copy(
                source.at[pair], target.at[pair], keep_sems.at[chip, index]
            )
            copy.start()
            kept.append(copy)

    def compute_sums(start, count):
        def compute(chip):
            def outputs(some):
                part = dot(pair_rows(active, chip), reduce_mat[:, some], ((1,), (0,)))
                set_pair(parts, chip, some, part)

            tiles(count, 256, outputs, start)

        return compute

    def between(index):
        if index < narrow_count:
            line_reduce.step(index)

    done = plane.run_gather(compute, between)
    for step in range(done, narrow_count - 1):
        line_reduce.step(step)
    plane.start_sums(compute_sums(early, width - cols))
    line_reduce.step(narrow_count - 1)
    keep_reduce = pltpu.make_async_copy(
        reduce_mat.at[pl.ds(0, filled)], reduce_out, load_sems.at[3]
    )
    keep_reduce.start()
    late_plane.start_sums(compute_sums(late, cols))
    plane.last_sums()
    late_plane.last_sums()
    plane.finish(feed)
    late_plane.finish(feed)

    row_sums[...] = jnp.zeros_like(row_sums)

    def norm_rows(i, carry):
        some = pl.ds(pl.multiple_of(i * 16, 16), 16)
        result, normed, inverse = normalize(
            residual_scale * hidden[some] + feed[some] + reduce_shift[...],
            gain[...],
            norm_shift[...],
        )
        layer_output[some] = result.astype(jnp.bfloat16)
        upstream = cotangent[some].astype(jnp.float32)
        total = normalize_back(upstream, normed, inverse, gain[...])
        sum_grad[some] = total
        feed_grad[some] = total.astype(jnp.bfloat16)
        row_sums[0:1] += jnp.sum(upstream * normed, axis=0, keepdims=True)
        row_sums[1:2] += jnp.sum(upstream, axis=0, keepdims=True)
        row_sums[2:3] += jnp.sum(total, axis=0, keepdims=True)
        return carry

    lax.fori_loop(0, own.shape[0] // 16, norm_rows, 0)
    plane.drain()
    late_plane.drain()
    keep_reduce.wait()
    line_reduce.drain()
    for copy in kept:
        copy.wait()


def geglu_forward(
    wide_count,
    narrow_count,
    hidden_low,
    expand,
    reduce_weight,
    shift,
    hidden,
    cotangent,
    reduce_shift,
    gain,
    norm_shift,
):
    rows, width = hidden_low.shape
    padded = shift.shape[1]
    anywhere = pl.BlockSpec(memory_space=pl.ANY)
    vmem = pl.BlockSpec(memory_space=pltpu.VMEM)
    kept = jax.ShapeDtypeStruct((wide_count, rows, padded), jnp.bfloat16)
    scratch = [pltpu.VMEM((rows, width), jnp.float32)]
    scratch += exchange_scratch(wide_count, rows, width) + [
        pltpu.VMEM((2, padded, width), jnp.bfloat16),
        pltpu.VMEM((padded, width), jnp.bfloat16),
        pltpu.VMEM((wide_count, rows, padded), jnp.bfloat16),
        pltpu.VMEM((wide_count, rows, padded), jnp.bfloat16),
        pltpu.VMEM((wide_count, rows, padded), jnp.bfloat16),
        pltpu.SemaphoreType.DMA((4,)),
        pltpu.SemaphoreType.DMA((wide_count // 2, 4)),
        pltpu.SemaphoreType.DMA((2, narrow_count)),
        pltpu.SemaphoreType.DMA((narrow_count,)),
    ] + sum_scratch(wide_count, rows, width)[3:]
    return pl.pallas_call(
        functools.partial(geglu_forward_kernel, wide_count, narrow_count),
        out_shape=(
            jax.ShapeDtypeStruct((reduce_weight.shape[0], width), jnp.bfloat16),
            jax.ShapeDtypeStruct((wide_count, rows, width), jnp.bfloat16),
            kept,
            kept,
            kept,
            jax.ShapeDtypeStruct((rows, width), jnp.bfloat16),
            jax.ShapeDtypeStruct((rows, width), jnp.float32),
            jax.ShapeDtypeStruct((rows, width), jnp.bfloat16),
            jax.ShapeDtypeStruct((3, width), jnp.float32),
        ),
        in_specs=[anywhere] * 3 + [vmem] * 6,
        out_specs=(anywhere,) * 5 + (vmem,) * 4,
        scratch_shapes=scratch,
        compiler_params=pltpu.CompilerParams(
            collective_id=1, has_side_effects=True, vmem_limit_bytes=kernel_memory
        ),
        cost_estimate=pl.CostEstimate(
            flops=6 * wide_count * rows * padded * width, bytes_accessed=200 * 2**20, transcendentals=0
        ),
        name="geglu_forward",
    )(
        hidden_low,
        expand,
        reduce_weight,
        shift,
        hidden,
        cotangent,
        reduce_shift,
        gain,
        norm_shift,
    )


def geglu_backward_kernel(
    wide_count,
    narrow_count,
    own,
    expand,
    reduce,
    slope_in,
    gelu_in,
    active_in,
    rows_in,
    reduce_grad,
    expand_part,
    hidden_grad,
    unit_sums,
    blocks,
    gather_send,
    gather_recv,
    own_sem,
    parts,
    from_mate,
    incoming,
    mate_send,
    mate_recv,
    sum_send,
    sum_recv,
    expand_mat,
    reduce_mat,
    slope,
    gelu,
    active,
    rows_all,
    staged,
    load_sems,
    keep_sems,
    line_in,
    line_send,
    line_recv,
):
    sems = (gather_send, gather_recv, mate_send, mate_recv, sum_send, sum_recv, own_sem)
    plane = PlaneExchange(wide_count, own, blocks, parts, from_mate, incoming, sems)
    loads = [
        load_padded(expand.at[0], expand_mat.at[0], load_sems.at[0]),
        load_padded(expand.at[1], expand_mat.at[1], load_sems.at[1]),
        load_padded(reduce, reduce_mat, load_sems.at[2]),
        pltpu.make_async_copy(slope_in, slope, load_sems.at[3]),
        pltpu.make_async_copy(gelu_in, gelu, load_sems.at[4]),
    ]
    late_loads = [
        pltpu.make_async_copy(active_in, active, load_sems.at[5]),
        pltpu.make_async_copy(rows_in, rows_all, load_sems.at[6]),
    ]
    for copy in loads[3:]:
        copy.start()
    unit_sums[...] = jnp.zeros_like(unit_sums)
    line = LineExchange(narrow_count)
    filled, line_cols = line_in.shape[2:]

    def line_part(block):
        return reduce_mat.at[
            pl.ds(0, filled), pl.ds(pl.multiple_of(block * line_cols, line_cols), line_cols)
        ]

    line_sum = LineSum(line, line_part, line_in, line_send, line_recv)
    greet_plane(plane)
    line.greet(3)
    for copy in late_loads:
        copy.start()
    kept = []
    waiting = list(loads)

    def compute(chip):
        while waiting:
            waiting.pop().wait()

        def units(cols):
            pulled = dot(pair_rows(blocks, chip), reduce_mat[cols], ((1,), (1,)))
            pair = pl.ds(2 * chip, 2)
            shape = pulled.shape
            gate_grad = pulled * slope[pair, :, cols].reshape(shape).astype(jnp.float32)
            upper_grad = pulled * gelu[pair, :, cols].reshape(shape).astype(jnp.float32)
            set_pair(slope, chip, cols, gate_grad)
            set_pair(gelu, chip, cols, upper_grad)
            unit_sums[0:1, cols] += jnp.sum(gate_grad, axis=0, keepdims=True)
            unit_sums[1:2, cols] += jnp.sum(upper_grad, axis=0, keepdims=True)

        tiles(slope.shape[2], 256, units)

    def compute_sums(chip):
        def outputs(cols):
            set_pair(
                parts,
                chip,
                cols,
                dot(pair_rows(slope, chip), expand_mat[0, :, cols], ((1,), (0,)))
                + dot(pair_rows(gelu, chip), expand_mat[1, :, cols], ((1,), (0,))),
            )

        tiles(parts.shape[2], 256, outputs)

    def product(left, right, start):
        tokens = left.shape[0] * left.shape[1]
        return dot(
            left[:, :, start : start + 256].reshape(tokens, 256),
            right[...].reshape(tokens, right.shape[2]),
            ((0,), (0,)),
        ).astype(jnp.bfloat16)

    def reduce_work():
        for copy in late_loads:
            copy.wait()

        def reduce_cols(index):
            cols = pl.ds(pl.multiple_of(index * line_cols, line_cols), line_cols)

            def units(some):
                tokens = active.shape[0] * active.shape[1]
                part = dot(
                    active[:, :, some].reshape(tokens, some.size),
                    blocks[:, :, cols].reshape(tokens, line_cols),
                    ((0,), (0,)),
                )
                reduce_mat[some, cols] = part.astype(jnp.bfloat16)

            tiles(active.shape[2], 256, units)

        for offset in range(narrow_count - 1, 0, -1):
            for way in range(2):

                @pl.when(line_sum.reaches(way, offset))
                def _():
                    reduce_cols(line_sum.target(way, offset))

            line_sum.begin(offset)
        reduce_cols(line.mine)

    def expand_work(left, start, target):
        def work():
            index = len(kept)
            if index >= 2:
                kept[index - 2].wait()
            staged[index % 2] = product(left, rows_all, start)
            stop = min(256, target.shape[0] - start)
            copy = pltpu.make_async_copy(
                staged.at[index % 2, pl.ds(0, stop)],
                target.at[pl.ds(start, stop)],
                keep_sems.at[index % 2],
            )
            copy.start()
            kept.append(copy)

        return work

    works = [
        expand_work(left, start, target)
        for left, target in ((slope, expand_part.at[0]), (gelu, expand_part.at[1]))
        for start in range(0, target.shape[0], 256)
    ]
    steps = [
        functools.partial(line_sum.step, offset) for offset in range(narrow_count - 2, 0, -1)
    ]
    third = len(works) // 3
    middle = (len(steps) + 1) // 2

    def many(calls):
        for call in calls:
            call()

    beside = functools.partial(many, steps[:middle] + works[:third])
    plane.run(compute, compute_sums, reduce_work, beside)
    many(works[third : 2 * third] + steps[middle:] + works[2 * third :])
    plane.finish(hidden_grad)
    plane.drain()
    line_sum.finish(reduce_grad)
    line_sum.drain()
    for copy in kept[-2:]:
        copy.wait()


def geglu_backward(
    wide_count,
    narrow_count,
    feed_grad,
    expand,
    reduce_full,
    slope,
    gelu,
    active,
    rows_all,
):
    rows, width = feed_grad.shape
    padded = slope.shape[2]
    anywhere = pl.BlockSpec(memory_space=pl.ANY)
    vmem = pl.BlockSpec(memory_space=pltpu.VMEM)
    scratch = exchange_scratch(wide_count, rows, width) + [
        pltpu.VMEM((2, padded, width), jnp.bfloat16),
        pltpu.VMEM((padded, width), jnp.bfloat16),
        pltpu.VMEM((wide_count, rows, padded), jnp.bfloat16),
        pltpu.VMEM((wide_count, rows, padded), jnp.bfloat16),
        pltpu.VMEM((wide_count, rows, padded), jnp.bfloat16),
        pltpu.VMEM((wide_count, rows, width), jnp.bfloat16),
        pltpu.VMEM((2, 256, width), jnp.bfloat16),
        pltpu.SemaphoreType.DMA((7,)),
        pltpu.SemaphoreType.DMA((2,)),
        pltpu.VMEM(
            (2, narrow_count - 1, reduce_full.shape[0], width // narrow_count), jnp.bfloat16
        ),
        pltpu.SemaphoreType.DMA((2, narrow_count - 1)),
        pltpu.SemaphoreType.DMA((2, narrow_count - 1)),
    ]
    return pl.pallas_call(
        functools.partial(geglu_backward_kernel, wide_count, narrow_count),
        out_shape=(
            jax.ShapeDtypeStruct(
                (reduce_full.shape[0], width // narrow_count), jnp.float32
            ),
            jax.ShapeDtypeStruct(expand.shape, jnp.bfloat16),
            jax.ShapeDtypeStruct((rows, width), jnp.float32),
            jax.ShapeDtypeStruct((2, padded), jnp.float32),
        ),
        in_specs=[anywhere] * 7,
        out_specs=(vmem, anywhere, vmem, vmem),
        scratch_shapes=scratch,
        compiler_params=pltpu.CompilerParams(
            collective_id=2, has_side_effects=True, vmem_limit_bytes=63 * 2**20
        ),
        cost_estimate=pl.CostEstimate(
            flops=12 * wide_count * rows * padded * width, bytes_accessed=200 * 2**20, transcendentals=0
        ),
        name="geglu_backward",
    )(feed_grad, expand, reduce_full, slope, gelu, active, rows_all)


def rotate_lanes(vectors, cosine, signed_sine):
    return vectors * cosine + pltpu.roll(vectors, vectors.shape[1] // 2, 1) * signed_sine


def attention_backward_kernel(
    wide_count,
    narrow_count,
    upper_grad,
    hidden_part,
    normed,
    inv_std,
    gain,
    merge,
    mixed,
    queries,
    keys,
    values,
    probs,
    cosine,
    signed_sine,
    triple,
    merge_grad,
    heads_sums,
    merge_sums,
    sum_grad,
    norm_sums,
    attended,
    upstream,
    outbound,
    probs_held,
    keys_turned,
    key_total,
    value_total,
    merge_out,
    merge_in,
    mixed_send,
    mixed_recv,
    merge_send,
    merge_recv,
    load_sems,
    parts,
    from_mate,
    incoming,
    mate_send,
    mate_recv,
    sum_send,
    sum_recv,
):
    sems = (None, None, mate_send, mate_recv, sum_send, sum_recv, None)
    plane = PlaneExchange(wide_count, None, None, parts, from_mate, incoming, sems)
    line = LineExchange(narrow_count)
    rows, width = sum_grad.shape
    own_cols = queries.shape[1]
    heads = own_cols // HDIM
    scale = HDIM ** (-0.5)

    def load(head):
        return pltpu.make_async_copy(
            probs.at[head], probs_held.at[head % 2], load_sems.at[head % 2]
        )

    load(0).start()
    greet_plane(plane)

    norm_sums[...] = jnp.zeros_like(norm_sums)
    merge_sums[...] = jnp.zeros_like(merge_sums)

    def norm_rows(i, carry):
        some = pl.ds(pl.multiple_of(i * 16, 16), 16)
        hidden_grad = residual_scale * upper_grad[some] + hidden_part[some]
        norm_sums[0:1] += jnp.sum(hidden_grad * normed[some], axis=0, keepdims=True)
        norm_sums[1:2] += jnp.sum(hidden_grad, axis=0, keepdims=True)
        total = normalize_back(hidden_grad, normed[some], inv_std[some], gain[...])
        sum_grad[some] = total
        merge_sums[...] += jnp.sum(total, axis=0, keepdims=True)
        attended[some] = total.astype(jnp.bfloat16)
        return carry

    lax.fori_loop(0, rows // 16, norm_rows, 0)
    line.greet(3)

    def mixed_part(target, where):
        part = dot(
            attended[...],
            merge[pl.ds(pl.multiple_of(where * own_cols, own_cols), own_cols)],
            ((1,), (1,)),
        )
        target[...] = part.astype(jnp.bfloat16)

    for offset in range(1, narrow_count):
        place = line.peer(offset)
        mixed_part(outbound.at[offset - 1], place)
        line.send(offset, outbound.at[offset - 1], upstream, mixed_send, mixed_recv)
    mixed_part(upstream.at[line.mine], line.mine)

    block = parts.shape[1]

    def merge_rows(i, carry):
        cols = pl.ds(pl.multiple_of(i * block, block), block)
        parts[i] = dot(mixed[:, cols], attended[...], ((0,), (0,))).astype(jnp.bfloat16)
        return carry

    lax.fori_loop(0, wide_count, merge_rows, 0)
    for offset in range(plane.ring):
        plane.share(offset)
    plane.first_sums()
    plane.far_sums()
    plane.last_sums()
    plane.finish(merge_out)
    count = merge_grad.shape[0]

    def z_rows(where):
        return pl.ds(pl.multiple_of(where * count, count), count)

    for offset in range(1, narrow_count):
        line.send(
            offset, merge_out.at[z_rows(line.peer(offset))], merge_in, merge_send, merge_recv
        )
    for offset in range(1, narrow_count):
        line.arrived(offset, upstream, mixed_send, mixed_recv)

    def one_head(head):
        cols = pl.ds(head * HDIM, HDIM)
        load(head).wait()
        if head + 1 < heads:
            load(head + 1).start()
        held = probs_held.at[head % 2]
        keys_turned[...] = keys[:, cols].astype(jnp.float32).T.astype(jnp.bfloat16)
        key_total[...] = jnp.zeros_like(key_total)
        value_total[...] = jnp.zeros_like(value_total)

        def chunk(i, carry):
            here = pl.ds(pl.multiple_of(i * rows, rows), rows)
            weights_low = held[:, here]
            up = upstream[i, :, cols]
            pulled = dot(values[:, cols], up, ((1,), (1,)))
            weights = weights_low.astype(jnp.float32)
            scaled = weights * pulled
            change = (scaled - weights * jnp.sum(scaled, axis=0, keepdims=True)).astype(
                jnp.bfloat16
            )
            key_total[...] += dot(change, queries[here, cols], ((1,), (0,)))
            value_total[...] += dot(weights_low, up, ((1,), (0,)))
            query_grad = dot(keys_turned[...], change, ((1,), (0,))).T * scale
            triple[here, cols] = rotate_lanes(
                query_grad, cosine[here], signed_sine[here]
            ).astype(jnp.bfloat16)
            return carry

        lax.fori_loop(0, narrow_count, chunk, 0)

        def ending(i, carry):
            here = pl.ds(pl.multiple_of(i * rows, rows), rows)
            triple[here, pl.ds(own_cols + head * HDIM, HDIM)] = rotate_lanes(
                key_total[here] * scale, cosine[here], signed_sine[here]
            ).astype(jnp.bfloat16)
            triple[here, pl.ds(2 * own_cols + head * HDIM, HDIM)] = value_total[here].astype(
                jnp.bfloat16
            )
            return carry

        lax.fori_loop(0, narrow_count, ending, 0)

    for head in range(heads):
        one_head(head)

    def column_sums(cols):
        heads_sums[:, cols] = jnp.sum(
            triple[:, cols].astype(jnp.float32), axis=0, keepdims=True
        )

    tiles(3 * own_cols, 256, column_sums)
    summed = merge_out[z_rows(line.mine)].astype(jnp.float32)
    for offset in range(1, narrow_count):
        line.arrived(offset, merge_in, merge_send, merge_recv)
        summed += merge_in[line.peer(offset)].astype(jnp.float32)
    merge_grad[...] = summed
    line.drain()
    plane.drain()


def attention_backward(
    wide_count,
    narrow_count,
    upper_grad,
    hidden_part,
    normed,
    inv_std,
    gain,
    merge_full,
    mixed,
    queries,
    keys,
    values,
    probs,
    cosine,
    signed_sine,
):
    rows, width = normed.shape
    bucket, own_cols = queries.shape
    block = width // wide_count
    count = block // narrow_count
    anywhere = pl.BlockSpec(memory_space=pl.ANY)
    vmem = pl.BlockSpec(memory_space=pltpu.VMEM)
    dma = pltpu.SemaphoreType.DMA
    return pl.pallas_call(
        functools.partial(attention_backward_kernel, wide_count, narrow_count),
        out_shape=(
            jax.ShapeDtypeStruct((bucket, 3 * own_cols), jnp.bfloat16),
            jax.ShapeDtypeStruct((count, width), jnp.float32),
            jax.ShapeDtypeStruct((1, 3 * own_cols), jnp.float32),
            jax.ShapeDtypeStruct((1, width), jnp.float32),
            jax.ShapeDtypeStruct((rows, width), jnp.float32),
            jax.ShapeDtypeStruct((2, width), jnp.float32),
        ),
        in_specs=[vmem] * 10 + [anywhere] + [vmem] * 2,
        out_specs=(vmem,) * 6,
        scratch_shapes=[
            pltpu.VMEM((rows, width), jnp.bfloat16),
            pltpu.VMEM((narrow_count, rows, own_cols), jnp.bfloat16),
            pltpu.VMEM((narrow_count - 1, rows, own_cols), jnp.bfloat16),
            pltpu.VMEM((2, bucket, bucket), jnp.bfloat16),
            pltpu.VMEM((HDIM, bucket), jnp.bfloat16),
            pltpu.VMEM((bucket, HDIM), jnp.float32),
            pltpu.VMEM((bucket, HDIM), jnp.float32),
            pltpu.VMEM((block, width), jnp.bfloat16),
            pltpu.VMEM((narrow_count, count, width), jnp.bfloat16),
            dma((narrow_count - 1,)),
            dma((narrow_count,)),
            dma((narrow_count - 1,)),
            dma((narrow_count,)),
            dma((2,)),
        ]
        + sum_scratch(wide_count, block, width),
        compiler_params=pltpu.CompilerParams(
            collective_id=3, has_side_effects=True, vmem_limit_bytes=kernel_memory
        ),
        cost_estimate=pl.CostEstimate(
            flops=60 * 10**9, bytes_accessed=200 * 2**20, transcendentals=0
        ),
        name="attention_backward",
    )(
        upper_grad,
        hidden_part,
        normed,
        inv_std,
        gain,
        merge_full,
        mixed,
        queries,
        keys,
        values,
        probs,
        cosine,
        signed_sine,
    )


def input_backward_kernel(
    wide_count,
    narrow_count,
    inputs,
    triple,
    heads_mat,
    small,
    input_part,
    heads_grad,
    small_out,
    line_parts,
    line_in,
    heads_out,
    heads_in,
    small_wide,
    small_sum,
    small_line,
    line_send,
    line_recv,
    heads_send,
    heads_recv,
    wide_send,
    wide_recv,
    small_send,
    small_recv,
    parts,
    from_mate,
    incoming,
    mate_send,
    mate_recv,
    sum_send,
    sum_recv,
):
    sems = (None, None, mate_send, mate_recv, sum_send, sum_recv, None)
    plane = PlaneExchange(wide_count, None, None, parts, from_mate, incoming, sems)
    line = LineExchange(narrow_count)
    rows, width = input_part.shape
    here = line.mine
    last = narrow_count - 1
    place = lax.axis_index("wide")

    def wide_peer(offset):
        return (place + offset) % wide_count

    barrier = pltpu.get_barrier_semaphore()
    for offset in range(1, wide_count):
        pl.semaphore_signal(
            barrier,
            inc=1,
            device_id={"wide": wide_peer(offset)},
            device_id_type=pl.DeviceIdType.MESH,
        )
    line.greet(wide_count - 1)

    def small_copy(offset, source, slot):
        return pltpu.make_async_remote_copy(
            src_ref=source,
            dst_ref=small_wide.at[slot],
            send_sem=wide_send.at[offset - 1],
            recv_sem=wide_recv.at[slot],
            device_id={"wide": wide_peer(offset)},
            device_id_type=pl.DeviceIdType.MESH,
        )

    small_copies = [
        small_copy(offset, small.at[wide_peer(offset)], place) for offset in range(1, wide_count)
    ]
    for copy in small_copies:
        copy.start()

    line_sum = LineSum(line, lambda target: line_parts.at[target], line_in, line_send, line_recv)

    def input_rows(index):
        some = pl.ds(pl.multiple_of(index * rows, rows), rows)

        def input_cols(cols):
            part = dot(triple[some], heads_mat[cols], ((1,), (1,)))
            line_parts[index, :, cols] = part.astype(jnp.bfloat16)

        tiles(width, 256, input_cols)

    for offset in range(last, 0, -1):
        for way in range(2):

            @pl.when(line_sum.reaches(way, offset))
            def _():
                input_rows(line_sum.target(way, offset))

        line_sum.begin(offset)
    input_rows(here)

    block = parts.shape[1]

    def heads_rows(i, carry):
        cols = pl.ds(pl.multiple_of(i * block, block), block)
        parts[i] = dot(inputs[:, cols], triple[...], ((0,), (0,))).astype(jnp.bfloat16)
        return carry

    lax.fori_loop(0, wide_count, heads_rows, 0)
    for offset in range(plane.ring):
        plane.share(offset)
    for offset in range(last - 1, last // 2, -1):
        line_sum.step(offset)
    plane.first_sums()
    plane.far_sums()

    for offset in range(1, wide_count):
        peer = wide_peer(offset)
        small_copy(offset, small_wide.at[peer], peer).wait_recv()
    small_wide[place] = small[place]
    total = small_wide[0]
    for index in range(1, wide_count):
        total += small_wide[index]
    small_sum[...] = total
    for offset in range(1, narrow_count):
        line.send(offset, small_sum.at[line.peer(offset)], small_line, small_send, small_recv)

    plane.last_sums()
    for offset in range(last // 2, 0, -1):
        line_sum.step(offset)
    plane.finish(heads_out)
    count = heads_grad.shape[0]

    def z_rows(where):
        return pl.ds(pl.multiple_of(where * count, count), count)

    for offset in range(1, narrow_count):
        line.send(
            offset, heads_out.at[z_rows(line.peer(offset))], heads_in, heads_send, heads_recv
        )
    heads_in[line.mine] = heads_out[z_rows(line.mine)]
    small_line[line.mine] = small_sum[line.mine]
    for offset in range(1, narrow_count):
        line.arrived(offset, small_line, small_send, small_recv)
    result = small_line[0]
    for index in range(1, narrow_count):
        result += small_line[index]
    small_out[...] = result

    line_sum.finish(input_part)
    for offset in range(1, narrow_count):
        line.arrived(offset, heads_in, heads_send, heads_recv)
    own_cols = triple.shape[1] // 3
    for index in range(narrow_count):
        for which in range(3):
            start = (which * narrow_count + index) * own_cols
            heads_grad[:, start : start + own_cols] = heads_in[
                index, :, which * own_cols : (which + 1) * own_cols
            ].astype(jnp.float32)
    line_sum.drain()
    for copy in small_copies:
        copy.wait_send()
    line.drain()
    plane.drain()


def input_backward(wide_count, narrow_count, inputs, triple_grad, heads_mat, small):
    bucket, width = inputs.shape
    rows = bucket // narrow_count
    columns = triple_grad.shape[1]
    block = width // wide_count
    count = block // narrow_count
    vmem = pl.BlockSpec(memory_space=pltpu.VMEM)
    dma = pltpu.SemaphoreType.DMA
    lines = small.shape[2]
    return pl.pallas_call(
        functools.partial(input_backward_kernel, wide_count, narrow_count),
        out_shape=(
            jax.ShapeDtypeStruct((rows, width), jnp.float32),
            jax.ShapeDtypeStruct((count, narrow_count * columns), jnp.float32),
            jax.ShapeDtypeStruct((lines, 128), jnp.float32),
        ),
        in_specs=[vmem] * 4,
        out_specs=(vmem, vmem, vmem),
        scratch_shapes=[
            pltpu.VMEM((narrow_count, rows, width), jnp.bfloat16),
            pltpu.VMEM((2, narrow_count - 1, rows, width), jnp.bfloat16),
            pltpu.VMEM((block, columns), jnp.bfloat16),
            pltpu.VMEM((narrow_count, count, columns), jnp.bfloat16),
            pltpu.VMEM((wide_count, narrow_count, lines, 128), jnp.float32),
            pltpu.VMEM((narrow_count, lines, 128), jnp.float32),
            pltpu.VMEM((narrow_count, lines, 128), jnp.float32),
            dma((2, narrow_count - 1)),
            dma((2, narrow_count - 1)),
            dma((narrow_count - 1,)),
            dma((narrow_count,)),
            dma((wide_count - 1,)),
            dma((wide_count,)),
            dma((narrow_count - 1,)),
            dma((narrow_count,)),
        ]
        + sum_scratch(wide_count, block, columns),
        compiler_params=pltpu.CompilerParams(
            collective_id=4, has_side_effects=True, vmem_limit_bytes=kernel_memory
        ),
        cost_estimate=pl.CostEstimate(
            flops=80 * 10**9, bytes_accessed=200 * 2**20, transcendentals=0
        ),
        name="input_backward",
    )(inputs, triple_grad, heads_mat, small)


def greet_all(wide_count, narrow_count):
    barrier = pltpu.get_barrier_semaphore()
    for axis, count in (("wide", wide_count), ("narrow", narrow_count)):
        place = lax.axis_index(axis)
        for offset in range(1, count):
            pl.semaphore_signal(
                barrier,
                inc=1,
                device_id={axis: (place + offset) % count},
                device_id_type=pl.DeviceIdType.MESH,
            )
    pl.semaphore_wait(barrier, wide_count + narrow_count - 2)


def gather_kernel(
    wide_count,
    narrow_count,
    own,
    heads_weight,
    merge_weight,
    small,
    buckets,
    speeds,
    rows_out,
    heads_out,
    merge_out,
    small_out,
    triple,
    cosine,
    signed_sine,
    first_query,
    last_query,
    rows_all,
    heads_all,
    merge_own,
    small_all,
    rows_send,
    rows_recv,
    heads_send,
    heads_recv,
    merge_send,
    merge_recv,
    small_send,
    small_recv,
    wide_send,
    wide_recv,
    local_sems,
    out_sems,
    heads_ring_send,
    heads_ring_recv,
):
    ring_sems = (heads_ring_send, heads_ring_recv, None, None, None, None, None)
    heads_ring = PlaneExchange(wide_count, None, heads_all, heads_all, None, None, ring_sems)
    line = LineExchange(narrow_count)
    here = line.mine
    last = narrow_count - 1
    place = lax.axis_index("wide")
    slot = heads_ring.slot(0)
    rows, width = own.shape
    count = heads_weight.shape[0]
    columns = heads_all.shape[2]
    own_cols = columns // 3

    def z_rows(where):
        return pl.ds(pl.multiple_of(where * count, count), count)

    def head_cols(which, where):
        start = which * narrow_count * own_cols + where * own_cols
        return pl.ds(pl.multiple_of(start, own_cols), own_cols)

    line_rows = LineGather(line, lambda block: rows_all.at[block], rows_send, rows_recv)

    keep_rows = pltpu.make_async_copy(own, rows_all.at[here], local_sems.at[0])
    keep_rows.start()
    keeps = [
        pltpu.make_async_copy(
            heads_weight.at[:, head_cols(which, here)],
            heads_all.at[slot, z_rows(here), pl.ds(which * own_cols, own_cols)],
            local_sems.at[2 + which],
        )
        for which in range(3)
    ]
    keep_merge = pltpu.make_async_copy(
        merge_weight, merge_own.at[z_rows(here)], local_sems.at[1]
    )
    for copy in keeps + [keep_merge]:
        copy.start()
    small_all[place, here] = small[...]
    greet_all(wide_count, narrow_count)

    def heads_copy(offset, which, where, sender):
        return line.copy(
            heads_weight.at[:, head_cols(which, where)],
            heads_all.at[slot, z_rows(sender), pl.ds(which * own_cols, own_cols)],
            heads_send.at[offset - 1, which],
            heads_recv.at[sender, which],
            where,
        )

    def merge_copy(offset, where, sender):
        return line.copy(
            merge_weight,
            merge_own.at[z_rows(sender)],
            merge_send.at[offset - 1],
            merge_recv.at[sender],
            where,
        )

    def small_copy(offset, where, sender):
        return line.copy(
            small,
            small_all.at[place, sender],
            small_send.at[offset - 1],
            small_recv.at[sender],
            where,
        )

    started = []

    def start(copy):
        copy.start()
        started.append(copy)

    for offset in range(1, narrow_count):
        for which in range(3):
            start(heads_copy(offset, which, line.peer(offset), here))
    for offset in range(1, narrow_count):
        start(small_copy(offset, line.peer(offset), here))
    keep_rows.wait()
    line_rows.send_own()

    halfway = narrow_count * rows // 2
    joined = buckets[0]

    def tables(i, carry):
        some = pl.ds(pl.multiple_of(i * rows, rows), rows)
        place_in = i * rows + lax.broadcasted_iota(jnp.int32, (rows, 1), 0)
        second = jnp.where(place_in >= halfway, 1 - joined, 0)
        local = place_in - second * halfway
        reach = jnp.where(
            joined == 1,
            buckets[1] + buckets[2],
            jnp.where(second == 1, buckets[2], buckets[1]),
        )
        first_query[some] = jnp.where(local < reach, place_in - local, place_in)
        last_query[some] = jnp.where(
            (joined == 1) | (second == 1), 2 * halfway - 1, halfway - 1
        ) + jnp.zeros_like(place_in)
        angles = local.astype(jnp.float32) * speeds[...]
        lane = lax.broadcasted_iota(jnp.int32, (rows, HDIM), 1)
        cosine[some] = jnp.cos(angles)
        sine = jnp.sin(angles)
        signed_sine[some] = jnp.where(lane < HDIM // 2, sine, -sine)
        return carry

    lax.fori_loop(0, narrow_count, tables, 0)

    for copy in keeps:
        copy.wait()
    for offset in range(1, narrow_count):
        for which in range(3):
            heads_copy(offset, which, line.peer(offset), line.peer(offset)).wait_recv()
    heads_ring.send_own()
    for offset in range(1, narrow_count):
        small_copy(offset, line.peer(offset), line.peer(offset)).wait_recv()

    def wide_copy(offset, sender):
        return pltpu.make_async_remote_copy(
            src_ref=small_all.at[sender],
            dst_ref=small_all.at[sender],
            send_sem=wide_send.at[offset - 1],
            recv_sem=wide_recv.at[sender],
            device_id={"wide": (place + offset) % wide_count},
            device_id_type=pl.DeviceIdType.MESH,
        )

    for offset in range(1, wide_count):
        start(wide_copy(offset, place))

    def project(block):
        def cols_step(cols):
            weight = heads_all[:, :, cols].reshape(width, cols.size)
            triple[pl.ds(pl.multiple_of(block * rows, rows), rows), cols] = dot(
                rows_all[block], weight, ((1,), (0,))
            )

        tiles(columns, 256, cols_step)

    def project_step(step):
        line_rows.each(step, project)

    def gather(ring, distance):
        ring.receive(distance)
        ring.receive_mate(-distance)
        if distance < ring.far:
            ring.receive_mate(distance)

    outs = []

    def keep_out(source, target):
        copy = pltpu.make_async_copy(source, target, out_sems.at[len(outs)])
        copy.start()
        outs.append(copy)

    line_rows.step(1)
    for offset in range(1, narrow_count):
        start(merge_copy(offset, line.peer(offset), here))
    heads_ring.receive_mate(0)
    for distance in range(1, heads_ring.far + 1):
        gather(heads_ring, distance)
    keep_out(heads_all, heads_out)
    project(here)
    for step in range(2, narrow_count):
        line_rows.step(step)
        project_step(step - 1)
    project_step(last)
    keep_merge.wait()
    for offset in range(1, narrow_count):
        merge_copy(offset, line.peer(offset), line.peer(offset)).wait_recv()
    keep_out(merge_own, merge_out)
    keep_out(rows_all, rows_out)
    for offset in range(1, wide_count):
        wide_copy(offset, (place + offset) % wide_count).wait_recv()
    keep_out(small_all, small_out)
    line_rows.drain()
    for copy in started:
        copy.wait_send()
    heads_ring.drain()
    for copy in outs:
        copy.wait()


def gather_front(
    wide_count, narrow_count, layer_input, heads_weight, merge_weight, small, buckets, speeds
):
    rows, width = layer_input.shape
    count, all_columns = heads_weight.shape
    columns = all_columns // narrow_count
    block = count * narrow_count
    anywhere = pl.BlockSpec(memory_space=pl.ANY)
    vmem = pl.BlockSpec(memory_space=pltpu.VMEM)
    dma = pltpu.SemaphoreType.DMA
    lines = small.shape[0]
    shapes = (
        (narrow_count, rows, width),
        (wide_count, block, columns),
        (block, width),
        (wide_count, narrow_count, lines, 128),
    )
    far = narrow_count - 1
    bucket = narrow_count * rows
    table = jax.ShapeDtypeStruct((bucket, HDIM), jnp.float32)
    reach = jax.ShapeDtypeStruct((bucket, 1), jnp.int32)
    return pl.pallas_call(
        functools.partial(gather_kernel, wide_count, narrow_count),
        out_shape=tuple(jax.ShapeDtypeStruct(shape, jnp.bfloat16) for shape in shapes)
        + (jax.ShapeDtypeStruct((bucket, columns), jnp.float32), table, table, reach, reach),
        in_specs=[anywhere, anywhere, anywhere, vmem, pl.BlockSpec(memory_space=pltpu.SMEM), vmem],
        out_specs=(anywhere,) * 4 + (vmem,) * 5,
        scratch_shapes=[pltpu.VMEM(shape, jnp.bfloat16) for shape in shapes]
        + [
            dma((2, narrow_count)),
            dma((narrow_count,)),
            dma((far, 3)),
            dma((narrow_count, 3)),
            dma((far,)),
            dma((narrow_count,)),
            dma((far,)),
            dma((narrow_count,)),
            dma((wide_count - 1,)),
            dma((wide_count,)),
            dma((5,)),
            dma((4,)),
            dma((3, wide_count, 2)),
            dma((wide_count, 2)),
        ],
        compiler_params=pltpu.CompilerParams(
            collective_id=5, has_side_effects=True, vmem_limit_bytes=kernel_memory
        ),
        cost_estimate=pl.CostEstimate(
            flops=80 * 10**9, bytes_accessed=200 * 2**20, transcendentals=0
        ),
        name="gather_front",
    )(layer_input, heads_weight, merge_weight, small, buckets, speeds)


def attention_forward_kernel(
    wide_count,
    narrow_count,
    triple,
    heads_shift,
    cosine,
    signed_sine,
    first_query,
    last_query,
    own,
    merge,
    merge_shift,
    gain,
    shift,
    queries,
    keys,
    values,
    probs,
    mixed_out,
    hidden,
    hidden_low,
    normed,
    inv_std,
    merge_out,
    merge_mat,
    probs_held,
    values_turned,
    outbound,
    mixed,
    mixed_send,
    mixed_recv,
    local_sems,
    ring_send,
    ring_recv,
    own_sem,
):
    line = LineExchange(narrow_count)
    ring_sems = (ring_send, ring_recv, None, None, None, None, own_sem)
    ring = PlaneExchange(wide_count, merge, merge_mat, merge_mat, None, None, ring_sems)
    bucket, own_cols = queries.shape
    rows, width = own.shape
    heads = own_cols // HDIM
    scale = HDIM ** (-0.5)
    greet_plane(ring)
    line.greet(3)
    keep_own = ring.send_own()
    ring_steps = [functools.partial(ring.receive, step) for step in range(1, ring.far + 1)]

    def keep(head):
        return pltpu.make_async_copy(
            probs_held.at[head % 2], probs.at[head], local_sems.at[head % 2]
        )

    def mixed_copy(head, offset, where, sender):
        cols = pl.ds(pl.multiple_of(sender * own_cols + head * HDIM, HDIM), HDIM)
        return line.copy(
            outbound.at[where, :, pl.ds(head * HDIM, HDIM)],
            mixed.at[:, cols],
            mixed_send.at[offset - 1, head],
            mixed_recv.at[sender, head],
            where,
        )

    started = []
    for head in range(heads):
        cols = pl.ds(head * HDIM, HDIM)

        def turn(i, carry):
            here = pl.ds(pl.multiple_of(i * rows, rows), rows)
            for which, target in enumerate((queries, keys, values)):
                wanted = pl.ds(which * own_cols + head * HDIM, HDIM)
                part = triple[here, wanted] + heads_shift[:, wanted]
                if which < 2:
                    part = rotate_lanes(part, cosine[here], -signed_sine[here])
                else:
                    values_turned[:, here] = part.T.astype(jnp.bfloat16)
                target[here, cols] = part.astype(jnp.bfloat16)
            return carry

        lax.fori_loop(0, narrow_count, turn, 0)
        if head >= 2:
            keep(head - 2).wait()
        held = probs_held.at[head % 2]

        def chunk(i, carry):
            here = pl.ds(pl.multiple_of(i * rows, rows), rows)
            scores = dot(keys[:, cols], queries[here, cols], ((1,), (1,))) * scale
            token = i * rows + lax.broadcasted_iota(jnp.int32, (bucket, rows), 1)
            seen = (token >= first_query[...]) & (token <= last_query[...])
            scores = jnp.where(seen, scores, masked_value)
            expo = jnp.exp(scores - jnp.max(scores, axis=0, keepdims=True))
            weights = (expo * (1 / jnp.sum(expo, axis=0, keepdims=True))).astype(jnp.bfloat16)
            held[:, here] = weights
            mixed_part = dot(values_turned[...], weights, ((1,), (0,)))
            outbound[i, :, cols] = mixed_part.T.astype(jnp.bfloat16)
            return carry

        lax.fori_loop(0, narrow_count, chunk, 0)
        keep(head).start()
        for offset in range(1, narrow_count):
            copy = mixed_copy(head, offset, line.peer(offset), line.mine)
            copy.start()
            started.append(copy)
        if ring_steps:
            ring_steps.pop(0)()
    own_mixed = pltpu.make_async_copy(
        outbound.at[line.mine],
        mixed.at[:, pl.ds(pl.multiple_of(line.mine * own_cols, own_cols), own_cols)],
        local_sems.at[3],
    )
    own_mixed.start()
    own_mixed.wait()
    keep_own.wait()
    for step in ring_steps:
        step()
    for offset in range(ring.ring):
        ring.receive_mate(offset)
    keep_merge = pltpu.make_async_copy(merge_mat, merge_out, local_sems.at[2])
    keep_merge.start()
    for offset in range(1, narrow_count):
        for head in range(heads):
            mixed_copy(head, offset, line.peer(offset), line.peer(offset)).wait_recv()
    mixed_out[...] = mixed[...]

    def merge_cols(cols):
        hidden[:, cols] = (
            residual_scale * own[:, cols].astype(jnp.float32)
            + dot(mixed[...], merge_mat[:, :, cols].reshape(width, cols.size), ((1,), (0,)))
            + merge_shift[:, cols]
        )

    tiles(width, 256, merge_cols)

    def norm_rows(i, carry):
        some = pl.ds(pl.multiple_of(i * 16, 16), 16)
        result, centred, inverse = normalize(hidden[some], gain[...], shift[...])
        hidden[some] = result
        hidden_low[some] = result.astype(jnp.bfloat16)
        normed[some] = centred
        inv_std[some] = inverse
        return carry

    lax.fori_loop(0, rows // 16, norm_rows, 0)
    for head in range(max(heads - 2, 0), heads):
        keep(head).wait()
    for copy in started:
        copy.wait_send()
    ring.drain()
    keep_merge.wait()


def attention_forward(
    wide_count,
    narrow_count,
    triple,
    heads_shift,
    cosine,
    signed_sine,
    first_query,
    last_query,
    layer_input,
    merge_block,
    merge_shift,
    gain,
    shift,
):
    bucket, columns = triple.shape
    rows, width = layer_input.shape
    own_cols = columns // 3
    heads = own_cols // HDIM
    anywhere = pl.BlockSpec(memory_space=pl.ANY)
    vmem = pl.BlockSpec(memory_space=pltpu.VMEM)
    dma = pltpu.SemaphoreType.DMA

    def low_shape(*shape):
        return jax.ShapeDtypeStruct(shape, jnp.bfloat16)

    def wide_shape(*shape):
        return jax.ShapeDtypeStruct(shape, jnp.float32)

    return pl.pallas_call(
        functools.partial(attention_forward_kernel, wide_count, narrow_count),
        out_shape=(
            low_shape(bucket, own_cols),
            low_shape(bucket, own_cols),
            low_shape(bucket, own_cols),
            low_shape(heads, bucket, bucket),
            low_shape(rows, width),
            wide_shape(rows, width),
            low_shape(rows, width),
            wide_shape(rows, width),
            wide_shape(rows, 1),
            low_shape(wide_count, *merge_block.shape),
        ),
        in_specs=[vmem] * 7 + [anywhere] + [vmem] * 3,
        out_specs=(vmem, vmem, vmem, anywhere) + (vmem,) * 5 + (anywhere,),
        scratch_shapes=[
            pltpu.VMEM((wide_count, *merge_block.shape), jnp.bfloat16),
            pltpu.VMEM((2, bucket, bucket), jnp.bfloat16),
            pltpu.VMEM((HDIM, bucket), jnp.bfloat16),
            pltpu.VMEM((narrow_count, rows, own_cols), jnp.bfloat16),
            pltpu.VMEM((rows, width), jnp.bfloat16),
            dma((narrow_count - 1, heads)),
            dma((narrow_count, heads)),
            dma((4,)),
            dma((3, wide_count, 2)),
            dma((wide_count, 2)),
            dma(()),
        ],
        compiler_params=pltpu.CompilerParams(
            collective_id=6, has_side_effects=True, vmem_limit_bytes=kernel_memory
        ),
        cost_estimate=pl.CostEstimate(
            flops=60 * 10**9, bytes_accessed=200 * 2**20, transcendentals=0
        ),
        name="attention_forward",
    )(
        triple,
        heads_shift,
        cosine,
        signed_sine,
        first_query,
        last_query,
        layer_input,
        merge_block,
        merge_shift,
        gain,
        shift,
    )


def shards(
    layer_input,
    heads_weight,
    heads_bias,
    merge_weight,
    merge_bias,
    norm_gains,
    norm_shifts,
    expand_weight,
    expand_bias,
    reduce_weight,
    reduce_bias,
    joined,
    prefix,
    cotangent,
):
    tok_rows, model_width = layer_input.shape
    wide_count = lax.axis_size("wide")
    narrow_count = lax.axis_size("narrow")
    count = wide_count * narrow_count
    bucket_len = tok_rows * narrow_count
    own_heads = HEADS // narrow_count
    own_cols = own_heads * HDIM
    share = expand_weight.shape[2]
    narrow_index = lax.axis_index("narrow")
    smalls = (heads_bias, merge_bias, norm_gains, norm_shifts, expand_bias, reduce_bias)
    (
        rows_input,
        heads_mat,
        merge_block,
        small_all,
        triple,
        cosine,
        signed_sine,
        first_query,
        last_query,
    ) = gather_front(
        wide_count,
        narrow_count,
        layer_input,
        heads_weight,
        merge_weight,
        pack_small(smalls),
        jnp.concatenate([joined, prefix[0]]),
        jnp.asarray(rotary_speeds(HDIM)),
    )
    rows_input = rows_input.reshape(bucket_len, model_width)
    heads_mat = heads_mat.reshape(model_width, 3 * own_cols)
    heads_shift, merge_shift, gains, shifts, expand_shift, reduce_shift = unpack_small(
        small_all, smalls
    )
    own_shift = lax.dynamic_index_in_dim(
        heads_shift.reshape(3, narrow_count, own_cols), narrow_index, 1, keepdims=False
    ).reshape(1, -1)
    (
        queries,
        keys,
        values,
        probs_low,
        mixed,
        hidden,
        hidden_low,
        normed_one,
        inv_one,
        merge_full,
    ) = attention_forward(
        wide_count,
        narrow_count,
        triple,
        own_shift,
        cosine,
        signed_sine,
        first_query,
        last_query,
        layer_input,
        merge_block,
        merge_shift.reshape(1, -1),
        gains[0].reshape(1, -1),
        shifts[0].reshape(1, -1),
    )

    tile_rows = -share % 16
    padded = -(-share // 256) * 256
    expand_low = jnp.pad(expand_weight.transpose(1, 2, 0), ((0, 0), (0, tile_rows), (0, 0)))
    expand_low, _ = lax.optimization_barrier((expand_low, small_all))
    expand_full = lax.all_gather(expand_low, "narrow", axis=2, tiled=True)
    reduce_low = jnp.pad(reduce_weight, ((0, tile_rows), (0, 0)))
    (
        reduce_full,
        rows_all,
        active,
        slope,
        gelu,
        layer_output,
        sum_two_grad,
        feed_grad,
        row_sums,
    ) = geglu_forward(
        wide_count,
        narrow_count,
        hidden_low,
        expand_full,
        reduce_low,
        jnp.pad(expand_shift, ((0, 0), (0, padded - share))),
        hidden,
        cotangent,
        reduce_shift.reshape(1, -1),
        gains[1].reshape(1, -1),
        shifts[1].reshape(1, -1),
    )
    reduce_weight_gradient, expand_part, hidden_part, unit_sums = geglu_backward(
        wide_count,
        narrow_count,
        feed_grad,
        expand_full,
        reduce_full,
        slope,
        gelu,
        active,
        rows_all,
    )
    expand_weight_gradient = (
        lax.psum_scatter(expand_part, "narrow", scatter_dimension=2, tiled=True)[:, :share]
        .astype(jnp.float32)
        .transpose(2, 0, 1)
    )
    (
        triple_grad,
        merge_weight_gradient,
        heads_sums,
        merge_sums,
        sum_one_grad,
        norm_one_sums,
    ) = attention_backward(
        wide_count,
        narrow_count,
        sum_two_grad,
        hidden_part,
        normed_one,
        inv_one,
        gains[0].reshape(1, -1),
        merge_full.reshape(model_width, model_width),
        mixed,
        queries,
        keys,
        values,
        probs_low,
        cosine,
        signed_sine,
    )

    mine_narrow = (jnp.arange(narrow_count) == narrow_index).astype(jnp.float32)
    mine_wide = (jnp.arange(wide_count) == lax.axis_index("wide")).astype(jnp.float32)
    heads_sums = heads_sums.reshape(3, 1, own_cols)
    heads_sums = (heads_sums * mine_narrow[None, :, None]).reshape(count, -1)
    merge_sums = merge_sums.reshape(count, -1)
    norm_sums = (
        jnp.stack([norm_one_sums[0], row_sums[0], norm_one_sums[1], row_sums[1]])
        .reshape(4, count, -1)
        .transpose(1, 0, 2)
        .reshape(count, -1)
    )
    expand_sums = unit_sums[:, :share]
    expand_sums = (
        expand_sums.reshape(2, narrow_count, -1).transpose(1, 0, 2).reshape(1, narrow_count, -1)
        * mine_wide[:, None, None]
    ).reshape(count, -1)
    reduce_sums = row_sums[2].reshape(1, narrow_count, -1)
    reduce_sums = jnp.broadcast_to(
        reduce_sums, (wide_count, narrow_count, reduce_sums.shape[2])
    ).reshape(count, -1)
    pieces = (heads_sums, merge_sums, norm_sums, expand_sums, reduce_sums)
    packed = jnp.concatenate(pieces, axis=1)
    packed = jnp.pad(packed, ((0, 0), (0, -packed.shape[1] % 1024)))
    input_part, heads_weight_gradient, summed = input_backward(
        wide_count,
        narrow_count,
        rows_input,
        triple_grad,
        heads_mat,
        packed.reshape(wide_count, narrow_count, -1, 128),
    )
    input_gradient = residual_scale * sum_one_grad + input_part
    summed = summed.reshape(-1)
    ends = []
    start = 0
    for piece in pieces:
        ends.append(summed[start : start + piece.shape[1]])
        start += piece.shape[1]
    norm_ends = ends[2].reshape(4, -1)
    return (
        layer_output,
        input_gradient,
        heads_weight_gradient,
        ends[0],
        merge_weight_gradient,
        ends[1],
        norm_ends[:2],
        norm_ends[2:],
        expand_weight_gradient,
        ends[3].reshape(2, -1),
        reduce_weight_gradient[:share],
        ends[4],
    )


def solution(mesh):
    return jax.shard_map(
        shards,
        mesh=mesh,
        in_specs=(
            P(("wide", "narrow"), None),
            P(("wide", "narrow"), None),
            P(("wide", "narrow")),
            P(("wide", "narrow"), None),
            P(("wide", "narrow")),
            P(None, ("wide", "narrow")),
            P(None, ("wide", "narrow")),
            P("narrow", None, "wide"),
            P(None, ("wide", "narrow")),
            P("wide", "narrow"),
            P("narrow"),
            P("wide"),
            P("wide", None),
            P(("wide", "narrow"), None),
        ),
        out_specs=(
            P(("wide", "narrow"), None),
            P(("wide", "narrow"), None),
            P(("wide", "narrow"), None),
            P(("wide", "narrow")),
            P(("wide", "narrow"), None),
            P(("wide", "narrow")),
            P(None, ("wide", "narrow")),
            P(None, ("wide", "narrow")),
            P("narrow", None, "wide"),
            P(None, ("wide", "narrow")),
            P("wide", "narrow"),
            P("narrow"),
        ),
        check_vma=False,
    )
```

```python
import functools
import math

import jax
import jax.numpy as jnp
import numpy as np
from jax import lax
from jax.experimental import pallas as pl
from jax.experimental.pallas import tpu as pltpu
from jax.sharding import PartitionSpec as P

HEADS = 16
HDIM = 128


residual_scale = 48.0**0.5
norm_eps = 1e-05
masked_value = -1e30
kernel_memory = 60 * 2**20


def rotary_speeds(head_size):
    index = np.arange(head_size) % (head_size // 2)
    return (10000.0 ** (-2.0 * index / head_size)).astype(np.float32)[None]


def normalize(values, gain, shift):
    centre = jnp.mean(values, axis=-1, keepdims=True)
    centred = values - centre
    variance = jnp.mean(centred * centred, axis=-1, keepdims=True)
    inv_std = lax.rsqrt(variance + norm_eps)
    normed = centred * inv_std
    return (normed * gain + shift, normed, inv_std)


def normalize_back(upstream, normed, inv_std, gain):
    scaled = upstream * gain
    return inv_std * (
        scaled
        - jnp.mean(scaled, axis=-1, keepdims=True)
        - normed * jnp.mean(scaled * normed, axis=-1, keepdims=True)
    )


def dot(left, right, dims):
    return lax.dot_general(left, right, (dims, ((), ())), preferred_element_type=jnp.float32)


def low(values):
    return values.astype(jnp.bfloat16)


def small_rows(part):
    return part.reshape(-1, part.shape[-1]).shape[0], -(-part.shape[-1] // 128)


def pack_small(parts):
    pieces = []
    for part in parts:
        first, rows = small_rows(part)
        part = part.reshape(first, -1)
        part = jnp.pad(part, ((0, 0), (0, rows * 128 - part.shape[1])))
        pieces.append(part.reshape(first * rows, 128))
    packed = jnp.concatenate(pieces, axis=0)
    return jnp.pad(packed, ((0, -packed.shape[0] % 16), (0, 0)))


def unpack_small(everyone, parts):
    pieces = []
    start = 0
    for part in parts:
        first, rows = small_rows(part)
        piece = everyone[:, :, start : start + first * rows].astype(jnp.float32)
        piece = piece.reshape(piece.shape[:2] + (first, rows * 128))
        pieces.append(piece[..., : part.shape[-1]])
        start += first * rows

    def pairs(piece):
        return piece.reshape((-1,) + piece.shape[-2:]).transpose(1, 0, 2).reshape(2, -1)

    own_expand = lax.dynamic_index_in_dim(
        pieces[4], lax.axis_index("wide"), 0, keepdims=False
    )
    return (
        pieces[0].reshape(-1),
        pieces[1].reshape(-1),
        pairs(pieces[2]),
        pairs(pieces[3]),
        pairs(own_expand),
        pieces[5][0].reshape(-1),
    )


def ring_place(wide_count):
    ring = wide_count // 2
    mine = lax.axis_index("wide")
    chip = mine // 2
    core = mine % 2
    position = 2 * (chip // 2) + (chip % 2 + chip // 2) % 2
    return ring, position, core


def chip_at(position, ring):
    position = (position + 2 * ring) % ring
    return 2 * (position // 2) + (position + position // 2) % 2


class PlaneExchange:
    def __init__(self, wide_count, own, blocks, parts, from_mate, incoming, sems, cols=None):
        self.ring, self.position, self.core = ring_place(wide_count)
        self.own, self.blocks, self.parts = own, blocks, parts
        self.from_mate, self.incoming = from_mate, incoming
        (
            self.gather_send,
            self.gather_recv,
            self.mate_send,
            self.mate_recv,
            self.sum_send,
            self.sum_recv,
            self.own_sem,
        ) = sems
        self.half = parts.shape[1] // 2
        self.cols = slice(None) if cols is None else cols
        self.far = self.ring // 2
        self.started = []

    def device(self, offset, mate=False):
        core = 1 - self.core if mate else self.core
        return {"wide": 2 * chip_at(self.position + offset, self.ring) + core}

    def slot(self, offset, mate=False):
        core = 1 - self.core if mate else self.core
        return 2 * chip_at(self.position + offset, self.ring) + core

    def rows(self, part):
        return pl.ds(part * self.half, self.half)

    def greet(self):
        barrier = pltpu.get_barrier_semaphore()
        for where in (self.device(-1), self.device(1), self.device(0, True)):
            pl.semaphore_signal(
                barrier, inc=1, device_id=where, device_id_type=pl.DeviceIdType.MESH
            )
        pl.semaphore_wait(barrier, 3)

    def start(self, source, target, send_sem, recv_sem, where):
        copy = pltpu.make_async_remote_copy(
            src_ref=source,
            dst_ref=target,
            send_sem=send_sem,
            recv_sem=recv_sem,
            device_id=where,
            device_id_type=pl.DeviceIdType.MESH,
        )
        copy.start()
        self.started.append(copy)

    def pass_on(self, lane, slot, part, where, source=None):
        target = self.blocks.at[slot, self.rows(part)]
        self.start(
            target if source is None else source,
            target,
            self.gather_send.at[lane, slot, part],
            self.gather_recv.at[slot, part],
            where,
        )

    def arrived(self, slot, part):
        target = self.blocks.at[slot, self.rows(part)]
        pltpu.make_async_remote_copy(
            src_ref=target,
            dst_ref=target,
            send_sem=self.gather_send.at[0, slot, part],
            recv_sem=self.gather_recv.at[slot, part],
            device_id=self.device(1),
            device_id_type=pl.DeviceIdType.MESH,
        ).wait_recv()

    def send_own(self):
        slot = self.slot(0)
        keep = None
        own = self.blocks.at[slot]
        if self.own is not None:
            own = self.own
            keep = pltpu.make_async_copy(own, self.blocks.at[slot], self.own_sem)
            keep.start()
        first, second = own.at[self.rows(0)], own.at[self.rows(1)]
        self.pass_on(0, slot, 0, self.device(1), first)
        self.pass_on(1, slot, 1, self.device(-1), second)
        self.pass_on(2, slot, 0, self.device(0, True), first)
        self.pass_on(2, slot, 1, self.device(0, True), second)
        self.pass_on(0, slot, 1, self.device(1), second)
        self.pass_on(1, slot, 0, self.device(-1), first)
        return keep

    def receive(self, distance):
        mate = self.device(0, True)
        left, right = self.slot(-distance), self.slot(distance)
        if distance == self.far:
            for part in range(2):
                self.arrived(left, part)
                self.pass_on(2, left, part, mate)
            return
        further = distance < self.far - 1
        self.arrived(left, 0)
        self.pass_on(0, left, 0, self.device(1))
        self.pass_on(2, left, 0, mate)
        self.arrived(right, 1)
        self.pass_on(1, right, 1, self.device(-1))
        self.pass_on(2, right, 1, mate)
        self.arrived(left, 1)
        if further:
            self.pass_on(0, left, 1, self.device(1))
        self.pass_on(2, left, 1, mate)
        self.arrived(right, 0)
        if further:
            self.pass_on(1, right, 0, self.device(-1))
        self.pass_on(2, right, 0, mate)

    def receive_mate(self, offset):
        for part in range(2):
            self.arrived(self.slot(offset, True), part)

    def share(self, offset):
        chip = chip_at(self.position + offset, self.ring)
        self.start(
            self.parts.at[self.slot(offset, True), :, self.cols],
            self.from_mate.at[chip, :, self.cols],
            self.mate_send.at[chip],
            self.mate_recv.at[chip],
            self.device(0, True),
        )

    def shared(self, offset):
        chip = chip_at(self.position + offset, self.ring)
        pltpu.make_async_remote_copy(
            src_ref=self.parts.at[self.slot(offset), :, self.cols],
            dst_ref=self.from_mate.at[chip, :, self.cols],
            send_sem=self.mate_send.at[chip],
            recv_sem=self.mate_recv.at[chip],
            device_id=self.device(0, True),
            device_id_type=pl.DeviceIdType.MESH,
        ).wait_recv()

    def chip_sum(self, offset, rows):
        chip = chip_at(self.position + offset, self.ring)
        return self.parts[self.slot(offset), rows, self.cols].astype(
            jnp.float32
        ) + self.from_mate[chip, rows, self.cols].astype(jnp.float32)

    def send_sum(self, way, distance, part):
        offset = distance if way == 0 else -distance
        begins = self.far if part == way else self.far - 1
        slot = self.slot(offset)
        if distance < begins:
            self.sum_arrived(way, distance, part)

        def chunk(i, carry):
            here = pl.ds(pl.multiple_of(i * 16, 16), 16)
            there = pl.ds(pl.multiple_of(part * self.half + i * 16, 16), 16)
            total = self.chip_sum(offset, there)
            if distance < begins:
                total += self.incoming[way, distance, part, here, self.cols].astype(jnp.float32)
            self.parts[slot, there, self.cols] = total.astype(jnp.bfloat16)
            return carry

        lax.fori_loop(0, self.half // 16, chunk, 0)
        self.start(
            self.parts.at[slot, self.rows(part), self.cols],
            self.incoming.at[way, distance - 1, part, :, self.cols],
            self.sum_send.at[way, distance - 1, part],
            self.sum_recv.at[way, distance - 1, part],
            self.device(1 if way == 0 else -1),
        )

    def sum_arrived(self, way, distance, part):
        target = self.incoming.at[way, distance, part, :, self.cols]
        pltpu.make_async_remote_copy(
            src_ref=target,
            dst_ref=target,
            send_sem=self.sum_send.at[way, distance, part],
            recv_sem=self.sum_recv.at[way, distance, part],
            device_id=self.device(1),
            device_id_type=pl.DeviceIdType.MESH,
        ).wait_recv()

    def run(self, first, second, before, after_far):
        def compute(chip):
            first(chip)
            second(chip)

        keep = self.send_own()
        keep.wait()
        self.receive_mate(0)
        compute(chip_at(self.position, self.ring))
        self.share(0)
        for distance in range(1, self.far):
            self.receive(distance)
            for offset in (-distance, distance):
                self.receive_mate(offset)
                compute(chip_at(self.position + offset, self.ring))
                self.share(offset)
            if distance == self.far - 1:
                self.first_sums()
        self.receive(self.far)
        self.receive_mate(self.far)
        farthest = chip_at(self.position + self.far, self.ring)
        first(farthest)
        before()
        second(farthest)
        self.share(self.far)
        self.far_sums()
        after_far()
        self.last_sums()

    def start_sums(self, compute):
        compute(chip_at(self.position + self.far, self.ring))
        self.share(self.far)
        for distance in range(self.far - 1, 0, -1):
            for offset in (-distance, distance):
                compute(chip_at(self.position + offset, self.ring))
                self.share(offset)
            if distance == self.far - 1:
                self.far_sums()
                self.first_sums()
        compute(chip_at(self.position, self.ring))
        self.share(0)

    def first_sums(self):
        distance = self.far - 1
        self.shared(distance)
        self.send_sum(0, distance, 1)
        self.shared(-distance)
        self.send_sum(1, distance, 0)

    def far_sums(self):
        self.shared(self.far)
        self.send_sum(0, self.far, 0)
        self.send_sum(1, self.far, 1)

    def last_sums(self):
        for distance in range(self.far - 1, 0, -1):
            if distance < self.far - 1:
                self.shared(distance)
                self.shared(-distance)
            self.send_sum(0, distance, 0)
            self.send_sum(1, distance, 1)
            if distance < self.far - 1:
                self.send_sum(0, distance, 1)
                self.send_sum(1, distance, 0)

    def finish(self, result):
        self.shared(0)
        for part in range(2):
            for way in range(2):
                self.sum_arrived(way, 0, part)

            def chunk(i, carry):
                here = pl.ds(pl.multiple_of(i * 16, 16), 16)
                there = pl.ds(pl.multiple_of(part * self.half + i * 16, 16), 16)
                total = self.chip_sum(0, there)
                for way in range(2):
                    total += self.incoming[way, 0, part, here, self.cols].astype(jnp.float32)
                result[there, self.cols] = total.astype(result.dtype)
                return carry

            lax.fori_loop(0, self.half // 16, chunk, 0)

    def drain(self):
        for copy in self.started:
            copy.wait_send()


def sum_scratch(wide_count, rows, width):
    ring = wide_count // 2
    far = ring // 2
    dma = pltpu.SemaphoreType.DMA
    return [
        pltpu.VMEM((wide_count, rows, width), jnp.bfloat16),
        pltpu.VMEM((ring, rows, width), jnp.bfloat16),
        pltpu.VMEM((2, far, 2, rows // 2, width), jnp.bfloat16),
        dma((ring,)),
        dma((ring,)),
        dma((2, far, 2)),
        dma((2, far, 2)),
    ]


def exchange_scratch(wide_count, rows, width):
    dma = pltpu.SemaphoreType.DMA
    return [
        pltpu.VMEM((wide_count, rows, width), jnp.bfloat16),
        dma((3, wide_count, 2)),
        dma((wide_count, 2)),
        dma(()),
    ] + sum_scratch(wide_count, rows, width)


def load_padded(source, target, sem):
    filled = source.shape[0]
    copy = pltpu.make_async_copy(source, target.at[pl.ds(0, filled)], sem)
    copy.start()
    if filled < target.shape[0]:
        target[pl.ds(filled, target.shape[0] - filled)] = jnp.zeros(
            (target.shape[0] - filled, target.shape[1]), target.dtype
        )
    return copy


def pair_rows(ref, chip):
    block = ref[pl.ds(2 * chip, 2)]
    return block.reshape(2 * block.shape[1], block.shape[2])


def set_pair(ref, chip, cols, value):
    rows = ref.shape[1]
    ref[2 * chip, :, cols] = value[:rows].astype(ref.dtype)
    ref[2 * chip + 1, :, cols] = value[rows:].astype(ref.dtype)


def tiles(count, tile, body, start=0):
    def step(i, carry):
        body(pl.ds(pl.multiple_of(start + i * tile, tile), tile))
        return carry

    lax.fori_loop(0, count // tile, step, 0)


class LineExchange:
    def __init__(self, narrow_count):
        self.count = narrow_count
        self.mine = lax.axis_index("narrow")
        self.started = []

    def peer(self, offset):
        return (self.mine + offset) % self.count

    def greet(self, extra=0):
        barrier = pltpu.get_barrier_semaphore()
        for offset in range(1, self.count):
            pl.semaphore_signal(
                barrier,
                inc=1,
                device_id={"narrow": self.peer(offset)},
                device_id_type=pl.DeviceIdType.MESH,
            )
        pl.semaphore_wait(barrier, self.count - 1 + extra)

    def copy(self, source, target, send_sem, recv_sem, where):
        return pltpu.make_async_remote_copy(
            src_ref=source,
            dst_ref=target,
            send_sem=send_sem,
            recv_sem=recv_sem,
            device_id={"narrow": where},
            device_id_type=pl.DeviceIdType.MESH,
        )

    def send(self, offset, source, landing, send_sems, recv_sems):
        peer = self.peer(offset)
        copy = self.copy(
            source, landing.at[self.mine], send_sems.at[offset - 1], recv_sems.at[self.mine], peer
        )
        copy.start()
        self.started.append(copy)

    def arrived(self, offset, landing, send_sems, recv_sems):
        peer = self.peer(offset)
        self.copy(
            landing.at[peer], landing.at[peer], send_sems.at[offset - 1], recv_sems.at[peer], peer
        ).wait_recv()

    def drain(self):
        for copy in self.started:
            copy.wait_send()


class LineSum:
    def __init__(self, line, view, landing, send_sems, recv_sems):
        self.line, self.view, self.landing = line, view, landing
        self.send_sems, self.recv_sems = send_sems, recv_sems
        self.last = line.count - 1

    def reaches(self, way, offset):
        here = self.line.mine
        return here + offset <= self.last if way == 0 else here - offset >= 0

    def follows(self, way):
        here = self.line.mine
        return here > 0 if way == 0 else here < self.last

    def target(self, way, offset):
        return self.line.mine + offset if way == 0 else self.line.mine - offset

    def copy(self, way, offset):
        return self.line.copy(
            self.view(self.target(way, offset)),
            self.landing.at[way, offset - 1],
            self.send_sems.at[way, offset - 1],
            self.recv_sems.at[way, offset - 1],
            self.line.mine + 1 if way == 0 else self.line.mine - 1,
        )

    def arrived(self, way, offset):
        landing = self.landing.at[way, offset]
        self.line.copy(
            landing,
            landing,
            self.send_sems.at[way, offset],
            self.recv_sems.at[way, offset],
            self.line.mine,
        ).wait_recv()

    def add(self, way, offset):
        held = self.view(self.target(way, offset))

        def chunk(i, carry):
            some = pl.ds(pl.multiple_of(i * 16, 16), 16)
            held[some] = (
                held[some].astype(jnp.float32)
                + self.landing[way, offset, some].astype(jnp.float32)
            ).astype(jnp.bfloat16)
            return carry

        lax.fori_loop(0, self.landing.shape[2] // 16, chunk, 0)

    def begin(self, offset):
        for way in range(2):

            @pl.when(self.reaches(way, offset) & jnp.logical_not(self.follows(way)))
            def _():
                self.copy(way, offset).start()

    def step(self, offset):
        for way in range(2):

            @pl.when(self.reaches(way, offset) & self.follows(way))
            def _():
                self.arrived(way, offset)
                self.add(way, offset)
                self.copy(way, offset).start()

    def finish(self, result):
        held = self.view(self.line.mine)
        count = self.landing.shape[2] // 16

        def begin(i, carry):
            some = pl.ds(pl.multiple_of(i * 16, 16), 16)
            result[some] = held[some].astype(result.dtype)
            return carry

        lax.fori_loop(0, count, begin, 0)
        for way in range(2):

            @pl.when(self.follows(way))
            def _():
                self.arrived(way, 0)

                def chunk(i, carry):
                    some = pl.ds(pl.multiple_of(i * 16, 16), 16)
                    result[some] += self.landing[way, 0, some].astype(result.dtype)
                    return carry

                lax.fori_loop(0, count, chunk, 0)

    def drain(self):
        for offset in range(1, self.last + 1):
            for way in range(2):

                @pl.when(self.reaches(way, offset))
                def _():
                    self.copy(way, offset).wait_send()


class LineGather:
    def __init__(self, line, view, send_sems, recv_sems):
        self.line, self.view = line, view
        self.send_sems, self.recv_sems = send_sems, recv_sems
        self.last = line.count - 1

    def copy(self, way, block):
        target = self.view(block)
        here = self.line.mine
        return self.line.copy(
            target,
            target,
            self.send_sems.at[way, block],
            self.recv_sems.at[block],
            here + 1 if way == 0 else here - 1,
        )

    def goes(self, way):
        return self.line.mine < self.last if way == 0 else self.line.mine > 0

    def has(self, way, step):
        here = self.line.mine
        return here - step >= 0 if way == 0 else here + step <= self.last

    def block(self, way, step):
        return self.line.mine - step if way == 0 else self.line.mine + step

    def send_own(self):
        for way in range(2):

            @pl.when(self.goes(way))
            def _():
                self.copy(way, self.line.mine).start()

    def step(self, step):
        for way in range(2):

            @pl.when(self.has(way, step))
            def _():
                self.copy(way, self.block(way, step)).wait_recv()

                @pl.when(self.goes(way))
                def _():
                    self.copy(way, self.block(way, step)).start()

    def each(self, step, body):
        for way in range(2):

            @pl.when(self.has(way, step))
            def _():
                body(self.block(way, step))

    def drain(self):
        for way in range(2):
            for step in range(self.last + 1):

                @pl.when(self.has(way, step) & self.goes(way))
                def _():
                    self.copy(way, self.block(way, step)).wait_send()


def greet_plane(plane):
    barrier = pltpu.get_barrier_semaphore()
    for where in (plane.device(-1), plane.device(1), plane.device(0, True)):
        pl.semaphore_signal(barrier, inc=1, device_id=where, device_id_type=pl.DeviceIdType.MESH)


def geglu_forward_kernel(
    wide_count,
    narrow_count,
    rows_all,
    expand,
    reduce,
    shift,
    hidden,
    cotangent,
    reduce_shift,
    gain,
    norm_shift,
    reduce_out,
    active_out,
    slope_out,
    gelu_out,
    layer_output,
    sum_grad,
    feed_grad,
    row_sums,
    feed,
    blocks,
    parts,
    from_mate,
    incoming,
    mate_send,
    mate_recv,
    sum_send,
    sum_recv,
    expand_mat,
    reduce_mat,
    active,
    slope,
    gelu,
    load_sems,
    keep_sems,
    reduce_send,
    reduce_recv,
    late_mate_send,
    late_mate_recv,
    late_sum_send,
    late_sum_recv,
):
    sems = (None, None, mate_send, mate_recv, sum_send, sum_recv, None)
    late_sems = (None, None, late_mate_send, late_mate_recv, late_sum_send, late_sum_recv, None)
    line = LineExchange(narrow_count)
    filled, cols = reduce.shape
    width = rows_all.shape[2]
    upper = (2 * line.mine) // narrow_count
    late = pl.multiple_of((1 - upper) * (width - cols), cols)
    early = pl.multiple_of(upper * cols, cols)
    plane = PlaneExchange(
        wide_count, None, None, parts, from_mate, incoming, sems, pl.ds(early, width - cols)
    )
    late_plane = PlaneExchange(
        wide_count, None, None, parts, from_mate, incoming, late_sems, pl.ds(late, cols)
    )
    loads = [
        load_padded(expand.at[0], expand_mat.at[0], load_sems.at[0]),
        load_padded(expand.at[1], expand_mat.at[1], load_sems.at[1]),
        pltpu.make_async_copy(rows_all, blocks, load_sems.at[4]),
    ]
    loads[2].start()

    def reduce_cols(block):
        return reduce_mat.at[
            pl.ds(0, filled), pl.ds(pl.multiple_of(block * cols, cols), cols)
        ]

    line_reduce = LineGather(line, reduce_cols, reduce_send, reduce_recv)
    own_reduce = pltpu.make_async_copy(reduce, reduce_cols(line.mine), load_sems.at[2])
    own_reduce.start()
    if filled < reduce_mat.shape[0]:
        reduce_mat[filled:] = jnp.zeros(
            (reduce_mat.shape[0] - filled, reduce_mat.shape[1]), reduce_mat.dtype
        )
    greet_plane(plane)
    line.greet(3)
    own_reduce.wait()
    line_reduce.send_own()
    kept = []
    waiting = list(loads)

    def compute(chip):
        while waiting:
            waiting.pop().wait()

        def units(cols):
            rows = pair_rows(blocks, chip)
            gate = dot(rows, expand_mat[0, cols], ((1,), (1,))) + shift[0:1, cols]
            upper = dot(rows, expand_mat[1, cols], ((1,), (1,))) + shift[1:2, cols]
            factor = math.sqrt(2 / math.pi)
            square = gate * gate
            bend = jnp.tanh(factor * gate * (1 + 0.044715 * square))
            value = 0.5 * gate * (1 + bend)
            pull = 0.5 * (1 + bend) + 0.5 * gate * (1 - bend * bend) * factor * (
                1 + 3 * 0.044715 * square
            )
            set_pair(active, chip, cols, value * upper)
            set_pair(slope, chip, cols, pull * upper)
            set_pair(gelu, chip, cols, value)

        tiles(active.shape[2], 256, units)

        pair = pl.ds(2 * chip, 2)
        for index, (source, target) in enumerate(
            ((active, active_out), (slope, slope_out), (gelu, gelu_out))
        ):
            copy = pltpu.make_async_copy(
                source.at[pair], target.at[pair], keep_sems.at[chip, index]
            )
            copy.start()
            kept.append(copy)

    def compute_sums(start, count):
        def compute(chip):
            def outputs(some):
                part = dot(pair_rows(active, chip), reduce_mat[:, some], ((1,), (0,)))
                set_pair(parts, chip, some, part)

            tiles(count, 256, outputs, start)

        return compute

    offsets = [0]
    for distance in range(1, plane.far):
        offsets += [-distance, distance]
    offsets.append(plane.far)
    chips = [chip_at(plane.position + offset, plane.ring) for offset in offsets]
    each = -(-len(chips) // (narrow_count - 2))
    for step in range(1, narrow_count - 1):
        if step == 1:
            compute(chips.pop(0))
        for _ in range(min(each, len(chips))):
            compute(chips.pop(0))
        line_reduce.step(step)
    plane.start_sums(compute_sums(early, width - cols))
    line_reduce.step(narrow_count - 1)
    keep_reduce = pltpu.make_async_copy(
        reduce_mat.at[pl.ds(0, filled)], reduce_out, load_sems.at[3]
    )
    keep_reduce.start()
    late_plane.start_sums(compute_sums(late, cols))
    plane.last_sums()
    late_plane.last_sums()
    plane.finish(feed)
    late_plane.finish(feed)

    row_sums[...] = jnp.zeros_like(row_sums)

    def norm_rows(i, carry):
        some = pl.ds(pl.multiple_of(i * 16, 16), 16)
        result, normed, inverse = normalize(
            residual_scale * hidden[some] + feed[some] + reduce_shift[...],
            gain[...],
            norm_shift[...],
        )
        layer_output[some] = result.astype(jnp.bfloat16)
        upstream = cotangent[some].astype(jnp.float32)
        total = normalize_back(upstream, normed, inverse, gain[...])
        sum_grad[some] = total
        feed_grad[some] = total.astype(jnp.bfloat16)
        row_sums[0:1] += jnp.sum(upstream * normed, axis=0, keepdims=True)
        row_sums[1:2] += jnp.sum(upstream, axis=0, keepdims=True)
        row_sums[2:3] += jnp.sum(total, axis=0, keepdims=True)
        return carry

    lax.fori_loop(0, rows_all.shape[1] // 16, norm_rows, 0)
    plane.drain()
    late_plane.drain()
    keep_reduce.wait()
    line_reduce.drain()
    for copy in kept:
        copy.wait()


def geglu_forward(
    wide_count,
    narrow_count,
    rows_all,
    expand,
    reduce_weight,
    shift,
    hidden,
    cotangent,
    reduce_shift,
    gain,
    norm_shift,
):
    _, rows, width = rows_all.shape
    padded = shift.shape[1]
    anywhere = pl.BlockSpec(memory_space=pl.ANY)
    vmem = pl.BlockSpec(memory_space=pltpu.VMEM)
    kept = jax.ShapeDtypeStruct((wide_count, rows, padded), jnp.bfloat16)
    scratch = [pltpu.VMEM((rows, width), jnp.float32)]
    scratch.append(pltpu.VMEM((wide_count, rows, width), jnp.bfloat16))
    scratch += sum_scratch(wide_count, rows, width) + [
        pltpu.VMEM((2, padded, width), jnp.bfloat16),
        pltpu.VMEM((padded, width), jnp.bfloat16),
        pltpu.VMEM((wide_count, rows, padded), jnp.bfloat16),
        pltpu.VMEM((wide_count, rows, padded), jnp.bfloat16),
        pltpu.VMEM((wide_count, rows, padded), jnp.bfloat16),
        pltpu.SemaphoreType.DMA((5,)),
        pltpu.SemaphoreType.DMA((wide_count // 2, 3)),
        pltpu.SemaphoreType.DMA((2, narrow_count)),
        pltpu.SemaphoreType.DMA((narrow_count,)),
    ] + sum_scratch(wide_count, rows, width)[3:]
    return pl.pallas_call(
        functools.partial(geglu_forward_kernel, wide_count, narrow_count),
        out_shape=(
            jax.ShapeDtypeStruct((reduce_weight.shape[0], width), jnp.bfloat16),
            kept,
            kept,
            kept,
            jax.ShapeDtypeStruct((rows, width), jnp.bfloat16),
            jax.ShapeDtypeStruct((rows, width), jnp.float32),
            jax.ShapeDtypeStruct((rows, width), jnp.bfloat16),
            jax.ShapeDtypeStruct((3, width), jnp.float32),
        ),
        in_specs=[anywhere] * 3 + [vmem] * 6,
        out_specs=(anywhere,) * 4 + (vmem,) * 4,
        scratch_shapes=scratch,
        compiler_params=pltpu.CompilerParams(
            collective_id=1, has_side_effects=True, vmem_limit_bytes=kernel_memory
        ),
        cost_estimate=pl.CostEstimate(
            flops=6 * wide_count * rows * padded * width, bytes_accessed=200 * 2**20, transcendentals=0
        ),
        name="geglu_forward",
    )(
        rows_all,
        expand,
        reduce_weight,
        shift,
        hidden,
        cotangent,
        reduce_shift,
        gain,
        norm_shift,
    )


def geglu_backward_kernel(
    wide_count,
    narrow_count,
    own,
    expand,
    reduce,
    slope_in,
    gelu_in,
    active_in,
    rows_in,
    reduce_grad,
    expand_part,
    hidden_grad,
    unit_sums,
    blocks,
    gather_send,
    gather_recv,
    own_sem,
    parts,
    from_mate,
    incoming,
    mate_send,
    mate_recv,
    sum_send,
    sum_recv,
    expand_mat,
    reduce_mat,
    slope,
    gelu,
    active,
    rows_all,
    staged,
    load_sems,
    keep_sems,
    line_in,
    line_send,
    line_recv,
):
    sems = (gather_send, gather_recv, mate_send, mate_recv, sum_send, sum_recv, own_sem)
    plane = PlaneExchange(wide_count, own, blocks, parts, from_mate, incoming, sems)
    loads = [
        load_padded(expand.at[0], expand_mat.at[0], load_sems.at[0]),
        load_padded(expand.at[1], expand_mat.at[1], load_sems.at[1]),
        load_padded(reduce, reduce_mat, load_sems.at[2]),
        pltpu.make_async_copy(slope_in, slope, load_sems.at[3]),
        pltpu.make_async_copy(gelu_in, gelu, load_sems.at[4]),
    ]
    late_loads = [
        pltpu.make_async_copy(active_in, active, load_sems.at[5]),
        pltpu.make_async_copy(rows_in, rows_all, load_sems.at[6]),
    ]
    for copy in loads[3:]:
        copy.start()
    unit_sums[...] = jnp.zeros_like(unit_sums)
    line = LineExchange(narrow_count)
    filled, line_cols = line_in.shape[2:]

    def line_part(block):
        return reduce_mat.at[
            pl.ds(0, filled), pl.ds(pl.multiple_of(block * line_cols, line_cols), line_cols)
        ]

    line_sum = LineSum(line, line_part, line_in, line_send, line_recv)
    greet_plane(plane)
    line.greet(3)
    for copy in late_loads:
        copy.start()
    kept = []
    waiting = list(loads)

    def compute(chip):
        while waiting:
            waiting.pop().wait()

        def units(cols):
            pulled = dot(pair_rows(blocks, chip), reduce_mat[cols], ((1,), (1,)))
            pair = pl.ds(2 * chip, 2)
            shape = pulled.shape
            gate_grad = pulled * slope[pair, :, cols].reshape(shape).astype(jnp.float32)
            upper_grad = pulled * gelu[pair, :, cols].reshape(shape).astype(jnp.float32)
            set_pair(slope, chip, cols, gate_grad)
            set_pair(gelu, chip, cols, upper_grad)
            unit_sums[0:1, cols] += jnp.sum(gate_grad, axis=0, keepdims=True)
            unit_sums[1:2, cols] += jnp.sum(upper_grad, axis=0, keepdims=True)

        tiles(slope.shape[2], 256, units)

    def compute_sums(chip):
        def outputs(cols):
            set_pair(
                parts,
                chip,
                cols,
                dot(pair_rows(slope, chip), expand_mat[0, :, cols], ((1,), (0,)))
                + dot(pair_rows(gelu, chip), expand_mat[1, :, cols], ((1,), (0,))),
            )

        tiles(parts.shape[2], 256, outputs)

    def product(left, right, start):
        tokens = left.shape[0] * left.shape[1]
        return dot(
            left[:, :, start : start + 256].reshape(tokens, 256),
            right[...].reshape(tokens, right.shape[2]),
            ((0,), (0,)),
        ).astype(jnp.bfloat16)

    def reduce_work():
        for copy in late_loads:
            copy.wait()

        def reduce_cols(index):
            cols = pl.ds(pl.multiple_of(index * line_cols, line_cols), line_cols)

            def units(some):
                tokens = active.shape[0] * active.shape[1]
                part = dot(
                    active[:, :, some].reshape(tokens, some.size),
                    blocks[:, :, cols].reshape(tokens, line_cols),
                    ((0,), (0,)),
                )
                reduce_mat[some, cols] = part.astype(jnp.bfloat16)

            tiles(active.shape[2], 256, units)

        for offset in range(narrow_count - 1, 0, -1):
            for way in range(2):

                @pl.when(line_sum.reaches(way, offset))
                def _():
                    reduce_cols(line_sum.target(way, offset))

            line_sum.begin(offset)
        reduce_cols(line.mine)

    def expand_work(left, start, target):
        def work():
            index = len(kept)
            if index >= 2:
                kept[index - 2].wait()
            staged[index % 2] = product(left, rows_all, start)
            stop = min(256, target.shape[0] - start)
            copy = pltpu.make_async_copy(
                staged.at[index % 2, pl.ds(0, stop)],
                target.at[pl.ds(start, stop)],
                keep_sems.at[index % 2],
            )
            copy.start()
            kept.append(copy)

        return work

    works = [
        expand_work(left, start, target)
        for left, target in ((slope, expand_part.at[0]), (gelu, expand_part.at[1]))
        for start in range(0, target.shape[0], 256)
    ]
    steps = [
        functools.partial(line_sum.step, offset) for offset in range(narrow_count - 2, 0, -1)
    ]
    third = len(works) // 3
    middle = (len(steps) + 1) // 2

    def many(calls):
        for call in calls:
            call()

    beside = functools.partial(many, steps[:middle] + works[:third])
    plane.run(compute, compute_sums, reduce_work, beside)
    many(works[third : 2 * third] + steps[middle:] + works[2 * third :])
    plane.finish(hidden_grad)
    plane.drain()
    line_sum.finish(reduce_grad)
    line_sum.drain()
    for copy in kept[-2:]:
        copy.wait()


def geglu_backward(
    wide_count,
    narrow_count,
    feed_grad,
    expand,
    reduce_full,
    slope,
    gelu,
    active,
    rows_all,
):
    rows, width = feed_grad.shape
    padded = slope.shape[2]
    anywhere = pl.BlockSpec(memory_space=pl.ANY)
    vmem = pl.BlockSpec(memory_space=pltpu.VMEM)
    scratch = exchange_scratch(wide_count, rows, width) + [
        pltpu.VMEM((2, padded, width), jnp.bfloat16),
        pltpu.VMEM((padded, width), jnp.bfloat16),
        pltpu.VMEM((wide_count, rows, padded), jnp.bfloat16),
        pltpu.VMEM((wide_count, rows, padded), jnp.bfloat16),
        pltpu.VMEM((wide_count, rows, padded), jnp.bfloat16),
        pltpu.VMEM((wide_count, rows, width), jnp.bfloat16),
        pltpu.VMEM((2, 256, width), jnp.bfloat16),
        pltpu.SemaphoreType.DMA((7,)),
        pltpu.SemaphoreType.DMA((2,)),
        pltpu.VMEM(
            (2, narrow_count - 1, reduce_full.shape[0], width // narrow_count), jnp.bfloat16
        ),
        pltpu.SemaphoreType.DMA((2, narrow_count - 1)),
        pltpu.SemaphoreType.DMA((2, narrow_count - 1)),
    ]
    return pl.pallas_call(
        functools.partial(geglu_backward_kernel, wide_count, narrow_count),
        out_shape=(
            jax.ShapeDtypeStruct(
                (reduce_full.shape[0], width // narrow_count), jnp.float32
            ),
            jax.ShapeDtypeStruct(expand.shape, jnp.bfloat16),
            jax.ShapeDtypeStruct((rows, width), jnp.float32),
            jax.ShapeDtypeStruct((2, padded), jnp.float32),
        ),
        in_specs=[anywhere] * 7,
        out_specs=(vmem, anywhere, vmem, vmem),
        scratch_shapes=scratch,
        compiler_params=pltpu.CompilerParams(
            collective_id=2, has_side_effects=True, vmem_limit_bytes=63 * 2**20
        ),
        cost_estimate=pl.CostEstimate(
            flops=12 * wide_count * rows * padded * width, bytes_accessed=200 * 2**20, transcendentals=0
        ),
        name="geglu_backward",
    )(feed_grad, expand, reduce_full, slope, gelu, active, rows_all)


def rotate_lanes(vectors, cosine, signed_sine):
    return vectors * cosine + pltpu.roll(vectors, vectors.shape[1] // 2, 1) * signed_sine


def attention_backward_kernel(
    wide_count,
    narrow_count,
    upper_grad,
    hidden_part,
    normed,
    inv_std,
    gain,
    merge,
    mixed,
    queries,
    keys,
    values,
    probs,
    cosine,
    signed_sine,
    triple,
    merge_grad,
    heads_sums,
    merge_sums,
    sum_grad,
    norm_sums,
    attended,
    upstream,
    outbound,
    probs_held,
    keys_turned,
    key_total,
    value_total,
    merge_out,
    merge_in,
    mixed_send,
    mixed_recv,
    merge_send,
    merge_recv,
    load_sems,
    parts,
    from_mate,
    incoming,
    mate_send,
    mate_recv,
    sum_send,
    sum_recv,
):
    sems = (None, None, mate_send, mate_recv, sum_send, sum_recv, None)
    plane = PlaneExchange(wide_count, None, None, parts, from_mate, incoming, sems)
    line = LineExchange(narrow_count)
    rows, width = sum_grad.shape
    own_cols = queries.shape[1]
    heads = own_cols // HDIM
    scale = HDIM ** (-0.5)

    def load(head):
        return pltpu.make_async_copy(
            probs.at[head], probs_held.at[head % 2], load_sems.at[head % 2]
        )

    load(0).start()
    greet_plane(plane)

    norm_sums[...] = jnp.zeros_like(norm_sums)
    merge_sums[...] = jnp.zeros_like(merge_sums)

    def norm_rows(i, carry):
        some = pl.ds(pl.multiple_of(i * 16, 16), 16)
        hidden_grad = residual_scale * upper_grad[some] + hidden_part[some]
        norm_sums[0:1] += jnp.sum(hidden_grad * normed[some], axis=0, keepdims=True)
        norm_sums[1:2] += jnp.sum(hidden_grad, axis=0, keepdims=True)
        total = normalize_back(hidden_grad, normed[some], inv_std[some], gain[...])
        sum_grad[some] = total
        merge_sums[...] += jnp.sum(total, axis=0, keepdims=True)
        attended[some] = total.astype(jnp.bfloat16)
        return carry

    lax.fori_loop(0, rows // 16, norm_rows, 0)
    line.greet(3)

    def mixed_part(target, where):
        part = dot(
            attended[...],
            merge[pl.ds(pl.multiple_of(where * own_cols, own_cols), own_cols)],
            ((1,), (1,)),
        )
        target[...] = part.astype(jnp.bfloat16)

    for offset in range(1, narrow_count):
        place = line.peer(offset)
        mixed_part(outbound.at[offset - 1], place)
        line.send(offset, outbound.at[offset - 1], upstream, mixed_send, mixed_recv)
    mixed_part(upstream.at[line.mine], line.mine)

    block = parts.shape[1]

    def merge_rows(i, carry):
        cols = pl.ds(pl.multiple_of(i * block, block), block)
        parts[i] = dot(mixed[:, cols], attended[...], ((0,), (0,))).astype(jnp.bfloat16)
        return carry

    lax.fori_loop(0, wide_count, merge_rows, 0)
    for offset in range(plane.ring):
        plane.share(offset)
    plane.first_sums()
    plane.far_sums()
    plane.last_sums()
    plane.finish(merge_out)
    count = merge_grad.shape[0]

    def z_rows(where):
        return pl.ds(pl.multiple_of(where * count, count), count)

    for offset in range(1, narrow_count):
        line.send(
            offset, merge_out.at[z_rows(line.peer(offset))], merge_in, merge_send, merge_recv
        )
    for offset in range(1, narrow_count):
        line.arrived(offset, upstream, mixed_send, mixed_recv)

    def one_head(head):
        cols = pl.ds(head * HDIM, HDIM)
        load(head).wait()
        if head + 1 < heads:
            load(head + 1).start()
        held = probs_held.at[head % 2]
        keys_turned[...] = keys[:, cols].astype(jnp.float32).T.astype(jnp.bfloat16)
        key_total[...] = jnp.zeros_like(key_total)
        value_total[...] = jnp.zeros_like(value_total)

        def chunk(i, carry):
            here = pl.ds(pl.multiple_of(i * rows, rows), rows)
            weights_low = held[:, here]
            up = upstream[i, :, cols]
            pulled = dot(values[:, cols], up, ((1,), (1,)))
            weights = weights_low.astype(jnp.float32)
            scaled = weights * pulled
            change = (scaled - weights * jnp.sum(scaled, axis=0, keepdims=True)).astype(
                jnp.bfloat16
            )
            key_total[...] += dot(change, queries[here, cols], ((1,), (0,)))
            value_total[...] += dot(weights_low, up, ((1,), (0,)))
            query_grad = dot(keys_turned[...], change, ((1,), (0,))).T * scale
            triple[here, cols] = rotate_lanes(
                query_grad, cosine[here], signed_sine[here]
            ).astype(jnp.bfloat16)
            return carry

        lax.fori_loop(0, narrow_count, chunk, 0)

        def ending(i, carry):
            here = pl.ds(pl.multiple_of(i * rows, rows), rows)
            triple[here, pl.ds(own_cols + head * HDIM, HDIM)] = rotate_lanes(
                key_total[here] * scale, cosine[here], signed_sine[here]
            ).astype(jnp.bfloat16)
            triple[here, pl.ds(2 * own_cols + head * HDIM, HDIM)] = value_total[here].astype(
                jnp.bfloat16
            )
            return carry

        lax.fori_loop(0, narrow_count, ending, 0)

    for head in range(heads):
        one_head(head)

    def column_sums(cols):
        heads_sums[:, cols] = jnp.sum(
            triple[:, cols].astype(jnp.float32), axis=0, keepdims=True
        )

    tiles(3 * own_cols, 256, column_sums)
    summed = merge_out[z_rows(line.mine)].astype(jnp.float32)
    for offset in range(1, narrow_count):
        line.arrived(offset, merge_in, merge_send, merge_recv)
        summed += merge_in[line.peer(offset)].astype(jnp.float32)
    merge_grad[...] = summed
    line.drain()
    plane.drain()


def attention_backward(
    wide_count,
    narrow_count,
    upper_grad,
    hidden_part,
    normed,
    inv_std,
    gain,
    merge_full,
    mixed,
    queries,
    keys,
    values,
    probs,
    cosine,
    signed_sine,
):
    rows, width = normed.shape
    bucket, own_cols = queries.shape
    block = width // wide_count
    count = block // narrow_count
    anywhere = pl.BlockSpec(memory_space=pl.ANY)
    vmem = pl.BlockSpec(memory_space=pltpu.VMEM)
    dma = pltpu.SemaphoreType.DMA
    return pl.pallas_call(
        functools.partial(attention_backward_kernel, wide_count, narrow_count),
        out_shape=(
            jax.ShapeDtypeStruct((bucket, 3 * own_cols), jnp.bfloat16),
            jax.ShapeDtypeStruct((count, width), jnp.float32),
            jax.ShapeDtypeStruct((1, 3 * own_cols), jnp.float32),
            jax.ShapeDtypeStruct((1, width), jnp.float32),
            jax.ShapeDtypeStruct((rows, width), jnp.float32),
            jax.ShapeDtypeStruct((2, width), jnp.float32),
        ),
        in_specs=[vmem] * 10 + [anywhere] + [vmem] * 2,
        out_specs=(vmem,) * 6,
        scratch_shapes=[
            pltpu.VMEM((rows, width), jnp.bfloat16),
            pltpu.VMEM((narrow_count, rows, own_cols), jnp.bfloat16),
            pltpu.VMEM((narrow_count - 1, rows, own_cols), jnp.bfloat16),
            pltpu.VMEM((2, bucket, bucket), jnp.bfloat16),
            pltpu.VMEM((HDIM, bucket), jnp.bfloat16),
            pltpu.VMEM((bucket, HDIM), jnp.float32),
            pltpu.VMEM((bucket, HDIM), jnp.float32),
            pltpu.VMEM((block, width), jnp.bfloat16),
            pltpu.VMEM((narrow_count, count, width), jnp.bfloat16),
            dma((narrow_count - 1,)),
            dma((narrow_count,)),
            dma((narrow_count - 1,)),
            dma((narrow_count,)),
            dma((2,)),
        ]
        + sum_scratch(wide_count, block, width),
        compiler_params=pltpu.CompilerParams(
            collective_id=3, has_side_effects=True, vmem_limit_bytes=kernel_memory
        ),
        cost_estimate=pl.CostEstimate(
            flops=60 * 10**9, bytes_accessed=200 * 2**20, transcendentals=0
        ),
        name="attention_backward",
    )(
        upper_grad,
        hidden_part,
        normed,
        inv_std,
        gain,
        merge_full,
        mixed,
        queries,
        keys,
        values,
        probs,
        cosine,
        signed_sine,
    )


def input_backward_kernel(
    wide_count,
    narrow_count,
    inputs,
    triple,
    heads_mat,
    small,
    sum_grad,
    input_part,
    heads_grad,
    small_out,
    line_parts,
    line_in,
    heads_out,
    heads_in,
    small_wide,
    small_sum,
    small_line,
    line_send,
    line_recv,
    heads_send,
    heads_recv,
    wide_send,
    wide_recv,
    small_send,
    small_recv,
    parts,
    from_mate,
    incoming,
    mate_send,
    mate_recv,
    sum_send,
    sum_recv,
):
    sems = (None, None, mate_send, mate_recv, sum_send, sum_recv, None)
    plane = PlaneExchange(wide_count, None, None, parts, from_mate, incoming, sems)
    line = LineExchange(narrow_count)
    rows, width = input_part.shape
    here = line.mine
    last = narrow_count - 1
    place = lax.axis_index("wide")

    def wide_peer(offset):
        return (place + offset) % wide_count

    barrier = pltpu.get_barrier_semaphore()
    for offset in range(1, wide_count):
        pl.semaphore_signal(
            barrier,
            inc=1,
            device_id={"wide": wide_peer(offset)},
            device_id_type=pl.DeviceIdType.MESH,
        )
    line.greet(wide_count - 1)

    def small_copy(offset, source, slot):
        return pltpu.make_async_remote_copy(
            src_ref=source,
            dst_ref=small_wide.at[slot],
            send_sem=wide_send.at[offset - 1],
            recv_sem=wide_recv.at[slot],
            device_id={"wide": wide_peer(offset)},
            device_id_type=pl.DeviceIdType.MESH,
        )

    small_copies = [
        small_copy(offset, small.at[wide_peer(offset)], place) for offset in range(1, wide_count)
    ]
    for copy in small_copies:
        copy.start()

    line_sum = LineSum(line, lambda target: line_parts.at[target], line_in, line_send, line_recv)

    def input_rows(index):
        some = pl.ds(pl.multiple_of(index * rows, rows), rows)

        def input_cols(cols):
            part = dot(triple[some], heads_mat[cols], ((1,), (1,)))
            line_parts[index, :, cols] = part.astype(jnp.bfloat16)

        tiles(width, 256, input_cols)

    for offset in range(last, 0, -1):
        for way in range(2):

            @pl.when(line_sum.reaches(way, offset))
            def _():
                input_rows(line_sum.target(way, offset))

        line_sum.begin(offset)
    input_rows(here)

    block = parts.shape[1]

    def heads_rows(i, carry):
        cols = pl.ds(pl.multiple_of(i * block, block), block)
        parts[i] = dot(inputs[:, cols], triple[...], ((0,), (0,))).astype(jnp.bfloat16)
        return carry

    lax.fori_loop(0, wide_count, heads_rows, 0)
    for offset in range(plane.ring):
        plane.share(offset)
    for offset in range(last - 1, last // 2, -1):
        line_sum.step(offset)
    plane.first_sums()
    plane.far_sums()

    for offset in range(1, wide_count):
        peer = wide_peer(offset)
        small_copy(offset, small_wide.at[peer], peer).wait_recv()
    small_wide[place] = small[place]
    total = small_wide[0]
    for index in range(1, wide_count):
        total += small_wide[index]
    small_sum[...] = total
    for offset in range(1, narrow_count):
        line.send(offset, small_sum.at[line.peer(offset)], small_line, small_send, small_recv)

    plane.last_sums()
    for offset in range(last // 2, 0, -1):
        line_sum.step(offset)
    plane.finish(heads_out)
    count = heads_grad.shape[0]

    def z_rows(where):
        return pl.ds(pl.multiple_of(where * count, count), count)

    for offset in range(1, narrow_count):
        line.send(
            offset, heads_out.at[z_rows(line.peer(offset))], heads_in, heads_send, heads_recv
        )
    heads_in[line.mine] = heads_out[z_rows(line.mine)]
    small_line[line.mine] = small_sum[line.mine]
    for offset in range(1, narrow_count):
        line.arrived(offset, small_line, small_send, small_recv)
    result = small_line[0]
    for index in range(1, narrow_count):
        result += small_line[index]
    small_out[...] = result

    line_sum.finish(input_part)

    def add_residual(i, carry):
        some = pl.ds(pl.multiple_of(i * 16, 16), 16)
        input_part[some] += residual_scale * sum_grad[some]
        return carry

    lax.fori_loop(0, rows // 16, add_residual, 0)
    for offset in range(1, narrow_count):
        line.arrived(offset, heads_in, heads_send, heads_recv)
    own_cols = triple.shape[1] // 3
    for index in range(narrow_count):
        for which in range(3):
            start = (which * narrow_count + index) * own_cols
            heads_grad[:, start : start + own_cols] = heads_in[
                index, :, which * own_cols : (which + 1) * own_cols
            ].astype(jnp.float32)
    line_sum.drain()
    for copy in small_copies:
        copy.wait_send()
    line.drain()
    plane.drain()


def input_backward(
    wide_count, narrow_count, inputs, triple_grad, heads_mat, small, sum_grad
):
    bucket, width = inputs.shape
    rows = bucket // narrow_count
    columns = triple_grad.shape[1]
    block = width // wide_count
    count = block // narrow_count
    vmem = pl.BlockSpec(memory_space=pltpu.VMEM)
    dma = pltpu.SemaphoreType.DMA
    lines = small.shape[2]
    return pl.pallas_call(
        functools.partial(input_backward_kernel, wide_count, narrow_count),
        out_shape=(
            jax.ShapeDtypeStruct((rows, width), jnp.float32),
            jax.ShapeDtypeStruct((count, narrow_count * columns), jnp.float32),
            jax.ShapeDtypeStruct((lines, 128), jnp.float32),
        ),
        in_specs=[vmem] * 5,
        out_specs=(vmem, vmem, vmem),
        scratch_shapes=[
            pltpu.VMEM((narrow_count, rows, width), jnp.bfloat16),
            pltpu.VMEM((2, narrow_count - 1, rows, width), jnp.bfloat16),
            pltpu.VMEM((block, columns), jnp.bfloat16),
            pltpu.VMEM((narrow_count, count, columns), jnp.bfloat16),
            pltpu.VMEM((wide_count, narrow_count, lines, 128), jnp.float32),
            pltpu.VMEM((narrow_count, lines, 128), jnp.float32),
            pltpu.VMEM((narrow_count, lines, 128), jnp.float32),
            dma((2, narrow_count - 1)),
            dma((2, narrow_count - 1)),
            dma((narrow_count - 1,)),
            dma((narrow_count,)),
            dma((wide_count - 1,)),
            dma((wide_count,)),
            dma((narrow_count - 1,)),
            dma((narrow_count,)),
        ]
        + sum_scratch(wide_count, block, columns),
        compiler_params=pltpu.CompilerParams(
            collective_id=4, has_side_effects=True, vmem_limit_bytes=kernel_memory
        ),
        cost_estimate=pl.CostEstimate(
            flops=80 * 10**9, bytes_accessed=200 * 2**20, transcendentals=0
        ),
        name="input_backward",
    )(inputs, triple_grad, heads_mat, small, sum_grad)


def greet_all(wide_count, narrow_count):
    barrier = pltpu.get_barrier_semaphore()
    for axis, count in (("wide", wide_count), ("narrow", narrow_count)):
        place = lax.axis_index(axis)
        for offset in range(1, count):
            pl.semaphore_signal(
                barrier,
                inc=1,
                device_id={axis: (place + offset) % count},
                device_id_type=pl.DeviceIdType.MESH,
            )
    pl.semaphore_wait(barrier, wide_count + narrow_count - 2)


def gather_kernel(
    wide_count,
    narrow_count,
    own,
    heads_weight,
    merge_weight,
    small,
    buckets,
    speeds,
    rows_out,
    heads_out,
    merge_out,
    small_out,
    triple,
    cosine,
    signed_sine,
    first_query,
    last_query,
    rows_all,
    heads_all,
    merge_own,
    small_all,
    rows_send,
    rows_recv,
    heads_send,
    heads_recv,
    merge_send,
    merge_recv,
    small_send,
    small_recv,
    wide_send,
    wide_recv,
    local_sems,
    out_sems,
    heads_ring_send,
    heads_ring_recv,
):
    ring_sems = (heads_ring_send, heads_ring_recv, None, None, None, None, None)
    heads_ring = PlaneExchange(wide_count, None, heads_all, heads_all, None, None, ring_sems)
    line = LineExchange(narrow_count)
    here = line.mine
    last = narrow_count - 1
    place = lax.axis_index("wide")
    slot = heads_ring.slot(0)
    rows, width = own.shape
    count = heads_weight.shape[0]
    columns = heads_all.shape[2]
    own_cols = columns // 3

    def z_rows(where):
        return pl.ds(pl.multiple_of(where * count, count), count)

    def head_cols(which, where):
        start = which * narrow_count * own_cols + where * own_cols
        return pl.ds(pl.multiple_of(start, own_cols), own_cols)

    line_rows = LineGather(line, lambda block: rows_all.at[block], rows_send, rows_recv)

    keep_rows = pltpu.make_async_copy(own, rows_all.at[here], local_sems.at[0])
    keep_rows.start()
    keeps = [
        pltpu.make_async_copy(
            heads_weight.at[:, head_cols(which, here)],
            heads_all.at[slot, z_rows(here), pl.ds(which * own_cols, own_cols)],
            local_sems.at[2 + which],
        )
        for which in range(3)
    ]
    keep_merge = pltpu.make_async_copy(
        merge_weight, merge_own.at[z_rows(here)], local_sems.at[1]
    )
    for copy in keeps + [keep_merge]:
        copy.start()
    small_all[place, here] = small[...]
    greet_all(wide_count, narrow_count)

    def heads_copy(offset, which, where, sender):
        return line.copy(
            heads_weight.at[:, head_cols(which, where)],
            heads_all.at[slot, z_rows(sender), pl.ds(which * own_cols, own_cols)],
            heads_send.at[offset - 1, which],
            heads_recv.at[sender, which],
            where,
        )

    def merge_copy(offset, where, sender):
        return line.copy(
            merge_weight,
            merge_own.at[z_rows(sender)],
            merge_send.at[offset - 1],
            merge_recv.at[sender],
            where,
        )

    def small_copy(offset, where, sender):
        return line.copy(
            small,
            small_all.at[place, sender],
            small_send.at[offset - 1],
            small_recv.at[sender],
            where,
        )

    started = []

    def start(copy):
        copy.start()
        started.append(copy)

    keep_rows.wait()
    line_rows.send_own()
    for offset in range(1, narrow_count):
        for which in range(3):
            start(heads_copy(offset, which, line.peer(offset), here))
    for offset in range(1, narrow_count):
        start(small_copy(offset, line.peer(offset), here))

    halfway = narrow_count * rows // 2
    joined = buckets[0]

    def tables(i, carry):
        some = pl.ds(pl.multiple_of(i * rows, rows), rows)
        place_in = i * rows + lax.broadcasted_iota(jnp.int32, (rows, 1), 0)
        second = jnp.where(place_in >= halfway, 1 - joined, 0)
        local = place_in - second * halfway
        reach = jnp.where(
            joined == 1,
            buckets[1] + buckets[2],
            jnp.where(second == 1, buckets[2], buckets[1]),
        )
        first_query[some] = jnp.where(local < reach, place_in - local, place_in)
        last_query[some] = jnp.where(
            (joined == 1) | (second == 1), 2 * halfway - 1, halfway - 1
        ) + jnp.zeros_like(place_in)
        angles = local.astype(jnp.float32) * speeds[...]
        lane = lax.broadcasted_iota(jnp.int32, (rows, HDIM), 1)
        cosine[some] = jnp.cos(angles)
        sine = jnp.sin(angles)
        signed_sine[some] = jnp.where(lane < HDIM // 2, sine, -sine)
        return carry

    lax.fori_loop(0, narrow_count, tables, 0)

    line_rows.step(1)
    for copy in keeps:
        copy.wait()
    for offset in range(1, narrow_count):
        for which in range(3):
            heads_copy(offset, which, line.peer(offset), line.peer(offset)).wait_recv()
    heads_ring.send_own()
    for offset in range(1, narrow_count):
        small_copy(offset, line.peer(offset), line.peer(offset)).wait_recv()

    def wide_copy(offset, sender):
        return pltpu.make_async_remote_copy(
            src_ref=small_all.at[sender],
            dst_ref=small_all.at[sender],
            send_sem=wide_send.at[offset - 1],
            recv_sem=wide_recv.at[sender],
            device_id={"wide": (place + offset) % wide_count},
            device_id_type=pl.DeviceIdType.MESH,
        )

    for offset in range(1, wide_count):
        start(wide_copy(offset, place))

    def project(block):
        def cols_step(cols):
            weight = heads_all[:, :, cols].reshape(width, cols.size)
            triple[pl.ds(pl.multiple_of(block * rows, rows), rows), cols] = dot(
                rows_all[block], weight, ((1,), (0,))
            )

        tiles(columns, 256, cols_step)

    def project_step(step):
        line_rows.each(step, project)

    def gather(ring, distance):
        ring.receive(distance)
        ring.receive_mate(-distance)
        if distance < ring.far:
            ring.receive_mate(distance)

    outs = []

    def keep_out(source, target):
        copy = pltpu.make_async_copy(source, target, out_sems.at[len(outs)])
        copy.start()
        outs.append(copy)

    for offset in range(1, narrow_count):
        start(merge_copy(offset, line.peer(offset), here))
    heads_ring.receive_mate(0)
    for distance in range(1, heads_ring.far):
        gather(heads_ring, distance)
    if last > 1:
        line_rows.step(2)
    gather(heads_ring, heads_ring.far)
    keep_out(heads_all, heads_out)
    project(here)
    for step in range(3, narrow_count):
        project_step(step - 2)
        line_rows.step(step)
    project_step(last - 1)
    project_step(last)
    keep_merge.wait()
    for offset in range(1, narrow_count):
        merge_copy(offset, line.peer(offset), line.peer(offset)).wait_recv()
    keep_out(merge_own, merge_out)
    keep_out(rows_all, rows_out)
    for offset in range(1, wide_count):
        wide_copy(offset, (place + offset) % wide_count).wait_recv()
    keep_out(small_all, small_out)
    line_rows.drain()
    for copy in started:
        copy.wait_send()
    heads_ring.drain()
    for copy in outs:
        copy.wait()


def gather_front(
    wide_count, narrow_count, layer_input, heads_weight, merge_weight, small, buckets, speeds
):
    rows, width = layer_input.shape
    count, all_columns = heads_weight.shape
    columns = all_columns // narrow_count
    block = count * narrow_count
    anywhere = pl.BlockSpec(memory_space=pl.ANY)
    vmem = pl.BlockSpec(memory_space=pltpu.VMEM)
    dma = pltpu.SemaphoreType.DMA
    lines = small.shape[0]
    shapes = (
        (narrow_count, rows, width),
        (wide_count, block, columns),
        (block, width),
        (wide_count, narrow_count, lines, 128),
    )
    far = narrow_count - 1
    bucket = narrow_count * rows
    table = jax.ShapeDtypeStruct((bucket, HDIM), jnp.float32)
    reach = jax.ShapeDtypeStruct((bucket, 1), jnp.int32)
    return pl.pallas_call(
        functools.partial(gather_kernel, wide_count, narrow_count),
        out_shape=tuple(jax.ShapeDtypeStruct(shape, jnp.bfloat16) for shape in shapes)
        + (jax.ShapeDtypeStruct((bucket, columns), jnp.float32), table, table, reach, reach),
        in_specs=[anywhere, anywhere, anywhere, vmem, pl.BlockSpec(memory_space=pltpu.SMEM), vmem],
        out_specs=(anywhere,) * 4 + (vmem,) * 5,
        scratch_shapes=[pltpu.VMEM(shape, jnp.bfloat16) for shape in shapes]
        + [
            dma((2, narrow_count)),
            dma((narrow_count,)),
            dma((far, 3)),
            dma((narrow_count, 3)),
            dma((far,)),
            dma((narrow_count,)),
            dma((far,)),
            dma((narrow_count,)),
            dma((wide_count - 1,)),
            dma((wide_count,)),
            dma((5,)),
            dma((4,)),
            dma((3, wide_count, 2)),
            dma((wide_count, 2)),
        ],
        compiler_params=pltpu.CompilerParams(
            collective_id=5, has_side_effects=True, vmem_limit_bytes=kernel_memory
        ),
        cost_estimate=pl.CostEstimate(
            flops=80 * 10**9, bytes_accessed=200 * 2**20, transcendentals=0
        ),
        name="gather_front",
    )(layer_input, heads_weight, merge_weight, small, buckets, speeds)


def attention_forward_kernel(
    wide_count,
    narrow_count,
    triple,
    heads_shift,
    cosine,
    signed_sine,
    first_query,
    last_query,
    own,
    merge,
    merge_shift,
    gain,
    shift,
    queries,
    keys,
    values,
    probs,
    mixed_out,
    hidden,
    hidden_low,
    normed,
    inv_std,
    merge_out,
    rows_out,
    merge_mat,
    probs_held,
    values_turned,
    outbound,
    mixed,
    mixed_send,
    mixed_recv,
    local_sems,
    ring_send,
    ring_recv,
    own_sem,
    rows_all,
    rows_send,
    rows_recv,
    rows_sem,
):
    line = LineExchange(narrow_count)
    ring_sems = (ring_send, ring_recv, None, None, None, None, own_sem)
    ring = PlaneExchange(wide_count, merge, merge_mat, merge_mat, None, None, ring_sems)
    rows_sems = (rows_send, rows_recv, None, None, None, None, rows_sem)
    rows_ring = PlaneExchange(wide_count, hidden_low, rows_all, rows_all, None, None, rows_sems)
    bucket, own_cols = queries.shape
    rows, width = own.shape
    heads = own_cols // HDIM
    scale = HDIM ** (-0.5)
    greet_plane(ring)
    line.greet(3)
    keep_own = ring.send_own()
    ring_steps = [functools.partial(ring.receive, step) for step in range(1, ring.far + 1)]

    def keep(head):
        return pltpu.make_async_copy(
            probs_held.at[head % 2], probs.at[head], local_sems.at[head % 2]
        )

    def mixed_copy(head, offset, where, sender):
        cols = pl.ds(pl.multiple_of(sender * own_cols + head * HDIM, HDIM), HDIM)
        return line.copy(
            outbound.at[where, :, pl.ds(head * HDIM, HDIM)],
            mixed.at[:, cols],
            mixed_send.at[offset - 1, head],
            mixed_recv.at[sender, head],
            where,
        )

    started = []
    for head in range(heads):
        cols = pl.ds(head * HDIM, HDIM)

        def turn(i, carry):
            here = pl.ds(pl.multiple_of(i * rows, rows), rows)
            for which, target in enumerate((queries, keys, values)):
                wanted = pl.ds(which * own_cols + head * HDIM, HDIM)
                part = triple[here, wanted] + heads_shift[:, wanted]
                if which < 2:
                    part = rotate_lanes(part, cosine[here], -signed_sine[here])
                else:
                    values_turned[:, here] = part.T.astype(jnp.bfloat16)
                target[here, cols] = part.astype(jnp.bfloat16)
            return carry

        lax.fori_loop(0, narrow_count, turn, 0)
        if head >= 2:
            keep(head - 2).wait()
        held = probs_held.at[head % 2]

        def chunk(i, carry):
            here = pl.ds(pl.multiple_of(i * rows, rows), rows)
            scores = dot(keys[:, cols], queries[here, cols], ((1,), (1,))) * scale
            token = i * rows + lax.broadcasted_iota(jnp.int32, (bucket, rows), 1)
            seen = (token >= first_query[...]) & (token <= last_query[...])
            scores = jnp.where(seen, scores, masked_value)
            expo = jnp.exp(scores - jnp.max(scores, axis=0, keepdims=True))
            weights = (expo * (1 / jnp.sum(expo, axis=0, keepdims=True))).astype(jnp.bfloat16)
            held[:, here] = weights
            mixed_part = dot(values_turned[...], weights, ((1,), (0,)))
            outbound[i, :, cols] = mixed_part.T.astype(jnp.bfloat16)
            return carry

        lax.fori_loop(0, narrow_count, chunk, 0)
        keep(head).start()
        for offset in range(1, narrow_count):
            copy = mixed_copy(head, offset, line.peer(offset), line.mine)
            copy.start()
            started.append(copy)
        if ring_steps and head >= heads - len(ring_steps):
            ring_steps.pop(0)()
    own_mixed = pltpu.make_async_copy(
        outbound.at[line.mine],
        mixed.at[:, pl.ds(pl.multiple_of(line.mine * own_cols, own_cols), own_cols)],
        local_sems.at[3],
    )
    own_mixed.start()
    own_mixed.wait()
    keep_own.wait()
    for step in ring_steps:
        step()
    for offset in range(ring.ring):
        ring.receive_mate(offset)
    keep_merge = pltpu.make_async_copy(merge_mat, merge_out, local_sems.at[2])
    keep_merge.start()
    for offset in range(1, narrow_count):
        for head in range(heads):
            mixed_copy(head, offset, line.peer(offset), line.peer(offset)).wait_recv()
    mixed_out[...] = mixed[...]

    def merge_cols(cols):
        hidden[:, cols] = (
            residual_scale * own[:, cols].astype(jnp.float32)
            + dot(mixed[...], merge_mat[:, :, cols].reshape(width, cols.size), ((1,), (0,)))
            + merge_shift[:, cols]
        )

    tiles(width, 256, merge_cols)

    def norm_rows(i, carry):
        some = pl.ds(pl.multiple_of(i * 16, 16), 16)
        result, centred, inverse = normalize(hidden[some], gain[...], shift[...])
        hidden[some] = result
        hidden_low[some] = result.astype(jnp.bfloat16)
        normed[some] = centred
        inv_std[some] = inverse
        return carry

    lax.fori_loop(0, rows // 16, norm_rows, 0)
    keep_rows = rows_ring.send_own()
    for step in range(1, rows_ring.far + 1):
        rows_ring.receive(step)
    for offset in range(rows_ring.ring):
        rows_ring.receive_mate(offset)
    keep_rows.wait()
    keep_rows = pltpu.make_async_copy(rows_all, rows_out, rows_sem)
    keep_rows.start()
    for head in range(max(heads - 2, 0), heads):
        keep(head).wait()
    for copy in started:
        copy.wait_send()
    ring.drain()
    rows_ring.drain()
    keep_merge.wait()
    keep_rows.wait()


def attention_forward(
    wide_count,
    narrow_count,
    triple,
    heads_shift,
    cosine,
    signed_sine,
    first_query,
    last_query,
    layer_input,
    merge_block,
    merge_shift,
    gain,
    shift,
):
    bucket, columns = triple.shape
    rows, width = layer_input.shape
    own_cols = columns // 3
    heads = own_cols // HDIM
    anywhere = pl.BlockSpec(memory_space=pl.ANY)
    vmem = pl.BlockSpec(memory_space=pltpu.VMEM)
    dma = pltpu.SemaphoreType.DMA

    def low_shape(*shape):
        return jax.ShapeDtypeStruct(shape, jnp.bfloat16)

    def wide_shape(*shape):
        return jax.ShapeDtypeStruct(shape, jnp.float32)

    return pl.pallas_call(
        functools.partial(attention_forward_kernel, wide_count, narrow_count),
        out_shape=(
            low_shape(bucket, own_cols),
            low_shape(bucket, own_cols),
            low_shape(bucket, own_cols),
            low_shape(heads, bucket, bucket),
            low_shape(rows, width),
            wide_shape(rows, width),
            low_shape(rows, width),
            wide_shape(rows, width),
            wide_shape(rows, 1),
            low_shape(wide_count, *merge_block.shape),
            low_shape(wide_count, rows, width),
        ),
        in_specs=[vmem] * 7 + [anywhere] + [vmem] * 3,
        out_specs=(vmem, vmem, vmem, anywhere) + (vmem,) * 5 + (anywhere,) * 2,
        scratch_shapes=[
            pltpu.VMEM((wide_count, *merge_block.shape), jnp.bfloat16),
            pltpu.VMEM((2, bucket, bucket), jnp.bfloat16),
            pltpu.VMEM((HDIM, bucket), jnp.bfloat16),
            pltpu.VMEM((narrow_count, rows, own_cols), jnp.bfloat16),
            pltpu.VMEM((rows, width), jnp.bfloat16),
            dma((narrow_count - 1, heads)),
            dma((narrow_count, heads)),
            dma((4,)),
            dma((3, wide_count, 2)),
            dma((wide_count, 2)),
            dma(()),
            pltpu.VMEM((wide_count, rows, width), jnp.bfloat16),
            dma((3, wide_count, 2)),
            dma((wide_count, 2)),
            dma(()),
        ],
        compiler_params=pltpu.CompilerParams(
            collective_id=6, has_side_effects=True, vmem_limit_bytes=kernel_memory
        ),
        cost_estimate=pl.CostEstimate(
            flops=60 * 10**9, bytes_accessed=200 * 2**20, transcendentals=0
        ),
        name="attention_forward",
    )(
        triple,
        heads_shift,
        cosine,
        signed_sine,
        first_query,
        last_query,
        layer_input,
        merge_block,
        merge_shift,
        gain,
        shift,
    )


def shards(
    layer_input,
    heads_weight,
    heads_bias,
    merge_weight,
    merge_bias,
    norm_gains,
    norm_shifts,
    expand_weight,
    expand_bias,
    reduce_weight,
    reduce_bias,
    joined,
    prefix,
    cotangent,
):
    tok_rows, model_width = layer_input.shape
    wide_count = lax.axis_size("wide")
    narrow_count = lax.axis_size("narrow")
    count = wide_count * narrow_count
    bucket_len = tok_rows * narrow_count
    own_heads = HEADS // narrow_count
    own_cols = own_heads * HDIM
    share = expand_weight.shape[2]
    narrow_index = lax.axis_index("narrow")
    smalls = (heads_bias, merge_bias, norm_gains, norm_shifts, expand_bias, reduce_bias)
    (
        rows_input,
        heads_mat,
        merge_block,
        small_all,
        triple,
        cosine,
        signed_sine,
        first_query,
        last_query,
    ) = gather_front(
        wide_count,
        narrow_count,
        layer_input,
        heads_weight,
        merge_weight,
        pack_small(smalls),
        jnp.concatenate([joined, prefix[0]]),
        jnp.asarray(rotary_speeds(HDIM)),
    )
    rows_input = rows_input.reshape(bucket_len, model_width)
    heads_mat = heads_mat.reshape(model_width, 3 * own_cols)
    heads_shift, merge_shift, gains, shifts, expand_shift, reduce_shift = unpack_small(
        small_all, smalls
    )
    own_shift = lax.dynamic_index_in_dim(
        heads_shift.reshape(3, narrow_count, own_cols), narrow_index, 1, keepdims=False
    ).reshape(1, -1)
    (
        queries,
        keys,
        values,
        probs_low,
        mixed,
        hidden,
        hidden_low,
        normed_one,
        inv_one,
        merge_full,
        rows_all,
    ) = attention_forward(
        wide_count,
        narrow_count,
        triple,
        own_shift,
        cosine,
        signed_sine,
        first_query,
        last_query,
        layer_input,
        merge_block,
        merge_shift.reshape(1, -1),
        gains[0].reshape(1, -1),
        shifts[0].reshape(1, -1),
    )

    tile_rows = -share % 16
    padded = -(-share // 256) * 256
    expand_low = jnp.pad(expand_weight.transpose(1, 2, 0), ((0, 0), (0, tile_rows), (0, 0)))
    expand_low, _ = lax.optimization_barrier((expand_low, small_all))
    expand_full = lax.all_gather(expand_low, "narrow", axis=2, tiled=True)
    reduce_low = jnp.pad(reduce_weight, ((0, tile_rows), (0, 0)))
    (
        reduce_full,
        active,
        slope,
        gelu,
        layer_output,
        sum_two_grad,
        feed_grad,
        row_sums,
    ) = geglu_forward(
        wide_count,
        narrow_count,
        rows_all,
        expand_full,
        reduce_low,
        jnp.pad(expand_shift, ((0, 0), (0, padded - share))),
        hidden,
        cotangent,
        reduce_shift.reshape(1, -1),
        gains[1].reshape(1, -1),
        shifts[1].reshape(1, -1),
    )
    reduce_weight_gradient, expand_part, hidden_part, unit_sums = geglu_backward(
        wide_count,
        narrow_count,
        feed_grad,
        expand_full,
        reduce_full,
        slope,
        gelu,
        active,
        rows_all,
    )
    expand_weight_gradient = (
        lax.psum_scatter(expand_part, "narrow", scatter_dimension=2, tiled=True)[:, :share]
        .astype(jnp.float32)
        .transpose(2, 0, 1)
    )
    (
        triple_grad,
        merge_weight_gradient,
        heads_sums,
        merge_sums,
        sum_one_grad,
        norm_one_sums,
    ) = attention_backward(
        wide_count,
        narrow_count,
        sum_two_grad,
        hidden_part,
        normed_one,
        inv_one,
        gains[0].reshape(1, -1),
        merge_full.reshape(model_width, model_width),
        mixed,
        queries,
        keys,
        values,
        probs_low,
        cosine,
        signed_sine,
    )

    mine_narrow = (jnp.arange(narrow_count) == narrow_index).astype(jnp.float32)
    mine_wide = (jnp.arange(wide_count) == lax.axis_index("wide")).astype(jnp.float32)
    heads_sums = heads_sums.reshape(3, 1, own_cols)
    heads_sums = (heads_sums * mine_narrow[None, :, None]).reshape(count, -1)
    merge_sums = merge_sums.reshape(count, -1)
    norm_sums = (
        jnp.stack([norm_one_sums[0], row_sums[0], norm_one_sums[1], row_sums[1]])
        .reshape(4, count, -1)
        .transpose(1, 0, 2)
        .reshape(count, -1)
    )
    expand_sums = unit_sums[:, :share]
    expand_sums = (
        expand_sums.reshape(2, narrow_count, -1).transpose(1, 0, 2).reshape(1, narrow_count, -1)
        * mine_wide[:, None, None]
    ).reshape(count, -1)
    reduce_sums = row_sums[2].reshape(1, narrow_count, -1)
    reduce_sums = jnp.broadcast_to(
        reduce_sums, (wide_count, narrow_count, reduce_sums.shape[2])
    ).reshape(count, -1)
    pieces = (heads_sums, merge_sums, norm_sums, expand_sums, reduce_sums)
    packed = jnp.concatenate(pieces, axis=1)
    packed = jnp.pad(packed, ((0, 0), (0, -packed.shape[1] % 1024)))
    input_gradient, heads_weight_gradient, summed = input_backward(
        wide_count,
        narrow_count,
        rows_input,
        triple_grad,
        heads_mat,
        packed.reshape(wide_count, narrow_count, -1, 128),
        sum_one_grad,
    )
    summed = summed.reshape(-1)
    ends = []
    start = 0
    for piece in pieces:
        ends.append(summed[start : start + piece.shape[1]])
        start += piece.shape[1]
    norm_ends = ends[2].reshape(4, -1)
    return (
        layer_output,
        input_gradient,
        heads_weight_gradient,
        ends[0],
        merge_weight_gradient,
        ends[1],
        norm_ends[:2],
        norm_ends[2:],
        expand_weight_gradient,
        ends[3].reshape(2, -1),
        reduce_weight_gradient[:share],
        ends[4],
    )


def solution(mesh):
    return jax.shard_map(
        shards,
        mesh=mesh,
        in_specs=(
            P(("wide", "narrow"), None),
            P(("wide", "narrow"), None),
            P(("wide", "narrow")),
            P(("wide", "narrow"), None),
            P(("wide", "narrow")),
            P(None, ("wide", "narrow")),
            P(None, ("wide", "narrow")),
            P("narrow", None, "wide"),
            P(None, ("wide", "narrow")),
            P("wide", "narrow"),
            P("narrow"),
            P("wide"),
            P("wide", None),
            P(("wide", "narrow"), None),
        ),
        out_specs=(
            P(("wide", "narrow"), None),
            P(("wide", "narrow"), None),
            P(("wide", "narrow"), None),
            P(("wide", "narrow")),
            P(("wide", "narrow"), None),
            P(("wide", "narrow")),
            P(None, ("wide", "narrow")),
            P(None, ("wide", "narrow")),
            P("narrow", None, "wide"),
            P(None, ("wide", "narrow")),
            P("wide", "narrow"),
            P("narrow"),
        ),
        check_vma=False,
    )
```

```python
import functools
import math

import jax
import jax.numpy as jnp
import numpy as np
from jax import lax
from jax.experimental import pallas as pl
from jax.experimental.pallas import tpu as pltpu
from jax.sharding import PartitionSpec as P

HEADS = 16
HDIM = 128


residual_scale = 48.0**0.5
norm_eps = 1e-05
masked_value = -1e30
kernel_memory = 60 * 2**20


def rotary_speeds(head_size):
    index = np.arange(head_size) % (head_size // 2)
    return (10000.0 ** (-2.0 * index / head_size)).astype(np.float32)[None]


def normalize(values, gain, shift):
    centre = jnp.mean(values, axis=-1, keepdims=True)
    centred = values - centre
    variance = jnp.mean(centred * centred, axis=-1, keepdims=True)
    inv_std = lax.rsqrt(variance + norm_eps)
    normed = centred * inv_std
    return (normed * gain + shift, normed, inv_std)


def normalize_back(upstream, normed, inv_std, gain):
    scaled = upstream * gain
    return inv_std * (
        scaled
        - jnp.mean(scaled, axis=-1, keepdims=True)
        - normed * jnp.mean(scaled * normed, axis=-1, keepdims=True)
    )


def dot(left, right, dims):
    return lax.dot_general(left, right, (dims, ((), ())), preferred_element_type=jnp.float32)


def low(values):
    return values.astype(jnp.bfloat16)


def small_rows(part):
    return part.reshape(-1, part.shape[-1]).shape[0], -(-part.shape[-1] // 128)


def pack_small(parts):
    pieces = []
    for part in parts:
        first, rows = small_rows(part)
        part = part.reshape(first, -1)
        part = jnp.pad(part, ((0, 0), (0, rows * 128 - part.shape[1])))
        pieces.append(part.reshape(first * rows, 128))
    packed = jnp.concatenate(pieces, axis=0)
    return jnp.pad(packed, ((0, -packed.shape[0] % 16), (0, 0)))


def unpack_small(everyone, parts):
    pieces = []
    start = 0
    for part in parts:
        first, rows = small_rows(part)
        piece = everyone[:, :, start : start + first * rows].astype(jnp.float32)
        piece = piece.reshape(piece.shape[:2] + (first, rows * 128))
        pieces.append(piece[..., : part.shape[-1]])
        start += first * rows

    def pairs(piece):
        return piece.reshape((-1,) + piece.shape[-2:]).transpose(1, 0, 2).reshape(2, -1)

    own_expand = lax.dynamic_index_in_dim(
        pieces[4], lax.axis_index("wide"), 0, keepdims=False
    )
    return (
        pieces[0].reshape(-1),
        pieces[1].reshape(-1),
        pairs(pieces[2]),
        pairs(pieces[3]),
        pairs(own_expand),
        pieces[5][0].reshape(-1),
    )


def ring_place(wide_count):
    ring = wide_count // 2
    mine = lax.axis_index("wide")
    chip = mine // 2
    core = mine % 2
    position = 2 * (chip // 2) + (chip % 2 + chip // 2) % 2
    return ring, position, core


def chip_at(position, ring):
    position = (position + 2 * ring) % ring
    return 2 * (position // 2) + (position + position // 2) % 2


class PlaneExchange:
    def __init__(self, wide_count, own, blocks, parts, from_mate, incoming, sems, cols=None):
        self.ring, self.position, self.core = ring_place(wide_count)
        self.own, self.blocks, self.parts = own, blocks, parts
        self.from_mate, self.incoming = from_mate, incoming
        (
            self.gather_send,
            self.gather_recv,
            self.mate_send,
            self.mate_recv,
            self.sum_send,
            self.sum_recv,
            self.own_sem,
        ) = sems
        self.half = parts.shape[1] // 2
        self.cols = slice(None) if cols is None else cols
        self.far = self.ring // 2
        self.started = []

    def device(self, offset, mate=False):
        core = 1 - self.core if mate else self.core
        return {"wide": 2 * chip_at(self.position + offset, self.ring) + core}

    def slot(self, offset, mate=False):
        core = 1 - self.core if mate else self.core
        return 2 * chip_at(self.position + offset, self.ring) + core

    def rows(self, part):
        return pl.ds(part * self.half, self.half)

    def greet(self):
        barrier = pltpu.get_barrier_semaphore()
        for where in (self.device(-1), self.device(1), self.device(0, True)):
            pl.semaphore_signal(
                barrier, inc=1, device_id=where, device_id_type=pl.DeviceIdType.MESH
            )
        pl.semaphore_wait(barrier, 3)

    def start(self, source, target, send_sem, recv_sem, where):
        copy = pltpu.make_async_remote_copy(
            src_ref=source,
            dst_ref=target,
            send_sem=send_sem,
            recv_sem=recv_sem,
            device_id=where,
            device_id_type=pl.DeviceIdType.MESH,
        )
        copy.start()
        self.started.append(copy)

    def pass_on(self, lane, slot, part, where, source=None):
        target = self.blocks.at[slot, self.rows(part)]
        self.start(
            target if source is None else source,
            target,
            self.gather_send.at[lane, slot, part],
            self.gather_recv.at[slot, part],
            where,
        )

    def arrived(self, slot, part):
        target = self.blocks.at[slot, self.rows(part)]
        pltpu.make_async_remote_copy(
            src_ref=target,
            dst_ref=target,
            send_sem=self.gather_send.at[0, slot, part],
            recv_sem=self.gather_recv.at[slot, part],
            device_id=self.device(1),
            device_id_type=pl.DeviceIdType.MESH,
        ).wait_recv()

    def send_own(self):
        slot = self.slot(0)
        keep = None
        own = self.blocks.at[slot]
        if self.own is not None:
            own = self.own
            keep = pltpu.make_async_copy(own, self.blocks.at[slot], self.own_sem)
            keep.start()
        first, second = own.at[self.rows(0)], own.at[self.rows(1)]
        self.pass_on(0, slot, 0, self.device(1), first)
        self.pass_on(1, slot, 1, self.device(-1), second)
        self.pass_on(2, slot, 0, self.device(0, True), first)
        self.pass_on(2, slot, 1, self.device(0, True), second)
        self.pass_on(0, slot, 1, self.device(1), second)
        self.pass_on(1, slot, 0, self.device(-1), first)
        return keep

    def receive(self, distance):
        mate = self.device(0, True)
        left, right = self.slot(-distance), self.slot(distance)
        if distance == self.far:
            for part in range(2):
                self.arrived(left, part)
                self.pass_on(2, left, part, mate)
            return
        further = distance < self.far - 1
        self.arrived(left, 0)
        self.pass_on(0, left, 0, self.device(1))
        self.pass_on(2, left, 0, mate)
        self.arrived(right, 1)
        self.pass_on(1, right, 1, self.device(-1))
        self.pass_on(2, right, 1, mate)
        self.arrived(left, 1)
        if further:
            self.pass_on(0, left, 1, self.device(1))
        self.pass_on(2, left, 1, mate)
        self.arrived(right, 0)
        if further:
            self.pass_on(1, right, 0, self.device(-1))
        self.pass_on(2, right, 0, mate)

    def receive_mate(self, offset):
        for part in range(2):
            self.arrived(self.slot(offset, True), part)

    def share(self, offset):
        chip = chip_at(self.position + offset, self.ring)
        self.start(
            self.parts.at[self.slot(offset, True), :, self.cols],
            self.from_mate.at[chip, :, self.cols],
            self.mate_send.at[chip],
            self.mate_recv.at[chip],
            self.device(0, True),
        )

    def shared(self, offset):
        chip = chip_at(self.position + offset, self.ring)
        pltpu.make_async_remote_copy(
            src_ref=self.parts.at[self.slot(offset), :, self.cols],
            dst_ref=self.from_mate.at[chip, :, self.cols],
            send_sem=self.mate_send.at[chip],
            recv_sem=self.mate_recv.at[chip],
            device_id=self.device(0, True),
            device_id_type=pl.DeviceIdType.MESH,
        ).wait_recv()

    def chip_sum(self, offset, rows):
        chip = chip_at(self.position + offset, self.ring)
        return self.parts[self.slot(offset), rows, self.cols].astype(
            jnp.float32
        ) + self.from_mate[chip, rows, self.cols].astype(jnp.float32)

    def send_sum(self, way, distance, part):
        offset = distance if way == 0 else -distance
        begins = self.far if part == way else self.far - 1
        slot = self.slot(offset)
        if distance < begins:
            self.sum_arrived(way, distance, part)

        def chunk(i, carry):
            here = pl.ds(pl.multiple_of(i * 16, 16), 16)
            there = pl.ds(pl.multiple_of(part * self.half + i * 16, 16), 16)
            total = self.chip_sum(offset, there)
            if distance < begins:
                total += self.incoming[way, distance, part, here, self.cols].astype(jnp.float32)
            self.parts[slot, there, self.cols] = total.astype(jnp.bfloat16)
            return carry

        lax.fori_loop(0, self.half // 16, chunk, 0)
        self.start(
            self.parts.at[slot, self.rows(part), self.cols],
            self.incoming.at[way, distance - 1, part, :, self.cols],
            self.sum_send.at[way, distance - 1, part],
            self.sum_recv.at[way, distance - 1, part],
            self.device(1 if way == 0 else -1),
        )

    def sum_arrived(self, way, distance, part):
        target = self.incoming.at[way, distance, part, :, self.cols]
        pltpu.make_async_remote_copy(
            src_ref=target,
            dst_ref=target,
            send_sem=self.sum_send.at[way, distance, part],
            recv_sem=self.sum_recv.at[way, distance, part],
            device_id=self.device(1),
            device_id_type=pl.DeviceIdType.MESH,
        ).wait_recv()

    def run(self, first, second, before, after_far):
        def compute(chip):
            first(chip)
            second(chip)

        keep = self.send_own()
        keep.wait()
        self.receive_mate(0)
        compute(chip_at(self.position, self.ring))
        self.share(0)
        for distance in range(1, self.far):
            self.receive(distance)
            for offset in (-distance, distance):
                self.receive_mate(offset)
                compute(chip_at(self.position + offset, self.ring))
                self.share(offset)
            if distance == self.far - 1:
                self.first_sums()
        self.receive(self.far)
        self.receive_mate(self.far)
        farthest = chip_at(self.position + self.far, self.ring)
        first(farthest)
        before()
        second(farthest)
        self.share(self.far)
        self.far_sums()
        after_far()
        self.last_sums()

    def start_sums(self, compute):
        compute(chip_at(self.position + self.far, self.ring))
        self.share(self.far)
        for distance in range(self.far - 1, 0, -1):
            for offset in (-distance, distance):
                compute(chip_at(self.position + offset, self.ring))
                self.share(offset)
            if distance == self.far - 1:
                self.far_sums()
                self.first_sums()
        compute(chip_at(self.position, self.ring))
        self.share(0)

    def first_sums(self):
        distance = self.far - 1
        self.shared(distance)
        self.send_sum(0, distance, 1)
        self.shared(-distance)
        self.send_sum(1, distance, 0)

    def far_sums(self):
        self.shared(self.far)
        self.send_sum(0, self.far, 0)
        self.send_sum(1, self.far, 1)

    def last_sums(self):
        for distance in range(self.far - 1, 0, -1):
            if distance < self.far - 1:
                self.shared(distance)
                self.shared(-distance)
            self.send_sum(0, distance, 0)
            self.send_sum(1, distance, 1)
            if distance < self.far - 1:
                self.send_sum(0, distance, 1)
                self.send_sum(1, distance, 0)

    def finish(self, result):
        self.shared(0)
        for part in range(2):
            for way in range(2):
                self.sum_arrived(way, 0, part)

            def chunk(i, carry):
                here = pl.ds(pl.multiple_of(i * 16, 16), 16)
                there = pl.ds(pl.multiple_of(part * self.half + i * 16, 16), 16)
                total = self.chip_sum(0, there)
                for way in range(2):
                    total += self.incoming[way, 0, part, here, self.cols].astype(jnp.float32)
                result[there, self.cols] = total.astype(result.dtype)
                return carry

            lax.fori_loop(0, self.half // 16, chunk, 0)

    def drain(self):
        for copy in self.started:
            copy.wait_send()


def sum_scratch(wide_count, rows, width):
    ring = wide_count // 2
    far = ring // 2
    dma = pltpu.SemaphoreType.DMA
    return [
        pltpu.VMEM((wide_count, rows, width), jnp.bfloat16),
        pltpu.VMEM((ring, rows, width), jnp.bfloat16),
        pltpu.VMEM((2, far, 2, rows // 2, width), jnp.bfloat16),
        dma((ring,)),
        dma((ring,)),
        dma((2, far, 2)),
        dma((2, far, 2)),
    ]


def exchange_scratch(wide_count, rows, width):
    dma = pltpu.SemaphoreType.DMA
    return [
        pltpu.VMEM((wide_count, rows, width), jnp.bfloat16),
        dma((3, wide_count, 2)),
        dma((wide_count, 2)),
        dma(()),
    ] + sum_scratch(wide_count, rows, width)


def load_padded(source, target, sem):
    filled = source.shape[0]
    copy = pltpu.make_async_copy(source, target.at[pl.ds(0, filled)], sem)
    copy.start()
    if filled < target.shape[0]:
        target[pl.ds(filled, target.shape[0] - filled)] = jnp.zeros(
            (target.shape[0] - filled, target.shape[1]), target.dtype
        )
    return copy


def pair_rows(ref, chip):
    block = ref[pl.ds(2 * chip, 2)]
    return block.reshape(2 * block.shape[1], block.shape[2])


def set_pair(ref, chip, cols, value):
    rows = ref.shape[1]
    ref[2 * chip, :, cols] = value[:rows].astype(ref.dtype)
    ref[2 * chip + 1, :, cols] = value[rows:].astype(ref.dtype)


def tiles(count, tile, body, start=0):
    def step(i, carry):
        body(pl.ds(pl.multiple_of(start + i * tile, tile), tile))
        return carry

    lax.fori_loop(0, count // tile, step, 0)


class LineExchange:
    def __init__(self, narrow_count):
        self.count = narrow_count
        self.mine = lax.axis_index("narrow")
        self.started = []

    def peer(self, offset):
        return (self.mine + offset) % self.count

    def greet(self, extra=0):
        barrier = pltpu.get_barrier_semaphore()
        for offset in range(1, self.count):
            pl.semaphore_signal(
                barrier,
                inc=1,
                device_id={"narrow": self.peer(offset)},
                device_id_type=pl.DeviceIdType.MESH,
            )
        pl.semaphore_wait(barrier, self.count - 1 + extra)

    def copy(self, source, target, send_sem, recv_sem, where):
        return pltpu.make_async_remote_copy(
            src_ref=source,
            dst_ref=target,
            send_sem=send_sem,
            recv_sem=recv_sem,
            device_id={"narrow": where},
            device_id_type=pl.DeviceIdType.MESH,
        )

    def send(self, offset, source, landing, send_sems, recv_sems):
        peer = self.peer(offset)
        copy = self.copy(
            source, landing.at[self.mine], send_sems.at[offset - 1], recv_sems.at[self.mine], peer
        )
        copy.start()
        self.started.append(copy)

    def arrived(self, offset, landing, send_sems, recv_sems):
        peer = self.peer(offset)
        self.copy(
            landing.at[peer], landing.at[peer], send_sems.at[offset - 1], recv_sems.at[peer], peer
        ).wait_recv()

    def drain(self):
        for copy in self.started:
            copy.wait_send()


class LineSum:
    def __init__(self, line, view, landing, send_sems, recv_sems):
        self.line, self.view, self.landing = line, view, landing
        self.send_sems, self.recv_sems = send_sems, recv_sems
        self.last = line.count - 1

    def reaches(self, way, offset):
        here = self.line.mine
        return here + offset <= self.last if way == 0 else here - offset >= 0

    def follows(self, way):
        here = self.line.mine
        return here > 0 if way == 0 else here < self.last

    def target(self, way, offset):
        return self.line.mine + offset if way == 0 else self.line.mine - offset

    def copy(self, way, offset):
        return self.line.copy(
            self.view(self.target(way, offset)),
            self.landing.at[way, offset - 1],
            self.send_sems.at[way, offset - 1],
            self.recv_sems.at[way, offset - 1],
            self.line.mine + 1 if way == 0 else self.line.mine - 1,
        )

    def arrived(self, way, offset):
        landing = self.landing.at[way, offset]
        self.line.copy(
            landing,
            landing,
            self.send_sems.at[way, offset],
            self.recv_sems.at[way, offset],
            self.line.mine,
        ).wait_recv()

    def add(self, way, offset):
        held = self.view(self.target(way, offset))

        def chunk(i, carry):
            some = pl.ds(pl.multiple_of(i * 16, 16), 16)
            held[some] = (
                held[some].astype(jnp.float32)
                + self.landing[way, offset, some].astype(jnp.float32)
            ).astype(jnp.bfloat16)
            return carry

        lax.fori_loop(0, self.landing.shape[2] // 16, chunk, 0)

    def begin(self, offset):
        for way in range(2):

            @pl.when(self.reaches(way, offset) & jnp.logical_not(self.follows(way)))
            def _():
                self.copy(way, offset).start()

    def step(self, offset):
        for way in range(2):

            @pl.when(self.reaches(way, offset) & self.follows(way))
            def _():
                self.arrived(way, offset)
                self.add(way, offset)
                self.copy(way, offset).start()

    def finish(self, result):
        held = self.view(self.line.mine)
        count = self.landing.shape[2] // 16

        def begin(i, carry):
            some = pl.ds(pl.multiple_of(i * 16, 16), 16)
            result[some] = held[some].astype(result.dtype)
            return carry

        lax.fori_loop(0, count, begin, 0)
        for way in range(2):

            @pl.when(self.follows(way))
            def _():
                self.arrived(way, 0)

                def chunk(i, carry):
                    some = pl.ds(pl.multiple_of(i * 16, 16), 16)
                    result[some] += self.landing[way, 0, some].astype(result.dtype)
                    return carry

                lax.fori_loop(0, count, chunk, 0)

    def drain(self):
        for offset in range(1, self.last + 1):
            for way in range(2):

                @pl.when(self.reaches(way, offset))
                def _():
                    self.copy(way, offset).wait_send()


class LineGather:
    def __init__(self, line, view, send_sems, recv_sems):
        self.line, self.view = line, view
        self.send_sems, self.recv_sems = send_sems, recv_sems
        self.last = line.count - 1

    def copy(self, way, block):
        target = self.view(block)
        here = self.line.mine
        return self.line.copy(
            target,
            target,
            self.send_sems.at[way, block],
            self.recv_sems.at[block],
            here + 1 if way == 0 else here - 1,
        )

    def goes(self, way):
        return self.line.mine < self.last if way == 0 else self.line.mine > 0

    def has(self, way, step):
        here = self.line.mine
        return here - step >= 0 if way == 0 else here + step <= self.last

    def block(self, way, step):
        return self.line.mine - step if way == 0 else self.line.mine + step

    def send_own(self):
        for way in range(2):

            @pl.when(self.goes(way))
            def _():
                self.copy(way, self.line.mine).start()

    def step(self, step):
        for way in range(2):

            @pl.when(self.has(way, step))
            def _():
                self.copy(way, self.block(way, step)).wait_recv()

                @pl.when(self.goes(way))
                def _():
                    self.copy(way, self.block(way, step)).start()

    def each(self, step, body):
        for way in range(2):

            @pl.when(self.has(way, step))
            def _():
                body(self.block(way, step))

    def drain(self):
        for way in range(2):
            for step in range(self.last + 1):

                @pl.when(self.has(way, step) & self.goes(way))
                def _():
                    self.copy(way, self.block(way, step)).wait_send()


def greet_plane(plane):
    barrier = pltpu.get_barrier_semaphore()
    for where in (plane.device(-1), plane.device(1), plane.device(0, True)):
        pl.semaphore_signal(barrier, inc=1, device_id=where, device_id_type=pl.DeviceIdType.MESH)


def geglu_forward_kernel(
    wide_count,
    narrow_count,
    rows_all,
    expand,
    reduce,
    shift,
    hidden,
    cotangent,
    reduce_shift,
    gain,
    norm_shift,
    reduce_out,
    active_out,
    slope_out,
    gelu_out,
    layer_output,
    sum_grad,
    feed_grad,
    row_sums,
    feed,
    blocks,
    parts,
    from_mate,
    incoming,
    mate_send,
    mate_recv,
    sum_send,
    sum_recv,
    expand_mat,
    reduce_mat,
    active,
    slope,
    gelu,
    load_sems,
    keep_sems,
    reduce_send,
    reduce_recv,
    late_mate_send,
    late_mate_recv,
    late_sum_send,
    late_sum_recv,
):
    sems = (None, None, mate_send, mate_recv, sum_send, sum_recv, None)
    late_sems = (None, None, late_mate_send, late_mate_recv, late_sum_send, late_sum_recv, None)
    line = LineExchange(narrow_count)
    filled, cols = reduce.shape
    width = rows_all.shape[2]
    upper = (2 * line.mine) // narrow_count
    late = pl.multiple_of((1 - upper) * (width - cols), cols)
    early = pl.multiple_of(upper * cols, cols)
    plane = PlaneExchange(
        wide_count, None, None, parts, from_mate, incoming, sems, pl.ds(early, width - cols)
    )
    late_plane = PlaneExchange(
        wide_count, None, None, parts, from_mate, incoming, late_sems, pl.ds(late, cols)
    )
    loads = [
        load_padded(expand.at[0], expand_mat.at[0], load_sems.at[0]),
        load_padded(expand.at[1], expand_mat.at[1], load_sems.at[1]),
        pltpu.make_async_copy(rows_all, blocks, load_sems.at[4]),
    ]
    loads[2].start()

    def reduce_cols(block):
        return reduce_mat.at[
            pl.ds(0, filled), pl.ds(pl.multiple_of(block * cols, cols), cols)
        ]

    line_reduce = LineGather(line, reduce_cols, reduce_send, reduce_recv)
    own_reduce = pltpu.make_async_copy(reduce, reduce_cols(line.mine), load_sems.at[2])
    own_reduce.start()
    if filled < reduce_mat.shape[0]:
        reduce_mat[filled:] = jnp.zeros(
            (reduce_mat.shape[0] - filled, reduce_mat.shape[1]), reduce_mat.dtype
        )
    greet_plane(plane)
    line.greet(3)
    own_reduce.wait()
    line_reduce.send_own()
    kept = []
    waiting = list(loads)

    def compute(chip):
        while waiting:
            waiting.pop().wait()

        def units(cols):
            rows = pair_rows(blocks, chip)
            gate = dot(rows, expand_mat[0, cols], ((1,), (1,))) + shift[0:1, cols]
            upper = dot(rows, expand_mat[1, cols], ((1,), (1,))) + shift[1:2, cols]
            factor = math.sqrt(2 / math.pi)
            square = gate * gate
            bend = jnp.tanh(factor * gate * (1 + 0.044715 * square))
            value = 0.5 * gate * (1 + bend)
            pull = 0.5 * (1 + bend) + 0.5 * gate * (1 - bend * bend) * factor * (
                1 + 3 * 0.044715 * square
            )
            set_pair(active, chip, cols, value * upper)
            set_pair(slope, chip, cols, pull * upper)
            set_pair(gelu, chip, cols, value)

        tiles(active.shape[2], 256, units)

        pair = pl.ds(2 * chip, 2)
        for index, (source, target) in enumerate(
            ((active, active_out), (slope, slope_out), (gelu, gelu_out))
        ):
            copy = pltpu.make_async_copy(
                source.at[pair], target.at[pair], keep_sems.at[chip, index]
            )
            copy.start()
            kept.append(copy)

    def compute_sums(start, count):
        def compute(chip):
            def outputs(some):
                part = dot(pair_rows(active, chip), reduce_mat[:, some], ((1,), (0,)))
                set_pair(parts, chip, some, part)

            tiles(count, 256, outputs, start)

        return compute

    offsets = [0]
    for distance in range(1, plane.far):
        offsets += [-distance, distance]
    offsets.append(plane.far)
    chips = [chip_at(plane.position + offset, plane.ring) for offset in offsets]
    each = -(-len(chips) // (narrow_count - 2))
    for step in range(1, narrow_count - 1):
        if step == 1:
            compute(chips.pop(0))
        for _ in range(min(each, len(chips))):
            compute(chips.pop(0))
        line_reduce.step(step)
    plane.start_sums(compute_sums(early, width - cols))
    line_reduce.step(narrow_count - 1)
    keep_reduce = pltpu.make_async_copy(
        reduce_mat.at[pl.ds(0, filled)], reduce_out, load_sems.at[3]
    )
    keep_reduce.start()
    late_plane.start_sums(compute_sums(late, cols))
    plane.last_sums()
    late_plane.last_sums()
    plane.finish(feed)
    late_plane.finish(feed)

    row_sums[...] = jnp.zeros_like(row_sums)

    def norm_rows(i, carry):
        some = pl.ds(pl.multiple_of(i * 16, 16), 16)
        result, normed, inverse = normalize(
            residual_scale * hidden[some] + feed[some] + reduce_shift[...],
            gain[...],
            norm_shift[...],
        )
        layer_output[some] = result.astype(jnp.bfloat16)
        upstream = cotangent[some].astype(jnp.float32)
        total = normalize_back(upstream, normed, inverse, gain[...])
        sum_grad[some] = total
        feed_grad[some] = total.astype(jnp.bfloat16)
        row_sums[0:1] += jnp.sum(upstream * normed, axis=0, keepdims=True)
        row_sums[1:2] += jnp.sum(upstream, axis=0, keepdims=True)
        row_sums[2:3] += jnp.sum(total, axis=0, keepdims=True)
        return carry

    lax.fori_loop(0, rows_all.shape[1] // 16, norm_rows, 0)
    plane.drain()
    late_plane.drain()
    keep_reduce.wait()
    line_reduce.drain()
    for copy in kept:
        copy.wait()


def geglu_forward(
    wide_count,
    narrow_count,
    rows_all,
    expand,
    reduce_weight,
    shift,
    hidden,
    cotangent,
    reduce_shift,
    gain,
    norm_shift,
):
    _, rows, width = rows_all.shape
    padded = shift.shape[1]
    anywhere = pl.BlockSpec(memory_space=pl.ANY)
    vmem = pl.BlockSpec(memory_space=pltpu.VMEM)
    kept = jax.ShapeDtypeStruct((wide_count, rows, padded), jnp.bfloat16)
    scratch = [pltpu.VMEM((rows, width), jnp.float32)]
    scratch.append(pltpu.VMEM((wide_count, rows, width), jnp.bfloat16))
    scratch += sum_scratch(wide_count, rows, width) + [
        pltpu.VMEM((2, padded, width), jnp.bfloat16),
        pltpu.VMEM((padded, width), jnp.bfloat16),
        pltpu.VMEM((wide_count, rows, padded), jnp.bfloat16),
        pltpu.VMEM((wide_count, rows, padded), jnp.bfloat16),
        pltpu.VMEM((wide_count, rows, padded), jnp.bfloat16),
        pltpu.SemaphoreType.DMA((5,)),
        pltpu.SemaphoreType.DMA((wide_count // 2, 3)),
        pltpu.SemaphoreType.DMA((2, narrow_count)),
        pltpu.SemaphoreType.DMA((narrow_count,)),
    ] + sum_scratch(wide_count, rows, width)[3:]
    return pl.pallas_call(
        functools.partial(geglu_forward_kernel, wide_count, narrow_count),
        out_shape=(
            jax.ShapeDtypeStruct((reduce_weight.shape[0], width), jnp.bfloat16),
            kept,
            kept,
            kept,
            jax.ShapeDtypeStruct((rows, width), jnp.bfloat16),
            jax.ShapeDtypeStruct((rows, width), jnp.float32),
            jax.ShapeDtypeStruct((rows, width), jnp.bfloat16),
            jax.ShapeDtypeStruct((3, width), jnp.float32),
        ),
        in_specs=[anywhere] * 3 + [vmem] * 6,
        out_specs=(anywhere,) * 4 + (vmem,) * 4,
        scratch_shapes=scratch,
        compiler_params=pltpu.CompilerParams(
            collective_id=1, has_side_effects=True, vmem_limit_bytes=kernel_memory
        ),
        cost_estimate=pl.CostEstimate(
            flops=6 * wide_count * rows * padded * width, bytes_accessed=200 * 2**20, transcendentals=0
        ),
        name="geglu_forward",
    )(
        rows_all,
        expand,
        reduce_weight,
        shift,
        hidden,
        cotangent,
        reduce_shift,
        gain,
        norm_shift,
    )


def geglu_backward_kernel(
    wide_count,
    narrow_count,
    own,
    expand,
    reduce,
    slope_in,
    gelu_in,
    active_in,
    rows_in,
    reduce_grad,
    expand_part,
    hidden_grad,
    unit_sums,
    blocks,
    gather_send,
    gather_recv,
    own_sem,
    parts,
    from_mate,
    incoming,
    mate_send,
    mate_recv,
    sum_send,
    sum_recv,
    expand_mat,
    reduce_mat,
    slope,
    gelu,
    active,
    rows_all,
    staged,
    load_sems,
    keep_sems,
    line_in,
    line_send,
    line_recv,
):
    sems = (gather_send, gather_recv, mate_send, mate_recv, sum_send, sum_recv, own_sem)
    plane = PlaneExchange(wide_count, own, blocks, parts, from_mate, incoming, sems)
    loads = [
        load_padded(expand.at[0], expand_mat.at[0], load_sems.at[0]),
        load_padded(expand.at[1], expand_mat.at[1], load_sems.at[1]),
        load_padded(reduce, reduce_mat, load_sems.at[2]),
        pltpu.make_async_copy(slope_in, slope, load_sems.at[3]),
        pltpu.make_async_copy(gelu_in, gelu, load_sems.at[4]),
    ]
    late_loads = [
        pltpu.make_async_copy(active_in, active, load_sems.at[5]),
        pltpu.make_async_copy(rows_in, rows_all, load_sems.at[6]),
    ]
    for copy in loads[3:]:
        copy.start()
    unit_sums[...] = jnp.zeros_like(unit_sums)
    line = LineExchange(narrow_count)
    filled, line_cols = line_in.shape[2:]

    def line_part(block):
        return reduce_mat.at[
            pl.ds(0, filled), pl.ds(pl.multiple_of(block * line_cols, line_cols), line_cols)
        ]

    line_sum = LineSum(line, line_part, line_in, line_send, line_recv)
    greet_plane(plane)
    line.greet(3)
    for copy in late_loads:
        copy.start()
    kept = []
    waiting = list(loads)

    def compute(chip):
        while waiting:
            waiting.pop().wait()

        def units(cols):
            pulled = dot(pair_rows(blocks, chip), reduce_mat[cols], ((1,), (1,)))
            pair = pl.ds(2 * chip, 2)
            shape = pulled.shape
            gate_grad = pulled * slope[pair, :, cols].reshape(shape).astype(jnp.float32)
            upper_grad = pulled * gelu[pair, :, cols].reshape(shape).astype(jnp.float32)
            set_pair(slope, chip, cols, gate_grad)
            set_pair(gelu, chip, cols, upper_grad)
            unit_sums[0:1, cols] += jnp.sum(gate_grad, axis=0, keepdims=True)
            unit_sums[1:2, cols] += jnp.sum(upper_grad, axis=0, keepdims=True)

        tiles(slope.shape[2], 256, units)

    def compute_sums(chip):
        def outputs(cols):
            set_pair(
                parts,
                chip,
                cols,
                dot(pair_rows(slope, chip), expand_mat[0, :, cols], ((1,), (0,)))
                + dot(pair_rows(gelu, chip), expand_mat[1, :, cols], ((1,), (0,))),
            )

        tiles(parts.shape[2], 256, outputs)

    def product(left, right, start):
        tokens = left.shape[0] * left.shape[1]
        return dot(
            left[:, :, start : start + 256].reshape(tokens, 256),
            right[...].reshape(tokens, right.shape[2]),
            ((0,), (0,)),
        ).astype(jnp.bfloat16)

    def reduce_work():
        for copy in late_loads:
            copy.wait()

        def reduce_cols(index):
            cols = pl.ds(pl.multiple_of(index * line_cols, line_cols), line_cols)

            def units(some):
                tokens = active.shape[0] * active.shape[1]
                part = dot(
                    active[:, :, some].reshape(tokens, some.size),
                    blocks[:, :, cols].reshape(tokens, line_cols),
                    ((0,), (0,)),
                )
                reduce_mat[some, cols] = part.astype(jnp.bfloat16)

            tiles(active.shape[2], 256, units)

        for offset in range(narrow_count - 1, 0, -1):
            for way in range(2):

                @pl.when(line_sum.reaches(way, offset))
                def _():
                    reduce_cols(line_sum.target(way, offset))

            line_sum.begin(offset)
        reduce_cols(line.mine)

    def expand_work(left, start, target):
        def work():
            index = len(kept)
            if index >= 2:
                kept[index - 2].wait()
            staged[index % 2] = product(left, rows_all, start)
            stop = min(256, target.shape[0] - start)
            copy = pltpu.make_async_copy(
                staged.at[index % 2, pl.ds(0, stop)],
                target.at[pl.ds(start, stop)],
                keep_sems.at[index % 2],
            )
            copy.start()
            kept.append(copy)

        return work

    works = [
        expand_work(left, start, target)
        for left, target in ((slope, expand_part.at[0]), (gelu, expand_part.at[1]))
        for start in range(0, target.shape[0], 256)
    ]
    steps = [
        functools.partial(line_sum.step, offset) for offset in range(narrow_count - 2, 0, -1)
    ]
    third = len(works) // 3
    middle = (len(steps) + 1) // 2

    def many(calls):
        for call in calls:
            call()

    beside = functools.partial(many, steps[:middle] + works[:third])
    plane.run(compute, compute_sums, reduce_work, beside)
    many(works[third : 2 * third] + steps[middle:] + works[2 * third :])
    plane.finish(hidden_grad)
    plane.drain()
    line_sum.finish(reduce_grad)
    line_sum.drain()
    for copy in kept[-2:]:
        copy.wait()


def geglu_backward(
    wide_count,
    narrow_count,
    feed_grad,
    expand,
    reduce_full,
    slope,
    gelu,
    active,
    rows_all,
):
    rows, width = feed_grad.shape
    padded = slope.shape[2]
    anywhere = pl.BlockSpec(memory_space=pl.ANY)
    vmem = pl.BlockSpec(memory_space=pltpu.VMEM)
    scratch = exchange_scratch(wide_count, rows, width) + [
        pltpu.VMEM((2, padded, width), jnp.bfloat16),
        pltpu.VMEM((padded, width), jnp.bfloat16),
        pltpu.VMEM((wide_count, rows, padded), jnp.bfloat16),
        pltpu.VMEM((wide_count, rows, padded), jnp.bfloat16),
        pltpu.VMEM((wide_count, rows, padded), jnp.bfloat16),
        pltpu.VMEM((wide_count, rows, width), jnp.bfloat16),
        pltpu.VMEM((2, 256, width), jnp.bfloat16),
        pltpu.SemaphoreType.DMA((7,)),
        pltpu.SemaphoreType.DMA((2,)),
        pltpu.VMEM(
            (2, narrow_count - 1, reduce_full.shape[0], width // narrow_count), jnp.bfloat16
        ),
        pltpu.SemaphoreType.DMA((2, narrow_count - 1)),
        pltpu.SemaphoreType.DMA((2, narrow_count - 1)),
    ]
    return pl.pallas_call(
        functools.partial(geglu_backward_kernel, wide_count, narrow_count),
        out_shape=(
            jax.ShapeDtypeStruct(
                (reduce_full.shape[0], width // narrow_count), jnp.float32
            ),
            jax.ShapeDtypeStruct(expand.shape, jnp.bfloat16),
            jax.ShapeDtypeStruct((rows, width), jnp.float32),
            jax.ShapeDtypeStruct((2, padded), jnp.float32),
        ),
        in_specs=[anywhere] * 7,
        out_specs=(vmem, anywhere, vmem, vmem),
        scratch_shapes=scratch,
        compiler_params=pltpu.CompilerParams(
            collective_id=2, has_side_effects=True, vmem_limit_bytes=63 * 2**20
        ),
        cost_estimate=pl.CostEstimate(
            flops=12 * wide_count * rows * padded * width, bytes_accessed=200 * 2**20, transcendentals=0
        ),
        name="geglu_backward",
    )(feed_grad, expand, reduce_full, slope, gelu, active, rows_all)


def rotate_lanes(vectors, cosine, signed_sine):
    return vectors * cosine + pltpu.roll(vectors, vectors.shape[1] // 2, 1) * signed_sine


def attention_backward_kernel(
    wide_count,
    narrow_count,
    upper_grad,
    hidden_part,
    normed,
    inv_std,
    gain,
    merge,
    mixed,
    queries,
    keys,
    values,
    probs,
    cosine,
    signed_sine,
    triple,
    merge_grad,
    heads_sums,
    merge_sums,
    sum_grad,
    norm_sums,
    attended,
    upstream,
    outbound,
    probs_held,
    keys_turned,
    key_total,
    value_total,
    merge_out,
    merge_in,
    mixed_send,
    mixed_recv,
    merge_send,
    merge_recv,
    load_sems,
    parts,
    from_mate,
    incoming,
    mate_send,
    mate_recv,
    sum_send,
    sum_recv,
):
    sems = (None, None, mate_send, mate_recv, sum_send, sum_recv, None)
    plane = PlaneExchange(wide_count, None, None, parts, from_mate, incoming, sems)
    line = LineExchange(narrow_count)
    rows, width = sum_grad.shape
    own_cols = queries.shape[1]
    heads = own_cols // HDIM
    scale = HDIM ** (-0.5)

    def load(head):
        return pltpu.make_async_copy(
            probs.at[head], probs_held.at[head % 2], load_sems.at[head % 2]
        )

    load(0).start()
    greet_plane(plane)

    norm_sums[...] = jnp.zeros_like(norm_sums)
    merge_sums[...] = jnp.zeros_like(merge_sums)

    def norm_rows(i, carry):
        some = pl.ds(pl.multiple_of(i * 16, 16), 16)
        hidden_grad = residual_scale * upper_grad[some] + hidden_part[some]
        norm_sums[0:1] += jnp.sum(hidden_grad * normed[some], axis=0, keepdims=True)
        norm_sums[1:2] += jnp.sum(hidden_grad, axis=0, keepdims=True)
        total = normalize_back(hidden_grad, normed[some], inv_std[some], gain[...])
        sum_grad[some] = total
        merge_sums[...] += jnp.sum(total, axis=0, keepdims=True)
        attended[some] = total.astype(jnp.bfloat16)
        return carry

    lax.fori_loop(0, rows // 16, norm_rows, 0)
    line.greet(3)

    def mixed_part(target, where):
        part = dot(
            attended[...],
            merge[pl.ds(pl.multiple_of(where * own_cols, own_cols), own_cols)],
            ((1,), (1,)),
        )
        target[...] = part.astype(jnp.bfloat16)

    for offset in range(1, narrow_count):
        place = line.peer(offset)
        mixed_part(outbound.at[offset - 1], place)
        line.send(offset, outbound.at[offset - 1], upstream, mixed_send, mixed_recv)
    mixed_part(upstream.at[line.mine], line.mine)

    block = parts.shape[1]

    def merge_rows(i, carry):
        cols = pl.ds(pl.multiple_of(i * block, block), block)
        parts[i] = dot(mixed[:, cols], attended[...], ((0,), (0,))).astype(jnp.bfloat16)
        return carry

    lax.fori_loop(0, wide_count, merge_rows, 0)
    for offset in range(plane.ring):
        plane.share(offset)
    plane.first_sums()
    plane.far_sums()
    plane.last_sums()
    plane.finish(merge_out)
    count = merge_grad.shape[0]

    def z_rows(where):
        return pl.ds(pl.multiple_of(where * count, count), count)

    for offset in range(1, narrow_count):
        line.send(
            offset, merge_out.at[z_rows(line.peer(offset))], merge_in, merge_send, merge_recv
        )
    for offset in range(1, narrow_count):
        line.arrived(offset, upstream, mixed_send, mixed_recv)

    def one_head(head):
        cols = pl.ds(head * HDIM, HDIM)
        load(head).wait()
        if head + 1 < heads:
            load(head + 1).start()
        held = probs_held.at[head % 2]
        keys_turned[...] = keys[:, cols].astype(jnp.float32).T.astype(jnp.bfloat16)
        key_total[...] = jnp.zeros_like(key_total)
        value_total[...] = jnp.zeros_like(value_total)

        def chunk(i, carry):
            here = pl.ds(pl.multiple_of(i * rows, rows), rows)
            weights_low = held[:, here]
            up = upstream[i, :, cols]
            pulled = dot(values[:, cols], up, ((1,), (1,)))
            weights = weights_low.astype(jnp.float32)
            scaled = weights * pulled
            change = (scaled - weights * jnp.sum(scaled, axis=0, keepdims=True)).astype(
                jnp.bfloat16
            )
            key_total[...] += dot(change, queries[here, cols], ((1,), (0,)))
            value_total[...] += dot(weights_low, up, ((1,), (0,)))
            query_grad = dot(keys_turned[...], change, ((1,), (0,))).T * scale
            triple[here, cols] = rotate_lanes(
                query_grad, cosine[here], signed_sine[here]
            ).astype(jnp.bfloat16)
            return carry

        lax.fori_loop(0, narrow_count, chunk, 0)

        def ending(i, carry):
            here = pl.ds(pl.multiple_of(i * rows, rows), rows)
            triple[here, pl.ds(own_cols + head * HDIM, HDIM)] = rotate_lanes(
                key_total[here] * scale, cosine[here], signed_sine[here]
            ).astype(jnp.bfloat16)
            triple[here, pl.ds(2 * own_cols + head * HDIM, HDIM)] = value_total[here].astype(
                jnp.bfloat16
            )
            return carry

        lax.fori_loop(0, narrow_count, ending, 0)

    for head in range(heads):
        one_head(head)

    def column_sums(cols):
        heads_sums[:, cols] = jnp.sum(
            triple[:, cols].astype(jnp.float32), axis=0, keepdims=True
        )

    tiles(3 * own_cols, 256, column_sums)
    summed = merge_out[z_rows(line.mine)].astype(jnp.float32)
    for offset in range(1, narrow_count):
        line.arrived(offset, merge_in, merge_send, merge_recv)
        summed += merge_in[line.peer(offset)].astype(jnp.float32)
    merge_grad[...] = summed
    line.drain()
    plane.drain()


def attention_backward(
    wide_count,
    narrow_count,
    upper_grad,
    hidden_part,
    normed,
    inv_std,
    gain,
    merge_full,
    mixed,
    queries,
    keys,
    values,
    probs,
    cosine,
    signed_sine,
):
    rows, width = normed.shape
    bucket, own_cols = queries.shape
    block = width // wide_count
    count = block // narrow_count
    anywhere = pl.BlockSpec(memory_space=pl.ANY)
    vmem = pl.BlockSpec(memory_space=pltpu.VMEM)
    dma = pltpu.SemaphoreType.DMA
    return pl.pallas_call(
        functools.partial(attention_backward_kernel, wide_count, narrow_count),
        out_shape=(
            jax.ShapeDtypeStruct((bucket, 3 * own_cols), jnp.bfloat16),
            jax.ShapeDtypeStruct((count, width), jnp.float32),
            jax.ShapeDtypeStruct((1, 3 * own_cols), jnp.float32),
            jax.ShapeDtypeStruct((1, width), jnp.float32),
            jax.ShapeDtypeStruct((rows, width), jnp.float32),
            jax.ShapeDtypeStruct((2, width), jnp.float32),
        ),
        in_specs=[vmem] * 10 + [anywhere] + [vmem] * 2,
        out_specs=(vmem,) * 6,
        scratch_shapes=[
            pltpu.VMEM((rows, width), jnp.bfloat16),
            pltpu.VMEM((narrow_count, rows, own_cols), jnp.bfloat16),
            pltpu.VMEM((narrow_count - 1, rows, own_cols), jnp.bfloat16),
            pltpu.VMEM((2, bucket, bucket), jnp.bfloat16),
            pltpu.VMEM((HDIM, bucket), jnp.bfloat16),
            pltpu.VMEM((bucket, HDIM), jnp.float32),
            pltpu.VMEM((bucket, HDIM), jnp.float32),
            pltpu.VMEM((block, width), jnp.bfloat16),
            pltpu.VMEM((narrow_count, count, width), jnp.bfloat16),
            dma((narrow_count - 1,)),
            dma((narrow_count,)),
            dma((narrow_count - 1,)),
            dma((narrow_count,)),
            dma((2,)),
        ]
        + sum_scratch(wide_count, block, width),
        compiler_params=pltpu.CompilerParams(
            collective_id=3, has_side_effects=True, vmem_limit_bytes=kernel_memory
        ),
        cost_estimate=pl.CostEstimate(
            flops=60 * 10**9, bytes_accessed=200 * 2**20, transcendentals=0
        ),
        name="attention_backward",
    )(
        upper_grad,
        hidden_part,
        normed,
        inv_std,
        gain,
        merge_full,
        mixed,
        queries,
        keys,
        values,
        probs,
        cosine,
        signed_sine,
    )


def input_backward_kernel(
    wide_count,
    narrow_count,
    inputs,
    triple,
    heads_mat,
    small,
    sum_grad,
    input_part,
    heads_grad,
    heads_bias_grad,
    merge_bias_grad,
    gains_grad,
    shifts_grad,
    expand_bias_grad,
    reduce_bias_grad,
    small_result,
    line_parts,
    line_in,
    heads_out,
    heads_in,
    small_wide,
    small_sum,
    small_line,
    line_send,
    line_recv,
    heads_send,
    heads_recv,
    wide_send,
    wide_recv,
    small_send,
    small_recv,
    parts,
    from_mate,
    incoming,
    mate_send,
    mate_recv,
    sum_send,
    sum_recv,
):
    sems = (None, None, mate_send, mate_recv, sum_send, sum_recv, None)
    plane = PlaneExchange(wide_count, None, None, parts, from_mate, incoming, sems)
    line = LineExchange(narrow_count)
    rows, width = input_part.shape
    here = line.mine
    last = narrow_count - 1
    place = lax.axis_index("wide")

    def wide_peer(offset):
        return (place + offset) % wide_count

    barrier = pltpu.get_barrier_semaphore()
    for offset in range(1, wide_count):
        pl.semaphore_signal(
            barrier,
            inc=1,
            device_id={"wide": wide_peer(offset)},
            device_id_type=pl.DeviceIdType.MESH,
        )
    line.greet(wide_count - 1)

    def small_copy(offset, source, slot):
        return pltpu.make_async_remote_copy(
            src_ref=source,
            dst_ref=small_wide.at[slot],
            send_sem=wide_send.at[offset - 1],
            recv_sem=wide_recv.at[slot],
            device_id={"wide": wide_peer(offset)},
            device_id_type=pl.DeviceIdType.MESH,
        )

    small_copies = [
        small_copy(offset, small.at[wide_peer(offset)], place) for offset in range(1, wide_count)
    ]
    for copy in small_copies:
        copy.start()

    line_sum = LineSum(line, lambda target: line_parts.at[target], line_in, line_send, line_recv)

    def input_rows(index):
        some = pl.ds(pl.multiple_of(index * rows, rows), rows)

        def input_cols(cols):
            part = dot(triple[some], heads_mat[cols], ((1,), (1,)))
            line_parts[index, :, cols] = part.astype(jnp.bfloat16)

        tiles(width, 256, input_cols)

    for offset in range(last, 0, -1):
        for way in range(2):

            @pl.when(line_sum.reaches(way, offset))
            def _():
                input_rows(line_sum.target(way, offset))

        line_sum.begin(offset)
    input_rows(here)

    block = parts.shape[1]

    def heads_rows(i, carry):
        cols = pl.ds(pl.multiple_of(i * block, block), block)
        parts[i] = dot(inputs[:, cols], triple[...], ((0,), (0,))).astype(jnp.bfloat16)
        return carry

    lax.fori_loop(0, wide_count, heads_rows, 0)
    for offset in range(plane.ring):
        plane.share(offset)
    for offset in range(last - 1, last // 2, -1):
        line_sum.step(offset)
    plane.first_sums()
    plane.far_sums()

    for offset in range(1, wide_count):
        peer = wide_peer(offset)
        small_copy(offset, small_wide.at[peer], peer).wait_recv()
    small_wide[place] = small[place]
    total = small_wide[0]
    for index in range(1, wide_count):
        total += small_wide[index]
    small_sum[...] = total
    for offset in range(1, narrow_count):
        line.send(offset, small_sum.at[line.peer(offset)], small_line, small_send, small_recv)

    plane.last_sums()
    for offset in range(last // 2, 0, -1):
        line_sum.step(offset)
    plane.finish(heads_out)
    count = heads_grad.shape[0]

    def z_rows(where):
        return pl.ds(pl.multiple_of(where * count, count), count)

    for offset in range(1, narrow_count):
        line.send(
            offset, heads_out.at[z_rows(line.peer(offset))], heads_in, heads_send, heads_recv
        )
    heads_in[line.mine] = heads_out[z_rows(line.mine)]
    small_line[line.mine] = small_sum[line.mine]
    for offset in range(1, narrow_count):
        line.arrived(offset, small_line, small_send, small_recv)
    result = small_line[0]
    for index in range(1, narrow_count):
        result += small_line[index]
    small_result[...] = result
    row = 0
    for target in (
        heads_bias_grad,
        merge_bias_grad,
        gains_grad,
        shifts_grad,
        expand_bias_grad,
        reduce_bias_grad,
    ):
        first, size = target.shape
        for index in range(first):
            for start in range(0, size, 128):
                stop = min(start + 128, size)
                target[index : index + 1, start:stop] = small_result[
                    row : row + 1, 0 : stop - start
                ]
                row += 1

    line_sum.finish(input_part)

    def add_residual(i, carry):
        some = pl.ds(pl.multiple_of(i * 16, 16), 16)
        input_part[some] += residual_scale * sum_grad[some]
        return carry

    lax.fori_loop(0, rows // 16, add_residual, 0)
    for offset in range(1, narrow_count):
        line.arrived(offset, heads_in, heads_send, heads_recv)
    own_cols = triple.shape[1] // 3
    for index in range(narrow_count):
        for which in range(3):
            start = (which * narrow_count + index) * own_cols
            heads_grad[:, start : start + own_cols] = heads_in[
                index, :, which * own_cols : (which + 1) * own_cols
            ].astype(jnp.float32)
    line_sum.drain()
    for copy in small_copies:
        copy.wait_send()
    line.drain()
    plane.drain()


def input_backward(
    wide_count, narrow_count, inputs, triple_grad, heads_mat, small, sum_grad, small_shapes
):
    bucket, width = inputs.shape
    rows = bucket // narrow_count
    columns = triple_grad.shape[1]
    block = width // wide_count
    count = block // narrow_count
    vmem = pl.BlockSpec(memory_space=pltpu.VMEM)
    dma = pltpu.SemaphoreType.DMA
    lines = small.shape[2]
    return pl.pallas_call(
        functools.partial(input_backward_kernel, wide_count, narrow_count),
        out_shape=(
            jax.ShapeDtypeStruct((rows, width), jnp.float32),
            jax.ShapeDtypeStruct((count, narrow_count * columns), jnp.float32),
        )
        + tuple(jax.ShapeDtypeStruct(shape, jnp.float32) for shape in small_shapes),
        in_specs=[vmem] * 5,
        out_specs=(vmem,) * 8,
        scratch_shapes=[
            pltpu.VMEM((lines, 128), jnp.float32),
            pltpu.VMEM((narrow_count, rows, width), jnp.bfloat16),
            pltpu.VMEM((2, narrow_count - 1, rows, width), jnp.bfloat16),
            pltpu.VMEM((block, columns), jnp.bfloat16),
            pltpu.VMEM((narrow_count, count, columns), jnp.bfloat16),
            pltpu.VMEM((wide_count, narrow_count, lines, 128), jnp.float32),
            pltpu.VMEM((narrow_count, lines, 128), jnp.float32),
            pltpu.VMEM((narrow_count, lines, 128), jnp.float32),
            dma((2, narrow_count - 1)),
            dma((2, narrow_count - 1)),
            dma((narrow_count - 1,)),
            dma((narrow_count,)),
            dma((wide_count - 1,)),
            dma((wide_count,)),
            dma((narrow_count - 1,)),
            dma((narrow_count,)),
        ]
        + sum_scratch(wide_count, block, columns),
        compiler_params=pltpu.CompilerParams(
            collective_id=4, has_side_effects=True, vmem_limit_bytes=kernel_memory
        ),
        cost_estimate=pl.CostEstimate(
            flops=80 * 10**9, bytes_accessed=200 * 2**20, transcendentals=0
        ),
        name="input_backward",
    )(inputs, triple_grad, heads_mat, small, sum_grad)


def greet_all(wide_count, narrow_count):
    barrier = pltpu.get_barrier_semaphore()
    for axis, count in (("wide", wide_count), ("narrow", narrow_count)):
        place = lax.axis_index(axis)
        for offset in range(1, count):
            pl.semaphore_signal(
                barrier,
                inc=1,
                device_id={axis: (place + offset) % count},
                device_id_type=pl.DeviceIdType.MESH,
            )
    pl.semaphore_wait(barrier, wide_count + narrow_count - 2)


def gather_kernel(
    wide_count,
    narrow_count,
    own,
    heads_weight,
    merge_weight,
    small,
    buckets,
    speeds,
    rows_out,
    heads_out,
    merge_out,
    small_out,
    triple,
    cosine,
    signed_sine,
    first_query,
    last_query,
    rows_all,
    triple_all,
    heads_all,
    merge_own,
    small_all,
    rows_send,
    rows_recv,
    heads_send,
    heads_recv,
    merge_send,
    merge_recv,
    small_send,
    small_recv,
    wide_send,
    wide_recv,
    local_sems,
    out_sems,
    heads_ring_send,
    heads_ring_recv,
    block_sems,
):
    ring_sems = (heads_ring_send, heads_ring_recv, None, None, None, None, None)
    heads_ring = PlaneExchange(wide_count, None, heads_all, heads_all, None, None, ring_sems)
    line = LineExchange(narrow_count)
    here = line.mine
    last = narrow_count - 1
    place = lax.axis_index("wide")
    slot = heads_ring.slot(0)
    rows, width = own.shape
    count = heads_weight.shape[0]
    columns = heads_all.shape[2]
    own_cols = columns // 3

    def z_rows(where):
        return pl.ds(pl.multiple_of(where * count, count), count)

    def head_cols(which, where):
        start = which * narrow_count * own_cols + where * own_cols
        return pl.ds(pl.multiple_of(start, own_cols), own_cols)

    line_rows = LineGather(line, lambda block: rows_all.at[block], rows_send, rows_recv)

    keep_rows = pltpu.make_async_copy(own, rows_all.at[here], local_sems.at[0])
    keep_rows.start()
    keeps = [
        pltpu.make_async_copy(
            heads_weight.at[:, head_cols(which, here)],
            heads_all.at[slot, z_rows(here), pl.ds(which * own_cols, own_cols)],
            local_sems.at[2 + which],
        )
        for which in range(3)
    ]
    keep_merge = pltpu.make_async_copy(
        merge_weight, merge_own.at[z_rows(here)], local_sems.at[1]
    )
    for copy in keeps + [keep_merge]:
        copy.start()
    small_all[place, here] = small[...]
    greet_all(wide_count, narrow_count)

    def heads_copy(offset, which, where, sender):
        return line.copy(
            heads_weight.at[:, head_cols(which, where)],
            heads_all.at[slot, z_rows(sender), pl.ds(which * own_cols, own_cols)],
            heads_send.at[offset - 1, which],
            heads_recv.at[sender, which],
            where,
        )

    def merge_copy(offset, where, sender):
        return line.copy(
            merge_weight,
            merge_own.at[z_rows(sender)],
            merge_send.at[offset - 1],
            merge_recv.at[sender],
            where,
        )

    def small_copy(offset, where, sender):
        return line.copy(
            small,
            small_all.at[place, sender],
            small_send.at[offset - 1],
            small_recv.at[sender],
            where,
        )

    started = []

    def start(copy):
        copy.start()
        started.append(copy)

    keep_rows.wait()
    line_rows.send_own()
    for offset in range(1, narrow_count):
        for which in range(3):
            start(heads_copy(offset, which, line.peer(offset), here))
    for offset in range(1, narrow_count):
        start(small_copy(offset, line.peer(offset), here))

    halfway = narrow_count * rows // 2
    joined = buckets[0]

    def tables(i, carry):
        some = pl.ds(pl.multiple_of(i * rows, rows), rows)
        place_in = i * rows + lax.broadcasted_iota(jnp.int32, (rows, 1), 0)
        second = jnp.where(place_in >= halfway, 1 - joined, 0)
        local = place_in - second * halfway
        reach = jnp.where(
            joined == 1,
            buckets[1] + buckets[2],
            jnp.where(second == 1, buckets[2], buckets[1]),
        )
        first_query[some] = jnp.where(local < reach, place_in - local, place_in)
        last_query[some] = jnp.where(
            (joined == 1) | (second == 1), 2 * halfway - 1, halfway - 1
        ) + jnp.zeros_like(place_in)
        angles = local.astype(jnp.float32) * speeds[...]
        lane = lax.broadcasted_iota(jnp.int32, (rows, HDIM), 1)
        cosine[some] = jnp.cos(angles)
        sine = jnp.sin(angles)
        signed_sine[some] = jnp.where(lane < HDIM // 2, sine, -sine)
        return carry

    lax.fori_loop(0, narrow_count, tables, 0)

    line_rows.step(1)
    for copy in keeps:
        copy.wait()
    for offset in range(1, narrow_count):
        for which in range(3):
            heads_copy(offset, which, line.peer(offset), line.peer(offset)).wait_recv()
    heads_ring.send_own()
    for offset in range(1, narrow_count):
        small_copy(offset, line.peer(offset), line.peer(offset)).wait_recv()

    def wide_copy(offset, sender):
        return pltpu.make_async_remote_copy(
            src_ref=small_all.at[sender],
            dst_ref=small_all.at[sender],
            send_sem=wide_send.at[offset - 1],
            recv_sem=wide_recv.at[sender],
            device_id={"wide": (place + offset) % wide_count},
            device_id_type=pl.DeviceIdType.MESH,
        )

    for offset in range(1, wide_count):
        start(wide_copy(offset, place))

    def leave_rows(block):
        return pltpu.make_async_copy(rows_all.at[block], rows_out.at[block], block_sems.at[0, block])

    def leave_triple(block):
        return pltpu.make_async_copy(triple_all.at[block], triple.at[block], block_sems.at[1, block])

    def project(block):
        leave_rows(block).start()

        def cols_step(cols):
            weight = heads_all[:, :, cols].reshape(width, cols.size)
            triple_all[block, :, cols] = dot(rows_all[block], weight, ((1,), (0,)))

        tiles(columns, 256, cols_step)
        leave_triple(block).start()

    def project_step(step):
        line_rows.each(step, project)

    def gather(ring, distance):
        ring.receive(distance)
        ring.receive_mate(-distance)
        if distance < ring.far:
            ring.receive_mate(distance)

    outs = []

    def keep_out(source, target):
        copy = pltpu.make_async_copy(source, target, out_sems.at[len(outs)])
        copy.start()
        outs.append(copy)

    for offset in range(1, narrow_count):
        start(merge_copy(offset, line.peer(offset), here))
    heads_ring.receive_mate(0)
    for distance in range(1, heads_ring.far):
        gather(heads_ring, distance)
    if last > 1:
        line_rows.step(2)
    gather(heads_ring, heads_ring.far)
    keep_out(heads_all, heads_out)
    project(here)
    project_step(1)
    for step in range(3, narrow_count):
        project_step(step - 1)
        line_rows.step(step)
    project_step(last)
    keep_merge.wait()
    for offset in range(1, narrow_count):
        merge_copy(offset, line.peer(offset), line.peer(offset)).wait_recv()
    keep_out(merge_own, merge_out)
    for offset in range(1, wide_count):
        wide_copy(offset, (place + offset) % wide_count).wait_recv()
    keep_out(small_all, small_out)
    line_rows.drain()
    for copy in started:
        copy.wait_send()
    heads_ring.drain()
    for copy in outs:
        copy.wait()

    def left(block, carry):
        leave_rows(block).wait()
        leave_triple(block).wait()
        return carry

    lax.fori_loop(0, narrow_count, left, 0)


def gather_front(
    wide_count, narrow_count, layer_input, heads_weight, merge_weight, small, buckets, speeds
):
    rows, width = layer_input.shape
    count, all_columns = heads_weight.shape
    columns = all_columns // narrow_count
    block = count * narrow_count
    anywhere = pl.BlockSpec(memory_space=pl.ANY)
    vmem = pl.BlockSpec(memory_space=pltpu.VMEM)
    dma = pltpu.SemaphoreType.DMA
    lines = small.shape[0]
    shapes = (
        (narrow_count, rows, width),
        (wide_count, block, columns),
        (block, width),
        (wide_count, narrow_count, lines, 128),
    )
    far = narrow_count - 1
    bucket = narrow_count * rows
    table = jax.ShapeDtypeStruct((bucket, HDIM), jnp.float32)
    reach = jax.ShapeDtypeStruct((bucket, 1), jnp.int32)
    return pl.pallas_call(
        functools.partial(gather_kernel, wide_count, narrow_count),
        out_shape=tuple(jax.ShapeDtypeStruct(shape, jnp.bfloat16) for shape in shapes)
        + (
            jax.ShapeDtypeStruct((narrow_count, rows, columns), jnp.float32),
            table,
            table,
            reach,
            reach,
        ),
        in_specs=[anywhere, anywhere, anywhere, vmem, pl.BlockSpec(memory_space=pltpu.SMEM), vmem],
        out_specs=(anywhere,) * 5 + (vmem,) * 4,
        scratch_shapes=[
            pltpu.VMEM(shapes[0], jnp.bfloat16),
            pltpu.VMEM((narrow_count, rows, columns), jnp.float32),
        ]
        + [pltpu.VMEM(shape, jnp.bfloat16) for shape in shapes[1:]]
        + [
            dma((2, narrow_count)),
            dma((narrow_count,)),
            dma((far, 3)),
            dma((narrow_count, 3)),
            dma((far,)),
            dma((narrow_count,)),
            dma((far,)),
            dma((narrow_count,)),
            dma((wide_count - 1,)),
            dma((wide_count,)),
            dma((5,)),
            dma((4,)),
            dma((3, wide_count, 2)),
            dma((wide_count, 2)),
            dma((2, narrow_count)),
        ],
        compiler_params=pltpu.CompilerParams(
            collective_id=5, has_side_effects=True, vmem_limit_bytes=kernel_memory
        ),
        cost_estimate=pl.CostEstimate(
            flops=80 * 10**9, bytes_accessed=200 * 2**20, transcendentals=0
        ),
        name="gather_front",
    )(layer_input, heads_weight, merge_weight, small, buckets, speeds)


def attention_forward_kernel(
    wide_count,
    narrow_count,
    triple,
    heads_shift,
    cosine,
    signed_sine,
    first_query,
    last_query,
    own,
    merge,
    merge_shift,
    gain,
    shift,
    queries,
    keys,
    values,
    probs,
    mixed_out,
    hidden,
    hidden_low,
    normed,
    inv_std,
    merge_out,
    rows_out,
    merge_mat,
    probs_held,
    values_turned,
    outbound,
    mixed,
    mixed_send,
    mixed_recv,
    local_sems,
    ring_send,
    ring_recv,
    own_sem,
    rows_all,
    rows_send,
    rows_recv,
    rows_sem,
):
    line = LineExchange(narrow_count)
    ring_sems = (ring_send, ring_recv, None, None, None, None, own_sem)
    ring = PlaneExchange(wide_count, merge, merge_mat, merge_mat, None, None, ring_sems)
    rows_sems = (rows_send, rows_recv, None, None, None, None, rows_sem)
    rows_ring = PlaneExchange(wide_count, hidden_low, rows_all, rows_all, None, None, rows_sems)
    bucket, own_cols = queries.shape
    rows, width = own.shape
    heads = own_cols // HDIM
    scale = HDIM ** (-0.5)
    greet_plane(ring)
    line.greet(3)
    keep_own = ring.send_own()
    ring_steps = [functools.partial(ring.receive, step) for step in range(1, ring.far + 1)]

    def keep(head):
        return pltpu.make_async_copy(
            probs_held.at[head % 2], probs.at[head], local_sems.at[head % 2]
        )

    def mixed_copy(head, offset, where, sender):
        cols = pl.ds(pl.multiple_of(sender * own_cols + head * HDIM, HDIM), HDIM)
        return line.copy(
            outbound.at[where, :, pl.ds(head * HDIM, HDIM)],
            mixed.at[:, cols],
            mixed_send.at[offset - 1, head],
            mixed_recv.at[sender, head],
            where,
        )

    started = []
    for head in range(heads):
        cols = pl.ds(head * HDIM, HDIM)

        def turn(i, carry):
            here = pl.ds(pl.multiple_of(i * rows, rows), rows)
            for which, target in enumerate((queries, keys, values)):
                wanted = pl.ds(which * own_cols + head * HDIM, HDIM)
                part = triple[here, wanted] + heads_shift[:, wanted]
                if which < 2:
                    part = rotate_lanes(part, cosine[here], -signed_sine[here])
                else:
                    values_turned[:, here] = part.T.astype(jnp.bfloat16)
                target[here, cols] = part.astype(jnp.bfloat16)
            return carry

        lax.fori_loop(0, narrow_count, turn, 0)
        if head >= 2:
            keep(head - 2).wait()
        held = probs_held.at[head % 2]

        def chunk(i, carry):
            here = pl.ds(pl.multiple_of(i * rows, rows), rows)
            scores = dot(keys[:, cols], queries[here, cols], ((1,), (1,))) * scale
            token = i * rows + lax.broadcasted_iota(jnp.int32, (bucket, rows), 1)
            seen = (token >= first_query[...]) & (token <= last_query[...])
            scores = jnp.where(seen, scores, masked_value)
            expo = jnp.exp(scores - jnp.max(scores, axis=0, keepdims=True))
            weights = (expo * (1 / jnp.sum(expo, axis=0, keepdims=True))).astype(jnp.bfloat16)
            held[:, here] = weights
            mixed_part = dot(values_turned[...], weights, ((1,), (0,)))
            outbound[i, :, cols] = mixed_part.T.astype(jnp.bfloat16)
            return carry

        lax.fori_loop(0, narrow_count, chunk, 0)
        keep(head).start()
        for offset in range(1, narrow_count):
            copy = mixed_copy(head, offset, line.peer(offset), line.mine)
            copy.start()
            started.append(copy)
        if ring_steps and head >= heads - len(ring_steps):
            ring_steps.pop(0)()
    own_mixed = pltpu.make_async_copy(
        outbound.at[line.mine],
        mixed.at[:, pl.ds(pl.multiple_of(line.mine * own_cols, own_cols), own_cols)],
        local_sems.at[3],
    )
    own_mixed.start()
    own_mixed.wait()
    keep_own.wait()
    for step in ring_steps:
        step()
    for offset in range(ring.ring):
        ring.receive_mate(offset)
    keep_merge = pltpu.make_async_copy(merge_mat, merge_out, local_sems.at[2])
    keep_merge.start()
    for offset in range(1, narrow_count):
        for head in range(heads):
            mixed_copy(head, offset, line.peer(offset), line.peer(offset)).wait_recv()
    mixed_out[...] = mixed[...]

    def merge_cols(cols):
        hidden[:, cols] = (
            residual_scale * own[:, cols].astype(jnp.float32)
            + dot(mixed[...], merge_mat[:, :, cols].reshape(width, cols.size), ((1,), (0,)))
            + merge_shift[:, cols]
        )

    tiles(width, 256, merge_cols)

    def norm_rows(i, carry):
        some = pl.ds(pl.multiple_of(i * 16, 16), 16)
        result, centred, inverse = normalize(hidden[some], gain[...], shift[...])
        hidden[some] = result
        hidden_low[some] = result.astype(jnp.bfloat16)
        normed[some] = centred
        inv_std[some] = inverse
        return carry

    lax.fori_loop(0, rows // 16, norm_rows, 0)
    keep_rows = rows_ring.send_own()
    for step in range(1, rows_ring.far + 1):
        rows_ring.receive(step)
    for offset in range(rows_ring.ring):
        rows_ring.receive_mate(offset)
    keep_rows.wait()
    keep_rows = pltpu.make_async_copy(rows_all, rows_out, rows_sem)
    keep_rows.start()
    for head in range(max(heads - 2, 0), heads):
        keep(head).wait()
    for copy in started:
        copy.wait_send()
    ring.drain()
    rows_ring.drain()
    keep_merge.wait()
    keep_rows.wait()


def attention_forward(
    wide_count,
    narrow_count,
    triple,
    heads_shift,
    cosine,
    signed_sine,
    first_query,
    last_query,
    layer_input,
    merge_block,
    merge_shift,
    gain,
    shift,
):
    bucket, columns = triple.shape
    rows, width = layer_input.shape
    own_cols = columns // 3
    heads = own_cols // HDIM
    anywhere = pl.BlockSpec(memory_space=pl.ANY)
    vmem = pl.BlockSpec(memory_space=pltpu.VMEM)
    dma = pltpu.SemaphoreType.DMA

    def low_shape(*shape):
        return jax.ShapeDtypeStruct(shape, jnp.bfloat16)

    def wide_shape(*shape):
        return jax.ShapeDtypeStruct(shape, jnp.float32)

    return pl.pallas_call(
        functools.partial(attention_forward_kernel, wide_count, narrow_count),
        out_shape=(
            low_shape(bucket, own_cols),
            low_shape(bucket, own_cols),
            low_shape(bucket, own_cols),
            low_shape(heads, bucket, bucket),
            low_shape(rows, width),
            wide_shape(rows, width),
            low_shape(rows, width),
            wide_shape(rows, width),
            wide_shape(rows, 1),
            low_shape(wide_count, *merge_block.shape),
            low_shape(wide_count, rows, width),
        ),
        in_specs=[vmem] * 7 + [anywhere] + [vmem] * 3,
        out_specs=(vmem, vmem, vmem, anywhere) + (vmem,) * 5 + (anywhere,) * 2,
        scratch_shapes=[
            pltpu.VMEM((wide_count, *merge_block.shape), jnp.bfloat16),
            pltpu.VMEM((2, bucket, bucket), jnp.bfloat16),
            pltpu.VMEM((HDIM, bucket), jnp.bfloat16),
            pltpu.VMEM((narrow_count, rows, own_cols), jnp.bfloat16),
            pltpu.VMEM((rows, width), jnp.bfloat16),
            dma((narrow_count - 1, heads)),
            dma((narrow_count, heads)),
            dma((4,)),
            dma((3, wide_count, 2)),
            dma((wide_count, 2)),
            dma(()),
            pltpu.VMEM((wide_count, rows, width), jnp.bfloat16),
            dma((3, wide_count, 2)),
            dma((wide_count, 2)),
            dma(()),
        ],
        compiler_params=pltpu.CompilerParams(
            collective_id=6, has_side_effects=True, vmem_limit_bytes=kernel_memory
        ),
        cost_estimate=pl.CostEstimate(
            flops=60 * 10**9, bytes_accessed=200 * 2**20, transcendentals=0
        ),
        name="attention_forward",
    )(
        triple,
        heads_shift,
        cosine,
        signed_sine,
        first_query,
        last_query,
        layer_input,
        merge_block,
        merge_shift,
        gain,
        shift,
    )


def shards(
    layer_input,
    heads_weight,
    heads_bias,
    merge_weight,
    merge_bias,
    norm_gains,
    norm_shifts,
    expand_weight,
    expand_bias,
    reduce_weight,
    reduce_bias,
    joined,
    prefix,
    cotangent,
):
    tok_rows, model_width = layer_input.shape
    wide_count = lax.axis_size("wide")
    narrow_count = lax.axis_size("narrow")
    count = wide_count * narrow_count
    bucket_len = tok_rows * narrow_count
    own_heads = HEADS // narrow_count
    own_cols = own_heads * HDIM
    share = expand_weight.shape[2]
    narrow_index = lax.axis_index("narrow")
    smalls = (heads_bias, merge_bias, norm_gains, norm_shifts, expand_bias, reduce_bias)
    (
        rows_input,
        heads_mat,
        merge_block,
        small_all,
        triple,
        cosine,
        signed_sine,
        first_query,
        last_query,
    ) = gather_front(
        wide_count,
        narrow_count,
        layer_input,
        heads_weight,
        merge_weight,
        pack_small(smalls),
        jnp.concatenate([joined, prefix[0]]),
        jnp.asarray(rotary_speeds(HDIM)),
    )
    rows_input = rows_input.reshape(bucket_len, model_width)
    heads_mat = heads_mat.reshape(model_width, 3 * own_cols)
    triple = triple.reshape(bucket_len, 3 * own_cols)
    heads_shift, merge_shift, gains, shifts = unpack_small(small_all, smalls)[:4]
    own_shift = lax.dynamic_index_in_dim(
        heads_shift.reshape(3, narrow_count, own_cols), narrow_index, 1, keepdims=False
    ).reshape(1, -1)
    (
        queries,
        keys,
        values,
        probs_low,
        mixed,
        hidden,
        hidden_low,
        normed_one,
        inv_one,
        merge_full,
        rows_all,
    ) = attention_forward(
        wide_count,
        narrow_count,
        triple,
        own_shift,
        cosine,
        signed_sine,
        first_query,
        last_query,
        layer_input,
        merge_block,
        merge_shift.reshape(1, -1),
        gains[0].reshape(1, -1),
        shifts[0].reshape(1, -1),
    )

    small_late, hidden = lax.optimization_barrier((small_all, hidden))
    late_gains, late_shifts, expand_shift, reduce_shift = unpack_small(small_late, smalls)[2:]
    tile_rows = -share % 16
    padded = -(-share // 256) * 256
    expand_low = jnp.pad(expand_weight.transpose(1, 2, 0), ((0, 0), (0, tile_rows), (0, 0)))
    expand_low, _ = lax.optimization_barrier((expand_low, small_all))
    expand_full = lax.all_gather(expand_low, "narrow", axis=2, tiled=True)
    reduce_low = jnp.pad(reduce_weight, ((0, tile_rows), (0, 0)))
    (
        reduce_full,
        active,
        slope,
        gelu,
        layer_output,
        sum_two_grad,
        feed_grad,
        row_sums,
    ) = geglu_forward(
        wide_count,
        narrow_count,
        rows_all,
        expand_full,
        reduce_low,
        jnp.pad(expand_shift, ((0, 0), (0, padded - share))),
        hidden,
        cotangent,
        reduce_shift.reshape(1, -1),
        late_gains[1].reshape(1, -1),
        late_shifts[1].reshape(1, -1),
    )
    reduce_weight_gradient, expand_part, hidden_part, unit_sums = geglu_backward(
        wide_count,
        narrow_count,
        feed_grad,
        expand_full,
        reduce_full,
        slope,
        gelu,
        active,
        rows_all,
    )
    expand_weight_gradient = (
        lax.psum_scatter(expand_part, "narrow", scatter_dimension=2, tiled=True)[:, :share]
        .astype(jnp.float32)
        .transpose(2, 0, 1)
    )
    (
        triple_grad,
        merge_weight_gradient,
        heads_sums,
        merge_sums,
        sum_one_grad,
        norm_one_sums,
    ) = attention_backward(
        wide_count,
        narrow_count,
        sum_two_grad,
        hidden_part,
        normed_one,
        inv_one,
        late_gains[0].reshape(1, -1),
        merge_full.reshape(model_width, model_width),
        mixed,
        queries,
        keys,
        values,
        probs_low,
        cosine,
        signed_sine,
    )

    mine_narrow = (jnp.arange(narrow_count) == narrow_index).astype(jnp.float32)
    mine_wide = (jnp.arange(wide_count) == lax.axis_index("wide")).astype(jnp.float32)
    heads_sums = (heads_sums.reshape(3, 1, own_cols) * mine_narrow[None, :, None]).reshape(count, 1, -1)
    norm_sums = jnp.stack([norm_one_sums[0], row_sums[0], norm_one_sums[1], row_sums[1]])
    norm_sums = norm_sums.reshape(4, count, -1).transpose(1, 0, 2)
    expand_sums = unit_sums[:, :share].reshape(2, narrow_count, -1).transpose(1, 0, 2)[None]
    expand_sums = (expand_sums * mine_wide[:, None, None, None]).reshape(count, 2, -1)
    reduce_sums = row_sums[2].reshape(1, narrow_count, 1, -1)
    reduce_sums = jnp.broadcast_to(
        reduce_sums, (wide_count, narrow_count, 1, reduce_sums.shape[3])
    ).reshape(count, 1, -1)
    pieces = (heads_sums, merge_sums.reshape(count, 1, -1), norm_sums, expand_sums, reduce_sums)
    packed = []
    for piece in pieces:
        piece = jnp.pad(piece, ((0, 0), (0, 0), (0, -piece.shape[2] % 128)))
        packed.append(piece.reshape(count, -1, 128))
    packed = jnp.concatenate(packed, axis=1)
    packed = jnp.pad(packed, ((0, 0), (0, -packed.shape[1] % 8), (0, 0)))
    (
        input_gradient,
        heads_weight_gradient,
        heads_bias_gradient,
        merge_bias_gradient,
        gains_gradient,
        shifts_gradient,
        expand_bias_gradient,
        reduce_bias_gradient,
    ) = input_backward(
        wide_count,
        narrow_count,
        rows_input,
        triple_grad,
        heads_mat,
        packed.reshape(wide_count, narrow_count, -1, 128),
        sum_one_grad,
        (
            (1, heads_bias.size),
            (1, merge_bias.size),
            norm_gains.shape,
            norm_shifts.shape,
            expand_bias.shape,
            (1, reduce_bias.size),
        ),
    )
    return (
        layer_output,
        input_gradient,
        heads_weight_gradient,
        heads_bias_gradient[0],
        merge_weight_gradient,
        merge_bias_gradient[0],
        gains_gradient,
        shifts_gradient,
        expand_weight_gradient,
        expand_bias_gradient,
        reduce_weight_gradient[:share],
        reduce_bias_gradient[0],
    )


def solution(mesh):
    return jax.shard_map(
        shards,
        mesh=mesh,
        in_specs=(
            P(("wide", "narrow"), None),
            P(("wide", "narrow"), None),
            P(("wide", "narrow")),
            P(("wide", "narrow"), None),
            P(("wide", "narrow")),
            P(None, ("wide", "narrow")),
            P(None, ("wide", "narrow")),
            P("narrow", None, "wide"),
            P(None, ("wide", "narrow")),
            P("wide", "narrow"),
            P("narrow"),
            P("wide"),
            P("wide", None),
            P(("wide", "narrow"), None),
        ),
        out_specs=(
            P(("wide", "narrow"), None),
            P(("wide", "narrow"), None),
            P(("wide", "narrow"), None),
            P(("wide", "narrow")),
            P(("wide", "narrow"), None),
            P(("wide", "narrow")),
            P(None, ("wide", "narrow")),
            P(None, ("wide", "narrow")),
            P("narrow", None, "wide"),
            P(None, ("wide", "narrow")),
            P("wide", "narrow"),
            P("narrow"),
        ),
        check_vma=False,
    )
```

```python
import functools
import math

import jax
import jax.numpy as jnp
import numpy as np
from jax import lax
from jax.experimental import pallas as pl
from jax.experimental.pallas import tpu as pltpu
from jax.sharding import PartitionSpec as P

HEADS = 16
HDIM = 128


residual_scale = 48.0**0.5
norm_eps = 1e-05
masked_value = -1e30
kernel_memory = 60 * 2**20


def rotary_speeds(head_size):
    index = np.arange(head_size) % (head_size // 2)
    return (10000.0 ** (-2.0 * index / head_size)).astype(np.float32)[None]


def normalize(values, gain, shift):
    centre = jnp.mean(values, axis=-1, keepdims=True)
    centred = values - centre
    variance = jnp.mean(centred * centred, axis=-1, keepdims=True)
    inv_std = lax.rsqrt(variance + norm_eps)
    normed = centred * inv_std
    return (normed * gain + shift, normed, inv_std)


def normalize_back(upstream, normed, inv_std, gain):
    scaled = upstream * gain
    return inv_std * (
        scaled
        - jnp.mean(scaled, axis=-1, keepdims=True)
        - normed * jnp.mean(scaled * normed, axis=-1, keepdims=True)
    )


def dot(left, right, dims):
    return lax.dot_general(left, right, (dims, ((), ())), preferred_element_type=jnp.float32)


def low(values):
    return values.astype(jnp.bfloat16)


def row_places(shapes):
    places = []
    start = 0
    for first, size in shapes:
        places.append((start, first, size))
        start += first * -(-size // 128)
    return places, start + -start % 8


def small_piece(block, place, index):
    start, _, size = place
    rows = -(-size // 128)
    pieces = []
    for row in range(rows):
        stop = min(size - 128 * row, 128)
        here = start + index * rows + row
        pieces.append(block[here : here + 1, 0:stop])
    return pieces


def spread_small(target, small, place, index, row=0):
    at = 0
    for wide in range(small.shape[0]):
        for narrow in range(small.shape[1]):
            for piece in small_piece(small.at[wide, narrow], place, index):
                target[row : row + 1, at : at + piece.shape[1]] = piece
                at += piece.shape[1]


def ring_place(wide_count):
    ring = wide_count // 2
    mine = lax.axis_index("wide")
    chip = mine // 2
    core = mine % 2
    position = 2 * (chip // 2) + (chip % 2 + chip // 2) % 2
    return ring, position, core


def chip_at(position, ring):
    position = (position + 2 * ring) % ring
    return 2 * (position // 2) + (position + position // 2) % 2


class PlaneExchange:
    def __init__(self, wide_count, own, blocks, parts, from_mate, incoming, sems, cols=None):
        self.ring, self.position, self.core = ring_place(wide_count)
        self.own, self.blocks, self.parts = own, blocks, parts
        self.from_mate, self.incoming = from_mate, incoming
        (
            self.gather_send,
            self.gather_recv,
            self.mate_send,
            self.mate_recv,
            self.sum_send,
            self.sum_recv,
            self.own_sem,
        ) = sems
        self.half = parts.shape[1] // 2
        self.cols = slice(None) if cols is None else cols
        self.far = self.ring // 2
        self.started = []

    def device(self, offset, mate=False):
        core = 1 - self.core if mate else self.core
        return {"wide": 2 * chip_at(self.position + offset, self.ring) + core}

    def slot(self, offset, mate=False):
        core = 1 - self.core if mate else self.core
        return 2 * chip_at(self.position + offset, self.ring) + core

    def rows(self, part):
        return pl.ds(part * self.half, self.half)

    def greet(self):
        barrier = pltpu.get_barrier_semaphore()
        for where in (self.device(-1), self.device(1), self.device(0, True)):
            pl.semaphore_signal(
                barrier, inc=1, device_id=where, device_id_type=pl.DeviceIdType.MESH
            )
        pl.semaphore_wait(barrier, 3)

    def start(self, source, target, send_sem, recv_sem, where):
        copy = pltpu.make_async_remote_copy(
            src_ref=source,
            dst_ref=target,
            send_sem=send_sem,
            recv_sem=recv_sem,
            device_id=where,
            device_id_type=pl.DeviceIdType.MESH,
        )
        copy.start()
        self.started.append(copy)

    def pass_on(self, lane, slot, part, where, source=None):
        target = self.blocks.at[slot, self.rows(part)]
        self.start(
            target if source is None else source,
            target,
            self.gather_send.at[lane, slot, part],
            self.gather_recv.at[slot, part],
            where,
        )

    def arrived(self, slot, part):
        target = self.blocks.at[slot, self.rows(part)]
        pltpu.make_async_remote_copy(
            src_ref=target,
            dst_ref=target,
            send_sem=self.gather_send.at[0, slot, part],
            recv_sem=self.gather_recv.at[slot, part],
            device_id=self.device(1),
            device_id_type=pl.DeviceIdType.MESH,
        ).wait_recv()

    def send_own(self):
        slot = self.slot(0)
        keep = None
        own = self.blocks.at[slot]
        if self.own is not None:
            own = self.own
            keep = pltpu.make_async_copy(own, self.blocks.at[slot], self.own_sem)
            keep.start()
        first, second = own.at[self.rows(0)], own.at[self.rows(1)]
        self.pass_on(0, slot, 0, self.device(1), first)
        self.pass_on(1, slot, 1, self.device(-1), second)
        self.pass_on(2, slot, 0, self.device(0, True), first)
        self.pass_on(2, slot, 1, self.device(0, True), second)
        self.pass_on(0, slot, 1, self.device(1), second)
        self.pass_on(1, slot, 0, self.device(-1), first)
        return keep

    def receive(self, distance):
        mate = self.device(0, True)
        left, right = self.slot(-distance), self.slot(distance)
        if distance == self.far:
            for part in range(2):
                self.arrived(left, part)
                self.pass_on(2, left, part, mate)
            return
        further = distance < self.far - 1
        self.arrived(left, 0)
        self.pass_on(0, left, 0, self.device(1))
        self.pass_on(2, left, 0, mate)
        self.arrived(right, 1)
        self.pass_on(1, right, 1, self.device(-1))
        self.pass_on(2, right, 1, mate)
        self.arrived(left, 1)
        if further:
            self.pass_on(0, left, 1, self.device(1))
        self.pass_on(2, left, 1, mate)
        self.arrived(right, 0)
        if further:
            self.pass_on(1, right, 0, self.device(-1))
        self.pass_on(2, right, 0, mate)

    def receive_mate(self, offset):
        for part in range(2):
            self.arrived(self.slot(offset, True), part)

    def share(self, offset):
        chip = chip_at(self.position + offset, self.ring)
        self.start(
            self.parts.at[self.slot(offset, True), :, self.cols],
            self.from_mate.at[chip, :, self.cols],
            self.mate_send.at[chip],
            self.mate_recv.at[chip],
            self.device(0, True),
        )

    def shared(self, offset):
        chip = chip_at(self.position + offset, self.ring)
        pltpu.make_async_remote_copy(
            src_ref=self.parts.at[self.slot(offset), :, self.cols],
            dst_ref=self.from_mate.at[chip, :, self.cols],
            send_sem=self.mate_send.at[chip],
            recv_sem=self.mate_recv.at[chip],
            device_id=self.device(0, True),
            device_id_type=pl.DeviceIdType.MESH,
        ).wait_recv()

    def chip_sum(self, offset, rows):
        chip = chip_at(self.position + offset, self.ring)
        return self.parts[self.slot(offset), rows, self.cols].astype(
            jnp.float32
        ) + self.from_mate[chip, rows, self.cols].astype(jnp.float32)

    def send_sum(self, way, distance, part):
        offset = distance if way == 0 else -distance
        begins = self.far if part == way else self.far - 1
        slot = self.slot(offset)
        if distance < begins:
            self.sum_arrived(way, distance, part)

        def chunk(i, carry):
            here = pl.ds(pl.multiple_of(i * 16, 16), 16)
            there = pl.ds(pl.multiple_of(part * self.half + i * 16, 16), 16)
            total = self.chip_sum(offset, there)
            if distance < begins:
                total += self.incoming[way, distance, part, here, self.cols].astype(jnp.float32)
            self.parts[slot, there, self.cols] = total.astype(jnp.bfloat16)
            return carry

        lax.fori_loop(0, self.half // 16, chunk, 0)
        self.start(
            self.parts.at[slot, self.rows(part), self.cols],
            self.incoming.at[way, distance - 1, part, :, self.cols],
            self.sum_send.at[way, distance - 1, part],
            self.sum_recv.at[way, distance - 1, part],
            self.device(1 if way == 0 else -1),
        )

    def sum_arrived(self, way, distance, part):
        target = self.incoming.at[way, distance, part, :, self.cols]
        pltpu.make_async_remote_copy(
            src_ref=target,
            dst_ref=target,
            send_sem=self.sum_send.at[way, distance, part],
            recv_sem=self.sum_recv.at[way, distance, part],
            device_id=self.device(1),
            device_id_type=pl.DeviceIdType.MESH,
        ).wait_recv()

    def run(self, first, second, before, after_far):
        def compute(chip):
            first(chip)
            second(chip)

        keep = self.send_own()
        keep.wait()
        self.receive_mate(0)
        compute(chip_at(self.position, self.ring))
        self.share(0)
        for distance in range(1, self.far):
            self.receive(distance)
            for offset in (-distance, distance):
                self.receive_mate(offset)
                compute(chip_at(self.position + offset, self.ring))
                self.share(offset)
            if distance == self.far - 1:
                self.first_sums()
        self.receive(self.far)
        self.receive_mate(self.far)
        farthest = chip_at(self.position + self.far, self.ring)
        first(farthest)
        before()
        second(farthest)
        self.share(self.far)
        self.far_sums()
        after_far()
        self.last_sums()

    def start_sums(self, compute):
        compute(chip_at(self.position + self.far, self.ring))
        self.share(self.far)
        for distance in range(self.far - 1, 0, -1):
            for offset in (-distance, distance):
                compute(chip_at(self.position + offset, self.ring))
                self.share(offset)
            if distance == self.far - 1:
                self.far_sums()
                self.first_sums()
        compute(chip_at(self.position, self.ring))
        self.share(0)

    def first_sums(self):
        distance = self.far - 1
        self.shared(distance)
        self.send_sum(0, distance, 1)
        self.shared(-distance)
        self.send_sum(1, distance, 0)

    def far_sums(self):
        self.shared(self.far)
        self.send_sum(0, self.far, 0)
        self.send_sum(1, self.far, 1)

    def last_sums(self):
        for distance in range(self.far - 1, 0, -1):
            if distance < self.far - 1:
                self.shared(distance)
                self.shared(-distance)
            self.send_sum(0, distance, 0)
            self.send_sum(1, distance, 1)
            if distance < self.far - 1:
                self.send_sum(0, distance, 1)
                self.send_sum(1, distance, 0)

    def finish(self, result):
        self.shared(0)
        for part in range(2):
            for way in range(2):
                self.sum_arrived(way, 0, part)

            def chunk(i, carry):
                here = pl.ds(pl.multiple_of(i * 16, 16), 16)
                there = pl.ds(pl.multiple_of(part * self.half + i * 16, 16), 16)
                total = self.chip_sum(0, there)
                for way in range(2):
                    total += self.incoming[way, 0, part, here, self.cols].astype(jnp.float32)
                result[there, self.cols] = total.astype(result.dtype)
                return carry

            lax.fori_loop(0, self.half // 16, chunk, 0)

    def drain(self):
        for copy in self.started:
            copy.wait_send()


def sum_scratch(wide_count, rows, width):
    ring = wide_count // 2
    far = ring // 2
    dma = pltpu.SemaphoreType.DMA
    return [
        pltpu.VMEM((wide_count, rows, width), jnp.bfloat16),
        pltpu.VMEM((ring, rows, width), jnp.bfloat16),
        pltpu.VMEM((2, far, 2, rows // 2, width), jnp.bfloat16),
        dma((ring,)),
        dma((ring,)),
        dma((2, far, 2)),
        dma((2, far, 2)),
    ]


def exchange_scratch(wide_count, rows, width):
    dma = pltpu.SemaphoreType.DMA
    return [
        pltpu.VMEM((wide_count, rows, width), jnp.bfloat16),
        dma((3, wide_count, 2)),
        dma((wide_count, 2)),
        dma(()),
    ] + sum_scratch(wide_count, rows, width)


def load_padded(source, target, sem):
    filled = source.shape[0]
    copy = pltpu.make_async_copy(source, target.at[pl.ds(0, filled)], sem)
    copy.start()
    if filled < target.shape[0]:
        target[pl.ds(filled, target.shape[0] - filled)] = jnp.zeros(
            (target.shape[0] - filled, target.shape[1]), target.dtype
        )
    return copy


def pair_rows(ref, chip):
    block = ref[pl.ds(2 * chip, 2)]
    return block.reshape(2 * block.shape[1], block.shape[2])


def set_pair(ref, chip, cols, value):
    rows = ref.shape[1]
    ref[2 * chip, :, cols] = value[:rows].astype(ref.dtype)
    ref[2 * chip + 1, :, cols] = value[rows:].astype(ref.dtype)


def tiles(count, tile, body, start=0):
    def step(i, carry):
        body(pl.ds(pl.multiple_of(start + i * tile, tile), tile))
        return carry

    lax.fori_loop(0, count // tile, step, 0)


class LineExchange:
    def __init__(self, narrow_count):
        self.count = narrow_count
        self.mine = lax.axis_index("narrow")
        self.started = []

    def peer(self, offset):
        return (self.mine + offset) % self.count

    def greet(self, extra=0):
        barrier = pltpu.get_barrier_semaphore()
        for offset in range(1, self.count):
            pl.semaphore_signal(
                barrier,
                inc=1,
                device_id={"narrow": self.peer(offset)},
                device_id_type=pl.DeviceIdType.MESH,
            )
        pl.semaphore_wait(barrier, self.count - 1 + extra)

    def copy(self, source, target, send_sem, recv_sem, where):
        return pltpu.make_async_remote_copy(
            src_ref=source,
            dst_ref=target,
            send_sem=send_sem,
            recv_sem=recv_sem,
            device_id={"narrow": where},
            device_id_type=pl.DeviceIdType.MESH,
        )

    def send(self, offset, source, landing, send_sems, recv_sems):
        peer = self.peer(offset)
        copy = self.copy(
            source, landing.at[self.mine], send_sems.at[offset - 1], recv_sems.at[self.mine], peer
        )
        copy.start()
        self.started.append(copy)

    def arrived(self, offset, landing, send_sems, recv_sems):
        peer = self.peer(offset)
        self.copy(
            landing.at[peer], landing.at[peer], send_sems.at[offset - 1], recv_sems.at[peer], peer
        ).wait_recv()

    def drain(self):
        for copy in self.started:
            copy.wait_send()


class LineSum:
    def __init__(self, line, view, landing, send_sems, recv_sems):
        self.line, self.view, self.landing = line, view, landing
        self.send_sems, self.recv_sems = send_sems, recv_sems
        self.last = line.count - 1

    def reaches(self, way, offset):
        here = self.line.mine
        return here + offset <= self.last if way == 0 else here - offset >= 0

    def follows(self, way):
        here = self.line.mine
        return here > 0 if way == 0 else here < self.last

    def target(self, way, offset):
        return self.line.mine + offset if way == 0 else self.line.mine - offset

    def copy(self, way, offset):
        return self.line.copy(
            self.view(self.target(way, offset)),
            self.landing.at[way, offset - 1],
            self.send_sems.at[way, offset - 1],
            self.recv_sems.at[way, offset - 1],
            self.line.mine + 1 if way == 0 else self.line.mine - 1,
        )

    def arrived(self, way, offset):
        landing = self.landing.at[way, offset]
        self.line.copy(
            landing,
            landing,
            self.send_sems.at[way, offset],
            self.recv_sems.at[way, offset],
            self.line.mine,
        ).wait_recv()

    def add(self, way, offset):
        held = self.view(self.target(way, offset))

        def chunk(i, carry):
            some = pl.ds(pl.multiple_of(i * 16, 16), 16)
            held[some] = (
                held[some].astype(jnp.float32)
                + self.landing[way, offset, some].astype(jnp.float32)
            ).astype(jnp.bfloat16)
            return carry

        lax.fori_loop(0, self.landing.shape[2] // 16, chunk, 0)

    def begin(self, offset):
        for way in range(2):

            @pl.when(self.reaches(way, offset) & jnp.logical_not(self.follows(way)))
            def _():
                self.copy(way, offset).start()

    def step(self, offset):
        for way in range(2):

            @pl.when(self.reaches(way, offset) & self.follows(way))
            def _():
                self.arrived(way, offset)
                self.add(way, offset)
                self.copy(way, offset).start()

    def finish(self, result):
        held = self.view(self.line.mine)
        count = self.landing.shape[2] // 16

        def begin(i, carry):
            some = pl.ds(pl.multiple_of(i * 16, 16), 16)
            result[some] = held[some].astype(result.dtype)
            return carry

        lax.fori_loop(0, count, begin, 0)
        for way in range(2):

            @pl.when(self.follows(way))
            def _():
                self.arrived(way, 0)

                def chunk(i, carry):
                    some = pl.ds(pl.multiple_of(i * 16, 16), 16)
                    result[some] += self.landing[way, 0, some].astype(result.dtype)
                    return carry

                lax.fori_loop(0, count, chunk, 0)

    def drain(self):
        for offset in range(1, self.last + 1):
            for way in range(2):

                @pl.when(self.reaches(way, offset))
                def _():
                    self.copy(way, offset).wait_send()


class LineGather:
    def __init__(self, line, view, send_sems, recv_sems):
        self.line, self.view = line, view
        self.send_sems, self.recv_sems = send_sems, recv_sems
        self.last = line.count - 1

    def copy(self, way, block):
        target = self.view(block)
        here = self.line.mine
        return self.line.copy(
            target,
            target,
            self.send_sems.at[way, block],
            self.recv_sems.at[block],
            here + 1 if way == 0 else here - 1,
        )

    def goes(self, way):
        return self.line.mine < self.last if way == 0 else self.line.mine > 0

    def has(self, way, step):
        here = self.line.mine
        return here - step >= 0 if way == 0 else here + step <= self.last

    def block(self, way, step):
        return self.line.mine - step if way == 0 else self.line.mine + step

    def send_own(self):
        for way in range(2):

            @pl.when(self.goes(way))
            def _():
                self.copy(way, self.line.mine).start()

    def step(self, step):
        for way in range(2):

            @pl.when(self.has(way, step))
            def _():
                self.copy(way, self.block(way, step)).wait_recv()

                @pl.when(self.goes(way))
                def _():
                    self.copy(way, self.block(way, step)).start()

    def each(self, step, body):
        for way in range(2):

            @pl.when(self.has(way, step))
            def _():
                body(self.block(way, step))

    def drain(self):
        for way in range(2):
            for step in range(self.last + 1):

                @pl.when(self.has(way, step) & self.goes(way))
                def _():
                    self.copy(way, self.block(way, step)).wait_send()


def greet_plane(plane):
    barrier = pltpu.get_barrier_semaphore()
    for where in (plane.device(-1), plane.device(1), plane.device(0, True)):
        pl.semaphore_signal(barrier, inc=1, device_id=where, device_id_type=pl.DeviceIdType.MESH)


def geglu_forward_kernel(
    wide_count,
    narrow_count,
    places,
    rows_all,
    expand,
    reduce,
    small,
    hidden,
    cotangent,
    reduce_out,
    active_out,
    slope_out,
    gelu_out,
    layer_output,
    sum_grad,
    feed_grad,
    row_sums,
    feed,
    blocks,
    parts,
    from_mate,
    incoming,
    mate_send,
    mate_recv,
    sum_send,
    sum_recv,
    expand_mat,
    reduce_mat,
    active,
    slope,
    gelu,
    load_sems,
    keep_sems,
    reduce_send,
    reduce_recv,
    late_mate_send,
    late_mate_recv,
    late_sum_send,
    late_sum_recv,
    shift,
    vectors,
):
    sems = (None, None, mate_send, mate_recv, sum_send, sum_recv, None)
    late_sems = (None, None, late_mate_send, late_mate_recv, late_sum_send, late_sum_recv, None)
    line = LineExchange(narrow_count)
    filled, cols = reduce.shape
    width = rows_all.shape[2]
    upper = (2 * line.mine) // narrow_count
    late = pl.multiple_of((1 - upper) * (width - cols), cols)
    early = pl.multiple_of(upper * cols, cols)
    plane = PlaneExchange(
        wide_count, None, None, parts, from_mate, incoming, sems, pl.ds(early, width - cols)
    )
    late_plane = PlaneExchange(
        wide_count, None, None, parts, from_mate, incoming, late_sems, pl.ds(late, cols)
    )
    loads = [
        load_padded(expand.at[0], expand_mat.at[0], load_sems.at[0]),
        load_padded(expand.at[1], expand_mat.at[1], load_sems.at[1]),
        pltpu.make_async_copy(rows_all, blocks, load_sems.at[4]),
    ]
    loads[2].start()

    def reduce_cols(block):
        return reduce_mat.at[
            pl.ds(0, filled), pl.ds(pl.multiple_of(block * cols, cols), cols)
        ]

    line_reduce = LineGather(line, reduce_cols, reduce_send, reduce_recv)
    own_reduce = pltpu.make_async_copy(reduce, reduce_cols(line.mine), load_sems.at[2])
    own_reduce.start()
    if filled < reduce_mat.shape[0]:
        reduce_mat[filled:] = jnp.zeros(
            (reduce_mat.shape[0] - filled, reduce_mat.shape[1]), reduce_mat.dtype
        )
    greet_plane(plane)
    line.greet(3)
    place = lax.axis_index("wide")
    shift[...] = jnp.zeros_like(shift)
    for index in range(2):
        at = 0
        for block in range(narrow_count):
            for piece in small_piece(small.at[place, block], places[4], index):
                shift[index : index + 1, at : at + piece.shape[1]] = piece
                at += piece.shape[1]
    at = 0
    for block in range(narrow_count):
        for piece in small_piece(small.at[0, block], places[5], 0):
            vectors[0:1, at : at + piece.shape[1]] = piece
            at += piece.shape[1]
    spread_small(vectors, small, places[2], 1, 1)
    spread_small(vectors, small, places[3], 1, 2)
    own_reduce.wait()
    line_reduce.send_own()
    kept = []
    waiting = list(loads)

    def compute(chip):
        while waiting:
            waiting.pop().wait()

        def units(cols):
            rows = pair_rows(blocks, chip)
            gate = dot(rows, expand_mat[0, cols], ((1,), (1,))) + shift[0:1, cols]
            upper = dot(rows, expand_mat[1, cols], ((1,), (1,))) + shift[1:2, cols]
            factor = math.sqrt(2 / math.pi)
            square = gate * gate
            bend = jnp.tanh(factor * gate * (1 + 0.044715 * square))
            value = 0.5 * gate * (1 + bend)
            pull = 0.5 * (1 + bend) + 0.5 * gate * (1 - bend * bend) * factor * (
                1 + 3 * 0.044715 * square
            )
            set_pair(active, chip, cols, value * upper)
            set_pair(slope, chip, cols, pull * upper)
            set_pair(gelu, chip, cols, value)

        tiles(active.shape[2], 256, units)

        pair = pl.ds(2 * chip, 2)
        for index, (source, target) in enumerate(
            ((active, active_out), (slope, slope_out), (gelu, gelu_out))
        ):
            copy = pltpu.make_async_copy(
                source.at[pair], target.at[pair], keep_sems.at[chip, index]
            )
            copy.start()
            kept.append(copy)

    def compute_sums(start, count):
        def compute(chip):
            def outputs(some):
                part = dot(pair_rows(active, chip), reduce_mat[:, some], ((1,), (0,)))
                set_pair(parts, chip, some, part)

            tiles(count, 256, outputs, start)

        return compute

    offsets = [0]
    for distance in range(1, plane.far):
        offsets += [-distance, distance]
    offsets.append(plane.far)
    chips = [chip_at(plane.position + offset, plane.ring) for offset in offsets]
    each = -(-len(chips) // (narrow_count - 2))
    for step in range(1, narrow_count - 1):
        if step == 1:
            compute(chips.pop(0))
        for _ in range(min(each, len(chips))):
            compute(chips.pop(0))
        line_reduce.step(step)
    plane.start_sums(compute_sums(early, width - cols))
    line_reduce.step(narrow_count - 1)
    keep_reduce = pltpu.make_async_copy(
        reduce_mat.at[pl.ds(0, filled)], reduce_out, load_sems.at[3]
    )
    keep_reduce.start()
    late_plane.start_sums(compute_sums(late, cols))
    plane.last_sums()
    late_plane.last_sums()
    plane.finish(feed)
    late_plane.finish(feed)

    row_sums[...] = jnp.zeros_like(row_sums)

    def norm_rows(i, carry):
        some = pl.ds(pl.multiple_of(i * 16, 16), 16)
        result, normed, inverse = normalize(
            residual_scale * hidden[some] + feed[some] + vectors[0:1],
            vectors[1:2],
            vectors[2:3],
        )
        layer_output[some] = result.astype(jnp.bfloat16)
        upstream = cotangent[some].astype(jnp.float32)
        total = normalize_back(upstream, normed, inverse, vectors[1:2])
        sum_grad[some] = total
        feed_grad[some] = total.astype(jnp.bfloat16)
        row_sums[0:1] += jnp.sum(upstream * normed, axis=0, keepdims=True)
        row_sums[1:2] += jnp.sum(upstream, axis=0, keepdims=True)
        row_sums[2:3] += jnp.sum(total, axis=0, keepdims=True)
        return carry

    lax.fori_loop(0, rows_all.shape[1] // 16, norm_rows, 0, unroll=2)
    plane.drain()
    late_plane.drain()
    keep_reduce.wait()
    line_reduce.drain()
    for copy in kept:
        copy.wait()


def geglu_forward(
    wide_count,
    narrow_count,
    places,
    rows_all,
    expand,
    reduce_weight,
    small,
    hidden,
    cotangent,
):
    _, rows, width = rows_all.shape
    padded = -(-expand.shape[1] // 256) * 256
    anywhere = pl.BlockSpec(memory_space=pl.ANY)
    vmem = pl.BlockSpec(memory_space=pltpu.VMEM)
    kept = jax.ShapeDtypeStruct((wide_count, rows, padded), jnp.bfloat16)
    scratch = [pltpu.VMEM((rows, width), jnp.float32)]
    scratch.append(pltpu.VMEM((wide_count, rows, width), jnp.bfloat16))
    scratch += sum_scratch(wide_count, rows, width) + [
        pltpu.VMEM((2, padded, width), jnp.bfloat16),
        pltpu.VMEM((padded, width), jnp.bfloat16),
        pltpu.VMEM((wide_count, rows, padded), jnp.bfloat16),
        pltpu.VMEM((wide_count, rows, padded), jnp.bfloat16),
        pltpu.VMEM((wide_count, rows, padded), jnp.bfloat16),
        pltpu.SemaphoreType.DMA((5,)),
        pltpu.SemaphoreType.DMA((wide_count // 2, 3)),
        pltpu.SemaphoreType.DMA((2, narrow_count)),
        pltpu.SemaphoreType.DMA((narrow_count,)),
    ] + sum_scratch(wide_count, rows, width)[3:]
    scratch += [pltpu.VMEM((2, padded), jnp.float32), pltpu.VMEM((3, width), jnp.float32)]
    return pl.pallas_call(
        functools.partial(geglu_forward_kernel, wide_count, narrow_count, places),
        out_shape=(
            jax.ShapeDtypeStruct((reduce_weight.shape[0], width), jnp.bfloat16),
            kept,
            kept,
            kept,
            jax.ShapeDtypeStruct((rows, width), jnp.bfloat16),
            jax.ShapeDtypeStruct((rows, width), jnp.float32),
            jax.ShapeDtypeStruct((rows, width), jnp.bfloat16),
            jax.ShapeDtypeStruct((3, width), jnp.float32),
        ),
        in_specs=[anywhere] * 3 + [vmem] * 3,
        out_specs=(anywhere,) * 4 + (vmem,) * 4,
        scratch_shapes=scratch,
        compiler_params=pltpu.CompilerParams(
            collective_id=1, has_side_effects=True, vmem_limit_bytes=kernel_memory
        ),
        cost_estimate=pl.CostEstimate(
            flops=6 * wide_count * rows * padded * width, bytes_accessed=200 * 2**20, transcendentals=0
        ),
        name="geglu_forward",
    )(
        rows_all,
        expand,
        reduce_weight,
        small,
        hidden,
        cotangent,
    )


def geglu_backward_kernel(
    wide_count,
    narrow_count,
    own,
    expand,
    reduce,
    slope_in,
    gelu_in,
    active_in,
    rows_in,
    reduce_grad,
    expand_part,
    hidden_grad,
    unit_sums,
    blocks,
    gather_send,
    gather_recv,
    own_sem,
    parts,
    from_mate,
    incoming,
    mate_send,
    mate_recv,
    sum_send,
    sum_recv,
    expand_mat,
    reduce_mat,
    slope,
    gelu,
    active,
    rows_all,
    staged,
    load_sems,
    keep_sems,
    line_in,
    line_send,
    line_recv,
):
    sems = (gather_send, gather_recv, mate_send, mate_recv, sum_send, sum_recv, own_sem)
    plane = PlaneExchange(wide_count, own, blocks, parts, from_mate, incoming, sems)
    loads = [
        load_padded(expand.at[0], expand_mat.at[0], load_sems.at[0]),
        load_padded(expand.at[1], expand_mat.at[1], load_sems.at[1]),
        load_padded(reduce, reduce_mat, load_sems.at[2]),
        pltpu.make_async_copy(slope_in, slope, load_sems.at[3]),
        pltpu.make_async_copy(gelu_in, gelu, load_sems.at[4]),
    ]
    late_loads = [
        pltpu.make_async_copy(active_in, active, load_sems.at[5]),
        pltpu.make_async_copy(rows_in, rows_all, load_sems.at[6]),
    ]
    for copy in loads[3:]:
        copy.start()
    unit_sums[...] = jnp.zeros_like(unit_sums)
    line = LineExchange(narrow_count)
    filled, line_cols = line_in.shape[2:]

    def line_part(block):
        return reduce_mat.at[
            pl.ds(0, filled), pl.ds(pl.multiple_of(block * line_cols, line_cols), line_cols)
        ]

    line_sum = LineSum(line, line_part, line_in, line_send, line_recv)
    greet_plane(plane)
    line.greet(3)
    for copy in late_loads:
        copy.start()
    kept = []
    waiting = list(loads)

    def compute(chip):
        while waiting:
            waiting.pop().wait()

        def units(cols):
            pulled = dot(pair_rows(blocks, chip), reduce_mat[cols], ((1,), (1,)))
            pair = pl.ds(2 * chip, 2)
            shape = pulled.shape
            gate_grad = pulled * slope[pair, :, cols].reshape(shape).astype(jnp.float32)
            upper_grad = pulled * gelu[pair, :, cols].reshape(shape).astype(jnp.float32)
            set_pair(slope, chip, cols, gate_grad)
            set_pair(gelu, chip, cols, upper_grad)
            unit_sums[0:1, cols] += jnp.sum(gate_grad, axis=0, keepdims=True)
            unit_sums[1:2, cols] += jnp.sum(upper_grad, axis=0, keepdims=True)

        tiles(slope.shape[2], 256, units)

    def compute_sums(chip):
        def outputs(cols):
            set_pair(
                parts,
                chip,
                cols,
                dot(pair_rows(slope, chip), expand_mat[0, :, cols], ((1,), (0,)))
                + dot(pair_rows(gelu, chip), expand_mat[1, :, cols], ((1,), (0,))),
            )

        tiles(parts.shape[2], 256, outputs)

    def product(left, right, start):
        tokens = left.shape[0] * left.shape[1]
        return dot(
            left[:, :, start : start + 256].reshape(tokens, 256),
            right[...].reshape(tokens, right.shape[2]),
            ((0,), (0,)),
        ).astype(jnp.bfloat16)

    def reduce_work():
        for copy in late_loads:
            copy.wait()

        def reduce_cols(index):
            cols = pl.ds(pl.multiple_of(index * line_cols, line_cols), line_cols)

            def units(some):
                tokens = active.shape[0] * active.shape[1]
                part = dot(
                    active[:, :, some].reshape(tokens, some.size),
                    blocks[:, :, cols].reshape(tokens, line_cols),
                    ((0,), (0,)),
                )
                reduce_mat[some, cols] = part.astype(jnp.bfloat16)

            tiles(active.shape[2], 256, units)

        for offset in range(narrow_count - 1, 0, -1):
            for way in range(2):

                @pl.when(line_sum.reaches(way, offset))
                def _():
                    reduce_cols(line_sum.target(way, offset))

            line_sum.begin(offset)
        reduce_cols(line.mine)

    def expand_work(left, start, target):
        def work():
            index = len(kept)
            if index >= 2:
                kept[index - 2].wait()
            staged[index % 2] = product(left, rows_all, start)
            stop = min(256, target.shape[0] - start)
            copy = pltpu.make_async_copy(
                staged.at[index % 2, pl.ds(0, stop)],
                target.at[pl.ds(start, stop)],
                keep_sems.at[index % 2],
            )
            copy.start()
            kept.append(copy)

        return work

    works = [
        expand_work(left, start, target)
        for left, target in ((slope, expand_part.at[0]), (gelu, expand_part.at[1]))
        for start in range(0, target.shape[0], 256)
    ]
    steps = [
        functools.partial(line_sum.step, offset) for offset in range(narrow_count - 2, 0, -1)
    ]
    third = len(works) // 3
    middle = (len(steps) + 1) // 2

    def many(calls):
        for call in calls:
            call()

    beside = functools.partial(many, steps[:middle] + works[:third])
    plane.run(compute, compute_sums, reduce_work, beside)
    many(works[third : 2 * third] + steps[middle:] + works[2 * third :])
    plane.finish(hidden_grad)
    plane.drain()
    line_sum.finish(reduce_grad)
    line_sum.drain()
    for copy in kept[-2:]:
        copy.wait()


def geglu_backward(
    wide_count,
    narrow_count,
    feed_grad,
    expand,
    reduce_full,
    slope,
    gelu,
    active,
    rows_all,
):
    rows, width = feed_grad.shape
    padded = slope.shape[2]
    anywhere = pl.BlockSpec(memory_space=pl.ANY)
    vmem = pl.BlockSpec(memory_space=pltpu.VMEM)
    scratch = exchange_scratch(wide_count, rows, width) + [
        pltpu.VMEM((2, padded, width), jnp.bfloat16),
        pltpu.VMEM((padded, width), jnp.bfloat16),
        pltpu.VMEM((wide_count, rows, padded), jnp.bfloat16),
        pltpu.VMEM((wide_count, rows, padded), jnp.bfloat16),
        pltpu.VMEM((wide_count, rows, padded), jnp.bfloat16),
        pltpu.VMEM((wide_count, rows, width), jnp.bfloat16),
        pltpu.VMEM((2, 256, width), jnp.bfloat16),
        pltpu.SemaphoreType.DMA((7,)),
        pltpu.SemaphoreType.DMA((2,)),
        pltpu.VMEM(
            (2, narrow_count - 1, reduce_full.shape[0], width // narrow_count), jnp.bfloat16
        ),
        pltpu.SemaphoreType.DMA((2, narrow_count - 1)),
        pltpu.SemaphoreType.DMA((2, narrow_count - 1)),
    ]
    return pl.pallas_call(
        functools.partial(geglu_backward_kernel, wide_count, narrow_count),
        out_shape=(
            jax.ShapeDtypeStruct(
                (reduce_full.shape[0], width // narrow_count), jnp.float32
            ),
            jax.ShapeDtypeStruct(expand.shape, jnp.bfloat16),
            jax.ShapeDtypeStruct((rows, width), jnp.float32),
            jax.ShapeDtypeStruct((2, padded), jnp.float32),
        ),
        in_specs=[anywhere] * 7,
        out_specs=(vmem, anywhere, vmem, vmem),
        scratch_shapes=scratch,
        compiler_params=pltpu.CompilerParams(
            collective_id=2, has_side_effects=True, vmem_limit_bytes=63 * 2**20
        ),
        cost_estimate=pl.CostEstimate(
            flops=12 * wide_count * rows * padded * width, bytes_accessed=200 * 2**20, transcendentals=0
        ),
        name="geglu_backward",
    )(feed_grad, expand, reduce_full, slope, gelu, active, rows_all)


def rotate_lanes(vectors, cosine, signed_sine):
    return vectors * cosine + pltpu.roll(vectors, vectors.shape[1] // 2, 1) * signed_sine


def attention_backward_kernel(
    wide_count,
    narrow_count,
    places,
    upper_grad,
    hidden_part,
    normed,
    inv_std,
    small,
    merge,
    mixed,
    queries,
    keys,
    values,
    probs,
    cosine,
    signed_sine,
    triple,
    merge_grad,
    heads_sums,
    merge_sums,
    sum_grad,
    norm_sums,
    gain,
    attended,
    upstream,
    outbound,
    probs_held,
    keys_turned,
    key_total,
    value_total,
    merge_out,
    merge_in,
    mixed_send,
    mixed_recv,
    merge_send,
    merge_recv,
    load_sems,
    parts,
    from_mate,
    incoming,
    mate_send,
    mate_recv,
    sum_send,
    sum_recv,
):
    sems = (None, None, mate_send, mate_recv, sum_send, sum_recv, None)
    plane = PlaneExchange(wide_count, None, None, parts, from_mate, incoming, sems)
    line = LineExchange(narrow_count)
    rows, width = sum_grad.shape
    own_cols = queries.shape[1]
    heads = own_cols // HDIM
    scale = HDIM ** (-0.5)

    def load(head):
        return pltpu.make_async_copy(
            probs.at[head], probs_held.at[head % 2], load_sems.at[head % 2]
        )

    load(0).start()
    greet_plane(plane)

    spread_small(gain, small, places[2], 0)
    norm_sums[...] = jnp.zeros_like(norm_sums)
    merge_sums[...] = jnp.zeros_like(merge_sums)

    def norm_rows(i, carry):
        some = pl.ds(pl.multiple_of(i * 16, 16), 16)
        hidden_grad = residual_scale * upper_grad[some] + hidden_part[some]
        norm_sums[0:1] += jnp.sum(hidden_grad * normed[some], axis=0, keepdims=True)
        norm_sums[1:2] += jnp.sum(hidden_grad, axis=0, keepdims=True)
        total = normalize_back(hidden_grad, normed[some], inv_std[some], gain[...])
        sum_grad[some] = total
        merge_sums[...] += jnp.sum(total, axis=0, keepdims=True)
        attended[some] = total.astype(jnp.bfloat16)
        return carry

    lax.fori_loop(0, rows // 16, norm_rows, 0, unroll=2)
    line.greet(3)

    def mixed_part(target, where):
        part = dot(
            attended[...],
            merge[pl.ds(pl.multiple_of(where * own_cols, own_cols), own_cols)],
            ((1,), (1,)),
        )
        target[...] = part.astype(jnp.bfloat16)

    for offset in range(1, narrow_count):
        place = line.peer(offset)
        mixed_part(outbound.at[offset - 1], place)
        line.send(offset, outbound.at[offset - 1], upstream, mixed_send, mixed_recv)
    mixed_part(upstream.at[line.mine], line.mine)

    block = parts.shape[1]

    def merge_rows(i, carry):
        cols = pl.ds(pl.multiple_of(i * block, block), block)
        parts[i] = dot(mixed[:, cols], attended[...], ((0,), (0,))).astype(jnp.bfloat16)
        return carry

    lax.fori_loop(0, wide_count, merge_rows, 0)
    for offset in range(plane.ring):
        plane.share(offset)
    plane.first_sums()
    plane.far_sums()
    plane.last_sums()
    plane.finish(merge_out)
    count = merge_grad.shape[0]

    def z_rows(where):
        return pl.ds(pl.multiple_of(where * count, count), count)

    for offset in range(1, narrow_count):
        line.send(
            offset, merge_out.at[z_rows(line.peer(offset))], merge_in, merge_send, merge_recv
        )
    for offset in range(1, narrow_count):
        line.arrived(offset, upstream, mixed_send, mixed_recv)

    def one_head(head):
        cols = pl.ds(head * HDIM, HDIM)
        load(head).wait()
        if head + 1 < heads:
            load(head + 1).start()
        held = probs_held.at[head % 2]
        keys_turned[...] = keys[:, cols].astype(jnp.float32).T.astype(jnp.bfloat16)
        key_total[...] = jnp.zeros_like(key_total)
        value_total[...] = jnp.zeros_like(value_total)

        def chunk(i, carry):
            here = pl.ds(pl.multiple_of(i * rows, rows), rows)
            weights_low = held[:, here]
            up = upstream[i, :, cols]
            pulled = dot(values[:, cols], up, ((1,), (1,)))
            weights = weights_low.astype(jnp.float32)
            scaled = weights * pulled
            change = (scaled - weights * jnp.sum(scaled, axis=0, keepdims=True)).astype(
                jnp.bfloat16
            )
            key_total[...] += dot(change, queries[here, cols], ((1,), (0,)))
            value_total[...] += dot(weights_low, up, ((1,), (0,)))
            query_grad = dot(keys_turned[...], change, ((1,), (0,))).T * scale
            triple[here, cols] = rotate_lanes(
                query_grad, cosine[here], signed_sine[here]
            ).astype(jnp.bfloat16)
            return carry

        lax.fori_loop(0, narrow_count, chunk, 0)

        def ending(i, carry):
            here = pl.ds(pl.multiple_of(i * rows, rows), rows)
            triple[here, pl.ds(own_cols + head * HDIM, HDIM)] = rotate_lanes(
                key_total[here] * scale, cosine[here], signed_sine[here]
            ).astype(jnp.bfloat16)
            triple[here, pl.ds(2 * own_cols + head * HDIM, HDIM)] = value_total[here].astype(
                jnp.bfloat16
            )
            return carry

        lax.fori_loop(0, narrow_count, ending, 0)

    for head in range(heads):
        one_head(head)

    def column_sums(cols):
        heads_sums[:, cols] = jnp.sum(
            triple[:, cols].astype(jnp.float32), axis=0, keepdims=True
        )

    tiles(3 * own_cols, 256, column_sums)
    summed = merge_out[z_rows(line.mine)].astype(jnp.float32)
    for offset in range(1, narrow_count):
        line.arrived(offset, merge_in, merge_send, merge_recv)
        summed += merge_in[line.peer(offset)].astype(jnp.float32)
    merge_grad[...] = summed
    line.drain()
    plane.drain()


def attention_backward(
    wide_count,
    narrow_count,
    places,
    upper_grad,
    hidden_part,
    normed,
    inv_std,
    small,
    merge_full,
    mixed,
    queries,
    keys,
    values,
    probs,
    cosine,
    signed_sine,
):
    rows, width = normed.shape
    bucket, own_cols = queries.shape
    block = width // wide_count
    count = block // narrow_count
    anywhere = pl.BlockSpec(memory_space=pl.ANY)
    vmem = pl.BlockSpec(memory_space=pltpu.VMEM)
    dma = pltpu.SemaphoreType.DMA
    return pl.pallas_call(
        functools.partial(attention_backward_kernel, wide_count, narrow_count, places),
        out_shape=(
            jax.ShapeDtypeStruct((bucket, 3 * own_cols), jnp.bfloat16),
            jax.ShapeDtypeStruct((count, width), jnp.float32),
            jax.ShapeDtypeStruct((1, 3 * own_cols), jnp.float32),
            jax.ShapeDtypeStruct((1, width), jnp.float32),
            jax.ShapeDtypeStruct((rows, width), jnp.float32),
            jax.ShapeDtypeStruct((2, width), jnp.float32),
        ),
        in_specs=[vmem] * 10 + [anywhere] + [vmem] * 2,
        out_specs=(vmem,) * 6,
        scratch_shapes=[
            pltpu.VMEM((1, width), jnp.float32),
            pltpu.VMEM((rows, width), jnp.bfloat16),
            pltpu.VMEM((narrow_count, rows, own_cols), jnp.bfloat16),
            pltpu.VMEM((narrow_count - 1, rows, own_cols), jnp.bfloat16),
            pltpu.VMEM((2, bucket, bucket), jnp.bfloat16),
            pltpu.VMEM((HDIM, bucket), jnp.bfloat16),
            pltpu.VMEM((bucket, HDIM), jnp.float32),
            pltpu.VMEM((bucket, HDIM), jnp.float32),
            pltpu.VMEM((block, width), jnp.bfloat16),
            pltpu.VMEM((narrow_count, count, width), jnp.bfloat16),
            dma((narrow_count - 1,)),
            dma((narrow_count,)),
            dma((narrow_count - 1,)),
            dma((narrow_count,)),
            dma((2,)),
        ]
        + sum_scratch(wide_count, block, width),
        compiler_params=pltpu.CompilerParams(
            collective_id=3, has_side_effects=True, vmem_limit_bytes=kernel_memory
        ),
        cost_estimate=pl.CostEstimate(
            flops=60 * 10**9, bytes_accessed=200 * 2**20, transcendentals=0
        ),
        name="attention_backward",
    )(
        upper_grad,
        hidden_part,
        normed,
        inv_std,
        small,
        merge_full,
        mixed,
        queries,
        keys,
        values,
        probs,
        cosine,
        signed_sine,
    )


def input_backward_kernel(
    wide_count,
    narrow_count,
    inputs,
    triple,
    heads_mat,
    small,
    sum_grad,
    input_part,
    heads_grad,
    heads_bias_grad,
    merge_bias_grad,
    gains_grad,
    shifts_grad,
    expand_bias_grad,
    reduce_bias_grad,
    small_result,
    line_parts,
    line_in,
    heads_out,
    heads_in,
    small_wide,
    small_sum,
    small_line,
    line_send,
    line_recv,
    heads_send,
    heads_recv,
    wide_send,
    wide_recv,
    small_send,
    small_recv,
    parts,
    from_mate,
    incoming,
    mate_send,
    mate_recv,
    sum_send,
    sum_recv,
):
    sems = (None, None, mate_send, mate_recv, sum_send, sum_recv, None)
    plane = PlaneExchange(wide_count, None, None, parts, from_mate, incoming, sems)
    line = LineExchange(narrow_count)
    rows, width = input_part.shape
    here = line.mine
    last = narrow_count - 1
    place = lax.axis_index("wide")

    def wide_peer(offset):
        return (place + offset) % wide_count

    barrier = pltpu.get_barrier_semaphore()
    for offset in range(1, wide_count):
        pl.semaphore_signal(
            barrier,
            inc=1,
            device_id={"wide": wide_peer(offset)},
            device_id_type=pl.DeviceIdType.MESH,
        )
    line.greet(wide_count - 1)

    def small_copy(offset, source, slot):
        return pltpu.make_async_remote_copy(
            src_ref=source,
            dst_ref=small_wide.at[slot],
            send_sem=wide_send.at[offset - 1],
            recv_sem=wide_recv.at[slot],
            device_id={"wide": wide_peer(offset)},
            device_id_type=pl.DeviceIdType.MESH,
        )

    small_copies = [
        small_copy(offset, small.at[wide_peer(offset)], place) for offset in range(1, wide_count)
    ]
    for copy in small_copies:
        copy.start()

    line_sum = LineSum(line, lambda target: line_parts.at[target], line_in, line_send, line_recv)

    def input_rows(index):
        some = pl.ds(pl.multiple_of(index * rows, rows), rows)

        def input_cols(cols):
            part = dot(triple[some], heads_mat[cols], ((1,), (1,)))
            line_parts[index, :, cols] = part.astype(jnp.bfloat16)

        tiles(width, 256, input_cols)

    for offset in range(last, 0, -1):
        for way in range(2):

            @pl.when(line_sum.reaches(way, offset))
            def _():
                input_rows(line_sum.target(way, offset))

        line_sum.begin(offset)
    input_rows(here)

    block = parts.shape[1]

    def heads_rows(i, carry):
        cols = pl.ds(pl.multiple_of(i * block, block), block)
        parts[i] = dot(inputs[:, cols], triple[...], ((0,), (0,))).astype(jnp.bfloat16)
        return carry

    lax.fori_loop(0, wide_count, heads_rows, 0)
    for offset in range(plane.ring):
        plane.share(offset)
    for offset in range(last - 1, last // 2, -1):
        line_sum.step(offset)
    plane.first_sums()
    plane.far_sums()

    for offset in range(1, wide_count):
        peer = wide_peer(offset)
        small_copy(offset, small_wide.at[peer], peer).wait_recv()
    small_wide[place] = small[place]
    total = small_wide[0]
    for index in range(1, wide_count):
        total += small_wide[index]
    small_sum[...] = total
    for offset in range(1, narrow_count):
        line.send(offset, small_sum.at[line.peer(offset)], small_line, small_send, small_recv)

    plane.last_sums()
    for offset in range(last // 2, 0, -1):
        line_sum.step(offset)
    plane.finish(heads_out)
    count = heads_grad.shape[0]

    def z_rows(where):
        return pl.ds(pl.multiple_of(where * count, count), count)

    for offset in range(1, narrow_count):
        line.send(
            offset, heads_out.at[z_rows(line.peer(offset))], heads_in, heads_send, heads_recv
        )
    heads_in[line.mine] = heads_out[z_rows(line.mine)]
    small_line[line.mine] = small_sum[line.mine]
    for offset in range(1, narrow_count):
        line.arrived(offset, small_line, small_send, small_recv)
    result = small_line[0]
    for index in range(1, narrow_count):
        result += small_line[index]
    small_result[...] = result
    row = 0
    for target in (
        heads_bias_grad,
        merge_bias_grad,
        gains_grad,
        shifts_grad,
        expand_bias_grad,
        reduce_bias_grad,
    ):
        first, size = target.shape
        for index in range(first):
            for start in range(0, size, 128):
                stop = min(start + 128, size)
                target[index : index + 1, start:stop] = small_result[
                    row : row + 1, 0 : stop - start
                ]
                row += 1

    line_sum.finish(input_part)

    def add_residual(i, carry):
        some = pl.ds(pl.multiple_of(i * 16, 16), 16)
        input_part[some] += residual_scale * sum_grad[some]
        return carry

    lax.fori_loop(0, rows // 16, add_residual, 0)
    for offset in range(1, narrow_count):
        line.arrived(offset, heads_in, heads_send, heads_recv)
    own_cols = triple.shape[1] // 3
    for index in range(narrow_count):
        for which in range(3):
            start = (which * narrow_count + index) * own_cols
            heads_grad[:, start : start + own_cols] = heads_in[
                index, :, which * own_cols : (which + 1) * own_cols
            ].astype(jnp.float32)
    line_sum.drain()
    for copy in small_copies:
        copy.wait_send()
    line.drain()
    plane.drain()


def input_backward(
    wide_count, narrow_count, inputs, triple_grad, heads_mat, small, sum_grad, small_shapes
):
    bucket, width = inputs.shape
    rows = bucket // narrow_count
    columns = triple_grad.shape[1]
    block = width // wide_count
    count = block // narrow_count
    vmem = pl.BlockSpec(memory_space=pltpu.VMEM)
    dma = pltpu.SemaphoreType.DMA
    lines = small.shape[2]
    return pl.pallas_call(
        functools.partial(input_backward_kernel, wide_count, narrow_count),
        out_shape=(
            jax.ShapeDtypeStruct((rows, width), jnp.float32),
            jax.ShapeDtypeStruct((count, narrow_count * columns), jnp.float32),
        )
        + tuple(jax.ShapeDtypeStruct(shape, jnp.float32) for shape in small_shapes),
        in_specs=[vmem] * 5,
        out_specs=(vmem,) * 8,
        scratch_shapes=[
            pltpu.VMEM((lines, 128), jnp.float32),
            pltpu.VMEM((narrow_count, rows, width), jnp.bfloat16),
            pltpu.VMEM((2, narrow_count - 1, rows, width), jnp.bfloat16),
            pltpu.VMEM((block, columns), jnp.bfloat16),
            pltpu.VMEM((narrow_count, count, columns), jnp.bfloat16),
            pltpu.VMEM((wide_count, narrow_count, lines, 128), jnp.float32),
            pltpu.VMEM((narrow_count, lines, 128), jnp.float32),
            pltpu.VMEM((narrow_count, lines, 128), jnp.float32),
            dma((2, narrow_count - 1)),
            dma((2, narrow_count - 1)),
            dma((narrow_count - 1,)),
            dma((narrow_count,)),
            dma((wide_count - 1,)),
            dma((wide_count,)),
            dma((narrow_count - 1,)),
            dma((narrow_count,)),
        ]
        + sum_scratch(wide_count, block, columns),
        compiler_params=pltpu.CompilerParams(
            collective_id=4, has_side_effects=True, vmem_limit_bytes=kernel_memory
        ),
        cost_estimate=pl.CostEstimate(
            flops=80 * 10**9, bytes_accessed=200 * 2**20, transcendentals=0
        ),
        name="input_backward",
    )(inputs, triple_grad, heads_mat, small, sum_grad)


def greet_all(wide_count, narrow_count):
    barrier = pltpu.get_barrier_semaphore()
    for axis, count in (("wide", wide_count), ("narrow", narrow_count)):
        place = lax.axis_index(axis)
        for offset in range(1, count):
            pl.semaphore_signal(
                barrier,
                inc=1,
                device_id={axis: (place + offset) % count},
                device_id_type=pl.DeviceIdType.MESH,
            )
    pl.semaphore_wait(barrier, wide_count + narrow_count - 2)


def gather_kernel(
    wide_count,
    narrow_count,
    own,
    heads_weight,
    merge_weight,
    heads_bias,
    merge_bias,
    norm_gains,
    norm_shifts,
    expand_bias,
    reduce_bias,
    joined_ref,
    prefix_ref,
    speeds,
    rows_out,
    heads_out,
    merge_out,
    small_out,
    triple,
    cosine,
    signed_sine,
    first_query,
    last_query,
    small,
    rows_all,
    triple_all,
    heads_all,
    merge_own,
    small_all,
    rows_send,
    rows_recv,
    heads_send,
    heads_recv,
    merge_send,
    merge_recv,
    small_send,
    small_recv,
    wide_send,
    wide_recv,
    local_sems,
    out_sems,
    heads_ring_send,
    heads_ring_recv,
    block_sems,
):
    ring_sems = (heads_ring_send, heads_ring_recv, None, None, None, None, None)
    heads_ring = PlaneExchange(wide_count, None, heads_all, heads_all, None, None, ring_sems)
    line = LineExchange(narrow_count)
    here = line.mine
    last = narrow_count - 1
    place = lax.axis_index("wide")
    slot = heads_ring.slot(0)
    rows, width = own.shape
    count = heads_weight.shape[0]
    columns = heads_all.shape[2]
    own_cols = columns // 3

    def z_rows(where):
        return pl.ds(pl.multiple_of(where * count, count), count)

    def head_cols(which, where):
        start = which * narrow_count * own_cols + where * own_cols
        return pl.ds(pl.multiple_of(start, own_cols), own_cols)

    line_rows = LineGather(line, lambda block: rows_all.at[block], rows_send, rows_recv)

    keep_rows = pltpu.make_async_copy(own, rows_all.at[here], local_sems.at[0])
    keep_rows.start()
    keeps = [
        pltpu.make_async_copy(
            heads_weight.at[:, head_cols(which, here)],
            heads_all.at[slot, z_rows(here), pl.ds(which * own_cols, own_cols)],
            local_sems.at[2 + which],
        )
        for which in range(3)
    ]
    keep_merge = pltpu.make_async_copy(
        merge_weight, merge_own.at[z_rows(here)], local_sems.at[1]
    )
    for copy in keeps + [keep_merge]:
        copy.start()
    smalls = (heads_bias, merge_bias, norm_gains, norm_shifts, expand_bias, reduce_bias)
    small[...] = jnp.zeros_like(small)
    row = 0
    for part in smalls:
        first, size = part.shape
        for index in range(first):
            for begin in range(0, size, 128):
                stop = min(begin + 128, size)
                small[row : row + 1, 0 : stop - begin] = part[
                    index : index + 1, begin:stop
                ].astype(jnp.float32)
                row += 1
    small_all[place, here] = small[...]
    greet_all(wide_count, narrow_count)

    def heads_copy(offset, which, where, sender):
        return line.copy(
            heads_weight.at[:, head_cols(which, where)],
            heads_all.at[slot, z_rows(sender), pl.ds(which * own_cols, own_cols)],
            heads_send.at[offset - 1, which],
            heads_recv.at[sender, which],
            where,
        )

    def merge_copy(offset, where, sender):
        return line.copy(
            merge_weight,
            merge_own.at[z_rows(sender)],
            merge_send.at[offset - 1],
            merge_recv.at[sender],
            where,
        )

    def small_copy(offset, where, sender):
        return line.copy(
            small,
            small_all.at[place, sender],
            small_send.at[offset - 1],
            small_recv.at[sender],
            where,
        )

    started = []

    def start(copy):
        copy.start()
        started.append(copy)

    keep_rows.wait()
    line_rows.send_own()
    for offset in range(1, narrow_count):
        for which in range(3):
            start(heads_copy(offset, which, line.peer(offset), here))
    for offset in range(1, narrow_count):
        start(small_copy(offset, line.peer(offset), here))

    halfway = narrow_count * rows // 2
    joined = joined_ref[0]

    def tables(i, carry):
        some = pl.ds(pl.multiple_of(i * rows, rows), rows)
        place_in = i * rows + lax.broadcasted_iota(jnp.int32, (rows, 1), 0)
        second = jnp.where(place_in >= halfway, 1 - joined, 0)
        local = place_in - second * halfway
        reach = jnp.where(
            joined == 1,
            prefix_ref[0, 0] + prefix_ref[0, 1],
            jnp.where(second == 1, prefix_ref[0, 1], prefix_ref[0, 0]),
        )
        first_query[some] = jnp.where(local < reach, place_in - local, place_in)
        last_query[some] = jnp.where(
            (joined == 1) | (second == 1), 2 * halfway - 1, halfway - 1
        ) + jnp.zeros_like(place_in)
        angles = local.astype(jnp.float32) * speeds[...]
        lane = lax.broadcasted_iota(jnp.int32, (rows, HDIM), 1)
        cosine[some] = jnp.cos(angles)
        sine = jnp.sin(angles)
        signed_sine[some] = jnp.where(lane < HDIM // 2, sine, -sine)
        return carry

    lax.fori_loop(0, narrow_count, tables, 0)

    line_rows.step(1)
    for copy in keeps:
        copy.wait()
    for offset in range(1, narrow_count):
        for which in range(3):
            heads_copy(offset, which, line.peer(offset), line.peer(offset)).wait_recv()
    heads_ring.send_own()
    for offset in range(1, narrow_count):
        small_copy(offset, line.peer(offset), line.peer(offset)).wait_recv()

    def wide_copy(offset, sender):
        return pltpu.make_async_remote_copy(
            src_ref=small_all.at[sender],
            dst_ref=small_all.at[sender],
            send_sem=wide_send.at[offset - 1],
            recv_sem=wide_recv.at[sender],
            device_id={"wide": (place + offset) % wide_count},
            device_id_type=pl.DeviceIdType.MESH,
        )

    for offset in range(1, wide_count):
        start(wide_copy(offset, place))

    def leave_rows(block):
        return pltpu.make_async_copy(rows_all.at[block], rows_out.at[block], block_sems.at[0, block])

    def leave_triple(block):
        return pltpu.make_async_copy(triple_all.at[block], triple.at[block], block_sems.at[1, block])

    def project(block):
        leave_rows(block).start()

        def cols_step(cols):
            weight = heads_all[:, :, cols].reshape(width, cols.size)
            triple_all[block, :, cols] = dot(rows_all[block], weight, ((1,), (0,)))

        tiles(columns, 256, cols_step)
        leave_triple(block).start()

    def project_step(step):
        line_rows.each(step, project)

    def gather(ring, distance):
        ring.receive(distance)
        ring.receive_mate(-distance)
        if distance < ring.far:
            ring.receive_mate(distance)

    outs = []

    def keep_out(source, target):
        copy = pltpu.make_async_copy(source, target, out_sems.at[len(outs)])
        copy.start()
        outs.append(copy)

    for offset in range(1, narrow_count):
        start(merge_copy(offset, line.peer(offset), here))
    heads_ring.receive_mate(0)
    for distance in range(1, heads_ring.far):
        gather(heads_ring, distance)
    if last > 1:
        line_rows.step(2)
    gather(heads_ring, heads_ring.far)
    keep_out(heads_all, heads_out)
    project(here)
    project_step(1)
    for step in range(3, narrow_count):
        project_step(step - 1)
        line_rows.step(step)
    project_step(last)
    keep_merge.wait()
    for offset in range(1, narrow_count):
        merge_copy(offset, line.peer(offset), line.peer(offset)).wait_recv()
    keep_out(merge_own, merge_out)
    for offset in range(1, wide_count):
        wide_copy(offset, (place + offset) % wide_count).wait_recv()
    keep_out(small_all, small_out)
    line_rows.drain()
    for copy in started:
        copy.wait_send()
    heads_ring.drain()
    for copy in outs:
        copy.wait()

    def left(block, carry):
        leave_rows(block).wait()
        leave_triple(block).wait()
        return carry

    lax.fori_loop(0, narrow_count, left, 0)


def gather_front(
    wide_count, narrow_count, layer_input, heads_weight, merge_weight, smalls, joined, prefix, speeds
):
    rows, width = layer_input.shape
    count, all_columns = heads_weight.shape
    columns = all_columns // narrow_count
    block = count * narrow_count
    anywhere = pl.BlockSpec(memory_space=pl.ANY)
    vmem = pl.BlockSpec(memory_space=pltpu.VMEM)
    dma = pltpu.SemaphoreType.DMA
    lines = row_places([part.shape for part in smalls])[1]
    shapes = (
        (narrow_count, rows, width),
        (wide_count, block, columns),
        (block, width),
        (wide_count, narrow_count, lines, 128),
    )
    far = narrow_count - 1
    bucket = narrow_count * rows
    table = jax.ShapeDtypeStruct((bucket, HDIM), jnp.float32)
    reach = jax.ShapeDtypeStruct((bucket, 1), jnp.int32)
    return pl.pallas_call(
        functools.partial(gather_kernel, wide_count, narrow_count),
        out_shape=tuple(jax.ShapeDtypeStruct(shape, jnp.bfloat16) for shape in shapes[:3])
        + (
            jax.ShapeDtypeStruct(shapes[3], jnp.float32),
            jax.ShapeDtypeStruct((narrow_count, rows, columns), jnp.float32),
            table,
            table,
            reach,
            reach,
        ),
        in_specs=[anywhere] * 3 + [vmem] * 6 + [pl.BlockSpec(memory_space=pltpu.SMEM)] * 2 + [vmem],
        out_specs=(anywhere,) * 5 + (vmem,) * 4,
        scratch_shapes=[
            pltpu.VMEM((lines, 128), jnp.float32),
            pltpu.VMEM(shapes[0], jnp.bfloat16),
            pltpu.VMEM((narrow_count, rows, columns), jnp.float32),
        ]
        + [pltpu.VMEM(shape, jnp.bfloat16) for shape in shapes[1:3]]
        + [pltpu.VMEM(shapes[3], jnp.float32)]
        + [
            dma((2, narrow_count)),
            dma((narrow_count,)),
            dma((far, 3)),
            dma((narrow_count, 3)),
            dma((far,)),
            dma((narrow_count,)),
            dma((far,)),
            dma((narrow_count,)),
            dma((wide_count - 1,)),
            dma((wide_count,)),
            dma((5,)),
            dma((4,)),
            dma((3, wide_count, 2)),
            dma((wide_count, 2)),
            dma((2, narrow_count)),
        ],
        compiler_params=pltpu.CompilerParams(
            collective_id=5, has_side_effects=True, vmem_limit_bytes=kernel_memory
        ),
        cost_estimate=pl.CostEstimate(
            flops=80 * 10**9, bytes_accessed=200 * 2**20, transcendentals=0
        ),
        name="gather_front",
    )(layer_input, heads_weight, merge_weight, *smalls, joined, prefix, speeds)


def attention_forward_kernel(
    wide_count,
    narrow_count,
    places,
    triple,
    small,
    cosine,
    signed_sine,
    first_query,
    last_query,
    own,
    merge,
    queries,
    keys,
    values,
    probs,
    mixed_out,
    hidden,
    hidden_low,
    normed,
    inv_std,
    merge_out,
    rows_out,
    merge_mat,
    probs_held,
    values_turned,
    outbound,
    mixed,
    mixed_send,
    mixed_recv,
    local_sems,
    ring_send,
    ring_recv,
    own_sem,
    rows_all,
    rows_send,
    rows_recv,
    rows_sem,
    heads_full,
    vectors,
):
    line = LineExchange(narrow_count)
    ring_sems = (ring_send, ring_recv, None, None, None, None, own_sem)
    ring = PlaneExchange(wide_count, merge, merge_mat, merge_mat, None, None, ring_sems)
    rows_sems = (rows_send, rows_recv, None, None, None, None, rows_sem)
    rows_ring = PlaneExchange(wide_count, hidden_low, rows_all, rows_all, None, None, rows_sems)
    bucket, own_cols = queries.shape
    rows, width = own.shape
    heads = own_cols // HDIM
    scale = HDIM ** (-0.5)
    greet_plane(ring)
    line.greet(3)
    keep_own = ring.send_own()
    spread_small(heads_full, small, places[0], 0)
    spread_small(vectors, small, places[1], 0, 0)
    spread_small(vectors, small, places[2], 0, 1)
    spread_small(vectors, small, places[3], 0, 2)
    ring_steps = [functools.partial(ring.receive, step) for step in range(1, ring.far + 1)]

    def keep(head):
        return pltpu.make_async_copy(
            probs_held.at[head % 2], probs.at[head], local_sems.at[head % 2]
        )

    def mixed_copy(head, offset, where, sender):
        cols = pl.ds(pl.multiple_of(sender * own_cols + head * HDIM, HDIM), HDIM)
        return line.copy(
            outbound.at[where, :, pl.ds(head * HDIM, HDIM)],
            mixed.at[:, cols],
            mixed_send.at[offset - 1, head],
            mixed_recv.at[sender, head],
            where,
        )

    started = []
    for head in range(heads):
        cols = pl.ds(head * HDIM, HDIM)

        def turn(i, carry):
            here = pl.ds(pl.multiple_of(i * rows, rows), rows)
            for which, target in enumerate((queries, keys, values)):
                wanted = pl.ds(which * own_cols + head * HDIM, HDIM)
                begin = (which * narrow_count + line.mine) * own_cols + head * HDIM
                bias = heads_full[:, pl.ds(pl.multiple_of(begin, HDIM), HDIM)]
                part = triple[here, wanted] + bias
                if which < 2:
                    part = rotate_lanes(part, cosine[here], -signed_sine[here])
                else:
                    values_turned[:, here] = part.T.astype(jnp.bfloat16)
                target[here, cols] = part.astype(jnp.bfloat16)
            return carry

        lax.fori_loop(0, narrow_count, turn, 0)
        if head >= 2:
            keep(head - 2).wait()
        held = probs_held.at[head % 2]

        def chunk(i, carry):
            here = pl.ds(pl.multiple_of(i * rows, rows), rows)
            scores = dot(keys[:, cols], queries[here, cols], ((1,), (1,))) * scale
            token = i * rows + lax.broadcasted_iota(jnp.int32, (bucket, rows), 1)
            seen = (token >= first_query[...]) & (token <= last_query[...])
            scores = jnp.where(seen, scores, masked_value)
            expo = jnp.exp(scores - jnp.max(scores, axis=0, keepdims=True))
            weights = (expo * (1 / jnp.sum(expo, axis=0, keepdims=True))).astype(jnp.bfloat16)
            held[:, here] = weights
            mixed_part = dot(values_turned[...], weights, ((1,), (0,)))
            outbound[i, :, cols] = mixed_part.T.astype(jnp.bfloat16)
            return carry

        lax.fori_loop(0, narrow_count, chunk, 0)
        keep(head).start()
        for offset in range(1, narrow_count):
            copy = mixed_copy(head, offset, line.peer(offset), line.mine)
            copy.start()
            started.append(copy)
        if ring_steps and head >= heads - len(ring_steps):
            ring_steps.pop(0)()
    own_mixed = pltpu.make_async_copy(
        outbound.at[line.mine],
        mixed.at[:, pl.ds(pl.multiple_of(line.mine * own_cols, own_cols), own_cols)],
        local_sems.at[3],
    )
    own_mixed.start()
    own_mixed.wait()
    keep_own.wait()
    for step in ring_steps:
        step()
    for offset in range(ring.ring):
        ring.receive_mate(offset)
    keep_merge = pltpu.make_async_copy(merge_mat, merge_out, local_sems.at[2])
    keep_merge.start()
    for offset in range(1, narrow_count):
        for head in range(heads):
            mixed_copy(head, offset, line.peer(offset), line.peer(offset)).wait_recv()
    mixed_out[...] = mixed[...]

    def merge_cols(cols):
        hidden[:, cols] = (
            residual_scale * own[:, cols].astype(jnp.float32)
            + dot(mixed[...], merge_mat[:, :, cols].reshape(width, cols.size), ((1,), (0,)))
            + vectors[0:1, cols]
        )

    tiles(width, 256, merge_cols)

    def norm_rows(i, carry):
        some = pl.ds(pl.multiple_of(i * 16, 16), 16)
        result, centred, inverse = normalize(hidden[some], vectors[1:2], vectors[2:3])
        hidden[some] = result
        hidden_low[some] = result.astype(jnp.bfloat16)
        normed[some] = centred
        inv_std[some] = inverse
        return carry

    lax.fori_loop(0, rows // 16, norm_rows, 0, unroll=2)
    keep_rows = rows_ring.send_own()
    for step in range(1, rows_ring.far + 1):
        rows_ring.receive(step)
    for offset in range(rows_ring.ring):
        rows_ring.receive_mate(offset)
    keep_rows.wait()
    keep_rows = pltpu.make_async_copy(rows_all, rows_out, rows_sem)
    keep_rows.start()
    for head in range(max(heads - 2, 0), heads):
        keep(head).wait()
    for copy in started:
        copy.wait_send()
    ring.drain()
    rows_ring.drain()
    keep_merge.wait()
    keep_rows.wait()


def attention_forward(
    wide_count,
    narrow_count,
    places,
    triple,
    small,
    cosine,
    signed_sine,
    first_query,
    last_query,
    layer_input,
    merge_block,
):
    bucket, columns = triple.shape
    rows, width = layer_input.shape
    own_cols = columns // 3
    heads = own_cols // HDIM
    anywhere = pl.BlockSpec(memory_space=pl.ANY)
    vmem = pl.BlockSpec(memory_space=pltpu.VMEM)
    dma = pltpu.SemaphoreType.DMA

    def low_shape(*shape):
        return jax.ShapeDtypeStruct(shape, jnp.bfloat16)

    def wide_shape(*shape):
        return jax.ShapeDtypeStruct(shape, jnp.float32)

    return pl.pallas_call(
        functools.partial(attention_forward_kernel, wide_count, narrow_count, places),
        out_shape=(
            low_shape(bucket, own_cols),
            low_shape(bucket, own_cols),
            low_shape(bucket, own_cols),
            low_shape(heads, bucket, bucket),
            low_shape(rows, width),
            wide_shape(rows, width),
            low_shape(rows, width),
            wide_shape(rows, width),
            wide_shape(rows, 1),
            low_shape(wide_count, *merge_block.shape),
            low_shape(wide_count, rows, width),
        ),
        in_specs=[vmem] * 7 + [anywhere],
        out_specs=(vmem, vmem, vmem, anywhere) + (vmem,) * 5 + (anywhere,) * 2,
        scratch_shapes=[
            pltpu.VMEM((wide_count, *merge_block.shape), jnp.bfloat16),
            pltpu.VMEM((2, bucket, bucket), jnp.bfloat16),
            pltpu.VMEM((HDIM, bucket), jnp.bfloat16),
            pltpu.VMEM((narrow_count, rows, own_cols), jnp.bfloat16),
            pltpu.VMEM((rows, width), jnp.bfloat16),
            dma((narrow_count - 1, heads)),
            dma((narrow_count, heads)),
            dma((4,)),
            dma((3, wide_count, 2)),
            dma((wide_count, 2)),
            dma(()),
            pltpu.VMEM((wide_count, rows, width), jnp.bfloat16),
            dma((3, wide_count, 2)),
            dma((wide_count, 2)),
            dma(()),
            pltpu.VMEM((1, 3 * width), jnp.float32),
            pltpu.VMEM((3, width), jnp.float32),
        ],
        compiler_params=pltpu.CompilerParams(
            collective_id=6, has_side_effects=True, vmem_limit_bytes=kernel_memory
        ),
        cost_estimate=pl.CostEstimate(
            flops=60 * 10**9, bytes_accessed=200 * 2**20, transcendentals=0
        ),
        name="attention_forward",
    )(
        triple,
        small,
        cosine,
        signed_sine,
        first_query,
        last_query,
        layer_input,
        merge_block,
    )


def shards(
    layer_input,
    heads_weight,
    heads_bias,
    merge_weight,
    merge_bias,
    norm_gains,
    norm_shifts,
    expand_weight,
    expand_bias,
    reduce_weight,
    reduce_bias,
    joined,
    prefix,
    cotangent,
):
    tok_rows, model_width = layer_input.shape
    wide_count = lax.axis_size("wide")
    narrow_count = lax.axis_size("narrow")
    count = wide_count * narrow_count
    bucket_len = tok_rows * narrow_count
    own_heads = HEADS // narrow_count
    own_cols = own_heads * HDIM
    share = expand_weight.shape[2]
    narrow_index = lax.axis_index("narrow")
    smalls = (
        heads_bias.reshape(1, -1),
        merge_bias.reshape(1, -1),
        norm_gains,
        norm_shifts,
        expand_bias,
        reduce_bias.reshape(1, -1),
    )
    places = row_places([part.shape for part in smalls])[0]
    (
        rows_input,
        heads_mat,
        merge_block,
        small_all,
        triple,
        cosine,
        signed_sine,
        first_query,
        last_query,
    ) = gather_front(
        wide_count,
        narrow_count,
        layer_input,
        heads_weight,
        merge_weight,
        smalls,
        joined,
        prefix,
        jnp.asarray(rotary_speeds(HDIM)),
    )
    rows_input = rows_input.reshape(bucket_len, model_width)
    heads_mat = heads_mat.reshape(model_width, 3 * own_cols)
    triple = triple.reshape(bucket_len, 3 * own_cols)
    (
        queries,
        keys,
        values,
        probs_low,
        mixed,
        hidden,
        hidden_low,
        normed_one,
        inv_one,
        merge_full,
        rows_all,
    ) = attention_forward(
        wide_count,
        narrow_count,
        places,
        triple,
        small_all,
        cosine,
        signed_sine,
        first_query,
        last_query,
        layer_input,
        merge_block,
    )

    tile_rows = -share % 16
    padded = -(-share // 256) * 256
    expand_low = jnp.pad(expand_weight.transpose(1, 2, 0), ((0, 0), (0, tile_rows), (0, 0)))
    expand_low, _ = lax.optimization_barrier((expand_low, small_all))
    expand_full = lax.all_gather(expand_low, "narrow", axis=2, tiled=True)
    reduce_low = jnp.pad(reduce_weight, ((0, tile_rows), (0, 0)))
    (
        reduce_full,
        active,
        slope,
        gelu,
        layer_output,
        sum_two_grad,
        feed_grad,
        row_sums,
    ) = geglu_forward(
        wide_count,
        narrow_count,
        places,
        rows_all,
        expand_full,
        reduce_low,
        small_all,
        hidden,
        cotangent,
    )
    reduce_weight_gradient, expand_part, hidden_part, unit_sums = geglu_backward(
        wide_count,
        narrow_count,
        feed_grad,
        expand_full,
        reduce_full,
        slope,
        gelu,
        active,
        rows_all,
    )
    expand_weight_gradient = (
        lax.psum_scatter(expand_part, "narrow", scatter_dimension=2, tiled=True)[:, :share]
        .astype(jnp.float32)
        .transpose(2, 0, 1)
    )
    (
        triple_grad,
        merge_weight_gradient,
        heads_sums,
        merge_sums,
        sum_one_grad,
        norm_one_sums,
    ) = attention_backward(
        wide_count,
        narrow_count,
        places,
        sum_two_grad,
        hidden_part,
        normed_one,
        inv_one,
        small_all,
        merge_full.reshape(model_width, model_width),
        mixed,
        queries,
        keys,
        values,
        probs_low,
        cosine,
        signed_sine,
    )

    mine_narrow = (jnp.arange(narrow_count) == narrow_index).astype(jnp.float32)
    mine_wide = (jnp.arange(wide_count) == lax.axis_index("wide")).astype(jnp.float32)
    heads_sums = (heads_sums.reshape(3, 1, own_cols) * mine_narrow[None, :, None]).reshape(count, 1, -1)
    norm_sums = jnp.stack([norm_one_sums[0], row_sums[0], norm_one_sums[1], row_sums[1]])
    norm_sums = norm_sums.reshape(4, count, -1).transpose(1, 0, 2)
    expand_sums = unit_sums[:, :share].reshape(2, narrow_count, -1).transpose(1, 0, 2)[None]
    expand_sums = (expand_sums * mine_wide[:, None, None, None]).reshape(count, 2, -1)
    reduce_sums = row_sums[2].reshape(1, narrow_count, 1, -1)
    reduce_sums = jnp.broadcast_to(
        reduce_sums, (wide_count, narrow_count, 1, reduce_sums.shape[3])
    ).reshape(count, 1, -1)
    pieces = (heads_sums, merge_sums.reshape(count, 1, -1), norm_sums, expand_sums, reduce_sums)
    packed = []
    for piece in pieces:
        piece = jnp.pad(piece, ((0, 0), (0, 0), (0, -piece.shape[2] % 128)))
        packed.append(piece.reshape(count, -1, 128))
    packed = jnp.concatenate(packed, axis=1)
    packed = jnp.pad(packed, ((0, 0), (0, -packed.shape[1] % 8), (0, 0)))
    (
        input_gradient,
        heads_weight_gradient,
        heads_bias_gradient,
        merge_bias_gradient,
        gains_gradient,
        shifts_gradient,
        expand_bias_gradient,
        reduce_bias_gradient,
    ) = input_backward(
        wide_count,
        narrow_count,
        rows_input,
        triple_grad,
        heads_mat,
        packed.reshape(wide_count, narrow_count, -1, 128),
        sum_one_grad,
        (
            (1, heads_bias.size),
            (1, merge_bias.size),
            norm_gains.shape,
            norm_shifts.shape,
            expand_bias.shape,
            (1, reduce_bias.size),
        ),
    )
    return (
        layer_output,
        input_gradient,
        heads_weight_gradient,
        heads_bias_gradient[0],
        merge_weight_gradient,
        merge_bias_gradient[0],
        gains_gradient,
        shifts_gradient,
        expand_weight_gradient,
        expand_bias_gradient,
        reduce_weight_gradient[:share],
        reduce_bias_gradient[0],
    )


def solution(mesh):
    return jax.shard_map(
        shards,
        mesh=mesh,
        in_specs=(
            P(("wide", "narrow"), None),
            P(("wide", "narrow"), None),
            P(("wide", "narrow")),
            P(("wide", "narrow"), None),
            P(("wide", "narrow")),
            P(None, ("wide", "narrow")),
            P(None, ("wide", "narrow")),
            P("narrow", None, "wide"),
            P(None, ("wide", "narrow")),
            P("wide", "narrow"),
            P("narrow"),
            P("wide"),
            P("wide", None),
            P(("wide", "narrow"), None),
        ),
        out_specs=(
            P(("wide", "narrow"), None),
            P(("wide", "narrow"), None),
            P(("wide", "narrow"), None),
            P(("wide", "narrow")),
            P(("wide", "narrow"), None),
            P(("wide", "narrow")),
            P(None, ("wide", "narrow")),
            P(None, ("wide", "narrow")),
            P("narrow", None, "wide"),
            P(None, ("wide", "narrow")),
            P("wide", "narrow"),
            P("narrow"),
        ),
        check_vma=False,
    )
```

```python
import functools
import math

import jax
import jax.numpy as jnp
import numpy as np
from jax import lax
from jax.experimental import pallas as pl
from jax.experimental.pallas import tpu as pltpu
from jax.sharding import PartitionSpec as P

HEADS = 16
HDIM = 128


residual_scale = 48.0**0.5
norm_eps = 1e-05
masked_value = -1e30
kernel_memory = 60 * 2**20


def rotary_speeds(head_size):
    index = np.arange(head_size) % (head_size // 2)
    return (10000.0 ** (-2.0 * index / head_size)).astype(np.float32)[None]


def normalize(values, gain, shift):
    centre = jnp.mean(values, axis=-1, keepdims=True)
    centred = values - centre
    variance = jnp.mean(centred * centred, axis=-1, keepdims=True)
    inv_std = lax.rsqrt(variance + norm_eps)
    normed = centred * inv_std
    return (normed * gain + shift, normed, inv_std)


def normalize_back(upstream, normed, inv_std, gain):
    scaled = upstream * gain
    return inv_std * (
        scaled
        - jnp.mean(scaled, axis=-1, keepdims=True)
        - normed * jnp.mean(scaled * normed, axis=-1, keepdims=True)
    )


def dot(left, right, dims):
    return lax.dot_general(left, right, (dims, ((), ())), preferred_element_type=jnp.float32)


def low(values):
    return values.astype(jnp.bfloat16)


def row_places(shapes):
    places = []
    start = 0
    for first, size in shapes:
        places.append((start, first, size))
        start += first * -(-size // 128)
    return places, start + -start % 8


def small_piece(block, place, index):
    start, _, size = place
    rows = -(-size // 128)
    pieces = []
    for row in range(rows):
        stop = min(size - 128 * row, 128)
        here = start + index * rows + row
        pieces.append(block[here : here + 1, 0:stop])
    return pieces


def spread_small(target, small, place, index, row=0):
    at = 0
    for wide in range(small.shape[0]):
        for narrow in range(small.shape[1]):
            for piece in small_piece(small.at[wide, narrow], place, index):
                target[row : row + 1, at : at + piece.shape[1]] = piece
                at += piece.shape[1]


def ring_place(wide_count):
    ring = wide_count // 2
    mine = lax.axis_index("wide")
    chip = mine // 2
    core = mine % 2
    position = 2 * (chip // 2) + (chip % 2 + chip // 2) % 2
    return ring, position, core


def chip_at(position, ring):
    position = (position + 2 * ring) % ring
    return 2 * (position // 2) + (position + position // 2) % 2


class PlaneExchange:
    def __init__(self, wide_count, own, blocks, parts, from_mate, incoming, sems, cols=None):
        self.ring, self.position, self.core = ring_place(wide_count)
        self.own, self.blocks, self.parts = own, blocks, parts
        self.from_mate, self.incoming = from_mate, incoming
        (
            self.gather_send,
            self.gather_recv,
            self.mate_send,
            self.mate_recv,
            self.sum_send,
            self.sum_recv,
            self.own_sem,
        ) = sems
        self.half = parts.shape[1] // 2
        self.cols = slice(None) if cols is None else cols
        self.far = self.ring // 2
        self.started = []

    def device(self, offset, mate=False):
        core = 1 - self.core if mate else self.core
        return {"wide": 2 * chip_at(self.position + offset, self.ring) + core}

    def slot(self, offset, mate=False):
        core = 1 - self.core if mate else self.core
        return 2 * chip_at(self.position + offset, self.ring) + core

    def rows(self, part):
        return pl.ds(part * self.half, self.half)

    def greet(self):
        barrier = pltpu.get_barrier_semaphore()
        for where in (self.device(-1), self.device(1), self.device(0, True)):
            pl.semaphore_signal(
                barrier, inc=1, device_id=where, device_id_type=pl.DeviceIdType.MESH
            )
        pl.semaphore_wait(barrier, 3)

    def start(self, source, target, send_sem, recv_sem, where):
        copy = pltpu.make_async_remote_copy(
            src_ref=source,
            dst_ref=target,
            send_sem=send_sem,
            recv_sem=recv_sem,
            device_id=where,
            device_id_type=pl.DeviceIdType.MESH,
        )
        copy.start()
        self.started.append(copy)

    def pass_on(self, lane, slot, part, where, source=None):
        target = self.blocks.at[slot, self.rows(part)]
        self.start(
            target if source is None else source,
            target,
            self.gather_send.at[lane, slot, part],
            self.gather_recv.at[slot, part],
            where,
        )

    def arrived(self, slot, part):
        target = self.blocks.at[slot, self.rows(part)]
        pltpu.make_async_remote_copy(
            src_ref=target,
            dst_ref=target,
            send_sem=self.gather_send.at[0, slot, part],
            recv_sem=self.gather_recv.at[slot, part],
            device_id=self.device(1),
            device_id_type=pl.DeviceIdType.MESH,
        ).wait_recv()

    def send_own(self):
        slot = self.slot(0)
        keep = None
        own = self.blocks.at[slot]
        if self.own is not None:
            own = self.own
            keep = pltpu.make_async_copy(own, self.blocks.at[slot], self.own_sem)
            keep.start()
        first, second = own.at[self.rows(0)], own.at[self.rows(1)]
        self.pass_on(0, slot, 0, self.device(1), first)
        self.pass_on(1, slot, 1, self.device(-1), second)
        self.pass_on(2, slot, 0, self.device(0, True), first)
        self.pass_on(2, slot, 1, self.device(0, True), second)
        self.pass_on(0, slot, 1, self.device(1), second)
        self.pass_on(1, slot, 0, self.device(-1), first)
        return keep

    def receive(self, distance):
        mate = self.device(0, True)
        left, right = self.slot(-distance), self.slot(distance)
        if distance == self.far:
            for part in range(2):
                self.arrived(left, part)
                self.pass_on(2, left, part, mate)
            return
        further = distance < self.far - 1
        self.arrived(left, 0)
        self.pass_on(0, left, 0, self.device(1))
        self.pass_on(2, left, 0, mate)
        self.arrived(right, 1)
        self.pass_on(1, right, 1, self.device(-1))
        self.pass_on(2, right, 1, mate)
        self.arrived(left, 1)
        if further:
            self.pass_on(0, left, 1, self.device(1))
        self.pass_on(2, left, 1, mate)
        self.arrived(right, 0)
        if further:
            self.pass_on(1, right, 0, self.device(-1))
        self.pass_on(2, right, 0, mate)

    def receive_mate(self, offset):
        for part in range(2):
            self.arrived(self.slot(offset, True), part)

    def share(self, offset):
        chip = chip_at(self.position + offset, self.ring)
        self.start(
            self.parts.at[self.slot(offset, True), :, self.cols],
            self.from_mate.at[chip, :, self.cols],
            self.mate_send.at[chip],
            self.mate_recv.at[chip],
            self.device(0, True),
        )

    def shared(self, offset):
        chip = chip_at(self.position + offset, self.ring)
        pltpu.make_async_remote_copy(
            src_ref=self.parts.at[self.slot(offset), :, self.cols],
            dst_ref=self.from_mate.at[chip, :, self.cols],
            send_sem=self.mate_send.at[chip],
            recv_sem=self.mate_recv.at[chip],
            device_id=self.device(0, True),
            device_id_type=pl.DeviceIdType.MESH,
        ).wait_recv()

    def chip_sum(self, offset, rows):
        chip = chip_at(self.position + offset, self.ring)
        return self.parts[self.slot(offset), rows, self.cols].astype(
            jnp.float32
        ) + self.from_mate[chip, rows, self.cols].astype(jnp.float32)

    def send_sum(self, way, distance, part):
        offset = distance if way == 0 else -distance
        begins = self.far if part == way else self.far - 1
        slot = self.slot(offset)
        if distance < begins:
            self.sum_arrived(way, distance, part)

        def chunk(i, carry):
            here = pl.ds(pl.multiple_of(i * 16, 16), 16)
            there = pl.ds(pl.multiple_of(part * self.half + i * 16, 16), 16)
            total = self.chip_sum(offset, there)
            if distance < begins:
                total += self.incoming[way, distance, part, here, self.cols].astype(jnp.float32)
            self.parts[slot, there, self.cols] = total.astype(jnp.bfloat16)
            return carry

        lax.fori_loop(0, self.half // 16, chunk, 0)
        self.start(
            self.parts.at[slot, self.rows(part), self.cols],
            self.incoming.at[way, distance - 1, part, :, self.cols],
            self.sum_send.at[way, distance - 1, part],
            self.sum_recv.at[way, distance - 1, part],
            self.device(1 if way == 0 else -1),
        )

    def sum_arrived(self, way, distance, part):
        target = self.incoming.at[way, distance, part, :, self.cols]
        pltpu.make_async_remote_copy(
            src_ref=target,
            dst_ref=target,
            send_sem=self.sum_send.at[way, distance, part],
            recv_sem=self.sum_recv.at[way, distance, part],
            device_id=self.device(1),
            device_id_type=pl.DeviceIdType.MESH,
        ).wait_recv()

    def run(self, first, second, before, after_far):
        def compute(chip):
            first(chip)
            second(chip)

        keep = self.send_own()
        keep.wait()
        self.receive_mate(0)
        compute(chip_at(self.position, self.ring))
        self.share(0)
        for distance in range(1, self.far):
            self.receive(distance)
            for offset in (-distance, distance):
                self.receive_mate(offset)
                compute(chip_at(self.position + offset, self.ring))
                self.share(offset)
            if distance == self.far - 1:
                self.first_sums()
        self.receive(self.far)
        self.receive_mate(self.far)
        farthest = chip_at(self.position + self.far, self.ring)
        first(farthest)
        before()
        second(farthest)
        self.share(self.far)
        self.far_sums()
        after_far()
        self.last_sums()

    def start_sums(self, compute):
        compute(chip_at(self.position + self.far, self.ring))
        self.share(self.far)
        for distance in range(self.far - 1, 0, -1):
            for offset in (-distance, distance):
                compute(chip_at(self.position + offset, self.ring))
                self.share(offset)
            if distance == self.far - 1:
                self.far_sums()
                self.first_sums()
        compute(chip_at(self.position, self.ring))
        self.share(0)

    def first_sums(self):
        distance = self.far - 1
        self.shared(distance)
        self.send_sum(0, distance, 1)
        self.shared(-distance)
        self.send_sum(1, distance, 0)

    def far_sums(self):
        self.shared(self.far)
        self.send_sum(0, self.far, 0)
        self.send_sum(1, self.far, 1)

    def last_sums(self):
        for distance in range(self.far - 1, 0, -1):
            if distance < self.far - 1:
                self.shared(distance)
                self.shared(-distance)
            self.send_sum(0, distance, 0)
            self.send_sum(1, distance, 1)
            if distance < self.far - 1:
                self.send_sum(0, distance, 1)
                self.send_sum(1, distance, 0)

    def finish(self, result):
        self.shared(0)
        for part in range(2):
            for way in range(2):
                self.sum_arrived(way, 0, part)

            def chunk(i, carry):
                here = pl.ds(pl.multiple_of(i * 16, 16), 16)
                there = pl.ds(pl.multiple_of(part * self.half + i * 16, 16), 16)
                total = self.chip_sum(0, there)
                for way in range(2):
                    total += self.incoming[way, 0, part, here, self.cols].astype(jnp.float32)
                result[there, self.cols] = total.astype(result.dtype)
                return carry

            lax.fori_loop(0, self.half // 16, chunk, 0)

    def drain(self):
        for copy in self.started:
            copy.wait_send()


def sum_scratch(wide_count, rows, width):
    ring = wide_count // 2
    far = ring // 2
    dma = pltpu.SemaphoreType.DMA
    return [
        pltpu.VMEM((wide_count, rows, width), jnp.bfloat16),
        pltpu.VMEM((ring, rows, width), jnp.bfloat16),
        pltpu.VMEM((2, far, 2, rows // 2, width), jnp.bfloat16),
        dma((ring,)),
        dma((ring,)),
        dma((2, far, 2)),
        dma((2, far, 2)),
    ]


def exchange_scratch(wide_count, rows, width):
    dma = pltpu.SemaphoreType.DMA
    return [
        pltpu.VMEM((wide_count, rows, width), jnp.bfloat16),
        dma((3, wide_count, 2)),
        dma((wide_count, 2)),
        dma(()),
    ] + sum_scratch(wide_count, rows, width)


def load_padded(source, target, sem):
    filled = source.shape[0]
    copy = pltpu.make_async_copy(source, target.at[pl.ds(0, filled)], sem)
    copy.start()
    if filled < target.shape[0]:
        target[pl.ds(filled, target.shape[0] - filled)] = jnp.zeros(
            (target.shape[0] - filled, target.shape[1]), target.dtype
        )
    return copy


def pair_rows(ref, chip):
    block = ref[pl.ds(2 * chip, 2)]
    return block.reshape(2 * block.shape[1], block.shape[2])


def set_pair(ref, chip, cols, value):
    rows = ref.shape[1]
    ref[2 * chip, :, cols] = value[:rows].astype(ref.dtype)
    ref[2 * chip + 1, :, cols] = value[rows:].astype(ref.dtype)


def tiles(count, tile, body, start=0):
    def step(i, carry):
        body(pl.ds(pl.multiple_of(start + i * tile, tile), tile))
        return carry

    lax.fori_loop(0, count // tile, step, 0)


class LineExchange:
    def __init__(self, narrow_count):
        self.count = narrow_count
        self.mine = lax.axis_index("narrow")
        self.started = []

    def peer(self, offset):
        return (self.mine + offset) % self.count

    def greet(self, extra=0):
        barrier = pltpu.get_barrier_semaphore()
        for offset in range(1, self.count):
            pl.semaphore_signal(
                barrier,
                inc=1,
                device_id={"narrow": self.peer(offset)},
                device_id_type=pl.DeviceIdType.MESH,
            )
        pl.semaphore_wait(barrier, self.count - 1 + extra)

    def copy(self, source, target, send_sem, recv_sem, where):
        return pltpu.make_async_remote_copy(
            src_ref=source,
            dst_ref=target,
            send_sem=send_sem,
            recv_sem=recv_sem,
            device_id={"narrow": where},
            device_id_type=pl.DeviceIdType.MESH,
        )

    def send(self, offset, source, landing, send_sems, recv_sems):
        peer = self.peer(offset)
        copy = self.copy(
            source, landing.at[self.mine], send_sems.at[offset - 1], recv_sems.at[self.mine], peer
        )
        copy.start()
        self.started.append(copy)

    def arrived(self, offset, landing, send_sems, recv_sems):
        peer = self.peer(offset)
        self.copy(
            landing.at[peer], landing.at[peer], send_sems.at[offset - 1], recv_sems.at[peer], peer
        ).wait_recv()

    def drain(self):
        for copy in self.started:
            copy.wait_send()


class LineSum:
    def __init__(self, line, view, landing, send_sems, recv_sems):
        self.line, self.view, self.landing = line, view, landing
        self.send_sems, self.recv_sems = send_sems, recv_sems
        self.last = line.count - 1

    def reaches(self, way, offset):
        here = self.line.mine
        return here + offset <= self.last if way == 0 else here - offset >= 0

    def follows(self, way):
        here = self.line.mine
        return here > 0 if way == 0 else here < self.last

    def target(self, way, offset):
        return self.line.mine + offset if way == 0 else self.line.mine - offset

    def copy(self, way, offset):
        return self.line.copy(
            self.view(self.target(way, offset)),
            self.landing.at[way, offset - 1],
            self.send_sems.at[way, offset - 1],
            self.recv_sems.at[way, offset - 1],
            self.line.mine + 1 if way == 0 else self.line.mine - 1,
        )

    def arrived(self, way, offset):
        landing = self.landing.at[way, offset]
        self.line.copy(
            landing,
            landing,
            self.send_sems.at[way, offset],
            self.recv_sems.at[way, offset],
            self.line.mine,
        ).wait_recv()

    def add(self, way, offset):
        held = self.view(self.target(way, offset))

        def chunk(i, carry):
            some = pl.ds(pl.multiple_of(i * 16, 16), 16)
            held[some] = (
                held[some].astype(jnp.float32)
                + self.landing[way, offset, some].astype(jnp.float32)
            ).astype(jnp.bfloat16)
            return carry

        lax.fori_loop(0, self.landing.shape[2] // 16, chunk, 0)

    def begin(self, offset):
        for way in range(2):

            @pl.when(self.reaches(way, offset) & jnp.logical_not(self.follows(way)))
            def _():
                self.copy(way, offset).start()

    def step(self, offset):
        for way in range(2):

            @pl.when(self.reaches(way, offset) & self.follows(way))
            def _():
                self.arrived(way, offset)
                self.add(way, offset)
                self.copy(way, offset).start()

    def finish(self, result):
        held = self.view(self.line.mine)
        count = self.landing.shape[2] // 16

        def begin(i, carry):
            some = pl.ds(pl.multiple_of(i * 16, 16), 16)
            result[some] = held[some].astype(result.dtype)
            return carry

        lax.fori_loop(0, count, begin, 0)
        for way in range(2):

            @pl.when(self.follows(way))
            def _():
                self.arrived(way, 0)

                def chunk(i, carry):
                    some = pl.ds(pl.multiple_of(i * 16, 16), 16)
                    result[some] += self.landing[way, 0, some].astype(result.dtype)
                    return carry

                lax.fori_loop(0, count, chunk, 0)

    def drain(self):
        for offset in range(1, self.last + 1):
            for way in range(2):

                @pl.when(self.reaches(way, offset))
                def _():
                    self.copy(way, offset).wait_send()


class LineGather:
    def __init__(self, line, view, send_sems, recv_sems):
        self.line, self.view = line, view
        self.send_sems, self.recv_sems = send_sems, recv_sems
        self.last = line.count - 1

    def copy(self, way, block):
        target = self.view(block)
        here = self.line.mine
        return self.line.copy(
            target,
            target,
            self.send_sems.at[way, block],
            self.recv_sems.at[block],
            here + 1 if way == 0 else here - 1,
        )

    def goes(self, way):
        return self.line.mine < self.last if way == 0 else self.line.mine > 0

    def has(self, way, step):
        here = self.line.mine
        return here - step >= 0 if way == 0 else here + step <= self.last

    def block(self, way, step):
        return self.line.mine - step if way == 0 else self.line.mine + step

    def send_own(self):
        for way in range(2):

            @pl.when(self.goes(way))
            def _():
                self.copy(way, self.line.mine).start()

    def step(self, step):
        for way in range(2):

            @pl.when(self.has(way, step))
            def _():
                self.copy(way, self.block(way, step)).wait_recv()

                @pl.when(self.goes(way))
                def _():
                    self.copy(way, self.block(way, step)).start()

    def each(self, step, body):
        for way in range(2):

            @pl.when(self.has(way, step))
            def _():
                body(self.block(way, step))

    def drain(self):
        for way in range(2):
            for step in range(self.last + 1):

                @pl.when(self.has(way, step) & self.goes(way))
                def _():
                    self.copy(way, self.block(way, step)).wait_send()


def greet_plane(plane):
    barrier = pltpu.get_barrier_semaphore()
    for where in (plane.device(-1), plane.device(1), plane.device(0, True)):
        pl.semaphore_signal(barrier, inc=1, device_id=where, device_id_type=pl.DeviceIdType.MESH)


def geglu_forward_kernel(
    wide_count,
    narrow_count,
    places,
    rows_all,
    expand,
    reduce,
    small,
    hidden,
    cotangent,
    reduce_out,
    active_out,
    slope_out,
    gelu_out,
    layer_output,
    sum_grad,
    feed_grad,
    row_sums,
    feed,
    blocks,
    parts,
    from_mate,
    incoming,
    mate_send,
    mate_recv,
    sum_send,
    sum_recv,
    expand_mat,
    reduce_mat,
    active,
    slope,
    gelu,
    load_sems,
    keep_sems,
    reduce_send,
    reduce_recv,
    next_mate_send,
    next_mate_recv,
    next_sum_send,
    next_sum_recv,
    late_mate_send,
    late_mate_recv,
    late_sum_send,
    late_sum_recv,
    shift,
    vectors,
):
    line = LineExchange(narrow_count)
    filled, cols = reduce.shape
    width = rows_all.shape[2]
    upper = (2 * line.mine) // narrow_count
    half = narrow_count // 2
    windows = (
        (half * upper, half, half - 1),
        (half - upper * (half - 1), half - 1, narrow_count - 2),
        ((narrow_count - 1) * (1 - upper), 1, narrow_count - 1),
    )
    sems = (
        (mate_send, mate_recv, sum_send, sum_recv),
        (next_mate_send, next_mate_recv, next_sum_send, next_sum_recv),
        (late_mate_send, late_mate_recv, late_sum_send, late_sum_recv),
    )
    planes = [
        PlaneExchange(
            wide_count,
            None,
            None,
            parts,
            from_mate,
            incoming,
            (None, None, *own_sems, None),
            pl.ds(pl.multiple_of(first * cols, cols), blocks_in * cols),
        )
        for (first, blocks_in, _), own_sems in zip(windows, sems)
    ]
    plane = planes[0]
    loads = [
        load_padded(expand.at[0], expand_mat.at[0], load_sems.at[0]),
        load_padded(expand.at[1], expand_mat.at[1], load_sems.at[1]),
        pltpu.make_async_copy(rows_all, blocks, load_sems.at[4]),
    ]
    loads[2].start()

    def reduce_cols(block):
        return reduce_mat.at[
            pl.ds(0, filled), pl.ds(pl.multiple_of(block * cols, cols), cols)
        ]

    line_reduce = LineGather(line, reduce_cols, reduce_send, reduce_recv)
    own_reduce = pltpu.make_async_copy(reduce, reduce_cols(line.mine), load_sems.at[2])
    own_reduce.start()
    if filled < reduce_mat.shape[0]:
        reduce_mat[filled:] = jnp.zeros(
            (reduce_mat.shape[0] - filled, reduce_mat.shape[1]), reduce_mat.dtype
        )
    greet_plane(plane)
    line.greet(3)
    place = lax.axis_index("wide")
    shift[...] = jnp.zeros_like(shift)
    for index in range(2):
        at = 0
        for block in range(narrow_count):
            for piece in small_piece(small.at[place, block], places[4], index):
                shift[index : index + 1, at : at + piece.shape[1]] = piece
                at += piece.shape[1]
    at = 0
    for block in range(narrow_count):
        for piece in small_piece(small.at[0, block], places[5], 0):
            vectors[0:1, at : at + piece.shape[1]] = piece
            at += piece.shape[1]
    spread_small(vectors, small, places[2], 1, 1)
    spread_small(vectors, small, places[3], 1, 2)
    own_reduce.wait()
    line_reduce.send_own()
    kept = []
    waiting = list(loads)

    def compute(chip):
        while waiting:
            waiting.pop().wait()

        def units(cols):
            rows = pair_rows(blocks, chip)
            gate = dot(rows, expand_mat[0, cols], ((1,), (1,))) + shift[0:1, cols]
            upper = dot(rows, expand_mat[1, cols], ((1,), (1,))) + shift[1:2, cols]
            factor = math.sqrt(2 / math.pi)
            square = gate * gate
            bend = jnp.tanh(factor * gate * (1 + 0.044715 * square))
            value = 0.5 * gate * (1 + bend)
            pull = 0.5 * (1 + bend) + 0.5 * gate * (1 - bend * bend) * factor * (
                1 + 3 * 0.044715 * square
            )
            set_pair(active, chip, cols, value * upper)
            set_pair(slope, chip, cols, pull * upper)
            set_pair(gelu, chip, cols, value)

        tiles(active.shape[2], 256, units)

        pair = pl.ds(2 * chip, 2)
        for index, (source, target) in enumerate(
            ((active, active_out), (slope, slope_out), (gelu, gelu_out))
        ):
            copy = pltpu.make_async_copy(
                source.at[pair], target.at[pair], keep_sems.at[chip, index]
            )
            copy.start()
            kept.append(copy)

    def compute_sums(start, count):
        def compute(chip):
            def outputs(some):
                part = dot(pair_rows(active, chip), reduce_mat[:, some], ((1,), (0,)))
                set_pair(parts, chip, some, part)

            tiles(count, 256, outputs, start)

        return compute

    offsets = [0]
    for distance in range(1, plane.far):
        offsets += [-distance, distance]
    offsets.append(plane.far)
    chips = [chip_at(plane.position + offset, plane.ring) for offset in offsets]
    for index, chip in enumerate(chips):
        if index == len(chips) - 1:
            line_reduce.step(1)
        compute(chip)
    step = 1
    for window, (first, blocks_in, needed) in enumerate(windows):
        while step < needed:
            step += 1
            line_reduce.step(step)
        start = pl.multiple_of(first * cols, cols)
        planes[window].start_sums(compute_sums(start, blocks_in * cols))
        if window > 0:
            planes[window - 1].last_sums()
    planes[-1].last_sums()
    keep_reduce = pltpu.make_async_copy(
        reduce_mat.at[pl.ds(0, filled)], reduce_out, load_sems.at[3]
    )
    keep_reduce.start()
    for part in planes:
        part.finish(feed)

    row_sums[...] = jnp.zeros_like(row_sums)

    def norm_rows(i, carry):
        some = pl.ds(pl.multiple_of(i * 16, 16), 16)
        result, normed, inverse = normalize(
            residual_scale * hidden[some] + feed[some] + vectors[0:1],
            vectors[1:2],
            vectors[2:3],
        )
        layer_output[some] = result.astype(jnp.bfloat16)
        upstream = cotangent[some].astype(jnp.float32)
        total = normalize_back(upstream, normed, inverse, vectors[1:2])
        sum_grad[some] = total
        feed_grad[some] = total.astype(jnp.bfloat16)
        row_sums[0:1] += jnp.sum(upstream * normed, axis=0, keepdims=True)
        row_sums[1:2] += jnp.sum(upstream, axis=0, keepdims=True)
        row_sums[2:3] += jnp.sum(total, axis=0, keepdims=True)
        return carry

    lax.fori_loop(0, rows_all.shape[1] // 16, norm_rows, 0, unroll=2)
    for part in planes:
        part.drain()
    keep_reduce.wait()
    line_reduce.drain()
    for copy in kept:
        copy.wait()


def geglu_forward(
    wide_count,
    narrow_count,
    places,
    rows_all,
    expand,
    reduce_weight,
    small,
    hidden,
    cotangent,
):
    _, rows, width = rows_all.shape
    padded = -(-expand.shape[1] // 256) * 256
    anywhere = pl.BlockSpec(memory_space=pl.ANY)
    vmem = pl.BlockSpec(memory_space=pltpu.VMEM)
    kept = jax.ShapeDtypeStruct((wide_count, rows, padded), jnp.bfloat16)
    scratch = [pltpu.VMEM((rows, width), jnp.float32)]
    scratch.append(pltpu.VMEM((wide_count, rows, width), jnp.bfloat16))
    scratch += sum_scratch(wide_count, rows, width) + [
        pltpu.VMEM((2, padded, width), jnp.bfloat16),
        pltpu.VMEM((padded, width), jnp.bfloat16),
        pltpu.VMEM((wide_count, rows, padded), jnp.bfloat16),
        pltpu.VMEM((wide_count, rows, padded), jnp.bfloat16),
        pltpu.VMEM((wide_count, rows, padded), jnp.bfloat16),
        pltpu.SemaphoreType.DMA((5,)),
        pltpu.SemaphoreType.DMA((wide_count // 2, 3)),
        pltpu.SemaphoreType.DMA((2, narrow_count)),
        pltpu.SemaphoreType.DMA((narrow_count,)),
    ] + 2 * sum_scratch(wide_count, rows, width)[3:]
    scratch += [pltpu.VMEM((2, padded), jnp.float32), pltpu.VMEM((3, width), jnp.float32)]
    return pl.pallas_call(
        functools.partial(geglu_forward_kernel, wide_count, narrow_count, places),
        out_shape=(
            jax.ShapeDtypeStruct((reduce_weight.shape[0], width), jnp.bfloat16),
            kept,
            kept,
            kept,
            jax.ShapeDtypeStruct((rows, width), jnp.bfloat16),
            jax.ShapeDtypeStruct((rows, width), jnp.float32),
            jax.ShapeDtypeStruct((rows, width), jnp.bfloat16),
            jax.ShapeDtypeStruct((3, width), jnp.float32),
        ),
        in_specs=[anywhere] * 3 + [vmem] * 3,
        out_specs=(anywhere,) * 4 + (vmem,) * 4,
        scratch_shapes=scratch,
        compiler_params=pltpu.CompilerParams(
            collective_id=1, has_side_effects=True, vmem_limit_bytes=kernel_memory
        ),
        cost_estimate=pl.CostEstimate(
            flops=6 * wide_count * rows * padded * width, bytes_accessed=200 * 2**20, transcendentals=0
        ),
        name="geglu_forward",
    )(
        rows_all,
        expand,
        reduce_weight,
        small,
        hidden,
        cotangent,
    )


def geglu_backward_kernel(
    wide_count,
    narrow_count,
    own,
    expand,
    reduce,
    slope_in,
    gelu_in,
    active_in,
    rows_in,
    reduce_grad,
    expand_part,
    hidden_grad,
    unit_sums,
    blocks,
    gather_send,
    gather_recv,
    own_sem,
    parts,
    from_mate,
    incoming,
    mate_send,
    mate_recv,
    sum_send,
    sum_recv,
    expand_mat,
    reduce_mat,
    slope,
    gelu,
    active,
    rows_all,
    staged,
    load_sems,
    keep_sems,
    line_in,
    line_send,
    line_recv,
):
    sems = (gather_send, gather_recv, mate_send, mate_recv, sum_send, sum_recv, own_sem)
    plane = PlaneExchange(wide_count, own, blocks, parts, from_mate, incoming, sems)
    loads = [
        load_padded(expand.at[0], expand_mat.at[0], load_sems.at[0]),
        load_padded(expand.at[1], expand_mat.at[1], load_sems.at[1]),
        load_padded(reduce, reduce_mat, load_sems.at[2]),
        pltpu.make_async_copy(slope_in, slope, load_sems.at[3]),
        pltpu.make_async_copy(gelu_in, gelu, load_sems.at[4]),
    ]
    late_loads = [
        pltpu.make_async_copy(active_in, active, load_sems.at[5]),
        pltpu.make_async_copy(rows_in, rows_all, load_sems.at[6]),
    ]
    for copy in loads[3:]:
        copy.start()
    unit_sums[...] = jnp.zeros_like(unit_sums)
    line = LineExchange(narrow_count)
    filled, line_cols = line_in.shape[2:]

    def line_part(block):
        return reduce_mat.at[
            pl.ds(0, filled), pl.ds(pl.multiple_of(block * line_cols, line_cols), line_cols)
        ]

    line_sum = LineSum(line, line_part, line_in, line_send, line_recv)
    greet_plane(plane)
    line.greet(3)
    for copy in late_loads:
        copy.start()
    kept = []
    waiting = list(loads)

    def compute(chip):
        while waiting:
            waiting.pop().wait()

        def units(cols):
            pulled = dot(pair_rows(blocks, chip), reduce_mat[cols], ((1,), (1,)))
            pair = pl.ds(2 * chip, 2)
            shape = pulled.shape
            gate_grad = pulled * slope[pair, :, cols].reshape(shape).astype(jnp.float32)
            upper_grad = pulled * gelu[pair, :, cols].reshape(shape).astype(jnp.float32)
            set_pair(slope, chip, cols, gate_grad)
            set_pair(gelu, chip, cols, upper_grad)
            unit_sums[0:1, cols] += jnp.sum(gate_grad, axis=0, keepdims=True)
            unit_sums[1:2, cols] += jnp.sum(upper_grad, axis=0, keepdims=True)

        tiles(slope.shape[2], 256, units)

    def compute_sums(chip):
        def outputs(cols):
            set_pair(
                parts,
                chip,
                cols,
                dot(pair_rows(slope, chip), expand_mat[0, :, cols], ((1,), (0,)))
                + dot(pair_rows(gelu, chip), expand_mat[1, :, cols], ((1,), (0,))),
            )

        tiles(parts.shape[2], 256, outputs)

    def product(left, right, start):
        tokens = left.shape[0] * left.shape[1]
        return dot(
            left[:, :, start : start + 256].reshape(tokens, 256),
            right[...].reshape(tokens, right.shape[2]),
            ((0,), (0,)),
        ).astype(jnp.bfloat16)

    def reduce_work():
        for copy in late_loads:
            copy.wait()

        def reduce_cols(index):
            cols = pl.ds(pl.multiple_of(index * line_cols, line_cols), line_cols)

            def units(some):
                tokens = active.shape[0] * active.shape[1]
                part = dot(
                    active[:, :, some].reshape(tokens, some.size),
                    blocks[:, :, cols].reshape(tokens, line_cols),
                    ((0,), (0,)),
                )
                reduce_mat[some, cols] = part.astype(jnp.bfloat16)

            tiles(active.shape[2], 256, units)

        for offset in range(narrow_count - 1, 0, -1):
            for way in range(2):

                @pl.when(line_sum.reaches(way, offset))
                def _():
                    reduce_cols(line_sum.target(way, offset))

            line_sum.begin(offset)
        reduce_cols(line.mine)

    def expand_work(left, start, target):
        def work():
            index = len(kept)
            if index >= 2:
                kept[index - 2].wait()
            staged[index % 2] = product(left, rows_all, start)
            stop = min(256, target.shape[0] - start)
            copy = pltpu.make_async_copy(
                staged.at[index % 2, pl.ds(0, stop)],
                target.at[pl.ds(start, stop)],
                keep_sems.at[index % 2],
            )
            copy.start()
            kept.append(copy)

        return work

    works = [
        expand_work(left, start, target)
        for left, target in ((slope, expand_part.at[0]), (gelu, expand_part.at[1]))
        for start in range(0, target.shape[0], 256)
    ]
    steps = [
        functools.partial(line_sum.step, offset) for offset in range(narrow_count - 2, 0, -1)
    ]
    third = len(works) // 3
    middle = (len(steps) + 1) // 2

    def many(calls):
        for call in calls:
            call()

    beside = functools.partial(many, steps[:middle] + works[:third])
    plane.run(compute, compute_sums, reduce_work, beside)
    many(works[third : 2 * third] + steps[middle:] + works[2 * third :])
    plane.finish(hidden_grad)
    plane.drain()
    line_sum.finish(reduce_grad)
    line_sum.drain()
    for copy in kept[-2:]:
        copy.wait()


def geglu_backward(
    wide_count,
    narrow_count,
    feed_grad,
    expand,
    reduce_full,
    slope,
    gelu,
    active,
    rows_all,
):
    rows, width = feed_grad.shape
    padded = slope.shape[2]
    anywhere = pl.BlockSpec(memory_space=pl.ANY)
    vmem = pl.BlockSpec(memory_space=pltpu.VMEM)
    scratch = exchange_scratch(wide_count, rows, width) + [
        pltpu.VMEM((2, padded, width), jnp.bfloat16),
        pltpu.VMEM((padded, width), jnp.bfloat16),
        pltpu.VMEM((wide_count, rows, padded), jnp.bfloat16),
        pltpu.VMEM((wide_count, rows, padded), jnp.bfloat16),
        pltpu.VMEM((wide_count, rows, padded), jnp.bfloat16),
        pltpu.VMEM((wide_count, rows, width), jnp.bfloat16),
        pltpu.VMEM((2, 256, width), jnp.bfloat16),
        pltpu.SemaphoreType.DMA((7,)),
        pltpu.SemaphoreType.DMA((2,)),
        pltpu.VMEM(
            (2, narrow_count - 1, reduce_full.shape[0], width // narrow_count), jnp.bfloat16
        ),
        pltpu.SemaphoreType.DMA((2, narrow_count - 1)),
        pltpu.SemaphoreType.DMA((2, narrow_count - 1)),
    ]
    return pl.pallas_call(
        functools.partial(geglu_backward_kernel, wide_count, narrow_count),
        out_shape=(
            jax.ShapeDtypeStruct(
                (reduce_full.shape[0], width // narrow_count), jnp.float32
            ),
            jax.ShapeDtypeStruct(expand.shape, jnp.bfloat16),
            jax.ShapeDtypeStruct((rows, width), jnp.float32),
            jax.ShapeDtypeStruct((2, padded), jnp.float32),
        ),
        in_specs=[anywhere] * 7,
        out_specs=(vmem, anywhere, vmem, vmem),
        scratch_shapes=scratch,
        compiler_params=pltpu.CompilerParams(
            collective_id=2, has_side_effects=True, vmem_limit_bytes=63 * 2**20
        ),
        cost_estimate=pl.CostEstimate(
            flops=12 * wide_count * rows * padded * width, bytes_accessed=200 * 2**20, transcendentals=0
        ),
        name="geglu_backward",
    )(feed_grad, expand, reduce_full, slope, gelu, active, rows_all)


def rotate_lanes(vectors, cosine, signed_sine):
    return vectors * cosine + pltpu.roll(vectors, vectors.shape[1] // 2, 1) * signed_sine


def attention_backward_kernel(
    wide_count,
    narrow_count,
    places,
    upper_grad,
    hidden_part,
    normed,
    inv_std,
    small,
    merge,
    mixed,
    queries,
    keys,
    values,
    probs,
    cosine,
    signed_sine,
    triple,
    merge_grad,
    heads_sums,
    merge_sums,
    sum_grad,
    norm_sums,
    gain,
    attended,
    upstream,
    outbound,
    probs_held,
    keys_turned,
    key_total,
    value_total,
    merge_out,
    merge_in,
    mixed_send,
    mixed_recv,
    merge_send,
    merge_recv,
    load_sems,
    parts,
    from_mate,
    incoming,
    mate_send,
    mate_recv,
    sum_send,
    sum_recv,
):
    sems = (None, None, mate_send, mate_recv, sum_send, sum_recv, None)
    plane = PlaneExchange(wide_count, None, None, parts, from_mate, incoming, sems)
    line = LineExchange(narrow_count)
    rows, width = sum_grad.shape
    own_cols = queries.shape[1]
    heads = own_cols // HDIM
    scale = HDIM ** (-0.5)

    def load(head):
        return pltpu.make_async_copy(
            probs.at[head], probs_held.at[head % 2], load_sems.at[head % 2]
        )

    load(0).start()
    greet_plane(plane)

    spread_small(gain, small, places[2], 0)
    norm_sums[...] = jnp.zeros_like(norm_sums)
    merge_sums[...] = jnp.zeros_like(merge_sums)

    def norm_rows(i, carry):
        some = pl.ds(pl.multiple_of(i * 16, 16), 16)
        hidden_grad = residual_scale * upper_grad[some] + hidden_part[some]
        norm_sums[0:1] += jnp.sum(hidden_grad * normed[some], axis=0, keepdims=True)
        norm_sums[1:2] += jnp.sum(hidden_grad, axis=0, keepdims=True)
        total = normalize_back(hidden_grad, normed[some], inv_std[some], gain[...])
        sum_grad[some] = total
        merge_sums[...] += jnp.sum(total, axis=0, keepdims=True)
        attended[some] = total.astype(jnp.bfloat16)
        return carry

    lax.fori_loop(0, rows // 16, norm_rows, 0, unroll=2)
    line.greet(3)

    def mixed_part(target, where):
        part = dot(
            attended[...],
            merge[pl.ds(pl.multiple_of(where * own_cols, own_cols), own_cols)],
            ((1,), (1,)),
        )
        target[...] = part.astype(jnp.bfloat16)

    for offset in range(1, narrow_count):
        place = line.peer(offset)
        mixed_part(outbound.at[offset - 1], place)
        line.send(offset, outbound.at[offset - 1], upstream, mixed_send, mixed_recv)
    mixed_part(upstream.at[line.mine], line.mine)

    block = parts.shape[1]

    def merge_rows(i, carry):
        cols = pl.ds(pl.multiple_of(i * block, block), block)
        parts[i] = dot(mixed[:, cols], attended[...], ((0,), (0,))).astype(jnp.bfloat16)
        return carry

    lax.fori_loop(0, wide_count, merge_rows, 0)
    for offset in range(plane.ring):
        plane.share(offset)
    plane.first_sums()
    plane.far_sums()
    plane.last_sums()
    plane.finish(merge_out)
    count = merge_grad.shape[0]

    def z_rows(where):
        return pl.ds(pl.multiple_of(where * count, count), count)

    for offset in range(1, narrow_count):
        line.send(
            offset, merge_out.at[z_rows(line.peer(offset))], merge_in, merge_send, merge_recv
        )
    for offset in range(1, narrow_count):
        line.arrived(offset, upstream, mixed_send, mixed_recv)

    def one_head(head):
        cols = pl.ds(head * HDIM, HDIM)
        load(head).wait()
        if head + 1 < heads:
            load(head + 1).start()
        held = probs_held.at[head % 2]
        keys_turned[...] = keys[:, cols].astype(jnp.float32).T.astype(jnp.bfloat16)
        key_total[...] = jnp.zeros_like(key_total)
        value_total[...] = jnp.zeros_like(value_total)

        def chunk(i, carry):
            here = pl.ds(pl.multiple_of(i * rows, rows), rows)
            weights_low = held[:, here]
            up = upstream[i, :, cols]
            pulled = dot(values[:, cols], up, ((1,), (1,)))
            weights = weights_low.astype(jnp.float32)
            scaled = weights * pulled
            change = (scaled - weights * jnp.sum(scaled, axis=0, keepdims=True)).astype(
                jnp.bfloat16
            )
            key_total[...] += dot(change, queries[here, cols], ((1,), (0,)))
            value_total[...] += dot(weights_low, up, ((1,), (0,)))
            query_grad = dot(keys_turned[...], change, ((1,), (0,))).T * scale
            triple[here, cols] = rotate_lanes(
                query_grad, cosine[here], signed_sine[here]
            ).astype(jnp.bfloat16)
            return carry

        lax.fori_loop(0, narrow_count, chunk, 0)

        def ending(i, carry):
            here = pl.ds(pl.multiple_of(i * rows, rows), rows)
            triple[here, pl.ds(own_cols + head * HDIM, HDIM)] = rotate_lanes(
                key_total[here] * scale, cosine[here], signed_sine[here]
            ).astype(jnp.bfloat16)
            triple[here, pl.ds(2 * own_cols + head * HDIM, HDIM)] = value_total[here].astype(
                jnp.bfloat16
            )
            return carry

        lax.fori_loop(0, narrow_count, ending, 0)

    for head in range(heads):
        one_head(head)

    def column_sums(cols):
        heads_sums[:, cols] = jnp.sum(
            triple[:, cols].astype(jnp.float32), axis=0, keepdims=True
        )

    tiles(3 * own_cols, 256, column_sums)
    summed = merge_out[z_rows(line.mine)].astype(jnp.float32)
    for offset in range(1, narrow_count):
        line.arrived(offset, merge_in, merge_send, merge_recv)
        summed += merge_in[line.peer(offset)].astype(jnp.float32)
    merge_grad[...] = summed
    line.drain()
    plane.drain()


def attention_backward(
    wide_count,
    narrow_count,
    places,
    upper_grad,
    hidden_part,
    normed,
    inv_std,
    small,
    merge_full,
    mixed,
    queries,
    keys,
    values,
    probs,
    cosine,
    signed_sine,
):
    rows, width = normed.shape
    bucket, own_cols = queries.shape
    block = width // wide_count
    count = block // narrow_count
    anywhere = pl.BlockSpec(memory_space=pl.ANY)
    vmem = pl.BlockSpec(memory_space=pltpu.VMEM)
    dma = pltpu.SemaphoreType.DMA
    return pl.pallas_call(
        functools.partial(attention_backward_kernel, wide_count, narrow_count, places),
        out_shape=(
            jax.ShapeDtypeStruct((bucket, 3 * own_cols), jnp.bfloat16),
            jax.ShapeDtypeStruct((count, width), jnp.float32),
            jax.ShapeDtypeStruct((1, 3 * own_cols), jnp.float32),
            jax.ShapeDtypeStruct((1, width), jnp.float32),
            jax.ShapeDtypeStruct((rows, width), jnp.float32),
            jax.ShapeDtypeStruct((2, width), jnp.float32),
        ),
        in_specs=[vmem] * 10 + [anywhere] + [vmem] * 2,
        out_specs=(vmem,) * 6,
        scratch_shapes=[
            pltpu.VMEM((1, width), jnp.float32),
            pltpu.VMEM((rows, width), jnp.bfloat16),
            pltpu.VMEM((narrow_count, rows, own_cols), jnp.bfloat16),
            pltpu.VMEM((narrow_count - 1, rows, own_cols), jnp.bfloat16),
            pltpu.VMEM((2, bucket, bucket), jnp.bfloat16),
            pltpu.VMEM((HDIM, bucket), jnp.bfloat16),
            pltpu.VMEM((bucket, HDIM), jnp.float32),
            pltpu.VMEM((bucket, HDIM), jnp.float32),
            pltpu.VMEM((block, width), jnp.bfloat16),
            pltpu.VMEM((narrow_count, count, width), jnp.bfloat16),
            dma((narrow_count - 1,)),
            dma((narrow_count,)),
            dma((narrow_count - 1,)),
            dma((narrow_count,)),
            dma((2,)),
        ]
        + sum_scratch(wide_count, block, width),
        compiler_params=pltpu.CompilerParams(
            collective_id=3, has_side_effects=True, vmem_limit_bytes=kernel_memory
        ),
        cost_estimate=pl.CostEstimate(
            flops=60 * 10**9, bytes_accessed=200 * 2**20, transcendentals=0
        ),
        name="attention_backward",
    )(
        upper_grad,
        hidden_part,
        normed,
        inv_std,
        small,
        merge_full,
        mixed,
        queries,
        keys,
        values,
        probs,
        cosine,
        signed_sine,
    )


def input_backward_kernel(
    wide_count,
    narrow_count,
    inputs,
    triple,
    heads_mat,
    small,
    sum_grad,
    input_part,
    heads_grad,
    heads_bias_grad,
    merge_bias_grad,
    gains_grad,
    shifts_grad,
    expand_bias_grad,
    reduce_bias_grad,
    small_result,
    line_parts,
    line_in,
    heads_out,
    heads_in,
    small_wide,
    small_sum,
    small_line,
    line_send,
    line_recv,
    heads_send,
    heads_recv,
    wide_send,
    wide_recv,
    small_send,
    small_recv,
    parts,
    from_mate,
    incoming,
    mate_send,
    mate_recv,
    sum_send,
    sum_recv,
):
    sems = (None, None, mate_send, mate_recv, sum_send, sum_recv, None)
    plane = PlaneExchange(wide_count, None, None, parts, from_mate, incoming, sems)
    line = LineExchange(narrow_count)
    rows, width = input_part.shape
    here = line.mine
    last = narrow_count - 1
    place = lax.axis_index("wide")

    def wide_peer(offset):
        return (place + offset) % wide_count

    barrier = pltpu.get_barrier_semaphore()
    for offset in range(1, wide_count):
        pl.semaphore_signal(
            barrier,
            inc=1,
            device_id={"wide": wide_peer(offset)},
            device_id_type=pl.DeviceIdType.MESH,
        )
    line.greet(wide_count - 1)

    def small_copy(offset, source, slot):
        return pltpu.make_async_remote_copy(
            src_ref=source,
            dst_ref=small_wide.at[slot],
            send_sem=wide_send.at[offset - 1],
            recv_sem=wide_recv.at[slot],
            device_id={"wide": wide_peer(offset)},
            device_id_type=pl.DeviceIdType.MESH,
        )

    small_copies = [
        small_copy(offset, small.at[wide_peer(offset)], place) for offset in range(1, wide_count)
    ]
    for copy in small_copies:
        copy.start()

    line_sum = LineSum(line, lambda target: line_parts.at[target], line_in, line_send, line_recv)

    def input_rows(index):
        some = pl.ds(pl.multiple_of(index * rows, rows), rows)

        def input_cols(cols):
            part = dot(triple[some], heads_mat[cols], ((1,), (1,)))
            line_parts[index, :, cols] = part.astype(jnp.bfloat16)

        tiles(width, 256, input_cols)

    for offset in range(last, 0, -1):
        for way in range(2):

            @pl.when(line_sum.reaches(way, offset))
            def _():
                input_rows(line_sum.target(way, offset))

        line_sum.begin(offset)
    input_rows(here)

    block = parts.shape[1]

    def heads_rows(i, carry):
        cols = pl.ds(pl.multiple_of(i * block, block), block)
        parts[i] = dot(inputs[:, cols], triple[...], ((0,), (0,))).astype(jnp.bfloat16)
        return carry

    lax.fori_loop(0, wide_count, heads_rows, 0)
    for offset in range(plane.ring):
        plane.share(offset)
    for offset in range(last - 1, last // 2, -1):
        line_sum.step(offset)
    plane.first_sums()
    plane.far_sums()

    for offset in range(1, wide_count):
        peer = wide_peer(offset)
        small_copy(offset, small_wide.at[peer], peer).wait_recv()
    small_wide[place] = small[place]
    total = small_wide[0]
    for index in range(1, wide_count):
        total += small_wide[index]
    small_sum[...] = total
    for offset in range(1, narrow_count):
        line.send(offset, small_sum.at[line.peer(offset)], small_line, small_send, small_recv)

    plane.last_sums()
    for offset in range(last // 2, 0, -1):
        line_sum.step(offset)
    plane.finish(heads_out)
    count = heads_grad.shape[0]

    def z_rows(where):
        return pl.ds(pl.multiple_of(where * count, count), count)

    for offset in range(1, narrow_count):
        line.send(
            offset, heads_out.at[z_rows(line.peer(offset))], heads_in, heads_send, heads_recv
        )
    heads_in[line.mine] = heads_out[z_rows(line.mine)]
    small_line[line.mine] = small_sum[line.mine]
    for offset in range(1, narrow_count):
        line.arrived(offset, small_line, small_send, small_recv)
    result = small_line[0]
    for index in range(1, narrow_count):
        result += small_line[index]
    small_result[...] = result
    row = 0
    for target in (
        heads_bias_grad,
        merge_bias_grad,
        gains_grad,
        shifts_grad,
        expand_bias_grad,
        reduce_bias_grad,
    ):
        first, size = target.shape
        for index in range(first):
            for start in range(0, size, 128):
                stop = min(start + 128, size)
                target[index : index + 1, start:stop] = small_result[
                    row : row + 1, 0 : stop - start
                ]
                row += 1

    line_sum.finish(input_part)

    def add_residual(i, carry):
        some = pl.ds(pl.multiple_of(i * 16, 16), 16)
        input_part[some] += residual_scale * sum_grad[some]
        return carry

    lax.fori_loop(0, rows // 16, add_residual, 0)
    for offset in range(1, narrow_count):
        line.arrived(offset, heads_in, heads_send, heads_recv)
    own_cols = triple.shape[1] // 3
    for index in range(narrow_count):
        for which in range(3):
            start = (which * narrow_count + index) * own_cols
            heads_grad[:, start : start + own_cols] = heads_in[
                index, :, which * own_cols : (which + 1) * own_cols
            ].astype(jnp.float32)
    line_sum.drain()
    for copy in small_copies:
        copy.wait_send()
    line.drain()
    plane.drain()


def input_backward(
    wide_count, narrow_count, inputs, triple_grad, heads_mat, small, sum_grad, small_shapes
):
    bucket, width = inputs.shape
    rows = bucket // narrow_count
    columns = triple_grad.shape[1]
    block = width // wide_count
    count = block // narrow_count
    vmem = pl.BlockSpec(memory_space=pltpu.VMEM)
    dma = pltpu.SemaphoreType.DMA
    lines = small.shape[2]
    return pl.pallas_call(
        functools.partial(input_backward_kernel, wide_count, narrow_count),
        out_shape=(
            jax.ShapeDtypeStruct((rows, width), jnp.float32),
            jax.ShapeDtypeStruct((count, narrow_count * columns), jnp.float32),
        )
        + tuple(jax.ShapeDtypeStruct(shape, jnp.float32) for shape in small_shapes),
        in_specs=[vmem] * 5,
        out_specs=(vmem,) * 8,
        scratch_shapes=[
            pltpu.VMEM((lines, 128), jnp.float32),
            pltpu.VMEM((narrow_count, rows, width), jnp.bfloat16),
            pltpu.VMEM((2, narrow_count - 1, rows, width), jnp.bfloat16),
            pltpu.VMEM((block, columns), jnp.bfloat16),
            pltpu.VMEM((narrow_count, count, columns), jnp.bfloat16),
            pltpu.VMEM((wide_count, narrow_count, lines, 128), jnp.float32),
            pltpu.VMEM((narrow_count, lines, 128), jnp.float32),
            pltpu.VMEM((narrow_count, lines, 128), jnp.float32),
            dma((2, narrow_count - 1)),
            dma((2, narrow_count - 1)),
            dma((narrow_count - 1,)),
            dma((narrow_count,)),
            dma((wide_count - 1,)),
            dma((wide_count,)),
            dma((narrow_count - 1,)),
            dma((narrow_count,)),
        ]
        + sum_scratch(wide_count, block, columns),
        compiler_params=pltpu.CompilerParams(
            collective_id=4, has_side_effects=True, vmem_limit_bytes=kernel_memory
        ),
        cost_estimate=pl.CostEstimate(
            flops=80 * 10**9, bytes_accessed=200 * 2**20, transcendentals=0
        ),
        name="input_backward",
    )(inputs, triple_grad, heads_mat, small, sum_grad)


def greet_all(wide_count, narrow_count):
    barrier = pltpu.get_barrier_semaphore()
    for axis, count in (("wide", wide_count), ("narrow", narrow_count)):
        place = lax.axis_index(axis)
        for offset in range(1, count):
            pl.semaphore_signal(
                barrier,
                inc=1,
                device_id={axis: (place + offset) % count},
                device_id_type=pl.DeviceIdType.MESH,
            )
    pl.semaphore_wait(barrier, wide_count + narrow_count - 2)


def gather_kernel(
    wide_count,
    narrow_count,
    own,
    heads_weight,
    merge_weight,
    heads_bias,
    merge_bias,
    norm_gains,
    norm_shifts,
    expand_bias,
    reduce_bias,
    joined_ref,
    prefix_ref,
    speeds,
    rows_out,
    heads_out,
    merge_out,
    small_out,
    triple,
    cosine,
    signed_sine,
    first_query,
    last_query,
    small,
    rows_all,
    triple_all,
    heads_all,
    merge_own,
    small_all,
    rows_send,
    rows_recv,
    heads_send,
    heads_recv,
    merge_send,
    merge_recv,
    small_send,
    small_recv,
    wide_send,
    wide_recv,
    local_sems,
    out_sems,
    heads_ring_send,
    heads_ring_recv,
    block_sems,
):
    ring_sems = (heads_ring_send, heads_ring_recv, None, None, None, None, None)
    heads_ring = PlaneExchange(wide_count, None, heads_all, heads_all, None, None, ring_sems)
    line = LineExchange(narrow_count)
    here = line.mine
    last = narrow_count - 1
    place = lax.axis_index("wide")
    slot = heads_ring.slot(0)
    rows, width = own.shape
    count = heads_weight.shape[0]
    columns = heads_all.shape[2]
    own_cols = columns // 3

    def z_rows(where):
        return pl.ds(pl.multiple_of(where * count, count), count)

    def head_cols(which, where):
        start = which * narrow_count * own_cols + where * own_cols
        return pl.ds(pl.multiple_of(start, own_cols), own_cols)

    line_rows = LineGather(line, lambda block: rows_all.at[block], rows_send, rows_recv)

    keep_rows = pltpu.make_async_copy(own, rows_all.at[here], local_sems.at[0])
    keep_rows.start()
    keeps = [
        pltpu.make_async_copy(
            heads_weight.at[:, head_cols(which, here)],
            heads_all.at[slot, z_rows(here), pl.ds(which * own_cols, own_cols)],
            local_sems.at[2 + which],
        )
        for which in range(3)
    ]
    keep_merge = pltpu.make_async_copy(
        merge_weight, merge_own.at[z_rows(here)], local_sems.at[1]
    )
    for copy in keeps + [keep_merge]:
        copy.start()
    smalls = (heads_bias, merge_bias, norm_gains, norm_shifts, expand_bias, reduce_bias)
    small[...] = jnp.zeros_like(small)
    row = 0
    for part in smalls:
        first, size = part.shape
        for index in range(first):
            for begin in range(0, size, 128):
                stop = min(begin + 128, size)
                small[row : row + 1, 0 : stop - begin] = part[
                    index : index + 1, begin:stop
                ].astype(jnp.float32)
                row += 1
    small_all[place, here] = small[...]
    greet_all(wide_count, narrow_count)

    def heads_copy(offset, which, where, sender):
        return line.copy(
            heads_weight.at[:, head_cols(which, where)],
            heads_all.at[slot, z_rows(sender), pl.ds(which * own_cols, own_cols)],
            heads_send.at[offset - 1, which],
            heads_recv.at[sender, which],
            where,
        )

    def merge_copy(offset, where, sender):
        return line.copy(
            merge_weight,
            merge_own.at[z_rows(sender)],
            merge_send.at[offset - 1],
            merge_recv.at[sender],
            where,
        )

    def small_copy(offset, where, sender):
        return line.copy(
            small,
            small_all.at[place, sender],
            small_send.at[offset - 1],
            small_recv.at[sender],
            where,
        )

    started = []

    def start(copy):
        copy.start()
        started.append(copy)

    keep_rows.wait()
    line_rows.send_own()
    for offset in range(1, narrow_count):
        for which in range(3):
            start(heads_copy(offset, which, line.peer(offset), here))
    for offset in range(1, narrow_count):
        start(small_copy(offset, line.peer(offset), here))

    halfway = narrow_count * rows // 2
    joined = joined_ref[0]

    def tables(i, carry):
        some = pl.ds(pl.multiple_of(i * rows, rows), rows)
        place_in = i * rows + lax.broadcasted_iota(jnp.int32, (rows, 1), 0)
        second = jnp.where(place_in >= halfway, 1 - joined, 0)
        local = place_in - second * halfway
        reach = jnp.where(
            joined == 1,
            prefix_ref[0, 0] + prefix_ref[0, 1],
            jnp.where(second == 1, prefix_ref[0, 1], prefix_ref[0, 0]),
        )
        first_query[some] = jnp.where(local < reach, place_in - local, place_in)
        last_query[some] = jnp.where(
            (joined == 1) | (second == 1), 2 * halfway - 1, halfway - 1
        ) + jnp.zeros_like(place_in)
        angles = local.astype(jnp.float32) * speeds[...]
        lane = lax.broadcasted_iota(jnp.int32, (rows, HDIM), 1)
        cosine[some] = jnp.cos(angles)
        sine = jnp.sin(angles)
        signed_sine[some] = jnp.where(lane < HDIM // 2, sine, -sine)
        return carry

    lax.fori_loop(0, narrow_count, tables, 0)

    line_rows.step(1)
    for copy in keeps:
        copy.wait()
    for offset in range(1, narrow_count):
        for which in range(3):
            heads_copy(offset, which, line.peer(offset), line.peer(offset)).wait_recv()
    heads_ring.send_own()
    for offset in range(1, narrow_count):
        small_copy(offset, line.peer(offset), line.peer(offset)).wait_recv()

    def wide_copy(offset, sender):
        return pltpu.make_async_remote_copy(
            src_ref=small_all.at[sender],
            dst_ref=small_all.at[sender],
            send_sem=wide_send.at[offset - 1],
            recv_sem=wide_recv.at[sender],
            device_id={"wide": (place + offset) % wide_count},
            device_id_type=pl.DeviceIdType.MESH,
        )

    for offset in range(1, wide_count):
        start(wide_copy(offset, place))

    def leave_rows(block):
        return pltpu.make_async_copy(rows_all.at[block], rows_out.at[block], block_sems.at[0, block])

    def leave_triple(block):
        return pltpu.make_async_copy(triple_all.at[block], triple.at[block], block_sems.at[1, block])

    def project(block):
        leave_rows(block).start()

        def cols_step(cols):
            weight = heads_all[:, :, cols].reshape(width, cols.size)
            triple_all[block, :, cols] = dot(rows_all[block], weight, ((1,), (0,)))

        tiles(columns, 256, cols_step)
        leave_triple(block).start()

    def project_step(step):
        line_rows.each(step, project)

    def gather(ring, distance):
        ring.receive(distance)
        ring.receive_mate(-distance)
        if distance < ring.far:
            ring.receive_mate(distance)

    outs = []

    def keep_out(source, target):
        copy = pltpu.make_async_copy(source, target, out_sems.at[len(outs)])
        copy.start()
        outs.append(copy)

    for offset in range(1, narrow_count):
        start(merge_copy(offset, line.peer(offset), here))
    heads_ring.receive_mate(0)
    for distance in range(1, heads_ring.far):
        gather(heads_ring, distance)
    if last > 1:
        line_rows.step(2)
    gather(heads_ring, heads_ring.far)
    keep_out(heads_all, heads_out)
    project(here)
    project_step(1)
    for step in range(3, narrow_count):
        project_step(step - 1)
        line_rows.step(step)
    project_step(last)
    keep_merge.wait()
    for offset in range(1, narrow_count):
        merge_copy(offset, line.peer(offset), line.peer(offset)).wait_recv()
    keep_out(merge_own, merge_out)
    for offset in range(1, wide_count):
        wide_copy(offset, (place + offset) % wide_count).wait_recv()
    keep_out(small_all, small_out)
    line_rows.drain()
    for copy in started:
        copy.wait_send()
    heads_ring.drain()
    for copy in outs:
        copy.wait()

    def left(block, carry):
        leave_rows(block).wait()
        leave_triple(block).wait()
        return carry

    lax.fori_loop(0, narrow_count, left, 0)


def gather_front(
    wide_count, narrow_count, layer_input, heads_weight, merge_weight, smalls, joined, prefix, speeds
):
    rows, width = layer_input.shape
    count, all_columns = heads_weight.shape
    columns = all_columns // narrow_count
    block = count * narrow_count
    anywhere = pl.BlockSpec(memory_space=pl.ANY)
    vmem = pl.BlockSpec(memory_space=pltpu.VMEM)
    dma = pltpu.SemaphoreType.DMA
    lines = row_places([part.shape for part in smalls])[1]
    shapes = (
        (narrow_count, rows, width),
        (wide_count, block, columns),
        (block, width),
        (wide_count, narrow_count, lines, 128),
    )
    far = narrow_count - 1
    bucket = narrow_count * rows
    table = jax.ShapeDtypeStruct((bucket, HDIM), jnp.float32)
    reach = jax.ShapeDtypeStruct((bucket, 1), jnp.int32)
    return pl.pallas_call(
        functools.partial(gather_kernel, wide_count, narrow_count),
        out_shape=tuple(jax.ShapeDtypeStruct(shape, jnp.bfloat16) for shape in shapes[:3])
        + (
            jax.ShapeDtypeStruct(shapes[3], jnp.float32),
            jax.ShapeDtypeStruct((narrow_count, rows, columns), jnp.float32),
            table,
            table,
            reach,
            reach,
        ),
        in_specs=[anywhere] * 3 + [vmem] * 6 + [pl.BlockSpec(memory_space=pltpu.SMEM)] * 2 + [vmem],
        out_specs=(anywhere,) * 5 + (vmem,) * 4,
        scratch_shapes=[
            pltpu.VMEM((lines, 128), jnp.float32),
            pltpu.VMEM(shapes[0], jnp.bfloat16),
            pltpu.VMEM((narrow_count, rows, columns), jnp.float32),
        ]
        + [pltpu.VMEM(shape, jnp.bfloat16) for shape in shapes[1:3]]
        + [pltpu.VMEM(shapes[3], jnp.float32)]
        + [
            dma((2, narrow_count)),
            dma((narrow_count,)),
            dma((far, 3)),
            dma((narrow_count, 3)),
            dma((far,)),
            dma((narrow_count,)),
            dma((far,)),
            dma((narrow_count,)),
            dma((wide_count - 1,)),
            dma((wide_count,)),
            dma((5,)),
            dma((4,)),
            dma((3, wide_count, 2)),
            dma((wide_count, 2)),
            dma((2, narrow_count)),
        ],
        compiler_params=pltpu.CompilerParams(
            collective_id=5, has_side_effects=True, vmem_limit_bytes=kernel_memory
        ),
        cost_estimate=pl.CostEstimate(
            flops=80 * 10**9, bytes_accessed=200 * 2**20, transcendentals=0
        ),
        name="gather_front",
    )(layer_input, heads_weight, merge_weight, *smalls, joined, prefix, speeds)


def attention_forward_kernel(
    wide_count,
    narrow_count,
    places,
    triple,
    small,
    cosine,
    signed_sine,
    first_query,
    last_query,
    own,
    merge,
    queries,
    keys,
    values,
    probs,
    mixed_out,
    hidden,
    hidden_low,
    normed,
    inv_std,
    merge_out,
    rows_out,
    merge_mat,
    probs_held,
    values_turned,
    outbound,
    mixed,
    mixed_send,
    mixed_recv,
    local_sems,
    ring_send,
    ring_recv,
    own_sem,
    rows_all,
    rows_send,
    rows_recv,
    rows_sem,
    heads_full,
    vectors,
):
    line = LineExchange(narrow_count)
    ring_sems = (ring_send, ring_recv, None, None, None, None, own_sem)
    ring = PlaneExchange(wide_count, merge, merge_mat, merge_mat, None, None, ring_sems)
    rows_sems = (rows_send, rows_recv, None, None, None, None, rows_sem)
    rows_ring = PlaneExchange(wide_count, hidden_low, rows_all, rows_all, None, None, rows_sems)
    bucket, own_cols = queries.shape
    rows, width = own.shape
    heads = own_cols // HDIM
    scale = HDIM ** (-0.5)
    greet_plane(ring)
    line.greet(3)
    keep_own = ring.send_own()
    spread_small(heads_full, small, places[0], 0)
    spread_small(vectors, small, places[1], 0, 0)
    spread_small(vectors, small, places[2], 0, 1)
    spread_small(vectors, small, places[3], 0, 2)
    ring_steps = [functools.partial(ring.receive, step) for step in range(1, ring.far + 1)]

    def keep(head):
        return pltpu.make_async_copy(
            probs_held.at[head % 2], probs.at[head], local_sems.at[head % 2]
        )

    def mixed_copy(head, offset, where, sender):
        cols = pl.ds(pl.multiple_of(sender * own_cols + head * HDIM, HDIM), HDIM)
        return line.copy(
            outbound.at[where, :, pl.ds(head * HDIM, HDIM)],
            mixed.at[:, cols],
            mixed_send.at[offset - 1, head],
            mixed_recv.at[sender, head],
            where,
        )

    started = []
    for head in range(heads):
        cols = pl.ds(head * HDIM, HDIM)

        def turn(i, carry):
            here = pl.ds(pl.multiple_of(i * rows, rows), rows)
            for which, target in enumerate((queries, keys, values)):
                wanted = pl.ds(which * own_cols + head * HDIM, HDIM)
                begin = (which * narrow_count + line.mine) * own_cols + head * HDIM
                bias = heads_full[:, pl.ds(pl.multiple_of(begin, HDIM), HDIM)]
                part = triple[here, wanted] + bias
                if which < 2:
                    part = rotate_lanes(part, cosine[here], -signed_sine[here])
                else:
                    values_turned[:, here] = part.T.astype(jnp.bfloat16)
                target[here, cols] = part.astype(jnp.bfloat16)
            return carry

        lax.fori_loop(0, narrow_count, turn, 0)
        if head >= 2:
            keep(head - 2).wait()
        held = probs_held.at[head % 2]

        def chunk(i, carry):
            here = pl.ds(pl.multiple_of(i * rows, rows), rows)
            scores = dot(keys[:, cols], queries[here, cols], ((1,), (1,))) * scale
            token = i * rows + lax.broadcasted_iota(jnp.int32, (bucket, rows), 1)
            seen = (token >= first_query[...]) & (token <= last_query[...])
            scores = jnp.where(seen, scores, masked_value)
            expo = jnp.exp(scores - jnp.max(scores, axis=0, keepdims=True))
            weights = (expo * (1 / jnp.sum(expo, axis=0, keepdims=True))).astype(jnp.bfloat16)
            held[:, here] = weights
            mixed_part = dot(values_turned[...], weights, ((1,), (0,)))
            outbound[i, :, cols] = mixed_part.T.astype(jnp.bfloat16)
            return carry

        lax.fori_loop(0, narrow_count, chunk, 0)
        keep(head).start()
        for offset in range(1, narrow_count):
            copy = mixed_copy(head, offset, line.peer(offset), line.mine)
            copy.start()
            started.append(copy)
        if ring_steps and head >= heads - len(ring_steps):
            ring_steps.pop(0)()
    own_mixed = pltpu.make_async_copy(
        outbound.at[line.mine],
        mixed.at[:, pl.ds(pl.multiple_of(line.mine * own_cols, own_cols), own_cols)],
        local_sems.at[3],
    )
    own_mixed.start()
    own_mixed.wait()
    keep_own.wait()
    for step in ring_steps:
        step()
    for offset in range(ring.ring):
        ring.receive_mate(offset)
    keep_merge = pltpu.make_async_copy(merge_mat, merge_out, local_sems.at[2])
    keep_merge.start()
    for offset in range(1, narrow_count):
        for head in range(heads):
            mixed_copy(head, offset, line.peer(offset), line.peer(offset)).wait_recv()
    mixed_out[...] = mixed[...]

    def merge_cols(cols):
        hidden[:, cols] = (
            residual_scale * own[:, cols].astype(jnp.float32)
            + dot(mixed[...], merge_mat[:, :, cols].reshape(width, cols.size), ((1,), (0,)))
            + vectors[0:1, cols]
        )

    tiles(width, 256, merge_cols)

    def norm_rows(i, carry):
        some = pl.ds(pl.multiple_of(i * 16, 16), 16)
        result, centred, inverse = normalize(hidden[some], vectors[1:2], vectors[2:3])
        hidden[some] = result
        hidden_low[some] = result.astype(jnp.bfloat16)
        normed[some] = centred
        inv_std[some] = inverse
        return carry

    lax.fori_loop(0, rows // 16, norm_rows, 0, unroll=2)
    keep_rows = rows_ring.send_own()
    for step in range(1, rows_ring.far + 1):
        rows_ring.receive(step)
    for offset in range(rows_ring.ring):
        rows_ring.receive_mate(offset)
    keep_rows.wait()
    keep_rows = pltpu.make_async_copy(rows_all, rows_out, rows_sem)
    keep_rows.start()
    for head in range(max(heads - 2, 0), heads):
        keep(head).wait()
    for copy in started:
        copy.wait_send()
    ring.drain()
    rows_ring.drain()
    keep_merge.wait()
    keep_rows.wait()


def attention_forward(
    wide_count,
    narrow_count,
    places,
    triple,
    small,
    cosine,
    signed_sine,
    first_query,
    last_query,
    layer_input,
    merge_block,
):
    bucket, columns = triple.shape
    rows, width = layer_input.shape
    own_cols = columns // 3
    heads = own_cols // HDIM
    anywhere = pl.BlockSpec(memory_space=pl.ANY)
    vmem = pl.BlockSpec(memory_space=pltpu.VMEM)
    dma = pltpu.SemaphoreType.DMA

    def low_shape(*shape):
        return jax.ShapeDtypeStruct(shape, jnp.bfloat16)

    def wide_shape(*shape):
        return jax.ShapeDtypeStruct(shape, jnp.float32)

    return pl.pallas_call(
        functools.partial(attention_forward_kernel, wide_count, narrow_count, places),
        out_shape=(
            low_shape(bucket, own_cols),
            low_shape(bucket, own_cols),
            low_shape(bucket, own_cols),
            low_shape(heads, bucket, bucket),
            low_shape(rows, width),
            wide_shape(rows, width),
            low_shape(rows, width),
            wide_shape(rows, width),
            wide_shape(rows, 1),
            low_shape(wide_count, *merge_block.shape),
            low_shape(wide_count, rows, width),
        ),
        in_specs=[vmem] * 7 + [anywhere],
        out_specs=(vmem, vmem, vmem, anywhere) + (vmem,) * 5 + (anywhere,) * 2,
        scratch_shapes=[
            pltpu.VMEM((wide_count, *merge_block.shape), jnp.bfloat16),
            pltpu.VMEM((2, bucket, bucket), jnp.bfloat16),
            pltpu.VMEM((HDIM, bucket), jnp.bfloat16),
            pltpu.VMEM((narrow_count, rows, own_cols), jnp.bfloat16),
            pltpu.VMEM((rows, width), jnp.bfloat16),
            dma((narrow_count - 1, heads)),
            dma((narrow_count, heads)),
            dma((4,)),
            dma((3, wide_count, 2)),
            dma((wide_count, 2)),
            dma(()),
            pltpu.VMEM((wide_count, rows, width), jnp.bfloat16),
            dma((3, wide_count, 2)),
            dma((wide_count, 2)),
            dma(()),
            pltpu.VMEM((1, 3 * width), jnp.float32),
            pltpu.VMEM((3, width), jnp.float32),
        ],
        compiler_params=pltpu.CompilerParams(
            collective_id=6, has_side_effects=True, vmem_limit_bytes=kernel_memory
        ),
        cost_estimate=pl.CostEstimate(
            flops=60 * 10**9, bytes_accessed=200 * 2**20, transcendentals=0
        ),
        name="attention_forward",
    )(
        triple,
        small,
        cosine,
        signed_sine,
        first_query,
        last_query,
        layer_input,
        merge_block,
    )


def shards(
    layer_input,
    heads_weight,
    heads_bias,
    merge_weight,
    merge_bias,
    norm_gains,
    norm_shifts,
    expand_weight,
    expand_bias,
    reduce_weight,
    reduce_bias,
    joined,
    prefix,
    cotangent,
):
    tok_rows, model_width = layer_input.shape
    wide_count = lax.axis_size("wide")
    narrow_count = lax.axis_size("narrow")
    count = wide_count * narrow_count
    bucket_len = tok_rows * narrow_count
    own_heads = HEADS // narrow_count
    own_cols = own_heads * HDIM
    share = expand_weight.shape[2]
    narrow_index = lax.axis_index("narrow")
    smalls = (
        heads_bias.reshape(1, -1),
        merge_bias.reshape(1, -1),
        norm_gains,
        norm_shifts,
        expand_bias,
        reduce_bias.reshape(1, -1),
    )
    places = row_places([part.shape for part in smalls])[0]
    (
        rows_input,
        heads_mat,
        merge_block,
        small_all,
        triple,
        cosine,
        signed_sine,
        first_query,
        last_query,
    ) = gather_front(
        wide_count,
        narrow_count,
        layer_input,
        heads_weight,
        merge_weight,
        smalls,
        joined,
        prefix,
        jnp.asarray(rotary_speeds(HDIM)),
    )
    rows_input = rows_input.reshape(bucket_len, model_width)
    heads_mat = heads_mat.reshape(model_width, 3 * own_cols)
    triple = triple.reshape(bucket_len, 3 * own_cols)
    (
        queries,
        keys,
        values,
        probs_low,
        mixed,
        hidden,
        hidden_low,
        normed_one,
        inv_one,
        merge_full,
        rows_all,
    ) = attention_forward(
        wide_count,
        narrow_count,
        places,
        triple,
        small_all,
        cosine,
        signed_sine,
        first_query,
        last_query,
        layer_input,
        merge_block,
    )

    tile_rows = -share % 16
    padded = -(-share // 256) * 256
    expand_low = jnp.pad(expand_weight.transpose(1, 2, 0), ((0, 0), (0, tile_rows), (0, 0)))
    expand_low, _ = lax.optimization_barrier((expand_low, small_all))
    expand_full = lax.all_gather(expand_low, "narrow", axis=2, tiled=True)
    reduce_low = jnp.pad(reduce_weight, ((0, tile_rows), (0, 0)))
    (
        reduce_full,
        active,
        slope,
        gelu,
        layer_output,
        sum_two_grad,
        feed_grad,
        row_sums,
    ) = geglu_forward(
        wide_count,
        narrow_count,
        places,
        rows_all,
        expand_full,
        reduce_low,
        small_all,
        hidden,
        cotangent,
    )
    reduce_weight_gradient, expand_part, hidden_part, unit_sums = geglu_backward(
        wide_count,
        narrow_count,
        feed_grad,
        expand_full,
        reduce_full,
        slope,
        gelu,
        active,
        rows_all,
    )
    expand_weight_gradient = (
        lax.psum_scatter(expand_part, "narrow", scatter_dimension=2, tiled=True)[:, :share]
        .astype(jnp.float32)
        .transpose(2, 0, 1)
    )
    (
        triple_grad,
        merge_weight_gradient,
        heads_sums,
        merge_sums,
        sum_one_grad,
        norm_one_sums,
    ) = attention_backward(
        wide_count,
        narrow_count,
        places,
        sum_two_grad,
        hidden_part,
        normed_one,
        inv_one,
        small_all,
        merge_full.reshape(model_width, model_width),
        mixed,
        queries,
        keys,
        values,
        probs_low,
        cosine,
        signed_sine,
    )

    mine_narrow = (jnp.arange(narrow_count) == narrow_index).astype(jnp.float32)
    mine_wide = (jnp.arange(wide_count) == lax.axis_index("wide")).astype(jnp.float32)
    heads_sums = (heads_sums.reshape(3, 1, own_cols) * mine_narrow[None, :, None]).reshape(count, 1, -1)
    norm_sums = jnp.stack([norm_one_sums[0], row_sums[0], norm_one_sums[1], row_sums[1]])
    norm_sums = norm_sums.reshape(4, count, -1).transpose(1, 0, 2)
    expand_sums = unit_sums[:, :share].reshape(2, narrow_count, -1).transpose(1, 0, 2)[None]
    expand_sums = (expand_sums * mine_wide[:, None, None, None]).reshape(count, 2, -1)
    reduce_sums = row_sums[2].reshape(1, narrow_count, 1, -1)
    reduce_sums = jnp.broadcast_to(
        reduce_sums, (wide_count, narrow_count, 1, reduce_sums.shape[3])
    ).reshape(count, 1, -1)
    pieces = (heads_sums, merge_sums.reshape(count, 1, -1), norm_sums, expand_sums, reduce_sums)
    packed = []
    for piece in pieces:
        piece = jnp.pad(piece, ((0, 0), (0, 0), (0, -piece.shape[2] % 128)))
        packed.append(piece.reshape(count, -1, 128))
    packed = jnp.concatenate(packed, axis=1)
    packed = jnp.pad(packed, ((0, 0), (0, -packed.shape[1] % 8), (0, 0)))
    (
        input_gradient,
        heads_weight_gradient,
        heads_bias_gradient,
        merge_bias_gradient,
        gains_gradient,
        shifts_gradient,
        expand_bias_gradient,
        reduce_bias_gradient,
    ) = input_backward(
        wide_count,
        narrow_count,
        rows_input,
        triple_grad,
        heads_mat,
        packed.reshape(wide_count, narrow_count, -1, 128),
        sum_one_grad,
        (
            (1, heads_bias.size),
            (1, merge_bias.size),
            norm_gains.shape,
            norm_shifts.shape,
            expand_bias.shape,
            (1, reduce_bias.size),
        ),
    )
    return (
        layer_output,
        input_gradient,
        heads_weight_gradient,
        heads_bias_gradient[0],
        merge_weight_gradient,
        merge_bias_gradient[0],
        gains_gradient,
        shifts_gradient,
        expand_weight_gradient,
        expand_bias_gradient,
        reduce_weight_gradient[:share],
        reduce_bias_gradient[0],
    )


def solution(mesh):
    return jax.shard_map(
        shards,
        mesh=mesh,
        in_specs=(
            P(("wide", "narrow"), None),
            P(("wide", "narrow"), None),
            P(("wide", "narrow")),
            P(("wide", "narrow"), None),
            P(("wide", "narrow")),
            P(None, ("wide", "narrow")),
            P(None, ("wide", "narrow")),
            P("narrow", None, "wide"),
            P(None, ("wide", "narrow")),
            P("wide", "narrow"),
            P("narrow"),
            P("wide"),
            P("wide", None),
            P(("wide", "narrow"), None),
        ),
        out_specs=(
            P(("wide", "narrow"), None),
            P(("wide", "narrow"), None),
            P(("wide", "narrow"), None),
            P(("wide", "narrow")),
            P(("wide", "narrow"), None),
            P(("wide", "narrow")),
            P(None, ("wide", "narrow")),
            P(None, ("wide", "narrow")),
            P("narrow", None, "wide"),
            P(None, ("wide", "narrow")),
            P("wide", "narrow"),
            P("narrow"),
        ),
        check_vma=False,
    )
```

```python
import functools
import math

import jax
import jax.numpy as jnp
import numpy as np
from jax import lax
from jax.experimental import pallas as pl
from jax.experimental.pallas import tpu as pltpu
from jax.sharding import PartitionSpec as P

HEADS = 16
HDIM = 128


residual_scale = 48.0**0.5
norm_eps = 1e-05
masked_value = -1e30
kernel_memory = 60 * 2**20


def rotary_speeds(head_size):
    index = np.arange(head_size) % (head_size // 2)
    return (10000.0 ** (-2.0 * index / head_size)).astype(np.float32)[None]


def normalize(values, gain, shift):
    centre = jnp.mean(values, axis=-1, keepdims=True)
    centred = values - centre
    variance = jnp.mean(centred * centred, axis=-1, keepdims=True)
    inv_std = lax.rsqrt(variance + norm_eps)
    normed = centred * inv_std
    return (normed * gain + shift, normed, inv_std)


def normalize_back(upstream, normed, inv_std, gain):
    scaled = upstream * gain
    return inv_std * (
        scaled
        - jnp.mean(scaled, axis=-1, keepdims=True)
        - normed * jnp.mean(scaled * normed, axis=-1, keepdims=True)
    )


def dot(left, right, dims):
    return lax.dot_general(left, right, (dims, ((), ())), preferred_element_type=jnp.float32)


def low(values):
    return values.astype(jnp.bfloat16)


def row_places(shapes):
    places = []
    start = 0
    for first, size in shapes:
        places.append((start, first, size))
        start += first * -(-size // 128)
    return places, start + -start % 8


def small_piece(block, place, index):
    start, _, size = place
    rows = -(-size // 128)
    pieces = []
    for row in range(rows):
        stop = min(size - 128 * row, 128)
        here = start + index * rows + row
        pieces.append(block[here : here + 1, 0:stop])
    return pieces


def spread_small(target, small, place, index, row=0):
    at = 0
    for wide in range(small.shape[0]):
        for narrow in range(small.shape[1]):
            for piece in small_piece(small.at[wide, narrow], place, index):
                target[row : row + 1, at : at + piece.shape[1]] = piece
                at += piece.shape[1]


def ring_place(wide_count):
    ring = wide_count // 2
    mine = lax.axis_index("wide")
    chip = mine // 2
    core = mine % 2
    position = 2 * (chip // 2) + (chip % 2 + chip // 2) % 2
    return ring, position, core


def chip_at(position, ring):
    position = (position + 2 * ring) % ring
    return 2 * (position // 2) + (position + position // 2) % 2


class PlaneExchange:
    def __init__(self, wide_count, own, blocks, parts, from_mate, incoming, sems, cols=None):
        self.ring, self.position, self.core = ring_place(wide_count)
        self.own, self.blocks, self.parts = own, blocks, parts
        self.from_mate, self.incoming = from_mate, incoming
        (
            self.gather_send,
            self.gather_recv,
            self.mate_send,
            self.mate_recv,
            self.sum_send,
            self.sum_recv,
            self.own_sem,
        ) = sems
        self.half = parts.shape[1] // 2
        self.cols = slice(None) if cols is None else cols
        self.far = self.ring // 2
        self.started = []

    def device(self, offset, mate=False):
        core = 1 - self.core if mate else self.core
        return {"wide": 2 * chip_at(self.position + offset, self.ring) + core}

    def slot(self, offset, mate=False):
        core = 1 - self.core if mate else self.core
        return 2 * chip_at(self.position + offset, self.ring) + core

    def rows(self, part):
        return pl.ds(part * self.half, self.half)

    def greet(self):
        barrier = pltpu.get_barrier_semaphore()
        for where in (self.device(-1), self.device(1), self.device(0, True)):
            pl.semaphore_signal(
                barrier, inc=1, device_id=where, device_id_type=pl.DeviceIdType.MESH
            )
        pl.semaphore_wait(barrier, 3)

    def start(self, source, target, send_sem, recv_sem, where):
        copy = pltpu.make_async_remote_copy(
            src_ref=source,
            dst_ref=target,
            send_sem=send_sem,
            recv_sem=recv_sem,
            device_id=where,
            device_id_type=pl.DeviceIdType.MESH,
        )
        copy.start()
        self.started.append(copy)

    def pass_on(self, lane, slot, part, where, source=None):
        target = self.blocks.at[slot, self.rows(part)]
        self.start(
            target if source is None else source,
            target,
            self.gather_send.at[lane, slot, part],
            self.gather_recv.at[slot, part],
            where,
        )

    def arrived(self, slot, part):
        target = self.blocks.at[slot, self.rows(part)]
        pltpu.make_async_remote_copy(
            src_ref=target,
            dst_ref=target,
            send_sem=self.gather_send.at[0, slot, part],
            recv_sem=self.gather_recv.at[slot, part],
            device_id=self.device(1),
            device_id_type=pl.DeviceIdType.MESH,
        ).wait_recv()

    def send_own(self):
        slot = self.slot(0)
        keep = None
        own = self.blocks.at[slot]
        if self.own is not None:
            own = self.own
            keep = pltpu.make_async_copy(own, self.blocks.at[slot], self.own_sem)
            keep.start()
        first, second = own.at[self.rows(0)], own.at[self.rows(1)]
        self.pass_on(0, slot, 0, self.device(1), first)
        self.pass_on(1, slot, 1, self.device(-1), second)
        self.pass_on(2, slot, 0, self.device(0, True), first)
        self.pass_on(2, slot, 1, self.device(0, True), second)
        self.pass_on(0, slot, 1, self.device(1), second)
        self.pass_on(1, slot, 0, self.device(-1), first)
        return keep

    def receive(self, distance):
        mate = self.device(0, True)
        left, right = self.slot(-distance), self.slot(distance)
        if distance == self.far:
            for part in range(2):
                self.arrived(left, part)
                self.pass_on(2, left, part, mate)
            return
        further = distance < self.far - 1
        self.arrived(left, 0)
        self.pass_on(0, left, 0, self.device(1))
        self.pass_on(2, left, 0, mate)
        self.arrived(right, 1)
        self.pass_on(1, right, 1, self.device(-1))
        self.pass_on(2, right, 1, mate)
        self.arrived(left, 1)
        if further:
            self.pass_on(0, left, 1, self.device(1))
        self.pass_on(2, left, 1, mate)
        self.arrived(right, 0)
        if further:
            self.pass_on(1, right, 0, self.device(-1))
        self.pass_on(2, right, 0, mate)

    def receive_mate(self, offset):
        for part in range(2):
            self.arrived(self.slot(offset, True), part)

    def share(self, offset):
        chip = chip_at(self.position + offset, self.ring)
        self.start(
            self.parts.at[self.slot(offset, True), :, self.cols],
            self.from_mate.at[chip, :, self.cols],
            self.mate_send.at[chip],
            self.mate_recv.at[chip],
            self.device(0, True),
        )

    def shared(self, offset):
        chip = chip_at(self.position + offset, self.ring)
        pltpu.make_async_remote_copy(
            src_ref=self.parts.at[self.slot(offset), :, self.cols],
            dst_ref=self.from_mate.at[chip, :, self.cols],
            send_sem=self.mate_send.at[chip],
            recv_sem=self.mate_recv.at[chip],
            device_id=self.device(0, True),
            device_id_type=pl.DeviceIdType.MESH,
        ).wait_recv()

    def chip_sum(self, offset, rows):
        chip = chip_at(self.position + offset, self.ring)
        return self.parts[self.slot(offset), rows, self.cols].astype(
            jnp.float32
        ) + self.from_mate[chip, rows, self.cols].astype(jnp.float32)

    def send_sum(self, way, distance, part):
        offset = distance if way == 0 else -distance
        begins = self.far if part == way else self.far - 1
        slot = self.slot(offset)
        if distance < begins:
            self.sum_arrived(way, distance, part)

        def chunk(i, carry):
            here = pl.ds(pl.multiple_of(i * 16, 16), 16)
            there = pl.ds(pl.multiple_of(part * self.half + i * 16, 16), 16)
            total = self.chip_sum(offset, there)
            if distance < begins:
                total += self.incoming[way, distance, part, here, self.cols].astype(jnp.float32)
            self.parts[slot, there, self.cols] = total.astype(jnp.bfloat16)
            return carry

        lax.fori_loop(0, self.half // 16, chunk, 0, unroll=2)
        self.start(
            self.parts.at[slot, self.rows(part), self.cols],
            self.incoming.at[way, distance - 1, part, :, self.cols],
            self.sum_send.at[way, distance - 1, part],
            self.sum_recv.at[way, distance - 1, part],
            self.device(1 if way == 0 else -1),
        )

    def sum_arrived(self, way, distance, part):
        target = self.incoming.at[way, distance, part, :, self.cols]
        pltpu.make_async_remote_copy(
            src_ref=target,
            dst_ref=target,
            send_sem=self.sum_send.at[way, distance, part],
            recv_sem=self.sum_recv.at[way, distance, part],
            device_id=self.device(1),
            device_id_type=pl.DeviceIdType.MESH,
        ).wait_recv()

    def run(self, first, second, before, after_far):
        def compute(chip):
            first(chip)
            second(chip)

        keep = self.send_own()
        keep.wait()
        self.receive_mate(0)
        compute(chip_at(self.position, self.ring))
        self.share(0)
        for distance in range(1, self.far):
            self.receive(distance)
            for offset in (-distance, distance):
                self.receive_mate(offset)
                compute(chip_at(self.position + offset, self.ring))
                self.share(offset)
            if distance == self.far - 1:
                self.first_sums()
        self.receive(self.far)
        self.receive_mate(self.far)
        farthest = chip_at(self.position + self.far, self.ring)
        first(farthest)
        before()
        second(farthest)
        self.share(self.far)
        self.far_sums()
        after_far()
        self.last_sums()

    def start_sums(self, compute):
        compute(chip_at(self.position + self.far, self.ring))
        self.share(self.far)
        for distance in range(self.far - 1, 0, -1):
            for offset in (-distance, distance):
                compute(chip_at(self.position + offset, self.ring))
                self.share(offset)
            if distance == self.far - 1:
                self.far_sums()
                self.first_sums()
        compute(chip_at(self.position, self.ring))
        self.share(0)

    def first_sums(self):
        distance = self.far - 1
        self.shared(distance)
        self.send_sum(0, distance, 1)
        self.shared(-distance)
        self.send_sum(1, distance, 0)

    def far_sums(self):
        self.shared(self.far)
        self.send_sum(0, self.far, 0)
        self.send_sum(1, self.far, 1)

    def last_sums(self):
        for distance in range(self.far - 1, 0, -1):
            if distance < self.far - 1:
                self.shared(distance)
                self.shared(-distance)
            self.send_sum(0, distance, 0)
            self.send_sum(1, distance, 1)
            if distance < self.far - 1:
                self.send_sum(0, distance, 1)
                self.send_sum(1, distance, 0)

    def finish(self, result):
        self.shared(0)
        for part in range(2):
            for way in range(2):
                self.sum_arrived(way, 0, part)

            def chunk(i, carry):
                here = pl.ds(pl.multiple_of(i * 16, 16), 16)
                there = pl.ds(pl.multiple_of(part * self.half + i * 16, 16), 16)
                total = self.chip_sum(0, there)
                for way in range(2):
                    total += self.incoming[way, 0, part, here, self.cols].astype(jnp.float32)
                result[there, self.cols] = total.astype(result.dtype)
                return carry

            lax.fori_loop(0, self.half // 16, chunk, 0, unroll=2)

    def drain(self):
        for copy in self.started:
            copy.wait_send()


def sum_scratch(wide_count, rows, width):
    ring = wide_count // 2
    far = ring // 2
    dma = pltpu.SemaphoreType.DMA
    return [
        pltpu.VMEM((wide_count, rows, width), jnp.bfloat16),
        pltpu.VMEM((ring, rows, width), jnp.bfloat16),
        pltpu.VMEM((2, far, 2, rows // 2, width), jnp.bfloat16),
        dma((ring,)),
        dma((ring,)),
        dma((2, far, 2)),
        dma((2, far, 2)),
    ]


def exchange_scratch(wide_count, rows, width):
    dma = pltpu.SemaphoreType.DMA
    return [
        pltpu.VMEM((wide_count, rows, width), jnp.bfloat16),
        dma((3, wide_count, 2)),
        dma((wide_count, 2)),
        dma(()),
    ] + sum_scratch(wide_count, rows, width)


def load_padded(source, target, sem):
    filled = source.shape[0]
    copy = pltpu.make_async_copy(source, target.at[pl.ds(0, filled)], sem)
    copy.start()
    if filled < target.shape[0]:
        target[pl.ds(filled, target.shape[0] - filled)] = jnp.zeros(
            (target.shape[0] - filled, target.shape[1]), target.dtype
        )
    return copy


def pair_rows(ref, chip):
    block = ref[pl.ds(2 * chip, 2)]
    return block.reshape(2 * block.shape[1], block.shape[2])


def set_pair(ref, chip, cols, value):
    rows = ref.shape[1]
    ref[2 * chip, :, cols] = value[:rows].astype(ref.dtype)
    ref[2 * chip + 1, :, cols] = value[rows:].astype(ref.dtype)


def tiles(count, tile, body, start=0):
    def step(i, carry):
        body(pl.ds(pl.multiple_of(start + i * tile, tile), tile))
        return carry

    lax.fori_loop(0, count // tile, step, 0)


class LineExchange:
    def __init__(self, narrow_count):
        self.count = narrow_count
        self.mine = lax.axis_index("narrow")
        self.started = []

    def peer(self, offset):
        return (self.mine + offset) % self.count

    def greet(self, extra=0):
        barrier = pltpu.get_barrier_semaphore()
        for offset in range(1, self.count):
            pl.semaphore_signal(
                barrier,
                inc=1,
                device_id={"narrow": self.peer(offset)},
                device_id_type=pl.DeviceIdType.MESH,
            )
        pl.semaphore_wait(barrier, self.count - 1 + extra)

    def copy(self, source, target, send_sem, recv_sem, where):
        return pltpu.make_async_remote_copy(
            src_ref=source,
            dst_ref=target,
            send_sem=send_sem,
            recv_sem=recv_sem,
            device_id={"narrow": where},
            device_id_type=pl.DeviceIdType.MESH,
        )

    def send(self, offset, source, landing, send_sems, recv_sems):
        peer = self.peer(offset)
        copy = self.copy(
            source, landing.at[self.mine], send_sems.at[offset - 1], recv_sems.at[self.mine], peer
        )
        copy.start()
        self.started.append(copy)

    def arrived(self, offset, landing, send_sems, recv_sems):
        peer = self.peer(offset)
        self.copy(
            landing.at[peer], landing.at[peer], send_sems.at[offset - 1], recv_sems.at[peer], peer
        ).wait_recv()

    def drain(self):
        for copy in self.started:
            copy.wait_send()


class LineSum:
    def __init__(self, line, view, landing, send_sems, recv_sems):
        self.line, self.view, self.landing = line, view, landing
        self.send_sems, self.recv_sems = send_sems, recv_sems
        self.last = line.count - 1

    def reaches(self, way, offset):
        here = self.line.mine
        return here + offset <= self.last if way == 0 else here - offset >= 0

    def follows(self, way):
        here = self.line.mine
        return here > 0 if way == 0 else here < self.last

    def target(self, way, offset):
        return self.line.mine + offset if way == 0 else self.line.mine - offset

    def copy(self, way, offset):
        return self.line.copy(
            self.view(self.target(way, offset)),
            self.landing.at[way, offset - 1],
            self.send_sems.at[way, offset - 1],
            self.recv_sems.at[way, offset - 1],
            self.line.mine + 1 if way == 0 else self.line.mine - 1,
        )

    def arrived(self, way, offset):
        landing = self.landing.at[way, offset]
        self.line.copy(
            landing,
            landing,
            self.send_sems.at[way, offset],
            self.recv_sems.at[way, offset],
            self.line.mine,
        ).wait_recv()

    def add(self, way, offset):
        held = self.view(self.target(way, offset))

        def chunk(i, carry):
            some = pl.ds(pl.multiple_of(i * 16, 16), 16)
            held[some] = (
                held[some].astype(jnp.float32)
                + self.landing[way, offset, some].astype(jnp.float32)
            ).astype(jnp.bfloat16)
            return carry

        lax.fori_loop(0, self.landing.shape[2] // 16, chunk, 0, unroll=2)

    def begin(self, offset):
        for way in range(2):

            @pl.when(self.reaches(way, offset) & jnp.logical_not(self.follows(way)))
            def _():
                self.copy(way, offset).start()

    def step(self, offset):
        for way in range(2):

            @pl.when(self.reaches(way, offset) & self.follows(way))
            def _():
                self.arrived(way, offset)
                self.add(way, offset)
                self.copy(way, offset).start()

    def finish(self, result):
        held = self.view(self.line.mine)
        count = self.landing.shape[2] // 16

        def begin(i, carry):
            some = pl.ds(pl.multiple_of(i * 16, 16), 16)
            result[some] = held[some].astype(result.dtype)
            return carry

        lax.fori_loop(0, count, begin, 0, unroll=2)
        for way in range(2):

            @pl.when(self.follows(way))
            def _():
                self.arrived(way, 0)

                def chunk(i, carry):
                    some = pl.ds(pl.multiple_of(i * 16, 16), 16)
                    result[some] += self.landing[way, 0, some].astype(result.dtype)
                    return carry

                lax.fori_loop(0, count, chunk, 0, unroll=2)

    def drain(self):
        for offset in range(1, self.last + 1):
            for way in range(2):

                @pl.when(self.reaches(way, offset))
                def _():
                    self.copy(way, offset).wait_send()


class LineGather:
    def __init__(self, line, view, send_sems, recv_sems):
        self.line, self.view = line, view
        self.send_sems, self.recv_sems = send_sems, recv_sems
        self.last = line.count - 1

    def copy(self, way, block):
        target = self.view(block)
        here = self.line.mine
        return self.line.copy(
            target,
            target,
            self.send_sems.at[way, block],
            self.recv_sems.at[block],
            here + 1 if way == 0 else here - 1,
        )

    def goes(self, way):
        return self.line.mine < self.last if way == 0 else self.line.mine > 0

    def has(self, way, step):
        here = self.line.mine
        return here - step >= 0 if way == 0 else here + step <= self.last

    def block(self, way, step):
        return self.line.mine - step if way == 0 else self.line.mine + step

    def send_own(self):
        for way in range(2):

            @pl.when(self.goes(way))
            def _():
                self.copy(way, self.line.mine).start()

    def step(self, step):
        for way in range(2):

            @pl.when(self.has(way, step))
            def _():
                self.copy(way, self.block(way, step)).wait_recv()

                @pl.when(self.goes(way))
                def _():
                    self.copy(way, self.block(way, step)).start()

    def each(self, step, body):
        for way in range(2):

            @pl.when(self.has(way, step))
            def _():
                body(self.block(way, step))

    def drain(self):
        for way in range(2):
            for step in range(self.last + 1):

                @pl.when(self.has(way, step) & self.goes(way))
                def _():
                    self.copy(way, self.block(way, step)).wait_send()


def greet_plane(plane):
    barrier = pltpu.get_barrier_semaphore()
    for where in (plane.device(-1), plane.device(1), plane.device(0, True)):
        pl.semaphore_signal(barrier, inc=1, device_id=where, device_id_type=pl.DeviceIdType.MESH)


def geglu_forward_kernel(
    wide_count,
    narrow_count,
    places,
    rows_all,
    expand,
    reduce,
    small,
    hidden,
    cotangent,
    reduce_out,
    active_out,
    slope_out,
    gelu_out,
    layer_output,
    sum_grad,
    feed_grad,
    row_sums,
    feed,
    blocks,
    parts,
    from_mate,
    incoming,
    mate_send,
    mate_recv,
    sum_send,
    sum_recv,
    expand_mat,
    reduce_mat,
    active,
    slope,
    gelu,
    load_sems,
    keep_sems,
    reduce_send,
    reduce_recv,
    next_mate_send,
    next_mate_recv,
    next_sum_send,
    next_sum_recv,
    late_mate_send,
    late_mate_recv,
    late_sum_send,
    late_sum_recv,
    shift,
    vectors,
):
    line = LineExchange(narrow_count)
    filled, cols = reduce.shape
    width = rows_all.shape[2]
    upper = (2 * line.mine) // narrow_count
    half = narrow_count // 2
    windows = (
        (half * upper, half, half - 1),
        (half - upper * (half - 1), half - 1, narrow_count - 2),
        ((narrow_count - 1) * (1 - upper), 1, narrow_count - 1),
    )
    sems = (
        (mate_send, mate_recv, sum_send, sum_recv),
        (next_mate_send, next_mate_recv, next_sum_send, next_sum_recv),
        (late_mate_send, late_mate_recv, late_sum_send, late_sum_recv),
    )
    planes = [
        PlaneExchange(
            wide_count,
            None,
            None,
            parts,
            from_mate,
            incoming,
            (None, None, *own_sems, None),
            pl.ds(pl.multiple_of(first * cols, cols), blocks_in * cols),
        )
        for (first, blocks_in, _), own_sems in zip(windows, sems)
    ]
    plane = planes[0]
    loads = [
        load_padded(expand.at[0], expand_mat.at[0], load_sems.at[0]),
        load_padded(expand.at[1], expand_mat.at[1], load_sems.at[1]),
        pltpu.make_async_copy(rows_all, blocks, load_sems.at[4]),
    ]
    loads[2].start()

    def reduce_cols(block):
        return reduce_mat.at[
            pl.ds(0, filled), pl.ds(pl.multiple_of(block * cols, cols), cols)
        ]

    line_reduce = LineGather(line, reduce_cols, reduce_send, reduce_recv)
    own_reduce = pltpu.make_async_copy(reduce, reduce_cols(line.mine), load_sems.at[2])
    own_reduce.start()
    if filled < reduce_mat.shape[0]:
        reduce_mat[filled:] = jnp.zeros(
            (reduce_mat.shape[0] - filled, reduce_mat.shape[1]), reduce_mat.dtype
        )
    greet_plane(plane)
    line.greet(3)
    place = lax.axis_index("wide")
    shift[...] = jnp.zeros_like(shift)
    for index in range(2):
        at = 0
        for block in range(narrow_count):
            for piece in small_piece(small.at[place, block], places[4], index):
                shift[index : index + 1, at : at + piece.shape[1]] = piece
                at += piece.shape[1]
    at = 0
    for block in range(narrow_count):
        for piece in small_piece(small.at[0, block], places[5], 0):
            vectors[0:1, at : at + piece.shape[1]] = piece
            at += piece.shape[1]
    spread_small(vectors, small, places[2], 1, 1)
    spread_small(vectors, small, places[3], 1, 2)
    own_reduce.wait()
    line_reduce.send_own()
    kept = []
    waiting = list(loads)

    def compute(chip):
        while waiting:
            waiting.pop().wait()

        def units(cols):
            rows = pair_rows(blocks, chip)
            gate = dot(rows, expand_mat[0, cols], ((1,), (1,))) + shift[0:1, cols]
            upper = dot(rows, expand_mat[1, cols], ((1,), (1,))) + shift[1:2, cols]
            factor = math.sqrt(2 / math.pi)
            square = gate * gate
            bend = jnp.tanh(factor * gate * (1 + 0.044715 * square))
            value = 0.5 * gate * (1 + bend)
            pull = 0.5 * (1 + bend) + 0.5 * gate * (1 - bend * bend) * factor * (
                1 + 3 * 0.044715 * square
            )
            set_pair(active, chip, cols, value * upper)
            set_pair(slope, chip, cols, pull * upper)
            set_pair(gelu, chip, cols, value)

        tiles(active.shape[2], 256, units)

        pair = pl.ds(2 * chip, 2)
        for index, (source, target) in enumerate(
            ((active, active_out), (slope, slope_out), (gelu, gelu_out))
        ):
            copy = pltpu.make_async_copy(
                source.at[pair], target.at[pair], keep_sems.at[chip, index]
            )
            copy.start()
            kept.append(copy)

    def compute_sums(start, count):
        def compute(chip):
            def outputs(some):
                part = dot(pair_rows(active, chip), reduce_mat[:, some], ((1,), (0,)))
                set_pair(parts, chip, some, part)

            tiles(count, 256, outputs, start)

        return compute

    offsets = [0]
    for distance in range(1, plane.far):
        offsets += [-distance, distance]
    offsets.append(plane.far)
    chips = [chip_at(plane.position + offset, plane.ring) for offset in offsets]
    for index, chip in enumerate(chips):
        if index == len(chips) - 1:
            line_reduce.step(1)
        compute(chip)
    step = 1
    for window, (first, blocks_in, needed) in enumerate(windows):
        while step < needed:
            step += 1
            line_reduce.step(step)
        start = pl.multiple_of(first * cols, cols)
        planes[window].start_sums(compute_sums(start, blocks_in * cols))
        if window > 0:
            planes[window - 1].last_sums()
    planes[-1].last_sums()
    keep_reduce = pltpu.make_async_copy(
        reduce_mat.at[pl.ds(0, filled)], reduce_out, load_sems.at[3]
    )
    keep_reduce.start()
    for part in planes:
        part.finish(feed)

    row_sums[...] = jnp.zeros_like(row_sums)

    def norm_rows(i, carry):
        some = pl.ds(pl.multiple_of(i * 16, 16), 16)
        result, normed, inverse = normalize(
            residual_scale * hidden[some] + feed[some] + vectors[0:1],
            vectors[1:2],
            vectors[2:3],
        )
        layer_output[some] = result.astype(jnp.bfloat16)
        upstream = cotangent[some].astype(jnp.float32)
        total = normalize_back(upstream, normed, inverse, vectors[1:2])
        sum_grad[some] = total
        feed_grad[some] = total.astype(jnp.bfloat16)
        row_sums[0:1] += jnp.sum(upstream * normed, axis=0, keepdims=True)
        row_sums[1:2] += jnp.sum(upstream, axis=0, keepdims=True)
        row_sums[2:3] += jnp.sum(total, axis=0, keepdims=True)
        return carry

    lax.fori_loop(0, rows_all.shape[1] // 16, norm_rows, 0, unroll=2)
    for part in planes:
        part.drain()
    keep_reduce.wait()
    line_reduce.drain()
    for copy in kept:
        copy.wait()


def geglu_forward(
    wide_count,
    narrow_count,
    places,
    rows_all,
    expand,
    reduce_weight,
    small,
    hidden,
    cotangent,
):
    _, rows, width = rows_all.shape
    padded = -(-expand.shape[1] // 256) * 256
    anywhere = pl.BlockSpec(memory_space=pl.ANY)
    vmem = pl.BlockSpec(memory_space=pltpu.VMEM)
    kept = jax.ShapeDtypeStruct((wide_count, rows, padded), jnp.bfloat16)
    scratch = [pltpu.VMEM((rows, width), jnp.float32)]
    scratch.append(pltpu.VMEM((wide_count, rows, width), jnp.bfloat16))
    scratch += sum_scratch(wide_count, rows, width) + [
        pltpu.VMEM((2, padded, width), jnp.bfloat16),
        pltpu.VMEM((padded, width), jnp.bfloat16),
        pltpu.VMEM((wide_count, rows, padded), jnp.bfloat16),
        pltpu.VMEM((wide_count, rows, padded), jnp.bfloat16),
        pltpu.VMEM((wide_count, rows, padded), jnp.bfloat16),
        pltpu.SemaphoreType.DMA((5,)),
        pltpu.SemaphoreType.DMA((wide_count // 2, 3)),
        pltpu.SemaphoreType.DMA((2, narrow_count)),
        pltpu.SemaphoreType.DMA((narrow_count,)),
    ] + 2 * sum_scratch(wide_count, rows, width)[3:]
    scratch += [pltpu.VMEM((2, padded), jnp.float32), pltpu.VMEM((3, width), jnp.float32)]
    return pl.pallas_call(
        functools.partial(geglu_forward_kernel, wide_count, narrow_count, places),
        out_shape=(
            jax.ShapeDtypeStruct((reduce_weight.shape[0], width), jnp.bfloat16),
            kept,
            kept,
            kept,
            jax.ShapeDtypeStruct((rows, width), jnp.bfloat16),
            jax.ShapeDtypeStruct((rows, width), jnp.float32),
            jax.ShapeDtypeStruct((rows, width), jnp.bfloat16),
            jax.ShapeDtypeStruct((3, width), jnp.float32),
        ),
        in_specs=[anywhere] * 3 + [vmem] * 3,
        out_specs=(anywhere,) * 4 + (vmem,) * 4,
        scratch_shapes=scratch,
        compiler_params=pltpu.CompilerParams(
            collective_id=1, has_side_effects=True, vmem_limit_bytes=kernel_memory
        ),
        cost_estimate=pl.CostEstimate(
            flops=6 * wide_count * rows * padded * width, bytes_accessed=200 * 2**20, transcendentals=0
        ),
        name="geglu_forward",
    )(
        rows_all,
        expand,
        reduce_weight,
        small,
        hidden,
        cotangent,
    )


def geglu_backward_kernel(
    wide_count,
    narrow_count,
    own,
    expand,
    reduce,
    slope_in,
    gelu_in,
    active_in,
    rows_in,
    reduce_grad,
    expand_part,
    hidden_grad,
    unit_sums,
    blocks,
    gather_send,
    gather_recv,
    own_sem,
    parts,
    from_mate,
    incoming,
    mate_send,
    mate_recv,
    sum_send,
    sum_recv,
    expand_mat,
    reduce_mat,
    slope,
    gelu,
    active,
    rows_all,
    staged,
    load_sems,
    keep_sems,
    line_in,
    line_send,
    line_recv,
):
    sems = (gather_send, gather_recv, mate_send, mate_recv, sum_send, sum_recv, own_sem)
    plane = PlaneExchange(wide_count, own, blocks, parts, from_mate, incoming, sems)
    loads = [
        load_padded(expand.at[0], expand_mat.at[0], load_sems.at[0]),
        load_padded(expand.at[1], expand_mat.at[1], load_sems.at[1]),
        load_padded(reduce, reduce_mat, load_sems.at[2]),
        pltpu.make_async_copy(slope_in, slope, load_sems.at[3]),
        pltpu.make_async_copy(gelu_in, gelu, load_sems.at[4]),
    ]
    late_loads = [
        pltpu.make_async_copy(active_in, active, load_sems.at[5]),
        pltpu.make_async_copy(rows_in, rows_all, load_sems.at[6]),
    ]
    for copy in loads[3:]:
        copy.start()
    unit_sums[...] = jnp.zeros_like(unit_sums)
    line = LineExchange(narrow_count)
    filled, line_cols = line_in.shape[2:]

    def line_part(block):
        return reduce_mat.at[
            pl.ds(0, filled), pl.ds(pl.multiple_of(block * line_cols, line_cols), line_cols)
        ]

    line_sum = LineSum(line, line_part, line_in, line_send, line_recv)
    greet_plane(plane)
    line.greet(3)
    for copy in late_loads:
        copy.start()
    kept = []
    waiting = list(loads)

    def compute(chip):
        while waiting:
            waiting.pop().wait()

        def units(cols):
            pulled = dot(pair_rows(blocks, chip), reduce_mat[cols], ((1,), (1,)))
            pair = pl.ds(2 * chip, 2)
            shape = pulled.shape
            gate_grad = pulled * slope[pair, :, cols].reshape(shape).astype(jnp.float32)
            upper_grad = pulled * gelu[pair, :, cols].reshape(shape).astype(jnp.float32)
            set_pair(slope, chip, cols, gate_grad)
            set_pair(gelu, chip, cols, upper_grad)
            unit_sums[0:1, cols] += jnp.sum(gate_grad, axis=0, keepdims=True)
            unit_sums[1:2, cols] += jnp.sum(upper_grad, axis=0, keepdims=True)

        tiles(slope.shape[2], 256, units)

    def compute_sums(chip):
        def outputs(cols):
            set_pair(
                parts,
                chip,
                cols,
                dot(pair_rows(slope, chip), expand_mat[0, :, cols], ((1,), (0,)))
                + dot(pair_rows(gelu, chip), expand_mat[1, :, cols], ((1,), (0,))),
            )

        tiles(parts.shape[2], 256, outputs)

    def product(left, right, start):
        tokens = left.shape[0] * left.shape[1]
        return dot(
            left[:, :, start : start + 256].reshape(tokens, 256),
            right[...].reshape(tokens, right.shape[2]),
            ((0,), (0,)),
        ).astype(jnp.bfloat16)

    def reduce_work():
        for copy in late_loads:
            copy.wait()

        def reduce_cols(index):
            cols = pl.ds(pl.multiple_of(index * line_cols, line_cols), line_cols)

            def units(some):
                tokens = active.shape[0] * active.shape[1]
                part = dot(
                    active[:, :, some].reshape(tokens, some.size),
                    blocks[:, :, cols].reshape(tokens, line_cols),
                    ((0,), (0,)),
                )
                reduce_mat[some, cols] = part.astype(jnp.bfloat16)

            tiles(active.shape[2], 256, units)

        for offset in range(narrow_count - 1, 0, -1):
            for way in range(2):

                @pl.when(line_sum.reaches(way, offset))
                def _():
                    reduce_cols(line_sum.target(way, offset))

            line_sum.begin(offset)
        reduce_cols(line.mine)

    def expand_work(left, start, target):
        def work():
            index = len(kept)
            if index >= 2:
                kept[index - 2].wait()
            staged[index % 2] = product(left, rows_all, start)
            stop = min(256, target.shape[0] - start)
            copy = pltpu.make_async_copy(
                staged.at[index % 2, pl.ds(0, stop)],
                target.at[pl.ds(start, stop)],
                keep_sems.at[index % 2],
            )
            copy.start()
            kept.append(copy)

        return work

    works = [
        expand_work(left, start, target)
        for left, target in ((slope, expand_part.at[0]), (gelu, expand_part.at[1]))
        for start in range(0, target.shape[0], 256)
    ]
    steps = [
        functools.partial(line_sum.step, offset) for offset in range(narrow_count - 2, 0, -1)
    ]
    third = len(works) // 3
    middle = (len(steps) + 1) // 2

    def many(calls):
        for call in calls:
            call()

    beside = functools.partial(many, steps[:middle] + works[:third])
    plane.run(compute, compute_sums, reduce_work, beside)
    many(works[third : 2 * third] + steps[middle:] + works[2 * third :])
    plane.finish(hidden_grad)
    plane.drain()
    line_sum.finish(reduce_grad)
    line_sum.drain()
    for copy in kept[-2:]:
        copy.wait()


def geglu_backward(
    wide_count,
    narrow_count,
    feed_grad,
    expand,
    reduce_full,
    slope,
    gelu,
    active,
    rows_all,
):
    rows, width = feed_grad.shape
    padded = slope.shape[2]
    anywhere = pl.BlockSpec(memory_space=pl.ANY)
    vmem = pl.BlockSpec(memory_space=pltpu.VMEM)
    scratch = exchange_scratch(wide_count, rows, width) + [
        pltpu.VMEM((2, padded, width), jnp.bfloat16),
        pltpu.VMEM((padded, width), jnp.bfloat16),
        pltpu.VMEM((wide_count, rows, padded), jnp.bfloat16),
        pltpu.VMEM((wide_count, rows, padded), jnp.bfloat16),
        pltpu.VMEM((wide_count, rows, padded), jnp.bfloat16),
        pltpu.VMEM((wide_count, rows, width), jnp.bfloat16),
        pltpu.VMEM((2, 256, width), jnp.bfloat16),
        pltpu.SemaphoreType.DMA((7,)),
        pltpu.SemaphoreType.DMA((2,)),
        pltpu.VMEM(
            (2, narrow_count - 1, reduce_full.shape[0], width // narrow_count), jnp.bfloat16
        ),
        pltpu.SemaphoreType.DMA((2, narrow_count - 1)),
        pltpu.SemaphoreType.DMA((2, narrow_count - 1)),
    ]
    return pl.pallas_call(
        functools.partial(geglu_backward_kernel, wide_count, narrow_count),
        out_shape=(
            jax.ShapeDtypeStruct(
                (reduce_full.shape[0], width // narrow_count), jnp.float32
            ),
            jax.ShapeDtypeStruct(expand.shape, jnp.bfloat16),
            jax.ShapeDtypeStruct((rows, width), jnp.float32),
            jax.ShapeDtypeStruct((2, padded), jnp.float32),
        ),
        in_specs=[anywhere] * 7,
        out_specs=(vmem, anywhere, vmem, vmem),
        scratch_shapes=scratch,
        compiler_params=pltpu.CompilerParams(
            collective_id=2, has_side_effects=True, vmem_limit_bytes=63 * 2**20
        ),
        cost_estimate=pl.CostEstimate(
            flops=12 * wide_count * rows * padded * width, bytes_accessed=200 * 2**20, transcendentals=0
        ),
        name="geglu_backward",
    )(feed_grad, expand, reduce_full, slope, gelu, active, rows_all)


def rotate_lanes(vectors, cosine, signed_sine):
    return vectors * cosine + pltpu.roll(vectors, vectors.shape[1] // 2, 1) * signed_sine


def attention_backward_kernel(
    wide_count,
    narrow_count,
    places,
    upper_grad,
    hidden_part,
    normed,
    inv_std,
    small,
    merge,
    mixed,
    queries,
    keys,
    values,
    probs,
    cosine,
    signed_sine,
    triple,
    merge_grad,
    heads_sums,
    merge_sums,
    sum_grad,
    norm_sums,
    gain,
    attended,
    upstream,
    outbound,
    probs_held,
    keys_turned,
    key_total,
    value_total,
    merge_out,
    merge_in,
    mixed_send,
    mixed_recv,
    merge_send,
    merge_recv,
    load_sems,
    parts,
    from_mate,
    incoming,
    mate_send,
    mate_recv,
    sum_send,
    sum_recv,
):
    sems = (None, None, mate_send, mate_recv, sum_send, sum_recv, None)
    plane = PlaneExchange(wide_count, None, None, parts, from_mate, incoming, sems)
    line = LineExchange(narrow_count)
    rows, width = sum_grad.shape
    own_cols = queries.shape[1]
    heads = own_cols // HDIM
    scale = HDIM ** (-0.5)

    def load(head):
        return pltpu.make_async_copy(
            probs.at[head], probs_held.at[head % 2], load_sems.at[head % 2]
        )

    load(0).start()
    greet_plane(plane)

    spread_small(gain, small, places[2], 0)
    norm_sums[...] = jnp.zeros_like(norm_sums)
    merge_sums[...] = jnp.zeros_like(merge_sums)

    def norm_rows(i, carry):
        some = pl.ds(pl.multiple_of(i * 16, 16), 16)
        hidden_grad = residual_scale * upper_grad[some] + hidden_part[some]
        norm_sums[0:1] += jnp.sum(hidden_grad * normed[some], axis=0, keepdims=True)
        norm_sums[1:2] += jnp.sum(hidden_grad, axis=0, keepdims=True)
        total = normalize_back(hidden_grad, normed[some], inv_std[some], gain[...])
        sum_grad[some] = total
        merge_sums[...] += jnp.sum(total, axis=0, keepdims=True)
        attended[some] = total.astype(jnp.bfloat16)
        return carry

    lax.fori_loop(0, rows // 16, norm_rows, 0, unroll=2)
    line.greet(3)

    def mixed_part(target, where):
        part = dot(
            attended[...],
            merge[pl.ds(pl.multiple_of(where * own_cols, own_cols), own_cols)],
            ((1,), (1,)),
        )
        target[...] = part.astype(jnp.bfloat16)

    for offset in range(1, narrow_count):
        place = line.peer(offset)
        mixed_part(outbound.at[offset - 1], place)
        line.send(offset, outbound.at[offset - 1], upstream, mixed_send, mixed_recv)
    mixed_part(upstream.at[line.mine], line.mine)

    block = parts.shape[1]

    def merge_rows(i, carry):
        cols = pl.ds(pl.multiple_of(i * block, block), block)
        parts[i] = dot(mixed[:, cols], attended[...], ((0,), (0,))).astype(jnp.bfloat16)
        return carry

    lax.fori_loop(0, wide_count, merge_rows, 0)
    for offset in range(plane.ring):
        plane.share(offset)
    plane.first_sums()
    plane.far_sums()
    plane.last_sums()
    plane.finish(merge_out)
    count = merge_grad.shape[0]

    def z_rows(where):
        return pl.ds(pl.multiple_of(where * count, count), count)

    for offset in range(1, narrow_count):
        line.send(
            offset, merge_out.at[z_rows(line.peer(offset))], merge_in, merge_send, merge_recv
        )
    for offset in range(1, narrow_count):
        line.arrived(offset, upstream, mixed_send, mixed_recv)

    def one_head(head):
        cols = pl.ds(head * HDIM, HDIM)
        load(head).wait()
        if head + 1 < heads:
            load(head + 1).start()
        held = probs_held.at[head % 2]
        keys_turned[...] = keys[:, cols].astype(jnp.float32).T.astype(jnp.bfloat16)
        key_total[...] = jnp.zeros_like(key_total)
        value_total[...] = jnp.zeros_like(value_total)

        def chunk(i, carry):
            here = pl.ds(pl.multiple_of(i * rows, rows), rows)
            weights_low = held[:, here]
            up = upstream[i, :, cols]
            pulled = dot(values[:, cols], up, ((1,), (1,)))
            weights = weights_low.astype(jnp.float32)
            scaled = weights * pulled
            change = (scaled - weights * jnp.sum(scaled, axis=0, keepdims=True)).astype(
                jnp.bfloat16
            )
            key_total[...] += dot(change, queries[here, cols], ((1,), (0,)))
            value_total[...] += dot(weights_low, up, ((1,), (0,)))
            query_grad = dot(keys_turned[...], change, ((1,), (0,))).T * scale
            triple[here, cols] = rotate_lanes(
                query_grad, cosine[here], signed_sine[here]
            ).astype(jnp.bfloat16)
            return carry

        lax.fori_loop(0, narrow_count, chunk, 0)

        def ending(i, carry):
            here = pl.ds(pl.multiple_of(i * rows, rows), rows)
            triple[here, pl.ds(own_cols + head * HDIM, HDIM)] = rotate_lanes(
                key_total[here] * scale, cosine[here], signed_sine[here]
            ).astype(jnp.bfloat16)
            triple[here, pl.ds(2 * own_cols + head * HDIM, HDIM)] = value_total[here].astype(
                jnp.bfloat16
            )
            return carry

        lax.fori_loop(0, narrow_count, ending, 0)

    for head in range(heads):
        one_head(head)

    def column_sums(cols):
        heads_sums[:, cols] = jnp.sum(
            triple[:, cols].astype(jnp.float32), axis=0, keepdims=True
        )

    tiles(3 * own_cols, 256, column_sums)
    summed = merge_out[z_rows(line.mine)].astype(jnp.float32)
    for offset in range(1, narrow_count):
        line.arrived(offset, merge_in, merge_send, merge_recv)
        summed += merge_in[line.peer(offset)].astype(jnp.float32)
    merge_grad[...] = summed
    line.drain()
    plane.drain()


def attention_backward(
    wide_count,
    narrow_count,
    places,
    upper_grad,
    hidden_part,
    normed,
    inv_std,
    small,
    merge_full,
    mixed,
    queries,
    keys,
    values,
    probs,
    cosine,
    signed_sine,
):
    rows, width = normed.shape
    bucket, own_cols = queries.shape
    block = width // wide_count
    count = block // narrow_count
    anywhere = pl.BlockSpec(memory_space=pl.ANY)
    vmem = pl.BlockSpec(memory_space=pltpu.VMEM)
    dma = pltpu.SemaphoreType.DMA
    return pl.pallas_call(
        functools.partial(attention_backward_kernel, wide_count, narrow_count, places),
        out_shape=(
            jax.ShapeDtypeStruct((bucket, 3 * own_cols), jnp.bfloat16),
            jax.ShapeDtypeStruct((count, width), jnp.float32),
            jax.ShapeDtypeStruct((1, 3 * own_cols), jnp.float32),
            jax.ShapeDtypeStruct((1, width), jnp.float32),
            jax.ShapeDtypeStruct((rows, width), jnp.float32),
            jax.ShapeDtypeStruct((2, width), jnp.float32),
        ),
        in_specs=[vmem] * 10 + [anywhere] + [vmem] * 2,
        out_specs=(vmem,) * 6,
        scratch_shapes=[
            pltpu.VMEM((1, width), jnp.float32),
            pltpu.VMEM((rows, width), jnp.bfloat16),
            pltpu.VMEM((narrow_count, rows, own_cols), jnp.bfloat16),
            pltpu.VMEM((narrow_count - 1, rows, own_cols), jnp.bfloat16),
            pltpu.VMEM((2, bucket, bucket), jnp.bfloat16),
            pltpu.VMEM((HDIM, bucket), jnp.bfloat16),
            pltpu.VMEM((bucket, HDIM), jnp.float32),
            pltpu.VMEM((bucket, HDIM), jnp.float32),
            pltpu.VMEM((block, width), jnp.bfloat16),
            pltpu.VMEM((narrow_count, count, width), jnp.bfloat16),
            dma((narrow_count - 1,)),
            dma((narrow_count,)),
            dma((narrow_count - 1,)),
            dma((narrow_count,)),
            dma((2,)),
        ]
        + sum_scratch(wide_count, block, width),
        compiler_params=pltpu.CompilerParams(
            collective_id=3, has_side_effects=True, vmem_limit_bytes=kernel_memory
        ),
        cost_estimate=pl.CostEstimate(
            flops=60 * 10**9, bytes_accessed=200 * 2**20, transcendentals=0
        ),
        name="attention_backward",
    )(
        upper_grad,
        hidden_part,
        normed,
        inv_std,
        small,
        merge_full,
        mixed,
        queries,
        keys,
        values,
        probs,
        cosine,
        signed_sine,
    )


def input_backward_kernel(
    wide_count,
    narrow_count,
    inputs,
    triple,
    heads_mat,
    small,
    sum_grad,
    input_part,
    heads_grad,
    heads_bias_grad,
    merge_bias_grad,
    gains_grad,
    shifts_grad,
    expand_bias_grad,
    reduce_bias_grad,
    small_result,
    line_parts,
    line_in,
    heads_out,
    heads_in,
    small_wide,
    small_sum,
    small_line,
    line_send,
    line_recv,
    heads_send,
    heads_recv,
    wide_send,
    wide_recv,
    small_send,
    small_recv,
    parts,
    from_mate,
    incoming,
    mate_send,
    mate_recv,
    sum_send,
    sum_recv,
):
    sems = (None, None, mate_send, mate_recv, sum_send, sum_recv, None)
    plane = PlaneExchange(wide_count, None, None, parts, from_mate, incoming, sems)
    line = LineExchange(narrow_count)
    rows, width = input_part.shape
    here = line.mine
    last = narrow_count - 1
    place = lax.axis_index("wide")

    def wide_peer(offset):
        return (place + offset) % wide_count

    barrier = pltpu.get_barrier_semaphore()
    for offset in range(1, wide_count):
        pl.semaphore_signal(
            barrier,
            inc=1,
            device_id={"wide": wide_peer(offset)},
            device_id_type=pl.DeviceIdType.MESH,
        )
    line.greet(wide_count - 1)

    def small_copy(offset, source, slot):
        return pltpu.make_async_remote_copy(
            src_ref=source,
            dst_ref=small_wide.at[slot],
            send_sem=wide_send.at[offset - 1],
            recv_sem=wide_recv.at[slot],
            device_id={"wide": wide_peer(offset)},
            device_id_type=pl.DeviceIdType.MESH,
        )

    small_copies = [
        small_copy(offset, small.at[wide_peer(offset)], place) for offset in range(1, wide_count)
    ]
    for copy in small_copies:
        copy.start()

    line_sum = LineSum(line, lambda target: line_parts.at[target], line_in, line_send, line_recv)

    def input_rows(index):
        some = pl.ds(pl.multiple_of(index * rows, rows), rows)

        def input_cols(cols):
            part = dot(triple[some], heads_mat[cols], ((1,), (1,)))
            line_parts[index, :, cols] = part.astype(jnp.bfloat16)

        tiles(width, 256, input_cols)

    for offset in range(last, 0, -1):
        for way in range(2):

            @pl.when(line_sum.reaches(way, offset))
            def _():
                input_rows(line_sum.target(way, offset))

        line_sum.begin(offset)
    input_rows(here)

    block = parts.shape[1]

    def heads_rows(i, carry):
        cols = pl.ds(pl.multiple_of(i * block, block), block)
        parts[i] = dot(inputs[:, cols], triple[...], ((0,), (0,))).astype(jnp.bfloat16)
        return carry

    lax.fori_loop(0, wide_count, heads_rows, 0)
    for offset in range(plane.ring):
        plane.share(offset)
    for offset in range(last - 1, last // 2, -1):
        line_sum.step(offset)
    plane.first_sums()
    plane.far_sums()

    for offset in range(1, wide_count):
        peer = wide_peer(offset)
        small_copy(offset, small_wide.at[peer], peer).wait_recv()
    small_wide[place] = small[place]
    total = small_wide[0]
    for index in range(1, wide_count):
        total += small_wide[index]
    small_sum[...] = total
    for offset in range(1, narrow_count):
        line.send(offset, small_sum.at[line.peer(offset)], small_line, small_send, small_recv)

    plane.last_sums()
    for offset in range(last // 2, 0, -1):
        line_sum.step(offset)
    plane.finish(heads_out)
    count = heads_grad.shape[0]

    def z_rows(where):
        return pl.ds(pl.multiple_of(where * count, count), count)

    for offset in range(1, narrow_count):
        line.send(
            offset, heads_out.at[z_rows(line.peer(offset))], heads_in, heads_send, heads_recv
        )
    heads_in[line.mine] = heads_out[z_rows(line.mine)]
    small_line[line.mine] = small_sum[line.mine]
    for offset in range(1, narrow_count):
        line.arrived(offset, small_line, small_send, small_recv)
    result = small_line[0]
    for index in range(1, narrow_count):
        result += small_line[index]
    small_result[...] = result
    row = 0
    for target in (
        heads_bias_grad,
        merge_bias_grad,
        gains_grad,
        shifts_grad,
        expand_bias_grad,
        reduce_bias_grad,
    ):
        first, size = target.shape
        for index in range(first):
            for start in range(0, size, 128):
                stop = min(start + 128, size)
                target[index : index + 1, start:stop] = small_result[
                    row : row + 1, 0 : stop - start
                ]
                row += 1

    line_sum.finish(input_part)

    def add_residual(i, carry):
        some = pl.ds(pl.multiple_of(i * 16, 16), 16)
        input_part[some] += residual_scale * sum_grad[some]
        return carry

    lax.fori_loop(0, rows // 16, add_residual, 0, unroll=2)
    for offset in range(1, narrow_count):
        line.arrived(offset, heads_in, heads_send, heads_recv)
    own_cols = triple.shape[1] // 3
    for index in range(narrow_count):
        for which in range(3):
            start = (which * narrow_count + index) * own_cols
            heads_grad[:, start : start + own_cols] = heads_in[
                index, :, which * own_cols : (which + 1) * own_cols
            ].astype(jnp.float32)
    line_sum.drain()
    for copy in small_copies:
        copy.wait_send()
    line.drain()
    plane.drain()


def input_backward(
    wide_count, narrow_count, inputs, triple_grad, heads_mat, small, sum_grad, small_shapes
):
    bucket, width = inputs.shape
    rows = bucket // narrow_count
    columns = triple_grad.shape[1]
    block = width // wide_count
    count = block // narrow_count
    vmem = pl.BlockSpec(memory_space=pltpu.VMEM)
    dma = pltpu.SemaphoreType.DMA
    lines = small.shape[2]
    return pl.pallas_call(
        functools.partial(input_backward_kernel, wide_count, narrow_count),
        out_shape=(
            jax.ShapeDtypeStruct((rows, width), jnp.float32),
            jax.ShapeDtypeStruct((count, narrow_count * columns), jnp.float32),
        )
        + tuple(jax.ShapeDtypeStruct(shape, jnp.float32) for shape in small_shapes),
        in_specs=[vmem] * 5,
        out_specs=(vmem,) * 8,
        scratch_shapes=[
            pltpu.VMEM((lines, 128), jnp.float32),
            pltpu.VMEM((narrow_count, rows, width), jnp.bfloat16),
            pltpu.VMEM((2, narrow_count - 1, rows, width), jnp.bfloat16),
            pltpu.VMEM((block, columns), jnp.bfloat16),
            pltpu.VMEM((narrow_count, count, columns), jnp.bfloat16),
            pltpu.VMEM((wide_count, narrow_count, lines, 128), jnp.float32),
            pltpu.VMEM((narrow_count, lines, 128), jnp.float32),
            pltpu.VMEM((narrow_count, lines, 128), jnp.float32),
            dma((2, narrow_count - 1)),
            dma((2, narrow_count - 1)),
            dma((narrow_count - 1,)),
            dma((narrow_count,)),
            dma((wide_count - 1,)),
            dma((wide_count,)),
            dma((narrow_count - 1,)),
            dma((narrow_count,)),
        ]
        + sum_scratch(wide_count, block, columns),
        compiler_params=pltpu.CompilerParams(
            collective_id=4, has_side_effects=True, vmem_limit_bytes=kernel_memory
        ),
        cost_estimate=pl.CostEstimate(
            flops=80 * 10**9, bytes_accessed=200 * 2**20, transcendentals=0
        ),
        name="input_backward",
    )(inputs, triple_grad, heads_mat, small, sum_grad)


def greet_all(wide_count, narrow_count):
    barrier = pltpu.get_barrier_semaphore()
    for axis, count in (("wide", wide_count), ("narrow", narrow_count)):
        place = lax.axis_index(axis)
        for offset in range(1, count):
            pl.semaphore_signal(
                barrier,
                inc=1,
                device_id={axis: (place + offset) % count},
                device_id_type=pl.DeviceIdType.MESH,
            )
    pl.semaphore_wait(barrier, wide_count + narrow_count - 2)


def gather_kernel(
    wide_count,
    narrow_count,
    own,
    heads_weight,
    merge_weight,
    heads_bias,
    merge_bias,
    norm_gains,
    norm_shifts,
    expand_bias,
    reduce_bias,
    joined_ref,
    prefix_ref,
    speeds,
    rows_out,
    heads_out,
    merge_out,
    small_out,
    triple,
    cosine,
    signed_sine,
    first_query,
    last_query,
    small,
    rows_all,
    triple_all,
    heads_all,
    merge_own,
    small_all,
    rows_send,
    rows_recv,
    heads_send,
    heads_recv,
    merge_send,
    merge_recv,
    small_send,
    small_recv,
    wide_send,
    wide_recv,
    local_sems,
    out_sems,
    heads_ring_send,
    heads_ring_recv,
    block_sems,
):
    ring_sems = (heads_ring_send, heads_ring_recv, None, None, None, None, None)
    heads_ring = PlaneExchange(wide_count, None, heads_all, heads_all, None, None, ring_sems)
    line = LineExchange(narrow_count)
    here = line.mine
    last = narrow_count - 1
    place = lax.axis_index("wide")
    slot = heads_ring.slot(0)
    rows, width = own.shape
    count = heads_weight.shape[0]
    columns = heads_all.shape[2]
    own_cols = columns // 3

    def z_rows(where):
        return pl.ds(pl.multiple_of(where * count, count), count)

    def head_cols(which, where):
        start = which * narrow_count * own_cols + where * own_cols
        return pl.ds(pl.multiple_of(start, own_cols), own_cols)

    line_rows = LineGather(line, lambda block: rows_all.at[block], rows_send, rows_recv)

    keep_rows = pltpu.make_async_copy(own, rows_all.at[here], local_sems.at[0])
    keep_rows.start()
    keeps = [
        pltpu.make_async_copy(
            heads_weight.at[:, head_cols(which, here)],
            heads_all.at[slot, z_rows(here), pl.ds(which * own_cols, own_cols)],
            local_sems.at[2 + which],
        )
        for which in range(3)
    ]
    keep_merge = pltpu.make_async_copy(
        merge_weight, merge_own.at[z_rows(here)], local_sems.at[1]
    )
    for copy in keeps + [keep_merge]:
        copy.start()
    smalls = (heads_bias, merge_bias, norm_gains, norm_shifts, expand_bias, reduce_bias)
    small[...] = jnp.zeros_like(small)
    row = 0
    for part in smalls:
        first, size = part.shape
        for index in range(first):
            for begin in range(0, size, 128):
                stop = min(begin + 128, size)
                small[row : row + 1, 0 : stop - begin] = part[
                    index : index + 1, begin:stop
                ].astype(jnp.float32)
                row += 1
    small_all[place, here] = small[...]
    greet_all(wide_count, narrow_count)

    def heads_copy(offset, which, where, sender):
        return line.copy(
            heads_weight.at[:, head_cols(which, where)],
            heads_all.at[slot, z_rows(sender), pl.ds(which * own_cols, own_cols)],
            heads_send.at[offset - 1, which],
            heads_recv.at[sender, which],
            where,
        )

    def merge_copy(offset, where, sender):
        return line.copy(
            merge_weight,
            merge_own.at[z_rows(sender)],
            merge_send.at[offset - 1],
            merge_recv.at[sender],
            where,
        )

    def small_copy(offset, where, sender):
        return line.copy(
            small,
            small_all.at[place, sender],
            small_send.at[offset - 1],
            small_recv.at[sender],
            where,
        )

    started = []

    def start(copy):
        copy.start()
        started.append(copy)

    keep_rows.wait()
    line_rows.send_own()
    for offset in range(1, narrow_count):
        for which in range(3):
            start(heads_copy(offset, which, line.peer(offset), here))
    for offset in range(1, narrow_count):
        start(small_copy(offset, line.peer(offset), here))

    halfway = narrow_count * rows // 2
    joined = joined_ref[0]

    def tables(i, carry):
        some = pl.ds(pl.multiple_of(i * rows, rows), rows)
        place_in = i * rows + lax.broadcasted_iota(jnp.int32, (rows, 1), 0)
        second = jnp.where(place_in >= halfway, 1 - joined, 0)
        local = place_in - second * halfway
        reach = jnp.where(
            joined == 1,
            prefix_ref[0, 0] + prefix_ref[0, 1],
            jnp.where(second == 1, prefix_ref[0, 1], prefix_ref[0, 0]),
        )
        first_query[some] = jnp.where(local < reach, place_in - local, place_in)
        last_query[some] = jnp.where(
            (joined == 1) | (second == 1), 2 * halfway - 1, halfway - 1
        ) + jnp.zeros_like(place_in)
        angles = local.astype(jnp.float32) * speeds[...]
        lane = lax.broadcasted_iota(jnp.int32, (rows, HDIM), 1)
        cosine[some] = jnp.cos(angles)
        sine = jnp.sin(angles)
        signed_sine[some] = jnp.where(lane < HDIM // 2, sine, -sine)
        return carry

    lax.fori_loop(0, narrow_count, tables, 0)

    line_rows.step(1)
    for copy in keeps:
        copy.wait()
    for offset in range(1, narrow_count):
        for which in range(3):
            heads_copy(offset, which, line.peer(offset), line.peer(offset)).wait_recv()
    heads_ring.send_own()
    for offset in range(1, narrow_count):
        small_copy(offset, line.peer(offset), line.peer(offset)).wait_recv()

    def wide_copy(offset, sender):
        return pltpu.make_async_remote_copy(
            src_ref=small_all.at[sender],
            dst_ref=small_all.at[sender],
            send_sem=wide_send.at[offset - 1],
            recv_sem=wide_recv.at[sender],
            device_id={"wide": (place + offset) % wide_count},
            device_id_type=pl.DeviceIdType.MESH,
        )

    for offset in range(1, wide_count):
        start(wide_copy(offset, place))

    def leave_rows(block):
        return pltpu.make_async_copy(rows_all.at[block], rows_out.at[block], block_sems.at[0, block])

    def leave_triple(block):
        return pltpu.make_async_copy(triple_all.at[block], triple.at[block], block_sems.at[1, block])

    def project(block):
        leave_rows(block).start()

        def cols_step(cols):
            weight = heads_all[:, :, cols].reshape(width, cols.size)
            triple_all[block, :, cols] = dot(rows_all[block], weight, ((1,), (0,)))

        tiles(columns, 256, cols_step)
        leave_triple(block).start()

    def project_step(step):
        line_rows.each(step, project)

    def gather(ring, distance):
        ring.receive(distance)
        ring.receive_mate(-distance)
        if distance < ring.far:
            ring.receive_mate(distance)

    outs = []

    def keep_out(source, target):
        copy = pltpu.make_async_copy(source, target, out_sems.at[len(outs)])
        copy.start()
        outs.append(copy)

    for offset in range(1, narrow_count):
        start(merge_copy(offset, line.peer(offset), here))
    heads_ring.receive_mate(0)
    for distance in range(1, heads_ring.far):
        gather(heads_ring, distance)
    if last > 1:
        line_rows.step(2)
    gather(heads_ring, heads_ring.far)
    keep_out(heads_all, heads_out)
    project(here)
    project_step(1)
    for step in range(3, narrow_count):
        project_step(step - 1)
        line_rows.step(step)
    project_step(last)
    keep_merge.wait()
    for offset in range(1, narrow_count):
        merge_copy(offset, line.peer(offset), line.peer(offset)).wait_recv()
    keep_out(merge_own, merge_out)
    for offset in range(1, wide_count):
        wide_copy(offset, (place + offset) % wide_count).wait_recv()
    keep_out(small_all, small_out)
    line_rows.drain()
    for copy in started:
        copy.wait_send()
    heads_ring.drain()
    for copy in outs:
        copy.wait()

    def left(block, carry):
        leave_rows(block).wait()
        leave_triple(block).wait()
        return carry

    lax.fori_loop(0, narrow_count, left, 0)


def gather_front(
    wide_count, narrow_count, layer_input, heads_weight, merge_weight, smalls, joined, prefix, speeds
):
    rows, width = layer_input.shape
    count, all_columns = heads_weight.shape
    columns = all_columns // narrow_count
    block = count * narrow_count
    anywhere = pl.BlockSpec(memory_space=pl.ANY)
    vmem = pl.BlockSpec(memory_space=pltpu.VMEM)
    dma = pltpu.SemaphoreType.DMA
    lines = row_places([part.shape for part in smalls])[1]
    shapes = (
        (narrow_count, rows, width),
        (wide_count, block, columns),
        (block, width),
        (wide_count, narrow_count, lines, 128),
    )
    far = narrow_count - 1
    bucket = narrow_count * rows
    table = jax.ShapeDtypeStruct((bucket, HDIM), jnp.float32)
    reach = jax.ShapeDtypeStruct((bucket, 1), jnp.int32)
    return pl.pallas_call(
        functools.partial(gather_kernel, wide_count, narrow_count),
        out_shape=tuple(jax.ShapeDtypeStruct(shape, jnp.bfloat16) for shape in shapes[:3])
        + (
            jax.ShapeDtypeStruct(shapes[3], jnp.float32),
            jax.ShapeDtypeStruct((narrow_count, rows, columns), jnp.float32),
            table,
            table,
            reach,
            reach,
        ),
        in_specs=[anywhere] * 3 + [vmem] * 6 + [pl.BlockSpec(memory_space=pltpu.SMEM)] * 2 + [vmem],
        out_specs=(anywhere,) * 5 + (vmem,) * 4,
        scratch_shapes=[
            pltpu.VMEM((lines, 128), jnp.float32),
            pltpu.VMEM(shapes[0], jnp.bfloat16),
            pltpu.VMEM((narrow_count, rows, columns), jnp.float32),
        ]
        + [pltpu.VMEM(shape, jnp.bfloat16) for shape in shapes[1:3]]
        + [pltpu.VMEM(shapes[3], jnp.float32)]
        + [
            dma((2, narrow_count)),
            dma((narrow_count,)),
            dma((far, 3)),
            dma((narrow_count, 3)),
            dma((far,)),
            dma((narrow_count,)),
            dma((far,)),
            dma((narrow_count,)),
            dma((wide_count - 1,)),
            dma((wide_count,)),
            dma((5,)),
            dma((4,)),
            dma((3, wide_count, 2)),
            dma((wide_count, 2)),
            dma((2, narrow_count)),
        ],
        compiler_params=pltpu.CompilerParams(
            collective_id=5, has_side_effects=True, vmem_limit_bytes=kernel_memory
        ),
        cost_estimate=pl.CostEstimate(
            flops=80 * 10**9, bytes_accessed=200 * 2**20, transcendentals=0
        ),
        name="gather_front",
    )(layer_input, heads_weight, merge_weight, *smalls, joined, prefix, speeds)


def attention_forward_kernel(
    wide_count,
    narrow_count,
    places,
    triple,
    small,
    cosine,
    signed_sine,
    first_query,
    last_query,
    own,
    merge,
    queries,
    keys,
    values,
    probs,
    mixed_out,
    hidden,
    hidden_low,
    normed,
    inv_std,
    merge_out,
    rows_out,
    merge_mat,
    probs_held,
    values_turned,
    outbound,
    mixed,
    mixed_send,
    mixed_recv,
    local_sems,
    ring_send,
    ring_recv,
    own_sem,
    rows_all,
    rows_send,
    rows_recv,
    rows_sem,
    heads_full,
    vectors,
):
    line = LineExchange(narrow_count)
    ring_sems = (ring_send, ring_recv, None, None, None, None, own_sem)
    ring = PlaneExchange(wide_count, merge, merge_mat, merge_mat, None, None, ring_sems)
    rows_sems = (rows_send, rows_recv, None, None, None, None, rows_sem)
    rows_ring = PlaneExchange(wide_count, hidden_low, rows_all, rows_all, None, None, rows_sems)
    bucket, own_cols = queries.shape
    rows, width = own.shape
    heads = own_cols // HDIM
    scale = HDIM ** (-0.5)
    greet_plane(ring)
    line.greet(3)
    keep_own = ring.send_own()
    spread_small(heads_full, small, places[0], 0)
    spread_small(vectors, small, places[1], 0, 0)
    spread_small(vectors, small, places[2], 0, 1)
    spread_small(vectors, small, places[3], 0, 2)
    ring_steps = [functools.partial(ring.receive, step) for step in range(1, ring.far + 1)]

    def keep(head):
        return pltpu.make_async_copy(
            probs_held.at[head % 2], probs.at[head], local_sems.at[head % 2]
        )

    def mixed_copy(head, offset, where, sender):
        cols = pl.ds(pl.multiple_of(sender * own_cols + head * HDIM, HDIM), HDIM)
        return line.copy(
            outbound.at[where, :, pl.ds(head * HDIM, HDIM)],
            mixed.at[:, cols],
            mixed_send.at[offset - 1, head],
            mixed_recv.at[sender, head],
            where,
        )

    started = []
    for head in range(heads):
        cols = pl.ds(head * HDIM, HDIM)

        def turn(i, carry):
            here = pl.ds(pl.multiple_of(i * rows, rows), rows)
            for which, target in enumerate((queries, keys, values)):
                wanted = pl.ds(which * own_cols + head * HDIM, HDIM)
                begin = (which * narrow_count + line.mine) * own_cols + head * HDIM
                bias = heads_full[:, pl.ds(pl.multiple_of(begin, HDIM), HDIM)]
                part = triple[here, wanted] + bias
                if which < 2:
                    part = rotate_lanes(part, cosine[here], -signed_sine[here])
                else:
                    values_turned[:, here] = part.T.astype(jnp.bfloat16)
                target[here, cols] = part.astype(jnp.bfloat16)
            return carry

        lax.fori_loop(0, narrow_count, turn, 0)
        if head >= 2:
            keep(head - 2).wait()
        held = probs_held.at[head % 2]

        def chunk(i, carry):
            here = pl.ds(pl.multiple_of(i * rows, rows), rows)
            scores = dot(keys[:, cols], queries[here, cols], ((1,), (1,))) * scale
            token = i * rows + lax.broadcasted_iota(jnp.int32, (bucket, rows), 1)
            seen = (token >= first_query[...]) & (token <= last_query[...])
            scores = jnp.where(seen, scores, masked_value)
            expo = jnp.exp(scores - jnp.max(scores, axis=0, keepdims=True))
            weights = (expo * (1 / jnp.sum(expo, axis=0, keepdims=True))).astype(jnp.bfloat16)
            held[:, here] = weights
            mixed_part = dot(values_turned[...], weights, ((1,), (0,)))
            outbound[i, :, cols] = mixed_part.T.astype(jnp.bfloat16)
            return carry

        lax.fori_loop(0, narrow_count, chunk, 0)
        keep(head).start()
        for offset in range(1, narrow_count):
            copy = mixed_copy(head, offset, line.peer(offset), line.mine)
            copy.start()
            started.append(copy)
        if ring_steps and head >= heads - len(ring_steps):
            ring_steps.pop(0)()
    own_mixed = pltpu.make_async_copy(
        outbound.at[line.mine],
        mixed.at[:, pl.ds(pl.multiple_of(line.mine * own_cols, own_cols), own_cols)],
        local_sems.at[3],
    )
    own_mixed.start()
    own_mixed.wait()
    keep_own.wait()
    for step in ring_steps:
        step()
    for offset in range(ring.ring):
        ring.receive_mate(offset)
    keep_merge = pltpu.make_async_copy(merge_mat, merge_out, local_sems.at[2])
    keep_merge.start()
    for offset in range(1, narrow_count):
        for head in range(heads):
            mixed_copy(head, offset, line.peer(offset), line.peer(offset)).wait_recv()
    mixed_out[...] = mixed[...]

    def merge_cols(cols):
        hidden[:, cols] = (
            residual_scale * own[:, cols].astype(jnp.float32)
            + dot(mixed[...], merge_mat[:, :, cols].reshape(width, cols.size), ((1,), (0,)))
            + vectors[0:1, cols]
        )

    tiles(width, 256, merge_cols)

    def norm_rows(i, carry):
        some = pl.ds(pl.multiple_of(i * 16, 16), 16)
        result, centred, inverse = normalize(hidden[some], vectors[1:2], vectors[2:3])
        hidden[some] = result
        hidden_low[some] = result.astype(jnp.bfloat16)
        normed[some] = centred
        inv_std[some] = inverse
        return carry

    lax.fori_loop(0, rows // 16, norm_rows, 0, unroll=2)
    keep_rows = rows_ring.send_own()
    for step in range(1, rows_ring.far + 1):
        rows_ring.receive(step)
    for offset in range(rows_ring.ring):
        rows_ring.receive_mate(offset)
    keep_rows.wait()
    keep_rows = pltpu.make_async_copy(rows_all, rows_out, rows_sem)
    keep_rows.start()
    for head in range(max(heads - 2, 0), heads):
        keep(head).wait()
    for copy in started:
        copy.wait_send()
    ring.drain()
    rows_ring.drain()
    keep_merge.wait()
    keep_rows.wait()


def attention_forward(
    wide_count,
    narrow_count,
    places,
    triple,
    small,
    cosine,
    signed_sine,
    first_query,
    last_query,
    layer_input,
    merge_block,
):
    bucket, columns = triple.shape
    rows, width = layer_input.shape
    own_cols = columns // 3
    heads = own_cols // HDIM
    anywhere = pl.BlockSpec(memory_space=pl.ANY)
    vmem = pl.BlockSpec(memory_space=pltpu.VMEM)
    dma = pltpu.SemaphoreType.DMA

    def low_shape(*shape):
        return jax.ShapeDtypeStruct(shape, jnp.bfloat16)

    def wide_shape(*shape):
        return jax.ShapeDtypeStruct(shape, jnp.float32)

    return pl.pallas_call(
        functools.partial(attention_forward_kernel, wide_count, narrow_count, places),
        out_shape=(
            low_shape(bucket, own_cols),
            low_shape(bucket, own_cols),
            low_shape(bucket, own_cols),
            low_shape(heads, bucket, bucket),
            low_shape(rows, width),
            wide_shape(rows, width),
            low_shape(rows, width),
            wide_shape(rows, width),
            wide_shape(rows, 1),
            low_shape(wide_count, *merge_block.shape),
            low_shape(wide_count, rows, width),
        ),
        in_specs=[vmem] * 7 + [anywhere],
        out_specs=(vmem, vmem, vmem, anywhere) + (vmem,) * 5 + (anywhere,) * 2,
        scratch_shapes=[
            pltpu.VMEM((wide_count, *merge_block.shape), jnp.bfloat16),
            pltpu.VMEM((2, bucket, bucket), jnp.bfloat16),
            pltpu.VMEM((HDIM, bucket), jnp.bfloat16),
            pltpu.VMEM((narrow_count, rows, own_cols), jnp.bfloat16),
            pltpu.VMEM((rows, width), jnp.bfloat16),
            dma((narrow_count - 1, heads)),
            dma((narrow_count, heads)),
            dma((4,)),
            dma((3, wide_count, 2)),
            dma((wide_count, 2)),
            dma(()),
            pltpu.VMEM((wide_count, rows, width), jnp.bfloat16),
            dma((3, wide_count, 2)),
            dma((wide_count, 2)),
            dma(()),
            pltpu.VMEM((1, 3 * width), jnp.float32),
            pltpu.VMEM((3, width), jnp.float32),
        ],
        compiler_params=pltpu.CompilerParams(
            collective_id=6, has_side_effects=True, vmem_limit_bytes=kernel_memory
        ),
        cost_estimate=pl.CostEstimate(
            flops=60 * 10**9, bytes_accessed=200 * 2**20, transcendentals=0
        ),
        name="attention_forward",
    )(
        triple,
        small,
        cosine,
        signed_sine,
        first_query,
        last_query,
        layer_input,
        merge_block,
    )


def shards(
    layer_input,
    heads_weight,
    heads_bias,
    merge_weight,
    merge_bias,
    norm_gains,
    norm_shifts,
    expand_weight,
    expand_bias,
    reduce_weight,
    reduce_bias,
    joined,
    prefix,
    cotangent,
):
    tok_rows, model_width = layer_input.shape
    wide_count = lax.axis_size("wide")
    narrow_count = lax.axis_size("narrow")
    count = wide_count * narrow_count
    bucket_len = tok_rows * narrow_count
    own_heads = HEADS // narrow_count
    own_cols = own_heads * HDIM
    share = expand_weight.shape[2]
    narrow_index = lax.axis_index("narrow")
    smalls = (
        heads_bias.reshape(1, -1),
        merge_bias.reshape(1, -1),
        norm_gains,
        norm_shifts,
        expand_bias,
        reduce_bias.reshape(1, -1),
    )
    places = row_places([part.shape for part in smalls])[0]
    (
        rows_input,
        heads_mat,
        merge_block,
        small_all,
        triple,
        cosine,
        signed_sine,
        first_query,
        last_query,
    ) = gather_front(
        wide_count,
        narrow_count,
        layer_input,
        heads_weight,
        merge_weight,
        smalls,
        joined,
        prefix,
        jnp.asarray(rotary_speeds(HDIM)),
    )
    rows_input = rows_input.reshape(bucket_len, model_width)
    heads_mat = heads_mat.reshape(model_width, 3 * own_cols)
    triple = triple.reshape(bucket_len, 3 * own_cols)
    (
        queries,
        keys,
        values,
        probs_low,
        mixed,
        hidden,
        hidden_low,
        normed_one,
        inv_one,
        merge_full,
        rows_all,
    ) = attention_forward(
        wide_count,
        narrow_count,
        places,
        triple,
        small_all,
        cosine,
        signed_sine,
        first_query,
        last_query,
        layer_input,
        merge_block,
    )

    tile_rows = -share % 16
    padded = -(-share // 256) * 256
    expand_low = jnp.pad(expand_weight.transpose(1, 2, 0), ((0, 0), (0, tile_rows), (0, 0)))
    expand_low, _ = lax.optimization_barrier((expand_low, small_all))
    expand_full = lax.all_gather(expand_low, "narrow", axis=2, tiled=True)
    reduce_low = jnp.pad(reduce_weight, ((0, tile_rows), (0, 0)))
    (
        reduce_full,
        active,
        slope,
        gelu,
        layer_output,
        sum_two_grad,
        feed_grad,
        row_sums,
    ) = geglu_forward(
        wide_count,
        narrow_count,
        places,
        rows_all,
        expand_full,
        reduce_low,
        small_all,
        hidden,
        cotangent,
    )
    reduce_weight_gradient, expand_part, hidden_part, unit_sums = geglu_backward(
        wide_count,
        narrow_count,
        feed_grad,
        expand_full,
        reduce_full,
        slope,
        gelu,
        active,
        rows_all,
    )
    expand_weight_gradient = (
        lax.psum_scatter(expand_part, "narrow", scatter_dimension=2, tiled=True)[:, :share]
        .astype(jnp.float32)
        .transpose(2, 0, 1)
    )
    (
        triple_grad,
        merge_weight_gradient,
        heads_sums,
        merge_sums,
        sum_one_grad,
        norm_one_sums,
    ) = attention_backward(
        wide_count,
        narrow_count,
        places,
        sum_two_grad,
        hidden_part,
        normed_one,
        inv_one,
        small_all,
        merge_full.reshape(model_width, model_width),
        mixed,
        queries,
        keys,
        values,
        probs_low,
        cosine,
        signed_sine,
    )

    mine_narrow = (jnp.arange(narrow_count) == narrow_index).astype(jnp.float32)
    mine_wide = (jnp.arange(wide_count) == lax.axis_index("wide")).astype(jnp.float32)
    heads_sums = (heads_sums.reshape(3, 1, own_cols) * mine_narrow[None, :, None]).reshape(count, 1, -1)
    norm_sums = jnp.stack([norm_one_sums[0], row_sums[0], norm_one_sums[1], row_sums[1]])
    norm_sums = norm_sums.reshape(4, count, -1).transpose(1, 0, 2)
    expand_sums = unit_sums[:, :share].reshape(2, narrow_count, -1).transpose(1, 0, 2)[None]
    expand_sums = (expand_sums * mine_wide[:, None, None, None]).reshape(count, 2, -1)
    reduce_sums = row_sums[2].reshape(1, narrow_count, 1, -1)
    reduce_sums = jnp.broadcast_to(
        reduce_sums, (wide_count, narrow_count, 1, reduce_sums.shape[3])
    ).reshape(count, 1, -1)
    pieces = (heads_sums, merge_sums.reshape(count, 1, -1), norm_sums, expand_sums, reduce_sums)
    packed = []
    for piece in pieces:
        piece = jnp.pad(piece, ((0, 0), (0, 0), (0, -piece.shape[2] % 128)))
        packed.append(piece.reshape(count, -1, 128))
    packed = jnp.concatenate(packed, axis=1)
    packed = jnp.pad(packed, ((0, 0), (0, -packed.shape[1] % 8), (0, 0)))
    (
        input_gradient,
        heads_weight_gradient,
        heads_bias_gradient,
        merge_bias_gradient,
        gains_gradient,
        shifts_gradient,
        expand_bias_gradient,
        reduce_bias_gradient,
    ) = input_backward(
        wide_count,
        narrow_count,
        rows_input,
        triple_grad,
        heads_mat,
        packed.reshape(wide_count, narrow_count, -1, 128),
        sum_one_grad,
        (
            (1, heads_bias.size),
            (1, merge_bias.size),
            norm_gains.shape,
            norm_shifts.shape,
            expand_bias.shape,
            (1, reduce_bias.size),
        ),
    )
    return (
        layer_output,
        input_gradient,
        heads_weight_gradient,
        heads_bias_gradient[0],
        merge_weight_gradient,
        merge_bias_gradient[0],
        gains_gradient,
        shifts_gradient,
        expand_weight_gradient,
        expand_bias_gradient,
        reduce_weight_gradient[:share],
        reduce_bias_gradient[0],
    )


def solution(mesh):
    return jax.shard_map(
        shards,
        mesh=mesh,
        in_specs=(
            P(("wide", "narrow"), None),
            P(("wide", "narrow"), None),
            P(("wide", "narrow")),
            P(("wide", "narrow"), None),
            P(("wide", "narrow")),
            P(None, ("wide", "narrow")),
            P(None, ("wide", "narrow")),
            P("narrow", None, "wide"),
            P(None, ("wide", "narrow")),
            P("wide", "narrow"),
            P("narrow"),
            P("wide"),
            P("wide", None),
            P(("wide", "narrow"), None),
        ),
        out_specs=(
            P(("wide", "narrow"), None),
            P(("wide", "narrow"), None),
            P(("wide", "narrow"), None),
            P(("wide", "narrow")),
            P(("wide", "narrow"), None),
            P(("wide", "narrow")),
            P(None, ("wide", "narrow")),
            P(None, ("wide", "narrow")),
            P("narrow", None, "wide"),
            P(None, ("wide", "narrow")),
            P("wide", "narrow"),
            P("narrow"),
        ),
        check_vma=False,
    )
```

```python
import functools
import math

import jax
import jax.numpy as jnp
import numpy as np
from jax import lax
from jax.experimental import pallas as pl
from jax.experimental.pallas import tpu as pltpu
from jax.sharding import PartitionSpec as P

HEADS = 16
HDIM = 128


residual_scale = 48.0**0.5
norm_eps = 1e-05
masked_value = -1e30
kernel_memory = 60 * 2**20


def rotary_speeds(head_size):
    index = np.arange(head_size) % (head_size // 2)
    return (10000.0 ** (-2.0 * index / head_size)).astype(np.float32)[None]


def normalize(values, gain, shift):
    centre = jnp.mean(values, axis=-1, keepdims=True)
    centred = values - centre
    variance = jnp.mean(centred * centred, axis=-1, keepdims=True)
    inv_std = lax.rsqrt(variance + norm_eps)
    normed = centred * inv_std
    return (normed * gain + shift, normed, inv_std)


def normalize_back(upstream, normed, inv_std, gain):
    scaled = upstream * gain
    return inv_std * (
        scaled
        - jnp.mean(scaled, axis=-1, keepdims=True)
        - normed * jnp.mean(scaled * normed, axis=-1, keepdims=True)
    )


def dot(left, right, dims):
    return lax.dot_general(left, right, (dims, ((), ())), preferred_element_type=jnp.float32)


def low(values):
    return values.astype(jnp.bfloat16)


def row_places(shapes):
    places = []
    start = 0
    for first, size in shapes:
        places.append((start, first, size))
        start += first * -(-size // 128)
    return places, start + -start % 8


def small_piece(block, place, index):
    start, _, size = place
    rows = -(-size // 128)
    pieces = []
    for row in range(rows):
        stop = min(size - 128 * row, 128)
        here = start + index * rows + row
        pieces.append(block[here : here + 1, 0:stop])
    return pieces


def spread_small(target, small, place, index, row=0):
    at = 0
    for wide in range(small.shape[0]):
        for narrow in range(small.shape[1]):
            for piece in small_piece(small.at[wide, narrow], place, index):
                target[row : row + 1, at : at + piece.shape[1]] = piece
                at += piece.shape[1]


def ring_place(wide_count):
    ring = wide_count // 2
    mine = lax.axis_index("wide")
    chip = mine // 2
    core = mine % 2
    position = 2 * (chip // 2) + (chip % 2 + chip // 2) % 2
    return ring, position, core


def chip_at(position, ring):
    position = (position + 2 * ring) % ring
    return 2 * (position // 2) + (position + position // 2) % 2


class PlaneExchange:
    def __init__(self, wide_count, own, blocks, parts, from_mate, incoming, sems, cols=None):
        self.ring, self.position, self.core = ring_place(wide_count)
        self.own, self.blocks, self.parts = own, blocks, parts
        self.from_mate, self.incoming = from_mate, incoming
        (
            self.gather_send,
            self.gather_recv,
            self.mate_send,
            self.mate_recv,
            self.sum_send,
            self.sum_recv,
            self.own_sem,
        ) = sems
        self.half = parts.shape[1] // 2
        self.cols = slice(None) if cols is None else cols
        self.far = self.ring // 2
        self.started = []

    def device(self, offset, mate=False):
        core = 1 - self.core if mate else self.core
        return {"wide": 2 * chip_at(self.position + offset, self.ring) + core}

    def slot(self, offset, mate=False):
        core = 1 - self.core if mate else self.core
        return 2 * chip_at(self.position + offset, self.ring) + core

    def rows(self, part):
        return pl.ds(part * self.half, self.half)

    def greet(self):
        barrier = pltpu.get_barrier_semaphore()
        for where in (self.device(-1), self.device(1), self.device(0, True)):
            pl.semaphore_signal(
                barrier, inc=1, device_id=where, device_id_type=pl.DeviceIdType.MESH
            )
        pl.semaphore_wait(barrier, 3)

    def start(self, source, target, send_sem, recv_sem, where):
        copy = pltpu.make_async_remote_copy(
            src_ref=source,
            dst_ref=target,
            send_sem=send_sem,
            recv_sem=recv_sem,
            device_id=where,
            device_id_type=pl.DeviceIdType.MESH,
        )
        copy.start()
        self.started.append(copy)

    def pass_on(self, lane, slot, part, where, source=None):
        target = self.blocks.at[slot, self.rows(part)]
        self.start(
            target if source is None else source,
            target,
            self.gather_send.at[lane, slot, part],
            self.gather_recv.at[slot, part],
            where,
        )

    def arrived(self, slot, part):
        target = self.blocks.at[slot, self.rows(part)]
        pltpu.make_async_remote_copy(
            src_ref=target,
            dst_ref=target,
            send_sem=self.gather_send.at[0, slot, part],
            recv_sem=self.gather_recv.at[slot, part],
            device_id=self.device(1),
            device_id_type=pl.DeviceIdType.MESH,
        ).wait_recv()

    def send_own(self):
        slot = self.slot(0)
        keep = None
        own = self.blocks.at[slot]
        if self.own is not None:
            own = self.own
            keep = pltpu.make_async_copy(own, self.blocks.at[slot], self.own_sem)
            keep.start()
        first, second = own.at[self.rows(0)], own.at[self.rows(1)]
        self.pass_on(0, slot, 0, self.device(1), first)
        self.pass_on(1, slot, 1, self.device(-1), second)
        self.pass_on(2, slot, 0, self.device(0, True), first)
        self.pass_on(2, slot, 1, self.device(0, True), second)
        self.pass_on(0, slot, 1, self.device(1), second)
        self.pass_on(1, slot, 0, self.device(-1), first)
        return keep

    def receive(self, distance):
        mate = self.device(0, True)
        left, right = self.slot(-distance), self.slot(distance)
        if distance == self.far:
            for part in range(2):
                self.arrived(left, part)
                self.pass_on(2, left, part, mate)
            return
        further = distance < self.far - 1
        self.arrived(left, 0)
        self.pass_on(0, left, 0, self.device(1))
        self.pass_on(2, left, 0, mate)
        self.arrived(right, 1)
        self.pass_on(1, right, 1, self.device(-1))
        self.pass_on(2, right, 1, mate)
        self.arrived(left, 1)
        if further:
            self.pass_on(0, left, 1, self.device(1))
        self.pass_on(2, left, 1, mate)
        self.arrived(right, 0)
        if further:
            self.pass_on(1, right, 0, self.device(-1))
        self.pass_on(2, right, 0, mate)

    def receive_mate(self, offset):
        for part in range(2):
            self.arrived(self.slot(offset, True), part)

    def share(self, offset):
        chip = chip_at(self.position + offset, self.ring)
        self.start(
            self.parts.at[self.slot(offset, True), :, self.cols],
            self.from_mate.at[chip, :, self.cols],
            self.mate_send.at[chip],
            self.mate_recv.at[chip],
            self.device(0, True),
        )

    def shared(self, offset):
        chip = chip_at(self.position + offset, self.ring)
        pltpu.make_async_remote_copy(
            src_ref=self.parts.at[self.slot(offset), :, self.cols],
            dst_ref=self.from_mate.at[chip, :, self.cols],
            send_sem=self.mate_send.at[chip],
            recv_sem=self.mate_recv.at[chip],
            device_id=self.device(0, True),
            device_id_type=pl.DeviceIdType.MESH,
        ).wait_recv()

    def chip_sum(self, offset, rows):
        chip = chip_at(self.position + offset, self.ring)
        return self.parts[self.slot(offset), rows, self.cols].astype(
            jnp.float32
        ) + self.from_mate[chip, rows, self.cols].astype(jnp.float32)

    def send_sum(self, way, distance, part):
        offset = distance if way == 0 else -distance
        begins = self.far if part == way else self.far - 1
        slot = self.slot(offset)
        if distance < begins:
            self.sum_arrived(way, distance, part)

        def chunk(i, carry):
            here = pl.ds(pl.multiple_of(i * 16, 16), 16)
            there = pl.ds(pl.multiple_of(part * self.half + i * 16, 16), 16)
            total = self.chip_sum(offset, there)
            if distance < begins:
                total += self.incoming[way, distance, part, here, self.cols].astype(jnp.float32)
            self.parts[slot, there, self.cols] = total.astype(jnp.bfloat16)
            return carry

        lax.fori_loop(0, self.half // 16, chunk, 0)
        self.start(
            self.parts.at[slot, self.rows(part), self.cols],
            self.incoming.at[way, distance - 1, part, :, self.cols],
            self.sum_send.at[way, distance - 1, part],
            self.sum_recv.at[way, distance - 1, part],
            self.device(1 if way == 0 else -1),
        )

    def sum_arrived(self, way, distance, part):
        target = self.incoming.at[way, distance, part, :, self.cols]
        pltpu.make_async_remote_copy(
            src_ref=target,
            dst_ref=target,
            send_sem=self.sum_send.at[way, distance, part],
            recv_sem=self.sum_recv.at[way, distance, part],
            device_id=self.device(1),
            device_id_type=pl.DeviceIdType.MESH,
        ).wait_recv()

    def run(self, first, second, before, after_far):
        def compute(chip):
            first(chip)
            second(chip)

        keep = self.send_own()
        keep.wait()
        self.receive_mate(0)
        compute(chip_at(self.position, self.ring))
        self.share(0)
        for distance in range(1, self.far):
            self.receive(distance)
            for offset in (-distance, distance):
                self.receive_mate(offset)
                compute(chip_at(self.position + offset, self.ring))
                self.share(offset)
            if distance == self.far - 1:
                self.first_sums()
        self.receive(self.far)
        self.receive_mate(self.far)
        farthest = chip_at(self.position + self.far, self.ring)
        first(farthest)
        before()
        second(farthest)
        self.share(self.far)
        self.far_sums()
        after_far()
        self.last_sums()

    def start_sums(self, compute):
        compute(chip_at(self.position + self.far, self.ring))
        self.share(self.far)
        for distance in range(self.far - 1, 0, -1):
            for offset in (-distance, distance):
                compute(chip_at(self.position + offset, self.ring))
                self.share(offset)
            if distance == self.far - 1:
                self.far_sums()
                self.first_sums()
        compute(chip_at(self.position, self.ring))
        self.share(0)

    def first_sums(self):
        distance = self.far - 1
        self.shared(distance)
        self.send_sum(0, distance, 1)
        self.shared(-distance)
        self.send_sum(1, distance, 0)

    def far_sums(self):
        self.shared(self.far)
        self.send_sum(0, self.far, 0)
        self.send_sum(1, self.far, 1)

    def last_sums(self):
        for distance in range(self.far - 1, 0, -1):
            if distance < self.far - 1:
                self.shared(distance)
                self.shared(-distance)
            self.send_sum(0, distance, 0)
            self.send_sum(1, distance, 1)
            if distance < self.far - 1:
                self.send_sum(0, distance, 1)
                self.send_sum(1, distance, 0)

    def finish(self, result):
        self.shared(0)
        for part in range(2):
            for way in range(2):
                self.sum_arrived(way, 0, part)

            def chunk(i, carry):
                here = pl.ds(pl.multiple_of(i * 16, 16), 16)
                there = pl.ds(pl.multiple_of(part * self.half + i * 16, 16), 16)
                total = self.chip_sum(0, there)
                for way in range(2):
                    total += self.incoming[way, 0, part, here, self.cols].astype(jnp.float32)
                result[there, self.cols] = total.astype(result.dtype)
                return carry

            lax.fori_loop(0, self.half // 16, chunk, 0)

    def drain(self):
        for copy in self.started:
            copy.wait_send()


def sum_scratch(wide_count, rows, width):
    ring = wide_count // 2
    far = ring // 2
    dma = pltpu.SemaphoreType.DMA
    return [
        pltpu.VMEM((wide_count, rows, width), jnp.bfloat16),
        pltpu.VMEM((ring, rows, width), jnp.bfloat16),
        pltpu.VMEM((2, far, 2, rows // 2, width), jnp.bfloat16),
        dma((ring,)),
        dma((ring,)),
        dma((2, far, 2)),
        dma((2, far, 2)),
    ]


def exchange_scratch(wide_count, rows, width):
    dma = pltpu.SemaphoreType.DMA
    return [
        pltpu.VMEM((wide_count, rows, width), jnp.bfloat16),
        dma((3, wide_count, 2)),
        dma((wide_count, 2)),
        dma(()),
    ] + sum_scratch(wide_count, rows, width)


def load_padded(source, target, sem):
    filled = source.shape[0]
    copy = pltpu.make_async_copy(source, target.at[pl.ds(0, filled)], sem)
    copy.start()
    if filled < target.shape[0]:
        target[pl.ds(filled, target.shape[0] - filled)] = jnp.zeros(
            (target.shape[0] - filled, target.shape[1]), target.dtype
        )
    return copy


def pair_rows(ref, chip):
    block = ref[pl.ds(2 * chip, 2)]
    return block.reshape(2 * block.shape[1], block.shape[2])


def set_pair(ref, chip, cols, value):
    rows = ref.shape[1]
    ref[2 * chip, :, cols] = value[:rows].astype(ref.dtype)
    ref[2 * chip + 1, :, cols] = value[rows:].astype(ref.dtype)


def tiles(count, tile, body, start=0):
    def step(i, carry):
        body(pl.ds(pl.multiple_of(start + i * tile, tile), tile))
        return carry

    lax.fori_loop(0, count // tile, step, 0)


class LineExchange:
    def __init__(self, narrow_count):
        self.count = narrow_count
        self.mine = lax.axis_index("narrow")
        self.started = []

    def peer(self, offset):
        return (self.mine + offset) % self.count

    def greet(self, extra=0):
        barrier = pltpu.get_barrier_semaphore()
        for offset in range(1, self.count):
            pl.semaphore_signal(
                barrier,
                inc=1,
                device_id={"narrow": self.peer(offset)},
                device_id_type=pl.DeviceIdType.MESH,
            )
        pl.semaphore_wait(barrier, self.count - 1 + extra)

    def copy(self, source, target, send_sem, recv_sem, where):
        return pltpu.make_async_remote_copy(
            src_ref=source,
            dst_ref=target,
            send_sem=send_sem,
            recv_sem=recv_sem,
            device_id={"narrow": where},
            device_id_type=pl.DeviceIdType.MESH,
        )

    def send(self, offset, source, landing, send_sems, recv_sems):
        peer = self.peer(offset)
        copy = self.copy(
            source, landing.at[self.mine], send_sems.at[offset - 1], recv_sems.at[self.mine], peer
        )
        copy.start()
        self.started.append(copy)

    def arrived(self, offset, landing, send_sems, recv_sems):
        peer = self.peer(offset)
        self.copy(
            landing.at[peer], landing.at[peer], send_sems.at[offset - 1], recv_sems.at[peer], peer
        ).wait_recv()

    def drain(self):
        for copy in self.started:
            copy.wait_send()


class LineSum:
    def __init__(self, line, view, landing, send_sems, recv_sems):
        self.line, self.view, self.landing = line, view, landing
        self.send_sems, self.recv_sems = send_sems, recv_sems
        self.last = line.count - 1

    def reaches(self, way, offset):
        here = self.line.mine
        return here + offset <= self.last if way == 0 else here - offset >= 0

    def follows(self, way):
        here = self.line.mine
        return here > 0 if way == 0 else here < self.last

    def target(self, way, offset):
        return self.line.mine + offset if way == 0 else self.line.mine - offset

    def copy(self, way, offset):
        return self.line.copy(
            self.view(self.target(way, offset)),
            self.landing.at[way, offset - 1],
            self.send_sems.at[way, offset - 1],
            self.recv_sems.at[way, offset - 1],
            self.line.mine + 1 if way == 0 else self.line.mine - 1,
        )

    def arrived(self, way, offset):
        landing = self.landing.at[way, offset]
        self.line.copy(
            landing,
            landing,
            self.send_sems.at[way, offset],
            self.recv_sems.at[way, offset],
            self.line.mine,
        ).wait_recv()

    def add(self, way, offset):
        held = self.view(self.target(way, offset))

        def chunk(i, carry):
            some = pl.ds(pl.multiple_of(i * 16, 16), 16)
            held[some] = (
                held[some].astype(jnp.float32)
                + self.landing[way, offset, some].astype(jnp.float32)
            ).astype(jnp.bfloat16)
            return carry

        lax.fori_loop(0, self.landing.shape[2] // 16, chunk, 0)

    def begin(self, offset):
        for way in range(2):

            @pl.when(self.reaches(way, offset) & jnp.logical_not(self.follows(way)))
            def _():
                self.copy(way, offset).start()

    def step(self, offset):
        for way in range(2):

            @pl.when(self.reaches(way, offset) & self.follows(way))
            def _():
                self.arrived(way, offset)
                self.add(way, offset)
                self.copy(way, offset).start()

    def finish(self, result):
        held = self.view(self.line.mine)
        count = self.landing.shape[2] // 16

        def begin(i, carry):
            some = pl.ds(pl.multiple_of(i * 16, 16), 16)
            result[some] = held[some].astype(result.dtype)
            return carry

        lax.fori_loop(0, count, begin, 0)
        for way in range(2):

            @pl.when(self.follows(way))
            def _():
                self.arrived(way, 0)

                def chunk(i, carry):
                    some = pl.ds(pl.multiple_of(i * 16, 16), 16)
                    result[some] += self.landing[way, 0, some].astype(result.dtype)
                    return carry

                lax.fori_loop(0, count, chunk, 0)

    def drain(self):
        for offset in range(1, self.last + 1):
            for way in range(2):

                @pl.when(self.reaches(way, offset))
                def _():
                    self.copy(way, offset).wait_send()


class LineGather:
    def __init__(self, line, view, send_sems, recv_sems):
        self.line, self.view = line, view
        self.send_sems, self.recv_sems = send_sems, recv_sems
        self.last = line.count - 1

    def copy(self, way, block):
        target = self.view(block)
        here = self.line.mine
        return self.line.copy(
            target,
            target,
            self.send_sems.at[way, block],
            self.recv_sems.at[block],
            here + 1 if way == 0 else here - 1,
        )

    def goes(self, way):
        return self.line.mine < self.last if way == 0 else self.line.mine > 0

    def has(self, way, step):
        here = self.line.mine
        return here - step >= 0 if way == 0 else here + step <= self.last

    def block(self, way, step):
        return self.line.mine - step if way == 0 else self.line.mine + step

    def send_own(self):
        for way in range(2):

            @pl.when(self.goes(way))
            def _():
                self.copy(way, self.line.mine).start()

    def step(self, step):
        for way in range(2):

            @pl.when(self.has(way, step))
            def _():
                self.copy(way, self.block(way, step)).wait_recv()

                @pl.when(self.goes(way))
                def _():
                    self.copy(way, self.block(way, step)).start()

    def each(self, step, body):
        for way in range(2):

            @pl.when(self.has(way, step))
            def _():
                body(self.block(way, step))

    def drain(self):
        for way in range(2):
            for step in range(self.last + 1):

                @pl.when(self.has(way, step) & self.goes(way))
                def _():
                    self.copy(way, self.block(way, step)).wait_send()


def greet_plane(plane):
    barrier = pltpu.get_barrier_semaphore()
    for where in (plane.device(-1), plane.device(1), plane.device(0, True)):
        pl.semaphore_signal(barrier, inc=1, device_id=where, device_id_type=pl.DeviceIdType.MESH)


def geglu_forward_kernel(
    wide_count,
    narrow_count,
    places,
    rows_all,
    expand,
    reduce,
    small,
    hidden,
    cotangent,
    reduce_out,
    active_out,
    slope_out,
    gelu_out,
    layer_output,
    sum_grad,
    feed_grad,
    row_sums,
    feed,
    blocks,
    parts,
    from_mate,
    incoming,
    mate_send,
    mate_recv,
    sum_send,
    sum_recv,
    expand_mat,
    reduce_mat,
    active,
    slope,
    gelu,
    load_sems,
    keep_sems,
    reduce_send,
    reduce_recv,
    next_mate_send,
    next_mate_recv,
    next_sum_send,
    next_sum_recv,
    late_mate_send,
    late_mate_recv,
    late_sum_send,
    late_sum_recv,
    shift,
    vectors,
):
    line = LineExchange(narrow_count)
    filled, cols = reduce.shape
    width = rows_all.shape[2]
    upper = (2 * line.mine) // narrow_count
    half = narrow_count // 2
    windows = (
        (half * upper, half, half - 1),
        (half - upper * (half - 1), half - 1, narrow_count - 2),
        ((narrow_count - 1) * (1 - upper), 1, narrow_count - 1),
    )
    sems = (
        (mate_send, mate_recv, sum_send, sum_recv),
        (next_mate_send, next_mate_recv, next_sum_send, next_sum_recv),
        (late_mate_send, late_mate_recv, late_sum_send, late_sum_recv),
    )
    planes = [
        PlaneExchange(
            wide_count,
            None,
            None,
            parts,
            from_mate,
            incoming,
            (None, None, *own_sems, None),
            pl.ds(pl.multiple_of(first * cols, cols), blocks_in * cols),
        )
        for (first, blocks_in, _), own_sems in zip(windows, sems)
    ]
    plane = planes[0]
    loads = [
        load_padded(expand.at[0], expand_mat.at[0], load_sems.at[0]),
        load_padded(expand.at[1], expand_mat.at[1], load_sems.at[1]),
        pltpu.make_async_copy(rows_all, blocks, load_sems.at[4]),
    ]
    loads[2].start()

    def reduce_cols(block):
        return reduce_mat.at[
            pl.ds(0, filled), pl.ds(pl.multiple_of(block * cols, cols), cols)
        ]

    line_reduce = LineGather(line, reduce_cols, reduce_send, reduce_recv)
    own_reduce = pltpu.make_async_copy(reduce, reduce_cols(line.mine), load_sems.at[2])
    own_reduce.start()
    if filled < reduce_mat.shape[0]:
        reduce_mat[filled:] = jnp.zeros(
            (reduce_mat.shape[0] - filled, reduce_mat.shape[1]), reduce_mat.dtype
        )
    greet_plane(plane)
    line.greet(3)
    place = lax.axis_index("wide")
    shift[...] = jnp.zeros_like(shift)
    for index in range(2):
        at = 0
        for block in range(narrow_count):
            for piece in small_piece(small.at[place, block], places[4], index):
                shift[index : index + 1, at : at + piece.shape[1]] = piece
                at += piece.shape[1]
    at = 0
    for block in range(narrow_count):
        for piece in small_piece(small.at[0, block], places[5], 0):
            vectors[0:1, at : at + piece.shape[1]] = piece
            at += piece.shape[1]
    spread_small(vectors, small, places[2], 1, 1)
    spread_small(vectors, small, places[3], 1, 2)
    own_reduce.wait()
    line_reduce.send_own()
    kept = []
    waiting = list(loads)

    def compute(chip):
        while waiting:
            waiting.pop().wait()

        def units(cols):
            rows = pair_rows(blocks, chip)
            gate = dot(rows, expand_mat[0, cols], ((1,), (1,))) + shift[0:1, cols]
            upper = dot(rows, expand_mat[1, cols], ((1,), (1,))) + shift[1:2, cols]
            factor = math.sqrt(2 / math.pi)
            square = gate * gate
            bend = jnp.tanh(factor * gate * (1 + 0.044715 * square))
            value = 0.5 * gate * (1 + bend)
            pull = 0.5 * (1 + bend) + 0.5 * gate * (1 - bend * bend) * factor * (
                1 + 3 * 0.044715 * square
            )
            set_pair(active, chip, cols, value * upper)
            set_pair(slope, chip, cols, pull * upper)
            set_pair(gelu, chip, cols, value)

        tiles(active.shape[2], 256, units)

        pair = pl.ds(2 * chip, 2)
        for index, (source, target) in enumerate(
            ((active, active_out), (slope, slope_out), (gelu, gelu_out))
        ):
            copy = pltpu.make_async_copy(
                source.at[pair], target.at[pair], keep_sems.at[chip, index]
            )
            copy.start()
            kept.append(copy)

    def compute_sums(start, count):
        def compute(chip):
            def outputs(some):
                part = dot(pair_rows(active, chip), reduce_mat[:, some], ((1,), (0,)))
                set_pair(parts, chip, some, part)

            tiles(count, 256, outputs, start)

        return compute

    offsets = [0]
    for distance in range(1, plane.far):
        offsets += [-distance, distance]
    offsets.append(plane.far)
    chips = [chip_at(plane.position + offset, plane.ring) for offset in offsets]
    for index, chip in enumerate(chips):
        if index == len(chips) - 1:
            line_reduce.step(1)
        compute(chip)
    step = 1
    for window, (first, blocks_in, needed) in enumerate(windows):
        while step < needed:
            step += 1
            line_reduce.step(step)
        start = pl.multiple_of(first * cols, cols)
        planes[window].start_sums(compute_sums(start, blocks_in * cols))
        if window > 0:
            planes[window - 1].last_sums()
    planes[-1].last_sums()
    keep_reduce = pltpu.make_async_copy(
        reduce_mat.at[pl.ds(0, filled)], reduce_out, load_sems.at[3]
    )
    keep_reduce.start()
    for part in planes:
        part.finish(feed)

    row_sums[...] = jnp.zeros_like(row_sums)

    def norm_rows(i, carry):
        some = pl.ds(pl.multiple_of(i * 16, 16), 16)
        result, normed, inverse = normalize(
            residual_scale * hidden[some] + feed[some] + vectors[0:1],
            vectors[1:2],
            vectors[2:3],
        )
        layer_output[some] = result.astype(jnp.bfloat16)
        upstream = cotangent[some].astype(jnp.float32)
        total = normalize_back(upstream, normed, inverse, vectors[1:2])
        sum_grad[some] = total
        feed_grad[some] = total.astype(jnp.bfloat16)
        row_sums[0:1] += jnp.sum(upstream * normed, axis=0, keepdims=True)
        row_sums[1:2] += jnp.sum(upstream, axis=0, keepdims=True)
        row_sums[2:3] += jnp.sum(total, axis=0, keepdims=True)
        return carry

    lax.fori_loop(0, rows_all.shape[1] // 16, norm_rows, 0, unroll=2)
    for part in planes:
        part.drain()
    keep_reduce.wait()
    line_reduce.drain()
    for copy in kept:
        copy.wait()


def geglu_forward(
    wide_count,
    narrow_count,
    places,
    rows_all,
    expand,
    reduce_weight,
    small,
    hidden,
    cotangent,
):
    _, rows, width = rows_all.shape
    padded = -(-expand.shape[1] // 256) * 256
    anywhere = pl.BlockSpec(memory_space=pl.ANY)
    vmem = pl.BlockSpec(memory_space=pltpu.VMEM)
    kept = jax.ShapeDtypeStruct((wide_count, rows, padded), jnp.bfloat16)
    scratch = [pltpu.VMEM((rows, width), jnp.float32)]
    scratch.append(pltpu.VMEM((wide_count, rows, width), jnp.bfloat16))
    scratch += sum_scratch(wide_count, rows, width) + [
        pltpu.VMEM((2, padded, width), jnp.bfloat16),
        pltpu.VMEM((padded, width), jnp.bfloat16),
        pltpu.VMEM((wide_count, rows, padded), jnp.bfloat16),
        pltpu.VMEM((wide_count, rows, padded), jnp.bfloat16),
        pltpu.VMEM((wide_count, rows, padded), jnp.bfloat16),
        pltpu.SemaphoreType.DMA((5,)),
        pltpu.SemaphoreType.DMA((wide_count // 2, 3)),
        pltpu.SemaphoreType.DMA((2, narrow_count)),
        pltpu.SemaphoreType.DMA((narrow_count,)),
    ] + 2 * sum_scratch(wide_count, rows, width)[3:]
    scratch += [pltpu.VMEM((2, padded), jnp.float32), pltpu.VMEM((3, width), jnp.float32)]
    return pl.pallas_call(
        functools.partial(geglu_forward_kernel, wide_count, narrow_count, places),
        out_shape=(
            jax.ShapeDtypeStruct((reduce_weight.shape[0], width), jnp.bfloat16),
            kept,
            kept,
            kept,
            jax.ShapeDtypeStruct((rows, width), jnp.bfloat16),
            jax.ShapeDtypeStruct((rows, width), jnp.float32),
            jax.ShapeDtypeStruct((rows, width), jnp.bfloat16),
            jax.ShapeDtypeStruct((3, width), jnp.float32),
        ),
        in_specs=[anywhere] * 3 + [vmem] * 3,
        out_specs=(anywhere,) * 4 + (vmem,) * 4,
        scratch_shapes=scratch,
        compiler_params=pltpu.CompilerParams(
            collective_id=1, has_side_effects=True, vmem_limit_bytes=kernel_memory
        ),
        cost_estimate=pl.CostEstimate(
            flops=6 * wide_count * rows * padded * width, bytes_accessed=200 * 2**20, transcendentals=0
        ),
        name="geglu_forward",
    )(
        rows_all,
        expand,
        reduce_weight,
        small,
        hidden,
        cotangent,
    )


def geglu_backward_kernel(
    wide_count,
    narrow_count,
    own,
    expand,
    reduce,
    slope_in,
    gelu_in,
    active_in,
    rows_in,
    reduce_grad,
    expand_part,
    hidden_grad,
    unit_sums,
    blocks,
    gather_send,
    gather_recv,
    own_sem,
    parts,
    from_mate,
    incoming,
    mate_send,
    mate_recv,
    sum_send,
    sum_recv,
    expand_mat,
    reduce_mat,
    slope,
    gelu,
    active,
    rows_all,
    staged,
    load_sems,
    keep_sems,
    line_in,
    line_send,
    line_recv,
):
    sems = (gather_send, gather_recv, mate_send, mate_recv, sum_send, sum_recv, own_sem)
    plane = PlaneExchange(wide_count, own, blocks, parts, from_mate, incoming, sems)
    loads = [
        load_padded(expand.at[0], expand_mat.at[0], load_sems.at[0]),
        load_padded(expand.at[1], expand_mat.at[1], load_sems.at[1]),
        load_padded(reduce, reduce_mat, load_sems.at[2]),
        pltpu.make_async_copy(slope_in, slope, load_sems.at[3]),
        pltpu.make_async_copy(gelu_in, gelu, load_sems.at[4]),
    ]
    late_loads = [
        pltpu.make_async_copy(active_in, active, load_sems.at[5]),
        pltpu.make_async_copy(rows_in, rows_all, load_sems.at[6]),
    ]
    for copy in loads[3:]:
        copy.start()
    unit_sums[...] = jnp.zeros_like(unit_sums)
    line = LineExchange(narrow_count)
    filled, line_cols = line_in.shape[2:]

    def line_part(block):
        return reduce_mat.at[
            pl.ds(0, filled), pl.ds(pl.multiple_of(block * line_cols, line_cols), line_cols)
        ]

    line_sum = LineSum(line, line_part, line_in, line_send, line_recv)
    greet_plane(plane)
    line.greet(3)
    for copy in late_loads:
        copy.start()
    kept = []
    waiting = list(loads)

    def compute(chip):
        while waiting:
            waiting.pop().wait()

        def units(cols):
            pulled = dot(pair_rows(blocks, chip), reduce_mat[cols], ((1,), (1,)))
            pair = pl.ds(2 * chip, 2)
            shape = pulled.shape
            gate_grad = pulled * slope[pair, :, cols].reshape(shape).astype(jnp.float32)
            upper_grad = pulled * gelu[pair, :, cols].reshape(shape).astype(jnp.float32)
            set_pair(slope, chip, cols, gate_grad)
            set_pair(gelu, chip, cols, upper_grad)
            unit_sums[0:1, cols] += jnp.sum(gate_grad, axis=0, keepdims=True)
            unit_sums[1:2, cols] += jnp.sum(upper_grad, axis=0, keepdims=True)

        tiles(slope.shape[2], 256, units)

    def compute_sums(chip):
        def outputs(cols):
            set_pair(
                parts,
                chip,
                cols,
                dot(pair_rows(slope, chip), expand_mat[0, :, cols], ((1,), (0,)))
                + dot(pair_rows(gelu, chip), expand_mat[1, :, cols], ((1,), (0,))),
            )

        tiles(parts.shape[2], 256, outputs)

    def product(left, right, start):
        tokens = left.shape[0] * left.shape[1]
        return dot(
            left[:, :, start : start + 256].reshape(tokens, 256),
            right[...].reshape(tokens, right.shape[2]),
            ((0,), (0,)),
        ).astype(jnp.bfloat16)

    def reduce_work():
        for copy in late_loads:
            copy.wait()

        def reduce_cols(index):
            cols = pl.ds(pl.multiple_of(index * line_cols, line_cols), line_cols)

            def units(some):
                tokens = active.shape[0] * active.shape[1]
                part = dot(
                    active[:, :, some].reshape(tokens, some.size),
                    blocks[:, :, cols].reshape(tokens, line_cols),
                    ((0,), (0,)),
                )
                reduce_mat[some, cols] = part.astype(jnp.bfloat16)

            tiles(active.shape[2], 256, units)

        for offset in range(narrow_count - 1, 0, -1):
            for way in range(2):

                @pl.when(line_sum.reaches(way, offset))
                def _():
                    reduce_cols(line_sum.target(way, offset))

            line_sum.begin(offset)
        reduce_cols(line.mine)

    def expand_work(left, start, target):
        def work():
            index = len(kept)
            if index >= 2:
                kept[index - 2].wait()
            staged[index % 2] = product(left, rows_all, start)
            stop = min(256, target.shape[0] - start)
            copy = pltpu.make_async_copy(
                staged.at[index % 2, pl.ds(0, stop)],
                target.at[pl.ds(start, stop)],
                keep_sems.at[index % 2],
            )
            copy.start()
            kept.append(copy)

        return work

    works = [
        expand_work(left, start, target)
        for left, target in ((slope, expand_part.at[0]), (gelu, expand_part.at[1]))
        for start in range(0, target.shape[0], 256)
    ]
    steps = [
        functools.partial(line_sum.step, offset) for offset in range(narrow_count - 2, 0, -1)
    ]
    third = len(works) // 3
    middle = (len(steps) + 1) // 2

    def many(calls):
        for call in calls:
            call()

    beside = functools.partial(many, steps[:middle] + works[:third])
    plane.run(compute, compute_sums, reduce_work, beside)
    many(works[third : 2 * third] + steps[middle:] + works[2 * third :])
    plane.finish(hidden_grad)
    plane.drain()
    line_sum.finish(reduce_grad)
    line_sum.drain()
    for copy in kept[-2:]:
        copy.wait()


def geglu_backward(
    wide_count,
    narrow_count,
    feed_grad,
    expand,
    reduce_full,
    slope,
    gelu,
    active,
    rows_all,
):
    rows, width = feed_grad.shape
    padded = slope.shape[2]
    anywhere = pl.BlockSpec(memory_space=pl.ANY)
    vmem = pl.BlockSpec(memory_space=pltpu.VMEM)
    scratch = exchange_scratch(wide_count, rows, width) + [
        pltpu.VMEM((2, padded, width), jnp.bfloat16),
        pltpu.VMEM((padded, width), jnp.bfloat16),
        pltpu.VMEM((wide_count, rows, padded), jnp.bfloat16),
        pltpu.VMEM((wide_count, rows, padded), jnp.bfloat16),
        pltpu.VMEM((wide_count, rows, padded), jnp.bfloat16),
        pltpu.VMEM((wide_count, rows, width), jnp.bfloat16),
        pltpu.VMEM((2, 256, width), jnp.bfloat16),
        pltpu.SemaphoreType.DMA((7,)),
        pltpu.SemaphoreType.DMA((2,)),
        pltpu.VMEM(
            (2, narrow_count - 1, reduce_full.shape[0], width // narrow_count), jnp.bfloat16
        ),
        pltpu.SemaphoreType.DMA((2, narrow_count - 1)),
        pltpu.SemaphoreType.DMA((2, narrow_count - 1)),
    ]
    return pl.pallas_call(
        functools.partial(geglu_backward_kernel, wide_count, narrow_count),
        out_shape=(
            jax.ShapeDtypeStruct(
                (reduce_full.shape[0], width // narrow_count), jnp.float32
            ),
            jax.ShapeDtypeStruct(expand.shape, jnp.bfloat16),
            jax.ShapeDtypeStruct((rows, width), jnp.float32),
            jax.ShapeDtypeStruct((2, padded), jnp.float32),
        ),
        in_specs=[anywhere] * 7,
        out_specs=(vmem, anywhere, vmem, vmem),
        scratch_shapes=scratch,
        compiler_params=pltpu.CompilerParams(
            collective_id=2, has_side_effects=True, vmem_limit_bytes=63 * 2**20
        ),
        cost_estimate=pl.CostEstimate(
            flops=12 * wide_count * rows * padded * width, bytes_accessed=200 * 2**20, transcendentals=0
        ),
        name="geglu_backward",
    )(feed_grad, expand, reduce_full, slope, gelu, active, rows_all)


def rotate_lanes(vectors, cosine, signed_sine):
    return vectors * cosine + pltpu.roll(vectors, vectors.shape[1] // 2, 1) * signed_sine


def attention_backward_kernel(
    wide_count,
    narrow_count,
    places,
    upper_grad,
    hidden_part,
    normed,
    inv_std,
    small,
    merge,
    mixed,
    queries,
    keys,
    values,
    probs,
    cosine,
    signed_sine,
    triple,
    merge_grad,
    heads_sums,
    merge_sums,
    sum_grad,
    norm_sums,
    gain,
    attended,
    upstream,
    outbound,
    probs_held,
    keys_turned,
    key_total,
    value_total,
    merge_out,
    merge_in,
    mixed_send,
    mixed_recv,
    merge_send,
    merge_recv,
    load_sems,
    parts,
    from_mate,
    incoming,
    mate_send,
    mate_recv,
    sum_send,
    sum_recv,
):
    sems = (None, None, mate_send, mate_recv, sum_send, sum_recv, None)
    plane = PlaneExchange(wide_count, None, None, parts, from_mate, incoming, sems)
    line = LineExchange(narrow_count)
    rows, width = sum_grad.shape
    own_cols = queries.shape[1]
    heads = own_cols // HDIM
    scale = HDIM ** (-0.5)

    def load(head):
        return pltpu.make_async_copy(
            probs.at[head], probs_held.at[head % 2], load_sems.at[head % 2]
        )

    load(0).start()
    greet_plane(plane)

    spread_small(gain, small, places[2], 0)
    norm_sums[...] = jnp.zeros_like(norm_sums)
    merge_sums[...] = jnp.zeros_like(merge_sums)

    def norm_rows(i, carry):
        some = pl.ds(pl.multiple_of(i * 16, 16), 16)
        hidden_grad = residual_scale * upper_grad[some] + hidden_part[some]
        norm_sums[0:1] += jnp.sum(hidden_grad * normed[some], axis=0, keepdims=True)
        norm_sums[1:2] += jnp.sum(hidden_grad, axis=0, keepdims=True)
        total = normalize_back(hidden_grad, normed[some], inv_std[some], gain[...])
        sum_grad[some] = total
        merge_sums[...] += jnp.sum(total, axis=0, keepdims=True)
        attended[some] = total.astype(jnp.bfloat16)
        return carry

    lax.fori_loop(0, rows // 16, norm_rows, 0, unroll=2)
    line.greet(3)

    def mixed_part(target, where):
        part = dot(
            attended[...],
            merge[pl.ds(pl.multiple_of(where * own_cols, own_cols), own_cols)],
            ((1,), (1,)),
        )
        target[...] = part.astype(jnp.bfloat16)

    for offset in range(1, narrow_count):
        place = line.peer(offset)
        mixed_part(outbound.at[offset - 1], place)
        line.send(offset, outbound.at[offset - 1], upstream, mixed_send, mixed_recv)
    mixed_part(upstream.at[line.mine], line.mine)

    block = parts.shape[1]

    def merge_rows(i, carry):
        cols = pl.ds(pl.multiple_of(i * block, block), block)
        parts[i] = dot(mixed[:, cols], attended[...], ((0,), (0,))).astype(jnp.bfloat16)
        return carry

    lax.fori_loop(0, wide_count, merge_rows, 0)
    for offset in range(plane.ring):
        plane.share(offset)
    plane.first_sums()
    plane.far_sums()
    plane.last_sums()
    plane.finish(merge_out)
    count = merge_grad.shape[0]

    def z_rows(where):
        return pl.ds(pl.multiple_of(where * count, count), count)

    for offset in range(1, narrow_count):
        line.send(
            offset, merge_out.at[z_rows(line.peer(offset))], merge_in, merge_send, merge_recv
        )
    for offset in range(1, narrow_count):
        line.arrived(offset, upstream, mixed_send, mixed_recv)

    def one_head(head):
        cols = pl.ds(head * HDIM, HDIM)
        load(head).wait()
        if head + 1 < heads:
            load(head + 1).start()
        held = probs_held.at[head % 2]
        keys_turned[...] = keys[:, cols].astype(jnp.float32).T.astype(jnp.bfloat16)
        key_total[...] = jnp.zeros_like(key_total)
        value_total[...] = jnp.zeros_like(value_total)

        def chunk(i, carry):
            here = pl.ds(pl.multiple_of(i * rows, rows), rows)
            weights_low = held[:, here]
            up = upstream[i, :, cols]
            pulled = dot(values[:, cols], up, ((1,), (1,)))
            weights = weights_low.astype(jnp.float32)
            scaled = weights * pulled
            change = (scaled - weights * jnp.sum(scaled, axis=0, keepdims=True)).astype(
                jnp.bfloat16
            )
            key_total[...] += dot(change, queries[here, cols], ((1,), (0,)))
            value_total[...] += dot(weights_low, up, ((1,), (0,)))
            query_grad = dot(keys_turned[...], change, ((1,), (0,))).T * scale
            triple[here, cols] = rotate_lanes(
                query_grad, cosine[here], signed_sine[here]
            ).astype(jnp.bfloat16)
            return carry

        lax.fori_loop(0, narrow_count, chunk, 0)

        def ending(i, carry):
            here = pl.ds(pl.multiple_of(i * rows, rows), rows)
            triple[here, pl.ds(own_cols + head * HDIM, HDIM)] = rotate_lanes(
                key_total[here] * scale, cosine[here], signed_sine[here]
            ).astype(jnp.bfloat16)
            triple[here, pl.ds(2 * own_cols + head * HDIM, HDIM)] = value_total[here].astype(
                jnp.bfloat16
            )
            return carry

        lax.fori_loop(0, narrow_count, ending, 0)

    for head in range(heads):
        one_head(head)

    def column_sums(cols):
        heads_sums[:, cols] = jnp.sum(
            triple[:, cols].astype(jnp.float32), axis=0, keepdims=True
        )

    tiles(3 * own_cols, 256, column_sums)
    summed = merge_out[z_rows(line.mine)].astype(jnp.float32)
    for offset in range(1, narrow_count):
        line.arrived(offset, merge_in, merge_send, merge_recv)
        summed += merge_in[line.peer(offset)].astype(jnp.float32)
    merge_grad[...] = summed
    line.drain()
    plane.drain()


def attention_backward(
    wide_count,
    narrow_count,
    places,
    upper_grad,
    hidden_part,
    normed,
    inv_std,
    small,
    merge_full,
    mixed,
    queries,
    keys,
    values,
    probs,
    cosine,
    signed_sine,
):
    rows, width = normed.shape
    bucket, own_cols = queries.shape
    block = width // wide_count
    count = block // narrow_count
    anywhere = pl.BlockSpec(memory_space=pl.ANY)
    vmem = pl.BlockSpec(memory_space=pltpu.VMEM)
    dma = pltpu.SemaphoreType.DMA
    return pl.pallas_call(
        functools.partial(attention_backward_kernel, wide_count, narrow_count, places),
        out_shape=(
            jax.ShapeDtypeStruct((bucket, 3 * own_cols), jnp.bfloat16),
            jax.ShapeDtypeStruct((count, width), jnp.float32),
            jax.ShapeDtypeStruct((1, 3 * own_cols), jnp.float32),
            jax.ShapeDtypeStruct((1, width), jnp.float32),
            jax.ShapeDtypeStruct((rows, width), jnp.float32),
            jax.ShapeDtypeStruct((2, width), jnp.float32),
        ),
        in_specs=[vmem] * 10 + [anywhere] + [vmem] * 2,
        out_specs=(vmem,) * 6,
        scratch_shapes=[
            pltpu.VMEM((1, width), jnp.float32),
            pltpu.VMEM((rows, width), jnp.bfloat16),
            pltpu.VMEM((narrow_count, rows, own_cols), jnp.bfloat16),
            pltpu.VMEM((narrow_count - 1, rows, own_cols), jnp.bfloat16),
            pltpu.VMEM((2, bucket, bucket), jnp.bfloat16),
            pltpu.VMEM((HDIM, bucket), jnp.bfloat16),
            pltpu.VMEM((bucket, HDIM), jnp.float32),
            pltpu.VMEM((bucket, HDIM), jnp.float32),
            pltpu.VMEM((block, width), jnp.bfloat16),
            pltpu.VMEM((narrow_count, count, width), jnp.bfloat16),
            dma((narrow_count - 1,)),
            dma((narrow_count,)),
            dma((narrow_count - 1,)),
            dma((narrow_count,)),
            dma((2,)),
        ]
        + sum_scratch(wide_count, block, width),
        compiler_params=pltpu.CompilerParams(
            collective_id=3, has_side_effects=True, vmem_limit_bytes=kernel_memory
        ),
        cost_estimate=pl.CostEstimate(
            flops=60 * 10**9, bytes_accessed=200 * 2**20, transcendentals=0
        ),
        name="attention_backward",
    )(
        upper_grad,
        hidden_part,
        normed,
        inv_std,
        small,
        merge_full,
        mixed,
        queries,
        keys,
        values,
        probs,
        cosine,
        signed_sine,
    )


def input_backward_kernel(
    wide_count,
    narrow_count,
    inputs,
    triple,
    heads_mat,
    small,
    sum_grad,
    input_part,
    heads_grad,
    heads_bias_grad,
    merge_bias_grad,
    gains_grad,
    shifts_grad,
    expand_bias_grad,
    reduce_bias_grad,
    small_result,
    line_parts,
    line_in,
    heads_out,
    heads_in,
    small_wide,
    small_sum,
    small_line,
    line_send,
    line_recv,
    heads_send,
    heads_recv,
    wide_send,
    wide_recv,
    small_send,
    small_recv,
    parts,
    from_mate,
    incoming,
    mate_send,
    mate_recv,
    sum_send,
    sum_recv,
):
    sems = (None, None, mate_send, mate_recv, sum_send, sum_recv, None)
    plane = PlaneExchange(wide_count, None, None, parts, from_mate, incoming, sems)
    line = LineExchange(narrow_count)
    rows, width = input_part.shape
    here = line.mine
    last = narrow_count - 1
    place = lax.axis_index("wide")

    def wide_peer(offset):
        return (place + offset) % wide_count

    barrier = pltpu.get_barrier_semaphore()
    for offset in range(1, wide_count):
        pl.semaphore_signal(
            barrier,
            inc=1,
            device_id={"wide": wide_peer(offset)},
            device_id_type=pl.DeviceIdType.MESH,
        )
    line.greet(wide_count - 1)

    def small_copy(offset, source, slot):
        return pltpu.make_async_remote_copy(
            src_ref=source,
            dst_ref=small_wide.at[slot],
            send_sem=wide_send.at[offset - 1],
            recv_sem=wide_recv.at[slot],
            device_id={"wide": wide_peer(offset)},
            device_id_type=pl.DeviceIdType.MESH,
        )

    small_copies = [
        small_copy(offset, small.at[wide_peer(offset)], place) for offset in range(1, wide_count)
    ]
    for copy in small_copies:
        copy.start()

    line_sum = LineSum(line, lambda target: line_parts.at[target], line_in, line_send, line_recv)

    def input_rows(index):
        some = pl.ds(pl.multiple_of(index * rows, rows), rows)

        def input_cols(cols):
            part = dot(triple[some], heads_mat[cols], ((1,), (1,)))
            line_parts[index, :, cols] = part.astype(jnp.bfloat16)

        tiles(width, 256, input_cols)

    for offset in range(last, 0, -1):
        for way in range(2):

            @pl.when(line_sum.reaches(way, offset))
            def _():
                input_rows(line_sum.target(way, offset))

        line_sum.begin(offset)
    input_rows(here)

    block = parts.shape[1]

    def heads_rows(i, carry):
        cols = pl.ds(pl.multiple_of(i * block, block), block)
        parts[i] = dot(inputs[:, cols], triple[...], ((0,), (0,))).astype(jnp.bfloat16)
        return carry

    lax.fori_loop(0, wide_count, heads_rows, 0)
    for offset in range(plane.ring):
        plane.share(offset)
    for offset in range(last - 1, last // 2, -1):
        line_sum.step(offset)
    plane.first_sums()
    plane.far_sums()

    for offset in range(1, wide_count):
        peer = wide_peer(offset)
        small_copy(offset, small_wide.at[peer], peer).wait_recv()
    small_wide[place] = small[place]
    total = small_wide[0]
    for index in range(1, wide_count):
        total += small_wide[index]
    small_sum[...] = total
    for offset in range(1, narrow_count):
        line.send(offset, small_sum.at[line.peer(offset)], small_line, small_send, small_recv)

    plane.last_sums()
    for offset in range(last // 2, 0, -1):
        line_sum.step(offset)
    plane.finish(heads_out)
    count = heads_grad.shape[0]

    def z_rows(where):
        return pl.ds(pl.multiple_of(where * count, count), count)

    for offset in range(1, narrow_count):
        line.send(
            offset, heads_out.at[z_rows(line.peer(offset))], heads_in, heads_send, heads_recv
        )
    heads_in[line.mine] = heads_out[z_rows(line.mine)]
    small_line[line.mine] = small_sum[line.mine]
    for offset in range(1, narrow_count):
        line.arrived(offset, small_line, small_send, small_recv)
    result = small_line[0]
    for index in range(1, narrow_count):
        result += small_line[index]
    small_result[...] = result
    row = 0
    for target in (
        heads_bias_grad,
        merge_bias_grad,
        gains_grad,
        shifts_grad,
        expand_bias_grad,
        reduce_bias_grad,
    ):
        first, size = target.shape
        for index in range(first):
            for start in range(0, size, 128):
                stop = min(start + 128, size)
                target[index : index + 1, start:stop] = small_result[
                    row : row + 1, 0 : stop - start
                ]
                row += 1

    line_sum.finish(input_part)

    def add_residual(i, carry):
        some = pl.ds(pl.multiple_of(i * 16, 16), 16)
        input_part[some] += residual_scale * sum_grad[some]
        return carry

    lax.fori_loop(0, rows // 16, add_residual, 0)
    for offset in range(1, narrow_count):
        line.arrived(offset, heads_in, heads_send, heads_recv)
    own_cols = triple.shape[1] // 3
    for index in range(narrow_count):
        for which in range(3):
            start = (which * narrow_count + index) * own_cols
            heads_grad[:, start : start + own_cols] = heads_in[
                index, :, which * own_cols : (which + 1) * own_cols
            ].astype(jnp.float32)
    line_sum.drain()
    for copy in small_copies:
        copy.wait_send()
    line.drain()
    plane.drain()


def input_backward(
    wide_count, narrow_count, inputs, triple_grad, heads_mat, small, sum_grad, small_shapes
):
    bucket, width = inputs.shape
    rows = bucket // narrow_count
    columns = triple_grad.shape[1]
    block = width // wide_count
    count = block // narrow_count
    vmem = pl.BlockSpec(memory_space=pltpu.VMEM)
    dma = pltpu.SemaphoreType.DMA
    lines = small.shape[2]
    return pl.pallas_call(
        functools.partial(input_backward_kernel, wide_count, narrow_count),
        out_shape=(
            jax.ShapeDtypeStruct((rows, width), jnp.float32),
            jax.ShapeDtypeStruct((count, narrow_count * columns), jnp.float32),
        )
        + tuple(jax.ShapeDtypeStruct(shape, jnp.float32) for shape in small_shapes),
        in_specs=[vmem] * 5,
        out_specs=(vmem,) * 8,
        scratch_shapes=[
            pltpu.VMEM((lines, 128), jnp.float32),
            pltpu.VMEM((narrow_count, rows, width), jnp.bfloat16),
            pltpu.VMEM((2, narrow_count - 1, rows, width), jnp.bfloat16),
            pltpu.VMEM((block, columns), jnp.bfloat16),
            pltpu.VMEM((narrow_count, count, columns), jnp.bfloat16),
            pltpu.VMEM((wide_count, narrow_count, lines, 128), jnp.float32),
            pltpu.VMEM((narrow_count, lines, 128), jnp.float32),
            pltpu.VMEM((narrow_count, lines, 128), jnp.float32),
            dma((2, narrow_count - 1)),
            dma((2, narrow_count - 1)),
            dma((narrow_count - 1,)),
            dma((narrow_count,)),
            dma((wide_count - 1,)),
            dma((wide_count,)),
            dma((narrow_count - 1,)),
            dma((narrow_count,)),
        ]
        + sum_scratch(wide_count, block, columns),
        compiler_params=pltpu.CompilerParams(
            collective_id=4, has_side_effects=True, vmem_limit_bytes=kernel_memory
        ),
        cost_estimate=pl.CostEstimate(
            flops=80 * 10**9, bytes_accessed=200 * 2**20, transcendentals=0
        ),
        name="input_backward",
    )(inputs, triple_grad, heads_mat, small, sum_grad)


def greet_all(wide_count, narrow_count):
    barrier = pltpu.get_barrier_semaphore()
    for axis, count in (("wide", wide_count), ("narrow", narrow_count)):
        place = lax.axis_index(axis)
        for offset in range(1, count):
            pl.semaphore_signal(
                barrier,
                inc=1,
                device_id={axis: (place + offset) % count},
                device_id_type=pl.DeviceIdType.MESH,
            )
    pl.semaphore_wait(barrier, wide_count + narrow_count - 2)


def gather_kernel(
    wide_count,
    narrow_count,
    own,
    heads_weight,
    merge_weight,
    heads_bias,
    merge_bias,
    norm_gains,
    norm_shifts,
    expand_bias,
    reduce_bias,
    joined_ref,
    prefix_ref,
    speeds,
    rows_out,
    heads_out,
    merge_out,
    small_out,
    triple,
    cosine,
    signed_sine,
    first_query,
    last_query,
    small,
    rows_all,
    triple_all,
    heads_all,
    merge_own,
    small_all,
    rows_send,
    rows_recv,
    heads_send,
    heads_recv,
    merge_send,
    merge_recv,
    small_send,
    small_recv,
    wide_send,
    wide_recv,
    local_sems,
    out_sems,
    heads_ring_send,
    heads_ring_recv,
    block_sems,
):
    ring_sems = (heads_ring_send, heads_ring_recv, None, None, None, None, None)
    heads_ring = PlaneExchange(wide_count, None, heads_all, heads_all, None, None, ring_sems)
    line = LineExchange(narrow_count)
    here = line.mine
    last = narrow_count - 1
    place = lax.axis_index("wide")
    slot = heads_ring.slot(0)
    rows, width = own.shape
    count = heads_weight.shape[0]
    columns = heads_all.shape[2]
    own_cols = columns // 3

    def z_rows(where):
        return pl.ds(pl.multiple_of(where * count, count), count)

    def head_cols(which, where):
        start = which * narrow_count * own_cols + where * own_cols
        return pl.ds(pl.multiple_of(start, own_cols), own_cols)

    line_rows = LineGather(line, lambda block: rows_all.at[block], rows_send, rows_recv)

    keep_rows = pltpu.make_async_copy(own, rows_all.at[here], local_sems.at[0])
    keep_rows.start()
    keeps = [
        pltpu.make_async_copy(
            heads_weight.at[:, head_cols(which, here)],
            heads_all.at[slot, z_rows(here), pl.ds(which * own_cols, own_cols)],
            local_sems.at[2 + which],
        )
        for which in range(3)
    ]
    keep_merge = pltpu.make_async_copy(
        merge_weight, merge_own.at[z_rows(here)], local_sems.at[1]
    )
    for copy in keeps + [keep_merge]:
        copy.start()
    smalls = (heads_bias, merge_bias, norm_gains, norm_shifts, expand_bias, reduce_bias)
    small[...] = jnp.zeros_like(small)
    row = 0
    for part in smalls:
        first, size = part.shape
        for index in range(first):
            for begin in range(0, size, 128):
                stop = min(begin + 128, size)
                small[row : row + 1, 0 : stop - begin] = part[
                    index : index + 1, begin:stop
                ].astype(jnp.float32)
                row += 1
    small_all[place, here] = small[...]
    greet_all(wide_count, narrow_count)

    def heads_copy(offset, which, where, sender):
        return line.copy(
            heads_weight.at[:, head_cols(which, where)],
            heads_all.at[slot, z_rows(sender), pl.ds(which * own_cols, own_cols)],
            heads_send.at[offset - 1, which],
            heads_recv.at[sender, which],
            where,
        )

    def merge_copy(offset, where, sender):
        return line.copy(
            merge_weight,
            merge_own.at[z_rows(sender)],
            merge_send.at[offset - 1],
            merge_recv.at[sender],
            where,
        )

    def small_copy(offset, where, sender):
        return line.copy(
            small,
            small_all.at[place, sender],
            small_send.at[offset - 1],
            small_recv.at[sender],
            where,
        )

    started = []

    def start(copy):
        copy.start()
        started.append(copy)

    keep_rows.wait()
    line_rows.send_own()
    for offset in range(1, narrow_count):
        for which in range(3):
            start(heads_copy(offset, which, line.peer(offset), here))
    for offset in range(1, narrow_count):
        start(small_copy(offset, line.peer(offset), here))

    halfway = narrow_count * rows // 2
    joined = joined_ref[0]

    def tables(i, carry):
        some = pl.ds(pl.multiple_of(i * rows, rows), rows)
        place_in = i * rows + lax.broadcasted_iota(jnp.int32, (rows, 1), 0)
        second = jnp.where(place_in >= halfway, 1 - joined, 0)
        local = place_in - second * halfway
        reach = jnp.where(
            joined == 1,
            prefix_ref[0, 0] + prefix_ref[0, 1],
            jnp.where(second == 1, prefix_ref[0, 1], prefix_ref[0, 0]),
        )
        first_query[some] = jnp.where(local < reach, place_in - local, place_in)
        last_query[some] = jnp.where(
            (joined == 1) | (second == 1), 2 * halfway - 1, halfway - 1
        ) + jnp.zeros_like(place_in)
        angles = local.astype(jnp.float32) * speeds[...]
        lane = lax.broadcasted_iota(jnp.int32, (rows, HDIM), 1)
        cosine[some] = jnp.cos(angles)
        sine = jnp.sin(angles)
        signed_sine[some] = jnp.where(lane < HDIM // 2, sine, -sine)
        return carry

    lax.fori_loop(0, narrow_count, tables, 0)

    line_rows.step(1)
    for copy in keeps:
        copy.wait()
    for offset in range(1, narrow_count):
        for which in range(3):
            heads_copy(offset, which, line.peer(offset), line.peer(offset)).wait_recv()
    heads_ring.send_own()
    for offset in range(1, narrow_count):
        small_copy(offset, line.peer(offset), line.peer(offset)).wait_recv()

    def wide_copy(offset, sender):
        return pltpu.make_async_remote_copy(
            src_ref=small_all.at[sender],
            dst_ref=small_all.at[sender],
            send_sem=wide_send.at[offset - 1],
            recv_sem=wide_recv.at[sender],
            device_id={"wide": (place + offset) % wide_count},
            device_id_type=pl.DeviceIdType.MESH,
        )

    for offset in range(1, wide_count):
        start(wide_copy(offset, place))

    def leave_rows(block):
        return pltpu.make_async_copy(rows_all.at[block], rows_out.at[block], block_sems.at[0, block])

    def leave_triple(block):
        return pltpu.make_async_copy(triple_all.at[block], triple.at[block], block_sems.at[1, block])

    def project(block):
        leave_rows(block).start()

        def cols_step(cols):
            weight = heads_all[:, :, cols].reshape(width, cols.size)
            triple_all[block, :, cols] = dot(rows_all[block], weight, ((1,), (0,)))

        tiles(columns, 256, cols_step)
        leave_triple(block).start()

    def project_step(step):
        line_rows.each(step, project)

    def gather(ring, distance):
        ring.receive(distance)
        ring.receive_mate(-distance)
        if distance < ring.far:
            ring.receive_mate(distance)

    outs = []

    def keep_out(source, target):
        copy = pltpu.make_async_copy(source, target, out_sems.at[len(outs)])
        copy.start()
        outs.append(copy)

    heads_ring.receive_mate(0)
    for distance in range(1, heads_ring.far):
        gather(heads_ring, distance)
    if last > 1:
        line_rows.step(2)
    for offset in range(1, narrow_count):
        start(merge_copy(offset, line.peer(offset), here))
    gather(heads_ring, heads_ring.far)
    keep_out(heads_all, heads_out)
    project(here)
    project_step(1)
    for step in range(3, narrow_count):
        project_step(step - 1)
        line_rows.step(step)
    project_step(last)
    keep_merge.wait()
    for offset in range(1, narrow_count):
        merge_copy(offset, line.peer(offset), line.peer(offset)).wait_recv()
    keep_out(merge_own, merge_out)
    for offset in range(1, wide_count):
        wide_copy(offset, (place + offset) % wide_count).wait_recv()
    keep_out(small_all, small_out)
    line_rows.drain()
    for copy in started:
        copy.wait_send()
    heads_ring.drain()
    for copy in outs:
        copy.wait()

    def left(block, carry):
        leave_rows(block).wait()
        leave_triple(block).wait()
        return carry

    lax.fori_loop(0, narrow_count, left, 0)


def gather_front(
    wide_count, narrow_count, layer_input, heads_weight, merge_weight, smalls, joined, prefix, speeds
):
    rows, width = layer_input.shape
    count, all_columns = heads_weight.shape
    columns = all_columns // narrow_count
    block = count * narrow_count
    anywhere = pl.BlockSpec(memory_space=pl.ANY)
    vmem = pl.BlockSpec(memory_space=pltpu.VMEM)
    dma = pltpu.SemaphoreType.DMA
    lines = row_places([part.shape for part in smalls])[1]
    shapes = (
        (narrow_count, rows, width),
        (wide_count, block, columns),
        (block, width),
        (wide_count, narrow_count, lines, 128),
    )
    far = narrow_count - 1
    bucket = narrow_count * rows
    table = jax.ShapeDtypeStruct((bucket, HDIM), jnp.float32)
    reach = jax.ShapeDtypeStruct((bucket, 1), jnp.int32)
    return pl.pallas_call(
        functools.partial(gather_kernel, wide_count, narrow_count),
        out_shape=tuple(jax.ShapeDtypeStruct(shape, jnp.bfloat16) for shape in shapes[:3])
        + (
            jax.ShapeDtypeStruct(shapes[3], jnp.float32),
            jax.ShapeDtypeStruct((narrow_count, rows, columns), jnp.float32),
            table,
            table,
            reach,
            reach,
        ),
        in_specs=[anywhere] * 3 + [vmem] * 6 + [pl.BlockSpec(memory_space=pltpu.SMEM)] * 2 + [vmem],
        out_specs=(anywhere,) * 5 + (vmem,) * 4,
        scratch_shapes=[
            pltpu.VMEM((lines, 128), jnp.float32),
            pltpu.VMEM(shapes[0], jnp.bfloat16),
            pltpu.VMEM((narrow_count, rows, columns), jnp.float32),
        ]
        + [pltpu.VMEM(shape, jnp.bfloat16) for shape in shapes[1:3]]
        + [pltpu.VMEM(shapes[3], jnp.float32)]
        + [
            dma((2, narrow_count)),
            dma((narrow_count,)),
            dma((far, 3)),
            dma((narrow_count, 3)),
            dma((far,)),
            dma((narrow_count,)),
            dma((far,)),
            dma((narrow_count,)),
            dma((wide_count - 1,)),
            dma((wide_count,)),
            dma((5,)),
            dma((4,)),
            dma((3, wide_count, 2)),
            dma((wide_count, 2)),
            dma((2, narrow_count)),
        ],
        compiler_params=pltpu.CompilerParams(
            collective_id=5, has_side_effects=True, vmem_limit_bytes=kernel_memory
        ),
        cost_estimate=pl.CostEstimate(
            flops=80 * 10**9, bytes_accessed=200 * 2**20, transcendentals=0
        ),
        name="gather_front",
    )(layer_input, heads_weight, merge_weight, *smalls, joined, prefix, speeds)


def attention_forward_kernel(
    wide_count,
    narrow_count,
    places,
    triple,
    small,
    cosine,
    signed_sine,
    first_query,
    last_query,
    own,
    merge,
    queries,
    keys,
    values,
    probs,
    mixed_out,
    hidden,
    hidden_low,
    normed,
    inv_std,
    merge_out,
    rows_out,
    merge_mat,
    probs_held,
    values_turned,
    outbound,
    mixed,
    mixed_send,
    mixed_recv,
    local_sems,
    ring_send,
    ring_recv,
    own_sem,
    rows_all,
    rows_send,
    rows_recv,
    rows_sem,
    heads_full,
    vectors,
):
    line = LineExchange(narrow_count)
    ring_sems = (ring_send, ring_recv, None, None, None, None, own_sem)
    ring = PlaneExchange(wide_count, merge, merge_mat, merge_mat, None, None, ring_sems)
    rows_sems = (rows_send, rows_recv, None, None, None, None, rows_sem)
    rows_ring = PlaneExchange(wide_count, hidden_low, rows_all, rows_all, None, None, rows_sems)
    bucket, own_cols = queries.shape
    rows, width = own.shape
    heads = own_cols // HDIM
    scale = HDIM ** (-0.5)
    greet_plane(ring)
    line.greet(3)
    keep_own = ring.send_own()
    spread_small(heads_full, small, places[0], 0)
    spread_small(vectors, small, places[1], 0, 0)
    spread_small(vectors, small, places[2], 0, 1)
    spread_small(vectors, small, places[3], 0, 2)
    ring_steps = [functools.partial(ring.receive, step) for step in range(1, ring.far + 1)]

    def keep(head):
        return pltpu.make_async_copy(
            probs_held.at[head % 2], probs.at[head], local_sems.at[head % 2]
        )

    def mixed_copy(head, offset, where, sender):
        cols = pl.ds(pl.multiple_of(sender * own_cols + head * HDIM, HDIM), HDIM)
        return line.copy(
            outbound.at[where, :, pl.ds(head * HDIM, HDIM)],
            mixed.at[:, cols],
            mixed_send.at[offset - 1, head],
            mixed_recv.at[sender, head],
            where,
        )

    started = []
    for head in range(heads):
        cols = pl.ds(head * HDIM, HDIM)

        def turn(i, carry):
            here = pl.ds(pl.multiple_of(i * rows, rows), rows)
            for which, target in enumerate((queries, keys, values)):
                wanted = pl.ds(which * own_cols + head * HDIM, HDIM)
                begin = (which * narrow_count + line.mine) * own_cols + head * HDIM
                bias = heads_full[:, pl.ds(pl.multiple_of(begin, HDIM), HDIM)]
                part = triple[here, wanted] + bias
                if which < 2:
                    part = rotate_lanes(part, cosine[here], -signed_sine[here])
                else:
                    values_turned[:, here] = part.T.astype(jnp.bfloat16)
                target[here, cols] = part.astype(jnp.bfloat16)
            return carry

        lax.fori_loop(0, narrow_count, turn, 0)
        if head >= 2:
            keep(head - 2).wait()
        held = probs_held.at[head % 2]

        def chunk(i, carry):
            here = pl.ds(pl.multiple_of(i * rows, rows), rows)
            scores = dot(keys[:, cols], queries[here, cols], ((1,), (1,))) * scale
            token = i * rows + lax.broadcasted_iota(jnp.int32, (bucket, rows), 1)
            seen = (token >= first_query[...]) & (token <= last_query[...])
            scores = jnp.where(seen, scores, masked_value)
            expo = jnp.exp(scores - jnp.max(scores, axis=0, keepdims=True))
            weights = (expo * (1 / jnp.sum(expo, axis=0, keepdims=True))).astype(jnp.bfloat16)
            held[:, here] = weights
            mixed_part = dot(values_turned[...], weights, ((1,), (0,)))
            outbound[i, :, cols] = mixed_part.T.astype(jnp.bfloat16)
            return carry

        lax.fori_loop(0, narrow_count, chunk, 0)
        keep(head).start()
        for offset in range(1, narrow_count):
            copy = mixed_copy(head, offset, line.peer(offset), line.mine)
            copy.start()
            started.append(copy)
        if ring_steps and head >= heads - len(ring_steps):
            ring_steps.pop(0)()
    own_mixed = pltpu.make_async_copy(
        outbound.at[line.mine],
        mixed.at[:, pl.ds(pl.multiple_of(line.mine * own_cols, own_cols), own_cols)],
        local_sems.at[3],
    )
    own_mixed.start()
    own_mixed.wait()
    keep_own.wait()
    for step in ring_steps:
        step()
    for offset in range(ring.ring):
        ring.receive_mate(offset)
    keep_merge = pltpu.make_async_copy(merge_mat, merge_out, local_sems.at[2])
    keep_merge.start()
    for offset in range(1, narrow_count):
        for head in range(heads):
            mixed_copy(head, offset, line.peer(offset), line.peer(offset)).wait_recv()
    mixed_out[...] = mixed[...]

    def merge_cols(cols):
        hidden[:, cols] = (
            residual_scale * own[:, cols].astype(jnp.float32)
            + dot(mixed[...], merge_mat[:, :, cols].reshape(width, cols.size), ((1,), (0,)))
            + vectors[0:1, cols]
        )

    tiles(width, 256, merge_cols)

    def norm_rows(i, carry):
        some = pl.ds(pl.multiple_of(i * 16, 16), 16)
        result, centred, inverse = normalize(hidden[some], vectors[1:2], vectors[2:3])
        hidden[some] = result
        hidden_low[some] = result.astype(jnp.bfloat16)
        normed[some] = centred
        inv_std[some] = inverse
        return carry

    lax.fori_loop(0, rows // 16, norm_rows, 0, unroll=2)
    keep_rows = rows_ring.send_own()
    for step in range(1, rows_ring.far + 1):
        rows_ring.receive(step)
    for offset in range(rows_ring.ring):
        rows_ring.receive_mate(offset)
    keep_rows.wait()
    keep_rows = pltpu.make_async_copy(rows_all, rows_out, rows_sem)
    keep_rows.start()
    for head in range(max(heads - 2, 0), heads):
        keep(head).wait()
    for copy in started:
        copy.wait_send()
    ring.drain()
    rows_ring.drain()
    keep_merge.wait()
    keep_rows.wait()


def attention_forward(
    wide_count,
    narrow_count,
    places,
    triple,
    small,
    cosine,
    signed_sine,
    first_query,
    last_query,
    layer_input,
    merge_block,
):
    bucket, columns = triple.shape
    rows, width = layer_input.shape
    own_cols = columns // 3
    heads = own_cols // HDIM
    anywhere = pl.BlockSpec(memory_space=pl.ANY)
    vmem = pl.BlockSpec(memory_space=pltpu.VMEM)
    dma = pltpu.SemaphoreType.DMA

    def low_shape(*shape):
        return jax.ShapeDtypeStruct(shape, jnp.bfloat16)

    def wide_shape(*shape):
        return jax.ShapeDtypeStruct(shape, jnp.float32)

    return pl.pallas_call(
        functools.partial(attention_forward_kernel, wide_count, narrow_count, places),
        out_shape=(
            low_shape(bucket, own_cols),
            low_shape(bucket, own_cols),
            low_shape(bucket, own_cols),
            low_shape(heads, bucket, bucket),
            low_shape(rows, width),
            wide_shape(rows, width),
            low_shape(rows, width),
            wide_shape(rows, width),
            wide_shape(rows, 1),
            low_shape(wide_count, *merge_block.shape),
            low_shape(wide_count, rows, width),
        ),
        in_specs=[vmem] * 7 + [anywhere],
        out_specs=(vmem, vmem, vmem, anywhere) + (vmem,) * 5 + (anywhere,) * 2,
        scratch_shapes=[
            pltpu.VMEM((wide_count, *merge_block.shape), jnp.bfloat16),
            pltpu.VMEM((2, bucket, bucket), jnp.bfloat16),
            pltpu.VMEM((HDIM, bucket), jnp.bfloat16),
            pltpu.VMEM((narrow_count, rows, own_cols), jnp.bfloat16),
            pltpu.VMEM((rows, width), jnp.bfloat16),
            dma((narrow_count - 1, heads)),
            dma((narrow_count, heads)),
            dma((4,)),
            dma((3, wide_count, 2)),
            dma((wide_count, 2)),
            dma(()),
            pltpu.VMEM((wide_count, rows, width), jnp.bfloat16),
            dma((3, wide_count, 2)),
            dma((wide_count, 2)),
            dma(()),
            pltpu.VMEM((1, 3 * width), jnp.float32),
            pltpu.VMEM((3, width), jnp.float32),
        ],
        compiler_params=pltpu.CompilerParams(
            collective_id=6, has_side_effects=True, vmem_limit_bytes=kernel_memory
        ),
        cost_estimate=pl.CostEstimate(
            flops=60 * 10**9, bytes_accessed=200 * 2**20, transcendentals=0
        ),
        name="attention_forward",
    )(
        triple,
        small,
        cosine,
        signed_sine,
        first_query,
        last_query,
        layer_input,
        merge_block,
    )


def shards(
    layer_input,
    heads_weight,
    heads_bias,
    merge_weight,
    merge_bias,
    norm_gains,
    norm_shifts,
    expand_weight,
    expand_bias,
    reduce_weight,
    reduce_bias,
    joined,
    prefix,
    cotangent,
):
    tok_rows, model_width = layer_input.shape
    wide_count = lax.axis_size("wide")
    narrow_count = lax.axis_size("narrow")
    count = wide_count * narrow_count
    bucket_len = tok_rows * narrow_count
    own_heads = HEADS // narrow_count
    own_cols = own_heads * HDIM
    share = expand_weight.shape[2]
    narrow_index = lax.axis_index("narrow")
    smalls = (
        heads_bias.reshape(1, -1),
        merge_bias.reshape(1, -1),
        norm_gains,
        norm_shifts,
        expand_bias,
        reduce_bias.reshape(1, -1),
    )
    places = row_places([part.shape for part in smalls])[0]
    (
        rows_input,
        heads_mat,
        merge_block,
        small_all,
        triple,
        cosine,
        signed_sine,
        first_query,
        last_query,
    ) = gather_front(
        wide_count,
        narrow_count,
        layer_input,
        heads_weight,
        merge_weight,
        smalls,
        joined,
        prefix,
        jnp.asarray(rotary_speeds(HDIM)),
    )
    rows_input = rows_input.reshape(bucket_len, model_width)
    heads_mat = heads_mat.reshape(model_width, 3 * own_cols)
    triple = triple.reshape(bucket_len, 3 * own_cols)
    (
        queries,
        keys,
        values,
        probs_low,
        mixed,
        hidden,
        hidden_low,
        normed_one,
        inv_one,
        merge_full,
        rows_all,
    ) = attention_forward(
        wide_count,
        narrow_count,
        places,
        triple,
        small_all,
        cosine,
        signed_sine,
        first_query,
        last_query,
        layer_input,
        merge_block,
    )

    tile_rows = -share % 16
    padded = -(-share // 256) * 256
    expand_low = jnp.pad(expand_weight.transpose(1, 2, 0), ((0, 0), (0, tile_rows), (0, 0)))
    expand_low, _ = lax.optimization_barrier((expand_low, small_all))
    expand_full = lax.all_gather(expand_low, "narrow", axis=2, tiled=True)
    reduce_low = jnp.pad(reduce_weight, ((0, tile_rows), (0, 0)))
    (
        reduce_full,
        active,
        slope,
        gelu,
        layer_output,
        sum_two_grad,
        feed_grad,
        row_sums,
    ) = geglu_forward(
        wide_count,
        narrow_count,
        places,
        rows_all,
        expand_full,
        reduce_low,
        small_all,
        hidden,
        cotangent,
    )
    reduce_weight_gradient, expand_part, hidden_part, unit_sums = geglu_backward(
        wide_count,
        narrow_count,
        feed_grad,
        expand_full,
        reduce_full,
        slope,
        gelu,
        active,
        rows_all,
    )
    expand_weight_gradient = (
        lax.psum_scatter(expand_part, "narrow", scatter_dimension=2, tiled=True)[:, :share]
        .astype(jnp.float32)
        .transpose(2, 0, 1)
    )
    (
        triple_grad,
        merge_weight_gradient,
        heads_sums,
        merge_sums,
        sum_one_grad,
        norm_one_sums,
    ) = attention_backward(
        wide_count,
        narrow_count,
        places,
        sum_two_grad,
        hidden_part,
        normed_one,
        inv_one,
        small_all,
        merge_full.reshape(model_width, model_width),
        mixed,
        queries,
        keys,
        values,
        probs_low,
        cosine,
        signed_sine,
    )

    mine_narrow = (jnp.arange(narrow_count) == narrow_index).astype(jnp.float32)
    mine_wide = (jnp.arange(wide_count) == lax.axis_index("wide")).astype(jnp.float32)
    heads_sums = (heads_sums.reshape(3, 1, own_cols) * mine_narrow[None, :, None]).reshape(count, 1, -1)
    norm_sums = jnp.stack([norm_one_sums[0], row_sums[0], norm_one_sums[1], row_sums[1]])
    norm_sums = norm_sums.reshape(4, count, -1).transpose(1, 0, 2)
    expand_sums = unit_sums[:, :share].reshape(2, narrow_count, -1).transpose(1, 0, 2)[None]
    expand_sums = (expand_sums * mine_wide[:, None, None, None]).reshape(count, 2, -1)
    reduce_sums = row_sums[2].reshape(1, narrow_count, 1, -1)
    reduce_sums = jnp.broadcast_to(
        reduce_sums, (wide_count, narrow_count, 1, reduce_sums.shape[3])
    ).reshape(count, 1, -1)
    pieces = (heads_sums, merge_sums.reshape(count, 1, -1), norm_sums, expand_sums, reduce_sums)
    packed = []
    for piece in pieces:
        piece = jnp.pad(piece, ((0, 0), (0, 0), (0, -piece.shape[2] % 128)))
        packed.append(piece.reshape(count, -1, 128))
    packed = jnp.concatenate(packed, axis=1)
    packed = jnp.pad(packed, ((0, 0), (0, -packed.shape[1] % 8), (0, 0)))
    (
        input_gradient,
        heads_weight_gradient,
        heads_bias_gradient,
        merge_bias_gradient,
        gains_gradient,
        shifts_gradient,
        expand_bias_gradient,
        reduce_bias_gradient,
    ) = input_backward(
        wide_count,
        narrow_count,
        rows_input,
        triple_grad,
        heads_mat,
        packed.reshape(wide_count, narrow_count, -1, 128),
        sum_one_grad,
        (
            (1, heads_bias.size),
            (1, merge_bias.size),
            norm_gains.shape,
            norm_shifts.shape,
            expand_bias.shape,
            (1, reduce_bias.size),
        ),
    )
    return (
        layer_output,
        input_gradient,
        heads_weight_gradient,
        heads_bias_gradient[0],
        merge_weight_gradient,
        merge_bias_gradient[0],
        gains_gradient,
        shifts_gradient,
        expand_weight_gradient,
        expand_bias_gradient,
        reduce_weight_gradient[:share],
        reduce_bias_gradient[0],
    )


def solution(mesh):
    return jax.shard_map(
        shards,
        mesh=mesh,
        in_specs=(
            P(("wide", "narrow"), None),
            P(("wide", "narrow"), None),
            P(("wide", "narrow")),
            P(("wide", "narrow"), None),
            P(("wide", "narrow")),
            P(None, ("wide", "narrow")),
            P(None, ("wide", "narrow")),
            P("narrow", None, "wide"),
            P(None, ("wide", "narrow")),
            P("wide", "narrow"),
            P("narrow"),
            P("wide"),
            P("wide", None),
            P(("wide", "narrow"), None),
        ),
        out_specs=(
            P(("wide", "narrow"), None),
            P(("wide", "narrow"), None),
            P(("wide", "narrow"), None),
            P(("wide", "narrow")),
            P(("wide", "narrow"), None),
            P(("wide", "narrow")),
            P(None, ("wide", "narrow")),
            P(None, ("wide", "narrow")),
            P("narrow", None, "wide"),
            P(None, ("wide", "narrow")),
            P("wide", "narrow"),
            P("narrow"),
        ),
        check_vma=False,
    )
```
